32 devices in a mesh: section: 2 (over x), dp: 4 (over z), seq: 4 (over y, core).
Axes of the slice: x: 2, y: 2, z: 4, core: 2. Of those that a mesh axis runs over, the one named last changes fastest.
Arguments:
- hidden_in: bfloat16 [2, 4, 1024, 1536], P(None, 'dp', 'seq'), may hold values from -6 to 6
- out_grad: bfloat16 [2, 4, 1024, 1536], P(None, 'dp', 'seq'), may hold values from -6 to 6
- attn_gain: bfloat16 [2, 1536], P('section', ('dp', 'seq')), may hold values from 0.5 to 1.5
- ffn_gain: bfloat16 [2, 1536], P('section', ('dp', 'seq')), may hold values from 0.5 to 1.5
- query_matrix: bfloat16 [2, 1536, 1536], P('section', ('dp', 'seq')), may hold values from -0.15625 to 0.15625
- key_matrix: bfloat16 [2, 1536, 512], P('section', ('dp', 'seq')), may hold values from -0.15625 to 0.15625
- value_matrix: bfloat16 [2, 1536, 512], P('section', ('dp', 'seq')), may hold values from -0.15625 to 0.15625
- output_matrix: bfloat16 [2, 1536, 1536], P('section', ('dp', 'seq')), may hold values from -2.5 to 2.5
- router_matrix: bfloat16 [2, 1536, 32], P('section', ('dp', 'seq')), may hold values from -0.079589844 to 0.079589844
- w_gate: bfloat16 [2, 32, 1536, 512], P('section', 'dp'), may hold values from -0.15625 to 0.15625
- w_up: bfloat16 [2, 32, 1536, 512], P('section', 'dp'), may hold values from -0.15625 to 0.15625
- w_down: bfloat16 [2, 32, 512, 1536], P('section', 'dp'), may hold values from -1 to 1
- routes: int32 [2, 2, 4, 1024, 8], P('section', None, 'dp', 'seq'), may hold values from 0 to 31, all different within a row; in each aligned block of 256 rows (0 to 255, 256 to 511, ..., all dimensions but the last counted through in order) at most 80 rows name the same one
Outputs:
- layer_outs: float32 [2, 2, 4, 1024, 1536], P('section', None, 'dp', 'seq')
- section_grads: float32 [2, 2, 4, 1024, 1536], P('section', None, 'dp', 'seq')
- grad_attn_gain: float32 [2, 1536], P('section', ('dp', 'seq'))
- grad_ffn_gain: float32 [2, 1536], P('section', ('dp', 'seq'))
- grad_query: float32 [2, 1536, 1536], P('section', ('dp', 'seq'))
- grad_key: float32 [2, 1536, 512], P('section', ('dp', 'seq'))
- grad_value: float32 [2, 1536, 512], P('section', ('dp', 'seq'))
- grad_out: float32 [2, 1536, 1536], P('section', ('dp', 'seq'))
- grad_router: float32 [2, 1536, 32], P('section', ('dp', 'seq'))
- grad_gate: float32 [2, 32, 1536, 512], P('section', 'dp', 'seq')
- grad_up: float32 [2, 32, 1536, 512], P('section', 'dp', 'seq')
- grad_down: float32 [2, 32, 512, 1536], P('section', 'dp', 'seq')
The draws below stay inside these ranges and needn't reach their ends.
Inputs may be any that keep to these rules, and one draw needn't show every extreme that they name: `routes`: each token names 8 different experts. In each aligned block of 256 rows (one block of positions of one sequence) no expert is named by more than 80 rows, a bound that some block reaches.
All inputs are finite; a program needn't handle non-finite values.
Results may differ from the reference program's by a relative error of at most 0.024.
Values may be sent and summed in bfloat16 or wider, within the bound.
A program may use at most 960 MiB of HBM per device.

```python
import math
from functools import partial
import jax
import jax.numpy as jnp
import numpy as np
from jax import lax

D = 1536
HEADS = 24
KV_HEADS = 8
HEAD_DIM = 64
FF = 512
TOP_K = 8
EXPERTS = 32
MICRO = 2
SLICE = 256
CAP = 80
SEQS = 4
LEN = 1024
N_SECTION = 2


def block_scale(stream_key, extent, split, least, largest):
    loudness, own = 1.0, jax.random.fold_in(stream_key, 6)
    for dim, shards_of in split:
        draws = jnp.exp(jax.random.uniform(jax.random.fold_in(own, dim), (shards_of,), jnp.float32, least / len(split), largest / len(split)))
        loudness = loudness * jnp.repeat(draws, extent[dim] // shards_of).reshape([-1 if axis == dim else 1 for axis in range(len(extent))])
    return loudness


def routed_block(stream_key, own, number, rows, number_of, top, reach, slope):
    order = jax.random.permutation(stream_key, number_of)
    crowded, ordinary = load_shares(number_of, rows * top, reach, slope, True), load_shares(number_of, rows * top, reach, slope, False)
    places = jnp.arange(number_of)

    def named(tallies, rotation):
        used = int((tallies > 0).sum())
        fixed = max(1, used // 4)
        passed = fixed + (places - fixed + rotation * (used - fixed)) % max(1, number_of - fixed)
        return jnp.zeros((number_of,), jnp.int32).at[order[jnp.where(places < fixed, places, passed)]].set(jnp.asarray(tallies, jnp.int32))

    tallies = jnp.where(number % 4 == 0, named(crowded, number // 4), named(ordinary, number - number // 4 - 1))
    mixed = jax.random.permutation(jax.random.fold_in(own, 3), number_of)
    donor, sink = mixed[0:number_of // 2 * 2:2], mixed[1:number_of // 2 * 2:2]
    room = jnp.minimum(tallies[donor] - 1, reach - tallies[sink]) // 2
    room = jnp.where((donor == order[0]) | (sink == order[0]) | (tallies[sink] == 0), 0, jnp.maximum(room, 0))
    passed = jax.random.randint(jax.random.fold_in(own, 4), (number_of // 2,), 0, 1 << 20) % (room + 1)
    tallies = tallies.at[donor].add(-passed).at[sink].add(passed)
    items = jnp.searchsorted(jnp.cumsum(tallies), jnp.arange(rows * top), side="right").astype(jnp.int32)
    table = items.reshape(top, rows).T
    table = table[jax.random.permutation(jax.random.fold_in(own, 1), rows)]
    rotation = jax.random.randint(jax.random.fold_in(own, 2), (rows, 1), 0, top)
    return jnp.take_along_axis(table, (jnp.arange(top)[None, :] + rotation) % top, axis=1)


def load_shares(count, total, bound, lean, full):
    loads = [(1 << 20) // math.isqrt(rank ** lean) + 1 for rank in range(1, count + 1)]
    largest = bound if full else min(bound, max(-(-total // count), total * loads[0] // sum(loads)))
    least = 1 if total - largest >= count - 1 else 0
    holding, surplus = [largest] + [least] * (count - 1), total - largest - least * (count - 1)
    while surplus > 0:
        movable = [i for i in range(1, count) if holding[i] < largest] or [i for i in range(1, count) if holding[i] < bound]
        pool, budget = sum([loads[i] for i in movable]), surplus
        for i in movable:
            extra = min(bound - holding[i], max(1, budget * loads[i] // pool), surplus)
            holding[i] = holding[i] + extra
            surplus = surplus - extra
    return np.array(holding)


def noise(key, dims, spread, bound, shards=(), kind=jnp.bfloat16):
    level = block_scale(key, dims, shards, -0.22, 0.18) if shards else 1.0
    values = jax.random.normal(key, dims, jnp.float32) * spread * level
    return jnp.minimum(jnp.maximum(values, -bound), bound).astype(kind)


def setup_inputs(seed: int = 0) -> dict:
    key_of = jax.random.split(jax.random.key(seed), 14)
    hidden_in = noise(key_of[0], (MICRO, SEQS, LEN, D), 1.0, 6.0, ((1, 4), (2, 4)))
    out_grad = noise(key_of[1], (MICRO, SEQS, LEN, D), 1.0, 6.0, ((1, 4), (2, 4)))
    attn_gain = jnp.clip(1.0 + 0.1 * jax.random.normal(key_of[2], (N_SECTION, D), jnp.float32), 0.5, 1.5).astype(jnp.bfloat16)
    ffn_gain = jnp.clip(1.0 + 0.1 * jax.random.normal(key_of[3], (N_SECTION, D), jnp.float32), 0.5, 1.5).astype(jnp.bfloat16)
    query_matrix = noise(key_of[4], (N_SECTION, D, HEADS * HEAD_DIM), D ** -0.5, 0.15625, ((0, 2), (1, 16)))
    key_matrix = noise(key_of[5], (N_SECTION, D, KV_HEADS * HEAD_DIM), D ** -0.5, 0.15625, ((0, 2), (1, 16)))
    value_matrix = noise(key_of[6], (N_SECTION, D, KV_HEADS * HEAD_DIM), D ** -0.5, 0.15625, ((0, 2), (1, 16)))
    output_matrix = noise(key_of[7], (N_SECTION, HEADS * HEAD_DIM, D), (max(D // 256, 4)) ** -0.5, 2.5, ((0, 2), (1, 16)))
    router_matrix = noise(key_of[8], (N_SECTION, D, EXPERTS), 0.0128, 0.079589844, ((0, 2), (1, 16)))
    w_gate = noise(key_of[9], (N_SECTION, EXPERTS, D, FF), D ** -0.5, 0.15625, ((0, 2), (1, 4)))
    w_up = noise(key_of[10], (N_SECTION, EXPERTS, D, FF), D ** -0.5, 0.15625, ((0, 2), (1, 4)))
    w_down = noise(key_of[11], (N_SECTION, EXPERTS, FF, D), (FF // 16) ** -0.5, 1.0, ((0, 2), (1, 4)))
    routes_keys = jax.random.split(jax.random.fold_in(key_of[12], 1), N_SECTION * MICRO * SEQS * LEN // SLICE)
    routes_turns = jax.random.permutation(jax.random.fold_in(key_of[12], 3), N_SECTION * MICRO * SEQS * LEN // SLICE)
    routes = jax.vmap(lambda own, number: routed_block(jax.random.fold_in(key_of[12], 2), own, number, SLICE, EXPERTS, TOP_K, CAP, 0))(routes_keys, routes_turns).reshape((N_SECTION, MICRO, SEQS, LEN, TOP_K))
    return dict(hidden_in=hidden_in, out_grad=out_grad, attn_gain=attn_gain, ffn_gain=ffn_gain, query_matrix=query_matrix, key_matrix=key_matrix, value_matrix=value_matrix, output_matrix=output_matrix, router_matrix=router_matrix, w_gate=w_gate, w_up=w_up, w_down=w_down, routes=routes)


@jax.custom_vjp
def low(v):
    return lax.optimization_barrier(v.astype(jnp.bfloat16)).astype(jnp.float32)

@jax.custom_vjp
def low_back(v):
    return v

def low_keep(v):
    return (low(v), None)

def low_pass(kept, grad):
    return (grad,)

def back_keep(v):
    return (v, None)

def back_low(kept, grad):
    return (low(grad),)
low.defvjp(low_keep, low_pass)
low_back.defvjp(back_keep, back_low)
epsilon = 1e-06
highest_precision = lax.Precision.HIGHEST

def rms_norm(values, norm_gain):
    return values * lax.rsqrt(lax.optimization_barrier(jnp.mean(values * values, axis=-1, keepdims=True)) + epsilon) * norm_gain

def rotary_tables(length):
    half_dim = HEAD_DIM // 2
    frequency = 10000.0 ** (-jnp.arange(half_dim, dtype=jnp.float32) * 2.0 / HEAD_DIM)
    angles = jnp.arange(length, dtype=jnp.float32)[:, None] * frequency[None, :]
    return (jnp.cos(angles)[:, None, :], jnp.sin(angles)[:, None, :])

def rotate(values, cos_table, sin_table):
    length = values.shape[0]
    split_heads = values.reshape(length, -1, HEAD_DIM)
    first_half = split_heads[..., :HEAD_DIM // 2]
    second_half = split_heads[..., HEAD_DIM // 2:]
    turned = jnp.concatenate([first_half * cos_table - second_half * sin_table, second_half * cos_table + first_half * sin_table], axis=-1)
    return turned.reshape(length, -1)

def slot_index(route):
    flat_route = route.reshape(-1).astype(jnp.int32)
    one_hot = (flat_route[:, None] == jnp.arange(EXPERTS, dtype=jnp.int32)[None, :]).astype(jnp.int32)
    position = lax.optimization_barrier(jnp.sum((jnp.cumsum(one_hot, axis=0) - 1) * one_hot, axis=1))
    return (flat_route * CAP + position).astype(jnp.int32)

def attend_sequence(block_item):
    query_rows, key, value_rows = block_item
    length = query_rows.shape[0]
    cos_table, sin_table = rotary_tables(length)
    query_rows = low(rotate(query_rows, cos_table, sin_table)).reshape(length, KV_HEADS, HEADS // KV_HEADS, HEAD_DIM)
    key = low(rotate(key, cos_table, sin_table)).reshape(length, KV_HEADS, HEAD_DIM)
    value_rows = value_rows.reshape(length, KV_HEADS, HEAD_DIM)
    scores = low_back(jnp.einsum('qhgd,khd->hgqk', query_rows, key, precision=highest_precision) * 0.125)
    causal = jnp.arange(length)[:, None] >= jnp.arange(length)[None, :]
    scores = jnp.where(causal, scores, -jnp.inf)
    probs_low = low(jax.nn.softmax(scores, axis=-1))
    attended = jnp.einsum('hgqk,khd->qhgd', probs_low, value_rows, precision=highest_precision)
    return low(low_back(attended.reshape(length, HEADS * HEAD_DIM)))

def layer(hidden_state, params, routes):
    attn_gain, ffn_gain, query_matrix, key_matrix, value_matrix, output_matrix, router_matrix, w_gate, w_up, w_down = params
    seq_count, length, width = hidden_state.shape
    normed_input = low(rms_norm(hidden_state, attn_gain))
    query_rows = low(low_back(jnp.einsum('ork,km->orm', normed_input, query_matrix, precision=highest_precision)))
    key = low(low_back(jnp.einsum('ork,km->orm', normed_input, key_matrix, precision=highest_precision)))
    value_rows = low(low_back(jnp.einsum('ork,km->orm', normed_input, value_matrix, precision=highest_precision)))
    mixed_output = lax.map(jax.checkpoint(attend_sequence), (query_rows, key, value_rows))
    after_update = hidden_state + low_back(jnp.einsum('ixv,vg->ixg', mixed_output, output_matrix, precision=highest_precision))
    normed_feedforward = low(rms_norm(after_update, ffn_gain))
    router_logits = low_back(jnp.einsum('yra,an->yrn', normed_feedforward, router_matrix, precision=highest_precision))
    gates = jax.nn.softmax(jnp.take_along_axis(router_logits, routes, axis=-1), axis=-1)

    def expert_block(block_item):
        block_rows, block_route = block_item
        slots = slot_index(block_route)
        copies = jnp.repeat(block_rows, TOP_K, axis=0)
        buffer = jnp.zeros((EXPERTS * CAP, width), block_rows.dtype).at[slots].set(copies)
        buffer = low_back(buffer).reshape(EXPERTS, CAP, width)
        gate_pre = low_back(jnp.einsum('ecd,edf->ecf', buffer, w_gate, precision=highest_precision))
        up_pre = low_back(jnp.einsum('ecd,edf->ecf', buffer, w_up, precision=highest_precision))
        hidden_act = low(jax.nn.silu(gate_pre) * up_pre)
        result = low(low_back(jnp.einsum('ecf,efd->ecd', hidden_act, w_down, precision=highest_precision)))
        return result.reshape(EXPERTS * CAP, width)[slots].reshape(SLICE, TOP_K, width)
    blocks = normed_feedforward.reshape(-1, SLICE, width)
    block_routes = routes.reshape(-1, SLICE, TOP_K)
    picked = lax.map(jax.checkpoint(expert_block), (blocks, block_routes))
    picked = picked.reshape(seq_count, length, TOP_K, width)
    return after_update + lax.optimization_barrier(jnp.sum(gates[..., None] * picked, axis=2))

def reference(hidden_in, out_grad, attn_gain, ffn_gain, query_matrix, key_matrix, value_matrix, output_matrix, router_matrix, w_gate, w_up, w_down, routes):
    weights = (attn_gain, ffn_gain, query_matrix, key_matrix, value_matrix, output_matrix, router_matrix, w_gate, w_up, w_down)
    first_params = tuple((weight[0].astype(jnp.float32) for weight in weights))
    second_params = tuple((weight[1].astype(jnp.float32) for weight in weights))
    batch = hidden_in.shape[0] * hidden_in.shape[1]
    start = hidden_in.astype(jnp.float32).reshape(batch, LEN, D)
    route_all = routes.reshape(2, batch, LEN, TOP_K).astype(jnp.int32)
    middle, first_back = jax.vjp(partial(layer, routes=route_all[0]), start, first_params)
    final, second_back = jax.vjp(partial(layer, routes=route_all[1]), middle, second_params)
    top_grad = out_grad.astype(jnp.float32).reshape(batch, LEN, D)
    middle_grad, second_grads = second_back(top_grad)
    start_grad, first_grads = first_back(middle_grad)
    full_shape = (2, MICRO, SEQS, LEN, D)
    layer_outs = jnp.stack([middle, final]).reshape(full_shape)
    section_grads = jnp.stack([start_grad, middle_grad]).reshape(full_shape)
    stacked = [jnp.stack([first_grads[number], second_grads[number]]) for number in range(10)]
    return (layer_outs, section_grads, stacked[0], stacked[1], stacked[2], stacked[3], stacked[4], stacked[5], stacked[6], stacked[7], stacked[8], stacked[9])
```

```python
from functools import partial

import jax
import jax.numpy as jnp
from jax import lax
from jax.sharding import PartitionSpec as P

HEADS = 24
KV_HEADS = 8
HEAD_DIM = 64
TOP_K = 8
EXPERTS = 32
CAP = 80
GROUP = HEADS // KV_HEADS
TOKENS = ("dp", "seq")

epsilon = 1e-06


def dot(a, b):
    return jnp.dot(a, b, preferred_element_type=jnp.float32)


def dot_t(a, b):
    return lax.dot_general(a, b, (((1,), (1,)), ((), ())), preferred_element_type=jnp.float32)


def t_dot(a, b):
    return lax.dot_general(a, b, (((0,), (0,)), ((), ())), preferred_element_type=jnp.float32)


def low(v):
    return v.astype(jnp.bfloat16)


def swap(block):
    return lax.ppermute(block, "section", [(0, 1), (1, 0)])


def pass_to(block, section):
    return lax.ppermute(block, "section", [(1 - section, section)])


def rms_norm(values, norm_gain):
    return (
        values * lax.rsqrt(jnp.mean(values * values, axis=-1, keepdims=True) + epsilon) * norm_gain
    )


def rotary_tables(length):
    half_dim = HEAD_DIM // 2
    frequency = 10000.0 ** (-jnp.arange(half_dim, dtype=jnp.float32) * 2.0 / HEAD_DIM)
    angles = jnp.arange(length, dtype=jnp.float32)[:, None] * frequency[None, :]
    return (jnp.cos(angles)[:, None, :], jnp.sin(angles)[:, None, :])


def rotate(values, cos_table, sin_table):
    length = values.shape[0]
    split_heads = values.reshape(length, -1, HEAD_DIM)
    first_half = split_heads[..., : HEAD_DIM // 2]
    second_half = split_heads[..., HEAD_DIM // 2 :]
    turned = jnp.concatenate(
        [
            first_half * cos_table - second_half * sin_table,
            second_half * cos_table + first_half * sin_table,
        ],
        axis=-1,
    )
    return turned.reshape(length, -1)


def attention_forward(q_heads, k_heads, v_heads):
    length = q_heads.shape[0]
    local_kv = k_heads.shape[1] // HEAD_DIM
    cos_table, sin_table = rotary_tables(length)
    q_rot = low(rotate(q_heads.astype(jnp.float32), cos_table, sin_table)).reshape(
        length, local_kv, GROUP, HEAD_DIM
    )
    k_rot = low(rotate(k_heads.astype(jnp.float32), cos_table, sin_table)).reshape(
        length, local_kv, HEAD_DIM
    )
    values = v_heads.reshape(length, local_kv, HEAD_DIM)
    block_rows = min(512, length)
    outputs = []
    totals_list = []
    for first_row in range(0, length, block_rows):
        key_end = first_row + block_rows
        scores = (
            jnp.einsum(
                "qhgd,khd->hgqk",
                q_rot[first_row:key_end],
                k_rot[:key_end],
                preferred_element_type=jnp.float32,
            )
            * 0.125
        )
        causal = (first_row + jnp.arange(block_rows, dtype=jnp.int32))[:, None] >= jnp.arange(
            key_end, dtype=jnp.int32
        )[None, :]
        scores = jnp.where(causal, scores, -jnp.inf)
        row_peak = jnp.max(scores, axis=-1, keepdims=True)
        exponents = jnp.exp(scores - row_peak)
        totals = jnp.sum(exponents, axis=-1, keepdims=True)
        attended = jnp.einsum(
            "hgqk,khd->qhgd",
            low(exponents / totals),
            values[:key_end],
            preferred_element_type=jnp.float32,
        )
        outputs.append(low(attended).reshape(block_rows, -1))
        totals_list.append((row_peak + jnp.log(totals))[..., 0])
    return (jnp.concatenate(outputs, axis=0), jnp.stack(totals_list), q_rot, k_rot, values)


def attention_backward(head_grad, q_rot, k_rot, values, log_total):
    length, local_kv = q_rot.shape[:2]
    cos_table, sin_table = rotary_tables(length)
    block_rows = min(512, length)
    grad_rows = head_grad.reshape(length, local_kv, GROUP, HEAD_DIM)
    key_acc = jnp.zeros((length, local_kv, HEAD_DIM), jnp.float32)
    value_acc = jnp.zeros((length, local_kv, HEAD_DIM), jnp.float32)
    query_parts = []
    for block_number, first_row in enumerate(range(0, length, block_rows)):
        key_end = first_row + block_rows
        q_block = q_rot[first_row:key_end]
        grad_block = grad_rows[first_row:key_end]
        key_part = k_rot[:key_end]
        scores = (
            jnp.einsum("qhgd,khd->hgqk", q_block, key_part, preferred_element_type=jnp.float32)
            * 0.125
        )
        causal = (first_row + jnp.arange(block_rows, dtype=jnp.int32))[:, None] >= jnp.arange(
            key_end, dtype=jnp.int32
        )[None, :]
        scores = jnp.where(causal, scores, -jnp.inf)
        probs_full = jnp.exp(scores - log_total[block_number][..., None])
        prob_grad = jnp.einsum(
            "qhgd,khd->hgqk", grad_block, values[:key_end], preferred_element_type=jnp.float32
        )
        score_grad = probs_full * (
            prob_grad - jnp.sum(probs_full * prob_grad, axis=-1, keepdims=True)
        )
        score_low = low(score_grad)
        query_parts.append(
            jnp.einsum("hgqk,khd->qhgd", score_low, key_part, preferred_element_type=jnp.float32)
            * 0.125
        )
        key_acc = key_acc.at[:key_end].add(
            jnp.einsum("hgqk,qhgd->khd", score_low, q_block, preferred_element_type=jnp.float32)
            * 0.125
        )
        value_acc = value_acc.at[:key_end].add(
            jnp.einsum(
                "hgqk,qhgd->khd", low(probs_full), grad_block, preferred_element_type=jnp.float32
            )
        )
    query_all = jnp.concatenate(query_parts, axis=0).reshape(length, -1)
    query_grad = rotate(query_all, cos_table, -sin_table)
    key_grad = rotate(key_acc.reshape(length, -1), cos_table, -sin_table)
    return jnp.concatenate(
        [low(query_grad), low(key_grad), low(value_acc).reshape(length, -1)], axis=1
    )


def token_choice(route):
    return route[..., None] == jnp.arange(EXPERTS, dtype=jnp.int32)


def routing(route_all, first_expert, count):
    chosen = jnp.any(token_choice(route_all), axis=2)
    mine = lax.dynamic_slice_in_dim(chosen, first_expert, count, axis=2)
    rows = mine.shape[1]
    earlier = jnp.tril(jnp.ones((rows, rows), jnp.bfloat16), -1)
    place = jnp.einsum(
        "ts,bsj->bjt", earlier, mine.astype(jnp.bfloat16), preferred_element_type=jnp.float32
    ).astype(jnp.int32)
    mine = jnp.transpose(mine, (0, 2, 1))
    slots = jnp.arange(CAP, dtype=jnp.int32)
    pick = (place[:, :, None, :] == slots[None, None, :, None]) & mine[:, :, None, :]
    return chosen, pick


def choose(pick, rows):
    picked = jnp.einsum("bct,btd->bcd", low(pick), rows, preferred_element_type=jnp.float32)
    return low(picked).reshape(-1, rows.shape[-1])


def give_back(picks, slot_rows):
    total = 0.0
    for pick, rows in zip(picks, slot_rows):
        blocks, count = pick.shape[:2]
        total = total + jnp.einsum(
            "bct,bcd->btd",
            low(pick),
            rows.reshape(blocks, count, -1),
            preferred_element_type=jnp.float32,
        )
    return total.reshape(-1, total.shape[-1])


def slot_values(pick, values):
    return jnp.sum(jnp.where(pick, values[:, None, :], 0.0), axis=2).reshape(-1, 1)


def forward_layer(layer_in, route_all, weights, experts, first_expert):
    attn_scale, ffn_scale, qkv_w, out_w, router_w = weights
    gate_w, up_w, down_w = experts
    count = gate_w.shape[0]
    normed_input = low(rms_norm(layer_in, attn_scale))
    normed_all = lax.all_gather(normed_input, "seq", axis=0, tiled=True)
    qkv = low(dot(normed_all, qkv_w))
    kv_width = KV_HEADS * HEAD_DIM // lax.axis_size("seq")
    q_width = GROUP * kv_width
    mixed, log_total, q_rot, k_rot, v_heads = attention_forward(
        qkv[:, :q_width], qkv[:, q_width : q_width + kv_width], qkv[:, q_width + kv_width :]
    )
    branch = lax.psum_scatter(low(dot(mixed, out_w)), "seq", scatter_dimension=0, tiled=True)
    after_update = layer_in + branch.astype(jnp.float32)
    normed_ffn = low(rms_norm(after_update, ffn_scale))
    ffn_all = lax.all_gather(normed_ffn, TOKENS, axis=0, tiled=True)
    chosen, pick = routing(route_all, first_expert, count)
    blocks, rows = chosen.shape[:2]
    logits = dot(ffn_all, router_w).reshape(blocks, rows, EXPERTS)
    logits = jnp.where(chosen, logits, -jnp.inf)
    gates = jax.nn.softmax(logits, axis=-1)
    mine = jnp.transpose(
        lax.dynamic_slice_in_dim(gates, first_expert, count, axis=2), (0, 2, 1)
    )
    ffn_blocks = ffn_all.reshape(blocks, rows, -1)
    results = []
    saved_experts = []
    for j in range(count):
        slot_rows = choose(pick[:, j], ffn_blocks)
        slot_gates = slot_values(pick[:, j], mine[:, j])
        gate_pre = dot(slot_rows, gate_w[j])
        up_pre = dot(slot_rows, up_w[j])
        hidden = jax.nn.silu(gate_pre) * up_pre
        scaled = low(slot_gates * hidden)
        results.append(low(dot(scaled, down_w[j])))
        saved_experts.append((slot_rows, slot_gates, gate_pre, up_pre, scaled))
    moe = give_back([pick[:, j] for j in range(count)], results)
    moe = lax.psum_scatter(low(moe), TOKENS, scatter_dimension=0, tiled=True)
    layer_out = after_update + moe.astype(jnp.float32)
    own_block = lax.axis_index("dp") * lax.axis_size("seq") + lax.axis_index("seq")
    own_gates = lax.dynamic_index_in_dim(gates, own_block, 0, keepdims=False)
    saved = (
        layer_in,
        normed_all,
        q_rot,
        k_rot,
        v_heads,
        log_total,
        mixed,
        after_update,
        normed_ffn,
        own_gates,
        pick,
        saved_experts,
    )
    return (layer_out, saved)


def backward_layer(layer_grad, saved, weights, experts):
    attn_scale, ffn_scale, qkv_w, out_w, router_w = weights
    gate_w, up_w, down_w = experts
    count = gate_w.shape[0]
    (
        layer_in,
        normed_all,
        q_rot,
        k_rot,
        v_heads,
        log_total,
        mixed,
        after_update,
        normed_ffn,
        own_gates,
        pick,
        saved_experts,
    ) = saved
    blocks, _, _, rows = pick.shape
    grad_all = lax.all_gather(low(layer_grad), TOKENS, axis=0, tiled=True)
    grad_blocks = grad_all.reshape(blocks, rows, -1)
    input_rows = []
    gate_terms = []
    expert_grads = ([], [], [])
    for j in range(count):
        slot_rows, slot_gates, gate_pre, up_pre, scaled = saved_experts[j]
        slot_grads = choose(pick[:, j], grad_blocks)
        plain_grad = dot_t(slot_grads, down_w[j])
        sigmoid = jax.nn.sigmoid(gate_pre)
        activated = gate_pre * sigmoid
        gate_term = jnp.sum(plain_grad * (activated * up_pre), axis=1).reshape(blocks, 1, -1)
        gate_terms.append(jnp.sum(jnp.where(pick[:, j], gate_term.reshape(blocks, -1, 1), 0.0), 1))
        hidden_grad = slot_gates * plain_grad
        gate_low = low(hidden_grad * up_pre * sigmoid * (1.0 + gate_pre * (1.0 - sigmoid)))
        up_low = low(hidden_grad * activated)
        input_rows.append(low(dot_t(gate_low, gate_w[j]) + dot_t(up_low, up_w[j])))
        expert_grads[0].append(low(t_dot(slot_rows, gate_low)))
        expert_grads[1].append(low(t_dot(slot_rows, up_low)))
        expert_grads[2].append(low(t_dot(scaled, slot_grads)))
    expert_grads = tuple(jnp.stack(parts) for parts in expert_grads)
    normed_grad = give_back([pick[:, j] for j in range(count)], input_rows)
    normed_grad = lax.psum_scatter(low(normed_grad), TOKENS, scatter_dimension=0, tiled=True)
    gate_terms = jnp.stack(gate_terms, axis=1)
    gate_terms = lax.all_to_all(gate_terms, TOKENS, split_axis=0, concat_axis=0, tiled=True)
    split = EXPERTS // (blocks * count) if blocks * count < EXPERTS else 1
    gate_terms = gate_terms.reshape(-1, rows)
    if gate_terms.shape[0] > EXPERTS:
        gate_terms = jnp.sum(gate_terms.reshape(EXPERTS, -1, rows), axis=1)
    gate_terms = gate_terms.T
    logit_grad = low(
        own_gates * (gate_terms - jnp.sum(own_gates * gate_terms, axis=-1, keepdims=True))
    )
    router_grad = t_dot(normed_ffn, logit_grad)
    normed_grad = normed_grad.astype(jnp.float32) + dot_t(logit_grad, router_w)
    after_part, ffn_gain_grad = jax.vjp(rms_norm, after_update, ffn_scale)[1](normed_grad)
    after_grad = after_part + layer_grad
    branch_all = lax.all_gather(low(after_grad), "seq", axis=0, tiled=True)
    out_grad = t_dot(mixed, branch_all)
    head_grad = low(dot_t(branch_all, out_w))
    qkv_grad = attention_backward(head_grad, q_rot, k_rot, v_heads, log_total)
    qkv_weight_grad = t_dot(normed_all, qkv_grad)
    normed_attn = low(dot_t(qkv_grad, qkv_w))
    normed_attn = lax.psum_scatter(normed_attn, "seq", scatter_dimension=0, tiled=True)
    input_part, attn_gain_grad = jax.vjp(rms_norm, layer_in, attn_scale)[1](
        normed_attn.astype(jnp.float32)
    )
    small_grads = jnp.concatenate(
        [router_grad, attn_gain_grad[:, None], ffn_gain_grad[:, None]], axis=1
    )
    return (input_part + after_grad, qkv_weight_grad, out_grad, small_grads, expert_grads)


def body(
    hidden_in,
    out_grad,
    attn_gain,
    ffn_gain,
    query_matrix,
    key_matrix,
    value_matrix,
    output_matrix,
    router_matrix,
    w_gate,
    w_up,
    w_down,
    routes,
):
    section = lax.axis_index("section")
    dp, seq = lax.axis_size("dp"), lax.axis_size("seq")
    seq_index = lax.axis_index("seq")
    first = section == 0
    slice_len = hidden_in.shape[2]
    width = hidden_in.shape[3]
    depth = query_matrix.shape[1]

    def by_layer(own, other):
        return [jnp.where(first, own, other), jnp.where(first, other, own)]

    layer_in = lax.dynamic_index_in_dim(hidden_in, section, 0, keepdims=False)[0]
    top_grad = lax.dynamic_index_in_dim(out_grad, section, 0, keepdims=False)[0]
    own_routes = lax.dynamic_index_in_dim(routes[0], section, 0, keepdims=False)[0]
    other_routes = lax.dynamic_index_in_dim(routes[0], 1 - section, 0, keepdims=False)[0]
    layer_routes = jnp.stack(by_layer(own_routes, swap(other_routes)))
    routes_all = lax.all_gather(layer_routes, TOKENS, axis=0, tiled=False)

    small = jnp.concatenate([router_matrix[0], attn_gain[0][:, None], ffn_gain[0][:, None]], axis=1)
    small = lax.all_gather(small, ("section", "dp", "seq"), axis=0, tiled=True)
    small = small.reshape(2, width, -1)
    by_group = jnp.concatenate(
        [
            matrix[0].reshape(depth, seq, -1)
            for matrix in (query_matrix, key_matrix, value_matrix)
        ],
        axis=2,
    )
    qkv_layers = []
    for part in by_layer(by_group, swap(by_group)):
        part = lax.all_to_all(part, "seq", split_axis=1, concat_axis=0, tiled=True)
        part = part.reshape(seq * depth, -1)
        qkv_layers.append(lax.all_gather(part, "dp", axis=0, tiled=True))
    devices = [(d, s) for d in range(dp) for s in range(seq)]
    to_group = []
    for flat in range(dp * seq):
        to_group.append((flat, (flat % dp) * seq + flat // dp))
    from_group = [(target, source) for source, target in to_group]
    grouped_out = lax.ppermute(output_matrix[0], TOKENS, to_group)
    out_layers = []
    for part in by_layer(grouped_out, swap(grouped_out)):
        out_layers.append(lax.all_gather(part, "dp", axis=0, tiled=True))

    local = w_gate.shape[1]
    hidden_units = w_gate.shape[3]
    if local >= seq:
        count, units = local // seq, hidden_units
        start, unit_start = seq_index * count, 0
    else:
        count, units = 1, hidden_units * local // seq
        start, unit_start = seq_index * local // seq, (seq_index % (seq // local)) * units
    first_expert = lax.axis_index("dp") * local + start
    own_experts = (
        lax.dynamic_slice(w_gate[0], (start, 0, unit_start), (count, width, units)),
        lax.dynamic_slice(w_up[0], (start, 0, unit_start), (count, width, units)),
        lax.dynamic_slice(w_down[0], (start, unit_start, 0), (count, units, width)),
    )
    expert_layers = list(zip(*[by_layer(own, swap(own)) for own in own_experts]))
    weights = []
    for number in range(2):
        weights.append(
            (
                small[number, :, EXPERTS].astype(jnp.float32),
                small[number, :, EXPERTS + 1].astype(jnp.float32),
                qkv_layers[number],
                out_layers[number],
                small[number, :, :EXPERTS],
            )
        )

    state = layer_in.astype(jnp.float32)
    layer_states = []
    saved_layers = []
    for number in range(2):
        state, saved = forward_layer(
            state, routes_all[:, number], weights[number], expert_layers[number], first_expert
        )
        layer_states.append(state)
        saved_layers.append(saved)
    grad = top_grad.astype(jnp.float32)
    layer_grads = [None, None]
    weight_grads = [None, None]
    for number in (1, 0):
        grad, *weight_grads[number] = backward_layer(
            grad, saved_layers[number], weights[number], expert_layers[number]
        )
        layer_grads[number] = grad

    def to_section(pieces):
        received = [pass_to(pieces[number], number) for number in range(2)]
        own = jnp.where(first, pieces[0], pieces[1])
        other = jnp.where(first, received[0], received[1])
        return jnp.stack(by_layer(own, other))[None, :, None]

    def summed(pieces):
        received = [pass_to(pieces[number], number) for number in range(2)]
        own = jnp.where(first, pieces[0], pieces[1]).astype(jnp.float32)
        return own + jnp.where(first, received[0], received[1]).astype(jnp.float32)

    def scatter_rows(part):
        part = lax.psum_scatter(low(part), "dp", scatter_dimension=0, tiled=True)
        return part

    qkv_parts = []
    out_parts = []
    small_parts = []
    for number in range(2):
        qkv_part, out_part, small_part, _ = weight_grads[number]
        qkv_part = scatter_rows(qkv_part).reshape(seq, depth, -1)
        qkv_part = lax.all_to_all(qkv_part, "seq", split_axis=0, concat_axis=0, tiled=True)
        qkv_parts.append(qkv_part)
        out_parts.append(lax.ppermute(scatter_rows(out_part), TOKENS, from_group))
        small_parts.append(
            lax.psum_scatter(small_part, TOKENS, scatter_dimension=0, tiled=True)
        )
    qkv_sum = summed(qkv_parts)
    out_sum = summed(out_parts)
    small_sum = summed(small_parts)
    kv_width = KV_HEADS * HEAD_DIM // seq
    q_width = GROUP * kv_width

    def columns(begin, end):
        return jnp.transpose(qkv_sum[:, :, begin:end], (1, 0, 2)).reshape(depth, -1)[None]

    expert_sums = []
    for kind in range(3):
        pieces = []
        for number in range(2):
            piece = weight_grads[number][3][kind]
            if local >= seq:
                piece = lax.all_to_all(piece, "seq", split_axis=1, concat_axis=0, tiled=True)
            else:
                share = seq // local
                if kind < 2:
                    piece = piece.reshape(seq, width // seq, units)
                    piece = lax.all_to_all(piece, "seq", split_axis=0, concat_axis=0, tiled=True)
                    piece = piece.reshape(local, share, width // seq, units)
                    piece = jnp.transpose(piece, (0, 2, 1, 3)).reshape(local, width // seq, -1)
                else:
                    rows = hidden_units // seq
                    piece = piece.reshape(-1, rows, width)
                    piece = whole_rows(piece, seq_index, share, seq)
            pieces.append(piece)
        expert_sums.append(summed(pieces)[None])
    return (
        to_section(layer_states),
        to_section(layer_grads),
        small_sum[:, EXPERTS][None],
        small_sum[:, EXPERTS + 1][None],
        columns(0, q_width),
        columns(q_width, q_width + kv_width),
        columns(q_width + kv_width, q_width + 2 * kv_width),
        out_sum[None],
        small_sum[:, :EXPERTS][None],
        *expert_sums,
    )


def whole_rows(piece, seq_index, share, seq):
    parts = piece.shape[0]
    spread = jnp.zeros((seq,) + piece.shape[1:], piece.dtype)
    spread = lax.dynamic_update_slice_in_dim(
        spread, piece, (seq_index % share) * parts, axis=0
    )
    spread = lax.all_to_all(spread, "seq", split_axis=0, concat_axis=0, tiled=True)
    spread = spread.reshape((-1, share) + piece.shape[1:])
    return jnp.sum(spread.astype(jnp.float32), axis=1).astype(piece.dtype)


def solution(mesh):
    return jax.shard_map(
        body,
        mesh=mesh,
        in_specs=(
            P(None, "dp", "seq", None),
            P(None, "dp", "seq", None),
            P("section", ("dp", "seq")),
            P("section", ("dp", "seq")),
            P("section", ("dp", "seq"), None),
            P("section", ("dp", "seq"), None),
            P("section", ("dp", "seq"), None),
            P("section", ("dp", "seq"), None),
            P("section", ("dp", "seq"), None),
            P("section", "dp", None, None),
            P("section", "dp", None, None),
            P("section", "dp", None, None),
            P("section", None, "dp", "seq", None),
        ),
        out_specs=(
            P("section", None, "dp", "seq", None),
            P("section", None, "dp", "seq", None),
            P("section", ("dp", "seq")),
            P("section", ("dp", "seq")),
            P("section", ("dp", "seq"), None),
            P("section", ("dp", "seq"), None),
            P("section", ("dp", "seq"), None),
            P("section", ("dp", "seq"), None),
            P("section", ("dp", "seq"), None),
            P("section", "dp", "seq", None),
            P("section", "dp", "seq", None),
            P("section", "dp", "seq", None),
        ),
        check_vma=False,
    )
```

```python
from functools import partial

import jax
import jax.numpy as jnp
from jax import lax
from jax.experimental import pallas as pl
from jax.experimental.pallas import tpu as pltpu
from jax.sharding import PartitionSpec as P

HEADS = 24
KV_HEADS = 8
HEAD_DIM = 64
TOP_K = 8
EXPERTS = 32
CAP = 80
GROUP = HEADS // KV_HEADS
TOKENS = ("dp", "seq")

epsilon = 1e-06


def dot(a, b):
    return jnp.dot(a, b, preferred_element_type=jnp.float32)


def dot_t(a, b):
    return lax.dot_general(a, b, (((1,), (1,)), ((), ())), preferred_element_type=jnp.float32)


def t_dot(a, b):
    return lax.dot_general(a, b, (((0,), (0,)), ((), ())), preferred_element_type=jnp.float32)


def low(v):
    return v.astype(jnp.bfloat16)


def swap(block):
    return lax.ppermute(block, "section", [(0, 1), (1, 0)])


def pass_to(block, section):
    return lax.ppermute(block, "section", [(1 - section, section)])


MESH = pl.DeviceIdType.MESH

def rdma(src, dst, ssem, rsem, **dev):
    return pltpu.make_async_remote_copy(src_ref=src, dst_ref=dst, send_sem=ssem, recv_sem=rsem, device_id=dev, device_id_type=MESH)

def greet(d, s, last):
    barrier = pltpu.get_barrier_semaphore()
    def sig(**dev):
        pl.semaphore_signal(barrier, inc=1, device_id=dev, device_id_type=MESH)
    sig(seq=s ^ 1)
    sig(seq=s ^ 2)
    @pl.when(d > 0)
    def _(): sig(dp=d - 1)
    @pl.when(d < last)
    def _(): sig(dp=d + 1)
    inner = (d > 0) & (d < last)
    @pl.when(inner)
    def _(): pl.semaphore_wait(barrier, 4)
    @pl.when(jnp.logical_not(inner))
    def _(): pl.semaphore_wait(barrier, 3)

def ag_kernel(x_ref, out_ref, lsem, zs, zr, ys, yr, cs, cr):
    d, s = lax.axis_index("dp"), lax.axis_index("seq")
    last = 3
    greet(d, s, last)
    def blk(z, sq): return out_ref.at[z * 4 + sq]
    own = pltpu.make_async_copy(x_ref, blk(d, s), lsem)
    own.start()
    def zc(src, z, right):
        return rdma(src, blk(z, s), zs.at[int(right), z], zr.at[z], dp=(d + 1 if right else d - 1))
    def yc(src, z): return rdma(src, blk(z, s), ys.at[z], yr.at[z], seq=s ^ 2)
    def cc(src, z, y):
        sq = s ^ 2 if y else s
        return rdma(src, blk(z, sq), cs.at[z, y], cr.at[z, y], seq=s ^ 1)
    def send(src, z):
        @pl.when((z <= d) & (d < last))
        def _(): zc(src, z, True).start()
        @pl.when((z >= d) & (d > 0))
        def _(): zc(src, z, False).start()
        yc(src, z).start()
        cc(src, z, 0).start()
    send(x_ref, d)
    for h in (1, 2, 3):
        for side in (-1, 1):
            z = d + side * h
            @pl.when((z >= 0) & (z <= last))
            def _():
                rdma(blk(z, s), blk(z, s), zs.at[0, z], zr.at[z], dp=d).wait_recv()
                send(blk(z, s), z)
    for h in (0, 1, 2, 3):
        for side in ((-1, 1) if h else (1,)):
            z = d + side * h
            @pl.when((z >= 0) & (z <= last))
            def _():
                yc(blk(z, s ^ 2), z).wait_recv()
                cc(blk(z, s ^ 2), z, 1).start()
    for z in range(4):
        for y in range(2):
            sq = (s ^ 1) ^ (2 * y)
            cc(blk(z, sq), z, y).wait_recv()
    for z in range(4):
        @pl.when((z <= d) & (d < last))
        def _(): zc(blk(z, s), z, True).wait_send()
        @pl.when((z >= d) & (d > 0))
        def _(): zc(blk(z, s), z, False).wait_send()
        yc(blk(z, s), z).wait_send()
        cc(blk(z, s), z, 0).wait_send()
        cc(blk(z, s), z, 1).wait_send()
    own.wait()

def ag16(x, space=pl.ANY, cid=0):
    D=pltpu.SemaphoreType.DMA
    return pl.pallas_call(ag_kernel,
        out_shape=jax.ShapeDtypeStruct((16,)+x.shape, x.dtype),
        in_specs=[pl.BlockSpec(memory_space=pl.ANY)], out_specs=pl.BlockSpec(memory_space=space),
        scratch_shapes=[D(()), D((2,4)), D((4,)), D((4,)), D((4,)), D((4,2)), D((4,2))],
        compiler_params=pltpu.CompilerParams(collective_id=cid, has_side_effects=True, vmem_limit_bytes=60<<20),
        name="ag16")(x)

def add_into(dst, a, b, rows, step=16):
    @pl.loop(0, rows // step)
    def _(i):
        r = pl.ds(i * step, step)
        dst[r, :] = (a[r, :].astype(jnp.float32) + b[r, :].astype(jnp.float32)).astype(dst.dtype)

def rs_kernel(p_ref, out_ref, own, cbuf, ybuf, zbuf, ls, zs, zr, ys, yr, cs, cr):
    d, s = lax.axis_index("dp"), lax.axis_index("seq")
    last = 3
    greet(d, s, last)
    rows = p_ref.shape[1]
    def cc(z, yy):
        return rdma(p_ref.at[z * 4 + ((s ^ 1) ^ (2 * yy))], cbuf.at[z, yy], cs.at[z, yy], cr.at[z, yy], seq=s ^ 1)
    def lc(z, yy):
        return pltpu.make_async_copy(p_ref.at[z * 4 + (s ^ (2 * yy))], own.at[z, yy], ls.at[z, yy])
    def yc(z): return rdma(own.at[z, 1], ybuf.at[z], ys.at[z], yr.at[z], seq=s ^ 2)
    def zc(z, right): return rdma(own.at[z, 0], zbuf.at[int(right), z], zs.at[z], zr.at[int(right), z], dp=(d + 1 if right else d - 1))
    for yy in (1, 0):
        for i in range(4):
            z = d ^ (3 - i)
            cc(z, yy).start()
            lc(z, yy).start()
    for i in range(4):
        z = d ^ (3 - i)
        lc(z, 1).wait()
        cc(z, 1).wait_recv()
        add_into(own.at[z, 1], own.at[z, 1], cbuf.at[z, 1], rows)
        yc(z).start()
    for i in range(4):
        z = d ^ (3 - i)
        lc(z, 0).wait()
        cc(z, 0).wait_recv()
        add_into(own.at[z, 0], own.at[z, 0], cbuf.at[z, 0], rows)
        yc(z).wait_recv()
        add_into(own.at[z, 0], own.at[z, 0], ybuf.at[z], rows)
        if i < 3:
            @pl.when(z < d)
            def _():
                @pl.when(d < last)
                def _():
                    zc(z, False).wait_recv()
                    add_into(own.at[z, 0], own.at[z, 0], zbuf.at[0, z], rows)
                zc(z, False).start()
            @pl.when(z > d)
            def _():
                @pl.when(d > 0)
                def _():
                    zc(z, True).wait_recv()
                    add_into(own.at[z, 0], own.at[z, 0], zbuf.at[1, z], rows)
                zc(z, True).start()
        else:
            @pl.when(d < last)
            def _():
                zc(d, False).wait_recv()
                add_into(own.at[d, 0], own.at[d, 0], zbuf.at[0, d], rows)
            @pl.when(d > 0)
            def _():
                zc(d, True).wait_recv()
                add_into(own.at[d, 0], own.at[d, 0], zbuf.at[1, d], rows)
            out_ref[...] = own[d, 0]
    for z in range(4):
        cc(z, 0).wait_send(); cc(z, 1).wait_send(); yc(z).wait_send()
        @pl.when(z < d)
        def _(): zc(z, False).wait_send()
        @pl.when(z > d)
        def _(): zc(z, True).wait_send()

def rs16(p, cid=1):
    D=pltpu.SemaphoreType.DMA
    rows, w = p.shape[1:]
    V=lambda *sh: pltpu.VMEM(sh+(rows,w), p.dtype)
    return pl.pallas_call(rs_kernel,
        out_shape=jax.ShapeDtypeStruct((rows,w), p.dtype),
        in_specs=[pl.BlockSpec(memory_space=pl.ANY)], out_specs=pl.BlockSpec(memory_space=pltpu.VMEM),
        scratch_shapes=[V(4,2),V(4,2),V(4),V(2,4), D((4,2)), D((4,)), D((2,4)), D((4,)), D((4,)), D((4,2)), D((4,2))],
        compiler_params=pltpu.CompilerParams(collective_id=cid, has_side_effects=True, vmem_limit_bytes=60<<20),
        name="rs16")(p)


def whole_tokens(block):
    if lax.axis_size("dp") == 4 and lax.axis_size("seq") == 4:
        return ag16(block).reshape(-1, block.shape[1])
    return lax.all_gather(block, TOKENS, axis=0, tiled=True)


def token_sums(partial_sums):
    if lax.axis_size("dp") == 4 and lax.axis_size("seq") == 4:
        return rs16(partial_sums.reshape(16, -1, partial_sums.shape[1]))
    return lax.psum_scatter(partial_sums, TOKENS, scatter_dimension=0, tiled=True)


def rms_norm(values, norm_gain):
    return (
        values * lax.rsqrt(jnp.mean(values * values, axis=-1, keepdims=True) + epsilon) * norm_gain
    )


def rotary_tables(length):
    half_dim = HEAD_DIM // 2
    frequency = 10000.0 ** (-jnp.arange(half_dim, dtype=jnp.float32) * 2.0 / HEAD_DIM)
    angles = jnp.arange(length, dtype=jnp.float32)[:, None] * frequency[None, :]
    return (jnp.cos(angles)[:, None, :], jnp.sin(angles)[:, None, :])


def rotate(values, cos_table, sin_table):
    length = values.shape[0]
    split_heads = values.reshape(length, -1, HEAD_DIM)
    first_half = split_heads[..., : HEAD_DIM // 2]
    second_half = split_heads[..., HEAD_DIM // 2 :]
    turned = jnp.concatenate(
        [
            first_half * cos_table - second_half * sin_table,
            second_half * cos_table + first_half * sin_table,
        ],
        axis=-1,
    )
    return turned.reshape(length, -1)


def attention_forward(q_heads, k_heads, v_heads):
    length = q_heads.shape[0]
    local_kv = k_heads.shape[1] // HEAD_DIM
    cos_table, sin_table = rotary_tables(length)
    q_rot = low(rotate(q_heads.astype(jnp.float32), cos_table, sin_table)).reshape(
        length, local_kv, GROUP, HEAD_DIM
    )
    k_rot = low(rotate(k_heads.astype(jnp.float32), cos_table, sin_table)).reshape(
        length, local_kv, HEAD_DIM
    )
    values = v_heads.reshape(length, local_kv, HEAD_DIM)
    block_rows = min(512, length)
    outputs = []
    totals_list = []
    for first_row in range(0, length, block_rows):
        key_end = first_row + block_rows
        scores = (
            jnp.einsum(
                "qhgd,khd->hgqk",
                q_rot[first_row:key_end],
                k_rot[:key_end],
                preferred_element_type=jnp.float32,
            )
            * 0.125
        )
        causal = (first_row + jnp.arange(block_rows, dtype=jnp.int32))[:, None] >= jnp.arange(
            key_end, dtype=jnp.int32
        )[None, :]
        scores = jnp.where(causal, scores, -jnp.inf)
        row_peak = jnp.max(scores, axis=-1, keepdims=True)
        exponents = jnp.exp(scores - row_peak)
        totals = jnp.sum(exponents, axis=-1, keepdims=True)
        attended = jnp.einsum(
            "hgqk,khd->qhgd",
            low(exponents / totals),
            values[:key_end],
            preferred_element_type=jnp.float32,
        )
        outputs.append(low(attended).reshape(block_rows, -1))
        totals_list.append((row_peak + jnp.log(totals))[..., 0])
    return (jnp.concatenate(outputs, axis=0), jnp.stack(totals_list), q_rot, k_rot, values)


def attention_backward(head_grad, q_rot, k_rot, values, log_total):
    length, local_kv = q_rot.shape[:2]
    cos_table, sin_table = rotary_tables(length)
    block_rows = min(512, length)
    grad_rows = head_grad.reshape(length, local_kv, GROUP, HEAD_DIM)
    key_acc = jnp.zeros((length, local_kv, HEAD_DIM), jnp.float32)
    value_acc = jnp.zeros((length, local_kv, HEAD_DIM), jnp.float32)
    query_parts = []
    for block_number, first_row in enumerate(range(0, length, block_rows)):
        key_end = first_row + block_rows
        q_block = q_rot[first_row:key_end]
        grad_block = grad_rows[first_row:key_end]
        key_part = k_rot[:key_end]
        scores = (
            jnp.einsum("qhgd,khd->hgqk", q_block, key_part, preferred_element_type=jnp.float32)
            * 0.125
        )
        causal = (first_row + jnp.arange(block_rows, dtype=jnp.int32))[:, None] >= jnp.arange(
            key_end, dtype=jnp.int32
        )[None, :]
        scores = jnp.where(causal, scores, -jnp.inf)
        probs_full = jnp.exp(scores - log_total[block_number][..., None])
        prob_grad = jnp.einsum(
            "qhgd,khd->hgqk", grad_block, values[:key_end], preferred_element_type=jnp.float32
        )
        score_grad = probs_full * (
            prob_grad - jnp.sum(probs_full * prob_grad, axis=-1, keepdims=True)
        )
        score_low = low(score_grad)
        query_parts.append(
            jnp.einsum("hgqk,khd->qhgd", score_low, key_part, preferred_element_type=jnp.float32)
            * 0.125
        )
        key_acc = key_acc.at[:key_end].add(
            jnp.einsum("hgqk,qhgd->khd", score_low, q_block, preferred_element_type=jnp.float32)
            * 0.125
        )
        value_acc = value_acc.at[:key_end].add(
            jnp.einsum(
                "hgqk,qhgd->khd", low(probs_full), grad_block, preferred_element_type=jnp.float32
            )
        )
    query_all = jnp.concatenate(query_parts, axis=0).reshape(length, -1)
    query_grad = rotate(query_all, cos_table, -sin_table)
    key_grad = rotate(key_acc.reshape(length, -1), cos_table, -sin_table)
    return jnp.concatenate(
        [low(query_grad), low(key_grad), low(value_acc).reshape(length, -1)], axis=1
    )


def token_choice(route):
    return route[..., None] == jnp.arange(EXPERTS, dtype=jnp.int32)


def routing(route_all, first_expert, count):
    chosen = jnp.any(token_choice(route_all), axis=2)
    mine = lax.dynamic_slice_in_dim(chosen, first_expert, count, axis=2)
    rows = mine.shape[1]
    earlier = jnp.tril(jnp.ones((rows, rows), jnp.bfloat16), -1)
    place = jnp.einsum(
        "ts,bsj->bjt", earlier, mine.astype(jnp.bfloat16), preferred_element_type=jnp.float32
    ).astype(jnp.int32)
    mine = jnp.transpose(mine, (0, 2, 1))
    slots = jnp.arange(CAP, dtype=jnp.int32)
    pick = (place[:, :, None, :] == slots[None, None, :, None]) & mine[:, :, None, :]
    return chosen, pick


def choose(pick, rows):
    picked = jnp.einsum("bct,btd->bcd", low(pick), rows, preferred_element_type=jnp.float32)
    return low(picked).reshape(-1, rows.shape[-1])


def give_back(picks, slot_rows):
    total = 0.0
    for pick, rows in zip(picks, slot_rows):
        blocks, count = pick.shape[:2]
        total = total + jnp.einsum(
            "bct,bcd->btd",
            low(pick),
            rows.reshape(blocks, count, -1),
            preferred_element_type=jnp.float32,
        )
    return total.reshape(-1, total.shape[-1])


def slot_values(pick, values):
    return jnp.sum(jnp.where(pick, values[:, None, :], 0.0), axis=2).reshape(-1, 1)


def forward_layer(layer_in, route_all, weights, experts, first_expert):
    attn_scale, ffn_scale, qkv_w, out_w, router_w = weights
    gate_w, up_w, down_w = experts
    count = gate_w.shape[0]
    normed_input = low(rms_norm(layer_in, attn_scale))
    normed_all = lax.all_gather(normed_input, "seq", axis=0, tiled=True)
    qkv = low(dot(normed_all, qkv_w))
    kv_width = KV_HEADS * HEAD_DIM // lax.axis_size("seq")
    q_width = GROUP * kv_width
    mixed, log_total, q_rot, k_rot, v_heads = attention_forward(
        qkv[:, :q_width], qkv[:, q_width : q_width + kv_width], qkv[:, q_width + kv_width :]
    )
    branch = lax.psum_scatter(low(dot(mixed, out_w)), "seq", scatter_dimension=0, tiled=True)
    after_update = layer_in + branch.astype(jnp.float32)
    normed_ffn = low(rms_norm(after_update, ffn_scale))
    ffn_all = whole_tokens(normed_ffn)
    chosen, pick = routing(route_all, first_expert, count)
    blocks, rows = chosen.shape[:2]
    logits = dot(ffn_all, router_w).reshape(blocks, rows, EXPERTS)
    logits = jnp.where(chosen, logits, -jnp.inf)
    gates = jax.nn.softmax(logits, axis=-1)
    mine = jnp.transpose(
        lax.dynamic_slice_in_dim(gates, first_expert, count, axis=2), (0, 2, 1)
    )
    ffn_blocks = ffn_all.reshape(blocks, rows, -1)
    results = []
    saved_experts = []
    for j in range(count):
        slot_rows = choose(pick[:, j], ffn_blocks)
        slot_gates = slot_values(pick[:, j], mine[:, j])
        gate_pre = dot(slot_rows, gate_w[j])
        up_pre = dot(slot_rows, up_w[j])
        hidden = jax.nn.silu(gate_pre) * up_pre
        scaled = low(slot_gates * hidden)
        results.append(low(dot(scaled, down_w[j])))
        saved_experts.append((slot_rows, slot_gates, gate_pre, up_pre, scaled))
    moe = give_back([pick[:, j] for j in range(count)], results)
    moe = token_sums(low(moe))
    layer_out = after_update + moe.astype(jnp.float32)
    own_block = lax.axis_index("dp") * lax.axis_size("seq") + lax.axis_index("seq")
    own_gates = lax.dynamic_index_in_dim(gates, own_block, 0, keepdims=False)
    saved = (
        layer_in,
        normed_all,
        q_rot,
        k_rot,
        v_heads,
        log_total,
        mixed,
        after_update,
        normed_ffn,
        own_gates,
        pick,
        saved_experts,
    )
    return (layer_out, saved)


def backward_layer(layer_grad, saved, weights, experts):
    attn_scale, ffn_scale, qkv_w, out_w, router_w = weights
    gate_w, up_w, down_w = experts
    count = gate_w.shape[0]
    (
        layer_in,
        normed_all,
        q_rot,
        k_rot,
        v_heads,
        log_total,
        mixed,
        after_update,
        normed_ffn,
        own_gates,
        pick,
        saved_experts,
    ) = saved
    blocks, _, _, rows = pick.shape
    grad_all = whole_tokens(low(layer_grad))
    grad_blocks = grad_all.reshape(blocks, rows, -1)
    input_rows = []
    gate_terms = []
    expert_grads = ([], [], [])
    for j in range(count):
        slot_rows, slot_gates, gate_pre, up_pre, scaled = saved_experts[j]
        slot_grads = choose(pick[:, j], grad_blocks)
        plain_grad = dot_t(slot_grads, down_w[j])
        sigmoid = jax.nn.sigmoid(gate_pre)
        activated = gate_pre * sigmoid
        gate_term = jnp.sum(plain_grad * (activated * up_pre), axis=1).reshape(blocks, 1, -1)
        gate_terms.append(jnp.sum(jnp.where(pick[:, j], gate_term.reshape(blocks, -1, 1), 0.0), 1))
        hidden_grad = slot_gates * plain_grad
        gate_low = low(hidden_grad * up_pre * sigmoid * (1.0 + gate_pre * (1.0 - sigmoid)))
        up_low = low(hidden_grad * activated)
        input_rows.append(low(dot_t(gate_low, gate_w[j]) + dot_t(up_low, up_w[j])))
        expert_grads[0].append(low(t_dot(slot_rows, gate_low)))
        expert_grads[1].append(low(t_dot(slot_rows, up_low)))
        expert_grads[2].append(low(t_dot(scaled, slot_grads)))
    expert_grads = tuple(jnp.stack(parts) for parts in expert_grads)
    normed_grad = give_back([pick[:, j] for j in range(count)], input_rows)
    normed_grad = token_sums(low(normed_grad))
    gate_terms = jnp.stack(gate_terms, axis=1)
    gate_terms = lax.all_to_all(gate_terms, TOKENS, split_axis=0, concat_axis=0, tiled=True)
    gate_terms = gate_terms.reshape(-1, rows)
    if gate_terms.shape[0] > EXPERTS:
        gate_terms = jnp.sum(gate_terms.reshape(EXPERTS, -1, rows), axis=1)
    gate_terms = gate_terms.T
    logit_grad = low(
        own_gates * (gate_terms - jnp.sum(own_gates * gate_terms, axis=-1, keepdims=True))
    )
    router_grad = t_dot(normed_ffn, logit_grad)
    normed_grad = normed_grad.astype(jnp.float32) + dot_t(logit_grad, router_w)
    after_part, ffn_gain_grad = jax.vjp(rms_norm, after_update, ffn_scale)[1](normed_grad)
    after_grad = after_part + layer_grad
    branch_all = lax.all_gather(low(after_grad), "seq", axis=0, tiled=True)
    out_grad = t_dot(mixed, branch_all)
    head_grad = low(dot_t(branch_all, out_w))
    qkv_grad = attention_backward(head_grad, q_rot, k_rot, v_heads, log_total)
    qkv_weight_grad = t_dot(normed_all, qkv_grad)
    normed_attn = low(dot_t(qkv_grad, qkv_w))
    normed_attn = lax.psum_scatter(normed_attn, "seq", scatter_dimension=0, tiled=True)
    input_part, attn_gain_grad = jax.vjp(rms_norm, layer_in, attn_scale)[1](
        normed_attn.astype(jnp.float32)
    )
    small_grads = jnp.concatenate(
        [router_grad, attn_gain_grad[:, None], ffn_gain_grad[:, None]], axis=1
    )
    return (input_part + after_grad, qkv_weight_grad, out_grad, small_grads, expert_grads)


def body(
    hidden_in,
    out_grad,
    attn_gain,
    ffn_gain,
    query_matrix,
    key_matrix,
    value_matrix,
    output_matrix,
    router_matrix,
    w_gate,
    w_up,
    w_down,
    routes,
):
    section = lax.axis_index("section")
    dp, seq = lax.axis_size("dp"), lax.axis_size("seq")
    seq_index = lax.axis_index("seq")
    first = section == 0
    slice_len = hidden_in.shape[2]
    width = hidden_in.shape[3]
    depth = query_matrix.shape[1]

    def by_layer(own, other):
        return [jnp.where(first, own, other), jnp.where(first, other, own)]

    layer_in = lax.dynamic_index_in_dim(hidden_in, section, 0, keepdims=False)[0]
    top_grad = lax.dynamic_index_in_dim(out_grad, section, 0, keepdims=False)[0]
    own_routes = lax.dynamic_index_in_dim(routes[0], section, 0, keepdims=False)[0]
    other_routes = lax.dynamic_index_in_dim(routes[0], 1 - section, 0, keepdims=False)[0]
    layer_routes = jnp.stack(by_layer(own_routes, swap(other_routes)))
    routes_all = lax.all_gather(layer_routes, TOKENS, axis=0, tiled=False)

    small = jnp.concatenate([router_matrix[0], attn_gain[0][:, None], ffn_gain[0][:, None]], axis=1)
    small = lax.all_gather(small, ("section", "dp", "seq"), axis=0, tiled=True)
    small = small.reshape(2, width, -1)
    by_group = jnp.concatenate(
        [
            matrix[0].reshape(depth, seq, -1)
            for matrix in (query_matrix, key_matrix, value_matrix)
        ],
        axis=2,
    )
    qkv_layers = []
    for part in by_layer(by_group, swap(by_group)):
        part = lax.all_to_all(part, "seq", split_axis=1, concat_axis=0, tiled=True)
        part = part.reshape(seq * depth, -1)
        qkv_layers.append(lax.all_gather(part, "dp", axis=0, tiled=True))
    devices = [(d, s) for d in range(dp) for s in range(seq)]
    to_group = []
    for flat in range(dp * seq):
        to_group.append((flat, (flat % dp) * seq + flat // dp))
    from_group = [(target, source) for source, target in to_group]
    grouped_out = lax.ppermute(output_matrix[0], TOKENS, to_group)
    out_layers = []
    for part in by_layer(grouped_out, swap(grouped_out)):
        out_layers.append(lax.all_gather(part, "dp", axis=0, tiled=True))

    local = w_gate.shape[1]
    hidden_units = w_gate.shape[3]
    if local >= seq:
        count, units = local // seq, hidden_units
        start, unit_start = seq_index * count, 0
    else:
        count, units = 1, hidden_units * local // seq
        start, unit_start = seq_index * local // seq, (seq_index % (seq // local)) * units
    first_expert = lax.axis_index("dp") * local + start
    own_experts = (
        lax.dynamic_slice(w_gate[0], (start, 0, unit_start), (count, width, units)),
        lax.dynamic_slice(w_up[0], (start, 0, unit_start), (count, width, units)),
        lax.dynamic_slice(w_down[0], (start, unit_start, 0), (count, units, width)),
    )
    expert_layers = list(zip(*[by_layer(own, swap(own)) for own in own_experts]))
    weights = []
    for number in range(2):
        weights.append(
            (
                small[number, :, EXPERTS].astype(jnp.float32),
                small[number, :, EXPERTS + 1].astype(jnp.float32),
                qkv_layers[number],
                out_layers[number],
                small[number, :, :EXPERTS],
            )
        )

    state = layer_in.astype(jnp.float32)
    layer_states = []
    saved_layers = []
    for number in range(2):
        state, saved = forward_layer(
            state, routes_all[:, number], weights[number], expert_layers[number], first_expert
        )
        layer_states.append(state)
        saved_layers.append(saved)
    grad = top_grad.astype(jnp.float32)
    layer_grads = [None, None]
    weight_grads = [None, None]
    for number in (1, 0):
        grad, *weight_grads[number] = backward_layer(
            grad, saved_layers[number], weights[number], expert_layers[number]
        )
        layer_grads[number] = grad

    def to_section(pieces):
        received = [pass_to(pieces[number], number) for number in range(2)]
        own = jnp.where(first, pieces[0], pieces[1])
        other = jnp.where(first, received[0], received[1])
        return jnp.stack(by_layer(own, other))[None, :, None]

    def summed(pieces):
        received = [pass_to(pieces[number], number) for number in range(2)]
        own = jnp.where(first, pieces[0], pieces[1]).astype(jnp.float32)
        return own + jnp.where(first, received[0], received[1]).astype(jnp.float32)

    def scatter_rows(part):
        part = lax.psum_scatter(low(part), "dp", scatter_dimension=0, tiled=True)
        return part

    qkv_parts = []
    out_parts = []
    small_parts = []
    for number in range(2):
        qkv_part, out_part, small_part, _ = weight_grads[number]
        qkv_part = scatter_rows(qkv_part).reshape(seq, depth, -1)
        qkv_part = lax.all_to_all(qkv_part, "seq", split_axis=0, concat_axis=0, tiled=True)
        qkv_parts.append(qkv_part)
        out_parts.append(lax.ppermute(scatter_rows(out_part), TOKENS, from_group))
        small_parts.append(
            lax.psum_scatter(small_part, TOKENS, scatter_dimension=0, tiled=True)
        )
    qkv_sum = summed(qkv_parts)
    out_sum = summed(out_parts)
    small_sum = summed(small_parts)
    kv_width = KV_HEADS * HEAD_DIM // seq
    q_width = GROUP * kv_width

    def columns(begin, end):
        return jnp.transpose(qkv_sum[:, :, begin:end], (1, 0, 2)).reshape(depth, -1)[None]

    expert_sums = []
    for kind in range(3):
        pieces = []
        for number in range(2):
            piece = weight_grads[number][3][kind]
            if local >= seq:
                piece = lax.all_to_all(piece, "seq", split_axis=1, concat_axis=0, tiled=True)
            else:
                share = seq // local
                if kind < 2:
                    piece = piece.reshape(seq, width // seq, units)
                    piece = lax.all_to_all(piece, "seq", split_axis=0, concat_axis=0, tiled=True)
                    piece = piece.reshape(local, share, width // seq, units)
                    piece = jnp.transpose(piece, (0, 2, 1, 3)).reshape(local, width // seq, -1)
                else:
                    rows = hidden_units // seq
                    piece = piece.reshape(-1, rows, width)
                    piece = whole_rows(piece, seq_index, share, seq)
            pieces.append(piece)
        expert_sums.append(summed(pieces)[None])
    return (
        to_section(layer_states),
        to_section(layer_grads),
        small_sum[:, EXPERTS][None],
        small_sum[:, EXPERTS + 1][None],
        columns(0, q_width),
        columns(q_width, q_width + kv_width),
        columns(q_width + kv_width, q_width + 2 * kv_width),
        out_sum[None],
        small_sum[:, :EXPERTS][None],
        *expert_sums,
    )


def whole_rows(piece, seq_index, share, seq):
    parts = piece.shape[0]
    spread = jnp.zeros((seq,) + piece.shape[1:], piece.dtype)
    spread = lax.dynamic_update_slice_in_dim(
        spread, piece, (seq_index % share) * parts, axis=0
    )
    spread = lax.all_to_all(spread, "seq", split_axis=0, concat_axis=0, tiled=True)
    spread = spread.reshape((-1, share) + piece.shape[1:])
    return jnp.sum(spread.astype(jnp.float32), axis=1).astype(piece.dtype)


def solution(mesh):
    return jax.shard_map(
        body,
        mesh=mesh,
        in_specs=(
            P(None, "dp", "seq", None),
            P(None, "dp", "seq", None),
            P("section", ("dp", "seq")),
            P("section", ("dp", "seq")),
            P("section", ("dp", "seq"), None),
            P("section", ("dp", "seq"), None),
            P("section", ("dp", "seq"), None),
            P("section", ("dp", "seq"), None),
            P("section", ("dp", "seq"), None),
            P("section", "dp", None, None),
            P("section", "dp", None, None),
            P("section", "dp", None, None),
            P("section", None, "dp", "seq", None),
        ),
        out_specs=(
            P("section", None, "dp", "seq", None),
            P("section", None, "dp", "seq", None),
            P("section", ("dp", "seq")),
            P("section", ("dp", "seq")),
            P("section", ("dp", "seq"), None),
            P("section", ("dp", "seq"), None),
            P("section", ("dp", "seq"), None),
            P("section", ("dp", "seq"), None),
            P("section", ("dp", "seq"), None),
            P("section", "dp", "seq", None),
            P("section", "dp", "seq", None),
            P("section", "dp", "seq", None),
        ),
        check_vma=False,
    )
```

```python
import jax
import jax.numpy as jnp
from jax import lax
from jax.experimental import pallas as pl
from jax.experimental.pallas import tpu as pltpu
from jax.sharding import PartitionSpec as P

HEADS = 24
KV_HEADS = 8
HEAD_DIM = 64
TOP_K = 8
EXPERTS = 32
CAP = 80
GROUP = HEADS // KV_HEADS
TOKENS = ("dp", "seq")
MESH = pl.DeviceIdType.MESH
DMA = pltpu.SemaphoreType.DMA

epsilon = 1e-06


def dot(a, b):
    return jnp.dot(a, b, preferred_element_type=jnp.float32)


def dot_t(a, b):
    return lax.dot_general(a, b, (((1,), (1,)), ((), ())), preferred_element_type=jnp.float32)


def t_dot(a, b):
    return lax.dot_general(a, b, (((0,), (0,)), ((), ())), preferred_element_type=jnp.float32)


def low(v):
    return v.astype(jnp.bfloat16)


def swap(block):
    return lax.ppermute(block, "section", [(0, 1), (1, 0)])


def pass_to(block, section):
    return lax.ppermute(block, "section", [(1 - section, section)])


def rms_norm(values, norm_gain):
    return (
        values * lax.rsqrt(jnp.mean(values * values, axis=-1, keepdims=True) + epsilon) * norm_gain
    )


def rotary_tables(length):
    half_dim = HEAD_DIM // 2
    frequency = 10000.0 ** (-jnp.arange(half_dim, dtype=jnp.float32) * 2.0 / HEAD_DIM)
    angles = jnp.arange(length, dtype=jnp.float32)[:, None] * frequency[None, :]
    return (jnp.cos(angles)[:, None, :], jnp.sin(angles)[:, None, :])


def rotate(values, cos_table, sin_table):
    length = values.shape[0]
    split_heads = values.reshape(length, -1, HEAD_DIM)
    first_half = split_heads[..., : HEAD_DIM // 2]
    second_half = split_heads[..., HEAD_DIM // 2 :]
    turned = jnp.concatenate(
        [
            first_half * cos_table - second_half * sin_table,
            second_half * cos_table + first_half * sin_table,
        ],
        axis=-1,
    )
    return turned.reshape(length, -1)


def attention_forward(q_heads, k_heads, v_heads):
    length = q_heads.shape[0]
    local_kv = k_heads.shape[1] // HEAD_DIM
    cos_table, sin_table = rotary_tables(length)
    q_rot = low(rotate(q_heads.astype(jnp.float32), cos_table, sin_table)).reshape(
        length, local_kv, GROUP, HEAD_DIM
    )
    k_rot = low(rotate(k_heads.astype(jnp.float32), cos_table, sin_table)).reshape(
        length, local_kv, HEAD_DIM
    )
    values = v_heads.reshape(length, local_kv, HEAD_DIM)
    block_rows = min(512, length)
    outputs = []
    totals_list = []
    for first_row in range(0, length, block_rows):
        key_end = first_row + block_rows
        scores = (
            jnp.einsum(
                "qhgd,khd->hgqk",
                q_rot[first_row:key_end],
                k_rot[:key_end],
                preferred_element_type=jnp.float32,
            )
            * 0.125
        )
        causal = (first_row + jnp.arange(block_rows, dtype=jnp.int32))[:, None] >= jnp.arange(
            key_end, dtype=jnp.int32
        )[None, :]
        scores = jnp.where(causal, scores, -jnp.inf)
        row_peak = jnp.max(scores, axis=-1, keepdims=True)
        exponents = jnp.exp(scores - row_peak)
        totals = jnp.sum(exponents, axis=-1, keepdims=True)
        attended = jnp.einsum(
            "hgqk,khd->qhgd",
            low(exponents / totals),
            values[:key_end],
            preferred_element_type=jnp.float32,
        )
        outputs.append(low(attended).reshape(block_rows, -1))
        totals_list.append((row_peak + jnp.log(totals))[..., 0])
    return (jnp.concatenate(outputs, axis=0), jnp.stack(totals_list), q_rot, k_rot, values)


def attention_backward(head_grad, q_rot, k_rot, values, log_total):
    length, local_kv = q_rot.shape[:2]
    cos_table, sin_table = rotary_tables(length)
    block_rows = min(512, length)
    grad_rows = head_grad.reshape(length, local_kv, GROUP, HEAD_DIM)
    key_acc = jnp.zeros((length, local_kv, HEAD_DIM), jnp.float32)
    value_acc = jnp.zeros((length, local_kv, HEAD_DIM), jnp.float32)
    query_parts = []
    for block_number, first_row in enumerate(range(0, length, block_rows)):
        key_end = first_row + block_rows
        q_block = q_rot[first_row:key_end]
        grad_block = grad_rows[first_row:key_end]
        key_part = k_rot[:key_end]
        scores = (
            jnp.einsum("qhgd,khd->hgqk", q_block, key_part, preferred_element_type=jnp.float32)
            * 0.125
        )
        causal = (first_row + jnp.arange(block_rows, dtype=jnp.int32))[:, None] >= jnp.arange(
            key_end, dtype=jnp.int32
        )[None, :]
        scores = jnp.where(causal, scores, -jnp.inf)
        probs_full = jnp.exp(scores - log_total[block_number][..., None])
        prob_grad = jnp.einsum(
            "qhgd,khd->hgqk", grad_block, values[:key_end], preferred_element_type=jnp.float32
        )
        score_grad = probs_full * (
            prob_grad - jnp.sum(probs_full * prob_grad, axis=-1, keepdims=True)
        )
        score_low = low(score_grad)
        query_parts.append(
            jnp.einsum("hgqk,khd->qhgd", score_low, key_part, preferred_element_type=jnp.float32)
            * 0.125
        )
        key_acc = key_acc.at[:key_end].add(
            jnp.einsum("hgqk,qhgd->khd", score_low, q_block, preferred_element_type=jnp.float32)
            * 0.125
        )
        value_acc = value_acc.at[:key_end].add(
            jnp.einsum(
                "hgqk,qhgd->khd", low(probs_full), grad_block, preferred_element_type=jnp.float32
            )
        )
    query_all = jnp.concatenate(query_parts, axis=0).reshape(length, -1)
    query_grad = rotate(query_all, cos_table, -sin_table)
    key_grad = rotate(key_acc.reshape(length, -1), cos_table, -sin_table)
    return jnp.concatenate(
        [low(query_grad), low(key_grad), low(value_acc).reshape(length, -1)], axis=1
    )


def remote(src, dst, send_sem, recv_sem, **device):
    return pltpu.make_async_remote_copy(
        src_ref=src,
        dst_ref=dst,
        send_sem=send_sem,
        recv_sem=recv_sem,
        device_id=device,
        device_id_type=MESH,
    )


def greet(d, s):
    barrier = pltpu.get_barrier_semaphore()

    def signal(**device):
        pl.semaphore_signal(barrier, inc=1, device_id=device, device_id_type=MESH)

    signal(seq=s ^ 1)
    signal(seq=s ^ 2)

    @pl.when(d > 0)
    def _():
        signal(dp=d - 1)

    @pl.when(d < 3)
    def _():
        signal(dp=d + 1)

    inner = (d > 0) & (d < 3)

    @pl.when(inner)
    def _():
        pl.semaphore_wait(barrier, 4)

    @pl.when(jnp.logical_not(inner))
    def _():
        pl.semaphore_wait(barrier, 3)


def gather_scratch(rows, width):
    return [
        pltpu.VMEM((16, rows, width), jnp.bfloat16),
        DMA(()),
        DMA((2, 4)),
        DMA((4,)),
        DMA((4,)),
        DMA((4,)),
        DMA((4, 2)),
        DMA((4, 2)),
    ]


def gather_blocks(x_ref, scratch, compute):
    land, lsem, zs, zr, ys, yr, cs, cr = scratch
    d, s = lax.axis_index("dp"), lax.axis_index("seq")

    def place(z, column):
        return land.at[z * 4 + column]

    def z_copy(src, z, right):
        target = d + 1 if right else d - 1
        return remote(src, place(z, s), zs.at[int(right), z], zr.at[z], dp=target)

    def y_copy(src, z):
        return remote(src, place(z, s), ys.at[z], yr.at[z], seq=s ^ 2)

    def core_copy(src, z, across):
        column = s ^ 2 if across else s
        return remote(src, place(z, column), cs.at[z, across], cr.at[z, across], seq=s ^ 1)

    greet(d, s)
    own = pltpu.make_async_copy(x_ref, place(d, s), lsem)
    own.start()

    @pl.when(d < 3)
    def _():
        z_copy(x_ref, d, True).start()

    @pl.when(d > 0)
    def _():
        z_copy(x_ref, d, False).start()

    y_copy(x_ref, d).start()
    core_copy(x_ref, d, 0).start()
    own.wait()

    @pl.loop(0, 4)
    def _(i):
        @pl.when(i < 3)
        def _():
            left, right = d - (i + 1), d + (i + 1)

            @pl.when(left >= 0)
            def _():
                z_copy(place(left, s), left, True).wait_recv()

                @pl.when(d < 3)
                def _():
                    z_copy(place(left, s), left, True).start()

            @pl.when(right <= 3)
            def _():
                z_copy(place(right, s), right, False).wait_recv()

                @pl.when(d > 0)
                def _():
                    z_copy(place(right, s), right, False).start()

            following = d ^ (i + 1)
            y_copy(place(following, s), following).start()
            core_copy(place(following, s), following, 0).start()

        z = d ^ i
        y_copy(place(z, s ^ 2), z).wait_recv()
        core_copy(place(z, s ^ 2), z, 1).start()
        core_copy(place(z, s ^ 1), z, 0).wait_recv()
        core_copy(place(z, s ^ 3), z, 1).wait_recv()
        compute(z)

    for z in range(4):

        @pl.when((z <= d) & (d < 3))
        def _():
            z_copy(place(z, s), z, True).wait_send()

        @pl.when((z >= d) & (d > 0))
        def _():
            z_copy(place(z, s), z, False).wait_send()

        y_copy(place(z, s), z).wait_send()
        core_copy(place(z, s), z, 0).wait_send()
        core_copy(place(z, s), z, 1).wait_send()
    return land


def pick_weights(own_refs, other_refs, held, sems, own_layer):
    mine = lax.axis_index("section") == own_layer

    @pl.when(mine)
    def _():
        for k, ref in enumerate(own_refs):
            pltpu.make_async_copy(ref, held[k], sems.at[k]).start()

    @pl.when(jnp.logical_not(mine))
    def _():
        for k, ref in enumerate(other_refs):
            pltpu.make_async_copy(ref, held[k], sems.at[k]).start()

    def ready(k):
        pltpu.make_async_copy(own_refs[k], held[k], sems.at[k]).wait()

    return ready


def expert_forward_kernel(
    layer, x_ref, pick_ref, chosen_ref, router_ref, mine_ref,
    wg_own, wu_own, wd_own, wg_other, wu_other, wd_other,
    rows_out, gate_out, up_out, hidden_out, slot_gate_out, y_out,
    wg, wu, wd, rows, gate, up, hidden, slot_gate, y, wsem, osem, *gather
):
    count = wg.shape[0]
    ready = pick_weights(
        (wg_own, wu_own, wd_own), (wg_other, wu_other, wd_other), (wg, wu, wd), wsem, layer
    )
    land = gather[0]
    d = lax.axis_index("dp")

    def outs(z):
        part = pl.ds(z * 4 * CAP, 4 * CAP)
        return [
            pltpu.make_async_copy(held.at[:, part], out.at[:, part], osem.at[k, z])
            for k, (held, out) in enumerate(
                ((rows, rows_out), (gate, gate_out), (up, up_out), (hidden, hidden_out), (slot_gate, slot_gate_out))
            )
        ] + [pltpu.make_async_copy(y.at[pl.ds(z * 4, 4)], y_out.at[pl.ds(z * 4, 4)], osem.at[5, z])]

    def compute(z):
        @pl.when(z == d)
        def _():
            for k in range(3):
                ready(k)

        for q in range(4):
            b = z * 4 + q
            picked = low(dot(pick_ref[b], land[b]))
            for j in range(count):
                rows[j, pl.ds(b * CAP, CAP), :] = picked[j * CAP : (j + 1) * CAP]
        part = pl.ds(z * 4 * CAP, 4 * CAP)

        @pl.loop(0, count)
        def _(j):
            x = rows[j, part, :]
            g = dot(x, wg[j])
            u = dot(x, wu[j])
            logits = dot(x, router_ref[...])
            for q in range(4):
                b = z * 4 + q
                slots = slice(q * CAP, (q + 1) * CAP)
                seen = dot(pick_ref[b, pl.ds(j * CAP, CAP), :], chosen_ref[b])
                masked = jnp.where(seen > 0.5, logits[slots], -1e30)
                power = jnp.exp(masked - jnp.max(masked, axis=1, keepdims=True))
                own = jnp.sum(power * mine_ref[j], axis=1, keepdims=True)
                value = own / jnp.sum(power, axis=1, keepdims=True)
                slot_gate[j, pl.ds(b * CAP, CAP), :] = jnp.broadcast_to(value, (CAP, 128))
            gate[j, part, :] = low(g)
            up[j, part, :] = low(u)
            h = low(g * jax.nn.sigmoid(g) * u * slot_gate[j, part, :][:, :1])
            hidden[j, part, :] = h
            result = low(dot(h, wd[j]))
            for q in range(4):
                y[z * 4 + q, pl.ds(j * CAP, CAP), :] = result[q * CAP : (q + 1) * CAP]

        for copy in outs(z):
            copy.start()

    gather_blocks(x_ref, gather, compute)
    for z in range(4):
        for copy in outs(z):
            copy.wait()


def expert_forward(layer, x, pick, chosen, router, mine, own, other, collective_id):
    count, width, units = own[0].shape
    rows = x.shape[0]
    slots = 16 * CAP
    bf = jnp.bfloat16
    anywhere = pl.BlockSpec(memory_space=pl.ANY)
    near = pl.BlockSpec(memory_space=pltpu.VMEM)
    results = [
        ((count, slots, width), bf),
        ((count, slots, units), bf),
        ((count, slots, units), bf),
        ((count, slots, units), bf),
        ((count, slots, 128), jnp.float32),
        ((16, count * CAP, width), bf),
    ]
    def kernel(*refs):
        expert_forward_kernel(layer, *refs)
    return pl.pallas_call(
        kernel,
        out_shape=[jax.ShapeDtypeStruct(*result) for result in results],
        in_specs=[anywhere, near, near, near, near] + [anywhere] * 6,
        out_specs=[anywhere] * 6,
        scratch_shapes=[pltpu.VMEM(weight.shape, bf) for weight in own]
        + [pltpu.VMEM(*result) for result in results]
        + [DMA((3,)), DMA((6, 4))]
        + gather_scratch(rows, width),
        compiler_params=pltpu.CompilerParams(
            collective_id=collective_id, has_side_effects=True, vmem_limit_bytes=60 << 20
        ),
        name="expert_forward",
    )(x, pick, chosen, router, mine, *own, *other)


def combine_kernel(pick_ref, y_ref, out_ref, y, sent, own, core_in, y_in, z_in, lsem, zs, zr, ys, yr, cs, cr):
    d, s = lax.axis_index("dp"), lax.axis_index("seq")
    half = out_ref.shape[0] // 2

    def loaded(b):
        return pltpu.make_async_copy(y_ref.at[b], y.at[b], lsem.at[b])

    def column(across, other_core):
        return s ^ (2 * across) ^ other_core

    for i in range(4):
        z = d ^ (3 - i)
        for across in (1, 0):
            for other_core in (1, 0):
                loaded(z * 4 + column(across, other_core)).start()
    greet(d, s)

    def rows(k):
        return pl.ds(pl.multiple_of(k * half, half), half)

    def partial_sum(z, k, across, other_core):
        b = z * 4 + column(across, other_core)

        @pl.when(k == 0)
        def _():
            loaded(b).wait()

        return dot(pick_ref[b, rows(k), :], y[b])

    def core_copy(z, k, across):
        return remote(
            sent.at[z, across, rows(k)],
            core_in.at[z, across, rows(k)],
            cs.at[z, k, across],
            cr.at[z, k, across],
            seq=s ^ 1,
        )

    def y_copy(z, k):
        return remote(own.at[z, 1, rows(k)], y_in.at[z, rows(k)], ys.at[z, k], yr.at[z, k], seq=s ^ 2)

    def z_copy(z, k, right):
        target = d + 1 if right else d - 1
        return remote(
            own.at[z, 0, rows(k)],
            z_in.at[int(right), z, rows(k)],
            zs.at[z, k],
            zr.at[int(right), z, k],
            dp=target,
        )

    def start(i):
        z, k = d ^ (3 - i // 2), i % 2
        sent[z, 1, rows(k), :] = low(partial_sum(z, k, 1, 1))
        core_copy(z, k, 1).start()
        total = partial_sum(z, k, 1, 0)
        core_copy(z, k, 1).wait_recv()
        own[z, 1, rows(k), :] = low(total + core_in[z, 1, rows(k), :].astype(jnp.float32))
        y_copy(z, k).start()
        sent[z, 0, rows(k), :] = low(partial_sum(z, k, 0, 1))
        core_copy(z, k, 0).start()

    start(0)

    @pl.loop(0, 8)
    def _(i):
        @pl.when(i < 7)
        def _():
            start(i + 1)

        z, k = d ^ (3 - i // 2), i % 2
        total = partial_sum(z, k, 0, 0)
        core_copy(z, k, 0).wait_recv()
        total = total + core_in[z, 0, rows(k), :].astype(jnp.float32)
        y_copy(z, k).wait_recv()
        total = total + y_in[z, rows(k), :].astype(jnp.float32)

        @pl.when(z < d)
        def _():
            @pl.when(d < 3)
            def _():
                z_copy(z, k, False).wait_recv()
                own[z, 0, rows(k), :] = low(total + z_in[0, z, rows(k), :].astype(jnp.float32))

            @pl.when(d == 3)
            def _():
                own[z, 0, rows(k), :] = low(total)

            z_copy(z, k, False).start()

        @pl.when(z > d)
        def _():
            @pl.when(d > 0)
            def _():
                z_copy(z, k, True).wait_recv()
                own[z, 0, rows(k), :] = low(total + z_in[1, z, rows(k), :].astype(jnp.float32))

            @pl.when(d == 0)
            def _():
                own[z, 0, rows(k), :] = low(total)

            z_copy(z, k, True).start()

        @pl.when(z == d)
        def _():
            out_ref[rows(k), :] = total

    for k in range(2):

        @pl.when(d < 3)
        def _():
            z_copy(d, k, False).wait_recv()
            out_ref[rows(k), :] += z_in[0, d, rows(k), :].astype(jnp.float32)

        @pl.when(d > 0)
        def _():
            z_copy(d, k, True).wait_recv()
            out_ref[rows(k), :] += z_in[1, d, rows(k), :].astype(jnp.float32)

    for z in range(4):
        for k in range(2):
            core_copy(z, k, 0).wait_send()
            core_copy(z, k, 1).wait_send()
            y_copy(z, k).wait_send()

            @pl.when(z < d)
            def _():
                z_copy(z, k, False).wait_send()

            @pl.when(z > d)
            def _():
                z_copy(z, k, True).wait_send()


def combine(pick_t, y, collective_id):
    rows, width = pick_t.shape[1], y.shape[2]

    def blocks(*lead):
        return pltpu.VMEM(lead + (rows, width), jnp.bfloat16)

    return pl.pallas_call(
        combine_kernel,
        out_shape=jax.ShapeDtypeStruct((rows, width), jnp.float32),
        in_specs=[pl.BlockSpec(memory_space=pltpu.VMEM), pl.BlockSpec(memory_space=pl.ANY)],
        out_specs=pl.BlockSpec(memory_space=pltpu.VMEM),
        scratch_shapes=[
            pltpu.VMEM(y.shape, jnp.bfloat16),
            blocks(4, 2),
            blocks(4, 2),
            blocks(4, 2),
            blocks(4),
            blocks(2, 4),
            DMA((16,)),
            DMA((4, 2)),
            DMA((2, 4, 2)),
            DMA((4, 2)),
            DMA((4, 2)),
            DMA((4, 2, 2)),
            DMA((4, 2, 2)),
        ],
        compiler_params=pltpu.CompilerParams(
            collective_id=collective_id, has_side_effects=True, vmem_limit_bytes=60 << 20
        ),
        name="combine",
    )(pick_t, y)


def expert_backward_kernel(
    layer, x_ref, pick_ref, gate_in, up_in, slot_gate_in,
    wg_own, wu_own, wd_own, wg_other, wu_other, wd_other,
    rows_out, gate_out, up_out, term_out, y_out,
    wg, wu, wd, rows, gate, up, slot_gate, y, wsem, isem, osem, *gather
):
    count = wg.shape[0]
    ready = pick_weights(
        (wg_own, wu_own, wd_own), (wg_other, wu_other, wd_other), (wg, wu, wd), wsem, layer
    )
    land = gather[0]
    d = lax.axis_index("dp")
    ins = [
        pltpu.make_async_copy(src, held, isem.at[k])
        for k, (src, held) in enumerate(((gate_in, gate), (up_in, up), (slot_gate_in, slot_gate)))
    ]
    for copy in ins:
        copy.start()

    def outs(z):
        part = pl.ds(z * 4 * CAP, 4 * CAP)
        return [
            pltpu.make_async_copy(held.at[:, part], out.at[:, part], osem.at[k, z])
            for k, (held, out) in enumerate(
                ((rows, rows_out), (gate, gate_out), (up, up_out), (slot_gate, term_out))
            )
        ] + [pltpu.make_async_copy(y.at[pl.ds(z * 4, 4)], y_out.at[pl.ds(z * 4, 4)], osem.at[4, z])]

    def compute(z):
        @pl.when(z == d)
        def _():
            for k in range(3):
                ready(k)
            for copy in ins:
                copy.wait()

        for q in range(4):
            b = z * 4 + q
            picked = low(dot(pick_ref[b], land[b]))
            for j in range(count):
                rows[j, pl.ds(b * CAP, CAP), :] = picked[j * CAP : (j + 1) * CAP]
        part = pl.ds(z * 4 * CAP, 4 * CAP)

        @pl.loop(0, count)
        def _(j):
            plain = dot_t(rows[j, part, :], wd[j])
            g = gate[j, part, :].astype(jnp.float32)
            u = up[j, part, :].astype(jnp.float32)
            sigmoid = jax.nn.sigmoid(g)
            active = g * sigmoid
            term = jnp.sum(plain * (active * u), axis=1, keepdims=True)
            grad = plain * slot_gate[j, part, :][:, :1]
            dg = low(grad * u * sigmoid * (1.0 + g * (1.0 - sigmoid)))
            du = low(grad * active)
            slot_gate[j, part, :] = jnp.broadcast_to(term, (4 * CAP, 128))
            gate[j, part, :] = dg
            up[j, part, :] = du
            result = low(dot_t(dg, wg[j]) + dot_t(du, wu[j]))
            for q in range(4):
                y[z * 4 + q, pl.ds(j * CAP, CAP), :] = result[q * CAP : (q + 1) * CAP]

        for copy in outs(z):
            copy.start()

    gather_blocks(x_ref, gather, compute)
    for z in range(4):
        for copy in outs(z):
            copy.wait()


def expert_backward(layer, x, pick, gate, up, slot_gate, own, other, collective_id):
    count, width, units = own[0].shape
    rows = x.shape[0]
    slots = 16 * CAP
    bf = jnp.bfloat16
    anywhere = pl.BlockSpec(memory_space=pl.ANY)
    near = pl.BlockSpec(memory_space=pltpu.VMEM)
    results = [
        ((count, slots, width), bf),
        ((count, slots, units), bf),
        ((count, slots, units), bf),
        ((count, slots, 128), jnp.float32),
        ((16, count * CAP, width), bf),
    ]
    def kernel(*refs):
        expert_backward_kernel(layer, *refs)
    return pl.pallas_call(
        kernel,
        out_shape=[jax.ShapeDtypeStruct(*result) for result in results],
        in_specs=[anywhere, near] + [anywhere] * 9,
        out_specs=[anywhere] * 5,
        scratch_shapes=[pltpu.VMEM(weight.shape, bf) for weight in own]
        + [pltpu.VMEM(*result) for result in results]
        + [DMA((3,)), DMA((3,)), DMA((5, 4))]
        + gather_scratch(rows, width),
        compiler_params=pltpu.CompilerParams(
            collective_id=collective_id, has_side_effects=True, vmem_limit_bytes=60 << 20
        ),
        name="expert_backward",
    )(x, pick, gate, up, slot_gate, *own, *other)


def token_choice(route):
    return route[..., None] == jnp.arange(EXPERTS, dtype=jnp.int32)


def routing(route_all, first_expert, count):
    chosen = jnp.any(token_choice(route_all), axis=2)
    blocks, rows = chosen.shape[:2]
    mine = lax.dynamic_slice_in_dim(chosen, first_expert, count, axis=2)
    earlier = jnp.tril(jnp.ones((rows, rows), jnp.bfloat16), -1)
    place = jnp.einsum(
        "ts,bsj->bjt", earlier, mine.astype(jnp.bfloat16), preferred_element_type=jnp.float32
    ).astype(jnp.int32)
    mine = jnp.transpose(mine, (0, 2, 1))
    place = jnp.where(mine, place, -1)
    slots = jnp.arange(CAP, dtype=jnp.int32)
    pick = low(place[:, :, None, :] == slots[None, None, :, None]).reshape(blocks, -1, rows)
    return chosen, pick, jnp.transpose(pick, (0, 2, 1))


def choose(pick, rows, count):
    picked = jnp.einsum("bct,btd->bcd", pick, rows, preferred_element_type=jnp.float32)
    blocks = pick.shape[0]
    picked = low(picked).reshape(blocks, count, CAP, -1)
    return jnp.transpose(picked, (1, 0, 2, 3)).reshape(count, blocks * CAP, -1)


def give_back(pick_t, slot_rows):
    blocks, rows = pick_t.shape[:2]
    count, _, width = slot_rows.shape
    slot_rows = jnp.transpose(slot_rows.reshape(count, blocks, CAP, width), (1, 0, 2, 3))
    slot_rows = slot_rows.reshape(blocks, count * CAP, width)
    total = jnp.einsum("btc,bcd->btd", pick_t, slot_rows, preferred_element_type=jnp.float32)
    return low(total).reshape(-1, width)


def each_dot(form, a, b):
    return jnp.einsum(form, a, b, preferred_element_type=jnp.float32)


def after(value, *others):
    return lax.optimization_barrier((value, *others))[0]


def has_kernels():
    return lax.axis_size("dp") == 4 and lax.axis_size("seq") == 4


def forward_layer(number, layer_in, picking, weights, experts):
    attn_scale, ffn_scale, qkv_w, out_w, router_w = weights
    chosen, pick, pick_t, first_expert = picking
    own, other = experts
    count = own[0].shape[0]
    blocks, rows = chosen.shape[:2]
    normed_input = low(rms_norm(layer_in, attn_scale))
    normed_all = lax.all_gather(normed_input, "seq", axis=0, tiled=True)
    qkv = low(dot(normed_all, qkv_w))
    kv_width = KV_HEADS * HEAD_DIM // lax.axis_size("seq")
    q_width = GROUP * kv_width
    mixed, log_total, q_rot, k_rot, v_heads = attention_forward(
        qkv[:, :q_width], qkv[:, q_width : q_width + kv_width], qkv[:, q_width + kv_width :]
    )
    branch = lax.psum_scatter(low(dot(mixed, out_w)), "seq", scatter_dimension=0, tiled=True)
    after_update = layer_in + branch.astype(jnp.float32)
    normed_ffn = low(rms_norm(after_update, ffn_scale))
    own_block = lax.axis_index("dp") * lax.axis_size("seq") + lax.axis_index("seq")
    own_chosen = lax.dynamic_index_in_dim(chosen, own_block, 0, keepdims=False)
    own_logits = jnp.where(own_chosen, dot(normed_ffn, router_w), -jnp.inf)
    own_gates = jax.nn.softmax(own_logits, axis=-1)
    mine = (
        jnp.arange(EXPERTS)[None, None, :] == first_expert + jnp.arange(count)[:, None, None]
    ).astype(jnp.float32)
    if has_kernels():
        *expert_state, slot_out = expert_forward(
            number, normed_ffn, pick, low(chosen), router_w, mine, own, other, 1 + number
        )
        moe = combine(pick_t, slot_out, 3)
    else:
        gate_w, up_w, down_w = by_layer(number, own, other)
        ffn_all = lax.all_gather(normed_ffn, TOKENS, axis=0, tiled=True)
        logits = dot(ffn_all, router_w).reshape(blocks, rows, EXPERTS)
        gates = jax.nn.softmax(jnp.where(chosen, logits, -jnp.inf), axis=-1)
        slot_rows = choose(pick, ffn_all.reshape(blocks, rows, -1), count)
        mine_gates = jnp.einsum("bte,jxe->bjt", gates, mine, precision=lax.Precision.HIGHEST)
        slot_gates = jnp.sum(
            pick.reshape(blocks, count, CAP, rows).astype(jnp.float32) * mine_gates[:, :, None, :],
            axis=3,
        )
        slot_gates = jnp.transpose(slot_gates, (1, 0, 2)).reshape(count, -1, 1)
        gate_pre = each_dot("ecd,edf->ecf", slot_rows, gate_w)
        up_pre = each_dot("ecd,edf->ecf", slot_rows, up_w)
        scaled = low(slot_gates * jax.nn.silu(gate_pre) * up_pre)
        slot_out = low(each_dot("ecf,efd->ecd", scaled, down_w))
        moe = lax.psum_scatter(
            give_back(pick_t, slot_out), TOKENS, scatter_dimension=0, tiled=True
        ).astype(jnp.float32)
        expert_state = (slot_rows, gate_pre, up_pre, scaled, slot_gates)
    layer_out = after_update + moe
    saved = (
        layer_in,
        normed_all,
        q_rot,
        k_rot,
        v_heads,
        log_total,
        mixed,
        after_update,
        normed_ffn,
        own_gates,
        expert_state,
    )
    return (layer_out, saved)


def backward_layer(number, layer_grad, saved, picking, weights, experts):
    attn_scale, ffn_scale, qkv_w, out_w, router_w = weights
    chosen, pick, pick_t, first_expert = picking
    own, other = experts
    count = own[0].shape[0]
    blocks, rows = chosen.shape[:2]
    (
        layer_in,
        normed_all,
        q_rot,
        k_rot,
        v_heads,
        log_total,
        mixed,
        after_update,
        normed_ffn,
        own_gates,
        (slot_rows, gate_pre, up_pre, scaled, slot_gates),
    ) = saved
    if has_kernels():
        slot_grads, gate_low, up_low, gate_term, slot_out = expert_backward(
            number, low(layer_grad), pick, gate_pre, up_pre, slot_gates, own, other, 4 + number
        )
        gate_term = gate_term[:, :, :1]
    else:
        gate_w, up_w, down_w = by_layer(number, own, other)
        grad_all = lax.all_gather(low(layer_grad), TOKENS, axis=0, tiled=True)
        slot_grads = choose(pick, grad_all.reshape(blocks, rows, -1), count)
        plain_grad = each_dot("ecd,efd->ecf", slot_grads, down_w)
        sigmoid = jax.nn.sigmoid(gate_pre)
        activated = gate_pre * sigmoid
        gate_term = jnp.sum(plain_grad * (activated * up_pre), axis=2, keepdims=True)
        hidden_grad = slot_gates * plain_grad
        gate_low = low(hidden_grad * up_pre * sigmoid * (1.0 + gate_pre * (1.0 - sigmoid)))
        up_low = low(hidden_grad * activated)
        slot_out = low(
            each_dot("ecf,edf->ecd", gate_low, gate_w) + each_dot("ecf,edf->ecd", up_low, up_w)
        )
    expert_grads = (
        low(each_dot("ecd,ecf->edf", slot_rows, gate_low)),
        low(each_dot("ecd,ecf->edf", slot_rows, up_low)),
        low(each_dot("ecf,ecd->efd", scaled, slot_grads)),
    )
    slot_out, *expert_grads = lax.optimization_barrier((slot_out, *expert_grads))
    if has_kernels():
        normed_grad = combine(pick_t, slot_out, 3)
    else:
        normed_grad = lax.psum_scatter(
            give_back(pick_t, slot_out), TOKENS, scatter_dimension=0, tiled=True
        ).astype(jnp.float32)
    by_slot = jnp.transpose(gate_term.reshape(count, blocks, CAP), (1, 0, 2))
    gate_terms = jnp.sum(
        pick.reshape(blocks, count, CAP, rows).astype(jnp.float32) * by_slot[..., None], axis=2
    )
    gate_terms = lax.all_to_all(gate_terms, TOKENS, split_axis=0, concat_axis=0, tiled=True)
    gate_terms = jnp.sum(gate_terms.reshape(EXPERTS, -1, rows), axis=1).T
    logit_grad = low(
        own_gates * (gate_terms - jnp.sum(own_gates * gate_terms, axis=-1, keepdims=True))
    )
    router_grad = t_dot(normed_ffn, logit_grad)
    normed_grad = normed_grad + dot_t(logit_grad, router_w)
    after_part, ffn_gain_grad = jax.vjp(rms_norm, after_update, ffn_scale)[1](normed_grad)
    after_grad = after_part + layer_grad
    branch_all = lax.all_gather(low(after_grad), "seq", axis=0, tiled=True)
    out_grad = t_dot(mixed, branch_all)
    head_grad = low(dot_t(branch_all, out_w))
    qkv_grad = attention_backward(head_grad, q_rot, k_rot, v_heads, log_total)
    qkv_weight_grad = t_dot(normed_all, qkv_grad)
    normed_attn = low(dot_t(qkv_grad, qkv_w))
    normed_attn = lax.psum_scatter(normed_attn, "seq", scatter_dimension=0, tiled=True)
    input_part, attn_gain_grad = jax.vjp(rms_norm, layer_in, attn_scale)[1](
        normed_attn.astype(jnp.float32)
    )
    gain_grads = jnp.stack([attn_gain_grad, ffn_gain_grad])
    return (
        input_part + after_grad,
        (low(qkv_weight_grad), low(out_grad), low(router_grad), gain_grads),
        expert_grads,
    )


def by_layer(number, own, other):
    is_own = lax.axis_index("section") == number
    return jax.tree.map(lambda mine, received: jnp.where(is_own, mine, received), own, other)


def body(
    hidden_in,
    out_grad,
    attn_gain,
    ffn_gain,
    query_matrix,
    key_matrix,
    value_matrix,
    output_matrix,
    router_matrix,
    w_gate,
    w_up,
    w_down,
    routes,
):
    section = lax.axis_index("section")
    dp, seq = lax.axis_size("dp"), lax.axis_size("seq")
    seq_index = lax.axis_index("seq")
    first = section == 0
    width = hidden_in.shape[3]
    depth = query_matrix.shape[1]

    layer_in = lax.dynamic_index_in_dim(hidden_in, section, 0, keepdims=False)[0]
    top_grad = lax.dynamic_index_in_dim(out_grad, section, 0, keepdims=False)[0]
    own_routes = lax.dynamic_index_in_dim(routes[0], section, 0, keepdims=False)[0]
    other_routes = lax.dynamic_index_in_dim(routes[0], 1 - section, 0, keepdims=False)[0]

    own_group = jnp.concatenate(
        [
            matrix[0].reshape(depth, seq, -1)
            for matrix in (query_matrix, key_matrix, value_matrix)
        ],
        axis=2,
    )
    to_group = []
    for flat in range(dp * seq):
        to_group.append((flat, (flat % dp) * seq + flat // dp))
    from_group = [(target, source) for source, target in to_group]
    other_group = swap(own_group)
    own_out = lax.ppermute(output_matrix[0], TOKENS, to_group)
    other_out = swap(own_out)
    other_routes = swap(other_routes)
    small = jnp.concatenate([router_matrix[0], attn_gain[0][:, None], ffn_gain[0][:, None]], axis=1)
    small = lax.all_gather(small, ("section", "dp", "seq"), axis=0, tiled=True)
    small = small.reshape(2, width, -1)

    local = w_gate.shape[1]
    hidden_units = w_gate.shape[3]
    if local >= seq:
        count, units = local // seq, hidden_units
        start, unit_start = seq_index * count, 0
    else:
        count, units = 1, hidden_units * local // seq
        start, unit_start = seq_index * local // seq, (seq_index % (seq // local)) * units
    first_expert = lax.axis_index("dp") * local + start
    own_experts = (
        lax.dynamic_slice(w_gate[0], (start, 0, unit_start), (count, width, units)),
        lax.dynamic_slice(w_up[0], (start, 0, unit_start), (count, width, units)),
        lax.dynamic_slice(w_down[0], (start, unit_start, 0), (count, units, width)),
    )
    other_gate = swap(after(own_experts[0], other_group, other_out))
    other_up = swap(after(own_experts[1], other_gate))
    other_down = swap(after(own_experts[2], other_up))
    experts = (own_experts, (other_gate, other_up, other_down))

    weights = []
    pickings = []
    for number in range(2):
        part = by_layer(number, own_group, other_group)
        part = lax.all_to_all(part, "seq", split_axis=1, concat_axis=0, tiled=True)
        qkv_w = lax.all_gather(part.reshape(seq * depth, -1), "dp", axis=0, tiled=True)
        out_w = lax.all_gather(
            by_layer(number, own_out, other_out), "dp", axis=0, tiled=True
        )
        weights.append(
            (
                small[number, :, EXPERTS].astype(jnp.float32),
                small[number, :, EXPERTS + 1].astype(jnp.float32),
                qkv_w,
                out_w,
                small[number, :, :EXPERTS],
            )
        )
        route = by_layer(number, own_routes, other_routes)
        route_all = lax.all_gather(route, TOKENS, axis=0, tiled=False)
        pickings.append(routing(route_all, first_expert, count) + (first_expert,))

    state = layer_in.astype(jnp.float32)
    layer_states = []
    saved_layers = []
    for number in range(2):
        state, saved = forward_layer(number, state, pickings[number], weights[number], experts)
        layer_states.append(state)
        saved_layers.append(saved)
    grad = top_grad.astype(jnp.float32)
    layer_grads = [None, None]
    dense_grads = [None, None]
    expert_grads = [None, None]
    received = [[None] * 3, [None] * 3]
    for number in (1, 0):
        grad, dense_grads[number], expert_grads[number] = backward_layer(
            number, grad, saved_layers[number], pickings[number], weights[number], experts
        )
        layer_grads[number] = grad
        last = None
        for kind in range(3):
            piece = expert_grads[number][kind]
            piece = piece if last is None else after(piece, last)
            last = received[number][kind] = pass_to(piece, number)

    def own_layer(pieces):
        return jnp.where(first, pieces[0], pieces[1])

    def to_section(pieces):
        other = own_layer([pass_to(pieces[number], number) for number in range(2)])
        own = own_layer(pieces)
        return jnp.stack([jnp.where(first, own, other), jnp.where(first, other, own)])[
            None, :, None
        ]

    def summed(pieces):
        other = own_layer([pass_to(pieces[number], number) for number in range(2)])
        return own_layer(pieces).astype(jnp.float32) + other.astype(jnp.float32)

    kv_width = KV_HEADS * HEAD_DIM // seq
    q_width = GROUP * kv_width
    qkv_width = q_width + 2 * kv_width
    qkv_parts = []
    out_parts = []
    gain_parts = []
    for number in range(2):
        qkv_part, out_part, router_part, gain_part = dense_grads[number]
        qkv_part = jnp.concatenate([qkv_part, router_part], axis=1)
        qkv_part = lax.psum_scatter(qkv_part, "dp", scatter_dimension=0, tiled=True)
        qkv_part = qkv_part.reshape(seq, depth, -1)
        qkv_parts.append(
            lax.all_to_all(qkv_part, "seq", split_axis=0, concat_axis=0, tiled=True)
        )
        out_part = lax.psum_scatter(out_part, "dp", scatter_dimension=0, tiled=True)
        out_parts.append(lax.ppermute(out_part, TOKENS, from_group))
        gain_part = gain_part.reshape(2, dp * seq, depth)
        gain_part = lax.all_to_all(gain_part, TOKENS, split_axis=1, concat_axis=1, tiled=True)
        gain_parts.append(jnp.sum(gain_part, axis=1))
    qkv_sum = summed(qkv_parts)
    out_sum = summed(out_parts)
    gain_sum = summed(gain_parts)

    def columns(begin, end):
        return jnp.transpose(qkv_sum[:, :, begin:end], (1, 0, 2)).reshape(depth, -1)[None]

    expert_sums = []
    for kind in range(3):
        own = own_layer([expert_grads[number][kind] for number in range(2)])
        other = own_layer([received[number][kind] for number in range(2)])
        piece = low(own.astype(jnp.float32) + other.astype(jnp.float32))
        rows = piece.shape[1] // seq
        if local >= seq:
            piece = piece.reshape(count, seq, rows, -1)
            piece = jnp.transpose(piece, (1, 0, 2, 3))
            piece = lax.all_to_all(piece, "seq", split_axis=0, concat_axis=0, tiled=True)
            piece = piece.reshape(local, rows, -1)
        elif kind < 2:
            share = seq // local
            piece = piece.reshape(seq, rows, units)
            piece = lax.all_to_all(piece, "seq", split_axis=0, concat_axis=0, tiled=True)
            piece = piece.reshape(local, share, rows, units)
            piece = jnp.transpose(piece, (0, 2, 1, 3)).reshape(local, rows, -1)
        else:
            rows = hidden_units // seq
            piece = whole_rows(piece.reshape(-1, rows, width), seq_index, seq // local, seq)
        expert_sums.append(piece.astype(jnp.float32)[None])
    return (
        to_section(layer_states),
        to_section(layer_grads),
        gain_sum[0][None],
        gain_sum[1][None],
        columns(0, q_width),
        columns(q_width, q_width + kv_width),
        columns(q_width + kv_width, qkv_width),
        out_sum[None],
        jnp.sum(qkv_sum[:, :, qkv_width:], axis=0)[None],
        *expert_sums,
    )


def whole_rows(piece, seq_index, share, seq):
    parts = piece.shape[0]
    spread = jnp.zeros((seq,) + piece.shape[1:], piece.dtype)
    spread = lax.dynamic_update_slice_in_dim(
        spread, piece, (seq_index % share) * parts, axis=0
    )
    spread = lax.all_to_all(spread, "seq", split_axis=0, concat_axis=0, tiled=True)
    spread = spread.reshape((-1, share) + piece.shape[1:])
    return jnp.sum(spread.astype(jnp.float32), axis=1).astype(piece.dtype)


def solution(mesh):
    return jax.shard_map(
        body,
        mesh=mesh,
        in_specs=(
            P(None, "dp", "seq", None),
            P(None, "dp", "seq", None),
            P("section", ("dp", "seq")),
            P("section", ("dp", "seq")),
            P("section", ("dp", "seq"), None),
            P("section", ("dp", "seq"), None),
            P("section", ("dp", "seq"), None),
            P("section", ("dp", "seq"), None),
            P("section", ("dp", "seq"), None),
            P("section", "dp", None, None),
            P("section", "dp", None, None),
            P("section", "dp", None, None),
            P("section", None, "dp", "seq", None),
        ),
        out_specs=(
            P("section", None, "dp", "seq", None),
            P("section", None, "dp", "seq", None),
            P("section", ("dp", "seq")),
            P("section", ("dp", "seq")),
            P("section", ("dp", "seq"), None),
            P("section", ("dp", "seq"), None),
            P("section", ("dp", "seq"), None),
            P("section", ("dp", "seq"), None),
            P("section", ("dp", "seq"), None),
            P("section", "dp", "seq", None),
            P("section", "dp", "seq", None),
            P("section", "dp", "seq", None),
        ),
        check_vma=False,
    )
```

```python
import jax
import jax.numpy as jnp
from jax import lax
from jax.experimental import pallas as pl
from jax.experimental.pallas import tpu as pltpu
from jax.sharding import PartitionSpec as P

HEADS = 24
KV_HEADS = 8
HEAD_DIM = 64
TOP_K = 8
EXPERTS = 32
CAP = 80
GROUP = HEADS // KV_HEADS
TOKENS = ("dp", "seq")
MESH = pl.DeviceIdType.MESH
DMA = pltpu.SemaphoreType.DMA

epsilon = 1e-06


def dot(a, b):
    return jnp.dot(a, b, preferred_element_type=jnp.float32)


def dot_t(a, b):
    return lax.dot_general(a, b, (((1,), (1,)), ((), ())), preferred_element_type=jnp.float32)


def t_dot(a, b):
    return lax.dot_general(a, b, (((0,), (0,)), ((), ())), preferred_element_type=jnp.float32)


def low(v):
    return v.astype(jnp.bfloat16)


def swap(block):
    return lax.ppermute(block, "section", [(0, 1), (1, 0)])


def pass_to(block, section):
    return lax.ppermute(block, "section", [(1 - section, section)])


def rms_norm(values, norm_gain):
    return (
        values * lax.rsqrt(jnp.mean(values * values, axis=-1, keepdims=True) + epsilon) * norm_gain
    )


def rotary_tables(length):
    half_dim = HEAD_DIM // 2
    frequency = 10000.0 ** (-jnp.arange(half_dim, dtype=jnp.float32) * 2.0 / HEAD_DIM)
    angles = jnp.arange(length, dtype=jnp.float32)[:, None] * frequency[None, :]
    return (jnp.cos(angles)[:, None, :], jnp.sin(angles)[:, None, :])


def rotate(values, cos_table, sin_table):
    length = values.shape[0]
    split_heads = values.reshape(length, -1, HEAD_DIM)
    first_half = split_heads[..., : HEAD_DIM // 2]
    second_half = split_heads[..., HEAD_DIM // 2 :]
    turned = jnp.concatenate(
        [
            first_half * cos_table - second_half * sin_table,
            second_half * cos_table + first_half * sin_table,
        ],
        axis=-1,
    )
    return turned.reshape(length, -1)


def attention_forward(q_heads, k_heads, v_heads):
    length = q_heads.shape[0]
    local_kv = k_heads.shape[1] // HEAD_DIM
    cos_table, sin_table = rotary_tables(length)
    q_rot = low(rotate(q_heads.astype(jnp.float32), cos_table, sin_table)).reshape(
        length, local_kv, GROUP, HEAD_DIM
    )
    k_rot = low(rotate(k_heads.astype(jnp.float32), cos_table, sin_table)).reshape(
        length, local_kv, HEAD_DIM
    )
    values = v_heads.reshape(length, local_kv, HEAD_DIM)
    block_rows = min(512, length)
    outputs = []
    totals_list = []
    for first_row in range(0, length, block_rows):
        key_end = first_row + block_rows
        scores = (
            jnp.einsum(
                "qhgd,khd->hgqk",
                q_rot[first_row:key_end],
                k_rot[:key_end],
                preferred_element_type=jnp.float32,
            )
            * 0.125
        )
        causal = (first_row + jnp.arange(block_rows, dtype=jnp.int32))[:, None] >= jnp.arange(
            key_end, dtype=jnp.int32
        )[None, :]
        scores = jnp.where(causal, scores, -jnp.inf)
        row_peak = jnp.max(scores, axis=-1, keepdims=True)
        exponents = jnp.exp(scores - row_peak)
        totals = jnp.sum(exponents, axis=-1, keepdims=True)
        attended = jnp.einsum(
            "hgqk,khd->qhgd",
            low(exponents / totals),
            values[:key_end],
            preferred_element_type=jnp.float32,
        )
        outputs.append(low(attended).reshape(block_rows, -1))
        totals_list.append((row_peak + jnp.log(totals))[..., 0])
    return (jnp.concatenate(outputs, axis=0), jnp.stack(totals_list), q_rot, k_rot, values)


def attention_backward(head_grad, q_rot, k_rot, values, log_total):
    length, local_kv = q_rot.shape[:2]
    cos_table, sin_table = rotary_tables(length)
    block_rows = min(512, length)
    grad_rows = head_grad.reshape(length, local_kv, GROUP, HEAD_DIM)
    key_acc = jnp.zeros((length, local_kv, HEAD_DIM), jnp.float32)
    value_acc = jnp.zeros((length, local_kv, HEAD_DIM), jnp.float32)
    query_parts = []
    for block_number, first_row in enumerate(range(0, length, block_rows)):
        key_end = first_row + block_rows
        q_block = q_rot[first_row:key_end]
        grad_block = grad_rows[first_row:key_end]
        key_part = k_rot[:key_end]
        scores = (
            jnp.einsum("qhgd,khd->hgqk", q_block, key_part, preferred_element_type=jnp.float32)
            * 0.125
        )
        causal = (first_row + jnp.arange(block_rows, dtype=jnp.int32))[:, None] >= jnp.arange(
            key_end, dtype=jnp.int32
        )[None, :]
        scores = jnp.where(causal, scores, -jnp.inf)
        probs_full = jnp.exp(scores - log_total[block_number][..., None])
        prob_grad = jnp.einsum(
            "qhgd,khd->hgqk", grad_block, values[:key_end], preferred_element_type=jnp.float32
        )
        score_grad = probs_full * (
            prob_grad - jnp.sum(probs_full * prob_grad, axis=-1, keepdims=True)
        )
        score_low = low(score_grad)
        query_parts.append(
            jnp.einsum("hgqk,khd->qhgd", score_low, key_part, preferred_element_type=jnp.float32)
            * 0.125
        )
        key_acc = key_acc.at[:key_end].add(
            jnp.einsum("hgqk,qhgd->khd", score_low, q_block, preferred_element_type=jnp.float32)
            * 0.125
        )
        value_acc = value_acc.at[:key_end].add(
            jnp.einsum(
                "hgqk,qhgd->khd", low(probs_full), grad_block, preferred_element_type=jnp.float32
            )
        )
    query_all = jnp.concatenate(query_parts, axis=0).reshape(length, -1)
    query_grad = rotate(query_all, cos_table, -sin_table)
    key_grad = rotate(key_acc.reshape(length, -1), cos_table, -sin_table)
    return jnp.concatenate(
        [low(query_grad), low(key_grad), low(value_acc).reshape(length, -1)], axis=1
    )


def remote(src, dst, send_sem, recv_sem, **device):
    return pltpu.make_async_remote_copy(
        src_ref=src,
        dst_ref=dst,
        send_sem=send_sem,
        recv_sem=recv_sem,
        device_id=device,
        device_id_type=MESH,
    )


def greet(d, s, section=None):
    barrier = pltpu.get_barrier_semaphore()

    def signal(**device):
        pl.semaphore_signal(barrier, inc=1, device_id=device, device_id_type=MESH)

    signal(seq=s ^ 1)
    signal(seq=s ^ 2)

    @pl.when(d > 0)
    def _():
        signal(dp=d - 1)

    @pl.when(d < 3)
    def _():
        signal(dp=d + 1)

    known = 3
    if section is not None:
        signal(section=1 - section)
        known = 4
    inner = (d > 0) & (d < 3)

    @pl.when(inner)
    def _():
        pl.semaphore_wait(barrier, known + 1)

    @pl.when(jnp.logical_not(inner))
    def _():
        pl.semaphore_wait(barrier, known)


class Carried:
    def __init__(self, sections, sources, targets, sems):
        self.section = lax.axis_index("section")
        self.copies = []
        for k, (to, source, target) in enumerate(zip(sections, sources, targets)):
            copy = remote(source, target, sems.at[k, 0], sems.at[k, 1], section=1 - self.section)
            self.copies.append((to, copy))

    def start(self):
        for to, copy in self.copies:
            if to is None:
                copy.start()
            else:

                @pl.when(self.section != to)
                def _():
                    copy.start()

    def finish(self):
        for to, copy in self.copies:
            if to is None:
                copy.wait()
            else:

                @pl.when(self.section != to)
                def _():
                    copy.wait_send()

                @pl.when(self.section == to)
                def _():
                    copy.wait_recv()


def cost():
    return pl.CostEstimate(flops=80_000_000_000, bytes_accessed=100_000_000, transcendentals=0)


def gather_scratch(rows, width):
    return [
        pltpu.VMEM((16, rows, width), jnp.bfloat16),
        DMA(()),
        DMA((2, 4)),
        DMA((4,)),
        DMA((4,)),
        DMA((4,)),
        DMA((4, 2)),
        DMA((4, 2)),
    ]


def gather_blocks(x_ref, scratch, compute, carried=None):
    land, lsem, zs, zr, ys, yr, cs, cr = scratch
    d, s = lax.axis_index("dp"), lax.axis_index("seq")

    def place(z, column):
        return land.at[z * 4 + column]

    def z_copy(src, z, right):
        target = d + 1 if right else d - 1
        return remote(src, place(z, s), zs.at[int(right), z], zr.at[z], dp=target)

    def y_copy(src, z):
        return remote(src, place(z, s), ys.at[z], yr.at[z], seq=s ^ 2)

    def core_copy(src, z, across):
        column = s ^ 2 if across else s
        return remote(src, place(z, column), cs.at[z, across], cr.at[z, across], seq=s ^ 1)

    greet(d, s, None if carried is None else carried.section)
    own = pltpu.make_async_copy(x_ref, place(d, s), lsem)
    own.start()
    if carried is not None:
        carried.start()

    @pl.when(d < 3)
    def _():
        z_copy(x_ref, d, True).start()

    @pl.when(d > 0)
    def _():
        z_copy(x_ref, d, False).start()

    y_copy(x_ref, d).start()
    core_copy(x_ref, d, 0).start()
    own.wait()

    @pl.loop(0, 4)
    def _(i):
        @pl.when(i < 3)
        def _():
            left, right = d - (i + 1), d + (i + 1)

            @pl.when(left >= 0)
            def _():
                z_copy(place(left, s), left, True).wait_recv()

                @pl.when(d < 3)
                def _():
                    z_copy(place(left, s), left, True).start()

            @pl.when(right <= 3)
            def _():
                z_copy(place(right, s), right, False).wait_recv()

                @pl.when(d > 0)
                def _():
                    z_copy(place(right, s), right, False).start()

            following = d ^ (i + 1)
            y_copy(place(following, s), following).start()
            core_copy(place(following, s), following, 0).start()

        z = d ^ i
        y_copy(place(z, s ^ 2), z).wait_recv()
        core_copy(place(z, s ^ 2), z, 1).start()
        core_copy(place(z, s ^ 1), z, 0).wait_recv()
        core_copy(place(z, s ^ 3), z, 1).wait_recv()
        compute(z)

    for z in range(4):

        @pl.when((z <= d) & (d < 3))
        def _():
            z_copy(place(z, s), z, True).wait_send()

        @pl.when((z >= d) & (d > 0))
        def _():
            z_copy(place(z, s), z, False).wait_send()

        y_copy(place(z, s), z).wait_send()
        core_copy(place(z, s), z, 0).wait_send()
        core_copy(place(z, s), z, 1).wait_send()
    return land


def pick_weights(own_refs, other_refs, held, sems, own_layer):
    mine = lax.axis_index("section") == own_layer

    @pl.when(mine)
    def _():
        for k, ref in enumerate(own_refs):
            pltpu.make_async_copy(ref, held[k], sems.at[k]).start()

    @pl.when(jnp.logical_not(mine))
    def _():
        for k, ref in enumerate(other_refs):
            pltpu.make_async_copy(ref, held[k], sems.at[k]).start()

    def ready(k):
        pltpu.make_async_copy(own_refs[k], held[k], sems.at[k]).wait()

    return ready


def expert_forward_kernel(
    layer, x_ref, pick_ref, chosen_ref, router_ref, mine_ref,
    wg_own, wu_own, wd_own, wg_other, wu_other, wd_other,
    rows_out, gate_out, up_out, hidden_out, slot_gate_out, y_out,
    wg, wu, wd, rows, gate, up, hidden, slot_gate, y, wsem, osem, carry_sem, *gather
):
    count = wg.shape[0]
    carried = None
    if layer == 0:
        carried = Carried((None,), (wd_own,), (wd_other,), carry_sem)
        ready = pick_weights((wg_own, wu_own), (wg_other, wu_other), (wg, wu), wsem, layer)
    else:
        ready = pick_weights(
            (wg_own, wu_own, wd_own), (wg_other, wu_other, wd_other), (wg, wu, wd), wsem, layer
        )
    land = gather[0]
    d = lax.axis_index("dp")

    def outs(z):
        part = pl.ds(z * 4 * CAP, 4 * CAP)
        return [
            pltpu.make_async_copy(held.at[:, part], out.at[:, part], osem.at[k, z])
            for k, (held, out) in enumerate(
                ((rows, rows_out), (gate, gate_out), (up, up_out), (hidden, hidden_out), (slot_gate, slot_gate_out))
            )
        ] + [pltpu.make_async_copy(y.at[pl.ds(z * 4, 4)], y_out.at[pl.ds(z * 4, 4)], osem.at[5, z])]

    def down(z):
        part = pl.ds(z * 4 * CAP, 4 * CAP)

        @pl.loop(0, count)
        def _(j):
            result = low(dot(hidden[j, part, :], wd[j]))
            for q in range(4):
                y[z * 4 + q, pl.ds(j * CAP, CAP), :] = result[q * CAP : (q + 1) * CAP]

    def compute(z):
        @pl.when(z == d)
        def _():
            for k in range(2 if layer == 0 else 3):
                ready(k)

        for q in range(4):
            b = z * 4 + q
            picked = low(dot(pick_ref[b], land[b]))
            for j in range(count):
                rows[j, pl.ds(b * CAP, CAP), :] = picked[j * CAP : (j + 1) * CAP]
        part = pl.ds(z * 4 * CAP, 4 * CAP)

        @pl.loop(0, count)
        def _(j):
            x = rows[j, part, :]
            g = dot(x, wg[j])
            u = dot(x, wu[j])
            logits = dot(x, router_ref[...])
            for q in range(4):
                b = z * 4 + q
                slots = slice(q * CAP, (q + 1) * CAP)
                seen = dot(pick_ref[b, pl.ds(j * CAP, CAP), :], chosen_ref[b])
                masked = jnp.where(seen > 0.5, logits[slots], -1e30)
                power = jnp.exp(masked - jnp.max(masked, axis=1, keepdims=True))
                own = jnp.sum(power * mine_ref[j], axis=1, keepdims=True)
                value = own / jnp.sum(power, axis=1, keepdims=True)
                slot_gate[j, pl.ds(b * CAP, CAP), :] = jnp.broadcast_to(value, (CAP, 128))
            gate[j, part, :] = low(g)
            up[j, part, :] = low(u)
            h = low(g * jax.nn.sigmoid(g) * u * slot_gate[j, part, :][:, :1])
            hidden[j, part, :] = h

        if layer != 0:
            down(z)
        for copy in outs(z)[: 5 if layer == 0 else 6]:
            copy.start()

    gather_blocks(x_ref, gather, compute, carried)
    if layer == 0:
        carried.finish()
        ready = pick_weights((wd_own,), (wd_other,), (wd,), wsem, layer)
        ready(0)
        for z in range(4):
            down(z)
            outs(z)[5].start()
    for z in range(4):
        for copy in outs(z):
            copy.wait()


def expert_forward(layer, x, pick, chosen, router, mine, own, other, collective_id):
    count, width, units = own[0].shape
    rows = x.shape[0]
    slots = 16 * CAP
    bf = jnp.bfloat16
    anywhere = pl.BlockSpec(memory_space=pl.ANY)
    near = pl.BlockSpec(memory_space=pltpu.VMEM)
    results = [
        ((count, slots, width), bf),
        ((count, slots, units), bf),
        ((count, slots, units), bf),
        ((count, slots, units), bf),
        ((count, slots, 128), jnp.float32),
        ((16, count * CAP, width), bf),
    ]

    def kernel(*refs):
        if layer == 0:
            refs = refs[:10] + refs[16:17] + refs[10:16] + refs[17:]
        expert_forward_kernel(layer, *refs)

    shapes = [jax.ShapeDtypeStruct(*result) for result in results]
    if layer == 0:
        shapes.append(jax.ShapeDtypeStruct(own[2].shape, bf))
        other = other[:2]
    operands = (x, pick, chosen, router, mine, *own, *other)
    return pl.pallas_call(
        kernel,
        out_shape=shapes,
        in_specs=[anywhere, near, near, near, near] + [anywhere] * (len(operands) - 5),
        out_specs=[anywhere] * len(shapes),
        scratch_shapes=[pltpu.VMEM(weight.shape, bf) for weight in own]
        + [pltpu.VMEM(*result) for result in results]
        + [DMA((3,)), DMA((6, 4)), DMA((1, 2))]
        + gather_scratch(rows, width),
        compiler_params=pltpu.CompilerParams(
            collective_id=collective_id, has_side_effects=True, vmem_limit_bytes=60 << 20
        ),
        cost_estimate=cost(),
        name="expert_forward",
    )(*operands)


def combine_kernel(sections, pick_ref, y_ref, *refs):
    kept = len(sections)
    sources, out_ref, targets = refs[:kept], refs[kept], refs[kept + 1 : 2 * kept + 1]
    y, sent, own, core_in, y_in, z_in, lsem, zs, zr, ys, yr, cs, cr, carry_sem = refs[2 * kept + 1 :]
    carried = Carried(sections, sources, targets, carry_sem)
    d, s = lax.axis_index("dp"), lax.axis_index("seq")
    half = out_ref.shape[0] // 2

    def loaded(b):
        return pltpu.make_async_copy(y_ref.at[b], y.at[b], lsem.at[b])

    def column(across, other_core):
        return s ^ (2 * across) ^ other_core

    for i in range(4):
        z = d ^ (3 - i)
        for across in (1, 0):
            for other_core in (1, 0):
                loaded(z * 4 + column(across, other_core)).start()
    greet(d, s, carried.section)
    carried.start()

    def rows(k):
        return pl.ds(pl.multiple_of(k * half, half), half)

    def partial_sum(z, k, across, other_core):
        b = z * 4 + column(across, other_core)

        @pl.when(k == 0)
        def _():
            loaded(b).wait()

        return dot(pick_ref[b, rows(k), :], y[b])

    def core_copy(z, k, across):
        return remote(
            sent.at[z, across, rows(k)],
            core_in.at[z, across, rows(k)],
            cs.at[z, k, across],
            cr.at[z, k, across],
            seq=s ^ 1,
        )

    def y_copy(z, k):
        return remote(own.at[z, 1, rows(k)], y_in.at[z, rows(k)], ys.at[z, k], yr.at[z, k], seq=s ^ 2)

    def z_copy(z, k, right):
        target = d + 1 if right else d - 1
        return remote(
            own.at[z, 0, rows(k)],
            z_in.at[int(right), z, rows(k)],
            zs.at[z, k],
            zr.at[int(right), z, k],
            dp=target,
        )

    def start(i):
        z, k = d ^ (3 - i // 2), i % 2
        sent[z, 1, rows(k), :] = low(partial_sum(z, k, 1, 1))
        core_copy(z, k, 1).start()
        total = partial_sum(z, k, 1, 0)
        core_copy(z, k, 1).wait_recv()
        own[z, 1, rows(k), :] = low(total + core_in[z, 1, rows(k), :].astype(jnp.float32))
        y_copy(z, k).start()
        sent[z, 0, rows(k), :] = low(partial_sum(z, k, 0, 1))
        core_copy(z, k, 0).start()

    start(0)

    @pl.loop(0, 8)
    def _(i):
        @pl.when(i < 7)
        def _():
            start(i + 1)

        z, k = d ^ (3 - i // 2), i % 2
        total = partial_sum(z, k, 0, 0)
        core_copy(z, k, 0).wait_recv()
        total = total + core_in[z, 0, rows(k), :].astype(jnp.float32)
        y_copy(z, k).wait_recv()
        total = total + y_in[z, rows(k), :].astype(jnp.float32)

        @pl.when(z < d)
        def _():
            @pl.when(d < 3)
            def _():
                z_copy(z, k, False).wait_recv()
                own[z, 0, rows(k), :] = low(total + z_in[0, z, rows(k), :].astype(jnp.float32))

            @pl.when(d == 3)
            def _():
                own[z, 0, rows(k), :] = low(total)

            z_copy(z, k, False).start()

        @pl.when(z > d)
        def _():
            @pl.when(d > 0)
            def _():
                z_copy(z, k, True).wait_recv()
                own[z, 0, rows(k), :] = low(total + z_in[1, z, rows(k), :].astype(jnp.float32))

            @pl.when(d == 0)
            def _():
                own[z, 0, rows(k), :] = low(total)

            z_copy(z, k, True).start()

        @pl.when(z == d)
        def _():
            out_ref[rows(k), :] = total

    for k in range(2):

        @pl.when(d < 3)
        def _():
            z_copy(d, k, False).wait_recv()
            out_ref[rows(k), :] += z_in[0, d, rows(k), :].astype(jnp.float32)

        @pl.when(d > 0)
        def _():
            z_copy(d, k, True).wait_recv()
            out_ref[rows(k), :] += z_in[1, d, rows(k), :].astype(jnp.float32)

    for z in range(4):
        for k in range(2):
            core_copy(z, k, 0).wait_send()
            core_copy(z, k, 1).wait_send()
            y_copy(z, k).wait_send()

            @pl.when(z < d)
            def _():
                z_copy(z, k, False).wait_send()

            @pl.when(z > d)
            def _():
                z_copy(z, k, True).wait_send()

    carried.finish()


def combine(pick_t, y, collective_id, carry):
    rows, width = pick_t.shape[1], y.shape[2]
    anywhere = pl.BlockSpec(memory_space=pl.ANY)
    near = pl.BlockSpec(memory_space=pltpu.VMEM)
    sections = tuple(to for to, _ in carry)
    arrays = [array for _, array in carry]

    def kernel(*refs):
        combine_kernel(sections, *refs)

    def blocks(*lead):
        return pltpu.VMEM(lead + (rows, width), jnp.bfloat16)

    return pl.pallas_call(
        kernel,
        out_shape=[jax.ShapeDtypeStruct((rows, width), jnp.float32)]
        + [jax.ShapeDtypeStruct(array.shape, array.dtype) for array in arrays],
        in_specs=[near, anywhere] + [anywhere] * len(arrays),
        out_specs=[near] + [anywhere] * len(arrays),
        scratch_shapes=[
            pltpu.VMEM(y.shape, jnp.bfloat16),
            blocks(4, 2),
            blocks(4, 2),
            blocks(4, 2),
            blocks(4),
            blocks(2, 4),
            DMA((16,)),
            DMA((4, 2)),
            DMA((2, 4, 2)),
            DMA((4, 2)),
            DMA((4, 2)),
            DMA((4, 2, 2)),
            DMA((4, 2, 2)),
            DMA((max(1, len(arrays)), 2)),
        ],
        compiler_params=pltpu.CompilerParams(
            collective_id=collective_id, has_side_effects=True, vmem_limit_bytes=60 << 20
        ),
        cost_estimate=cost(),
        name="combine",
    )(pick_t, y, *arrays)


def expert_backward_kernel(
    layer, sections, x_ref, pick_ref, gate_in, up_in, slot_gate_in,
    wg_own, wu_own, wd_own, wg_other, wu_other, wd_other, *refs
):
    kept = len(sections)
    sources, refs = refs[:kept], refs[kept:]
    rows_out, gate_out, up_out, term_out, y_out, *refs = refs
    targets, refs = refs[:kept], refs[kept:]
    wg, wu, wd, rows, gate, up, slot_gate, y, wsem, isem, osem, carry_sem, *gather = refs
    carried = Carried(sections, sources, targets, carry_sem)
    count = wg.shape[0]
    ready = pick_weights(
        (wg_own, wu_own, wd_own), (wg_other, wu_other, wd_other), (wg, wu, wd), wsem, layer
    )
    land = gather[0]
    d = lax.axis_index("dp")
    ins = [
        pltpu.make_async_copy(src, held, isem.at[k])
        for k, (src, held) in enumerate(((gate_in, gate), (up_in, up), (slot_gate_in, slot_gate)))
    ]
    for copy in ins:
        copy.start()

    def outs(z):
        part = pl.ds(z * 4 * CAP, 4 * CAP)
        return [
            pltpu.make_async_copy(held.at[:, part], out.at[:, part], osem.at[k, z])
            for k, (held, out) in enumerate(
                ((rows, rows_out), (gate, gate_out), (up, up_out), (slot_gate, term_out))
            )
        ] + [pltpu.make_async_copy(y.at[pl.ds(z * 4, 4)], y_out.at[pl.ds(z * 4, 4)], osem.at[4, z])]

    def compute(z):
        @pl.when(z == d)
        def _():
            for k in range(3):
                ready(k)
            for copy in ins:
                copy.wait()

        for q in range(4):
            b = z * 4 + q
            picked = low(dot(pick_ref[b], land[b]))
            for j in range(count):
                rows[j, pl.ds(b * CAP, CAP), :] = picked[j * CAP : (j + 1) * CAP]
        part = pl.ds(z * 4 * CAP, 4 * CAP)

        @pl.loop(0, count)
        def _(j):
            plain = dot_t(rows[j, part, :], wd[j])
            g = gate[j, part, :].astype(jnp.float32)
            u = up[j, part, :].astype(jnp.float32)
            sigmoid = jax.nn.sigmoid(g)
            active = g * sigmoid
            term = jnp.sum(plain * (active * u), axis=1, keepdims=True)
            grad = plain * slot_gate[j, part, :][:, :1]
            dg = low(grad * u * sigmoid * (1.0 + g * (1.0 - sigmoid)))
            du = low(grad * active)
            slot_gate[j, part, :] = jnp.broadcast_to(term, (4 * CAP, 128))
            gate[j, part, :] = dg
            up[j, part, :] = du
            result = low(dot_t(dg, wg[j]) + dot_t(du, wu[j]))
            for q in range(4):
                y[z * 4 + q, pl.ds(j * CAP, CAP), :] = result[q * CAP : (q + 1) * CAP]

        for copy in outs(z):
            copy.start()

    gather_blocks(x_ref, gather, compute, carried)
    carried.finish()
    for z in range(4):
        for copy in outs(z):
            copy.wait()


def expert_backward(layer, x, pick, gate, up, slot_gate, own, other, collective_id, carry):
    count, width, units = own[0].shape
    rows = x.shape[0]
    slots = 16 * CAP
    bf = jnp.bfloat16
    anywhere = pl.BlockSpec(memory_space=pl.ANY)
    near = pl.BlockSpec(memory_space=pltpu.VMEM)
    results = [
        ((count, slots, width), bf),
        ((count, slots, units), bf),
        ((count, slots, units), bf),
        ((count, slots, 128), jnp.float32),
        ((16, count * CAP, width), bf),
    ]
    sections = tuple(to for to, _ in carry)
    arrays = [array for _, array in carry]

    def kernel(*refs):
        expert_backward_kernel(layer, sections, *refs)

    return pl.pallas_call(
        kernel,
        out_shape=[jax.ShapeDtypeStruct(*result) for result in results]
        + [jax.ShapeDtypeStruct(array.shape, array.dtype) for array in arrays],
        in_specs=[anywhere, near] + [anywhere] * (9 + len(arrays)),
        out_specs=[anywhere] * (5 + len(arrays)),
        scratch_shapes=[pltpu.VMEM(weight.shape, bf) for weight in own]
        + [pltpu.VMEM(*result) for result in results]
        + [DMA((3,)), DMA((3,)), DMA((5, 4)), DMA((max(1, len(arrays)), 2))]
        + gather_scratch(rows, width),
        compiler_params=pltpu.CompilerParams(
            collective_id=collective_id, has_side_effects=True, vmem_limit_bytes=60 << 20
        ),
        cost_estimate=cost(),
        name="expert_backward",
    )(x, pick, gate, up, slot_gate, *own, *other, *arrays)


def token_choice(route):
    return route[..., None] == jnp.arange(EXPERTS, dtype=jnp.int32)


def routing(route_all, first_expert, count):
    chosen = jnp.any(token_choice(route_all), axis=2)
    blocks, rows = chosen.shape[:2]
    mine = lax.dynamic_slice_in_dim(chosen, first_expert, count, axis=2)
    earlier = jnp.tril(jnp.ones((rows, rows), jnp.bfloat16), -1)
    place = jnp.einsum(
        "ts,bsj->bjt", earlier, mine.astype(jnp.bfloat16), preferred_element_type=jnp.float32
    ).astype(jnp.int32)
    mine = jnp.transpose(mine, (0, 2, 1))
    place = jnp.where(mine, place, -1)
    slots = jnp.arange(CAP, dtype=jnp.int32)
    pick = low(place[:, :, None, :] == slots[None, None, :, None]).reshape(blocks, -1, rows)
    return chosen, pick, jnp.transpose(pick, (0, 2, 1))


def choose(pick, rows, count):
    picked = jnp.einsum("bct,btd->bcd", pick, rows, preferred_element_type=jnp.float32)
    blocks = pick.shape[0]
    picked = low(picked).reshape(blocks, count, CAP, -1)
    return jnp.transpose(picked, (1, 0, 2, 3)).reshape(count, blocks * CAP, -1)


def give_back(pick_t, slot_rows):
    blocks, rows = pick_t.shape[:2]
    count, _, width = slot_rows.shape
    slot_rows = jnp.transpose(slot_rows.reshape(count, blocks, CAP, width), (1, 0, 2, 3))
    slot_rows = slot_rows.reshape(blocks, count * CAP, width)
    total = jnp.einsum("btc,bcd->btd", pick_t, slot_rows, preferred_element_type=jnp.float32)
    return low(total).reshape(-1, width)


def each_dot(form, a, b):
    return jnp.einsum(form, a, b, preferred_element_type=jnp.float32)


def after(value, *others):
    return lax.optimization_barrier((value, *others))[0]


def has_kernels():
    return lax.axis_size("dp") == 4 and lax.axis_size("seq") == 4


def forward_layer(number, layer_in, picking, weights, experts):
    attn_scale, ffn_scale, qkv_w, out_w, router_w = weights
    chosen, pick, pick_t, first_expert = picking
    own, other = experts
    count = own[0].shape[0]
    blocks, rows = chosen.shape[:2]
    normed_input = low(rms_norm(layer_in, attn_scale))
    normed_all = lax.all_gather(normed_input, "seq", axis=0, tiled=True)
    qkv = low(dot(normed_all, qkv_w))
    kv_width = KV_HEADS * HEAD_DIM // lax.axis_size("seq")
    q_width = GROUP * kv_width
    mixed, log_total, q_rot, k_rot, v_heads = attention_forward(
        qkv[:, :q_width], qkv[:, q_width : q_width + kv_width], qkv[:, q_width + kv_width :]
    )
    branch = lax.psum_scatter(low(dot(mixed, out_w)), "seq", scatter_dimension=0, tiled=True)
    after_update = layer_in + branch.astype(jnp.float32)
    normed_ffn = low(rms_norm(after_update, ffn_scale))
    own_block = lax.axis_index("dp") * lax.axis_size("seq") + lax.axis_index("seq")
    own_chosen = lax.dynamic_index_in_dim(chosen, own_block, 0, keepdims=False)
    own_logits = jnp.where(own_chosen, dot(normed_ffn, router_w), -jnp.inf)
    own_gates = jax.nn.softmax(own_logits, axis=-1)
    mine = (
        jnp.arange(EXPERTS)[None, None, :] == first_expert + jnp.arange(count)[:, None, None]
    ).astype(jnp.float32)
    if has_kernels():
        *expert_state, slot_out = expert_forward(
            number, normed_ffn, pick, low(chosen), router_w, mine, own, other, 1 + number
        )
        if number == 0:
            *expert_state, slot_out, other_down = (*expert_state, slot_out)
            other = other[:2] + (other_down,)
    else:
        if number == 0:
            other = other[:2] + (swap(own[2]),)
        gate_w, up_w, down_w = by_layer(number, own, other)
        ffn_all = lax.all_gather(normed_ffn, TOKENS, axis=0, tiled=True)
        logits = dot(ffn_all, router_w).reshape(blocks, rows, EXPERTS)
        gates = jax.nn.softmax(jnp.where(chosen, logits, -jnp.inf), axis=-1)
        slot_rows = choose(pick, ffn_all.reshape(blocks, rows, -1), count)
        mine_gates = jnp.einsum("bte,jxe->bjt", gates, mine, precision=lax.Precision.HIGHEST)
        slot_gates = jnp.sum(
            pick.reshape(blocks, count, CAP, rows).astype(jnp.float32) * mine_gates[:, :, None, :],
            axis=3,
        )
        slot_gates = jnp.transpose(slot_gates, (1, 0, 2)).reshape(count, -1, 1)
        gate_pre = each_dot("ecd,edf->ecf", slot_rows, gate_w)
        up_pre = each_dot("ecd,edf->ecf", slot_rows, up_w)
        scaled = low(slot_gates * jax.nn.silu(gate_pre) * up_pre)
        slot_out = low(each_dot("ecf,efd->ecd", scaled, down_w))
        expert_state = (slot_rows, gate_pre, up_pre, scaled, slot_gates)
    saved = (
        layer_in,
        normed_all,
        q_rot,
        k_rot,
        v_heads,
        log_total,
        mixed,
        after_update,
        normed_ffn,
        own_gates,
        expert_state,
    )
    return (after_update, slot_out, saved, (own, other))


def token_sums(pick_t, slot_out, collective_id, *carry):
    if has_kernels():
        sums, *received = combine(pick_t, slot_out, collective_id, carry)
        return sums, received
    sums = lax.psum_scatter(give_back(pick_t, slot_out), TOKENS, scatter_dimension=0, tiled=True)
    return sums.astype(jnp.float32), [pass_to(array, to) for to, array in carry]


def expert_gradients(number, layer_grad, saved, picking, experts, *carry):
    chosen, pick, pick_t, first_expert = picking
    own, other = experts
    count = own[0].shape[0]
    blocks, rows = chosen.shape[:2]
    slot_rows, gate_pre, up_pre, scaled, slot_gates = saved[-1]
    if has_kernels():
        slot_grads, gate_low, up_low, gate_term, slot_out, *received = expert_backward(
            number, low(layer_grad), pick, gate_pre, up_pre, slot_gates, own, other, 4 + number, carry
        )
        gate_term = gate_term[:, :, :1]
    else:
        gate_w, up_w, down_w = by_layer(number, own, other)
        grad_all = lax.all_gather(low(layer_grad), TOKENS, axis=0, tiled=True)
        slot_grads = choose(pick, grad_all.reshape(blocks, rows, -1), count)
        plain_grad = each_dot("ecd,efd->ecf", slot_grads, down_w)
        sigmoid = jax.nn.sigmoid(gate_pre)
        activated = gate_pre * sigmoid
        gate_term = jnp.sum(plain_grad * (activated * up_pre), axis=2, keepdims=True)
        hidden_grad = slot_gates * plain_grad
        gate_low = low(hidden_grad * up_pre * sigmoid * (1.0 + gate_pre * (1.0 - sigmoid)))
        up_low = low(hidden_grad * activated)
        slot_out = low(
            each_dot("ecf,edf->ecd", gate_low, gate_w) + each_dot("ecf,edf->ecd", up_low, up_w)
        )
        received = [pass_to(array, to) for to, array in carry]
    expert_grads = (
        low(each_dot("ecd,ecf->edf", slot_rows, gate_low)),
        low(each_dot("ecd,ecf->edf", slot_rows, up_low)),
        low(each_dot("ecf,ecd->efd", scaled, slot_grads)),
    )
    slot_out, *expert_grads = lax.optimization_barrier((slot_out, *expert_grads))
    return slot_out, gate_term, expert_grads, received


def backward_layer(layer_grad, normed_grad, gate_term, saved, picking, weights):
    attn_scale, ffn_scale, qkv_w, out_w, router_w = weights
    chosen, pick, _, _ = picking
    (
        layer_in,
        normed_all,
        q_rot,
        k_rot,
        v_heads,
        log_total,
        mixed,
        after_update,
        normed_ffn,
        own_gates,
        _,
    ) = saved
    blocks, rows = chosen.shape[:2]
    count = gate_term.shape[0]
    by_slot = jnp.transpose(gate_term.reshape(count, blocks, CAP), (1, 0, 2))
    gate_terms = jnp.sum(
        pick.reshape(blocks, count, CAP, rows).astype(jnp.float32) * by_slot[..., None], axis=2
    )
    gate_terms = lax.all_to_all(gate_terms, TOKENS, split_axis=0, concat_axis=0, tiled=True)
    gate_terms = jnp.sum(gate_terms.reshape(EXPERTS, -1, rows), axis=1).T
    logit_grad = low(
        own_gates * (gate_terms - jnp.sum(own_gates * gate_terms, axis=-1, keepdims=True))
    )
    router_grad = t_dot(normed_ffn, logit_grad)
    normed_grad = normed_grad + dot_t(logit_grad, router_w)
    after_part, ffn_gain_grad = jax.vjp(rms_norm, after_update, ffn_scale)[1](normed_grad)
    after_grad = after_part + layer_grad
    branch_all = lax.all_gather(low(after_grad), "seq", axis=0, tiled=True)
    out_grad = t_dot(mixed, branch_all)
    head_grad = low(dot_t(branch_all, out_w))
    qkv_grad = attention_backward(head_grad, q_rot, k_rot, v_heads, log_total)
    qkv_weight_grad = t_dot(normed_all, qkv_grad)
    normed_attn = low(dot_t(qkv_grad, qkv_w))
    normed_attn = lax.psum_scatter(normed_attn, "seq", scatter_dimension=0, tiled=True)
    input_part, attn_gain_grad = jax.vjp(rms_norm, layer_in, attn_scale)[1](
        normed_attn.astype(jnp.float32)
    )
    gain_grads = jnp.stack([attn_gain_grad, ffn_gain_grad])
    return (
        input_part + after_grad,
        (low(qkv_weight_grad), low(out_grad), low(router_grad), gain_grads),
    )


def by_layer(number, own, other):
    is_own = lax.axis_index("section") == number
    return jax.tree.map(lambda mine, received: jnp.where(is_own, mine, received), own, other)


def body(
    hidden_in,
    out_grad,
    attn_gain,
    ffn_gain,
    query_matrix,
    key_matrix,
    value_matrix,
    output_matrix,
    router_matrix,
    w_gate,
    w_up,
    w_down,
    routes,
):
    section = lax.axis_index("section")
    dp, seq = lax.axis_size("dp"), lax.axis_size("seq")
    seq_index = lax.axis_index("seq")
    first = section == 0
    width = hidden_in.shape[3]
    depth = query_matrix.shape[1]

    layer_in = lax.dynamic_index_in_dim(hidden_in, section, 0, keepdims=False)[0]
    top_grad = lax.dynamic_index_in_dim(out_grad, section, 0, keepdims=False)[0]
    own_group = jnp.concatenate(
        [
            matrix[0].reshape(depth, seq, -1)
            for matrix in (query_matrix, key_matrix, value_matrix)
        ],
        axis=2,
    )
    to_group = []
    for flat in range(dp * seq):
        to_group.append((flat, (flat % dp) * seq + flat // dp))
    from_group = [(target, source) for source, target in to_group]
    other_group = swap(own_group)
    own_out = lax.ppermute(output_matrix[0], TOKENS, to_group)
    other_out = swap(own_out)
    small = jnp.concatenate([router_matrix[0].T, attn_gain, ffn_gain], axis=0).reshape(-1)
    known = small.shape[0]
    wide = jnp.concatenate(
        [low(routes[0, :, 0].reshape(-1)), small, jnp.zeros((-known % 4096,), jnp.bfloat16)]
    )
    wide = lax.all_gather(wide.reshape(-1, 256), ("section", "dp", "seq"), axis=0, tiled=True)
    wide = wide.reshape(2, dp * seq, -1)
    paths = wide[:, :, : routes[0].size].reshape(2, dp * seq, 2, -1, TOP_K)
    paths = lax.dynamic_index_in_dim(paths, section, 2, keepdims=False).astype(jnp.int32)
    small = wide[:, :, routes[0].size : routes[0].size + known]
    small = jnp.transpose(small.reshape(2, dp * seq, EXPERTS + 2, depth), (0, 2, 1, 3))
    small = small.reshape(2, EXPERTS + 2, width)

    local = w_gate.shape[1]
    hidden_units = w_gate.shape[3]
    if local >= seq:
        count, units = local // seq, hidden_units
        start, unit_start = seq_index * count, 0
    else:
        count, units = 1, hidden_units * local // seq
        start, unit_start = seq_index * local // seq, (seq_index % (seq // local)) * units
    first_expert = lax.axis_index("dp") * local + start
    own_experts = (
        lax.dynamic_slice(w_gate[0], (start, 0, unit_start), (count, width, units)),
        lax.dynamic_slice(w_up[0], (start, 0, unit_start), (count, width, units)),
        lax.dynamic_slice(w_down[0], (start, unit_start, 0), (count, units, width)),
    )
    other_gate = swap(after(own_experts[0], other_group))
    other_up = swap(after(own_experts[1], other_gate))
    experts = (own_experts, (other_gate, other_up))

    weights = []
    pickings = []
    for number in range(2):
        part = by_layer(number, own_group, other_group)
        part = lax.all_to_all(part, "seq", split_axis=1, concat_axis=0, tiled=True)
        qkv_w = lax.all_gather(part.reshape(seq * depth, -1), "dp", axis=0, tiled=True)
        out_w = lax.all_gather(
            by_layer(number, own_out, other_out), "dp", axis=0, tiled=True
        )
        weights.append(
            (
                small[number, EXPERTS].astype(jnp.float32),
                small[number, EXPERTS + 1].astype(jnp.float32),
                qkv_w,
                out_w,
                small[number, :EXPERTS].T,
            )
        )
        pickings.append(routing(paths[number], first_expert, count) + (first_expert,))

    first_in = layer_in.astype(jnp.float32)
    updated, slot_out, first_saved, experts = forward_layer(
        0, first_in, pickings[0], weights[0], experts
    )
    sums, _ = token_sums(pickings[0][2], slot_out, 3)
    first_out = updated + sums
    second_updated, second_slots, second_saved, experts = forward_layer(
        1, first_out, pickings[1], weights[1], experts
    )
    received = [[None] * 3, [None] * 3]
    top_grad = top_grad.astype(jnp.float32)
    slot_out, gate_term, second_experts, _ = expert_gradients(
        1, top_grad, second_saved, pickings[1], experts
    )
    sums, (received[1][0],) = token_sums(pickings[1][2], slot_out, 6, (1, second_experts[0]))
    middle_grad, second_dense = backward_layer(
        top_grad, sums, gate_term, second_saved, pickings[1], weights[1]
    )
    slot_out, gate_term, first_experts, (received[1][1],) = expert_gradients(
        0, middle_grad, first_saved, pickings[0], experts, (1, second_experts[1])
    )
    sums, (received[0][0], received[1][2]) = token_sums(
        pickings[0][2], slot_out, 7, (0, first_experts[0]), (1, second_experts[2])
    )
    received[0][1] = pass_to(after(first_experts[1], received[0][0]), 0)
    bottom_grad, first_dense = backward_layer(
        middle_grad, sums, gate_term, first_saved, pickings[0], weights[0]
    )
    second_slots = after(second_slots, received[0][1], bottom_grad)
    sums, (received[0][2],) = token_sums(
        pickings[1][2], second_slots, 8, (0, first_experts[2])
    )
    layer_states = [first_out, second_updated + sums]
    layer_grads = [bottom_grad, middle_grad]
    dense_grads = [first_dense, second_dense]
    expert_grads = [first_experts, second_experts]

    def own_layer(pieces):
        return jnp.where(first, pieces[0], pieces[1])

    def to_section(pieces):
        other = own_layer([pass_to(pieces[number], number) for number in range(2)])
        own = own_layer(pieces)
        return jnp.stack([jnp.where(first, own, other), jnp.where(first, other, own)])[
            None, :, None
        ]

    def summed(pieces):
        other = own_layer([pass_to(pieces[number], number) for number in range(2)])
        return own_layer(pieces).astype(jnp.float32) + other.astype(jnp.float32)

    kv_width = KV_HEADS * HEAD_DIM // seq
    q_width = GROUP * kv_width
    qkv_width = q_width + 2 * kv_width
    qkv_parts = []
    out_parts = []
    gain_parts = []
    for number in range(2):
        qkv_part, out_part, router_part, gain_part = dense_grads[number]
        qkv_part = jnp.concatenate([qkv_part, router_part], axis=1)
        qkv_part = lax.psum_scatter(qkv_part, "dp", scatter_dimension=0, tiled=True)
        qkv_part = qkv_part.reshape(seq, depth, -1)
        qkv_parts.append(
            lax.all_to_all(qkv_part, "seq", split_axis=0, concat_axis=0, tiled=True)
        )
        out_part = lax.psum_scatter(out_part, "dp", scatter_dimension=0, tiled=True)
        out_parts.append(lax.ppermute(out_part, TOKENS, from_group))
        gain_part = gain_part.reshape(2, dp * seq, depth)
        gain_part = lax.all_to_all(gain_part, TOKENS, split_axis=1, concat_axis=1, tiled=True)
        gain_parts.append(jnp.sum(gain_part, axis=1))
    qkv_sum = summed(qkv_parts)
    out_sum = summed(out_parts)
    gain_sum = summed(gain_parts)

    def columns(begin, end):
        return jnp.transpose(qkv_sum[:, :, begin:end], (1, 0, 2)).reshape(depth, -1)[None]

    expert_sums = []
    for kind in range(3):
        own = own_layer([expert_grads[number][kind] for number in range(2)])
        other = own_layer([received[number][kind] for number in range(2)])
        piece = low(own.astype(jnp.float32) + other.astype(jnp.float32))
        rows = piece.shape[1] // seq
        if local >= seq:
            piece = piece.reshape(count, seq, rows, -1)
            piece = jnp.transpose(piece, (1, 0, 2, 3))
            piece = lax.all_to_all(piece, "seq", split_axis=0, concat_axis=0, tiled=True)
            piece = piece.reshape(local, rows, -1)
        elif kind < 2:
            share = seq // local
            piece = piece.reshape(seq, rows, units)
            piece = lax.all_to_all(piece, "seq", split_axis=0, concat_axis=0, tiled=True)
            piece = piece.reshape(local, share, rows, units)
            piece = jnp.transpose(piece, (0, 2, 1, 3)).reshape(local, rows, -1)
        else:
            rows = hidden_units // seq
            piece = whole_rows(piece.reshape(-1, rows, width), seq_index, seq // local, seq)
        expert_sums.append(piece.astype(jnp.float32)[None])
    return (
        to_section(layer_states),
        to_section(layer_grads),
        gain_sum[0][None],
        gain_sum[1][None],
        columns(0, q_width),
        columns(q_width, q_width + kv_width),
        columns(q_width + kv_width, qkv_width),
        out_sum[None],
        jnp.sum(qkv_sum[:, :, qkv_width:], axis=0)[None],
        *expert_sums,
    )


def whole_rows(piece, seq_index, share, seq):
    parts = piece.shape[0]
    spread = jnp.zeros((seq,) + piece.shape[1:], piece.dtype)
    spread = lax.dynamic_update_slice_in_dim(
        spread, piece, (seq_index % share) * parts, axis=0
    )
    spread = lax.all_to_all(spread, "seq", split_axis=0, concat_axis=0, tiled=True)
    spread = spread.reshape((-1, share) + piece.shape[1:])
    return jnp.sum(spread.astype(jnp.float32), axis=1).astype(piece.dtype)


def solution(mesh):
    return jax.shard_map(
        body,
        mesh=mesh,
        in_specs=(
            P(None, "dp", "seq", None),
            P(None, "dp", "seq", None),
            P("section", ("dp", "seq")),
            P("section", ("dp", "seq")),
            P("section", ("dp", "seq"), None),
            P("section", ("dp", "seq"), None),
            P("section", ("dp", "seq"), None),
            P("section", ("dp", "seq"), None),
            P("section", ("dp", "seq"), None),
            P("section", "dp", None, None),
            P("section", "dp", None, None),
            P("section", "dp", None, None),
            P("section", None, "dp", "seq", None),
        ),
        out_specs=(
            P("section", None, "dp", "seq", None),
            P("section", None, "dp", "seq", None),
            P("section", ("dp", "seq")),
            P("section", ("dp", "seq")),
            P("section", ("dp", "seq"), None),
            P("section", ("dp", "seq"), None),
            P("section", ("dp", "seq"), None),
            P("section", ("dp", "seq"), None),
            P("section", ("dp", "seq"), None),
            P("section", "dp", "seq", None),
            P("section", "dp", "seq", None),
            P("section", "dp", "seq", None),
        ),
        check_vma=False,
    )
```

```python
import jax
import jax.numpy as jnp
from jax import lax
from jax.experimental import pallas as pl
from jax.experimental.pallas import tpu as pltpu
from jax.sharding import PartitionSpec as P

HEADS = 24
KV_HEADS = 8
HEAD_DIM = 64
TOP_K = 8
EXPERTS = 32
CAP = 80
GROUP = HEADS // KV_HEADS
TOKENS = ("dp", "seq")
MESH = pl.DeviceIdType.MESH
DMA = pltpu.SemaphoreType.DMA

epsilon = 1e-06


def dot(a, b):
    return jnp.dot(a, b, preferred_element_type=jnp.float32)


def dot_t(a, b):
    return lax.dot_general(a, b, (((1,), (1,)), ((), ())), preferred_element_type=jnp.float32)


def t_dot(a, b):
    return lax.dot_general(a, b, (((0,), (0,)), ((), ())), preferred_element_type=jnp.float32)


def low(v):
    return v.astype(jnp.bfloat16)


def swap(block):
    return lax.ppermute(block, "section", [(0, 1), (1, 0)])


def pass_to(block, section):
    return lax.ppermute(block, "section", [(1 - section, section)])


def rms_norm(values, norm_gain):
    return (
        values * lax.rsqrt(jnp.mean(values * values, axis=-1, keepdims=True) + epsilon) * norm_gain
    )


def rotary_tables(length):
    half_dim = HEAD_DIM // 2
    frequency = 10000.0 ** (-jnp.arange(half_dim, dtype=jnp.float32) * 2.0 / HEAD_DIM)
    angles = jnp.arange(length, dtype=jnp.float32)[:, None] * frequency[None, :]
    return (jnp.cos(angles)[:, None, :], jnp.sin(angles)[:, None, :])


def rotate(values, cos_table, sin_table):
    length = values.shape[0]
    split_heads = values.reshape(length, -1, HEAD_DIM)
    first_half = split_heads[..., : HEAD_DIM // 2]
    second_half = split_heads[..., HEAD_DIM // 2 :]
    turned = jnp.concatenate(
        [
            first_half * cos_table - second_half * sin_table,
            second_half * cos_table + first_half * sin_table,
        ],
        axis=-1,
    )
    return turned.reshape(length, -1)


def attention_forward(q_heads, k_heads, v_heads):
    length = q_heads.shape[0]
    local_kv = k_heads.shape[1] // HEAD_DIM
    cos_table, sin_table = rotary_tables(length)
    q_rot = low(rotate(q_heads.astype(jnp.float32), cos_table, sin_table)).reshape(
        length, local_kv, GROUP, HEAD_DIM
    )
    k_rot = low(rotate(k_heads.astype(jnp.float32), cos_table, sin_table)).reshape(
        length, local_kv, HEAD_DIM
    )
    values = v_heads.reshape(length, local_kv, HEAD_DIM)
    block_rows = min(512, length)
    outputs = []
    totals_list = []
    for first_row in range(0, length, block_rows):
        key_end = first_row + block_rows
        scores = (
            jnp.einsum(
                "qhgd,khd->hgqk",
                q_rot[first_row:key_end],
                k_rot[:key_end],
                preferred_element_type=jnp.float32,
            )
            * 0.125
        )
        causal = (first_row + jnp.arange(block_rows, dtype=jnp.int32))[:, None] >= jnp.arange(
            key_end, dtype=jnp.int32
        )[None, :]
        scores = jnp.where(causal, scores, -jnp.inf)
        row_peak = jnp.max(scores, axis=-1, keepdims=True)
        exponents = jnp.exp(scores - row_peak)
        totals = jnp.sum(exponents, axis=-1, keepdims=True)
        attended = jnp.einsum(
            "hgqk,khd->qhgd",
            low(exponents / totals),
            values[:key_end],
            preferred_element_type=jnp.float32,
        )
        outputs.append(low(attended).reshape(block_rows, -1))
        totals_list.append((row_peak + jnp.log(totals))[..., 0])
    return (jnp.concatenate(outputs, axis=0), jnp.stack(totals_list), q_rot, k_rot, values)


def attention_backward(head_grad, q_rot, k_rot, values, log_total):
    length, local_kv = q_rot.shape[:2]
    cos_table, sin_table = rotary_tables(length)
    block_rows = min(512, length)
    grad_rows = head_grad.reshape(length, local_kv, GROUP, HEAD_DIM)
    key_acc = jnp.zeros((length, local_kv, HEAD_DIM), jnp.float32)
    value_acc = jnp.zeros((length, local_kv, HEAD_DIM), jnp.float32)
    query_parts = []
    for block_number, first_row in enumerate(range(0, length, block_rows)):
        key_end = first_row + block_rows
        q_block = q_rot[first_row:key_end]
        grad_block = grad_rows[first_row:key_end]
        key_part = k_rot[:key_end]
        scores = (
            jnp.einsum("qhgd,khd->hgqk", q_block, key_part, preferred_element_type=jnp.float32)
            * 0.125
        )
        causal = (first_row + jnp.arange(block_rows, dtype=jnp.int32))[:, None] >= jnp.arange(
            key_end, dtype=jnp.int32
        )[None, :]
        scores = jnp.where(causal, scores, -jnp.inf)
        probs_full = jnp.exp(scores - log_total[block_number][..., None])
        prob_grad = jnp.einsum(
            "qhgd,khd->hgqk", grad_block, values[:key_end], preferred_element_type=jnp.float32
        )
        score_grad = probs_full * (
            prob_grad - jnp.sum(probs_full * prob_grad, axis=-1, keepdims=True)
        )
        score_low = low(score_grad)
        query_parts.append(
            jnp.einsum("hgqk,khd->qhgd", score_low, key_part, preferred_element_type=jnp.float32)
            * 0.125
        )
        key_acc = key_acc.at[:key_end].add(
            jnp.einsum("hgqk,qhgd->khd", score_low, q_block, preferred_element_type=jnp.float32)
            * 0.125
        )
        value_acc = value_acc.at[:key_end].add(
            jnp.einsum(
                "hgqk,qhgd->khd", low(probs_full), grad_block, preferred_element_type=jnp.float32
            )
        )
    query_all = jnp.concatenate(query_parts, axis=0).reshape(length, -1)
    query_grad = rotate(query_all, cos_table, -sin_table)
    key_grad = rotate(key_acc.reshape(length, -1), cos_table, -sin_table)
    return jnp.concatenate(
        [low(query_grad), low(key_grad), low(value_acc).reshape(length, -1)], axis=1
    )


def remote(src, dst, send_sem, recv_sem, **device):
    return pltpu.make_async_remote_copy(
        src_ref=src,
        dst_ref=dst,
        send_sem=send_sem,
        recv_sem=recv_sem,
        device_id=device,
        device_id_type=MESH,
    )


def greet(d, s, section=None):
    barrier = pltpu.get_barrier_semaphore()

    def signal(**device):
        pl.semaphore_signal(barrier, inc=1, device_id=device, device_id_type=MESH)

    signal(seq=s ^ 1)
    signal(seq=s ^ 2)

    @pl.when(d > 0)
    def _():
        signal(dp=d - 1)

    @pl.when(d < 3)
    def _():
        signal(dp=d + 1)

    known = 3
    if section is not None:
        signal(section=1 - section)
        known = 4
    inner = (d > 0) & (d < 3)

    @pl.when(inner)
    def _():
        pl.semaphore_wait(barrier, known + 1)

    @pl.when(jnp.logical_not(inner))
    def _():
        pl.semaphore_wait(barrier, known)


class Carried:
    def __init__(self, sections, sources, targets, sems):
        self.section = lax.axis_index("section")
        self.copies = []
        for k, (to, source, target) in enumerate(zip(sections, sources, targets)):
            copy = remote(source, target, sems.at[k, 0], sems.at[k, 1], section=1 - self.section)
            self.copies.append((to, copy))

    def start(self):
        for to, copy in self.copies:
            if to is None:
                copy.start()
            else:

                @pl.when(self.section != to)
                def _():
                    copy.start()

    def finish(self):
        for to, copy in self.copies:
            if to is None:
                copy.wait()
            else:

                @pl.when(self.section != to)
                def _():
                    copy.wait_send()

                @pl.when(self.section == to)
                def _():
                    copy.wait_recv()


def cost():
    return pl.CostEstimate(flops=80_000_000_000, bytes_accessed=100_000_000, transcendentals=0)


def gather_scratch(rows, width):
    return [
        pltpu.VMEM((16, rows, width), jnp.bfloat16),
        DMA(()),
        DMA((2, 4)),
        DMA((4,)),
        DMA((4,)),
        DMA((4,)),
        DMA((4, 2)),
        DMA((4, 2)),
    ]


def gather_blocks(x_ref, scratch, compute, carried=None):
    land, lsem, zs, zr, ys, yr, cs, cr = scratch
    d, s = lax.axis_index("dp"), lax.axis_index("seq")

    def place(z, column):
        return land.at[z * 4 + column]

    def z_copy(src, z, right):
        target = d + 1 if right else d - 1
        return remote(src, place(z, s), zs.at[int(right), z], zr.at[z], dp=target)

    def y_copy(src, z):
        return remote(src, place(z, s), ys.at[z], yr.at[z], seq=s ^ 2)

    def core_copy(src, z, across):
        column = s ^ 2 if across else s
        return remote(src, place(z, column), cs.at[z, across], cr.at[z, across], seq=s ^ 1)

    greet(d, s, None if carried is None else carried.section)
    own = pltpu.make_async_copy(x_ref, place(d, s), lsem)
    own.start()
    if carried is not None:
        carried.start()

    @pl.when(d < 3)
    def _():
        z_copy(x_ref, d, True).start()

    @pl.when(d > 0)
    def _():
        z_copy(x_ref, d, False).start()

    y_copy(x_ref, d).start()
    core_copy(x_ref, d, 0).start()
    own.wait()

    @pl.loop(0, 4)
    def _(i):
        @pl.when(i < 3)
        def _():
            left, right = d - (i + 1), d + (i + 1)

            @pl.when(left >= 0)
            def _():
                z_copy(place(left, s), left, True).wait_recv()

                @pl.when(d < 3)
                def _():
                    z_copy(place(left, s), left, True).start()

            @pl.when(right <= 3)
            def _():
                z_copy(place(right, s), right, False).wait_recv()

                @pl.when(d > 0)
                def _():
                    z_copy(place(right, s), right, False).start()

            following = d ^ (i + 1)
            y_copy(place(following, s), following).start()
            core_copy(place(following, s), following, 0).start()

        z = d ^ i
        y_copy(place(z, s ^ 2), z).wait_recv()
        core_copy(place(z, s ^ 2), z, 1).start()
        core_copy(place(z, s ^ 1), z, 0).wait_recv()
        core_copy(place(z, s ^ 3), z, 1).wait_recv()
        compute(z)

    for z in range(4):

        @pl.when((z <= d) & (d < 3))
        def _():
            z_copy(place(z, s), z, True).wait_send()

        @pl.when((z >= d) & (d > 0))
        def _():
            z_copy(place(z, s), z, False).wait_send()

        y_copy(place(z, s), z).wait_send()
        core_copy(place(z, s), z, 0).wait_send()
        core_copy(place(z, s), z, 1).wait_send()
    return land


def gather_small(x, collective_id):
    rows, width = x.shape

    def kernel(x_ref, out_ref, *scratch):
        gather_blocks(x_ref, scratch, lambda z: None)
        out_ref[...] = scratch[0][...]

    return pl.pallas_call(
        kernel,
        out_shape=jax.ShapeDtypeStruct((16, rows, width), x.dtype),
        in_specs=[pl.BlockSpec(memory_space=pl.ANY)],
        out_specs=pl.BlockSpec(memory_space=pltpu.VMEM),
        scratch_shapes=gather_scratch(rows, width),
        compiler_params=pltpu.CompilerParams(collective_id=collective_id, has_side_effects=True),
        name="gather_small",
    )(x)


def pick_weights(own_refs, other_refs, held, sems, own_layer):
    mine = lax.axis_index("section") == own_layer

    @pl.when(mine)
    def _():
        for k, ref in enumerate(own_refs):
            pltpu.make_async_copy(ref, held[k], sems.at[k]).start()

    @pl.when(jnp.logical_not(mine))
    def _():
        for k, ref in enumerate(other_refs):
            pltpu.make_async_copy(ref, held[k], sems.at[k]).start()

    def ready(k):
        pltpu.make_async_copy(own_refs[k], held[k], sems.at[k]).wait()

    return ready


def expert_forward_kernel(
    layer, x_ref, pick_ref, chosen_ref, router_ref, mine_ref,
    wg_own, wu_own, wd_own, wg_other, wu_other, wd_other,
    rows_out, gate_out, up_out, hidden_out, slot_gate_out, y_out,
    wg, wu, wd, rows, gate, up, hidden, slot_gate, y, wsem, osem, carry_sem, *gather
):
    count = wg.shape[0]
    carried = None
    if layer == 0:
        carried = Carried((None,), (wd_own,), (wd_other,), carry_sem)
        ready = pick_weights((wg_own, wu_own), (wg_other, wu_other), (wg, wu), wsem, layer)
    else:
        ready = pick_weights(
            (wg_own, wu_own, wd_own), (wg_other, wu_other, wd_other), (wg, wu, wd), wsem, layer
        )
    land = gather[0]
    d = lax.axis_index("dp")

    def outs(z):
        part = pl.ds(z * 4 * CAP, 4 * CAP)
        return [
            pltpu.make_async_copy(held.at[:, part], out.at[:, part], osem.at[k, z])
            for k, (held, out) in enumerate(
                ((rows, rows_out), (gate, gate_out), (up, up_out), (hidden, hidden_out), (slot_gate, slot_gate_out))
            )
        ] + [pltpu.make_async_copy(y.at[pl.ds(z * 4, 4)], y_out.at[pl.ds(z * 4, 4)], osem.at[5, z])]

    def down(z):
        part = pl.ds(z * 4 * CAP, 4 * CAP)

        @pl.loop(0, count)
        def _(j):
            result = low(dot(hidden[j, part, :], wd[j]))
            for q in range(4):
                y[z * 4 + q, pl.ds(j * CAP, CAP), :] = result[q * CAP : (q + 1) * CAP]

    def compute(z):
        @pl.when(z == d)
        def _():
            for k in range(2 if layer == 0 else 3):
                ready(k)

        for q in range(4):
            b = z * 4 + q
            picked = low(dot(pick_ref[b], land[b]))
            for j in range(count):
                rows[j, pl.ds(b * CAP, CAP), :] = picked[j * CAP : (j + 1) * CAP]
        part = pl.ds(z * 4 * CAP, 4 * CAP)

        @pl.loop(0, count)
        def _(j):
            x = rows[j, part, :]
            g = dot(x, wg[j])
            u = dot(x, wu[j])
            logits = dot(x, router_ref[...])
            for q in range(4):
                b = z * 4 + q
                slots = slice(q * CAP, (q + 1) * CAP)
                seen = dot(pick_ref[b, pl.ds(j * CAP, CAP), :], chosen_ref[b])
                masked = jnp.where(seen > 0.5, logits[slots], -1e30)
                power = jnp.exp(masked - jnp.max(masked, axis=1, keepdims=True))
                own = jnp.sum(power * mine_ref[j], axis=1, keepdims=True)
                value = own / jnp.sum(power, axis=1, keepdims=True)
                slot_gate[j, pl.ds(b * CAP, CAP), :] = jnp.broadcast_to(value, (CAP, 128))
            gate[j, part, :] = low(g)
            up[j, part, :] = low(u)
            h = low(g * jax.nn.sigmoid(g) * u * slot_gate[j, part, :][:, :1])
            hidden[j, part, :] = h

        if layer != 0:
            down(z)
        for copy in outs(z)[: 5 if layer == 0 else 6]:
            copy.start()

    gather_blocks(x_ref, gather, compute, carried)
    if layer == 0:
        carried.finish()
        ready = pick_weights((wd_own,), (wd_other,), (wd,), wsem, layer)
        ready(0)
        for z in range(4):
            down(z)
            outs(z)[5].start()
    for z in range(4):
        for copy in outs(z):
            copy.wait()


def expert_forward(layer, x, pick, chosen, router, mine, own, other, collective_id):
    count, width, units = own[0].shape
    rows = x.shape[0]
    slots = 16 * CAP
    bf = jnp.bfloat16
    anywhere = pl.BlockSpec(memory_space=pl.ANY)
    near = pl.BlockSpec(memory_space=pltpu.VMEM)
    results = [
        ((count, slots, width), bf),
        ((count, slots, units), bf),
        ((count, slots, units), bf),
        ((count, slots, units), bf),
        ((count, slots, 128), jnp.float32),
        ((16, count * CAP, width), bf),
    ]

    def kernel(*refs):
        if layer == 0:
            refs = refs[:10] + refs[16:17] + refs[10:16] + refs[17:]
        expert_forward_kernel(layer, *refs)

    shapes = [jax.ShapeDtypeStruct(*result) for result in results]
    if layer == 0:
        shapes.append(jax.ShapeDtypeStruct(own[2].shape, bf))
        other = other[:2]
    operands = (x, pick, chosen, router, mine, *own, *other)
    return pl.pallas_call(
        kernel,
        out_shape=shapes,
        in_specs=[anywhere, near, near, near, near] + [anywhere] * (len(operands) - 5),
        out_specs=[anywhere] * len(shapes),
        scratch_shapes=[pltpu.VMEM(weight.shape, bf) for weight in own]
        + [pltpu.VMEM(*result) for result in results]
        + [DMA((3,)), DMA((6, 4)), DMA((1, 2))]
        + gather_scratch(rows, width),
        compiler_params=pltpu.CompilerParams(
            collective_id=collective_id, has_side_effects=True, vmem_limit_bytes=60 << 20
        ),
        cost_estimate=cost(),
        name="expert_forward",
    )(*operands)


def combine_kernel(sections, pick_ref, y_ref, *refs):
    kept = len(sections)
    sources, out_ref, targets = refs[:kept], refs[kept], refs[kept + 1 : 2 * kept + 1]
    y, sent, own, core_in, y_in, z_in, lsem, zs, zr, ys, yr, cs, cr, carry_sem = refs[2 * kept + 1 :]
    carried = Carried(sections, sources, targets, carry_sem)
    d, s = lax.axis_index("dp"), lax.axis_index("seq")
    half = out_ref.shape[0] // 2

    def loaded(b):
        return pltpu.make_async_copy(y_ref.at[b], y.at[b], lsem.at[b])

    def column(across, other_core):
        return s ^ (2 * across) ^ other_core

    for i in range(4):
        z = d ^ (3 - i)
        for across in (1, 0):
            for other_core in (1, 0):
                loaded(z * 4 + column(across, other_core)).start()
    greet(d, s, carried.section)
    carried.start()

    def rows(k):
        return pl.ds(pl.multiple_of(k * half, half), half)

    def partial_sum(z, k, across, other_core):
        b = z * 4 + column(across, other_core)

        @pl.when(k == 0)
        def _():
            loaded(b).wait()

        return dot(pick_ref[b, rows(k), :], y[b])

    def core_copy(z, k, across):
        return remote(
            sent.at[z, across, rows(k)],
            core_in.at[z, across, rows(k)],
            cs.at[z, k, across],
            cr.at[z, k, across],
            seq=s ^ 1,
        )

    def y_copy(z, k):
        return remote(own.at[z, 1, rows(k)], y_in.at[z, rows(k)], ys.at[z, k], yr.at[z, k], seq=s ^ 2)

    def z_copy(z, k, right):
        target = d + 1 if right else d - 1
        return remote(
            own.at[z, 0, rows(k)],
            z_in.at[int(right), z, rows(k)],
            zs.at[z, k],
            zr.at[int(right), z, k],
            dp=target,
        )

    def start(i):
        z, k = d ^ (3 - i // 2), i % 2
        sent[z, 1, rows(k), :] = low(partial_sum(z, k, 1, 1))
        core_copy(z, k, 1).start()
        total = partial_sum(z, k, 1, 0)
        core_copy(z, k, 1).wait_recv()
        own[z, 1, rows(k), :] = low(total + core_in[z, 1, rows(k), :].astype(jnp.float32))
        y_copy(z, k).start()
        sent[z, 0, rows(k), :] = low(partial_sum(z, k, 0, 1))
        core_copy(z, k, 0).start()

    start(0)

    @pl.loop(0, 8)
    def _(i):
        @pl.when(i < 7)
        def _():
            start(i + 1)

        z, k = d ^ (3 - i // 2), i % 2
        total = partial_sum(z, k, 0, 0)
        core_copy(z, k, 0).wait_recv()
        total = total + core_in[z, 0, rows(k), :].astype(jnp.float32)
        y_copy(z, k).wait_recv()
        total = total + y_in[z, rows(k), :].astype(jnp.float32)

        @pl.when(z < d)
        def _():
            @pl.when(d < 3)
            def _():
                z_copy(z, k, False).wait_recv()
                own[z, 0, rows(k), :] = low(total + z_in[0, z, rows(k), :].astype(jnp.float32))

            @pl.when(d == 3)
            def _():
                own[z, 0, rows(k), :] = low(total)

            z_copy(z, k, False).start()

        @pl.when(z > d)
        def _():
            @pl.when(d > 0)
            def _():
                z_copy(z, k, True).wait_recv()
                own[z, 0, rows(k), :] = low(total + z_in[1, z, rows(k), :].astype(jnp.float32))

            @pl.when(d == 0)
            def _():
                own[z, 0, rows(k), :] = low(total)

            z_copy(z, k, True).start()

        @pl.when(z == d)
        def _():
            out_ref[rows(k), :] = total

    for k in range(2):

        @pl.when(d < 3)
        def _():
            z_copy(d, k, False).wait_recv()
            out_ref[rows(k), :] += z_in[0, d, rows(k), :].astype(jnp.float32)

        @pl.when(d > 0)
        def _():
            z_copy(d, k, True).wait_recv()
            out_ref[rows(k), :] += z_in[1, d, rows(k), :].astype(jnp.float32)

    for z in range(4):
        for k in range(2):
            core_copy(z, k, 0).wait_send()
            core_copy(z, k, 1).wait_send()
            y_copy(z, k).wait_send()

            @pl.when(z < d)
            def _():
                z_copy(z, k, False).wait_send()

            @pl.when(z > d)
            def _():
                z_copy(z, k, True).wait_send()

    carried.finish()


def combine(pick_t, y, collective_id, carry):
    rows, width = pick_t.shape[1], y.shape[2]
    anywhere = pl.BlockSpec(memory_space=pl.ANY)
    near = pl.BlockSpec(memory_space=pltpu.VMEM)
    sections = tuple(to for to, _ in carry)
    arrays = [array for _, array in carry]

    def kernel(*refs):
        combine_kernel(sections, *refs)

    def blocks(*lead):
        return pltpu.VMEM(lead + (rows, width), jnp.bfloat16)

    return pl.pallas_call(
        kernel,
        out_shape=[jax.ShapeDtypeStruct((rows, width), jnp.float32)]
        + [jax.ShapeDtypeStruct(array.shape, array.dtype) for array in arrays],
        in_specs=[near, anywhere] + [anywhere] * len(arrays),
        out_specs=[near] + [anywhere] * len(arrays),
        scratch_shapes=[
            pltpu.VMEM(y.shape, jnp.bfloat16),
            blocks(4, 2),
            blocks(4, 2),
            blocks(4, 2),
            blocks(4),
            blocks(2, 4),
            DMA((16,)),
            DMA((4, 2)),
            DMA((2, 4, 2)),
            DMA((4, 2)),
            DMA((4, 2)),
            DMA((4, 2, 2)),
            DMA((4, 2, 2)),
            DMA((max(1, len(arrays)), 2)),
        ],
        compiler_params=pltpu.CompilerParams(
            collective_id=collective_id, has_side_effects=True, vmem_limit_bytes=60 << 20
        ),
        cost_estimate=cost(),
        name="combine",
    )(pick_t, y, *arrays)


def expert_backward_kernel(
    layer, sections, x_ref, pick_ref, gate_in, up_in, slot_gate_in,
    wg_own, wu_own, wd_own, wg_other, wu_other, wd_other, *refs
):
    kept = len(sections)
    sources, refs = refs[:kept], refs[kept:]
    rows_out, gate_out, up_out, term_out, y_out, *refs = refs
    targets, refs = refs[:kept], refs[kept:]
    wg, wu, wd, rows, gate, up, slot_gate, y, wsem, isem, osem, carry_sem, *gather = refs
    carried = Carried(sections, sources, targets, carry_sem)
    count = wg.shape[0]
    ready = pick_weights(
        (wg_own, wu_own, wd_own), (wg_other, wu_other, wd_other), (wg, wu, wd), wsem, layer
    )
    land = gather[0]
    d = lax.axis_index("dp")
    ins = [
        pltpu.make_async_copy(src, held, isem.at[k])
        for k, (src, held) in enumerate(((gate_in, gate), (up_in, up), (slot_gate_in, slot_gate)))
    ]
    for copy in ins:
        copy.start()

    def outs(z):
        part = pl.ds(z * 4 * CAP, 4 * CAP)
        return [
            pltpu.make_async_copy(held.at[:, part], out.at[:, part], osem.at[k, z])
            for k, (held, out) in enumerate(
                ((rows, rows_out), (gate, gate_out), (up, up_out), (slot_gate, term_out))
            )
        ] + [pltpu.make_async_copy(y.at[pl.ds(z * 4, 4)], y_out.at[pl.ds(z * 4, 4)], osem.at[4, z])]

    def compute(z):
        @pl.when(z == d)
        def _():
            for k in range(3):
                ready(k)
            for copy in ins:
                copy.wait()

        for q in range(4):
            b = z * 4 + q
            picked = low(dot(pick_ref[b], land[b]))
            for j in range(count):
                rows[j, pl.ds(b * CAP, CAP), :] = picked[j * CAP : (j + 1) * CAP]
        part = pl.ds(z * 4 * CAP, 4 * CAP)

        @pl.loop(0, count)
        def _(j):
            plain = dot_t(rows[j, part, :], wd[j])
            g = gate[j, part, :].astype(jnp.float32)
            u = up[j, part, :].astype(jnp.float32)
            sigmoid = jax.nn.sigmoid(g)
            active = g * sigmoid
            term = jnp.sum(plain * (active * u), axis=1, keepdims=True)
            grad = plain * slot_gate[j, part, :][:, :1]
            dg = low(grad * u * sigmoid * (1.0 + g * (1.0 - sigmoid)))
            du = low(grad * active)
            slot_gate[j, part, :] = jnp.broadcast_to(term, (4 * CAP, 128))
            gate[j, part, :] = dg
            up[j, part, :] = du
            result = low(dot_t(dg, wg[j]) + dot_t(du, wu[j]))
            for q in range(4):
                y[z * 4 + q, pl.ds(j * CAP, CAP), :] = result[q * CAP : (q + 1) * CAP]

        for copy in outs(z):
            copy.start()

    gather_blocks(x_ref, gather, compute, carried)
    carried.finish()
    for z in range(4):
        for copy in outs(z):
            copy.wait()


def expert_backward(layer, x, pick, gate, up, slot_gate, own, other, collective_id, carry):
    count, width, units = own[0].shape
    rows = x.shape[0]
    slots = 16 * CAP
    bf = jnp.bfloat16
    anywhere = pl.BlockSpec(memory_space=pl.ANY)
    near = pl.BlockSpec(memory_space=pltpu.VMEM)
    results = [
        ((count, slots, width), bf),
        ((count, slots, units), bf),
        ((count, slots, units), bf),
        ((count, slots, 128), jnp.float32),
        ((16, count * CAP, width), bf),
    ]
    sections = tuple(to for to, _ in carry)
    arrays = [array for _, array in carry]

    def kernel(*refs):
        expert_backward_kernel(layer, sections, *refs)

    return pl.pallas_call(
        kernel,
        out_shape=[jax.ShapeDtypeStruct(*result) for result in results]
        + [jax.ShapeDtypeStruct(array.shape, array.dtype) for array in arrays],
        in_specs=[anywhere, near] + [anywhere] * (9 + len(arrays)),
        out_specs=[anywhere] * (5 + len(arrays)),
        scratch_shapes=[pltpu.VMEM(weight.shape, bf) for weight in own]
        + [pltpu.VMEM(*result) for result in results]
        + [DMA((3,)), DMA((3,)), DMA((5, 4)), DMA((max(1, len(arrays)), 2))]
        + gather_scratch(rows, width),
        compiler_params=pltpu.CompilerParams(
            collective_id=collective_id, has_side_effects=True, vmem_limit_bytes=60 << 20
        ),
        cost_estimate=cost(),
        name="expert_backward",
    )(x, pick, gate, up, slot_gate, *own, *other, *arrays)


def rope(x, cos_table, sin_table):
    lane = lax.broadcasted_iota(jnp.int32, x.shape, 1)
    turned = jnp.where(lane % HEAD_DIM < HEAD_DIM // 2, pltpu.roll(x, 128 - HEAD_DIM // 2, 1), pltpu.roll(x, HEAD_DIM // 2, 1))
    return x * cos_table + turned * sin_table


def seq_greet(s, section):
    barrier = pltpu.get_barrier_semaphore()
    for device in (dict(seq=s ^ 1), dict(seq=s ^ 2), dict(section=1 - section)):
        pl.semaphore_signal(barrier, inc=1, device_id=device, device_id_type=MESH)
    pl.semaphore_wait(barrier, 3)


def seq_scratch(rows, width):
    return [
        pltpu.VMEM((4, rows, width), jnp.bfloat16),
        pltpu.VMEM((2, rows, width), jnp.bfloat16),
        pltpu.VMEM((2, rows, width), jnp.bfloat16),
        pltpu.VMEM((rows, width), jnp.bfloat16),
        pltpu.VMEM((rows, width), jnp.bfloat16),
        DMA(()),
        DMA((4, 2)),
        DMA((3, 2)),
    ]


class Line:
    def __init__(self, scratch):
        self.land, self.sent, self.core_in, self.y_sent, self.y_in, self.lsem, self.ag, self.rs = scratch
        self.s = lax.axis_index("seq")

    def hop(self, src, dst, sems, k, flip):
        return remote(src, dst, sems.at[k, 0], sems.at[k, 1], seq=self.s ^ flip)

    def gather(self, x_ref, use):
        s, land = self.s, self.land
        own = pltpu.make_async_copy(x_ref, land.at[s], self.lsem)
        own.start()
        over = self.hop(x_ref, land.at[s], self.ag, 0, 2)
        beside = self.hop(x_ref, land.at[s], self.ag, 1, 1)
        over.start()
        beside.start()
        own.wait()
        use(s)
        beside.wait_recv()
        use(s ^ 1)
        over.wait_recv()
        further = self.hop(land.at[s ^ 2], land.at[s ^ 2], self.ag, 2, 1)
        further.start()
        use(s ^ 2)
        further.wait_recv()
        use(s ^ 3)
        over.wait_send()
        beside.wait_send()
        further.wait_send()

    def hand_over(self, t, partial, out_ref):
        relation = t ^ self.s

        @pl.when(relation == 3)
        def _():
            self.sent[0] = low(partial[...])
            self.hop(self.sent.at[0], self.core_in.at[0], self.rs, 0, 1).start()

        @pl.when(relation == 2)
        def _():
            self.hop(self.sent.at[0], self.core_in.at[0], self.rs, 0, 1).wait_recv()
            self.y_sent[...] = low(partial[...] + self.core_in[0].astype(jnp.float32))
            self.hop(self.y_sent, self.y_in, self.rs, 1, 2).start()

        @pl.when(relation == 1)
        def _():
            self.sent[1] = low(partial[...])
            self.hop(self.sent.at[1], self.core_in.at[1], self.rs, 2, 1).start()

        @pl.when(relation == 0)
        def _():
            out_ref[...] = partial[...]

    def finish(self, out_ref):
        self.hop(self.sent.at[1], self.core_in.at[1], self.rs, 2, 1).wait()
        out_ref[...] += self.core_in[1].astype(jnp.float32)
        self.hop(self.y_sent, self.y_in, self.rs, 1, 2).wait()
        out_ref[...] += self.y_in[...].astype(jnp.float32)
        self.hop(self.sent.at[0], self.core_in.at[0], self.rs, 0, 1).wait_send()


def attention_forward_kernel(sections, x_ref, qkv_ref, wo_ref, cos_ref, sin_ref, *refs):
    kept = len(sections)
    sources, refs = refs[:kept], refs[kept:]
    out_ref, all_out, heads_out, lse_out, ot_out, *refs = refs
    targets, refs = refs[:kept], refs[kept:]
    wqkv, wo, heads, lse, ot, partial, wsem, osem, carry_sem, *line = refs
    line = Line(line)
    carried = Carried(sections, sources, targets, carry_sem)
    s = line.s
    rows = out_ref.shape[0]
    kv = heads.shape[0] // (GROUP + 2)
    queries = GROUP * kv
    loads = [pltpu.make_async_copy(qkv_ref, wqkv, wsem.at[0]), pltpu.make_async_copy(wo_ref, wo, wsem.at[1])]
    for load in loads:
        load.start()
    seq_greet(s, carried.section)
    carried.start()
    lse[...] = jnp.zeros_like(lse)

    def project(t):
        part = pl.ds(pl.multiple_of(t * rows, rows), rows)

        @pl.when(t == s)
        def _():
            loads[0].wait()

        qkv = low(dot(line.land[t], wqkv[...]))
        for chunk in range((queries + kv) // 2):
            x = qkv[:, chunk * 128 : (chunk + 1) * 128].astype(jnp.float32)
            x = low(rope(x, cos_ref[part, :], sin_ref[part, :]))
            heads[2 * chunk, part, :] = x[:, :HEAD_DIM]
            heads[2 * chunk + 1, part, :] = x[:, HEAD_DIM:]
        for j in range(kv):
            begin = (queries + kv + j) * HEAD_DIM
            heads[queries + kv + j, part, :] = qkv[:, begin : begin + HEAD_DIM]

    line.gather(x_ref, project)
    saves = [pltpu.make_async_copy(line.land, all_out, osem.at[0]), pltpu.make_async_copy(heads, heads_out, osem.at[1])]
    for save in saves:
        save.start()
    loads[1].wait()

    def attend(block):
        keys = (block + 1) * rows
        columns = slice(block * rows, (block + 1) * rows)

        @pl.loop(0, queries)
        def _(h):
            j = h // GROUP
            scores = dot_t(heads[queries + j, :keys, :], heads[h, columns, :]) * 0.125
            key_at = lax.broadcasted_iota(jnp.int32, scores.shape, 0)
            query_at = lax.broadcasted_iota(jnp.int32, scores.shape, 1) + block * rows
            scores = jnp.where(key_at <= query_at, scores, -jnp.inf)
            peak = jnp.max(scores, axis=0, keepdims=True)
            power = jnp.exp(scores - peak)
            total = jnp.sum(power, axis=0, keepdims=True)
            attended = t_dot(heads[queries + kv + j, :keys, :], low(power / total))
            ot[pl.ds(pl.multiple_of(h * HEAD_DIM, HEAD_DIM), HEAD_DIM), columns] = low(attended)
            lse[pl.ds(h, 1), columns] = peak + jnp.log(total)

        partial[...] = t_dot(ot[:, columns], wo[...])

    @pl.loop(0, 4)
    def _(i):
        t = s ^ (3 - i)
        for block in range(4):

            @pl.when(t == block)
            def _():
                attend(block)

        line.hand_over(t, partial, out_ref)

    saves += [pltpu.make_async_copy(lse, lse_out, osem.at[2]), pltpu.make_async_copy(ot, ot_out, osem.at[3])]
    for save in saves[2:]:
        save.start()
    line.finish(out_ref)
    carried.finish()
    for save in saves:
        save.wait()


def attention_forward_call(x, qkv_w, out_w, tables, collective_id, carry):
    rows, width = x.shape
    local_heads = qkv_w.shape[1] // HEAD_DIM
    bf, f32 = jnp.bfloat16, jnp.float32
    anywhere = pl.BlockSpec(memory_space=pl.ANY)
    near = pl.BlockSpec(memory_space=pltpu.VMEM)
    sections = tuple(to for to, _ in carry)
    arrays = [array for _, array in carry]
    results = [
        ((rows, width), f32),
        ((4, rows, width), bf),
        ((local_heads, 4 * rows, HEAD_DIM), bf),
        ((8, 4 * rows), f32),
        ((out_w.shape[0], 4 * rows), bf),
    ]

    def kernel(*refs):
        attention_forward_kernel(sections, *refs)

    return pl.pallas_call(
        kernel,
        out_shape=[jax.ShapeDtypeStruct(*result) for result in results]
        + [jax.ShapeDtypeStruct(array.shape, array.dtype) for array in arrays],
        in_specs=[anywhere] * 3 + [near] * 2 + [anywhere] * len(arrays),
        out_specs=[near] + [anywhere] * (4 + len(arrays)),
        scratch_shapes=[
            pltpu.VMEM(qkv_w.shape, bf),
            pltpu.VMEM(out_w.shape, bf),
            pltpu.VMEM(*results[2]),
            pltpu.VMEM(*results[3]),
            pltpu.VMEM(*results[4]),
            pltpu.VMEM((rows, width), f32),
            DMA((2,)),
            DMA((4,)),
            DMA((max(1, len(arrays)), 2)),
        ]
        + seq_scratch(rows, width),
        compiler_params=pltpu.CompilerParams(
            collective_id=collective_id, has_side_effects=True, vmem_limit_bytes=60 << 20
        ),
        cost_estimate=cost(),
        name="attention_forward",
    )(x, qkv_w, out_w, *tables, *arrays)


def attention_backward_kernel(sections, x_ref, qkv_ref, wo_ref, cos_ref, sin_ref, heads_in, lse_ref, *refs):
    kept = len(sections)
    sources, refs = refs[:kept], refs[kept:]
    out_ref, all_out, grads_out, *refs = refs
    targets, refs = refs[:kept], refs[kept:]
    wqkv, wo, heads, douts, dk, dv, dqt, grads, partial, wsem, osem, carry_sem, *line = refs
    line = Line(line)
    carried = Carried(sections, sources, targets, carry_sem)
    s = line.s
    rows = out_ref.shape[0]
    kv = heads.shape[0] // (GROUP + 2)
    queries = GROUP * kv
    loads = [
        pltpu.make_async_copy(wo_ref, wo, wsem.at[0]),
        pltpu.make_async_copy(qkv_ref, wqkv, wsem.at[1]),
        pltpu.make_async_copy(heads_in, heads, wsem.at[2]),
    ]
    for load in loads:
        load.start()
    seq_greet(s, carried.section)
    carried.start()
    dk[...] = jnp.zeros_like(dk)
    dv[...] = jnp.zeros_like(dv)

    def project(t):
        part = pl.ds(pl.multiple_of(t * rows, rows), rows)

        @pl.when(t == s)
        def _():
            loads[0].wait()

        grad = low(dot_t(line.land[t], wo[...]))
        for h in range(queries):
            douts[h, part, :] = grad[:, h * HEAD_DIM : (h + 1) * HEAD_DIM]

    line.gather(x_ref, project)
    saves = [pltpu.make_async_copy(line.land, all_out, osem.at[0])]
    saves[0].start()
    loads[1].wait()
    loads[2].wait()

    for block in (3, 2, 1, 0):
        keys = (block + 1) * rows
        part = slice(block * rows, (block + 1) * rows)

        @pl.loop(0, queries)
        def _(h):
            j = h // GROUP
            key = heads[queries + j, :keys, :]
            query = heads[h, part, :]
            grad = douts[h, part, :]
            scores = dot_t(key, query) * 0.125
            key_at = lax.broadcasted_iota(jnp.int32, scores.shape, 0)
            query_at = lax.broadcasted_iota(jnp.int32, scores.shape, 1) + block * rows
            scores = jnp.where(key_at <= query_at, scores, -jnp.inf)
            probs = jnp.exp(scores - lse_ref[pl.ds(h, 1), part])
            dprobs = dot_t(heads[queries + kv + j, :keys, :], grad)
            mean = jnp.sum(probs * dprobs, axis=0, keepdims=True)
            dscores = low(probs * (dprobs - mean))
            dk[j, :keys, :] += dot(dscores, query) * 0.125
            dv[j, :keys, :] += dot(low(probs), grad)
            dqt[pl.ds(pl.multiple_of(h * HEAD_DIM, HEAD_DIM), HEAD_DIM), :] = t_dot(key, dscores) * 0.125

        cos_part, sin_part = cos_ref[part, :], -sin_ref[part, :]
        dq = dqt[...].T
        for chunk in range(queries // 2):
            lanes = slice(chunk * 128, (chunk + 1) * 128)
            grads[part, lanes] = low(rope(dq[:, lanes], cos_part, sin_part))
        for pair in range(kv // 2):
            both = jnp.concatenate([dk[2 * pair, part, :], dk[2 * pair + 1, part, :]], axis=1)
            begin = queries * HEAD_DIM + pair * 128
            grads[part, begin : begin + 128] = low(rope(both, cos_part, sin_part))
            both = jnp.concatenate([dv[2 * pair, part, :], dv[2 * pair + 1, part, :]], axis=1)
            begin = (queries + kv) * HEAD_DIM + pair * 128
            grads[part, begin : begin + 128] = low(both)
        partial[...] = dot_t(grads[part, :], wqkv[...])
        line.hand_over(block, partial, out_ref)

    saves.append(pltpu.make_async_copy(grads, grads_out, osem.at[1]))
    saves[1].start()
    line.finish(out_ref)
    carried.finish()
    for save in saves:
        save.wait()


def attention_backward_call(x, qkv_w, out_w, tables, heads, lse, collective_id, carry):
    rows, width = x.shape
    bf, f32 = jnp.bfloat16, jnp.float32
    anywhere = pl.BlockSpec(memory_space=pl.ANY)
    near = pl.BlockSpec(memory_space=pltpu.VMEM)
    sections = tuple(to for to, _ in carry)
    arrays = [array for _, array in carry]
    results = [((rows, width), f32), ((4, rows, width), bf), ((4 * rows, qkv_w.shape[1]), bf)]
    kv = heads.shape[0] // (GROUP + 2)
    queries = GROUP * kv

    def kernel(*refs):
        attention_backward_kernel(sections, *refs)

    return pl.pallas_call(
        kernel,
        out_shape=[jax.ShapeDtypeStruct(*result) for result in results]
        + [jax.ShapeDtypeStruct(array.shape, array.dtype) for array in arrays],
        in_specs=[anywhere] * 3 + [near] * 2 + [anywhere, near] + [anywhere] * len(arrays),
        out_specs=[near] + [anywhere] * (2 + len(arrays)),
        scratch_shapes=[
            pltpu.VMEM(qkv_w.shape, bf),
            pltpu.VMEM(out_w.shape, bf),
            pltpu.VMEM(heads.shape, bf),
            pltpu.VMEM((queries, 4 * rows, HEAD_DIM), bf),
            pltpu.VMEM((kv, 4 * rows, HEAD_DIM), f32),
            pltpu.VMEM((kv, 4 * rows, HEAD_DIM), f32),
            pltpu.VMEM((queries * HEAD_DIM, rows), f32),
            pltpu.VMEM(*results[2]),
            pltpu.VMEM((rows, width), f32),
            DMA((3,)),
            DMA((2,)),
            DMA((max(1, len(arrays)), 2)),
        ]
        + seq_scratch(rows, width),
        compiler_params=pltpu.CompilerParams(
            collective_id=collective_id, has_side_effects=True, vmem_limit_bytes=60 << 20
        ),
        cost_estimate=cost(),
        name="attention_backward",
    )(x, qkv_w, out_w, *tables, heads, lse, *arrays)


def wide_tables(length):
    cos_table, sin_table = rotary_tables(length)
    cos_table, sin_table = cos_table[:, 0], sin_table[:, 0]
    return (
        jnp.concatenate([cos_table] * 4, axis=1),
        jnp.concatenate([-sin_table, sin_table] * 2, axis=1),
    )


def token_choice(route):
    return route[..., None] == jnp.arange(EXPERTS, dtype=jnp.int32)


def routing(route_all, first_expert, count):
    chosen = jnp.any(token_choice(route_all), axis=2)
    blocks, rows = chosen.shape[:2]
    mine = lax.dynamic_slice_in_dim(chosen, first_expert, count, axis=2)
    earlier = jnp.tril(jnp.ones((rows, rows), jnp.bfloat16), -1)
    place = jnp.einsum(
        "ts,bsj->bjt", earlier, mine.astype(jnp.bfloat16), preferred_element_type=jnp.float32
    ).astype(jnp.int32)
    mine = jnp.transpose(mine, (0, 2, 1))
    place = jnp.where(mine, place, -1)
    slots = jnp.arange(CAP, dtype=jnp.int32)
    pick = low(place[:, :, None, :] == slots[None, None, :, None]).reshape(blocks, -1, rows)
    return chosen, pick, jnp.transpose(pick, (0, 2, 1))


def choose(pick, rows, count):
    picked = jnp.einsum("bct,btd->bcd", pick, rows, preferred_element_type=jnp.float32)
    blocks = pick.shape[0]
    picked = low(picked).reshape(blocks, count, CAP, -1)
    return jnp.transpose(picked, (1, 0, 2, 3)).reshape(count, blocks * CAP, -1)


def give_back(pick_t, slot_rows):
    blocks, rows = pick_t.shape[:2]
    count, _, width = slot_rows.shape
    slot_rows = jnp.transpose(slot_rows.reshape(count, blocks, CAP, width), (1, 0, 2, 3))
    slot_rows = slot_rows.reshape(blocks, count * CAP, width)
    total = jnp.einsum("btc,bcd->btd", pick_t, slot_rows, preferred_element_type=jnp.float32)
    return low(total).reshape(-1, width)


def each_dot(form, a, b):
    return jnp.einsum(form, a, b, preferred_element_type=jnp.float32)


def after(value, *others):
    return lax.optimization_barrier((value, *others))[0]


def has_kernels():
    return lax.axis_size("dp") == 4 and lax.axis_size("seq") == 4


def forward_layer(number, layer_in, picking, weights, experts, *carry):
    attn_scale, ffn_scale, qkv_w, out_w, router_w = weights
    chosen, pick, pick_t, first_expert = picking
    own, other = experts
    count = own[0].shape[0]
    blocks, rows = chosen.shape[:2]
    received = []
    normed_input = low(rms_norm(layer_in, attn_scale))
    if has_kernels():
        branch, normed_all, heads, log_total, mixed_t, *received = attention_forward_call(
            normed_input, qkv_w, out_w, wide_tables(4 * layer_in.shape[0]), 9 + number, carry
        )
        attention_state = (normed_all.reshape(-1, layer_in.shape[1]), mixed_t, heads, log_total)
    else:
        received = [swap(array) for _, array in carry]
        normed_all = lax.all_gather(normed_input, "seq", axis=0, tiled=True)
        qkv = low(dot(normed_all, qkv_w))
        kv_width = KV_HEADS * HEAD_DIM // lax.axis_size("seq")
        q_width = GROUP * kv_width
        mixed, log_total, q_rot, k_rot, v_heads = attention_forward(
            qkv[:, :q_width], qkv[:, q_width : q_width + kv_width], qkv[:, q_width + kv_width :]
        )
        branch = lax.psum_scatter(low(dot(mixed, out_w)), "seq", scatter_dimension=0, tiled=True)
        attention_state = (normed_all, mixed.T, (q_rot, k_rot, v_heads), log_total)
    after_update = layer_in + branch.astype(jnp.float32)
    normed_ffn = low(rms_norm(after_update, ffn_scale))
    own_block = lax.axis_index("dp") * lax.axis_size("seq") + lax.axis_index("seq")
    own_chosen = lax.dynamic_index_in_dim(chosen, own_block, 0, keepdims=False)
    own_logits = jnp.where(own_chosen, dot(normed_ffn, router_w), -jnp.inf)
    own_gates = jax.nn.softmax(own_logits, axis=-1)
    other = tuple(other) + tuple(received)
    mine = (
        jnp.arange(EXPERTS)[None, None, :] == first_expert + jnp.arange(count)[:, None, None]
    ).astype(jnp.float32)
    if has_kernels():
        *expert_state, slot_out = expert_forward(
            number, normed_ffn, pick, low(chosen), router_w, mine, own, other, 1 + number
        )
        if number == 0:
            *expert_state, slot_out, other_down = (*expert_state, slot_out)
            other = other[:2] + (other_down,)
    else:
        if number == 0:
            other = other[:2] + (swap(own[2]),)
        gate_w, up_w, down_w = by_layer(number, own, other)
        ffn_all = lax.all_gather(normed_ffn, TOKENS, axis=0, tiled=True)
        logits = dot(ffn_all, router_w).reshape(blocks, rows, EXPERTS)
        gates = jax.nn.softmax(jnp.where(chosen, logits, -jnp.inf), axis=-1)
        slot_rows = choose(pick, ffn_all.reshape(blocks, rows, -1), count)
        mine_gates = jnp.einsum("bte,jxe->bjt", gates, mine, precision=lax.Precision.HIGHEST)
        slot_gates = jnp.sum(
            pick.reshape(blocks, count, CAP, rows).astype(jnp.float32) * mine_gates[:, :, None, :],
            axis=3,
        )
        slot_gates = jnp.transpose(slot_gates, (1, 0, 2)).reshape(count, -1, 1)
        gate_pre = each_dot("ecd,edf->ecf", slot_rows, gate_w)
        up_pre = each_dot("ecd,edf->ecf", slot_rows, up_w)
        scaled = low(slot_gates * jax.nn.silu(gate_pre) * up_pre)
        slot_out = low(each_dot("ecf,efd->ecd", scaled, down_w))
        expert_state = (slot_rows, gate_pre, up_pre, scaled, slot_gates)
    saved = (
        layer_in,
        attention_state,
        after_update,
        normed_ffn,
        own_gates,
        expert_state,
    )
    return (after_update, slot_out, saved, (own, other))


def token_sums(pick_t, slot_out, collective_id, *carry):
    if has_kernels():
        sums, *received = combine(pick_t, slot_out, collective_id, carry)
        return sums, received
    sums = give_back(pick_t, slot_out).astype(jnp.float32)
    sums = lax.psum_scatter(sums, TOKENS, scatter_dimension=0, tiled=True)
    return sums, [pass_to(array, to) for to, array in carry]


def expert_gradients(number, layer_grad, saved, picking, experts, *carry):
    chosen, pick, pick_t, first_expert = picking
    own, other = experts
    count = own[0].shape[0]
    blocks, rows = chosen.shape[:2]
    slot_rows, gate_pre, up_pre, scaled, slot_gates = saved[-1]
    if has_kernels():
        slot_grads, gate_low, up_low, gate_term, slot_out, *received = expert_backward(
            number, low(layer_grad), pick, gate_pre, up_pre, slot_gates, own, other, 4 + number, carry
        )
        gate_term = gate_term[:, :, :1]
    else:
        gate_w, up_w, down_w = by_layer(number, own, other)
        grad_all = lax.all_gather(low(layer_grad), TOKENS, axis=0, tiled=True)
        slot_grads = choose(pick, grad_all.reshape(blocks, rows, -1), count)
        plain_grad = each_dot("ecd,efd->ecf", slot_grads, down_w)
        sigmoid = jax.nn.sigmoid(gate_pre)
        activated = gate_pre * sigmoid
        gate_term = jnp.sum(plain_grad * (activated * up_pre), axis=2, keepdims=True)
        hidden_grad = slot_gates * plain_grad
        gate_low = low(hidden_grad * up_pre * sigmoid * (1.0 + gate_pre * (1.0 - sigmoid)))
        up_low = low(hidden_grad * activated)
        slot_out = low(
            each_dot("ecf,edf->ecd", gate_low, gate_w) + each_dot("ecf,edf->ecd", up_low, up_w)
        )
        received = [pass_to(array, to) for to, array in carry]
    expert_grads = (
        low(each_dot("ecd,ecf->edf", slot_rows, gate_low)),
        low(each_dot("ecd,ecf->edf", slot_rows, up_low)),
        low(each_dot("ecf,ecd->efd", scaled, slot_grads)),
    )
    slot_out, *expert_grads = lax.optimization_barrier((slot_out, *expert_grads))
    return slot_out, gate_term, expert_grads, received


def backward_layer(number, layer_grad, normed_grad, gate_term, saved, picking, weights, *carry):
    attn_scale, ffn_scale, qkv_w, out_w, router_w = weights
    chosen, pick, _, _ = picking
    (
        layer_in,
        (normed_all, mixed_t, heads, log_total),
        after_update,
        normed_ffn,
        own_gates,
        _,
    ) = saved
    blocks, rows = chosen.shape[:2]
    count = gate_term.shape[0]
    by_slot = jnp.transpose(gate_term.reshape(count, blocks, CAP), (1, 0, 2))
    gate_terms = jnp.sum(
        pick.reshape(blocks, count, CAP, rows).astype(jnp.float32) * by_slot[..., None], axis=2
    )
    gate_terms = lax.all_to_all(gate_terms, TOKENS, split_axis=0, concat_axis=0, tiled=True)
    gate_terms = jnp.sum(gate_terms.reshape(EXPERTS, -1, rows), axis=1).T
    logit_grad = low(
        own_gates * (gate_terms - jnp.sum(own_gates * gate_terms, axis=-1, keepdims=True))
    )
    router_grad = t_dot(normed_ffn, logit_grad)
    normed_grad = normed_grad + dot_t(logit_grad, router_w)
    after_part, ffn_gain_grad = jax.vjp(rms_norm, after_update, ffn_scale)[1](normed_grad)
    after_grad = after_part + layer_grad
    if has_kernels():
        normed_attn, branch_all, qkv_grad, *received = attention_backward_call(
            low(after_grad),
            qkv_w,
            out_w,
            wide_tables(4 * layer_in.shape[0]),
            heads,
            log_total,
            11 + number,
            carry,
        )
        branch_all = branch_all.reshape(-1, layer_in.shape[1])
    else:
        branch_all = lax.all_gather(low(after_grad), "seq", axis=0, tiled=True)
        head_grad = low(dot_t(branch_all, out_w))
        qkv_grad = attention_backward(head_grad, *heads, log_total)
        normed_attn = low(dot_t(qkv_grad, qkv_w))
        normed_attn = lax.psum_scatter(normed_attn, "seq", scatter_dimension=0, tiled=True)
        received = [pass_to(array, to) for to, array in carry]
    out_grad = dot(mixed_t, branch_all)
    qkv_weight_grad = t_dot(normed_all, qkv_grad)
    input_part, attn_gain_grad = jax.vjp(rms_norm, layer_in, attn_scale)[1](
        normed_attn.astype(jnp.float32)
    )
    gain_grads = jnp.stack([attn_gain_grad, ffn_gain_grad])
    return (
        input_part + after_grad,
        (low(qkv_weight_grad), low(out_grad), low(router_grad), gain_grads),
        received,
    )


def by_layer(number, own, other):
    is_own = lax.axis_index("section") == number
    return jax.tree.map(lambda mine, received: jnp.where(is_own, mine, received), own, other)


def body(
    hidden_in,
    out_grad,
    attn_gain,
    ffn_gain,
    query_matrix,
    key_matrix,
    value_matrix,
    output_matrix,
    router_matrix,
    w_gate,
    w_up,
    w_down,
    routes,
):
    section = lax.axis_index("section")
    dp, seq = lax.axis_size("dp"), lax.axis_size("seq")
    seq_index = lax.axis_index("seq")
    first = section == 0
    width = hidden_in.shape[3]
    depth = query_matrix.shape[1]

    layer_in = lax.dynamic_index_in_dim(hidden_in, section, 0, keepdims=False)[0]
    top_grad = lax.dynamic_index_in_dim(out_grad, section, 0, keepdims=False)[0]
    own_group = jnp.concatenate(
        [
            matrix[0].reshape(depth, seq, -1)
            for matrix in (query_matrix, key_matrix, value_matrix)
        ],
        axis=2,
    )
    to_group = []
    for flat in range(dp * seq):
        to_group.append((flat, (flat % dp) * seq + flat // dp))
    from_group = [(target, source) for source, target in to_group]
    other_group = swap(own_group)
    own_out = lax.ppermute(output_matrix[0], TOKENS, to_group)
    other_out = swap(own_out)
    small = jnp.concatenate([router_matrix[0].T, attn_gain, ffn_gain], axis=0).reshape(-1)
    known = small.shape[0]
    wide = jnp.concatenate(
        [low(routes[0, :, 0].reshape(-1)), small, jnp.zeros((-known % 4096,), jnp.bfloat16)]
    )
    wide = wide.reshape(-1, 256)
    if has_kernels():
        other_wide = swap(wide)
        wide = jnp.stack(by_layer(0, [wide, other_wide], [other_wide, wide]))
        wide = gather_small(wide.reshape(-1, 256), 13).reshape(dp * seq, 2, -1)
        wide = jnp.transpose(wide, (1, 0, 2))
    else:
        wide = lax.all_gather(wide, ("section", "dp", "seq"), axis=0, tiled=True)
        wide = wide.reshape(2, dp * seq, -1)
    paths = wide[:, :, : routes[0].size].reshape(2, dp * seq, 2, -1, TOP_K)
    paths = lax.dynamic_index_in_dim(paths, section, 2, keepdims=False).astype(jnp.int32)
    small = wide[:, :, routes[0].size : routes[0].size + known]
    small = jnp.transpose(small.reshape(2, dp * seq, EXPERTS + 2, depth), (0, 2, 1, 3))
    small = small.reshape(2, EXPERTS + 2, width)

    local = w_gate.shape[1]
    hidden_units = w_gate.shape[3]
    if local >= seq:
        count, units = local // seq, hidden_units
        start, unit_start = seq_index * count, 0
    else:
        count, units = 1, hidden_units * local // seq
        start, unit_start = seq_index * local // seq, (seq_index % (seq // local)) * units
    first_expert = lax.axis_index("dp") * local + start
    own_experts = (
        lax.dynamic_slice(w_gate[0], (start, 0, unit_start), (count, width, units)),
        lax.dynamic_slice(w_up[0], (start, 0, unit_start), (count, width, units)),
        lax.dynamic_slice(w_down[0], (start, unit_start, 0), (count, units, width)),
    )
    other_gate = swap(after(own_experts[0], other_group))
    experts = (own_experts, (other_gate,))

    weights = []
    pickings = []
    for number in range(2):
        part = by_layer(number, own_group, other_group)
        part = lax.all_to_all(part, "seq", split_axis=1, concat_axis=0, tiled=True)
        qkv_w = lax.all_gather(part.reshape(seq * depth, -1), "dp", axis=0, tiled=True)
        out_w = lax.all_gather(
            by_layer(number, own_out, other_out), "dp", axis=0, tiled=True
        )
        weights.append(
            (
                small[number, EXPERTS].astype(jnp.float32),
                small[number, EXPERTS + 1].astype(jnp.float32),
                qkv_w,
                out_w,
                small[number, :EXPERTS].T,
            )
        )
        pickings.append(routing(paths[number], first_expert, count) + (first_expert,))

    first_in = after(layer_in, other_gate).astype(jnp.float32)
    updated, slot_out, first_saved, experts = forward_layer(
        0, first_in, pickings[0], weights[0], experts, (None, own_experts[1])
    )
    sums, _ = token_sums(pickings[0][2], slot_out, 3)
    first_out = updated + sums
    second_updated, second_slots, second_saved, experts = forward_layer(
        1, first_out, pickings[1], weights[1], experts
    )
    received = [[None] * 3, [None] * 3]
    top_grad = top_grad.astype(jnp.float32)
    slot_out, gate_term, second_experts, _ = expert_gradients(
        1, top_grad, second_saved, pickings[1], experts
    )
    sums, (received[1][0],) = token_sums(pickings[1][2], slot_out, 6, (1, second_experts[0]))
    middle_grad, second_dense, (received[1][1],) = backward_layer(
        1, top_grad, sums, gate_term, second_saved, pickings[1], weights[1], (1, second_experts[1])
    )
    slot_out, gate_term, first_experts, (received[1][2],) = expert_gradients(
        0, middle_grad, first_saved, pickings[0], experts, (1, second_experts[2])
    )
    sums, (received[0][0],) = token_sums(pickings[0][2], slot_out, 7, (0, first_experts[0]))
    bottom_grad, first_dense, (received[0][1],) = backward_layer(
        0, middle_grad, sums, gate_term, first_saved, pickings[0], weights[0], (0, first_experts[1])
    )
    second_slots = after(second_slots, received[0][1])
    sums, (received[0][2],) = token_sums(
        pickings[1][2], second_slots, 8, (0, first_experts[2])
    )
    layer_states = [first_out, second_updated + sums]
    layer_grads = [bottom_grad, middle_grad]
    dense_grads = [first_dense, second_dense]
    expert_grads = [first_experts, second_experts]

    def own_layer(pieces):
        return jnp.where(first, pieces[0], pieces[1])

    def to_section(pieces):
        other = own_layer([pass_to(pieces[number], number) for number in range(2)])
        own = own_layer(pieces)
        return jnp.stack([jnp.where(first, own, other), jnp.where(first, other, own)])[
            None, :, None
        ]

    def summed(pieces):
        other = own_layer([pass_to(pieces[number], number) for number in range(2)])
        return own_layer(pieces).astype(jnp.float32) + other.astype(jnp.float32)

    kv_width = KV_HEADS * HEAD_DIM // seq
    q_width = GROUP * kv_width
    qkv_width = q_width + 2 * kv_width
    qkv_parts = []
    out_parts = []
    gain_parts = []
    for number in range(2):
        qkv_part, out_part, router_part, gain_part = dense_grads[number]
        qkv_part = jnp.concatenate([qkv_part, router_part], axis=1)
        qkv_part = lax.psum_scatter(qkv_part, "dp", scatter_dimension=0, tiled=True)
        qkv_part = qkv_part.reshape(seq, depth, -1)
        qkv_parts.append(
            lax.all_to_all(qkv_part, "seq", split_axis=0, concat_axis=0, tiled=True)
        )
        out_part = lax.psum_scatter(out_part, "dp", scatter_dimension=0, tiled=True)
        out_parts.append(lax.ppermute(out_part, TOKENS, from_group))
        gain_part = gain_part.reshape(2, dp * seq, depth)
        gain_part = lax.all_to_all(gain_part, TOKENS, split_axis=1, concat_axis=1, tiled=True)
        gain_parts.append(jnp.sum(gain_part, axis=1))
    qkv_sum = summed(qkv_parts)
    out_sum = summed(out_parts)
    gain_sum = summed(gain_parts)

    def columns(begin, end):
        return jnp.transpose(qkv_sum[:, :, begin:end], (1, 0, 2)).reshape(depth, -1)[None]

    expert_sums = []
    for kind in range(3):
        own = own_layer([expert_grads[number][kind] for number in range(2)])
        other = own_layer([received[number][kind] for number in range(2)])
        piece = low(own.astype(jnp.float32) + other.astype(jnp.float32))
        rows = piece.shape[1] // seq
        if local >= seq:
            piece = piece.reshape(count, seq, rows, -1)
            piece = jnp.transpose(piece, (1, 0, 2, 3))
            piece = lax.all_to_all(piece, "seq", split_axis=0, concat_axis=0, tiled=True)
            piece = piece.reshape(local, rows, -1)
        elif kind < 2:
            share = seq // local
            piece = piece.reshape(seq, rows, units)
            piece = lax.all_to_all(piece, "seq", split_axis=0, concat_axis=0, tiled=True)
            piece = piece.reshape(local, share, rows, units)
            piece = jnp.transpose(piece, (0, 2, 1, 3)).reshape(local, rows, -1)
        else:
            rows = hidden_units // seq
            piece = whole_rows(piece.reshape(-1, rows, width), seq_index, seq // local, seq)
        expert_sums.append(piece.astype(jnp.float32)[None])
    return (
        to_section(layer_states),
        to_section(layer_grads),
        gain_sum[0][None],
        gain_sum[1][None],
        columns(0, q_width),
        columns(q_width, q_width + kv_width),
        columns(q_width + kv_width, qkv_width),
        out_sum[None],
        jnp.sum(qkv_sum[:, :, qkv_width:], axis=0)[None],
        *expert_sums,
    )


def whole_rows(piece, seq_index, share, seq):
    parts = piece.shape[0]
    spread = jnp.zeros((seq,) + piece.shape[1:], piece.dtype)
    spread = lax.dynamic_update_slice_in_dim(
        spread, piece, (seq_index % share) * parts, axis=0
    )
    spread = lax.all_to_all(spread, "seq", split_axis=0, concat_axis=0, tiled=True)
    spread = spread.reshape((-1, share) + piece.shape[1:])
    return jnp.sum(spread.astype(jnp.float32), axis=1).astype(piece.dtype)


def solution(mesh):
    return jax.shard_map(
        body,
        mesh=mesh,
        in_specs=(
            P(None, "dp", "seq", None),
            P(None, "dp", "seq", None),
            P("section", ("dp", "seq")),
            P("section", ("dp", "seq")),
            P("section", ("dp", "seq"), None),
            P("section", ("dp", "seq"), None),
            P("section", ("dp", "seq"), None),
            P("section", ("dp", "seq"), None),
            P("section", ("dp", "seq"), None),
            P("section", "dp", None, None),
            P("section", "dp", None, None),
            P("section", "dp", None, None),
            P("section", None, "dp", "seq", None),
        ),
        out_specs=(
            P("section", None, "dp", "seq", None),
            P("section", None, "dp", "seq", None),
            P("section", ("dp", "seq")),
            P("section", ("dp", "seq")),
            P("section", ("dp", "seq"), None),
            P("section", ("dp", "seq"), None),
            P("section", ("dp", "seq"), None),
            P("section", ("dp", "seq"), None),
            P("section", ("dp", "seq"), None),
            P("section", "dp", "seq", None),
            P("section", "dp", "seq", None),
            P("section", "dp", "seq", None),
        ),
        check_vma=False,
    )
```

```python
import jax
import jax.numpy as jnp
from jax import lax
from jax.experimental import pallas as pl
from jax.experimental.pallas import tpu as pltpu
from jax.sharding import PartitionSpec as P

HEADS = 24
KV_HEADS = 8
HEAD_DIM = 64
TOP_K = 8
EXPERTS = 32
CAP = 80
GROUP = HEADS // KV_HEADS
TOKENS = ("dp", "seq")
MESH = pl.DeviceIdType.MESH
DMA = pltpu.SemaphoreType.DMA

epsilon = 1e-06


def dot(a, b):
    return jnp.dot(a, b, preferred_element_type=jnp.float32)


def dot_t(a, b):
    return lax.dot_general(a, b, (((1,), (1,)), ((), ())), preferred_element_type=jnp.float32)


def t_dot(a, b):
    return lax.dot_general(a, b, (((0,), (0,)), ((), ())), preferred_element_type=jnp.float32)


def low(v):
    return v.astype(jnp.bfloat16)


def swap(block):
    return lax.ppermute(block, "section", [(0, 1), (1, 0)])


def pass_to(block, section):
    return lax.ppermute(block, "section", [(1 - section, section)])


def rms_norm(values, norm_gain):
    return (
        values * lax.rsqrt(jnp.mean(values * values, axis=-1, keepdims=True) + epsilon) * norm_gain
    )


def rotary_tables(length):
    half_dim = HEAD_DIM // 2
    frequency = 10000.0 ** (-jnp.arange(half_dim, dtype=jnp.float32) * 2.0 / HEAD_DIM)
    angles = jnp.arange(length, dtype=jnp.float32)[:, None] * frequency[None, :]
    return (jnp.cos(angles)[:, None, :], jnp.sin(angles)[:, None, :])


def rotate(values, cos_table, sin_table):
    length = values.shape[0]
    split_heads = values.reshape(length, -1, HEAD_DIM)
    first_half = split_heads[..., : HEAD_DIM // 2]
    second_half = split_heads[..., HEAD_DIM // 2 :]
    turned = jnp.concatenate(
        [
            first_half * cos_table - second_half * sin_table,
            second_half * cos_table + first_half * sin_table,
        ],
        axis=-1,
    )
    return turned.reshape(length, -1)


def attention_forward(q_heads, k_heads, v_heads):
    length = q_heads.shape[0]
    local_kv = k_heads.shape[1] // HEAD_DIM
    cos_table, sin_table = rotary_tables(length)
    q_rot = low(rotate(q_heads.astype(jnp.float32), cos_table, sin_table)).reshape(
        length, local_kv, GROUP, HEAD_DIM
    )
    k_rot = low(rotate(k_heads.astype(jnp.float32), cos_table, sin_table)).reshape(
        length, local_kv, HEAD_DIM
    )
    values = v_heads.reshape(length, local_kv, HEAD_DIM)
    block_rows = min(512, length)
    outputs = []
    totals_list = []
    for first_row in range(0, length, block_rows):
        key_end = first_row + block_rows
        scores = (
            jnp.einsum(
                "qhgd,khd->hgqk",
                q_rot[first_row:key_end],
                k_rot[:key_end],
                preferred_element_type=jnp.float32,
            )
            * 0.125
        )
        causal = (first_row + jnp.arange(block_rows, dtype=jnp.int32))[:, None] >= jnp.arange(
            key_end, dtype=jnp.int32
        )[None, :]
        scores = jnp.where(causal, scores, -jnp.inf)
        row_peak = jnp.max(scores, axis=-1, keepdims=True)
        exponents = jnp.exp(scores - row_peak)
        totals = jnp.sum(exponents, axis=-1, keepdims=True)
        attended = jnp.einsum(
            "hgqk,khd->qhgd",
            low(exponents / totals),
            values[:key_end],
            preferred_element_type=jnp.float32,
        )
        outputs.append(low(attended).reshape(block_rows, -1))
        totals_list.append((row_peak + jnp.log(totals))[..., 0])
    return (jnp.concatenate(outputs, axis=0), jnp.stack(totals_list), q_rot, k_rot, values)


def attention_backward(head_grad, q_rot, k_rot, values, log_total):
    length, local_kv = q_rot.shape[:2]
    cos_table, sin_table = rotary_tables(length)
    block_rows = min(512, length)
    grad_rows = head_grad.reshape(length, local_kv, GROUP, HEAD_DIM)
    key_acc = jnp.zeros((length, local_kv, HEAD_DIM), jnp.float32)
    value_acc = jnp.zeros((length, local_kv, HEAD_DIM), jnp.float32)
    query_parts = []
    for block_number, first_row in enumerate(range(0, length, block_rows)):
        key_end = first_row + block_rows
        q_block = q_rot[first_row:key_end]
        grad_block = grad_rows[first_row:key_end]
        key_part = k_rot[:key_end]
        scores = (
            jnp.einsum("qhgd,khd->hgqk", q_block, key_part, preferred_element_type=jnp.float32)
            * 0.125
        )
        causal = (first_row + jnp.arange(block_rows, dtype=jnp.int32))[:, None] >= jnp.arange(
            key_end, dtype=jnp.int32
        )[None, :]
        scores = jnp.where(causal, scores, -jnp.inf)
        probs_full = jnp.exp(scores - log_total[block_number][..., None])
        prob_grad = jnp.einsum(
            "qhgd,khd->hgqk", grad_block, values[:key_end], preferred_element_type=jnp.float32
        )
        score_grad = probs_full * (
            prob_grad - jnp.sum(probs_full * prob_grad, axis=-1, keepdims=True)
        )
        score_low = low(score_grad)
        query_parts.append(
            jnp.einsum("hgqk,khd->qhgd", score_low, key_part, preferred_element_type=jnp.float32)
            * 0.125
        )
        key_acc = key_acc.at[:key_end].add(
            jnp.einsum("hgqk,qhgd->khd", score_low, q_block, preferred_element_type=jnp.float32)
            * 0.125
        )
        value_acc = value_acc.at[:key_end].add(
            jnp.einsum(
                "hgqk,qhgd->khd", low(probs_full), grad_block, preferred_element_type=jnp.float32
            )
        )
    query_all = jnp.concatenate(query_parts, axis=0).reshape(length, -1)
    query_grad = rotate(query_all, cos_table, -sin_table)
    key_grad = rotate(key_acc.reshape(length, -1), cos_table, -sin_table)
    return jnp.concatenate(
        [low(query_grad), low(key_grad), low(value_acc).reshape(length, -1)], axis=1
    )


def remote(src, dst, send_sem, recv_sem, **device):
    return pltpu.make_async_remote_copy(
        src_ref=src,
        dst_ref=dst,
        send_sem=send_sem,
        recv_sem=recv_sem,
        device_id=device,
        device_id_type=MESH,
    )


def greet(d, s, section=None):
    barrier = pltpu.get_barrier_semaphore()

    def signal(**device):
        pl.semaphore_signal(barrier, inc=1, device_id=device, device_id_type=MESH)

    signal(seq=s ^ 1)
    signal(seq=s ^ 2)

    @pl.when(d > 0)
    def _():
        signal(dp=d - 1)

    @pl.when(d < 3)
    def _():
        signal(dp=d + 1)

    known = 3
    if section is not None:
        signal(section=1 - section)
        known = 4
    inner = (d > 0) & (d < 3)

    @pl.when(inner)
    def _():
        pl.semaphore_wait(barrier, known + 1)

    @pl.when(jnp.logical_not(inner))
    def _():
        pl.semaphore_wait(barrier, known)


class Carried:
    def __init__(self, sections, sources, targets, sems):
        self.section = lax.axis_index("section")
        self.copies = []
        for k, (to, source, target) in enumerate(zip(sections, sources, targets)):
            copy = remote(source, target, sems.at[k, 0], sems.at[k, 1], section=1 - self.section)
            self.copies.append((to, copy))

    def start(self):
        for to, copy in self.copies:
            if to is None:
                copy.start()
            else:

                @pl.when(self.section != to)
                def _():
                    copy.start()

    def finish(self):
        for to, copy in self.copies:
            if to is None:
                copy.wait()
            else:

                @pl.when(self.section != to)
                def _():
                    copy.wait_send()

                @pl.when(self.section == to)
                def _():
                    copy.wait_recv()


def cost():
    return pl.CostEstimate(flops=80_000_000_000, bytes_accessed=100_000_000, transcendentals=0)


def gather_scratch(rows, width):
    return [
        pltpu.VMEM((16, rows, width), jnp.bfloat16),
        DMA(()),
        DMA((2, 4)),
        DMA((4,)),
        DMA((4,)),
        DMA((4,)),
        DMA((4, 2)),
        DMA((4, 2)),
    ]


def gather_blocks(x_ref, scratch, compute, carried=None, first=None):
    land, lsem, zs, zr, ys, yr, cs, cr = scratch
    d, s = lax.axis_index("dp"), lax.axis_index("seq")

    def place(z, column):
        return land.at[z * 4 + column]

    def z_copy(src, z, right):
        target = d + 1 if right else d - 1
        return remote(src, place(z, s), zs.at[int(right), z], zr.at[z], dp=target)

    def y_copy(src, z):
        return remote(src, place(z, s), ys.at[z], yr.at[z], seq=s ^ 2)

    def core_copy(src, z, across):
        column = s ^ 2 if across else s
        return remote(src, place(z, column), cs.at[z, across], cr.at[z, across], seq=s ^ 1)

    greet(d, s, None if carried is None else carried.section)
    if first is not None:
        first()
    own = pltpu.make_async_copy(x_ref, place(d, s), lsem)
    own.start()
    if carried is not None and first is None:
        carried.start()

    @pl.when(d < 3)
    def _():
        z_copy(x_ref, d, True).start()

    @pl.when(d > 0)
    def _():
        z_copy(x_ref, d, False).start()

    y_copy(x_ref, d).start()
    core_copy(x_ref, d, 0).start()
    own.wait()

    @pl.loop(0, 4)
    def _(i):
        @pl.when(i < 3)
        def _():
            left, right = d - (i + 1), d + (i + 1)

            @pl.when(left >= 0)
            def _():
                z_copy(place(left, s), left, True).wait_recv()

                @pl.when(d < 3)
                def _():
                    z_copy(place(left, s), left, True).start()

            @pl.when(right <= 3)
            def _():
                z_copy(place(right, s), right, False).wait_recv()

                @pl.when(d > 0)
                def _():
                    z_copy(place(right, s), right, False).start()

            following = d ^ (i + 1)
            y_copy(place(following, s), following).start()
            core_copy(place(following, s), following, 0).start()

        z = d ^ i
        y_copy(place(z, s ^ 2), z).wait_recv()
        core_copy(place(z, s ^ 2), z, 1).start()
        core_copy(place(z, s ^ 1), z, 0).wait_recv()
        core_copy(place(z, s ^ 3), z, 1).wait_recv()
        compute(z)

    for z in range(4):

        @pl.when((z <= d) & (d < 3))
        def _():
            z_copy(place(z, s), z, True).wait_send()

        @pl.when((z >= d) & (d > 0))
        def _():
            z_copy(place(z, s), z, False).wait_send()

        y_copy(place(z, s), z).wait_send()
        core_copy(place(z, s), z, 0).wait_send()
        core_copy(place(z, s), z, 1).wait_send()
    return land


def prepare_kernel(x_ref, pick_out, pick_t_out, chosen_out, small_out, both, places, lsem, carry_sem, *gather):
    d, s, section = lax.axis_index("dp"), lax.axis_index("seq"), lax.axis_index("section")
    known = x_ref.shape[0]
    count = pick_out.shape[2] // CAP
    rows = pick_out.shape[3]
    land = gather[0]
    part = both.at[pl.ds(pl.multiple_of(section * known, known), known)]
    carried = Carried((None,), (x_ref,), (part,), carry_sem)

    def swap_first():
        carried.start()
        own = pltpu.make_async_copy(x_ref, part, lsem)
        own.start()
        own.wait()
        carried.finish()

    gather_blocks(both, gather, lambda z: None, carried, swap_first)
    first_expert = (d * 4 + s) * count
    before = lax.broadcasted_iota(jnp.int32, (rows, rows), 0)
    before = low(before < lax.broadcasted_iota(jnp.int32, (rows, rows), 1))
    slot = lax.broadcasted_iota(jnp.int32, (CAP, rows), 0)
    expert = lax.broadcasted_iota(jnp.int32, (EXPERTS, rows), 0)
    lane = lax.broadcasted_iota(jnp.int32, (rows, count * CAP), 1)

    @pl.loop(0, 2)
    def _(layer):
        @pl.loop(0, 16)
        def _(b):
            paths = land[b, pl.ds(pl.multiple_of(layer * known, 16), 16), :].astype(jnp.float32)
            paths = jnp.where(section == 0, paths[:TOP_K], paths[TOP_K:]).astype(jnp.int32)
            chosen = expert == paths[0:1]
            for k in range(1, TOP_K):
                chosen = chosen | (expert == paths[k : k + 1])
            chosen_out[layer, b] = low(chosen)
            mine = [
                jnp.max((paths == first_expert + j).astype(jnp.float32), axis=0, keepdims=True)
                for j in range(count)
            ]
            mine = jnp.concatenate(mine + [jnp.zeros((8 - count, rows), jnp.float32)], axis=0)
            place = jnp.where(mine > 0.5, dot(low(mine), before), -10000.0)
            places[...] = place
            for j in range(count):
                pick_out[layer, b, j * CAP : (j + 1) * CAP, :] = low(
                    slot == place[j : j + 1].astype(jnp.int32)
                )
            turned = places[...].T.astype(jnp.int32)
            pick_t = turned[:, 0:1] == lane
            for j in range(1, count):
                pick_t = pick_t & (lane < j * CAP) | (turned[:, j : j + 1] == lane - j * CAP)
            pick_t_out[layer, b] = low(pick_t)

        depth = small_out.shape[2] // 16
        for b in range(16):
            small = land[b, pl.ds(pl.multiple_of(layer * known + 16, 16), known - 16), :]
            small_out[layer, :, b * depth : (b + 1) * depth] = small[:, :depth]


def prepare(x, count, rows, depth, collective_id):
    known, width = x.shape
    bf = jnp.bfloat16
    near = pl.BlockSpec(memory_space=pltpu.VMEM)
    return pl.pallas_call(
        prepare_kernel,
        out_shape=[
            jax.ShapeDtypeStruct((2, 16, count * CAP, rows), bf),
            jax.ShapeDtypeStruct((2, 16, rows, count * CAP), bf),
            jax.ShapeDtypeStruct((2, 16, EXPERTS, rows), bf),
            jax.ShapeDtypeStruct((2, known - 16, 16 * depth), bf),
        ],
        in_specs=[pl.BlockSpec(memory_space=pl.ANY)],
        out_specs=[near] * 4,
        scratch_shapes=[
            pltpu.VMEM((2 * known, width), bf),
            pltpu.VMEM((8, rows), jnp.float32),
            DMA(()),
            DMA((1, 2)),
        ]
        + gather_scratch(2 * known, width),
        compiler_params=pltpu.CompilerParams(
            collective_id=collective_id, has_side_effects=True, vmem_limit_bytes=60 << 20
        ),
        cost_estimate=pl.CostEstimate(flops=20_000_000_000, bytes_accessed=10_000_000, transcendentals=0),
        name="prepare",
    )(x)


def pick_weights(own_refs, other_refs, held, sems, own_layer):
    mine = lax.axis_index("section") == own_layer

    @pl.when(mine)
    def _():
        for k, ref in enumerate(own_refs):
            pltpu.make_async_copy(ref, held[k], sems.at[k]).start()

    @pl.when(jnp.logical_not(mine))
    def _():
        for k, ref in enumerate(other_refs):
            pltpu.make_async_copy(ref, held[k], sems.at[k]).start()

    def ready(k):
        pltpu.make_async_copy(own_refs[k], held[k], sems.at[k]).wait()

    return ready


def expert_forward_kernel(
    layer, x_ref, pick_ref, chosen_ref, router_ref, mine_ref,
    wg_own, wu_own, wd_own, wg_other, wu_other, wd_other,
    rows_out, gate_out, up_out, hidden_out, slot_gate_out, y_out,
    wg, wu, wd, rows, gate, up, hidden, slot_gate, y, wsem, osem, carry_sem, *gather
):
    count = wg.shape[0]
    carried = None
    if layer == 0:
        carried = Carried((None,), (wd_own,), (wd_other,), carry_sem)
        ready = pick_weights((wg_own, wu_own), (wg_other, wu_other), (wg, wu), wsem, layer)
    else:
        ready = pick_weights(
            (wg_own, wu_own, wd_own), (wg_other, wu_other, wd_other), (wg, wu, wd), wsem, layer
        )
    land = gather[0]
    d = lax.axis_index("dp")

    def outs(z):
        part = pl.ds(z * 4 * CAP, 4 * CAP)
        return [
            pltpu.make_async_copy(held.at[:, part], out.at[:, part], osem.at[k, z])
            for k, (held, out) in enumerate(
                ((rows, rows_out), (gate, gate_out), (up, up_out), (hidden, hidden_out), (slot_gate, slot_gate_out))
            )
        ] + [pltpu.make_async_copy(y.at[pl.ds(z * 4, 4)], y_out.at[pl.ds(z * 4, 4)], osem.at[5, z])]

    def down(z):
        part = pl.ds(z * 4 * CAP, 4 * CAP)

        @pl.loop(0, count)
        def _(j):
            result = low(dot(hidden[j, part, :], wd[j]))
            for q in range(4):
                y[z * 4 + q, pl.ds(j * CAP, CAP), :] = result[q * CAP : (q + 1) * CAP]

    def compute(z):
        @pl.when(z == d)
        def _():
            for k in range(2 if layer == 0 else 3):
                ready(k)

        for q in range(4):
            b = z * 4 + q
            picked = low(dot(pick_ref[b], land[b]))
            for j in range(count):
                rows[j, pl.ds(b * CAP, CAP), :] = picked[j * CAP : (j + 1) * CAP]
        part = pl.ds(z * 4 * CAP, 4 * CAP)

        @pl.loop(0, count)
        def _(j):
            x = rows[j, part, :]
            g = dot(x, wg[j])
            u = dot(x, wu[j])
            logits = dot_t(x, router_ref[...])
            for q in range(4):
                b = z * 4 + q
                slots = slice(q * CAP, (q + 1) * CAP)
                seen = dot_t(pick_ref[b, pl.ds(j * CAP, CAP), :], chosen_ref[b])
                masked = jnp.where(seen > 0.5, logits[slots], -1e30)
                power = jnp.exp(masked - jnp.max(masked, axis=1, keepdims=True))
                own = jnp.sum(power * mine_ref[j], axis=1, keepdims=True)
                value = own / jnp.sum(power, axis=1, keepdims=True)
                slot_gate[j, pl.ds(b * CAP, CAP), :] = jnp.broadcast_to(value, (CAP, 128))
            gate[j, part, :] = low(g)
            up[j, part, :] = low(u)
            h = low(g * jax.nn.sigmoid(g) * u * slot_gate[j, part, :][:, :1])
            hidden[j, part, :] = h

        if layer != 0:
            down(z)
        for copy in outs(z)[: 5 if layer == 0 else 6]:
            copy.start()

    gather_blocks(x_ref, gather, compute, carried)
    if layer == 0:
        carried.finish()
        ready = pick_weights((wd_own,), (wd_other,), (wd,), wsem, layer)
        ready(0)
        for z in range(4):
            down(z)
            outs(z)[5].start()
    for z in range(4):
        for copy in outs(z):
            copy.wait()


def expert_forward(layer, x, pick, chosen, router, mine, own, other, collective_id):
    count, width, units = own[0].shape
    rows = x.shape[0]
    slots = 16 * CAP
    bf = jnp.bfloat16
    anywhere = pl.BlockSpec(memory_space=pl.ANY)
    near = pl.BlockSpec(memory_space=pltpu.VMEM)
    results = [
        ((count, slots, width), bf),
        ((count, slots, units), bf),
        ((count, slots, units), bf),
        ((count, slots, units), bf),
        ((count, slots, 128), jnp.float32),
        ((16, count * CAP, width), bf),
    ]

    def kernel(*refs):
        if layer == 0:
            refs = refs[:10] + refs[16:17] + refs[10:16] + refs[17:]
        expert_forward_kernel(layer, *refs)

    shapes = [jax.ShapeDtypeStruct(*result) for result in results]
    if layer == 0:
        shapes.append(jax.ShapeDtypeStruct(own[2].shape, bf))
        other = other[:2]
    operands = (x, pick, chosen, router, mine, *own, *other)
    return pl.pallas_call(
        kernel,
        out_shape=shapes,
        in_specs=[anywhere, near, near, near, near] + [anywhere] * (len(operands) - 5),
        out_specs=[anywhere] * len(shapes),
        scratch_shapes=[pltpu.VMEM(weight.shape, bf) for weight in own]
        + [pltpu.VMEM(*result) for result in results]
        + [DMA((3,)), DMA((6, 4)), DMA((1, 2))]
        + gather_scratch(rows, width),
        compiler_params=pltpu.CompilerParams(
            collective_id=collective_id, has_side_effects=True, vmem_limit_bytes=60 << 20
        ),
        cost_estimate=cost(),
        name="expert_forward",
    )(*operands)


def combine_kernel(sections, pick_ref, y_ref, *refs):
    kept = len(sections)
    sources, out_ref, targets = refs[:kept], refs[kept], refs[kept + 1 : 2 * kept + 1]
    y, sent, own, core_in, y_in, z_in, lsem, zs, zr, ys, yr, cs, cr, carry_sem = refs[2 * kept + 1 :]
    carried = Carried(sections, sources, targets, carry_sem)
    d, s = lax.axis_index("dp"), lax.axis_index("seq")
    half = out_ref.shape[0] // 2

    def loaded(b):
        return pltpu.make_async_copy(y_ref.at[b], y.at[b], lsem.at[b])

    def column(across, other_core):
        return s ^ (2 * across) ^ other_core

    for i in range(4):
        z = d ^ (3 - i)
        for across in (1, 0):
            for other_core in (1, 0):
                loaded(z * 4 + column(across, other_core)).start()
    greet(d, s, carried.section)
    carried.start()

    def rows(k):
        return pl.ds(pl.multiple_of(k * half, half), half)

    def partial_sum(z, k, across, other_core):
        b = z * 4 + column(across, other_core)

        @pl.when(k == 0)
        def _():
            loaded(b).wait()

        return dot(pick_ref[b, rows(k), :], y[b])

    def core_copy(z, k, across):
        return remote(
            sent.at[z, across, rows(k)],
            core_in.at[z, across, rows(k)],
            cs.at[z, k, across],
            cr.at[z, k, across],
            seq=s ^ 1,
        )

    def y_copy(z, k):
        return remote(own.at[z, 1, rows(k)], y_in.at[z, rows(k)], ys.at[z, k], yr.at[z, k], seq=s ^ 2)

    def z_copy(z, k, right):
        target = d + 1 if right else d - 1
        return remote(
            own.at[z, 0, rows(k)],
            z_in.at[int(right), z, rows(k)],
            zs.at[z, k],
            zr.at[int(right), z, k],
            dp=target,
        )

    def start(i):
        z, k = d ^ (3 - i // 2), i % 2
        sent[z, 1, rows(k), :] = low(partial_sum(z, k, 1, 1))
        core_copy(z, k, 1).start()
        total = partial_sum(z, k, 1, 0)
        core_copy(z, k, 1).wait_recv()
        own[z, 1, rows(k), :] = low(total + core_in[z, 1, rows(k), :].astype(jnp.float32))
        y_copy(z, k).start()
        sent[z, 0, rows(k), :] = low(partial_sum(z, k, 0, 1))
        core_copy(z, k, 0).start()

    start(0)

    @pl.loop(0, 8)
    def _(i):
        @pl.when(i < 7)
        def _():
            start(i + 1)

        z, k = d ^ (3 - i // 2), i % 2
        total = partial_sum(z, k, 0, 0)
        core_copy(z, k, 0).wait_recv()
        total = total + core_in[z, 0, rows(k), :].astype(jnp.float32)
        y_copy(z, k).wait_recv()
        total = total + y_in[z, rows(k), :].astype(jnp.float32)

        @pl.when(z < d)
        def _():
            @pl.when(d < 3)
            def _():
                z_copy(z, k, False).wait_recv()
                own[z, 0, rows(k), :] = low(total + z_in[0, z, rows(k), :].astype(jnp.float32))

            @pl.when(d == 3)
            def _():
                own[z, 0, rows(k), :] = low(total)

            z_copy(z, k, False).start()

        @pl.when(z > d)
        def _():
            @pl.when(d > 0)
            def _():
                z_copy(z, k, True).wait_recv()
                own[z, 0, rows(k), :] = low(total + z_in[1, z, rows(k), :].astype(jnp.float32))

            @pl.when(d == 0)
            def _():
                own[z, 0, rows(k), :] = low(total)

            z_copy(z, k, True).start()

        @pl.when(z == d)
        def _():
            out_ref[rows(k), :] = total

    for k in range(2):

        @pl.when(d < 3)
        def _():
            z_copy(d, k, False).wait_recv()
            out_ref[rows(k), :] += z_in[0, d, rows(k), :].astype(jnp.float32)

        @pl.when(d > 0)
        def _():
            z_copy(d, k, True).wait_recv()
            out_ref[rows(k), :] += z_in[1, d, rows(k), :].astype(jnp.float32)

    for z in range(4):
        for k in range(2):
            core_copy(z, k, 0).wait_send()
            core_copy(z, k, 1).wait_send()
            y_copy(z, k).wait_send()

            @pl.when(z < d)
            def _():
                z_copy(z, k, False).wait_send()

            @pl.when(z > d)
            def _():
                z_copy(z, k, True).wait_send()

    carried.finish()


def combine(pick_t, y, collective_id, carry):
    rows, width = pick_t.shape[1], y.shape[2]
    anywhere = pl.BlockSpec(memory_space=pl.ANY)
    near = pl.BlockSpec(memory_space=pltpu.VMEM)
    sections = tuple(to for to, _ in carry)
    arrays = [array for _, array in carry]

    def kernel(*refs):
        combine_kernel(sections, *refs)

    def blocks(*lead):
        return pltpu.VMEM(lead + (rows, width), jnp.bfloat16)

    return pl.pallas_call(
        kernel,
        out_shape=[jax.ShapeDtypeStruct((rows, width), jnp.float32)]
        + [jax.ShapeDtypeStruct(array.shape, array.dtype) for array in arrays],
        in_specs=[near, anywhere] + [anywhere] * len(arrays),
        out_specs=[near] + [anywhere] * len(arrays),
        scratch_shapes=[
            pltpu.VMEM(y.shape, jnp.bfloat16),
            blocks(4, 2),
            blocks(4, 2),
            blocks(4, 2),
            blocks(4),
            blocks(2, 4),
            DMA((16,)),
            DMA((4, 2)),
            DMA((2, 4, 2)),
            DMA((4, 2)),
            DMA((4, 2)),
            DMA((4, 2, 2)),
            DMA((4, 2, 2)),
            DMA((max(1, len(arrays)), 2)),
        ],
        compiler_params=pltpu.CompilerParams(
            collective_id=collective_id, has_side_effects=True, vmem_limit_bytes=60 << 20
        ),
        cost_estimate=cost(),
        name="combine",
    )(pick_t, y, *arrays)


def expert_backward_kernel(
    layer, sections, x_ref, pick_ref, gate_in, up_in, slot_gate_in,
    wg_own, wu_own, wd_own, wg_other, wu_other, wd_other, *refs
):
    kept = len(sections)
    sources, refs = refs[:kept], refs[kept:]
    rows_out, gate_out, up_out, term_out, y_out, *refs = refs
    targets, refs = refs[:kept], refs[kept:]
    wg, wu, wd, rows, gate, up, slot_gate, y, wsem, isem, osem, carry_sem, *gather = refs
    carried = Carried(sections, sources, targets, carry_sem)
    count = wg.shape[0]
    ready = pick_weights(
        (wg_own, wu_own, wd_own), (wg_other, wu_other, wd_other), (wg, wu, wd), wsem, layer
    )
    land = gather[0]
    d = lax.axis_index("dp")
    ins = [
        pltpu.make_async_copy(src, held, isem.at[k])
        for k, (src, held) in enumerate(((gate_in, gate), (up_in, up), (slot_gate_in, slot_gate)))
    ]
    for copy in ins:
        copy.start()

    def outs(z):
        part = pl.ds(z * 4 * CAP, 4 * CAP)
        return [
            pltpu.make_async_copy(held.at[:, part], out.at[:, part], osem.at[k, z])
            for k, (held, out) in enumerate(
                ((rows, rows_out), (gate, gate_out), (up, up_out), (slot_gate, term_out))
            )
        ] + [pltpu.make_async_copy(y.at[pl.ds(z * 4, 4)], y_out.at[pl.ds(z * 4, 4)], osem.at[4, z])]

    def compute(z):
        @pl.when(z == d)
        def _():
            for k in range(3):
                ready(k)
            for copy in ins:
                copy.wait()

        for q in range(4):
            b = z * 4 + q
            picked = low(dot(pick_ref[b], land[b]))
            for j in range(count):
                rows[j, pl.ds(b * CAP, CAP), :] = picked[j * CAP : (j + 1) * CAP]
        part = pl.ds(z * 4 * CAP, 4 * CAP)

        @pl.loop(0, count)
        def _(j):
            plain = dot_t(rows[j, part, :], wd[j])
            g = gate[j, part, :].astype(jnp.float32)
            u = up[j, part, :].astype(jnp.float32)
            sigmoid = jax.nn.sigmoid(g)
            active = g * sigmoid
            term = jnp.sum(plain * (active * u), axis=1, keepdims=True)
            grad = plain * slot_gate[j, part, :][:, :1]
            dg = low(grad * u * sigmoid * (1.0 + g * (1.0 - sigmoid)))
            du = low(grad * active)
            slot_gate[j, part, :] = jnp.broadcast_to(term, (4 * CAP, 128))
            gate[j, part, :] = dg
            up[j, part, :] = du
            result = low(dot_t(dg, wg[j]) + dot_t(du, wu[j]))
            for q in range(4):
                y[z * 4 + q, pl.ds(j * CAP, CAP), :] = result[q * CAP : (q + 1) * CAP]

        for copy in outs(z):
            copy.start()

    gather_blocks(x_ref, gather, compute, carried)
    carried.finish()
    for z in range(4):
        for copy in outs(z):
            copy.wait()


def expert_backward(layer, x, pick, gate, up, slot_gate, own, other, collective_id, carry):
    count, width, units = own[0].shape
    rows = x.shape[0]
    slots = 16 * CAP
    bf = jnp.bfloat16
    anywhere = pl.BlockSpec(memory_space=pl.ANY)
    near = pl.BlockSpec(memory_space=pltpu.VMEM)
    results = [
        ((count, slots, width), bf),
        ((count, slots, units), bf),
        ((count, slots, units), bf),
        ((count, slots, 128), jnp.float32),
        ((16, count * CAP, width), bf),
    ]
    sections = tuple(to for to, _ in carry)
    arrays = [array for _, array in carry]

    def kernel(*refs):
        expert_backward_kernel(layer, sections, *refs)

    return pl.pallas_call(
        kernel,
        out_shape=[jax.ShapeDtypeStruct(*result) for result in results]
        + [jax.ShapeDtypeStruct(array.shape, array.dtype) for array in arrays],
        in_specs=[anywhere, near] + [anywhere] * (9 + len(arrays)),
        out_specs=[anywhere] * (5 + len(arrays)),
        scratch_shapes=[pltpu.VMEM(weight.shape, bf) for weight in own]
        + [pltpu.VMEM(*result) for result in results]
        + [DMA((3,)), DMA((3,)), DMA((5, 4)), DMA((max(1, len(arrays)), 2))]
        + gather_scratch(rows, width),
        compiler_params=pltpu.CompilerParams(
            collective_id=collective_id, has_side_effects=True, vmem_limit_bytes=60 << 20
        ),
        cost_estimate=cost(),
        name="expert_backward",
    )(x, pick, gate, up, slot_gate, *own, *other, *arrays)


def rope(x, cos_table, sin_table):
    lane = lax.broadcasted_iota(jnp.int32, x.shape, 1)
    turned = jnp.where(lane % HEAD_DIM < HEAD_DIM // 2, pltpu.roll(x, 128 - HEAD_DIM // 2, 1), pltpu.roll(x, HEAD_DIM // 2, 1))
    return x * cos_table + turned * sin_table


def seq_greet(s, section):
    barrier = pltpu.get_barrier_semaphore()
    for device in (dict(seq=s ^ 1), dict(seq=s ^ 2), dict(section=1 - section)):
        pl.semaphore_signal(barrier, inc=1, device_id=device, device_id_type=MESH)
    pl.semaphore_wait(barrier, 3)


def seq_scratch(rows, width):
    return [
        pltpu.VMEM((4, rows, width), jnp.bfloat16),
        pltpu.VMEM((2, rows, width), jnp.bfloat16),
        pltpu.VMEM((2, rows, width), jnp.bfloat16),
        pltpu.VMEM((rows, width), jnp.bfloat16),
        pltpu.VMEM((rows, width), jnp.bfloat16),
        DMA(()),
        DMA((4, 2)),
        DMA((3, 2)),
    ]


class Line:
    def __init__(self, scratch):
        self.land, self.sent, self.core_in, self.y_sent, self.y_in, self.lsem, self.ag, self.rs = scratch
        self.s = lax.axis_index("seq")

    def hop(self, src, dst, sems, k, flip):
        return remote(src, dst, sems.at[k, 0], sems.at[k, 1], seq=self.s ^ flip)

    def gather(self, x_ref, use):
        s, land = self.s, self.land
        own = pltpu.make_async_copy(x_ref, land.at[s], self.lsem)
        own.start()
        over = self.hop(x_ref, land.at[s], self.ag, 0, 2)
        beside = self.hop(x_ref, land.at[s], self.ag, 1, 1)
        over.start()
        beside.start()
        own.wait()
        use(s)
        beside.wait_recv()
        use(s ^ 1)
        over.wait_recv()
        further = self.hop(land.at[s ^ 2], land.at[s ^ 2], self.ag, 2, 1)
        further.start()
        use(s ^ 2)
        further.wait_recv()
        use(s ^ 3)
        over.wait_send()
        beside.wait_send()
        further.wait_send()

    def hand_over(self, t, partial, out_ref):
        relation = t ^ self.s

        @pl.when(relation == 3)
        def _():
            self.sent[0] = low(partial[...])
            self.hop(self.sent.at[0], self.core_in.at[0], self.rs, 0, 1).start()

        @pl.when(relation == 2)
        def _():
            self.hop(self.sent.at[0], self.core_in.at[0], self.rs, 0, 1).wait_recv()
            self.y_sent[...] = low(partial[...] + self.core_in[0].astype(jnp.float32))
            self.hop(self.y_sent, self.y_in, self.rs, 1, 2).start()

        @pl.when(relation == 1)
        def _():
            self.sent[1] = low(partial[...])
            self.hop(self.sent.at[1], self.core_in.at[1], self.rs, 2, 1).start()

        @pl.when(relation == 0)
        def _():
            out_ref[...] = partial[...]

    def finish(self, out_ref):
        self.hop(self.sent.at[1], self.core_in.at[1], self.rs, 2, 1).wait()
        out_ref[...] += self.core_in[1].astype(jnp.float32)
        self.hop(self.y_sent, self.y_in, self.rs, 1, 2).wait()
        out_ref[...] += self.y_in[...].astype(jnp.float32)
        self.hop(self.sent.at[0], self.core_in.at[0], self.rs, 0, 1).wait_send()


def attention_forward_kernel(sections, x_ref, qkv_ref, wo_ref, cos_ref, sin_ref, *refs):
    kept = len(sections)
    sources, refs = refs[:kept], refs[kept:]
    out_ref, all_out, heads_out, lse_out, ot_out, *refs = refs
    targets, refs = refs[:kept], refs[kept:]
    wqkv, wo, heads, lse, ot, partial, wsem, osem, carry_sem, *line = refs
    line = Line(line)
    carried = Carried(sections, sources, targets, carry_sem)
    s = line.s
    rows = out_ref.shape[0]
    kv = heads.shape[0] // (GROUP + 2)
    queries = GROUP * kv
    loads = [pltpu.make_async_copy(qkv_ref, wqkv, wsem.at[0]), pltpu.make_async_copy(wo_ref, wo, wsem.at[1])]
    for load in loads:
        load.start()
    seq_greet(s, carried.section)
    carried.start()
    lse[...] = jnp.zeros_like(lse)

    def project(t):
        part = pl.ds(pl.multiple_of(t * rows, rows), rows)

        @pl.when(t == s)
        def _():
            loads[0].wait()

        qkv = low(dot(line.land[t], wqkv[...]))
        for chunk in range((queries + kv) // 2):
            x = qkv[:, chunk * 128 : (chunk + 1) * 128].astype(jnp.float32)
            x = low(rope(x, cos_ref[part, :], sin_ref[part, :]))
            heads[2 * chunk, part, :] = x[:, :HEAD_DIM]
            heads[2 * chunk + 1, part, :] = x[:, HEAD_DIM:]
        for j in range(kv):
            begin = (queries + kv + j) * HEAD_DIM
            heads[queries + kv + j, part, :] = qkv[:, begin : begin + HEAD_DIM]

    line.gather(x_ref, project)
    saves = [pltpu.make_async_copy(line.land, all_out, osem.at[0]), pltpu.make_async_copy(heads, heads_out, osem.at[1])]
    for save in saves:
        save.start()
    loads[1].wait()

    def attend(block):
        keys = (block + 1) * rows
        columns = slice(block * rows, (block + 1) * rows)

        @pl.loop(0, queries)
        def _(h):
            j = h // GROUP
            scores = dot_t(heads[queries + j, :keys, :], heads[h, columns, :]) * 0.125
            key_at = lax.broadcasted_iota(jnp.int32, scores.shape, 0)
            query_at = lax.broadcasted_iota(jnp.int32, scores.shape, 1) + block * rows
            scores = jnp.where(key_at <= query_at, scores, -jnp.inf)
            peak = jnp.max(scores, axis=0, keepdims=True)
            power = jnp.exp(scores - peak)
            total = jnp.sum(power, axis=0, keepdims=True)
            attended = t_dot(heads[queries + kv + j, :keys, :], low(power / total))
            ot[pl.ds(pl.multiple_of(h * HEAD_DIM, HEAD_DIM), HEAD_DIM), columns] = low(attended)
            lse[pl.ds(h, 1), columns] = peak + jnp.log(total)

        partial[...] = t_dot(ot[:, columns], wo[...])

    @pl.loop(0, 4)
    def _(i):
        t = s ^ (3 - i)
        for block in range(4):

            @pl.when(t == block)
            def _():
                attend(block)

        line.hand_over(t, partial, out_ref)

    saves += [pltpu.make_async_copy(lse, lse_out, osem.at[2]), pltpu.make_async_copy(ot, ot_out, osem.at[3])]
    for save in saves[2:]:
        save.start()
    line.finish(out_ref)
    carried.finish()
    for save in saves:
        save.wait()


def attention_forward_call(x, qkv_w, out_w, tables, collective_id, carry):
    rows, width = x.shape
    local_heads = qkv_w.shape[1] // HEAD_DIM
    bf, f32 = jnp.bfloat16, jnp.float32
    anywhere = pl.BlockSpec(memory_space=pl.ANY)
    near = pl.BlockSpec(memory_space=pltpu.VMEM)
    sections = tuple(to for to, _ in carry)
    arrays = [array for _, array in carry]
    results = [
        ((rows, width), f32),
        ((4, rows, width), bf),
        ((local_heads, 4 * rows, HEAD_DIM), bf),
        ((8, 4 * rows), f32),
        ((out_w.shape[0], 4 * rows), bf),
    ]

    def kernel(*refs):
        attention_forward_kernel(sections, *refs)

    return pl.pallas_call(
        kernel,
        out_shape=[jax.ShapeDtypeStruct(*result) for result in results]
        + [jax.ShapeDtypeStruct(array.shape, array.dtype) for array in arrays],
        in_specs=[anywhere] * 3 + [near] * 2 + [anywhere] * len(arrays),
        out_specs=[near] + [anywhere] * (4 + len(arrays)),
        scratch_shapes=[
            pltpu.VMEM(qkv_w.shape, bf),
            pltpu.VMEM(out_w.shape, bf),
            pltpu.VMEM(*results[2]),
            pltpu.VMEM(*results[3]),
            pltpu.VMEM(*results[4]),
            pltpu.VMEM((rows, width), f32),
            DMA((2,)),
            DMA((4,)),
            DMA((max(1, len(arrays)), 2)),
        ]
        + seq_scratch(rows, width),
        compiler_params=pltpu.CompilerParams(
            collective_id=collective_id, has_side_effects=True, vmem_limit_bytes=60 << 20
        ),
        cost_estimate=cost(),
        name="attention_forward",
    )(x, qkv_w, out_w, *tables, *arrays)


def attention_backward_kernel(sections, x_ref, qkv_ref, wo_ref, cos_ref, sin_ref, heads_in, lse_ref, *refs):
    kept = len(sections)
    sources, refs = refs[:kept], refs[kept:]
    out_ref, all_out, grads_out, *refs = refs
    targets, refs = refs[:kept], refs[kept:]
    wqkv, wo, heads, douts, dk, dv, dqt, grads, partial, wsem, osem, carry_sem, *line = refs
    line = Line(line)
    carried = Carried(sections, sources, targets, carry_sem)
    s = line.s
    rows = out_ref.shape[0]
    kv = heads.shape[0] // (GROUP + 2)
    queries = GROUP * kv
    loads = [
        pltpu.make_async_copy(wo_ref, wo, wsem.at[0]),
        pltpu.make_async_copy(qkv_ref, wqkv, wsem.at[1]),
        pltpu.make_async_copy(heads_in, heads, wsem.at[2]),
    ]
    for load in loads:
        load.start()
    seq_greet(s, carried.section)
    carried.start()
    dk[...] = jnp.zeros_like(dk)
    dv[...] = jnp.zeros_like(dv)

    def project(t):
        part = pl.ds(pl.multiple_of(t * rows, rows), rows)

        @pl.when(t == s)
        def _():
            loads[0].wait()

        grad = low(dot_t(line.land[t], wo[...]))
        for h in range(queries):
            douts[h, part, :] = grad[:, h * HEAD_DIM : (h + 1) * HEAD_DIM]

    line.gather(x_ref, project)
    saves = [pltpu.make_async_copy(line.land, all_out, osem.at[0])]
    saves[0].start()
    loads[1].wait()
    loads[2].wait()

    for block in (3, 2, 1, 0):
        keys = (block + 1) * rows
        part = slice(block * rows, (block + 1) * rows)

        @pl.loop(0, queries)
        def _(h):
            j = h // GROUP
            key = heads[queries + j, :keys, :]
            query = heads[h, part, :]
            grad = douts[h, part, :]
            scores = dot_t(key, query) * 0.125
            key_at = lax.broadcasted_iota(jnp.int32, scores.shape, 0)
            query_at = lax.broadcasted_iota(jnp.int32, scores.shape, 1) + block * rows
            scores = jnp.where(key_at <= query_at, scores, -jnp.inf)
            probs = jnp.exp(scores - lse_ref[pl.ds(h, 1), part])
            dprobs = dot_t(heads[queries + kv + j, :keys, :], grad)
            mean = jnp.sum(probs * dprobs, axis=0, keepdims=True)
            dscores = low(probs * (dprobs - mean))
            dk[j, :keys, :] += dot(dscores, query) * 0.125
            dv[j, :keys, :] += dot(low(probs), grad)
            dqt[pl.ds(pl.multiple_of(h * HEAD_DIM, HEAD_DIM), HEAD_DIM), :] = t_dot(key, dscores) * 0.125

        cos_part, sin_part = cos_ref[part, :], -sin_ref[part, :]
        dq = dqt[...].T
        for chunk in range(queries // 2):
            lanes = slice(chunk * 128, (chunk + 1) * 128)
            grads[part, lanes] = low(rope(dq[:, lanes], cos_part, sin_part))
        for pair in range(kv // 2):
            both = jnp.concatenate([dk[2 * pair, part, :], dk[2 * pair + 1, part, :]], axis=1)
            begin = queries * HEAD_DIM + pair * 128
            grads[part, begin : begin + 128] = low(rope(both, cos_part, sin_part))
            both = jnp.concatenate([dv[2 * pair, part, :], dv[2 * pair + 1, part, :]], axis=1)
            begin = (queries + kv) * HEAD_DIM + pair * 128
            grads[part, begin : begin + 128] = low(both)
        partial[...] = dot_t(grads[part, :], wqkv[...])
        line.hand_over(block, partial, out_ref)

    saves.append(pltpu.make_async_copy(grads, grads_out, osem.at[1]))
    saves[1].start()
    line.finish(out_ref)
    carried.finish()
    for save in saves:
        save.wait()


def attention_backward_call(x, qkv_w, out_w, tables, heads, lse, collective_id, carry):
    rows, width = x.shape
    bf, f32 = jnp.bfloat16, jnp.float32
    anywhere = pl.BlockSpec(memory_space=pl.ANY)
    near = pl.BlockSpec(memory_space=pltpu.VMEM)
    sections = tuple(to for to, _ in carry)
    arrays = [array for _, array in carry]
    results = [((rows, width), f32), ((4, rows, width), bf), ((4 * rows, qkv_w.shape[1]), bf)]
    kv = heads.shape[0] // (GROUP + 2)
    queries = GROUP * kv

    def kernel(*refs):
        attention_backward_kernel(sections, *refs)

    return pl.pallas_call(
        kernel,
        out_shape=[jax.ShapeDtypeStruct(*result) for result in results]
        + [jax.ShapeDtypeStruct(array.shape, array.dtype) for array in arrays],
        in_specs=[anywhere] * 3 + [near] * 2 + [anywhere, near] + [anywhere] * len(arrays),
        out_specs=[near] + [anywhere] * (2 + len(arrays)),
        scratch_shapes=[
            pltpu.VMEM(qkv_w.shape, bf),
            pltpu.VMEM(out_w.shape, bf),
            pltpu.VMEM(heads.shape, bf),
            pltpu.VMEM((queries, 4 * rows, HEAD_DIM), bf),
            pltpu.VMEM((kv, 4 * rows, HEAD_DIM), f32),
            pltpu.VMEM((kv, 4 * rows, HEAD_DIM), f32),
            pltpu.VMEM((queries * HEAD_DIM, rows), f32),
            pltpu.VMEM(*results[2]),
            pltpu.VMEM((rows, width), f32),
            DMA((3,)),
            DMA((2,)),
            DMA((max(1, len(arrays)), 2)),
        ]
        + seq_scratch(rows, width),
        compiler_params=pltpu.CompilerParams(
            collective_id=collective_id, has_side_effects=True, vmem_limit_bytes=60 << 20
        ),
        cost_estimate=cost(),
        name="attention_backward",
    )(x, qkv_w, out_w, *tables, heads, lse, *arrays)


def wide_tables(length):
    cos_table, sin_table = rotary_tables(length)
    cos_table, sin_table = cos_table[:, 0], sin_table[:, 0]
    return (
        jnp.concatenate([cos_table] * 4, axis=1),
        jnp.concatenate([-sin_table, sin_table] * 2, axis=1),
    )


def token_choice(route):
    return route[..., None] == jnp.arange(EXPERTS, dtype=jnp.int32)


def routing(route_all, first_expert, count):
    chosen = jnp.any(token_choice(route_all), axis=2)
    blocks, rows = chosen.shape[:2]
    mine = lax.dynamic_slice_in_dim(chosen, first_expert, count, axis=2)
    chosen = low(jnp.transpose(chosen, (0, 2, 1)))
    earlier = jnp.tril(jnp.ones((rows, rows), jnp.bfloat16), -1)
    place = jnp.einsum(
        "ts,bsj->bjt", earlier, mine.astype(jnp.bfloat16), preferred_element_type=jnp.float32
    ).astype(jnp.int32)
    mine = jnp.transpose(mine, (0, 2, 1))
    place = jnp.where(mine, place, -1)
    slots = jnp.arange(CAP, dtype=jnp.int32)
    pick = low(place[:, :, None, :] == slots[None, None, :, None]).reshape(blocks, -1, rows)
    return chosen, pick, jnp.transpose(pick, (0, 2, 1))


def choose(pick, rows, count):
    picked = jnp.einsum("bct,btd->bcd", pick, rows, preferred_element_type=jnp.float32)
    blocks = pick.shape[0]
    picked = low(picked).reshape(blocks, count, CAP, -1)
    return jnp.transpose(picked, (1, 0, 2, 3)).reshape(count, blocks * CAP, -1)


def give_back(pick_t, slot_rows):
    blocks, rows = pick_t.shape[:2]
    count, _, width = slot_rows.shape
    slot_rows = jnp.transpose(slot_rows.reshape(count, blocks, CAP, width), (1, 0, 2, 3))
    slot_rows = slot_rows.reshape(blocks, count * CAP, width)
    total = jnp.einsum("btc,bcd->btd", pick_t, slot_rows, preferred_element_type=jnp.float32)
    return low(total).reshape(-1, width)


def each_dot(form, a, b):
    return jnp.einsum(form, a, b, preferred_element_type=jnp.float32)


def after(value, *others):
    return lax.optimization_barrier((value, *others))[0]


def has_kernels():
    return lax.axis_size("dp") == 4 and lax.axis_size("seq") == 4


def forward_layer(number, layer_in, picking, weights, experts, *carry):
    attn_scale, ffn_scale, qkv_w, out_w, router_w = weights
    chosen, pick, pick_t, first_expert = picking
    own, other = experts
    count = own[0].shape[0]
    blocks, _, rows = chosen.shape
    received = []
    normed_input = low(rms_norm(layer_in, attn_scale))
    if has_kernels():
        branch, normed_all, heads, log_total, mixed_t, *received = attention_forward_call(
            normed_input, qkv_w, out_w, wide_tables(4 * layer_in.shape[0]), 9 + number, carry
        )
        attention_state = (normed_all.reshape(-1, layer_in.shape[1]), mixed_t, heads, log_total)
    else:
        received = [swap(array) if to is None else pass_to(array, to) for to, array in carry]
        normed_all = lax.all_gather(normed_input, "seq", axis=0, tiled=True)
        qkv = low(dot(normed_all, qkv_w))
        kv_width = KV_HEADS * HEAD_DIM // lax.axis_size("seq")
        q_width = GROUP * kv_width
        mixed, log_total, q_rot, k_rot, v_heads = attention_forward(
            qkv[:, :q_width], qkv[:, q_width : q_width + kv_width], qkv[:, q_width + kv_width :]
        )
        branch = lax.psum_scatter(low(dot(mixed, out_w)), "seq", scatter_dimension=0, tiled=True)
        attention_state = (normed_all, mixed.T, (q_rot, k_rot, v_heads), log_total)
    after_update = layer_in + branch.astype(jnp.float32)
    normed_ffn = low(rms_norm(after_update, ffn_scale))
    own_block = lax.axis_index("dp") * lax.axis_size("seq") + lax.axis_index("seq")
    own_chosen = lax.dynamic_index_in_dim(chosen, own_block, 0, keepdims=False)
    own_logits = jnp.where(own_chosen > 0, dot_t(router_w, normed_ffn), -jnp.inf)
    own_gates = jax.nn.softmax(own_logits, axis=0)
    if number == 0:
        other = other + (received[0],)
    mine = (
        jnp.arange(EXPERTS)[None, None, :] == first_expert + jnp.arange(count)[:, None, None]
    ).astype(jnp.float32)
    if has_kernels():
        *expert_state, slot_out = expert_forward(
            number, normed_ffn, pick, chosen, router_w, mine, own, other, 1 + number
        )
        if number == 0:
            *expert_state, slot_out, other_down = (*expert_state, slot_out)
            other = other[:2] + (other_down,)
    else:
        if number == 0:
            other = other[:2] + (swap(own[2]),)
        gate_w, up_w, down_w = by_layer(number, own, other)
        ffn_all = lax.all_gather(normed_ffn, TOKENS, axis=0, tiled=True)
        logits = dot_t(ffn_all, router_w).reshape(blocks, rows, EXPERTS)
        used = jnp.transpose(chosen, (0, 2, 1)) > 0
        gates = jax.nn.softmax(jnp.where(used, logits, -jnp.inf), axis=-1)
        slot_rows = choose(pick, ffn_all.reshape(blocks, rows, -1), count)
        mine_gates = jnp.einsum("bte,jxe->bjt", gates, mine, precision=lax.Precision.HIGHEST)
        slot_gates = jnp.sum(
            pick.reshape(blocks, count, CAP, rows).astype(jnp.float32) * mine_gates[:, :, None, :],
            axis=3,
        )
        slot_gates = jnp.transpose(slot_gates, (1, 0, 2)).reshape(count, -1, 1)
        gate_pre = each_dot("ecd,edf->ecf", slot_rows, gate_w)
        up_pre = each_dot("ecd,edf->ecf", slot_rows, up_w)
        scaled = low(slot_gates * jax.nn.silu(gate_pre) * up_pre)
        slot_out = low(each_dot("ecf,efd->ecd", scaled, down_w))
        expert_state = (slot_rows, gate_pre, up_pre, scaled, slot_gates)
    saved = (
        layer_in,
        attention_state,
        after_update,
        normed_ffn,
        own_gates,
        expert_state,
    )
    return (after_update, slot_out, saved, (own, other), received)


def token_sums(pick_t, slot_out, collective_id, *carry):
    if has_kernels():
        sums, *received = combine(pick_t, slot_out, collective_id, carry)
        return sums, received
    sums = give_back(pick_t, slot_out).astype(jnp.float32)
    sums = lax.psum_scatter(sums, TOKENS, scatter_dimension=0, tiled=True)
    return sums, [pass_to(array, to) for to, array in carry]


def expert_gradients(number, layer_grad, saved, picking, experts, *carry):
    chosen, pick, pick_t, first_expert = picking
    own, other = experts
    count = own[0].shape[0]
    blocks, _, rows = chosen.shape
    slot_rows, gate_pre, up_pre, scaled, slot_gates = saved[-1]
    if has_kernels():
        slot_grads, gate_low, up_low, gate_term, slot_out, *received = expert_backward(
            number, low(layer_grad), pick, gate_pre, up_pre, slot_gates, own, other, 4 + number, carry
        )
        gate_term = gate_term[:, :, :1]
    else:
        gate_w, up_w, down_w = by_layer(number, own, other)
        grad_all = lax.all_gather(low(layer_grad), TOKENS, axis=0, tiled=True)
        slot_grads = choose(pick, grad_all.reshape(blocks, rows, -1), count)
        plain_grad = each_dot("ecd,efd->ecf", slot_grads, down_w)
        sigmoid = jax.nn.sigmoid(gate_pre)
        activated = gate_pre * sigmoid
        gate_term = jnp.sum(plain_grad * (activated * up_pre), axis=2, keepdims=True)
        hidden_grad = slot_gates * plain_grad
        gate_low = low(hidden_grad * up_pre * sigmoid * (1.0 + gate_pre * (1.0 - sigmoid)))
        up_low = low(hidden_grad * activated)
        slot_out = low(
            each_dot("ecf,edf->ecd", gate_low, gate_w) + each_dot("ecf,edf->ecd", up_low, up_w)
        )
        received = [pass_to(array, to) for to, array in carry]
    expert_grads = (
        low(each_dot("ecd,ecf->edf", slot_rows, gate_low)),
        low(each_dot("ecd,ecf->edf", slot_rows, up_low)),
        low(each_dot("ecf,ecd->efd", scaled, slot_grads)),
    )
    slot_out, *expert_grads = lax.optimization_barrier((slot_out, *expert_grads))
    return slot_out, gate_term, expert_grads, received


def backward_layer(number, layer_grad, normed_grad, gate_term, saved, picking, weights, *carry):
    attn_scale, ffn_scale, qkv_w, out_w, router_w = weights
    chosen, pick, _, _ = picking
    (
        layer_in,
        (normed_all, mixed_t, heads, log_total),
        after_update,
        normed_ffn,
        own_gates,
        _,
    ) = saved
    blocks, _, rows = chosen.shape
    count = gate_term.shape[0]
    by_slot = jnp.transpose(gate_term.reshape(count, blocks, CAP), (1, 0, 2))
    gate_terms = jnp.sum(
        pick.reshape(blocks, count, CAP, rows).astype(jnp.float32) * by_slot[..., None], axis=2
    )
    gate_terms = lax.all_to_all(gate_terms, TOKENS, split_axis=0, concat_axis=0, tiled=True)
    gate_terms = jnp.sum(gate_terms.reshape(EXPERTS, -1, rows), axis=1)
    logit_grad = low(
        own_gates * (gate_terms - jnp.sum(own_gates * gate_terms, axis=0, keepdims=True))
    )
    router_grad = dot(logit_grad, normed_ffn)
    normed_grad = normed_grad + t_dot(logit_grad, router_w)
    after_part, ffn_gain_grad = jax.vjp(rms_norm, after_update, ffn_scale)[1](normed_grad)
    after_grad = after_part + layer_grad
    if has_kernels():
        normed_attn, branch_all, qkv_grad, *received = attention_backward_call(
            low(after_grad),
            qkv_w,
            out_w,
            wide_tables(4 * layer_in.shape[0]),
            heads,
            log_total,
            11 + number,
            carry,
        )
        branch_all = branch_all.reshape(-1, layer_in.shape[1])
    else:
        branch_all = lax.all_gather(low(after_grad), "seq", axis=0, tiled=True)
        head_grad = low(dot_t(branch_all, out_w))
        qkv_grad = attention_backward(head_grad, *heads, log_total)
        normed_attn = low(dot_t(qkv_grad, qkv_w))
        normed_attn = lax.psum_scatter(normed_attn, "seq", scatter_dimension=0, tiled=True)
        received = [pass_to(array, to) for to, array in carry]
    out_grad = dot(mixed_t, branch_all)
    qkv_weight_grad = t_dot(normed_all, qkv_grad)
    input_part, attn_gain_grad = jax.vjp(rms_norm, layer_in, attn_scale)[1](
        normed_attn.astype(jnp.float32)
    )
    small = [router_grad, attn_gain_grad[None], ffn_gain_grad[None]]
    small = jnp.concatenate(small + [jnp.zeros((128 - EXPERTS - 2, small[0].shape[1]))], axis=0)
    qkv_weight_grad = jnp.concatenate([low(qkv_weight_grad), low(small).T], axis=1)
    return (input_part + after_grad, (qkv_weight_grad, low(out_grad)), received)


def by_layer(number, own, other):
    is_own = lax.axis_index("section") == number
    return jax.tree.map(lambda mine, received: jnp.where(is_own, mine, received), own, other)


def body(
    hidden_in,
    out_grad,
    attn_gain,
    ffn_gain,
    query_matrix,
    key_matrix,
    value_matrix,
    output_matrix,
    router_matrix,
    w_gate,
    w_up,
    w_down,
    routes,
):
    section = lax.axis_index("section")
    dp, seq = lax.axis_size("dp"), lax.axis_size("seq")
    seq_index = lax.axis_index("seq")
    first = section == 0
    width = hidden_in.shape[3]
    depth = query_matrix.shape[1]

    layer_in = lax.dynamic_index_in_dim(hidden_in, section, 0, keepdims=False)[0]
    top_grad = lax.dynamic_index_in_dim(out_grad, section, 0, keepdims=False)[0]
    own_group = jnp.concatenate(
        [
            matrix[0].reshape(depth, seq, -1)
            for matrix in (query_matrix, key_matrix, value_matrix)
        ],
        axis=2,
    )
    to_group = []
    for flat in range(dp * seq):
        to_group.append((flat, (flat % dp) * seq + flat // dp))
    from_group = [(target, source) for source, target in to_group]
    other_group = swap(own_group)
    own_out = lax.ppermute(output_matrix[0], TOKENS, to_group)
    other_out = swap(own_out)
    local = w_gate.shape[1]
    hidden_units = w_gate.shape[3]
    if local >= seq:
        count, units = local // seq, hidden_units
        start, unit_start = seq_index * count, 0
    else:
        count, units = 1, hidden_units * local // seq
        start, unit_start = seq_index * local // seq, (seq_index % (seq // local)) * units
    first_expert = lax.axis_index("dp") * local + start
    own_experts = (
        lax.dynamic_slice(w_gate[0], (start, 0, unit_start), (count, width, units)),
        lax.dynamic_slice(w_up[0], (start, 0, unit_start), (count, width, units)),
        lax.dynamic_slice(w_down[0], (start, unit_start, 0), (count, units, width)),
    )
    other_gate = swap(after(own_experts[0], other_group))
    experts = (own_experts, (other_gate,))

    small = jnp.concatenate([router_matrix[0].T, attn_gain, ffn_gain], axis=0)
    paths = routes[0, :, 0]
    if has_kernels():
        small = jnp.pad(small, ((0, -small.shape[0] % 16), (0, 256 - depth)))
        paths = low(jnp.transpose(paths, (0, 2, 1)).reshape(2 * TOP_K, -1))
        picks, picks_t, chosens, small = prepare(
            jnp.concatenate([paths, small], axis=0), count, hidden_in.shape[2], depth, 13
        )
        pickings = [(chosens[n], picks[n], picks_t[n], first_expert) for n in range(2)]
    else:
        small = lax.all_gather(small, ("section", "dp", "seq"), axis=0, tiled=False)
        small = jnp.transpose(small.reshape(2, dp * seq, -1, depth), (0, 2, 1, 3))
        small = small.reshape(2, -1, width)
        paths = lax.all_gather(paths, ("section", "dp", "seq"), axis=0, tiled=False)
        paths = lax.dynamic_index_in_dim(paths, section, 1, keepdims=False)
        paths = paths.reshape(2, dp * seq, -1, TOP_K)
        pickings = [routing(paths[n], first_expert, count) + (first_expert,) for n in range(2)]

    weights = []
    for number in range(2):
        part = by_layer(number, own_group, other_group)
        part = lax.all_to_all(part, "seq", split_axis=1, concat_axis=0, tiled=True)
        qkv_w = lax.all_gather(part.reshape(seq * depth, -1), "dp", axis=0, tiled=True)
        out_w = lax.all_gather(
            by_layer(number, own_out, other_out), "dp", axis=0, tiled=True
        )
        weights.append(
            (
                small[number, EXPERTS].astype(jnp.float32),
                small[number, EXPERTS + 1].astype(jnp.float32),
                qkv_w,
                out_w,
                small[number, :EXPERTS],
            )
        )

    def spread(dense):
        qkv_part, out_part = dense
        qkv_part = lax.psum_scatter(qkv_part, "dp", scatter_dimension=0, tiled=True)
        qkv_part = qkv_part.reshape(seq, depth, -1)
        qkv_part = lax.all_to_all(qkv_part, "seq", split_axis=0, concat_axis=0, tiled=True)
        out_part = lax.psum_scatter(out_part, "dp", scatter_dimension=0, tiled=True)
        return (qkv_part, lax.ppermute(out_part, TOKENS, from_group))

    def own_layer(pieces):
        return jnp.where(first, pieces[0], pieces[1])

    def both_micros(own, other):
        return jnp.stack([jnp.where(first, own, other), jnp.where(first, other, own)])[
            None, :, None
        ]

    def summed(own, other):
        return own_layer(own).astype(jnp.float32) + own_layer(other).astype(jnp.float32)

    def rows_to_owners(piece, kind):
        rows = piece.shape[1] // seq
        if local >= seq:
            piece = piece.reshape(count, seq, rows, -1)
            piece = jnp.transpose(piece, (1, 0, 2, 3))
            piece = lax.all_to_all(piece, "seq", split_axis=0, concat_axis=0, tiled=True)
            piece = piece.reshape(local, rows, -1)
        elif kind < 2:
            share = seq // local
            piece = piece.reshape(seq, rows, units)
            piece = lax.all_to_all(piece, "seq", split_axis=0, concat_axis=0, tiled=True)
            piece = piece.reshape(local, share, rows, units)
            piece = jnp.transpose(piece, (0, 2, 1, 3)).reshape(local, rows, -1)
        else:
            rows = hidden_units // seq
            piece = whole_rows(piece.reshape(-1, rows, width), seq_index, seq // local, seq)
        return piece

    first_in = after(layer_in, other_gate).astype(jnp.float32)
    updated, slot_out, first_saved, experts, _ = forward_layer(
        0, first_in, pickings[0], weights[0], experts, (None, own_experts[1])
    )
    sums, _ = token_sums(pickings[0][2], slot_out, 3)
    first_out = updated + sums
    second_updated, second_slots, second_saved, experts, (other_out,) = forward_layer(
        1, first_out, pickings[1], weights[1], experts, (0, first_out)
    )
    top_grad = top_grad.astype(jnp.float32)
    slot_out, gate_term, second_experts, _ = expert_gradients(
        1, top_grad, second_saved, pickings[1], experts
    )
    sums, (second_gate,) = token_sums(pickings[1][2], slot_out, 6, (1, second_experts[0]))
    middle_grad, second_dense, (second_up,) = backward_layer(
        1, top_grad, sums, gate_term, second_saved, pickings[1], weights[1], (1, second_experts[1])
    )
    second_dense = spread(second_dense)
    slot_out, gate_term, first_experts, (second_down,) = expert_gradients(
        0, middle_grad, first_saved, pickings[0], experts, (1, second_experts[2])
    )
    sums, (first_gate, other_middle, *second_dense_in) = token_sums(
        pickings[0][2],
        slot_out,
        7,
        (0, first_experts[0]),
        (1, middle_grad),
        (1, second_dense[0]),
        (1, second_dense[1]),
    )
    gate_sum = low(summed((first_experts[0], second_experts[0]), (first_gate, second_gate)))
    gate_rows = rows_to_owners(gate_sum, 0)
    bottom_grad, first_dense, (first_up,) = backward_layer(
        0, middle_grad, sums, gate_term, first_saved, pickings[0], weights[0], (0, first_experts[1])
    )
    up_sum = low(summed((first_experts[1], second_experts[1]), (first_up, second_up)))
    second_slots = after(second_slots, up_sum, gate_rows, *first_dense)
    sums, (first_down, other_bottom) = token_sums(
        pickings[1][2], second_slots, 8, (0, first_experts[2]), (0, bottom_grad)
    )
    up_rows = rows_to_owners(up_sum, 1)
    second_out = second_updated + sums
    down_sum = low(summed((first_experts[2], second_experts[2]), (first_down, second_down)))
    expert_sums = [gate_rows, up_rows, rows_to_owners(down_sum, 2)]
    expert_sums = [piece.astype(jnp.float32)[None] for piece in expert_sums]
    own_out = own_layer((first_out, second_out))
    layer_outs = both_micros(own_out, own_layer((other_out, pass_to(second_out, 1))))
    own_grad = own_layer((bottom_grad, middle_grad))
    section_grads = both_micros(own_grad, own_layer((other_bottom, other_middle)))
    first_dense = spread(first_dense)
    first_dense_in = [pass_to(piece, 0) for piece in first_dense]
    qkv_sum, out_sum = [
        summed((first_dense[k], second_dense[k]), (first_dense_in[k], second_dense_in[k]))
        for k in range(2)
    ]
    kv_width = KV_HEADS * HEAD_DIM // seq
    q_width = GROUP * kv_width
    qkv_width = q_width + 2 * kv_width
    small_sum = jnp.sum(qkv_sum[:, :, qkv_width:], axis=0)

    def columns(begin, end):
        return jnp.transpose(qkv_sum[:, :, begin:end], (1, 0, 2)).reshape(depth, -1)[None]

    return (
        layer_outs,
        section_grads,
        small_sum[:, EXPERTS][None],
        small_sum[:, EXPERTS + 1][None],
        columns(0, q_width),
        columns(q_width, q_width + kv_width),
        columns(q_width + kv_width, qkv_width),
        out_sum[None],
        small_sum[:, :EXPERTS][None],
        *expert_sums,
    )


def whole_rows(piece, seq_index, share, seq):
    parts = piece.shape[0]
    spread = jnp.zeros((seq,) + piece.shape[1:], piece.dtype)
    spread = lax.dynamic_update_slice_in_dim(
        spread, piece, (seq_index % share) * parts, axis=0
    )
    spread = lax.all_to_all(spread, "seq", split_axis=0, concat_axis=0, tiled=True)
    spread = spread.reshape((-1, share) + piece.shape[1:])
    return jnp.sum(spread.astype(jnp.float32), axis=1).astype(piece.dtype)


def solution(mesh):
    return jax.shard_map(
        body,
        mesh=mesh,
        in_specs=(
            P(None, "dp", "seq", None),
            P(None, "dp", "seq", None),
            P("section", ("dp", "seq")),
            P("section", ("dp", "seq")),
            P("section", ("dp", "seq"), None),
            P("section", ("dp", "seq"), None),
            P("section", ("dp", "seq"), None),
            P("section", ("dp", "seq"), None),
            P("section", ("dp", "seq"), None),
            P("section", "dp", None, None),
            P("section", "dp", None, None),
            P("section", "dp", None, None),
            P("section", None, "dp", "seq", None),
        ),
        out_specs=(
            P("section", None, "dp", "seq", None),
            P("section", None, "dp", "seq", None),
            P("section", ("dp", "seq")),
            P("section", ("dp", "seq")),
            P("section", ("dp", "seq"), None),
            P("section", ("dp", "seq"), None),
            P("section", ("dp", "seq"), None),
            P("section", ("dp", "seq"), None),
            P("section", ("dp", "seq"), None),
            P("section", "dp", "seq", None),
            P("section", "dp", "seq", None),
            P("section", "dp", "seq", None),
        ),
        check_vma=False,
    )
```

```python
import jax
import jax.numpy as jnp
from jax import lax
from jax.experimental import pallas as pl
from jax.experimental.pallas import tpu as pltpu
from jax.sharding import PartitionSpec as P

HEADS = 24
KV_HEADS = 8
HEAD_DIM = 64
TOP_K = 8
EXPERTS = 32
CAP = 80
GROUP = HEADS // KV_HEADS
TOKENS = ("dp", "seq")
MESH = pl.DeviceIdType.MESH
DMA = pltpu.SemaphoreType.DMA

epsilon = 1e-06


def dot(a, b):
    return jnp.dot(a, b, preferred_element_type=jnp.float32)


def dot_t(a, b):
    return lax.dot_general(a, b, (((1,), (1,)), ((), ())), preferred_element_type=jnp.float32)


def t_dot(a, b):
    return lax.dot_general(a, b, (((0,), (0,)), ((), ())), preferred_element_type=jnp.float32)


def low(v):
    return v.astype(jnp.bfloat16)


def swap(block):
    return lax.ppermute(block, "section", [(0, 1), (1, 0)])


def pass_to(block, section):
    return lax.ppermute(block, "section", [(1 - section, section)])


def rms_norm(values, norm_gain):
    return (
        values * lax.rsqrt(jnp.mean(values * values, axis=-1, keepdims=True) + epsilon) * norm_gain
    )


def rotary_tables(length):
    half_dim = HEAD_DIM // 2
    frequency = 10000.0 ** (-jnp.arange(half_dim, dtype=jnp.float32) * 2.0 / HEAD_DIM)
    angles = jnp.arange(length, dtype=jnp.float32)[:, None] * frequency[None, :]
    return (jnp.cos(angles)[:, None, :], jnp.sin(angles)[:, None, :])


def rotate(values, cos_table, sin_table):
    length = values.shape[0]
    split_heads = values.reshape(length, -1, HEAD_DIM)
    first_half = split_heads[..., : HEAD_DIM // 2]
    second_half = split_heads[..., HEAD_DIM // 2 :]
    turned = jnp.concatenate(
        [
            first_half * cos_table - second_half * sin_table,
            second_half * cos_table + first_half * sin_table,
        ],
        axis=-1,
    )
    return turned.reshape(length, -1)


def attention_forward(q_heads, k_heads, v_heads):
    length = q_heads.shape[0]
    local_kv = k_heads.shape[1] // HEAD_DIM
    cos_table, sin_table = rotary_tables(length)
    q_rot = low(rotate(q_heads.astype(jnp.float32), cos_table, sin_table)).reshape(
        length, local_kv, GROUP, HEAD_DIM
    )
    k_rot = low(rotate(k_heads.astype(jnp.float32), cos_table, sin_table)).reshape(
        length, local_kv, HEAD_DIM
    )
    values = v_heads.reshape(length, local_kv, HEAD_DIM)
    block_rows = min(512, length)
    outputs = []
    totals_list = []
    for first_row in range(0, length, block_rows):
        key_end = first_row + block_rows
        scores = (
            jnp.einsum(
                "qhgd,khd->hgqk",
                q_rot[first_row:key_end],
                k_rot[:key_end],
                preferred_element_type=jnp.float32,
            )
            * 0.125
        )
        causal = (first_row + jnp.arange(block_rows, dtype=jnp.int32))[:, None] >= jnp.arange(
            key_end, dtype=jnp.int32
        )[None, :]
        scores = jnp.where(causal, scores, -jnp.inf)
        row_peak = jnp.max(scores, axis=-1, keepdims=True)
        exponents = jnp.exp(scores - row_peak)
        totals = jnp.sum(exponents, axis=-1, keepdims=True)
        attended = jnp.einsum(
            "hgqk,khd->qhgd",
            low(exponents / totals),
            values[:key_end],
            preferred_element_type=jnp.float32,
        )
        outputs.append(low(attended).reshape(block_rows, -1))
        totals_list.append((row_peak + jnp.log(totals))[..., 0])
    return (jnp.concatenate(outputs, axis=0), jnp.stack(totals_list), q_rot, k_rot, values)


def attention_backward(head_grad, q_rot, k_rot, values, log_total):
    length, local_kv = q_rot.shape[:2]
    cos_table, sin_table = rotary_tables(length)
    block_rows = min(512, length)
    grad_rows = head_grad.reshape(length, local_kv, GROUP, HEAD_DIM)
    key_acc = jnp.zeros((length, local_kv, HEAD_DIM), jnp.float32)
    value_acc = jnp.zeros((length, local_kv, HEAD_DIM), jnp.float32)
    query_parts = []
    for block_number, first_row in enumerate(range(0, length, block_rows)):
        key_end = first_row + block_rows
        q_block = q_rot[first_row:key_end]
        grad_block = grad_rows[first_row:key_end]
        key_part = k_rot[:key_end]
        scores = (
            jnp.einsum("qhgd,khd->hgqk", q_block, key_part, preferred_element_type=jnp.float32)
            * 0.125
        )
        causal = (first_row + jnp.arange(block_rows, dtype=jnp.int32))[:, None] >= jnp.arange(
            key_end, dtype=jnp.int32
        )[None, :]
        scores = jnp.where(causal, scores, -jnp.inf)
        probs_full = jnp.exp(scores - log_total[block_number][..., None])
        prob_grad = jnp.einsum(
            "qhgd,khd->hgqk", grad_block, values[:key_end], preferred_element_type=jnp.float32
        )
        score_grad = probs_full * (
            prob_grad - jnp.sum(probs_full * prob_grad, axis=-1, keepdims=True)
        )
        score_low = low(score_grad)
        query_parts.append(
            jnp.einsum("hgqk,khd->qhgd", score_low, key_part, preferred_element_type=jnp.float32)
            * 0.125
        )
        key_acc = key_acc.at[:key_end].add(
            jnp.einsum("hgqk,qhgd->khd", score_low, q_block, preferred_element_type=jnp.float32)
            * 0.125
        )
        value_acc = value_acc.at[:key_end].add(
            jnp.einsum(
                "hgqk,qhgd->khd", low(probs_full), grad_block, preferred_element_type=jnp.float32
            )
        )
    query_all = jnp.concatenate(query_parts, axis=0).reshape(length, -1)
    query_grad = rotate(query_all, cos_table, -sin_table)
    key_grad = rotate(key_acc.reshape(length, -1), cos_table, -sin_table)
    return jnp.concatenate(
        [low(query_grad), low(key_grad), low(value_acc).reshape(length, -1)], axis=1
    )


def remote(src, dst, send_sem, recv_sem, **device):
    return pltpu.make_async_remote_copy(
        src_ref=src,
        dst_ref=dst,
        send_sem=send_sem,
        recv_sem=recv_sem,
        device_id=device,
        device_id_type=MESH,
    )


def greet(d, s, section=None, spread=False):
    barrier = pltpu.get_barrier_semaphore()

    def signal(**device):
        pl.semaphore_signal(barrier, inc=1, device_id=device, device_id_type=MESH)

    signal(seq=s ^ 1)
    signal(seq=s ^ 2)

    @pl.when(d > 0)
    def _():
        signal(dp=d - 1)

    @pl.when(d < 3)
    def _():
        signal(dp=d + 1)

    known = 3
    if section is not None:
        signal(section=1 - section)
        known = 4
    if spread:
        signal(seq=s ^ 3)
        known = known + 1
    inner = (d > 0) & (d < 3)

    @pl.when(inner)
    def _():
        pl.semaphore_wait(barrier, known + 1)

    @pl.when(jnp.logical_not(inner))
    def _():
        pl.semaphore_wait(barrier, known)


class Carried:
    def __init__(self, sections, sources, targets, sems):
        self.section = lax.axis_index("section")
        self.copies = []
        for k, (to, source, target) in enumerate(zip(sections, sources, targets)):
            copy = remote(source, target, sems.at[k, 0], sems.at[k, 1], section=1 - self.section)
            self.copies.append((to, copy))

    def start(self):
        for to, copy in self.copies:
            if to is None:
                copy.start()
            else:

                @pl.when(self.section != to)
                def _():
                    copy.start()

    def finish(self):
        for to, copy in self.copies:
            if to is None:
                copy.wait()
            else:

                @pl.when(self.section != to)
                def _():
                    copy.wait_send()

                @pl.when(self.section == to)
                def _():
                    copy.wait_recv()


class Spread:
    def __init__(self, source, target, sems):
        s = lax.axis_index("seq")
        self.local = pltpu.make_async_copy(source.at[s], target.at[s], sems.at[0, 0])
        self.copies = [
            remote(source.at[s ^ flip], target.at[s], sems.at[flip, 0], sems.at[flip, 1], seq=s ^ flip)
            for flip in (3, 2, 1)
        ]

    def start(self):
        for copy in self.copies:
            copy.start()
        self.local.start()

    def finish(self):
        self.local.wait()
        for copy in self.copies:
            copy.wait()


def cost():
    return pl.CostEstimate(flops=80_000_000_000, bytes_accessed=100_000_000, transcendentals=0)


def gather_scratch(rows, width):
    return [
        pltpu.VMEM((16, rows, width), jnp.bfloat16),
        DMA(()),
        DMA((2, 4)),
        DMA((4,)),
        DMA((4,)),
        DMA((4,)),
        DMA((4, 2)),
        DMA((4, 2)),
    ]


def gather_blocks(x_ref, scratch, compute, carried=None, first=None):
    land, lsem, zs, zr, ys, yr, cs, cr = scratch
    d, s = lax.axis_index("dp"), lax.axis_index("seq")

    def place(z, column):
        return land.at[z * 4 + column]

    def z_copy(src, z, right):
        target = d + 1 if right else d - 1
        return remote(src, place(z, s), zs.at[int(right), z], zr.at[z], dp=target)

    def y_copy(src, z):
        return remote(src, place(z, s), ys.at[z], yr.at[z], seq=s ^ 2)

    def core_copy(src, z, across):
        column = s ^ 2 if across else s
        return remote(src, place(z, column), cs.at[z, across], cr.at[z, across], seq=s ^ 1)

    greet(d, s, None if carried is None else carried.section)
    if first is not None:
        first()
    own = pltpu.make_async_copy(x_ref, place(d, s), lsem)
    own.start()
    if carried is not None and first is None:
        carried.start()

    @pl.when(d < 3)
    def _():
        z_copy(x_ref, d, True).start()

    @pl.when(d > 0)
    def _():
        z_copy(x_ref, d, False).start()

    y_copy(x_ref, d).start()
    core_copy(x_ref, d, 0).start()
    own.wait()

    @pl.loop(0, 4)
    def _(i):
        @pl.when(i < 3)
        def _():
            left, right = d - (i + 1), d + (i + 1)

            @pl.when(left >= 0)
            def _():
                z_copy(place(left, s), left, True).wait_recv()

                @pl.when(d < 3)
                def _():
                    z_copy(place(left, s), left, True).start()

            @pl.when(right <= 3)
            def _():
                z_copy(place(right, s), right, False).wait_recv()

                @pl.when(d > 0)
                def _():
                    z_copy(place(right, s), right, False).start()

            following = d ^ (i + 1)
            y_copy(place(following, s), following).start()
            core_copy(place(following, s), following, 0).start()

        z = d ^ i
        y_copy(place(z, s ^ 2), z).wait_recv()
        core_copy(place(z, s ^ 2), z, 1).start()
        core_copy(place(z, s ^ 1), z, 0).wait_recv()
        core_copy(place(z, s ^ 3), z, 1).wait_recv()
        compute(z)

    for z in range(4):

        @pl.when((z <= d) & (d < 3))
        def _():
            z_copy(place(z, s), z, True).wait_send()

        @pl.when((z >= d) & (d > 0))
        def _():
            z_copy(place(z, s), z, False).wait_send()

        y_copy(place(z, s), z).wait_send()
        core_copy(place(z, s), z, 0).wait_send()
        core_copy(place(z, s), z, 1).wait_send()
    return land


def prepare_kernel(x_ref, pick_out, pick_t_out, chosen_out, small_out, both, places, lsem, carry_sem, *gather):
    d, s, section = lax.axis_index("dp"), lax.axis_index("seq"), lax.axis_index("section")
    known = x_ref.shape[0]
    count = pick_out.shape[2] // CAP
    rows = pick_out.shape[3]
    land = gather[0]
    part = both.at[pl.ds(pl.multiple_of(section * known, known), known)]
    carried = Carried((None,), (x_ref,), (part,), carry_sem)

    def swap_first():
        carried.start()
        own = pltpu.make_async_copy(x_ref, part, lsem)
        own.start()
        own.wait()
        carried.finish()

    gather_blocks(both, gather, lambda z: None, carried, swap_first)
    first_expert = (d * 4 + s) * count
    before = lax.broadcasted_iota(jnp.int32, (rows, rows), 0)
    before = low(before < lax.broadcasted_iota(jnp.int32, (rows, rows), 1))
    slot = lax.broadcasted_iota(jnp.int32, (CAP, rows), 0)
    expert = lax.broadcasted_iota(jnp.int32, (EXPERTS, rows), 0)
    lane = lax.broadcasted_iota(jnp.int32, (rows, count * CAP), 1)

    @pl.loop(0, 2)
    def _(layer):
        @pl.loop(0, 16)
        def _(b):
            paths = land[b, pl.ds(pl.multiple_of(layer * known, 16), 16), :].astype(jnp.float32)
            paths = jnp.where(section == 0, paths[:TOP_K], paths[TOP_K:]).astype(jnp.int32)
            chosen = expert == paths[0:1]
            for k in range(1, TOP_K):
                chosen = chosen | (expert == paths[k : k + 1])
            chosen_out[layer, b] = low(chosen)
            mine = [
                jnp.max((paths == first_expert + j).astype(jnp.float32), axis=0, keepdims=True)
                for j in range(count)
            ]
            mine = jnp.concatenate(mine + [jnp.zeros((8 - count, rows), jnp.float32)], axis=0)
            place = jnp.where(mine > 0.5, dot(low(mine), before), -10000.0)
            places[...] = place
            for j in range(count):
                pick_out[layer, b, j * CAP : (j + 1) * CAP, :] = low(
                    slot == place[j : j + 1].astype(jnp.int32)
                )
            turned = places[...].T.astype(jnp.int32)
            pick_t = turned[:, 0:1] == lane
            for j in range(1, count):
                pick_t = pick_t & (lane < j * CAP) | (turned[:, j : j + 1] == lane - j * CAP)
            pick_t_out[layer, b] = low(pick_t)

        depth = small_out.shape[2] // 16
        for b in range(16):
            small = land[b, pl.ds(pl.multiple_of(layer * known + 16, 16), known - 16), :]
            small_out[layer, :, b * depth : (b + 1) * depth] = small[:, :depth]


def prepare(x, count, rows, depth, collective_id):
    known, width = x.shape
    bf = jnp.bfloat16
    near = pl.BlockSpec(memory_space=pltpu.VMEM)
    return pl.pallas_call(
        prepare_kernel,
        out_shape=[
            jax.ShapeDtypeStruct((2, 16, count * CAP, rows), bf),
            jax.ShapeDtypeStruct((2, 16, rows, count * CAP), bf),
            jax.ShapeDtypeStruct((2, 16, EXPERTS, rows), bf),
            jax.ShapeDtypeStruct((2, known - 16, 16 * depth), bf),
        ],
        in_specs=[pl.BlockSpec(memory_space=pl.ANY)],
        out_specs=[near] * 4,
        scratch_shapes=[
            pltpu.VMEM((2 * known, width), bf),
            pltpu.VMEM((8, rows), jnp.float32),
            DMA(()),
            DMA((1, 2)),
        ]
        + gather_scratch(2 * known, width),
        compiler_params=pltpu.CompilerParams(
            collective_id=collective_id, has_side_effects=True, vmem_limit_bytes=60 << 20
        ),
        name="prepare",
    )(x)


def pick_weights(own_refs, other_refs, held, sems, own_layer):
    mine = lax.axis_index("section") == own_layer

    @pl.when(mine)
    def _():
        for k, ref in enumerate(own_refs):
            pltpu.make_async_copy(ref, held[k], sems.at[k]).start()

    @pl.when(jnp.logical_not(mine))
    def _():
        for k, ref in enumerate(other_refs):
            pltpu.make_async_copy(ref, held[k], sems.at[k]).start()

    def ready(k):
        pltpu.make_async_copy(own_refs[k], held[k], sems.at[k]).wait()

    return ready


def expert_forward_kernel(
    layer, x_ref, pick_ref, chosen_ref, router_ref, mine_ref,
    wg_own, wu_own, wd_own, wg_other, wu_other, wd_other,
    rows_out, gate_out, up_out, hidden_out, slot_gate_out, y_out,
    wg, wu, wd, rows, gate, up, hidden, slot_gate, y, wsem, osem, carry_sem, *gather
):
    count = wg.shape[0]
    carried = None
    if layer == 0:
        carried = Carried((None,), (wd_own,), (wd_other,), carry_sem)
        ready = pick_weights((wg_own, wu_own), (wg_other, wu_other), (wg, wu), wsem, layer)
    else:
        ready = pick_weights(
            (wg_own, wu_own, wd_own), (wg_other, wu_other, wd_other), (wg, wu, wd), wsem, layer
        )
    land = gather[0]
    d = lax.axis_index("dp")

    def outs(z):
        part = pl.ds(z * 4 * CAP, 4 * CAP)
        return [
            pltpu.make_async_copy(held.at[:, part], out.at[:, part], osem.at[k, z])
            for k, (held, out) in enumerate(
                ((rows, rows_out), (gate, gate_out), (up, up_out), (hidden, hidden_out), (slot_gate, slot_gate_out))
            )
        ] + [pltpu.make_async_copy(y.at[pl.ds(z * 4, 4)], y_out.at[pl.ds(z * 4, 4)], osem.at[5, z])]

    def down(z):
        part = pl.ds(z * 4 * CAP, 4 * CAP)

        @pl.loop(0, count)
        def _(j):
            result = low(dot(hidden[j, part, :], wd[j]))
            for q in range(4):
                y[z * 4 + q, pl.ds(j * CAP, CAP), :] = result[q * CAP : (q + 1) * CAP]

    def compute(z):
        @pl.when(z == d)
        def _():
            for k in range(2 if layer == 0 else 3):
                ready(k)

        for q in range(4):
            b = z * 4 + q
            picked = low(dot(pick_ref[b], land[b]))
            for j in range(count):
                rows[j, pl.ds(b * CAP, CAP), :] = picked[j * CAP : (j + 1) * CAP]
        part = pl.ds(z * 4 * CAP, 4 * CAP)

        @pl.loop(0, count)
        def _(j):
            x = rows[j, part, :]
            g = dot(x, wg[j])
            u = dot(x, wu[j])
            logits = dot_t(x, router_ref[...])
            for q in range(4):
                b = z * 4 + q
                slots = slice(q * CAP, (q + 1) * CAP)
                seen = dot_t(pick_ref[b, pl.ds(j * CAP, CAP), :], chosen_ref[b])
                masked = jnp.where(seen > 0.5, logits[slots], -1e30)
                power = jnp.exp(masked - jnp.max(masked, axis=1, keepdims=True))
                own = jnp.sum(power * mine_ref[j], axis=1, keepdims=True)
                value = own / jnp.sum(power, axis=1, keepdims=True)
                slot_gate[j, pl.ds(b * CAP, CAP), :] = jnp.broadcast_to(value, (CAP, 128))
            gate[j, part, :] = low(g)
            up[j, part, :] = low(u)
            h = low(g * jax.nn.sigmoid(g) * u * slot_gate[j, part, :][:, :1])
            hidden[j, part, :] = h

        if layer != 0:
            down(z)
        for copy in outs(z)[: 5 if layer == 0 else 6]:
            copy.start()

    gather_blocks(x_ref, gather, compute, carried)
    if layer == 0:
        carried.finish()
        ready = pick_weights((wd_own,), (wd_other,), (wd,), wsem, layer)
        ready(0)
        for z in range(4):
            down(z)
            outs(z)[5].start()
    for z in range(4):
        for copy in outs(z):
            copy.wait()


def expert_forward(layer, x, pick, chosen, router, mine, own, other, collective_id):
    count, width, units = own[0].shape
    rows = x.shape[0]
    slots = 16 * CAP
    bf = jnp.bfloat16
    anywhere = pl.BlockSpec(memory_space=pl.ANY)
    near = pl.BlockSpec(memory_space=pltpu.VMEM)
    results = [
        ((count, slots, width), bf),
        ((count, slots, units), bf),
        ((count, slots, units), bf),
        ((count, slots, units), bf),
        ((count, slots, 128), jnp.float32),
        ((16, count * CAP, width), bf),
    ]

    def kernel(*refs):
        if layer == 0:
            refs = refs[:10] + refs[16:17] + refs[10:16] + refs[17:]
        expert_forward_kernel(layer, *refs)

    shapes = [jax.ShapeDtypeStruct(*result) for result in results]
    if layer == 0:
        shapes.append(jax.ShapeDtypeStruct(own[2].shape, bf))
        other = other[:2]
    operands = (x, pick, chosen, router, mine, *own, *other)
    return pl.pallas_call(
        kernel,
        out_shape=shapes,
        in_specs=[anywhere, near, near, near, near] + [anywhere] * (len(operands) - 5),
        out_specs=[anywhere] * len(shapes),
        scratch_shapes=[pltpu.VMEM(weight.shape, bf) for weight in own]
        + [pltpu.VMEM(*result) for result in results]
        + [DMA((3,)), DMA((6, 4)), DMA((1, 2))]
        + gather_scratch(rows, width),
        compiler_params=pltpu.CompilerParams(
            collective_id=collective_id, has_side_effects=True, vmem_limit_bytes=60 << 20
        ),
        cost_estimate=cost(),
        name="expert_forward",
    )(*operands)


def combine_kernel(sections, spreads, pick_ref, y_ref, *refs):
    kept = len(sections)
    sources, refs = refs[:kept], refs[kept:]
    spread_sources, refs = refs[:spreads], refs[spreads:]
    out_ref, *refs = refs
    targets, refs = refs[:kept], refs[kept:]
    spread_targets, refs = refs[:spreads], refs[spreads:]
    y, sent, own, core_in, y_in, z_in, lsem, zs, zr, ys, yr, cs, cr, carry_sem, spread_sem = refs
    carried = Carried(sections, sources, targets, carry_sem)
    spread = [Spread(a, b, spread_sem) for a, b in zip(spread_sources, spread_targets)]
    d, s = lax.axis_index("dp"), lax.axis_index("seq")
    half = out_ref.shape[0] // 2

    def loaded(b):
        return pltpu.make_async_copy(y_ref.at[b], y.at[b], lsem.at[b])

    def column(across, other_core):
        return s ^ (2 * across) ^ other_core

    for i in range(4):
        z = d ^ (3 - i)
        for across in (1, 0):
            for other_core in (1, 0):
                loaded(z * 4 + column(across, other_core)).start()
    greet(d, s, carried.section, spreads > 0)
    carried.start()

    def rows(k):
        return pl.ds(pl.multiple_of(k * half, half), half)

    def partial_sum(z, k, across, other_core):
        b = z * 4 + column(across, other_core)

        @pl.when(k == 0)
        def _():
            loaded(b).wait()

        return dot(pick_ref[b, rows(k), :], y[b])

    def core_copy(z, k, across):
        return remote(
            sent.at[z, across, rows(k)],
            core_in.at[z, across, rows(k)],
            cs.at[z, k, across],
            cr.at[z, k, across],
            seq=s ^ 1,
        )

    def y_copy(z, k):
        return remote(own.at[z, 1, rows(k)], y_in.at[z, rows(k)], ys.at[z, k], yr.at[z, k], seq=s ^ 2)

    def z_copy(z, k, right):
        target = d + 1 if right else d - 1
        return remote(
            own.at[z, 0, rows(k)],
            z_in.at[int(right), z, rows(k)],
            zs.at[z, k],
            zr.at[int(right), z, k],
            dp=target,
        )

    def start(i):
        z, k = d ^ (3 - i // 2), i % 2
        sent[z, 1, rows(k), :] = low(partial_sum(z, k, 1, 1))
        core_copy(z, k, 1).start()
        total = partial_sum(z, k, 1, 0)
        core_copy(z, k, 1).wait_recv()
        own[z, 1, rows(k), :] = low(total + core_in[z, 1, rows(k), :].astype(jnp.float32))
        y_copy(z, k).start()
        sent[z, 0, rows(k), :] = low(partial_sum(z, k, 0, 1))
        core_copy(z, k, 0).start()

    start(0)
    for side in spread:
        side.start()

    @pl.loop(0, 8)
    def _(i):
        @pl.when(i < 7)
        def _():
            start(i + 1)

        z, k = d ^ (3 - i // 2), i % 2
        total = partial_sum(z, k, 0, 0)
        core_copy(z, k, 0).wait_recv()
        total = total + core_in[z, 0, rows(k), :].astype(jnp.float32)
        y_copy(z, k).wait_recv()
        total = total + y_in[z, rows(k), :].astype(jnp.float32)

        @pl.when(z < d)
        def _():
            @pl.when(d < 3)
            def _():
                z_copy(z, k, False).wait_recv()
                own[z, 0, rows(k), :] = low(total + z_in[0, z, rows(k), :].astype(jnp.float32))

            @pl.when(d == 3)
            def _():
                own[z, 0, rows(k), :] = low(total)

            z_copy(z, k, False).start()

        @pl.when(z > d)
        def _():
            @pl.when(d > 0)
            def _():
                z_copy(z, k, True).wait_recv()
                own[z, 0, rows(k), :] = low(total + z_in[1, z, rows(k), :].astype(jnp.float32))

            @pl.when(d == 0)
            def _():
                own[z, 0, rows(k), :] = low(total)

            z_copy(z, k, True).start()

        @pl.when(z == d)
        def _():
            out_ref[rows(k), :] = total

    for k in range(2):

        @pl.when(d < 3)
        def _():
            z_copy(d, k, False).wait_recv()
            out_ref[rows(k), :] += z_in[0, d, rows(k), :].astype(jnp.float32)

        @pl.when(d > 0)
        def _():
            z_copy(d, k, True).wait_recv()
            out_ref[rows(k), :] += z_in[1, d, rows(k), :].astype(jnp.float32)

    for z in range(4):
        for k in range(2):
            core_copy(z, k, 0).wait_send()
            core_copy(z, k, 1).wait_send()
            y_copy(z, k).wait_send()

            @pl.when(z < d)
            def _():
                z_copy(z, k, False).wait_send()

            @pl.when(z > d)
            def _():
                z_copy(z, k, True).wait_send()

    carried.finish()
    for side in spread:
        side.finish()


def combine(pick_t, y, collective_id, carry, spread=()):
    rows, width = pick_t.shape[1], y.shape[2]
    anywhere = pl.BlockSpec(memory_space=pl.ANY)
    near = pl.BlockSpec(memory_space=pltpu.VMEM)
    sections = tuple(to for to, _ in carry)
    arrays = [array for _, array in carry]

    arrays = arrays + list(spread)

    def kernel(*refs):
        combine_kernel(sections, len(spread), *refs)

    def blocks(*lead):
        return pltpu.VMEM(lead + (rows, width), jnp.bfloat16)

    return pl.pallas_call(
        kernel,
        out_shape=[jax.ShapeDtypeStruct((rows, width), jnp.float32)]
        + [jax.ShapeDtypeStruct(array.shape, array.dtype) for array in arrays],
        in_specs=[near, anywhere] + [anywhere] * len(arrays),
        out_specs=[near] + [anywhere] * len(arrays),
        scratch_shapes=[
            pltpu.VMEM(y.shape, jnp.bfloat16),
            blocks(4, 2),
            blocks(4, 2),
            blocks(4, 2),
            blocks(4),
            blocks(2, 4),
            DMA((16,)),
            DMA((4, 2)),
            DMA((2, 4, 2)),
            DMA((4, 2)),
            DMA((4, 2)),
            DMA((4, 2, 2)),
            DMA((4, 2, 2)),
            DMA((max(1, len(arrays)), 2)),
            DMA((4, 2)),
        ],
        compiler_params=pltpu.CompilerParams(
            collective_id=collective_id, has_side_effects=True, vmem_limit_bytes=60 << 20
        ),
        cost_estimate=cost(),
        name="combine",
    )(pick_t, y, *arrays)


def expert_backward_kernel(
    layer, sections, x_ref, pick_ref, gate_in, up_in, slot_gate_in,
    wg_own, wu_own, wd_own, wg_other, wu_other, wd_other, *refs
):
    kept = len(sections)
    sources, refs = refs[:kept], refs[kept:]
    rows_out, gate_out, up_out, term_out, y_out, *refs = refs
    targets, refs = refs[:kept], refs[kept:]
    wg, wu, wd, rows, gate, up, slot_gate, y, wsem, isem, osem, carry_sem, *gather = refs
    carried = Carried(sections, sources, targets, carry_sem)
    count = wg.shape[0]
    ready = pick_weights(
        (wg_own, wu_own, wd_own), (wg_other, wu_other, wd_other), (wg, wu, wd), wsem, layer
    )
    land = gather[0]
    d = lax.axis_index("dp")
    ins = [
        pltpu.make_async_copy(src, held, isem.at[k])
        for k, (src, held) in enumerate(((gate_in, gate), (up_in, up), (slot_gate_in, slot_gate)))
    ]
    for copy in ins:
        copy.start()

    def outs(z):
        part = pl.ds(z * 4 * CAP, 4 * CAP)
        return [
            pltpu.make_async_copy(held.at[:, part], out.at[:, part], osem.at[k, z])
            for k, (held, out) in enumerate(
                ((rows, rows_out), (gate, gate_out), (up, up_out), (slot_gate, term_out))
            )
        ] + [pltpu.make_async_copy(y.at[pl.ds(z * 4, 4)], y_out.at[pl.ds(z * 4, 4)], osem.at[4, z])]

    def compute(z):
        @pl.when(z == d)
        def _():
            for k in range(3):
                ready(k)
            for copy in ins:
                copy.wait()

        for q in range(4):
            b = z * 4 + q
            picked = low(dot(pick_ref[b], land[b]))
            for j in range(count):
                rows[j, pl.ds(b * CAP, CAP), :] = picked[j * CAP : (j + 1) * CAP]
        part = pl.ds(z * 4 * CAP, 4 * CAP)

        @pl.loop(0, count)
        def _(j):
            plain = dot_t(rows[j, part, :], wd[j])
            g = gate[j, part, :].astype(jnp.float32)
            u = up[j, part, :].astype(jnp.float32)
            sigmoid = jax.nn.sigmoid(g)
            active = g * sigmoid
            term = jnp.sum(plain * (active * u), axis=1, keepdims=True)
            grad = plain * slot_gate[j, part, :][:, :1]
            dg = low(grad * u * sigmoid * (1.0 + g * (1.0 - sigmoid)))
            du = low(grad * active)
            slot_gate[j, part, :] = jnp.broadcast_to(term, (4 * CAP, 128))
            gate[j, part, :] = dg
            up[j, part, :] = du
            result = low(dot_t(dg, wg[j]) + dot_t(du, wu[j]))
            for q in range(4):
                y[z * 4 + q, pl.ds(j * CAP, CAP), :] = result[q * CAP : (q + 1) * CAP]

        for copy in outs(z):
            copy.start()

    gather_blocks(x_ref, gather, compute, carried)
    carried.finish()
    for z in range(4):
        for copy in outs(z):
            copy.wait()


def expert_backward(layer, x, pick, gate, up, slot_gate, own, other, collective_id, carry):
    count, width, units = own[0].shape
    rows = x.shape[0]
    slots = 16 * CAP
    bf = jnp.bfloat16
    anywhere = pl.BlockSpec(memory_space=pl.ANY)
    near = pl.BlockSpec(memory_space=pltpu.VMEM)
    results = [
        ((count, slots, width), bf),
        ((count, slots, units), bf),
        ((count, slots, units), bf),
        ((count, slots, 128), jnp.float32),
        ((16, count * CAP, width), bf),
    ]
    sections = tuple(to for to, _ in carry)
    arrays = [array for _, array in carry]

    def kernel(*refs):
        expert_backward_kernel(layer, sections, *refs)

    return pl.pallas_call(
        kernel,
        out_shape=[jax.ShapeDtypeStruct(*result) for result in results]
        + [jax.ShapeDtypeStruct(array.shape, array.dtype) for array in arrays],
        in_specs=[anywhere, near] + [anywhere] * (9 + len(arrays)),
        out_specs=[anywhere] * (5 + len(arrays)),
        scratch_shapes=[pltpu.VMEM(weight.shape, bf) for weight in own]
        + [pltpu.VMEM(*result) for result in results]
        + [DMA((3,)), DMA((3,)), DMA((5, 4)), DMA((max(1, len(arrays)), 2))]
        + gather_scratch(rows, width),
        compiler_params=pltpu.CompilerParams(
            collective_id=collective_id, has_side_effects=True, vmem_limit_bytes=60 << 20
        ),
        cost_estimate=cost(),
        name="expert_backward",
    )(x, pick, gate, up, slot_gate, *own, *other, *arrays)


def rope(x, cos_table, sin_table):
    lane = lax.broadcasted_iota(jnp.int32, x.shape, 1)
    turned = jnp.where(lane % HEAD_DIM < HEAD_DIM // 2, pltpu.roll(x, 128 - HEAD_DIM // 2, 1), pltpu.roll(x, HEAD_DIM // 2, 1))
    return x * cos_table + turned * sin_table


def seq_greet(s, section, spread=False):
    barrier = pltpu.get_barrier_semaphore()
    devices = [dict(seq=s ^ 1), dict(seq=s ^ 2), dict(section=1 - section)]
    if spread:
        devices.append(dict(seq=s ^ 3))
    for device in devices:
        pl.semaphore_signal(barrier, inc=1, device_id=device, device_id_type=MESH)
    pl.semaphore_wait(barrier, len(devices))


def seq_scratch(rows, width):
    return [
        pltpu.VMEM((4, rows, width), jnp.bfloat16),
        pltpu.VMEM((2, rows, width), jnp.bfloat16),
        pltpu.VMEM((2, rows, width), jnp.bfloat16),
        pltpu.VMEM((rows, width), jnp.bfloat16),
        pltpu.VMEM((rows, width), jnp.bfloat16),
        DMA(()),
        DMA((4, 2)),
        DMA((3, 2)),
    ]


class Line:
    def __init__(self, scratch):
        self.land, self.sent, self.core_in, self.y_sent, self.y_in, self.lsem, self.ag, self.rs = scratch
        self.s = lax.axis_index("seq")

    def hop(self, src, dst, sems, k, flip):
        return remote(src, dst, sems.at[k, 0], sems.at[k, 1], seq=self.s ^ flip)

    def gather(self, x_ref, use):
        s, land = self.s, self.land
        own = pltpu.make_async_copy(x_ref, land.at[s], self.lsem)
        own.start()
        over = self.hop(x_ref, land.at[s], self.ag, 0, 2)
        beside = self.hop(x_ref, land.at[s], self.ag, 1, 1)
        over.start()
        beside.start()
        own.wait()
        use(s)
        beside.wait_recv()
        use(s ^ 1)
        over.wait_recv()
        further = self.hop(land.at[s ^ 2], land.at[s ^ 2], self.ag, 2, 1)
        further.start()
        use(s ^ 2)
        further.wait_recv()
        use(s ^ 3)
        over.wait_send()
        beside.wait_send()
        further.wait_send()

    def hand_over(self, t, partial, out_ref):
        relation = t ^ self.s

        @pl.when(relation == 3)
        def _():
            self.sent[0] = low(partial[...])
            self.hop(self.sent.at[0], self.core_in.at[0], self.rs, 0, 1).start()

        @pl.when(relation == 2)
        def _():
            self.hop(self.sent.at[0], self.core_in.at[0], self.rs, 0, 1).wait_recv()
            self.y_sent[...] = low(partial[...] + self.core_in[0].astype(jnp.float32))
            self.hop(self.y_sent, self.y_in, self.rs, 1, 2).start()

        @pl.when(relation == 1)
        def _():
            self.sent[1] = low(partial[...])
            self.hop(self.sent.at[1], self.core_in.at[1], self.rs, 2, 1).start()

        @pl.when(relation == 0)
        def _():
            out_ref[...] = partial[...]

    def finish(self, out_ref):
        self.hop(self.sent.at[1], self.core_in.at[1], self.rs, 2, 1).wait()
        out_ref[...] += self.core_in[1].astype(jnp.float32)
        self.hop(self.y_sent, self.y_in, self.rs, 1, 2).wait()
        out_ref[...] += self.y_in[...].astype(jnp.float32)
        self.hop(self.sent.at[0], self.core_in.at[0], self.rs, 0, 1).wait_send()


def attention_forward_kernel(sections, x_ref, qkv_ref, wo_ref, cos_ref, sin_ref, *refs):
    kept = len(sections)
    sources, refs = refs[:kept], refs[kept:]
    out_ref, all_out, heads_out, lse_out, ot_out, *refs = refs
    targets, refs = refs[:kept], refs[kept:]
    wqkv, wo, heads, lse, ot, partial, wsem, osem, carry_sem, *line = refs
    line = Line(line)
    carried = Carried(sections, sources, targets, carry_sem)
    s = line.s
    rows = out_ref.shape[0]
    kv = heads.shape[0] // (GROUP + 2)
    queries = GROUP * kv
    loads = [pltpu.make_async_copy(qkv_ref, wqkv, wsem.at[0]), pltpu.make_async_copy(wo_ref, wo, wsem.at[1])]
    for load in loads:
        load.start()
    seq_greet(s, carried.section)
    carried.start()
    lse[...] = jnp.zeros_like(lse)

    def project(t):
        part = pl.ds(pl.multiple_of(t * rows, rows), rows)

        @pl.when(t == s)
        def _():
            loads[0].wait()

        qkv = low(dot(line.land[t], wqkv[...]))
        for chunk in range((queries + kv) // 2):
            x = qkv[:, chunk * 128 : (chunk + 1) * 128].astype(jnp.float32)
            x = low(rope(x, cos_ref[part, :], sin_ref[part, :]))
            heads[2 * chunk, part, :] = x[:, :HEAD_DIM]
            heads[2 * chunk + 1, part, :] = x[:, HEAD_DIM:]
        for j in range(kv):
            begin = (queries + kv + j) * HEAD_DIM
            heads[queries + kv + j, part, :] = qkv[:, begin : begin + HEAD_DIM]

    line.gather(x_ref, project)
    saves = [pltpu.make_async_copy(line.land, all_out, osem.at[0]), pltpu.make_async_copy(heads, heads_out, osem.at[1])]
    for save in saves:
        save.start()
    loads[1].wait()

    def attend(block):
        keys = (block + 1) * rows
        columns = slice(block * rows, (block + 1) * rows)

        @pl.loop(0, queries)
        def _(h):
            j = h // GROUP
            scores = dot_t(heads[queries + j, :keys, :], heads[h, columns, :]) * 0.125
            key_at = lax.broadcasted_iota(jnp.int32, scores.shape, 0)
            query_at = lax.broadcasted_iota(jnp.int32, scores.shape, 1) + block * rows
            scores = jnp.where(key_at <= query_at, scores, -jnp.inf)
            peak = jnp.max(scores, axis=0, keepdims=True)
            power = jnp.exp(scores - peak)
            total = jnp.sum(power, axis=0, keepdims=True)
            attended = t_dot(heads[queries + kv + j, :keys, :], low(power / total))
            ot[pl.ds(pl.multiple_of(h * HEAD_DIM, HEAD_DIM), HEAD_DIM), columns] = low(attended)
            lse[pl.ds(h, 1), columns] = peak + jnp.log(total)

        partial[...] = t_dot(ot[:, columns], wo[...])

    @pl.loop(0, 4)
    def _(i):
        t = s ^ (3 - i)
        for block in range(4):

            @pl.when(t == block)
            def _():
                attend(block)

        line.hand_over(t, partial, out_ref)

    saves += [pltpu.make_async_copy(lse, lse_out, osem.at[2]), pltpu.make_async_copy(ot, ot_out, osem.at[3])]
    for save in saves[2:]:
        save.start()
    line.finish(out_ref)
    carried.finish()
    for save in saves:
        save.wait()


def attention_forward_call(x, qkv_w, out_w, tables, collective_id, carry):
    rows, width = x.shape
    local_heads = qkv_w.shape[1] // HEAD_DIM
    bf, f32 = jnp.bfloat16, jnp.float32
    anywhere = pl.BlockSpec(memory_space=pl.ANY)
    near = pl.BlockSpec(memory_space=pltpu.VMEM)
    sections = tuple(to for to, _ in carry)
    arrays = [array for _, array in carry]
    results = [
        ((rows, width), f32),
        ((4, rows, width), bf),
        ((local_heads, 4 * rows, HEAD_DIM), bf),
        ((8, 4 * rows), f32),
        ((out_w.shape[0], 4 * rows), bf),
    ]

    def kernel(*refs):
        attention_forward_kernel(sections, *refs)

    return pl.pallas_call(
        kernel,
        out_shape=[jax.ShapeDtypeStruct(*result) for result in results]
        + [jax.ShapeDtypeStruct(array.shape, array.dtype) for array in arrays],
        in_specs=[anywhere] * 3 + [near] * 2 + [anywhere] * len(arrays),
        out_specs=[near] + [anywhere] * (4 + len(arrays)),
        scratch_shapes=[
            pltpu.VMEM(qkv_w.shape, bf),
            pltpu.VMEM(out_w.shape, bf),
            pltpu.VMEM(*results[2]),
            pltpu.VMEM(*results[3]),
            pltpu.VMEM(*results[4]),
            pltpu.VMEM((rows, width), f32),
            DMA((2,)),
            DMA((4,)),
            DMA((max(1, len(arrays)), 2)),
        ]
        + seq_scratch(rows, width),
        compiler_params=pltpu.CompilerParams(
            collective_id=collective_id, has_side_effects=True, vmem_limit_bytes=60 << 20
        ),
        cost_estimate=cost(),
        name="attention_forward",
    )(x, qkv_w, out_w, *tables, *arrays)


def attention_backward_kernel(
    sections, spreads, x_ref, qkv_ref, wo_ref, cos_ref, sin_ref, heads_in, lse_ref, *refs
):
    kept = len(sections)
    sources, refs = refs[:kept], refs[kept:]
    spread_sources, refs = refs[:spreads], refs[spreads:]
    out_ref, all_out, grads_out, *refs = refs
    targets, refs = refs[:kept], refs[kept:]
    spread_targets, refs = refs[:spreads], refs[spreads:]
    wqkv, wo, heads, douts, dk, dv, dqt, grads, partial, wsem, osem, carry_sem, spread_sem, *line = refs
    spread = [Spread(a, b, spread_sem) for a, b in zip(spread_sources, spread_targets)]
    line = Line(line)
    carried = Carried(sections, sources, targets, carry_sem)
    s = line.s
    rows = out_ref.shape[0]
    kv = heads.shape[0] // (GROUP + 2)
    queries = GROUP * kv
    loads = [
        pltpu.make_async_copy(wo_ref, wo, wsem.at[0]),
        pltpu.make_async_copy(qkv_ref, wqkv, wsem.at[1]),
        pltpu.make_async_copy(heads_in, heads, wsem.at[2]),
    ]
    for load in loads:
        load.start()
    seq_greet(s, carried.section, spreads > 0)
    carried.start()
    dk[...] = jnp.zeros_like(dk)
    dv[...] = jnp.zeros_like(dv)

    def project(t):
        part = pl.ds(pl.multiple_of(t * rows, rows), rows)

        @pl.when(t == s)
        def _():
            loads[0].wait()

        grad = low(dot_t(line.land[t], wo[...]))
        for h in range(queries):
            douts[h, part, :] = grad[:, h * HEAD_DIM : (h + 1) * HEAD_DIM]

    line.gather(x_ref, project)
    saves = [pltpu.make_async_copy(line.land, all_out, osem.at[0])]
    saves[0].start()
    for side in spread:
        side.start()
    loads[1].wait()
    loads[2].wait()

    for block in (3, 2, 1, 0):
        keys = (block + 1) * rows
        part = slice(block * rows, (block + 1) * rows)

        @pl.loop(0, queries)
        def _(h):
            j = h // GROUP
            key = heads[queries + j, :keys, :]
            query = heads[h, part, :]
            grad = douts[h, part, :]
            scores = dot_t(key, query) * 0.125
            key_at = lax.broadcasted_iota(jnp.int32, scores.shape, 0)
            query_at = lax.broadcasted_iota(jnp.int32, scores.shape, 1) + block * rows
            scores = jnp.where(key_at <= query_at, scores, -jnp.inf)
            probs = jnp.exp(scores - lse_ref[pl.ds(h, 1), part])
            dprobs = dot_t(heads[queries + kv + j, :keys, :], grad)
            mean = jnp.sum(probs * dprobs, axis=0, keepdims=True)
            dscores = low(probs * (dprobs - mean))
            dk[j, :keys, :] += dot(dscores, query) * 0.125
            dv[j, :keys, :] += dot(low(probs), grad)
            dqt[pl.ds(pl.multiple_of(h * HEAD_DIM, HEAD_DIM), HEAD_DIM), :] = t_dot(key, dscores) * 0.125

        cos_part, sin_part = cos_ref[part, :], -sin_ref[part, :]
        dq = dqt[...].T
        for chunk in range(queries // 2):
            lanes = slice(chunk * 128, (chunk + 1) * 128)
            grads[part, lanes] = low(rope(dq[:, lanes], cos_part, sin_part))
        for pair in range(kv // 2):
            both = jnp.concatenate([dk[2 * pair, part, :], dk[2 * pair + 1, part, :]], axis=1)
            begin = queries * HEAD_DIM + pair * 128
            grads[part, begin : begin + 128] = low(rope(both, cos_part, sin_part))
            both = jnp.concatenate([dv[2 * pair, part, :], dv[2 * pair + 1, part, :]], axis=1)
            begin = (queries + kv) * HEAD_DIM + pair * 128
            grads[part, begin : begin + 128] = low(both)
        partial[...] = dot_t(grads[part, :], wqkv[...])
        line.hand_over(block, partial, out_ref)

    saves.append(pltpu.make_async_copy(grads, grads_out, osem.at[1]))
    saves[1].start()
    line.finish(out_ref)
    carried.finish()
    for side in spread:
        side.finish()
    for save in saves:
        save.wait()


def attention_backward_call(x, qkv_w, out_w, tables, heads, lse, collective_id, carry, spread=()):
    rows, width = x.shape
    bf, f32 = jnp.bfloat16, jnp.float32
    anywhere = pl.BlockSpec(memory_space=pl.ANY)
    near = pl.BlockSpec(memory_space=pltpu.VMEM)
    sections = tuple(to for to, _ in carry)
    arrays = [array for _, array in carry]
    results = [((rows, width), f32), ((4, rows, width), bf), ((4 * rows, qkv_w.shape[1]), bf)]
    kv = heads.shape[0] // (GROUP + 2)
    queries = GROUP * kv

    arrays = arrays + list(spread)

    def kernel(*refs):
        attention_backward_kernel(sections, len(spread), *refs)

    return pl.pallas_call(
        kernel,
        out_shape=[jax.ShapeDtypeStruct(*result) for result in results]
        + [jax.ShapeDtypeStruct(array.shape, array.dtype) for array in arrays],
        in_specs=[anywhere] * 3 + [near] * 2 + [anywhere, near] + [anywhere] * len(arrays),
        out_specs=[near] + [anywhere] * (2 + len(arrays)),
        scratch_shapes=[
            pltpu.VMEM(qkv_w.shape, bf),
            pltpu.VMEM(out_w.shape, bf),
            pltpu.VMEM(heads.shape, bf),
            pltpu.VMEM((queries, 4 * rows, HEAD_DIM), bf),
            pltpu.VMEM((kv, 4 * rows, HEAD_DIM), f32),
            pltpu.VMEM((kv, 4 * rows, HEAD_DIM), f32),
            pltpu.VMEM((queries * HEAD_DIM, rows), f32),
            pltpu.VMEM(*results[2]),
            pltpu.VMEM((rows, width), f32),
            DMA((3,)),
            DMA((2,)),
            DMA((max(1, len(arrays)), 2)),
            DMA((4, 2)),
        ]
        + seq_scratch(rows, width),
        compiler_params=pltpu.CompilerParams(
            collective_id=collective_id, has_side_effects=True, vmem_limit_bytes=60 << 20
        ),
        cost_estimate=cost(),
        name="attention_backward",
    )(x, qkv_w, out_w, *tables, heads, lse, *arrays)


def last_kernel(sections, down_ref, cols_ref, cols_other, out_ref, out_other, *refs):
    kept = len(sections)
    sources, refs = refs[:kept], refs[kept:]
    down_out, cols_out, rows_out, *refs = refs
    targets, refs = refs[:kept], refs[kept:]
    cols_in, cols, out_in, out_sum, down_sem, cols_sem, row_sem, swap_sem, carry_sem = refs
    d, s, section = lax.axis_index("dp"), lax.axis_index("seq"), lax.axis_index("section")
    barrier = pltpu.get_barrier_semaphore()

    def signal(**device):
        pl.semaphore_signal(barrier, inc=1, device_id=device, device_id_type=MESH)

    for flip in (1, 2, 3):
        signal(seq=s ^ flip)
    signal(section=1 - section)

    @pl.when(d != s)
    def _():
        signal(dp=s, seq=d)
        pl.semaphore_wait(barrier, 5)

    @pl.when(d == s)
    def _():
        pl.semaphore_wait(barrier, 4)

    swaps = Carried((None, None), (cols_other, out_other), (cols_in, out_in), swap_sem)
    carried = Carried(sections, sources, targets, carry_sem)
    down = Spread(down_ref, down_out, down_sem)
    swaps.start()
    down.start()
    swaps.finish()
    carried.start()
    cols[...] = low(cols_ref[...].astype(jnp.float32) + cols_in[...].astype(jnp.float32))
    out_sum[...] = low(out_ref[...].astype(jnp.float32) + out_in[...].astype(jnp.float32))
    spread = Spread(cols, cols_out, cols_sem)
    spread.start()
    rows = remote(out_sum, rows_out, row_sem.at[0], row_sem.at[1], dp=s, seq=d)

    @pl.when(d != s)
    def _():
        rows.start()
        rows.wait()

    @pl.when(d == s)
    def _():
        rows_out[...] = out_sum[...]

    spread.finish()
    down.finish()
    carried.finish()


def last_exchange(down, cols, cols_other, out, out_other, collective_id, carry):
    bf = jnp.bfloat16
    anywhere = pl.BlockSpec(memory_space=pl.ANY)
    near = pl.BlockSpec(memory_space=pltpu.VMEM)
    sections = tuple(to for to, _ in carry)
    arrays = [array for _, array in carry]

    def kernel(*refs):
        last_kernel(sections, *refs)

    return pl.pallas_call(
        kernel,
        out_shape=[
            jax.ShapeDtypeStruct(array.shape, array.dtype) for array in (down, cols, out, *arrays)
        ],
        in_specs=[anywhere, near, anywhere, near, anywhere] + [anywhere] * len(arrays),
        out_specs=[anywhere, near, near] + [anywhere] * len(arrays),
        scratch_shapes=[
            pltpu.VMEM(cols.shape, bf),
            pltpu.VMEM(cols.shape, bf),
            pltpu.VMEM(out.shape, bf),
            pltpu.VMEM(out.shape, bf),
            DMA((4, 2)),
            DMA((4, 2)),
            DMA((2,)),
            DMA((2, 2)),
            DMA((max(1, len(arrays)), 2)),
        ],
        compiler_params=pltpu.CompilerParams(
            collective_id=collective_id, has_side_effects=True, vmem_limit_bytes=60 << 20
        ),
        name="last_exchange",
    )(down, cols, cols_other, out, out_other, *arrays)


def wide_tables(length):
    cos_table, sin_table = rotary_tables(length)
    cos_table, sin_table = cos_table[:, 0], sin_table[:, 0]
    return (
        jnp.concatenate([cos_table] * 4, axis=1),
        jnp.concatenate([-sin_table, sin_table] * 2, axis=1),
    )


def token_choice(route):
    return route[..., None] == jnp.arange(EXPERTS, dtype=jnp.int32)


def routing(route_all, first_expert, count):
    chosen = jnp.any(token_choice(route_all), axis=2)
    blocks, rows = chosen.shape[:2]
    mine = lax.dynamic_slice_in_dim(chosen, first_expert, count, axis=2)
    chosen = low(jnp.transpose(chosen, (0, 2, 1)))
    earlier = jnp.tril(jnp.ones((rows, rows), jnp.bfloat16), -1)
    place = jnp.einsum(
        "ts,bsj->bjt", earlier, mine.astype(jnp.bfloat16), preferred_element_type=jnp.float32
    ).astype(jnp.int32)
    mine = jnp.transpose(mine, (0, 2, 1))
    place = jnp.where(mine, place, -1)
    slots = jnp.arange(CAP, dtype=jnp.int32)
    pick = low(place[:, :, None, :] == slots[None, None, :, None]).reshape(blocks, -1, rows)
    return chosen, pick, jnp.transpose(pick, (0, 2, 1))


def choose(pick, rows, count):
    picked = jnp.einsum("bct,btd->bcd", pick, rows, preferred_element_type=jnp.float32)
    blocks = pick.shape[0]
    picked = low(picked).reshape(blocks, count, CAP, -1)
    return jnp.transpose(picked, (1, 0, 2, 3)).reshape(count, blocks * CAP, -1)


def give_back(pick_t, slot_rows):
    blocks, rows = pick_t.shape[:2]
    count, _, width = slot_rows.shape
    slot_rows = jnp.transpose(slot_rows.reshape(count, blocks, CAP, width), (1, 0, 2, 3))
    slot_rows = slot_rows.reshape(blocks, count * CAP, width)
    total = jnp.einsum("btc,bcd->btd", pick_t, slot_rows, preferred_element_type=jnp.float32)
    return low(total).reshape(-1, width)


def each_dot(form, a, b):
    return jnp.einsum(form, a, b, preferred_element_type=jnp.float32)


def after(value, *others):
    return lax.optimization_barrier((value, *others))[0]


def has_kernels():
    return lax.axis_size("dp") == 4 and lax.axis_size("seq") == 4


def forward_layer(number, layer_in, picking, weights, experts, *carry):
    attn_scale, ffn_scale, qkv_w, out_w, router_w = weights
    chosen, pick, pick_t, first_expert = picking
    own, other = experts
    count = own[0].shape[0]
    blocks, _, rows = chosen.shape
    received = []
    normed_input = low(rms_norm(layer_in, attn_scale))
    if has_kernels():
        branch, normed_all, heads, log_total, mixed_t, *received = attention_forward_call(
            normed_input, qkv_w, out_w, wide_tables(4 * layer_in.shape[0]), 9 + number, carry
        )
        attention_state = (normed_all.reshape(-1, layer_in.shape[1]), mixed_t, heads, log_total)
    else:
        received = [swap(array) if to is None else pass_to(array, to) for to, array in carry]
        normed_all = lax.all_gather(normed_input, "seq", axis=0, tiled=True)
        qkv = low(dot(normed_all, qkv_w))
        kv_width = KV_HEADS * HEAD_DIM // lax.axis_size("seq")
        q_width = GROUP * kv_width
        mixed, log_total, q_rot, k_rot, v_heads = attention_forward(
            qkv[:, :q_width], qkv[:, q_width : q_width + kv_width], qkv[:, q_width + kv_width :]
        )
        branch = lax.psum_scatter(low(dot(mixed, out_w)), "seq", scatter_dimension=0, tiled=True)
        attention_state = (normed_all, mixed.T, (q_rot, k_rot, v_heads), log_total)
    after_update = layer_in + branch.astype(jnp.float32)
    normed_ffn = low(rms_norm(after_update, ffn_scale))
    own_block = lax.axis_index("dp") * lax.axis_size("seq") + lax.axis_index("seq")
    own_chosen = lax.dynamic_index_in_dim(chosen, own_block, 0, keepdims=False)
    own_logits = jnp.where(own_chosen > 0, dot_t(router_w, normed_ffn), -jnp.inf)
    own_gates = jax.nn.softmax(own_logits, axis=0)
    if number == 0:
        other = other + (received[0],)
    mine = (
        jnp.arange(EXPERTS)[None, None, :] == first_expert + jnp.arange(count)[:, None, None]
    ).astype(jnp.float32)
    if has_kernels():
        *expert_state, slot_out = expert_forward(
            number, normed_ffn, pick, chosen, router_w, mine, own, other, 1 + number
        )
        if number == 0:
            *expert_state, slot_out, other_down = (*expert_state, slot_out)
            other = other[:2] + (other_down,)
    else:
        if number == 0:
            other = other[:2] + (swap(own[2]),)
        gate_w, up_w, down_w = by_layer(number, own, other)
        ffn_all = lax.all_gather(normed_ffn, TOKENS, axis=0, tiled=True)
        logits = dot_t(ffn_all, router_w).reshape(blocks, rows, EXPERTS)
        used = jnp.transpose(chosen, (0, 2, 1)) > 0
        gates = jax.nn.softmax(jnp.where(used, logits, -jnp.inf), axis=-1)
        slot_rows = choose(pick, ffn_all.reshape(blocks, rows, -1), count)
        mine_gates = jnp.einsum("bte,jxe->bjt", gates, mine, precision=lax.Precision.HIGHEST)
        slot_gates = jnp.sum(
            pick.reshape(blocks, count, CAP, rows).astype(jnp.float32) * mine_gates[:, :, None, :],
            axis=3,
        )
        slot_gates = jnp.transpose(slot_gates, (1, 0, 2)).reshape(count, -1, 1)
        gate_pre = each_dot("ecd,edf->ecf", slot_rows, gate_w)
        up_pre = each_dot("ecd,edf->ecf", slot_rows, up_w)
        scaled = low(slot_gates * jax.nn.silu(gate_pre) * up_pre)
        slot_out = low(each_dot("ecf,efd->ecd", scaled, down_w))
        expert_state = (slot_rows, gate_pre, up_pre, scaled, slot_gates)
    saved = (
        layer_in,
        attention_state,
        after_update,
        normed_ffn,
        own_gates,
        expert_state,
    )
    return (after_update, slot_out, saved, (own, other), received)


def token_sums(pick_t, slot_out, collective_id, *carry, spread=()):
    if has_kernels():
        sums, *received = combine(pick_t, slot_out, collective_id, carry, spread)
        return sums, received
    sums = give_back(pick_t, slot_out).astype(jnp.float32)
    sums = lax.psum_scatter(sums, TOKENS, scatter_dimension=0, tiled=True)
    received = [pass_to(array, to) for to, array in carry]
    return sums, received + [spread_rows(array) for array in spread]


def spread_rows(parts):
    return lax.all_to_all(parts, "seq", split_axis=0, concat_axis=0, tiled=True)


def expert_gradients(number, layer_grad, saved, picking, experts, *carry):
    chosen, pick, pick_t, first_expert = picking
    own, other = experts
    count = own[0].shape[0]
    blocks, _, rows = chosen.shape
    slot_rows, gate_pre, up_pre, scaled, slot_gates = saved[-1]
    if has_kernels():
        slot_grads, gate_low, up_low, gate_term, slot_out, *received = expert_backward(
            number, low(layer_grad), pick, gate_pre, up_pre, slot_gates, own, other, 4 + number, carry
        )
        gate_term = gate_term[:, :, :1]
    else:
        gate_w, up_w, down_w = by_layer(number, own, other)
        grad_all = lax.all_gather(low(layer_grad), TOKENS, axis=0, tiled=True)
        slot_grads = choose(pick, grad_all.reshape(blocks, rows, -1), count)
        plain_grad = each_dot("ecd,efd->ecf", slot_grads, down_w)
        sigmoid = jax.nn.sigmoid(gate_pre)
        activated = gate_pre * sigmoid
        gate_term = jnp.sum(plain_grad * (activated * up_pre), axis=2, keepdims=True)
        hidden_grad = slot_gates * plain_grad
        gate_low = low(hidden_grad * up_pre * sigmoid * (1.0 + gate_pre * (1.0 - sigmoid)))
        up_low = low(hidden_grad * activated)
        slot_out = low(
            each_dot("ecf,edf->ecd", gate_low, gate_w) + each_dot("ecf,edf->ecd", up_low, up_w)
        )
        received = [pass_to(array, to) for to, array in carry]
    expert_grads = (
        low(each_dot("ecd,ecf->edf", slot_rows, gate_low)),
        low(each_dot("ecd,ecf->edf", slot_rows, up_low)),
        low(each_dot("ecf,ecd->efd", scaled, slot_grads)),
    )
    slot_out, *expert_grads = lax.optimization_barrier((slot_out, *expert_grads))
    return slot_out, gate_term, expert_grads, received


def backward_layer(
    number, layer_grad, normed_grad, gate_term, saved, picking, weights, *carry, spread=()
):
    attn_scale, ffn_scale, qkv_w, out_w, router_w = weights
    chosen, pick, _, _ = picking
    (
        layer_in,
        (normed_all, mixed_t, heads, log_total),
        after_update,
        normed_ffn,
        own_gates,
        _,
    ) = saved
    blocks, _, rows = chosen.shape
    count = gate_term.shape[0]
    by_slot = jnp.transpose(gate_term.reshape(count, blocks, CAP), (1, 0, 2))
    gate_terms = jnp.sum(
        pick.reshape(blocks, count, CAP, rows).astype(jnp.float32) * by_slot[..., None], axis=2
    )
    gate_terms = lax.all_to_all(gate_terms, TOKENS, split_axis=0, concat_axis=0, tiled=True)
    gate_terms = jnp.sum(gate_terms.reshape(EXPERTS, -1, rows), axis=1)
    logit_grad = low(
        own_gates * (gate_terms - jnp.sum(own_gates * gate_terms, axis=0, keepdims=True))
    )
    router_grad = dot(logit_grad, normed_ffn)
    normed_grad = normed_grad + t_dot(logit_grad, router_w)
    after_part, ffn_gain_grad = jax.vjp(rms_norm, after_update, ffn_scale)[1](normed_grad)
    after_grad = after_part + layer_grad
    if has_kernels():
        normed_attn, branch_all, qkv_grad, *received = attention_backward_call(
            low(after_grad),
            qkv_w,
            out_w,
            wide_tables(4 * layer_in.shape[0]),
            heads,
            log_total,
            11 + number,
            carry,
            spread,
        )
        branch_all = branch_all.reshape(-1, layer_in.shape[1])
    else:
        branch_all = lax.all_gather(low(after_grad), "seq", axis=0, tiled=True)
        head_grad = low(dot_t(branch_all, out_w))
        qkv_grad = attention_backward(head_grad, *heads, log_total)
        normed_attn = low(dot_t(qkv_grad, qkv_w))
        normed_attn = lax.psum_scatter(normed_attn, "seq", scatter_dimension=0, tiled=True)
        received = [pass_to(array, to) for to, array in carry]
        received = received + [spread_rows(array) for array in spread]
    out_grad = dot(mixed_t, branch_all)
    qkv_weight_grad = t_dot(normed_all, qkv_grad)
    input_part, attn_gain_grad = jax.vjp(rms_norm, layer_in, attn_scale)[1](
        normed_attn.astype(jnp.float32)
    )
    small = [router_grad, attn_gain_grad[None], ffn_gain_grad[None]]
    small = jnp.concatenate(small + [jnp.zeros((128 - EXPERTS - 2, small[0].shape[1]))], axis=0)
    qkv_weight_grad = jnp.concatenate([low(qkv_weight_grad), low(small).T], axis=1)
    return (input_part + after_grad, (qkv_weight_grad, low(out_grad)), received)


def by_layer(number, own, other):
    is_own = lax.axis_index("section") == number
    return jax.tree.map(lambda mine, received: jnp.where(is_own, mine, received), own, other)


def body(
    hidden_in,
    out_grad,
    attn_gain,
    ffn_gain,
    query_matrix,
    key_matrix,
    value_matrix,
    output_matrix,
    router_matrix,
    w_gate,
    w_up,
    w_down,
    routes,
):
    section = lax.axis_index("section")
    dp, seq = lax.axis_size("dp"), lax.axis_size("seq")
    seq_index = lax.axis_index("seq")
    first = section == 0
    width = hidden_in.shape[3]
    depth = query_matrix.shape[1]

    layer_in = lax.dynamic_index_in_dim(hidden_in, section, 0, keepdims=False)[0]
    top_grad = lax.dynamic_index_in_dim(out_grad, section, 0, keepdims=False)[0]
    own_group = jnp.concatenate(
        [
            matrix[0].reshape(depth, seq, -1)
            for matrix in (query_matrix, key_matrix, value_matrix)
        ],
        axis=2,
    )
    to_group = []
    for flat in range(dp * seq):
        to_group.append((flat, (flat % dp) * seq + flat // dp))
    from_group = [(target, source) for source, target in to_group]
    other_group = swap(own_group)
    own_out = lax.ppermute(output_matrix[0], TOKENS, to_group)
    other_out = swap(own_out)
    local = w_gate.shape[1]
    hidden_units = w_gate.shape[3]
    if local >= seq:
        count, units = local // seq, hidden_units
        start, unit_start = seq_index * count, 0
    else:
        count, units = 1, hidden_units * local // seq
        start, unit_start = seq_index * local // seq, (seq_index % (seq // local)) * units
    first_expert = lax.axis_index("dp") * local + start
    own_experts = (
        lax.dynamic_slice(w_gate[0], (start, 0, unit_start), (count, width, units)),
        lax.dynamic_slice(w_up[0], (start, 0, unit_start), (count, width, units)),
        lax.dynamic_slice(w_down[0], (start, unit_start, 0), (count, units, width)),
    )
    gate_slice, other_group = lax.optimization_barrier((own_experts[0], other_group))
    other_gate = swap(gate_slice)
    experts = (own_experts, (other_gate,))

    small = jnp.concatenate([router_matrix[0].T, attn_gain, ffn_gain], axis=0)
    paths = routes[0, :, 0]
    if has_kernels():
        small = jnp.pad(small, ((0, -small.shape[0] % 16), (0, 256 - depth)))
        paths = low(jnp.transpose(paths, (0, 2, 1)).reshape(2 * TOP_K, -1))
        picks, picks_t, chosens, small = prepare(
            jnp.concatenate([paths, small], axis=0), count, hidden_in.shape[2], depth, 13
        )
        pickings = [(chosens[n], picks[n], picks_t[n], first_expert) for n in range(2)]
    else:
        small = lax.all_gather(small, ("section", "dp", "seq"), axis=0, tiled=False)
        small = jnp.transpose(small.reshape(2, dp * seq, -1, depth), (0, 2, 1, 3))
        small = small.reshape(2, -1, width)
        paths = lax.all_gather(paths, ("section", "dp", "seq"), axis=0, tiled=False)
        paths = lax.dynamic_index_in_dim(paths, section, 1, keepdims=False)
        paths = paths.reshape(2, dp * seq, -1, TOP_K)
        pickings = [routing(paths[n], first_expert, count) + (first_expert,) for n in range(2)]

    weights = []
    for number in range(2):
        part = by_layer(number, own_group, other_group)
        part = lax.all_to_all(part, "seq", split_axis=1, concat_axis=0, tiled=True)
        qkv_w = lax.all_gather(part.reshape(seq * depth, -1), "dp", axis=0, tiled=True)
        out_w = lax.all_gather(
            by_layer(number, own_out, other_out), "dp", axis=0, tiled=True
        )
        weights.append(
            (
                small[number, EXPERTS].astype(jnp.float32),
                small[number, EXPERTS + 1].astype(jnp.float32),
                qkv_w,
                out_w,
                small[number, :EXPERTS],
            )
        )

    def own_layer(pieces):
        return jnp.where(first, pieces[0], pieces[1])

    def both_micros(own, other):
        return jnp.stack([jnp.where(first, own, other), jnp.where(first, other, own)])[
            None, :, None
        ]

    def summed(own, other):
        return own_layer(own).astype(jnp.float32) + own_layer(other).astype(jnp.float32)

    def dp_sums(dense):
        return [lax.psum_scatter(part, "dp", scatter_dimension=0, tiled=True) for part in dense]

    def row_parts(piece, kind):
        if local >= seq:
            piece = piece.reshape(count, seq, piece.shape[1] // seq, -1)
            return jnp.transpose(piece, (1, 0, 2, 3))
        if kind < 2:
            return piece.reshape(seq, -1, units)
        piece = piece.reshape(-1, hidden_units // seq, width)
        share = seq // local
        parts = jnp.zeros((seq,) + piece.shape[1:], piece.dtype)
        return lax.dynamic_update_slice_in_dim(
            parts, piece, (seq_index % share) * piece.shape[0], axis=0
        )

    def whole_rows(parts, kind):
        parts = parts.astype(jnp.float32)
        if local < seq:
            parts = parts.reshape((local, seq // local) + parts.shape[1:])
            if kind < 2:
                parts = jnp.transpose(parts, (0, 2, 1, 3))
            else:
                parts = jnp.sum(parts, axis=1)
            return parts.reshape((local,) + parts.shape[1 : 2] + (-1,))[None]
        return parts.reshape((local,) + parts.shape[2:])[None]

    layer_in, other_gate = lax.optimization_barrier((layer_in, other_gate))
    experts = (own_experts, (other_gate,))
    first_in = layer_in.astype(jnp.float32)
    updated, slot_out, first_saved, experts, _ = forward_layer(
        0, first_in, pickings[0], weights[0], experts, (None, own_experts[1])
    )
    sums, _ = token_sums(pickings[0][2], slot_out, 3)
    first_out = updated + sums
    second_updated, second_slots, second_saved, experts, (other_out,) = forward_layer(
        1, first_out, pickings[1], weights[1], experts, (0, first_out)
    )
    top_grad = top_grad.astype(jnp.float32)
    slot_out, gate_term, second_experts, _ = expert_gradients(
        1, top_grad, second_saved, pickings[1], experts
    )
    sums, (second_gate,) = token_sums(pickings[1][2], slot_out, 6, (1, second_experts[0]))
    middle_grad, second_dense, (second_up,) = backward_layer(
        1, top_grad, sums, gate_term, second_saved, pickings[1], weights[1], (1, second_experts[1])
    )
    slot_out, gate_term, first_experts, (second_down,) = expert_gradients(
        0, middle_grad, first_saved, pickings[0], experts, (1, second_experts[2])
    )
    sums, (first_gate, other_middle) = token_sums(
        pickings[0][2], slot_out, 7, (0, first_experts[0]), (1, middle_grad)
    )
    sums, *second_dense = lax.optimization_barrier((sums, *second_dense))
    second_dense = dp_sums(second_dense)
    gate_sum = low(summed((first_experts[0], second_experts[0]), (first_gate, second_gate)))
    bottom_grad, first_dense, (first_up, gate_rows) = backward_layer(
        0,
        middle_grad,
        sums,
        gate_term,
        first_saved,
        pickings[0],
        weights[0],
        (0, first_experts[1]),
        spread=(row_parts(gate_sum, 0),),
    )
    up_sum = low(summed((first_experts[1], second_experts[1]), (first_up, second_up)))
    second_slots, *first_dense, second_dense[0], second_dense[1] = lax.optimization_barrier(
        (second_slots, *first_dense, *second_dense)
    )
    first_dense = dp_sums(first_dense)
    sums, (first_down, up_rows) = token_sums(
        pickings[1][2],
        second_slots,
        8,
        (0, first_experts[2]),
        spread=(row_parts(up_sum, 1),),
    )
    sums, *first_dense = lax.optimization_barrier((sums, *first_dense))
    second_out = second_updated + sums
    down_sum = low(summed((first_experts[2], second_experts[2]), (first_down, second_down)))
    own_cols, own_rows = [own_layer((first_dense[k], second_dense[k])) for k in range(2)]
    other_cols, other_rows = [own_layer((second_dense[k], first_dense[k])) for k in range(2)]
    if has_kernels():
        down_rows, cols_sum, out_sum, other_second, other_bottom = last_exchange(
            row_parts(down_sum, 2),
            own_cols.reshape(seq, depth, -1),
            other_cols.reshape(seq, depth, -1),
            own_rows,
            other_rows,
            14,
            ((1, second_out), (0, bottom_grad)),
        )
    else:
        down_rows = spread_rows(row_parts(down_sum, 2))
        cols_sum = low(own_cols.astype(jnp.float32) + swap(other_cols).astype(jnp.float32))
        cols_sum = spread_rows(cols_sum.reshape(seq, depth, -1))
        out_sum = low(own_rows.astype(jnp.float32) + swap(other_rows).astype(jnp.float32))
        out_sum = lax.ppermute(out_sum, TOKENS, from_group)
        other_second, other_bottom = pass_to(second_out, 1), pass_to(bottom_grad, 0)
    expert_sums = [whole_rows(rows, k) for k, rows in enumerate((gate_rows, up_rows, down_rows))]
    layer_outs = both_micros(
        own_layer((first_out, second_out)), own_layer((other_out, other_second))
    )
    section_grads = both_micros(
        own_layer((bottom_grad, middle_grad)), own_layer((other_bottom, other_middle))
    )
    qkv_sum, out_sum = cols_sum.astype(jnp.float32), out_sum.astype(jnp.float32)
    kv_width = KV_HEADS * HEAD_DIM // seq
    q_width = GROUP * kv_width
    qkv_width = q_width + 2 * kv_width
    small_sum = jnp.sum(qkv_sum[:, :, qkv_width:], axis=0)

    def columns(begin, end):
        return jnp.transpose(qkv_sum[:, :, begin:end], (1, 0, 2)).reshape(depth, -1)[None]

    return (
        layer_outs,
        section_grads,
        small_sum[:, EXPERTS][None],
        small_sum[:, EXPERTS + 1][None],
        columns(0, q_width),
        columns(q_width, q_width + kv_width),
        columns(q_width + kv_width, qkv_width),
        out_sum[None],
        small_sum[:, :EXPERTS][None],
        *expert_sums,
    )


def solution(mesh):
    return jax.shard_map(
        body,
        mesh=mesh,
        in_specs=(
            P(None, "dp", "seq", None),
            P(None, "dp", "seq", None),
            P("section", ("dp", "seq")),
            P("section", ("dp", "seq")),
            P("section", ("dp", "seq"), None),
            P("section", ("dp", "seq"), None),
            P("section", ("dp", "seq"), None),
            P("section", ("dp", "seq"), None),
            P("section", ("dp", "seq"), None),
            P("section", "dp", None, None),
            P("section", "dp", None, None),
            P("section", "dp", None, None),
            P("section", None, "dp", "seq", None),
        ),
        out_specs=(
            P("section", None, "dp", "seq", None),
            P("section", None, "dp", "seq", None),
            P("section", ("dp", "seq")),
            P("section", ("dp", "seq")),
            P("section", ("dp", "seq"), None),
            P("section", ("dp", "seq"), None),
            P("section", ("dp", "seq"), None),
            P("section", ("dp", "seq"), None),
            P("section", ("dp", "seq"), None),
            P("section", "dp", "seq", None),
            P("section", "dp", "seq", None),
            P("section", "dp", "seq", None),
        ),
        check_vma=False,
    )
```

```python
import jax
import jax.numpy as jnp
from jax import lax
from jax.experimental import pallas as pl
from jax.experimental.pallas import tpu as pltpu
from jax.sharding import PartitionSpec as P

HEADS = 24
KV_HEADS = 8
HEAD_DIM = 64
TOP_K = 8
EXPERTS = 32
CAP = 80
GROUP = HEADS // KV_HEADS
TOKENS = ("dp", "seq")
MESH = pl.DeviceIdType.MESH
DMA = pltpu.SemaphoreType.DMA

epsilon = 1e-06


def dot(a, b):
    return jnp.dot(a, b, preferred_element_type=jnp.float32)


def dot_t(a, b):
    return lax.dot_general(a, b, (((1,), (1,)), ((), ())), preferred_element_type=jnp.float32)


def t_dot(a, b):
    return lax.dot_general(a, b, (((0,), (0,)), ((), ())), preferred_element_type=jnp.float32)


def low(v):
    return v.astype(jnp.bfloat16)


def swap(block):
    return lax.ppermute(block, "section", [(0, 1), (1, 0)])


def pass_to(block, section):
    return lax.ppermute(block, "section", [(1 - section, section)])


def rms_norm(values, norm_gain):
    return (
        values * lax.rsqrt(jnp.mean(values * values, axis=-1, keepdims=True) + epsilon) * norm_gain
    )


def rotary_tables(length):
    half_dim = HEAD_DIM // 2
    frequency = 10000.0 ** (-jnp.arange(half_dim, dtype=jnp.float32) * 2.0 / HEAD_DIM)
    angles = jnp.arange(length, dtype=jnp.float32)[:, None] * frequency[None, :]
    return (jnp.cos(angles)[:, None, :], jnp.sin(angles)[:, None, :])


def rotate(values, cos_table, sin_table):
    length = values.shape[0]
    split_heads = values.reshape(length, -1, HEAD_DIM)
    first_half = split_heads[..., : HEAD_DIM // 2]
    second_half = split_heads[..., HEAD_DIM // 2 :]
    turned = jnp.concatenate(
        [
            first_half * cos_table - second_half * sin_table,
            second_half * cos_table + first_half * sin_table,
        ],
        axis=-1,
    )
    return turned.reshape(length, -1)


def attention_forward(q_heads, k_heads, v_heads):
    length = q_heads.shape[0]
    local_kv = k_heads.shape[1] // HEAD_DIM
    cos_table, sin_table = rotary_tables(length)
    q_rot = low(rotate(q_heads.astype(jnp.float32), cos_table, sin_table)).reshape(
        length, local_kv, GROUP, HEAD_DIM
    )
    k_rot = low(rotate(k_heads.astype(jnp.float32), cos_table, sin_table)).reshape(
        length, local_kv, HEAD_DIM
    )
    values = v_heads.reshape(length, local_kv, HEAD_DIM)
    block_rows = min(512, length)
    outputs = []
    totals_list = []
    for first_row in range(0, length, block_rows):
        key_end = first_row + block_rows
        scores = (
            jnp.einsum(
                "qhgd,khd->hgqk",
                q_rot[first_row:key_end],
                k_rot[:key_end],
                preferred_element_type=jnp.float32,
            )
            * 0.125
        )
        causal = (first_row + jnp.arange(block_rows, dtype=jnp.int32))[:, None] >= jnp.arange(
            key_end, dtype=jnp.int32
        )[None, :]
        scores = jnp.where(causal, scores, -jnp.inf)
        row_peak = jnp.max(scores, axis=-1, keepdims=True)
        exponents = jnp.exp(scores - row_peak)
        totals = jnp.sum(exponents, axis=-1, keepdims=True)
        attended = jnp.einsum(
            "hgqk,khd->qhgd",
            low(exponents / totals),
            values[:key_end],
            preferred_element_type=jnp.float32,
        )
        outputs.append(low(attended).reshape(block_rows, -1))
        totals_list.append((row_peak + jnp.log(totals))[..., 0])
    return (jnp.concatenate(outputs, axis=0), jnp.stack(totals_list), q_rot, k_rot, values)


def attention_backward(head_grad, q_rot, k_rot, values, log_total):
    length, local_kv = q_rot.shape[:2]
    cos_table, sin_table = rotary_tables(length)
    block_rows = min(512, length)
    grad_rows = head_grad.reshape(length, local_kv, GROUP, HEAD_DIM)
    key_acc = jnp.zeros((length, local_kv, HEAD_DIM), jnp.float32)
    value_acc = jnp.zeros((length, local_kv, HEAD_DIM), jnp.float32)
    query_parts = []
    for block_number, first_row in enumerate(range(0, length, block_rows)):
        key_end = first_row + block_rows
        q_block = q_rot[first_row:key_end]
        grad_block = grad_rows[first_row:key_end]
        key_part = k_rot[:key_end]
        scores = (
            jnp.einsum("qhgd,khd->hgqk", q_block, key_part, preferred_element_type=jnp.float32)
            * 0.125
        )
        causal = (first_row + jnp.arange(block_rows, dtype=jnp.int32))[:, None] >= jnp.arange(
            key_end, dtype=jnp.int32
        )[None, :]
        scores = jnp.where(causal, scores, -jnp.inf)
        probs_full = jnp.exp(scores - log_total[block_number][..., None])
        prob_grad = jnp.einsum(
            "qhgd,khd->hgqk", grad_block, values[:key_end], preferred_element_type=jnp.float32
        )
        score_grad = probs_full * (
            prob_grad - jnp.sum(probs_full * prob_grad, axis=-1, keepdims=True)
        )
        score_low = low(score_grad)
        query_parts.append(
            jnp.einsum("hgqk,khd->qhgd", score_low, key_part, preferred_element_type=jnp.float32)
            * 0.125
        )
        key_acc = key_acc.at[:key_end].add(
            jnp.einsum("hgqk,qhgd->khd", score_low, q_block, preferred_element_type=jnp.float32)
            * 0.125
        )
        value_acc = value_acc.at[:key_end].add(
            jnp.einsum(
                "hgqk,qhgd->khd", low(probs_full), grad_block, preferred_element_type=jnp.float32
            )
        )
    query_all = jnp.concatenate(query_parts, axis=0).reshape(length, -1)
    query_grad = rotate(query_all, cos_table, -sin_table)
    key_grad = rotate(key_acc.reshape(length, -1), cos_table, -sin_table)
    return jnp.concatenate(
        [low(query_grad), low(key_grad), low(value_acc).reshape(length, -1)], axis=1
    )


def remote(src, dst, send_sem, recv_sem, **device):
    return pltpu.make_async_remote_copy(
        src_ref=src,
        dst_ref=dst,
        send_sem=send_sem,
        recv_sem=recv_sem,
        device_id=device,
        device_id_type=MESH,
    )


def greet(d, s, section=None, spread=False):
    barrier = pltpu.get_barrier_semaphore()

    def signal(**device):
        pl.semaphore_signal(barrier, inc=1, device_id=device, device_id_type=MESH)

    signal(seq=s ^ 1)
    signal(seq=s ^ 2)

    @pl.when(d > 0)
    def _():
        signal(dp=d - 1)

    @pl.when(d < 3)
    def _():
        signal(dp=d + 1)

    known = 3
    if section is not None:
        signal(section=1 - section)
        known = 4
    if spread:
        signal(seq=s ^ 3)
        known = known + 1
    inner = (d > 0) & (d < 3)

    @pl.when(inner)
    def _():
        pl.semaphore_wait(barrier, known + 1)

    @pl.when(jnp.logical_not(inner))
    def _():
        pl.semaphore_wait(barrier, known)


class Carried:
    def __init__(self, sections, sources, targets, sems):
        self.section = lax.axis_index("section")
        self.copies = []
        for k, (to, source, target) in enumerate(zip(sections, sources, targets)):
            copy = remote(source, target, sems.at[k, 0], sems.at[k, 1], section=1 - self.section)
            self.copies.append((to, copy))

    def start(self):
        for to, copy in self.copies:
            if to is None:
                copy.start()
            else:

                @pl.when(self.section != to)
                def _():
                    copy.start()

    def finish(self):
        for to, copy in self.copies:
            if to is None:
                copy.wait()
            else:

                @pl.when(self.section != to)
                def _():
                    copy.wait_send()

                @pl.when(self.section == to)
                def _():
                    copy.wait_recv()


class Spread:
    def __init__(self, source, target, sems):
        s = lax.axis_index("seq")
        self.local = pltpu.make_async_copy(source.at[s], target.at[s], sems.at[0, 0])
        self.copies = [
            remote(source.at[s ^ flip], target.at[s], sems.at[flip, 0], sems.at[flip, 1], seq=s ^ flip)
            for flip in (3, 2, 1)
        ]

    def start(self):
        for copy in self.copies:
            copy.start()
        self.local.start()

    def finish(self):
        self.local.wait()
        for copy in self.copies:
            copy.wait()


def cost():
    return pl.CostEstimate(flops=80_000_000_000, bytes_accessed=100_000_000, transcendentals=0)


def gather_scratch(rows, width):
    return [
        pltpu.VMEM((16, rows, width), jnp.bfloat16),
        DMA(()),
        DMA((2, 4)),
        DMA((4,)),
        DMA((4,)),
        DMA((4,)),
        DMA((4, 2)),
        DMA((4, 2)),
    ]


def gather_blocks(x_ref, scratch, compute, carried=None, first=None, spread=False):
    land, lsem, zs, zr, ys, yr, cs, cr = scratch
    d, s = lax.axis_index("dp"), lax.axis_index("seq")

    def place(z, column):
        return land.at[z * 4 + column]

    def z_copy(src, z, right):
        target = d + 1 if right else d - 1
        return remote(src, place(z, s), zs.at[int(right), z], zr.at[z], dp=target)

    def y_copy(src, z):
        return remote(src, place(z, s), ys.at[z], yr.at[z], seq=s ^ 2)

    def core_copy(src, z, across):
        column = s ^ 2 if across else s
        return remote(src, place(z, column), cs.at[z, across], cr.at[z, across], seq=s ^ 1)

    greet(d, s, None if carried is None else carried.section, spread)
    if first is not None:
        first()
    own = pltpu.make_async_copy(x_ref, place(d, s), lsem)
    own.start()
    if carried is not None and first is None:
        carried.start()

    @pl.when(d < 3)
    def _():
        z_copy(x_ref, d, True).start()

    @pl.when(d > 0)
    def _():
        z_copy(x_ref, d, False).start()

    y_copy(x_ref, d).start()
    core_copy(x_ref, d, 0).start()
    own.wait()

    @pl.loop(0, 4)
    def _(i):
        @pl.when(i < 3)
        def _():
            left, right = d - (i + 1), d + (i + 1)

            @pl.when(left >= 0)
            def _():
                z_copy(place(left, s), left, True).wait_recv()

                @pl.when(d < 3)
                def _():
                    z_copy(place(left, s), left, True).start()

            @pl.when(right <= 3)
            def _():
                z_copy(place(right, s), right, False).wait_recv()

                @pl.when(d > 0)
                def _():
                    z_copy(place(right, s), right, False).start()

            following = d ^ (i + 1)
            y_copy(place(following, s), following).start()
            core_copy(place(following, s), following, 0).start()

        z = d ^ i
        y_copy(place(z, s ^ 2), z).wait_recv()
        core_copy(place(z, s ^ 2), z, 1).start()
        core_copy(place(z, s ^ 1), z, 0).wait_recv()
        core_copy(place(z, s ^ 3), z, 1).wait_recv()
        compute(z)

    for z in range(4):

        @pl.when((z <= d) & (d < 3))
        def _():
            z_copy(place(z, s), z, True).wait_send()

        @pl.when((z >= d) & (d > 0))
        def _():
            z_copy(place(z, s), z, False).wait_send()

        y_copy(place(z, s), z).wait_send()
        core_copy(place(z, s), z, 0).wait_send()
        core_copy(place(z, s), z, 1).wait_send()
    return land


def prepare_kernel(
    x_ref, group_ref, gate_ref,
    pick_out, pick_t_out, chosen_out, small_out, qkv_out, parts_out, gate_out,
    both, places, groups, parts, lsem, carry_sem, spread_sem, qs, qr, *gather
):
    d, s, section = lax.axis_index("dp"), lax.axis_index("seq"), lax.axis_index("section")
    known = x_ref.shape[0]
    count = pick_out.shape[2] // CAP
    rows = pick_out.shape[3]
    land = gather[0]
    part = both.at[pl.ds(pl.multiple_of(section * known, known), known)]
    swaps = Carried((None, None), (x_ref, group_ref), (part, groups.at[section]), carry_sem)
    gates = Carried((None,), (gate_ref,), (gate_out,), carry_sem.at[pl.ds(2, 1)])
    spreads = [Spread(groups.at[n], parts.at[n], spread_sem.at[n]) for n in range(2)]
    own_columns = pltpu.make_async_copy(parts.at[0], qkv_out.at[d], lsem.at[2])

    def along(src, z, right):
        target = d + 1 if right else d - 1
        return remote(src, qkv_out.at[z], qs.at[int(right), z], qr.at[z], dp=target)

    def first():
        swaps.start()
        own = [
            pltpu.make_async_copy(x_ref, part, lsem.at[0]),
            pltpu.make_async_copy(group_ref, groups.at[section], lsem.at[1]),
        ]
        for copy in own:
            copy.start()
        for copy in own:
            copy.wait()
        swaps.finish()
        gates.start()
        for side in spreads:
            side.start()
        spreads[0].finish()
        own_columns.start()

        @pl.when(d < 3)
        def _():
            along(parts.at[0], d, True).start()

        @pl.when(d > 0)
        def _():
            along(parts.at[0], d, False).start()

    def hop(h):
        @pl.when(d - h >= 0)
        def _():
            along(qkv_out.at[d - h], d - h, True).wait_recv()

            @pl.when(d < 3)
            def _():
                along(qkv_out.at[d - h], d - h, True).start()

        @pl.when(d + h <= 3)
        def _():
            along(qkv_out.at[d + h], d + h, False).wait_recv()

            @pl.when(d > 0)
            def _():
                along(qkv_out.at[d + h], d + h, False).start()

    gather_blocks(both, gather, lambda z: None, gates, first, True)
    hop(1)
    first_expert = (d * 4 + s) * count
    before = lax.broadcasted_iota(jnp.int32, (rows, rows), 0)
    before = low(before < lax.broadcasted_iota(jnp.int32, (rows, rows), 1))
    slot = lax.broadcasted_iota(jnp.int32, (CAP, rows), 0)
    expert = lax.broadcasted_iota(jnp.int32, (EXPERTS, rows), 0)
    lane = lax.broadcasted_iota(jnp.int32, (rows, count * CAP), 1)

    @pl.loop(0, 2)
    def _(layer):
        @pl.loop(0, 16)
        def _(b):
            paths = land[b, pl.ds(pl.multiple_of(layer * known, 16), 16), :].astype(jnp.float32)
            paths = jnp.where(section == 0, paths[:TOP_K], paths[TOP_K:]).astype(jnp.int32)
            chosen = expert == paths[0:1]
            for k in range(1, TOP_K):
                chosen = chosen | (expert == paths[k : k + 1])
            chosen_out[layer, b] = low(chosen)
            mine = [
                jnp.max((paths == first_expert + j).astype(jnp.float32), axis=0, keepdims=True)
                for j in range(count)
            ]
            mine = jnp.concatenate(mine + [jnp.zeros((8 - count, rows), jnp.float32)], axis=0)
            place = jnp.where(mine > 0.5, dot(low(mine), before), -10000.0)
            places[...] = place
            for j in range(count):
                pick_out[layer, b, j * CAP : (j + 1) * CAP, :] = low(
                    slot == place[j : j + 1].astype(jnp.int32)
                )
            turned = places[...].T.astype(jnp.int32)
            pick_t = turned[:, 0:1] == lane
            for j in range(1, count):
                pick_t = pick_t & (lane < j * CAP) | (turned[:, j : j + 1] == lane - j * CAP)
            pick_t_out[layer, b] = low(pick_t)

        depth = small_out.shape[2] // 16
        for b in range(16):
            small = land[b, pl.ds(pl.multiple_of(layer * known + 16, 16), known - 16), :]
            small_out[layer, :, b * depth : (b + 1) * depth] = small[:, :depth]

        @pl.when(layer == 0)
        def _():
            hop(2)

    hop(3)
    spreads[1].finish()
    layer_1 = pltpu.make_async_copy(parts.at[1], parts_out, lsem.at[0])
    layer_1.start()
    for z in range(4):

        @pl.when((z <= d) & (d < 3))
        def _():
            along(parts.at[0], z, True).wait_send()

        @pl.when((z >= d) & (d > 0))
        def _():
            along(parts.at[0], z, False).wait_send()

    own_columns.wait()
    layer_1.wait()
    gates.finish()


def prepare(x, group, gate, count, rows, depth, collective_id):
    known, width = x.shape
    bf = jnp.bfloat16
    anywhere = pl.BlockSpec(memory_space=pl.ANY)
    near = pl.BlockSpec(memory_space=pltpu.VMEM)
    return pl.pallas_call(
        prepare_kernel,
        out_shape=[
            jax.ShapeDtypeStruct((2, 16, count * CAP, rows), bf),
            jax.ShapeDtypeStruct((2, 16, rows, count * CAP), bf),
            jax.ShapeDtypeStruct((2, 16, EXPERTS, rows), bf),
            jax.ShapeDtypeStruct((2, known - 16, 16 * depth), bf),
            jax.ShapeDtypeStruct((4,) + group.shape, bf),
            jax.ShapeDtypeStruct(group.shape, bf),
            jax.ShapeDtypeStruct(gate.shape, bf),
        ],
        in_specs=[anywhere] * 3,
        out_specs=[near] * 4 + [anywhere] * 3,
        scratch_shapes=[
            pltpu.VMEM((2 * known, width), bf),
            pltpu.VMEM((8, rows), jnp.float32),
            pltpu.VMEM((2,) + group.shape, bf),
            pltpu.VMEM((2,) + group.shape, bf),
            DMA((3,)),
            DMA((3, 2)),
            DMA((2, 4, 2)),
            DMA((2, 4)),
            DMA((4,)),
        ]
        + gather_scratch(2 * known, width),
        compiler_params=pltpu.CompilerParams(
            collective_id=collective_id, has_side_effects=True, vmem_limit_bytes=60 << 20
        ),
        cost_estimate=cost(),
        name="prepare",
    )(x, group, gate)


def pick_weights(own_refs, other_refs, held, sems, own_layer):
    mine = lax.axis_index("section") == own_layer

    @pl.when(mine)
    def _():
        for k, ref in enumerate(own_refs):
            pltpu.make_async_copy(ref, held[k], sems.at[k]).start()

    @pl.when(jnp.logical_not(mine))
    def _():
        for k, ref in enumerate(other_refs):
            pltpu.make_async_copy(ref, held[k], sems.at[k]).start()

    def ready(k):
        pltpu.make_async_copy(own_refs[k], held[k], sems.at[k]).wait()

    return ready


def expert_forward_kernel(
    layer, x_ref, pick_ref, chosen_ref, router_ref, mine_ref,
    wg_own, wu_own, wd_own, wg_other, wu_other, wd_other,
    rows_out, gate_out, up_out, hidden_out, slot_gate_out, y_out,
    wg, wu, wd, rows, gate, up, hidden, slot_gate, y, wsem, osem, carry_sem, *gather
):
    count = wg.shape[0]
    carried = None
    if layer == 0:
        carried = Carried((None,), (wd_own,), (wd_other,), carry_sem)
        ready = pick_weights((wg_own, wu_own), (wg_other, wu_other), (wg, wu), wsem, layer)
    else:
        ready = pick_weights(
            (wg_own, wu_own, wd_own), (wg_other, wu_other, wd_other), (wg, wu, wd), wsem, layer
        )
    land = gather[0]
    d = lax.axis_index("dp")

    def outs(z):
        part = pl.ds(z * 4 * CAP, 4 * CAP)
        return [
            pltpu.make_async_copy(held.at[:, part], out.at[:, part], osem.at[k, z])
            for k, (held, out) in enumerate(
                ((rows, rows_out), (gate, gate_out), (up, up_out), (hidden, hidden_out), (slot_gate, slot_gate_out))
            )
        ] + [pltpu.make_async_copy(y.at[pl.ds(z * 4, 4)], y_out.at[pl.ds(z * 4, 4)], osem.at[5, z])]

    def down(z):
        part = pl.ds(z * 4 * CAP, 4 * CAP)

        @pl.loop(0, count)
        def _(j):
            result = low(dot(hidden[j, part, :], wd[j]))
            for q in range(4):
                y[z * 4 + q, pl.ds(j * CAP, CAP), :] = result[q * CAP : (q + 1) * CAP]

    def compute(z):
        @pl.when(z == d)
        def _():
            for k in range(2 if layer == 0 else 3):
                ready(k)

        for q in range(4):
            b = z * 4 + q
            picked = low(dot(pick_ref[b], land[b]))
            for j in range(count):
                rows[j, pl.ds(b * CAP, CAP), :] = picked[j * CAP : (j + 1) * CAP]
        part = pl.ds(z * 4 * CAP, 4 * CAP)

        @pl.loop(0, count)
        def _(j):
            x = rows[j, part, :]
            g = dot(x, wg[j])
            u = dot(x, wu[j])
            logits = dot_t(x, router_ref[...])
            for q in range(4):
                b = z * 4 + q
                slots = slice(q * CAP, (q + 1) * CAP)
                seen = dot_t(pick_ref[b, pl.ds(j * CAP, CAP), :], chosen_ref[b])
                masked = jnp.where(seen > 0.5, logits[slots], -1e30)
                power = jnp.exp(masked - jnp.max(masked, axis=1, keepdims=True))
                own = jnp.sum(power * mine_ref[j], axis=1, keepdims=True)
                value = own / jnp.sum(power, axis=1, keepdims=True)
                slot_gate[j, pl.ds(b * CAP, CAP), :] = jnp.broadcast_to(value, (CAP, 128))
            gate[j, part, :] = low(g)
            up[j, part, :] = low(u)
            h = low(g * jax.nn.sigmoid(g) * u * slot_gate[j, part, :][:, :1])
            hidden[j, part, :] = h

        if layer != 0:
            down(z)
        for copy in outs(z)[: 5 if layer == 0 else 6]:
            copy.start()

    gather_blocks(x_ref, gather, compute, carried)
    if layer == 0:
        carried.finish()
        ready = pick_weights((wd_own,), (wd_other,), (wd,), wsem, layer)
        ready(0)
        for z in range(4):
            down(z)
            outs(z)[5].start()
    for z in range(4):
        for copy in outs(z):
            copy.wait()


def expert_forward(layer, x, pick, chosen, router, mine, own, other, collective_id):
    count, width, units = own[0].shape
    rows = x.shape[0]
    slots = 16 * CAP
    bf = jnp.bfloat16
    anywhere = pl.BlockSpec(memory_space=pl.ANY)
    near = pl.BlockSpec(memory_space=pltpu.VMEM)
    results = [
        ((count, slots, width), bf),
        ((count, slots, units), bf),
        ((count, slots, units), bf),
        ((count, slots, units), bf),
        ((count, slots, 128), jnp.float32),
        ((16, count * CAP, width), bf),
    ]

    def kernel(*refs):
        if layer == 0:
            refs = refs[:10] + refs[16:17] + refs[10:16] + refs[17:]
        expert_forward_kernel(layer, *refs)

    shapes = [jax.ShapeDtypeStruct(*result) for result in results]
    if layer == 0:
        shapes.append(jax.ShapeDtypeStruct(own[2].shape, bf))
        other = other[:2]
    operands = (x, pick, chosen, router, mine, *own, *other)
    return pl.pallas_call(
        kernel,
        out_shape=shapes,
        in_specs=[anywhere, near, near, near, near] + [anywhere] * (len(operands) - 5),
        out_specs=[anywhere] * len(shapes),
        scratch_shapes=[pltpu.VMEM(weight.shape, bf) for weight in own]
        + [pltpu.VMEM(*result) for result in results]
        + [DMA((3,)), DMA((6, 4)), DMA((1, 2))]
        + gather_scratch(rows, width),
        compiler_params=pltpu.CompilerParams(
            collective_id=collective_id, has_side_effects=True, vmem_limit_bytes=60 << 20
        ),
        cost_estimate=cost(),
        name="expert_forward",
    )(*operands)


def combine_kernel(sections, spreads, pick_ref, y_ref, *refs):
    kept = len(sections)
    sources, refs = refs[:kept], refs[kept:]
    spread_sources, refs = refs[:spreads], refs[spreads:]
    out_ref, *refs = refs
    targets, refs = refs[:kept], refs[kept:]
    spread_targets, refs = refs[:spreads], refs[spreads:]
    y, sent, own, core_in, y_in, z_in, lsem, zs, zr, ys, yr, cs, cr, carry_sem, spread_sem = refs
    carried = Carried(sections, sources, targets, carry_sem)
    spread = [Spread(a, b, spread_sem) for a, b in zip(spread_sources, spread_targets)]
    d, s = lax.axis_index("dp"), lax.axis_index("seq")
    half = out_ref.shape[0] // 2

    def loaded(b):
        return pltpu.make_async_copy(y_ref.at[b], y.at[b], lsem.at[b])

    def column(across, other_core):
        return s ^ (2 * across) ^ other_core

    for i in range(4):
        z = d ^ (3 - i)
        for across in (1, 0):
            for other_core in (1, 0):
                loaded(z * 4 + column(across, other_core)).start()
    greet(d, s, carried.section, spreads > 0)
    carried.start()

    def rows(k):
        return pl.ds(pl.multiple_of(k * half, half), half)

    def partial_sum(z, k, across, other_core):
        b = z * 4 + column(across, other_core)

        @pl.when(k == 0)
        def _():
            loaded(b).wait()

        return dot(pick_ref[b, rows(k), :], y[b])

    def core_copy(z, k, across):
        return remote(
            sent.at[z, across, rows(k)],
            core_in.at[z, across, rows(k)],
            cs.at[z, k, across],
            cr.at[z, k, across],
            seq=s ^ 1,
        )

    def y_copy(z, k):
        return remote(own.at[z, 1, rows(k)], y_in.at[z, rows(k)], ys.at[z, k], yr.at[z, k], seq=s ^ 2)

    def z_copy(z, k, right):
        target = d + 1 if right else d - 1
        return remote(
            own.at[z, 0, rows(k)],
            z_in.at[int(right), z, rows(k)],
            zs.at[z, k],
            zr.at[int(right), z, k],
            dp=target,
        )

    def start(i):
        z, k = d ^ (3 - i // 2), i % 2
        sent[z, 1, rows(k), :] = low(partial_sum(z, k, 1, 1))
        core_copy(z, k, 1).start()
        total = partial_sum(z, k, 1, 0)
        core_copy(z, k, 1).wait_recv()
        own[z, 1, rows(k), :] = low(total + core_in[z, 1, rows(k), :].astype(jnp.float32))
        y_copy(z, k).start()
        sent[z, 0, rows(k), :] = low(partial_sum(z, k, 0, 1))
        core_copy(z, k, 0).start()

    start(0)
    for side in spread:
        side.start()

    @pl.loop(0, 8)
    def _(i):
        @pl.when(i < 7)
        def _():
            start(i + 1)

        z, k = d ^ (3 - i // 2), i % 2
        total = partial_sum(z, k, 0, 0)
        core_copy(z, k, 0).wait_recv()
        total = total + core_in[z, 0, rows(k), :].astype(jnp.float32)
        y_copy(z, k).wait_recv()
        total = total + y_in[z, rows(k), :].astype(jnp.float32)

        @pl.when(z < d)
        def _():
            @pl.when(d < 3)
            def _():
                z_copy(z, k, False).wait_recv()
                own[z, 0, rows(k), :] = low(total + z_in[0, z, rows(k), :].astype(jnp.float32))

            @pl.when(d == 3)
            def _():
                own[z, 0, rows(k), :] = low(total)

            z_copy(z, k, False).start()

        @pl.when(z > d)
        def _():
            @pl.when(d > 0)
            def _():
                z_copy(z, k, True).wait_recv()
                own[z, 0, rows(k), :] = low(total + z_in[1, z, rows(k), :].astype(jnp.float32))

            @pl.when(d == 0)
            def _():
                own[z, 0, rows(k), :] = low(total)

            z_copy(z, k, True).start()

        @pl.when(z == d)
        def _():
            out_ref[rows(k), :] = total

    for k in range(2):

        @pl.when(d < 3)
        def _():
            z_copy(d, k, False).wait_recv()
            out_ref[rows(k), :] += z_in[0, d, rows(k), :].astype(jnp.float32)

        @pl.when(d > 0)
        def _():
            z_copy(d, k, True).wait_recv()
            out_ref[rows(k), :] += z_in[1, d, rows(k), :].astype(jnp.float32)

    for z in range(4):
        for k in range(2):
            core_copy(z, k, 0).wait_send()
            core_copy(z, k, 1).wait_send()
            y_copy(z, k).wait_send()

            @pl.when(z < d)
            def _():
                z_copy(z, k, False).wait_send()

            @pl.when(z > d)
            def _():
                z_copy(z, k, True).wait_send()

    carried.finish()
    for side in spread:
        side.finish()


def combine(pick_t, y, collective_id, carry, spread=()):
    rows, width = pick_t.shape[1], y.shape[2]
    anywhere = pl.BlockSpec(memory_space=pl.ANY)
    near = pl.BlockSpec(memory_space=pltpu.VMEM)
    sections = tuple(to for to, _ in carry)
    arrays = [array for _, array in carry]

    arrays = arrays + list(spread)

    def kernel(*refs):
        combine_kernel(sections, len(spread), *refs)

    def blocks(*lead):
        return pltpu.VMEM(lead + (rows, width), jnp.bfloat16)

    return pl.pallas_call(
        kernel,
        out_shape=[jax.ShapeDtypeStruct((rows, width), jnp.float32)]
        + [jax.ShapeDtypeStruct(array.shape, array.dtype) for array in arrays],
        in_specs=[near, anywhere] + [anywhere] * len(arrays),
        out_specs=[near] + [anywhere] * len(arrays),
        scratch_shapes=[
            pltpu.VMEM(y.shape, jnp.bfloat16),
            blocks(4, 2),
            blocks(4, 2),
            blocks(4, 2),
            blocks(4),
            blocks(2, 4),
            DMA((16,)),
            DMA((4, 2)),
            DMA((2, 4, 2)),
            DMA((4, 2)),
            DMA((4, 2)),
            DMA((4, 2, 2)),
            DMA((4, 2, 2)),
            DMA((max(1, len(arrays)), 2)),
            DMA((4, 2)),
        ],
        compiler_params=pltpu.CompilerParams(
            collective_id=collective_id, has_side_effects=True, vmem_limit_bytes=60 << 20
        ),
        cost_estimate=cost(),
        name="combine",
    )(pick_t, y, *arrays)


def expert_backward_kernel(
    layer, sections, x_ref, pick_ref, gate_in, up_in, slot_gate_in,
    wg_own, wu_own, wd_own, wg_other, wu_other, wd_other, *refs
):
    kept = len(sections)
    sources, refs = refs[:kept], refs[kept:]
    rows_out, gate_out, up_out, term_out, y_out, *refs = refs
    targets, refs = refs[:kept], refs[kept:]
    wg, wu, wd, rows, gate, up, slot_gate, y, wsem, isem, osem, carry_sem, *gather = refs
    carried = Carried(sections, sources, targets, carry_sem)
    count = wg.shape[0]
    ready = pick_weights(
        (wg_own, wu_own, wd_own), (wg_other, wu_other, wd_other), (wg, wu, wd), wsem, layer
    )
    land = gather[0]
    d = lax.axis_index("dp")
    ins = [
        pltpu.make_async_copy(src, held, isem.at[k])
        for k, (src, held) in enumerate(((gate_in, gate), (up_in, up), (slot_gate_in, slot_gate)))
    ]
    for copy in ins:
        copy.start()

    def outs(z):
        part = pl.ds(z * 4 * CAP, 4 * CAP)
        return [
            pltpu.make_async_copy(held.at[:, part], out.at[:, part], osem.at[k, z])
            for k, (held, out) in enumerate(
                ((rows, rows_out), (gate, gate_out), (up, up_out), (slot_gate, term_out))
            )
        ] + [pltpu.make_async_copy(y.at[pl.ds(z * 4, 4)], y_out.at[pl.ds(z * 4, 4)], osem.at[4, z])]

    def compute(z):
        @pl.when(z == d)
        def _():
            for k in range(3):
                ready(k)
            for copy in ins:
                copy.wait()

        for q in range(4):
            b = z * 4 + q
            picked = low(dot(pick_ref[b], land[b]))
            for j in range(count):
                rows[j, pl.ds(b * CAP, CAP), :] = picked[j * CAP : (j + 1) * CAP]
        part = pl.ds(z * 4 * CAP, 4 * CAP)

        @pl.loop(0, count)
        def _(j):
            plain = dot_t(rows[j, part, :], wd[j])
            g = gate[j, part, :].astype(jnp.float32)
            u = up[j, part, :].astype(jnp.float32)
            sigmoid = jax.nn.sigmoid(g)
            active = g * sigmoid
            term = jnp.sum(plain * (active * u), axis=1, keepdims=True)
            grad = plain * slot_gate[j, part, :][:, :1]
            dg = low(grad * u * sigmoid * (1.0 + g * (1.0 - sigmoid)))
            du = low(grad * active)
            slot_gate[j, part, :] = jnp.broadcast_to(term, (4 * CAP, 128))
            gate[j, part, :] = dg
            up[j, part, :] = du
            result = low(dot_t(dg, wg[j]) + dot_t(du, wu[j]))
            for q in range(4):
                y[z * 4 + q, pl.ds(j * CAP, CAP), :] = result[q * CAP : (q + 1) * CAP]

        for copy in outs(z):
            copy.start()

    gather_blocks(x_ref, gather, compute, carried)
    carried.finish()
    for z in range(4):
        for copy in outs(z):
            copy.wait()


def expert_backward(layer, x, pick, gate, up, slot_gate, own, other, collective_id, carry):
    count, width, units = own[0].shape
    rows = x.shape[0]
    slots = 16 * CAP
    bf = jnp.bfloat16
    anywhere = pl.BlockSpec(memory_space=pl.ANY)
    near = pl.BlockSpec(memory_space=pltpu.VMEM)
    results = [
        ((count, slots, width), bf),
        ((count, slots, units), bf),
        ((count, slots, units), bf),
        ((count, slots, 128), jnp.float32),
        ((16, count * CAP, width), bf),
    ]
    sections = tuple(to for to, _ in carry)
    arrays = [array for _, array in carry]

    def kernel(*refs):
        expert_backward_kernel(layer, sections, *refs)

    return pl.pallas_call(
        kernel,
        out_shape=[jax.ShapeDtypeStruct(*result) for result in results]
        + [jax.ShapeDtypeStruct(array.shape, array.dtype) for array in arrays],
        in_specs=[anywhere, near] + [anywhere] * (9 + len(arrays)),
        out_specs=[anywhere] * (5 + len(arrays)),
        scratch_shapes=[pltpu.VMEM(weight.shape, bf) for weight in own]
        + [pltpu.VMEM(*result) for result in results]
        + [DMA((3,)), DMA((3,)), DMA((5, 4)), DMA((max(1, len(arrays)), 2))]
        + gather_scratch(rows, width),
        compiler_params=pltpu.CompilerParams(
            collective_id=collective_id, has_side_effects=True, vmem_limit_bytes=60 << 20
        ),
        cost_estimate=cost(),
        name="expert_backward",
    )(x, pick, gate, up, slot_gate, *own, *other, *arrays)


def rope(x, cos_table, sin_table):
    lane = lax.broadcasted_iota(jnp.int32, x.shape, 1)
    turned = jnp.where(lane % HEAD_DIM < HEAD_DIM // 2, pltpu.roll(x, 128 - HEAD_DIM // 2, 1), pltpu.roll(x, HEAD_DIM // 2, 1))
    return x * cos_table + turned * sin_table


def seq_greet(s, section, spread=False):
    barrier = pltpu.get_barrier_semaphore()
    devices = [dict(seq=s ^ 1), dict(seq=s ^ 2), dict(section=1 - section)]
    if spread:
        devices.append(dict(seq=s ^ 3))
    for device in devices:
        pl.semaphore_signal(barrier, inc=1, device_id=device, device_id_type=MESH)
    pl.semaphore_wait(barrier, len(devices))


def seq_scratch(rows, width):
    return [
        pltpu.VMEM((4, rows, width), jnp.bfloat16),
        pltpu.VMEM((2, rows, width), jnp.bfloat16),
        pltpu.VMEM((2, rows, width), jnp.bfloat16),
        pltpu.VMEM((rows, width), jnp.bfloat16),
        pltpu.VMEM((rows, width), jnp.bfloat16),
        DMA(()),
        DMA((4, 2)),
        DMA((3, 2)),
    ]


class Line:
    def __init__(self, scratch):
        self.land, self.sent, self.core_in, self.y_sent, self.y_in, self.lsem, self.ag, self.rs = scratch
        self.s = lax.axis_index("seq")

    def hop(self, src, dst, sems, k, flip):
        return remote(src, dst, sems.at[k, 0], sems.at[k, 1], seq=self.s ^ flip)

    def gather(self, x_ref, use):
        s, land = self.s, self.land
        own = pltpu.make_async_copy(x_ref, land.at[s], self.lsem)
        own.start()
        over = self.hop(x_ref, land.at[s], self.ag, 0, 2)
        beside = self.hop(x_ref, land.at[s], self.ag, 1, 1)
        over.start()
        beside.start()
        own.wait()
        use(s)
        beside.wait_recv()
        use(s ^ 1)
        over.wait_recv()
        further = self.hop(land.at[s ^ 2], land.at[s ^ 2], self.ag, 2, 1)
        further.start()
        use(s ^ 2)
        further.wait_recv()
        use(s ^ 3)
        over.wait_send()
        beside.wait_send()
        further.wait_send()

    def hand_over(self, t, partial, out_ref):
        relation = t ^ self.s

        @pl.when(relation == 3)
        def _():
            self.sent[0] = low(partial[...])
            self.hop(self.sent.at[0], self.core_in.at[0], self.rs, 0, 1).start()

        @pl.when(relation == 2)
        def _():
            self.hop(self.sent.at[0], self.core_in.at[0], self.rs, 0, 1).wait_recv()
            self.y_sent[...] = low(partial[...] + self.core_in[0].astype(jnp.float32))
            self.hop(self.y_sent, self.y_in, self.rs, 1, 2).start()

        @pl.when(relation == 1)
        def _():
            self.sent[1] = low(partial[...])
            self.hop(self.sent.at[1], self.core_in.at[1], self.rs, 2, 1).start()

        @pl.when(relation == 0)
        def _():
            out_ref[...] = partial[...]

    def finish(self, out_ref):
        self.hop(self.sent.at[1], self.core_in.at[1], self.rs, 2, 1).wait()
        out_ref[...] += self.core_in[1].astype(jnp.float32)
        self.hop(self.y_sent, self.y_in, self.rs, 1, 2).wait()
        out_ref[...] += self.y_in[...].astype(jnp.float32)
        self.hop(self.sent.at[0], self.core_in.at[0], self.rs, 0, 1).wait_send()


def attention_forward_kernel(sections, x_ref, qkv_ref, wo_ref, cos_ref, sin_ref, *refs):
    kept = len(sections)
    sources, refs = refs[:kept], refs[kept:]
    out_ref, all_out, heads_out, lse_out, ot_out, *refs = refs
    targets, refs = refs[:kept], refs[kept:]
    wqkv, wo, heads, lse, ot, partial, wsem, osem, carry_sem, *line = refs
    line = Line(line)
    carried = Carried(sections, sources, targets, carry_sem)
    s = line.s
    rows = out_ref.shape[0]
    kv = heads.shape[0] // (GROUP + 2)
    queries = GROUP * kv
    loads = [pltpu.make_async_copy(qkv_ref, wqkv, wsem.at[0]), pltpu.make_async_copy(wo_ref, wo, wsem.at[1])]
    for load in loads:
        load.start()
    seq_greet(s, carried.section)
    carried.start()
    lse[...] = jnp.zeros_like(lse)

    def project(t):
        part = pl.ds(pl.multiple_of(t * rows, rows), rows)

        @pl.when(t == s)
        def _():
            loads[0].wait()

        qkv = low(dot(line.land[t], wqkv[...]))
        for chunk in range((queries + kv) // 2):
            x = qkv[:, chunk * 128 : (chunk + 1) * 128].astype(jnp.float32)
            x = low(rope(x, cos_ref[part, :], sin_ref[part, :]))
            heads[2 * chunk, part, :] = x[:, :HEAD_DIM]
            heads[2 * chunk + 1, part, :] = x[:, HEAD_DIM:]
        for j in range(kv):
            begin = (queries + kv + j) * HEAD_DIM
            heads[queries + kv + j, part, :] = qkv[:, begin : begin + HEAD_DIM]

    line.gather(x_ref, project)
    saves = [pltpu.make_async_copy(line.land, all_out, osem.at[0]), pltpu.make_async_copy(heads, heads_out, osem.at[1])]
    for save in saves:
        save.start()
    loads[1].wait()

    def attend(block):
        keys = (block + 1) * rows
        columns = slice(block * rows, (block + 1) * rows)

        @pl.loop(0, queries)
        def _(h):
            j = h // GROUP
            scores = dot_t(heads[queries + j, :keys, :], heads[h, columns, :]) * 0.125
            key_at = lax.broadcasted_iota(jnp.int32, scores.shape, 0)
            query_at = lax.broadcasted_iota(jnp.int32, scores.shape, 1) + block * rows
            scores = jnp.where(key_at <= query_at, scores, -jnp.inf)
            peak = jnp.max(scores, axis=0, keepdims=True)
            power = jnp.exp(scores - peak)
            total = jnp.sum(power, axis=0, keepdims=True)
            attended = t_dot(heads[queries + kv + j, :keys, :], low(power / total))
            ot[pl.ds(pl.multiple_of(h * HEAD_DIM, HEAD_DIM), HEAD_DIM), columns] = low(attended)
            lse[pl.ds(h, 1), columns] = peak + jnp.log(total)

        partial[...] = t_dot(ot[:, columns], wo[...])

    @pl.loop(0, 4)
    def _(i):
        t = s ^ (3 - i)
        for block in range(4):

            @pl.when(t == block)
            def _():
                attend(block)

        line.hand_over(t, partial, out_ref)

    saves += [pltpu.make_async_copy(lse, lse_out, osem.at[2]), pltpu.make_async_copy(ot, ot_out, osem.at[3])]
    for save in saves[2:]:
        save.start()
    line.finish(out_ref)
    carried.finish()
    for save in saves:
        save.wait()


def attention_forward_call(x, qkv_w, out_w, tables, collective_id, carry):
    rows, width = x.shape
    local_heads = qkv_w.shape[1] // HEAD_DIM
    bf, f32 = jnp.bfloat16, jnp.float32
    anywhere = pl.BlockSpec(memory_space=pl.ANY)
    near = pl.BlockSpec(memory_space=pltpu.VMEM)
    sections = tuple(to for to, _ in carry)
    arrays = [array for _, array in carry]
    results = [
        ((rows, width), f32),
        ((4, rows, width), bf),
        ((local_heads, 4 * rows, HEAD_DIM), bf),
        ((8, 4 * rows), f32),
        ((out_w.shape[0], 4 * rows), bf),
    ]

    def kernel(*refs):
        attention_forward_kernel(sections, *refs)

    return pl.pallas_call(
        kernel,
        out_shape=[jax.ShapeDtypeStruct(*result) for result in results]
        + [jax.ShapeDtypeStruct(array.shape, array.dtype) for array in arrays],
        in_specs=[anywhere] * 3 + [near] * 2 + [anywhere] * len(arrays),
        out_specs=[near] + [anywhere] * (4 + len(arrays)),
        scratch_shapes=[
            pltpu.VMEM(qkv_w.shape, bf),
            pltpu.VMEM(out_w.shape, bf),
            pltpu.VMEM(*results[2]),
            pltpu.VMEM(*results[3]),
            pltpu.VMEM(*results[4]),
            pltpu.VMEM((rows, width), f32),
            DMA((2,)),
            DMA((4,)),
            DMA((max(1, len(arrays)), 2)),
        ]
        + seq_scratch(rows, width),
        compiler_params=pltpu.CompilerParams(
            collective_id=collective_id, has_side_effects=True, vmem_limit_bytes=60 << 20
        ),
        cost_estimate=cost(),
        name="attention_forward",
    )(x, qkv_w, out_w, *tables, *arrays)


def attention_backward_kernel(
    sections, spreads, x_ref, qkv_ref, wo_ref, cos_ref, sin_ref, heads_in, lse_ref, *refs
):
    kept = len(sections)
    sources, refs = refs[:kept], refs[kept:]
    spread_sources, refs = refs[:spreads], refs[spreads:]
    out_ref, all_out, grads_out, *refs = refs
    targets, refs = refs[:kept], refs[kept:]
    spread_targets, refs = refs[:spreads], refs[spreads:]
    wqkv, wo, heads, douts, dk, dv, dqt, grads, partial, wsem, osem, carry_sem, spread_sem, *line = refs
    spread = [Spread(a, b, spread_sem) for a, b in zip(spread_sources, spread_targets)]
    line = Line(line)
    carried = Carried(sections, sources, targets, carry_sem)
    s = line.s
    rows = out_ref.shape[0]
    kv = heads.shape[0] // (GROUP + 2)
    queries = GROUP * kv
    loads = [
        pltpu.make_async_copy(wo_ref, wo, wsem.at[0]),
        pltpu.make_async_copy(qkv_ref, wqkv, wsem.at[1]),
        pltpu.make_async_copy(heads_in, heads, wsem.at[2]),
    ]
    for load in loads:
        load.start()
    seq_greet(s, carried.section, spreads > 0)
    carried.start()
    dk[...] = jnp.zeros_like(dk)
    dv[...] = jnp.zeros_like(dv)

    def project(t):
        part = pl.ds(pl.multiple_of(t * rows, rows), rows)

        @pl.when(t == s)
        def _():
            loads[0].wait()

        grad = low(dot_t(line.land[t], wo[...]))
        for h in range(queries):
            douts[h, part, :] = grad[:, h * HEAD_DIM : (h + 1) * HEAD_DIM]

    line.gather(x_ref, project)
    saves = [pltpu.make_async_copy(line.land, all_out, osem.at[0])]
    saves[0].start()
    for side in spread:
        side.start()
    loads[1].wait()
    loads[2].wait()

    for block in (3, 2, 1, 0):
        keys = (block + 1) * rows
        part = slice(block * rows, (block + 1) * rows)

        @pl.loop(0, queries)
        def _(h):
            j = h // GROUP
            key = heads[queries + j, :keys, :]
            query = heads[h, part, :]
            grad = douts[h, part, :]
            scores = dot_t(key, query) * 0.125
            key_at = lax.broadcasted_iota(jnp.int32, scores.shape, 0)
            query_at = lax.broadcasted_iota(jnp.int32, scores.shape, 1) + block * rows
            scores = jnp.where(key_at <= query_at, scores, -jnp.inf)
            probs = jnp.exp(scores - lse_ref[pl.ds(h, 1), part])
            dprobs = dot_t(heads[queries + kv + j, :keys, :], grad)
            mean = jnp.sum(probs * dprobs, axis=0, keepdims=True)
            dscores = low(probs * (dprobs - mean))
            dk[j, :keys, :] += dot(dscores, query) * 0.125
            dv[j, :keys, :] += dot(low(probs), grad)
            dqt[pl.ds(pl.multiple_of(h * HEAD_DIM, HEAD_DIM), HEAD_DIM), :] = t_dot(key, dscores) * 0.125

        cos_part, sin_part = cos_ref[part, :], -sin_ref[part, :]
        dq = dqt[...].T
        for chunk in range(queries // 2):
            lanes = slice(chunk * 128, (chunk + 1) * 128)
            grads[part, lanes] = low(rope(dq[:, lanes], cos_part, sin_part))
        for pair in range(kv // 2):
            both = jnp.concatenate([dk[2 * pair, part, :], dk[2 * pair + 1, part, :]], axis=1)
            begin = queries * HEAD_DIM + pair * 128
            grads[part, begin : begin + 128] = low(rope(both, cos_part, sin_part))
            both = jnp.concatenate([dv[2 * pair, part, :], dv[2 * pair + 1, part, :]], axis=1)
            begin = (queries + kv) * HEAD_DIM + pair * 128
            grads[part, begin : begin + 128] = low(both)
        partial[...] = dot_t(grads[part, :], wqkv[...])
        line.hand_over(block, partial, out_ref)

    saves.append(pltpu.make_async_copy(grads, grads_out, osem.at[1]))
    saves[1].start()
    line.finish(out_ref)
    carried.finish()
    for side in spread:
        side.finish()
    for save in saves:
        save.wait()


def attention_backward_call(x, qkv_w, out_w, tables, heads, lse, collective_id, carry, spread=()):
    rows, width = x.shape
    bf, f32 = jnp.bfloat16, jnp.float32
    anywhere = pl.BlockSpec(memory_space=pl.ANY)
    near = pl.BlockSpec(memory_space=pltpu.VMEM)
    sections = tuple(to for to, _ in carry)
    arrays = [array for _, array in carry]
    results = [((rows, width), f32), ((4, rows, width), bf), ((4 * rows, qkv_w.shape[1]), bf)]
    kv = heads.shape[0] // (GROUP + 2)
    queries = GROUP * kv

    arrays = arrays + list(spread)

    def kernel(*refs):
        attention_backward_kernel(sections, len(spread), *refs)

    return pl.pallas_call(
        kernel,
        out_shape=[jax.ShapeDtypeStruct(*result) for result in results]
        + [jax.ShapeDtypeStruct(array.shape, array.dtype) for array in arrays],
        in_specs=[anywhere] * 3 + [near] * 2 + [anywhere, near] + [anywhere] * len(arrays),
        out_specs=[near] + [anywhere] * (2 + len(arrays)),
        scratch_shapes=[
            pltpu.VMEM(qkv_w.shape, bf),
            pltpu.VMEM(out_w.shape, bf),
            pltpu.VMEM(heads.shape, bf),
            pltpu.VMEM((queries, 4 * rows, HEAD_DIM), bf),
            pltpu.VMEM((kv, 4 * rows, HEAD_DIM), f32),
            pltpu.VMEM((kv, 4 * rows, HEAD_DIM), f32),
            pltpu.VMEM((queries * HEAD_DIM, rows), f32),
            pltpu.VMEM(*results[2]),
            pltpu.VMEM((rows, width), f32),
            DMA((3,)),
            DMA((2,)),
            DMA((max(1, len(arrays)), 2)),
            DMA((4, 2)),
        ]
        + seq_scratch(rows, width),
        compiler_params=pltpu.CompilerParams(
            collective_id=collective_id, has_side_effects=True, vmem_limit_bytes=60 << 20
        ),
        cost_estimate=cost(),
        name="attention_backward",
    )(x, qkv_w, out_w, *tables, heads, lse, *arrays)


def last_kernel(sections, down_ref, cols_ref, cols_other, out_ref, out_other, *refs):
    kept = len(sections)
    sources, refs = refs[:kept], refs[kept:]
    down_out, cols_out, rows_out, *refs = refs
    targets, refs = refs[:kept], refs[kept:]
    cols_in, cols, out_in, out_sum, down_sem, cols_sem, row_sem, swap_sem, carry_sem = refs
    d, s, section = lax.axis_index("dp"), lax.axis_index("seq"), lax.axis_index("section")
    barrier = pltpu.get_barrier_semaphore()

    def signal(**device):
        pl.semaphore_signal(barrier, inc=1, device_id=device, device_id_type=MESH)

    for flip in (1, 2, 3):
        signal(seq=s ^ flip)
    signal(section=1 - section)

    @pl.when(d != s)
    def _():
        signal(dp=s, seq=d)
        pl.semaphore_wait(barrier, 5)

    @pl.when(d == s)
    def _():
        pl.semaphore_wait(barrier, 4)

    swaps = Carried((None, None), (cols_other, out_other), (cols_in, out_in), swap_sem)
    carried = Carried(sections, sources, targets, carry_sem)
    down = Spread(down_ref, down_out, down_sem)
    swaps.start()
    down.start()
    swaps.finish()
    carried.start()
    cols[...] = low(cols_ref[...].astype(jnp.float32) + cols_in[...].astype(jnp.float32))
    out_sum[...] = low(out_ref[...].astype(jnp.float32) + out_in[...].astype(jnp.float32))
    spread = Spread(cols, cols_out, cols_sem)
    spread.start()
    rows = remote(out_sum, rows_out, row_sem.at[0], row_sem.at[1], dp=s, seq=d)

    @pl.when(d != s)
    def _():
        rows.start()
        rows.wait()

    @pl.when(d == s)
    def _():
        rows_out[...] = out_sum[...]

    spread.finish()
    down.finish()
    carried.finish()


def last_exchange(down, cols, cols_other, out, out_other, collective_id, carry):
    bf = jnp.bfloat16
    anywhere = pl.BlockSpec(memory_space=pl.ANY)
    near = pl.BlockSpec(memory_space=pltpu.VMEM)
    sections = tuple(to for to, _ in carry)
    arrays = [array for _, array in carry]

    def kernel(*refs):
        last_kernel(sections, *refs)

    return pl.pallas_call(
        kernel,
        out_shape=[
            jax.ShapeDtypeStruct(array.shape, array.dtype) for array in (down, cols, out, *arrays)
        ],
        in_specs=[anywhere, near, anywhere, near, anywhere] + [anywhere] * len(arrays),
        out_specs=[anywhere, near, near] + [anywhere] * len(arrays),
        scratch_shapes=[
            pltpu.VMEM(cols.shape, bf),
            pltpu.VMEM(cols.shape, bf),
            pltpu.VMEM(out.shape, bf),
            pltpu.VMEM(out.shape, bf),
            DMA((4, 2)),
            DMA((4, 2)),
            DMA((2,)),
            DMA((2, 2)),
            DMA((max(1, len(arrays)), 2)),
        ],
        compiler_params=pltpu.CompilerParams(
            collective_id=collective_id, has_side_effects=True, vmem_limit_bytes=60 << 20
        ),
        name="last_exchange",
    )(down, cols, cols_other, out, out_other, *arrays)


def wide_tables(length):
    cos_table, sin_table = rotary_tables(length)
    cos_table, sin_table = cos_table[:, 0], sin_table[:, 0]
    return (
        jnp.concatenate([cos_table] * 4, axis=1),
        jnp.concatenate([-sin_table, sin_table] * 2, axis=1),
    )


def token_choice(route):
    return route[..., None] == jnp.arange(EXPERTS, dtype=jnp.int32)


def routing(route_all, first_expert, count):
    chosen = jnp.any(token_choice(route_all), axis=2)
    blocks, rows = chosen.shape[:2]
    mine = lax.dynamic_slice_in_dim(chosen, first_expert, count, axis=2)
    chosen = low(jnp.transpose(chosen, (0, 2, 1)))
    earlier = jnp.tril(jnp.ones((rows, rows), jnp.bfloat16), -1)
    place = jnp.einsum(
        "ts,bsj->bjt", earlier, mine.astype(jnp.bfloat16), preferred_element_type=jnp.float32
    ).astype(jnp.int32)
    mine = jnp.transpose(mine, (0, 2, 1))
    place = jnp.where(mine, place, -1)
    slots = jnp.arange(CAP, dtype=jnp.int32)
    pick = low(place[:, :, None, :] == slots[None, None, :, None]).reshape(blocks, -1, rows)
    return chosen, pick, jnp.transpose(pick, (0, 2, 1))


def choose(pick, rows, count):
    picked = jnp.einsum("bct,btd->bcd", pick, rows, preferred_element_type=jnp.float32)
    blocks = pick.shape[0]
    picked = low(picked).reshape(blocks, count, CAP, -1)
    return jnp.transpose(picked, (1, 0, 2, 3)).reshape(count, blocks * CAP, -1)


def give_back(pick_t, slot_rows):
    blocks, rows = pick_t.shape[:2]
    count, _, width = slot_rows.shape
    slot_rows = jnp.transpose(slot_rows.reshape(count, blocks, CAP, width), (1, 0, 2, 3))
    slot_rows = slot_rows.reshape(blocks, count * CAP, width)
    total = jnp.einsum("btc,bcd->btd", pick_t, slot_rows, preferred_element_type=jnp.float32)
    return low(total).reshape(-1, width)


def each_dot(form, a, b):
    return jnp.einsum(form, a, b, preferred_element_type=jnp.float32)


def after(value, *others):
    return lax.optimization_barrier((value, *others))[0]


def has_kernels():
    return lax.axis_size("dp") == 4 and lax.axis_size("seq") == 4


def forward_layer(number, layer_in, picking, weights, experts, *carry):
    attn_scale, ffn_scale, qkv_w, out_w, router_w = weights
    chosen, pick, pick_t, first_expert = picking
    own, other = experts
    count = own[0].shape[0]
    blocks, _, rows = chosen.shape
    received = []
    normed_input = low(rms_norm(layer_in, attn_scale))
    if has_kernels():
        branch, normed_all, heads, log_total, mixed_t, *received = attention_forward_call(
            normed_input, qkv_w, out_w, wide_tables(4 * layer_in.shape[0]), 9 + number, carry
        )
        attention_state = (normed_all.reshape(-1, layer_in.shape[1]), mixed_t, heads, log_total)
    else:
        received = [swap(array) if to is None else pass_to(array, to) for to, array in carry]
        normed_all = lax.all_gather(normed_input, "seq", axis=0, tiled=True)
        qkv = low(dot(normed_all, qkv_w))
        kv_width = KV_HEADS * HEAD_DIM // lax.axis_size("seq")
        q_width = GROUP * kv_width
        mixed, log_total, q_rot, k_rot, v_heads = attention_forward(
            qkv[:, :q_width], qkv[:, q_width : q_width + kv_width], qkv[:, q_width + kv_width :]
        )
        branch = lax.psum_scatter(low(dot(mixed, out_w)), "seq", scatter_dimension=0, tiled=True)
        attention_state = (normed_all, mixed.T, (q_rot, k_rot, v_heads), log_total)
    after_update = layer_in + branch.astype(jnp.float32)
    normed_ffn = low(rms_norm(after_update, ffn_scale))
    own_block = lax.axis_index("dp") * lax.axis_size("seq") + lax.axis_index("seq")
    own_chosen = lax.dynamic_index_in_dim(chosen, own_block, 0, keepdims=False)
    own_logits = jnp.where(own_chosen > 0, dot_t(router_w, normed_ffn), -jnp.inf)
    own_gates = jax.nn.softmax(own_logits, axis=0)
    if number == 0:
        other = other + (received[0],)
    mine = (
        jnp.arange(EXPERTS)[None, None, :] == first_expert + jnp.arange(count)[:, None, None]
    ).astype(jnp.float32)
    if has_kernels():
        *expert_state, slot_out = expert_forward(
            number, normed_ffn, pick, chosen, router_w, mine, own, other, 1 + number
        )
        if number == 0:
            *expert_state, slot_out, other_down = (*expert_state, slot_out)
            other = other[:2] + (other_down,)
    else:
        if number == 0:
            other = other[:2] + (swap(own[2]),)
        gate_w, up_w, down_w = by_layer(number, own, other)
        ffn_all = lax.all_gather(normed_ffn, TOKENS, axis=0, tiled=True)
        logits = dot_t(ffn_all, router_w).reshape(blocks, rows, EXPERTS)
        used = jnp.transpose(chosen, (0, 2, 1)) > 0
        gates = jax.nn.softmax(jnp.where(used, logits, -jnp.inf), axis=-1)
        slot_rows = choose(pick, ffn_all.reshape(blocks, rows, -1), count)
        mine_gates = jnp.einsum("bte,jxe->bjt", gates, mine, precision=lax.Precision.HIGHEST)
        slot_gates = jnp.sum(
            pick.reshape(blocks, count, CAP, rows).astype(jnp.float32) * mine_gates[:, :, None, :],
            axis=3,
        )
        slot_gates = jnp.transpose(slot_gates, (1, 0, 2)).reshape(count, -1, 1)
        gate_pre = each_dot("ecd,edf->ecf", slot_rows, gate_w)
        up_pre = each_dot("ecd,edf->ecf", slot_rows, up_w)
        scaled = low(slot_gates * jax.nn.silu(gate_pre) * up_pre)
        slot_out = low(each_dot("ecf,efd->ecd", scaled, down_w))
        expert_state = (slot_rows, gate_pre, up_pre, scaled, slot_gates)
    saved = (
        layer_in,
        attention_state,
        after_update,
        normed_ffn,
        own_gates,
        expert_state,
    )
    return (after_update, slot_out, saved, (own, other), received)


def token_sums(pick_t, slot_out, collective_id, *carry, spread=()):
    if has_kernels():
        sums, *received = combine(pick_t, slot_out, collective_id, carry, spread)
        return sums, received
    sums = give_back(pick_t, slot_out).astype(jnp.float32)
    sums = lax.psum_scatter(sums, TOKENS, scatter_dimension=0, tiled=True)
    received = [pass_to(array, to) for to, array in carry]
    return sums, received + [spread_rows(array) for array in spread]


def spread_rows(parts):
    return lax.all_to_all(parts, "seq", split_axis=0, concat_axis=0, tiled=True)


def expert_gradients(number, layer_grad, saved, picking, experts, *carry):
    chosen, pick, pick_t, first_expert = picking
    own, other = experts
    count = own[0].shape[0]
    blocks, _, rows = chosen.shape
    slot_rows, gate_pre, up_pre, scaled, slot_gates = saved[-1]
    if has_kernels():
        slot_grads, gate_low, up_low, gate_term, slot_out, *received = expert_backward(
            number, low(layer_grad), pick, gate_pre, up_pre, slot_gates, own, other, 4 + number, carry
        )
        gate_term = gate_term[:, :, :1]
    else:
        gate_w, up_w, down_w = by_layer(number, own, other)
        grad_all = lax.all_gather(low(layer_grad), TOKENS, axis=0, tiled=True)
        slot_grads = choose(pick, grad_all.reshape(blocks, rows, -1), count)
        plain_grad = each_dot("ecd,efd->ecf", slot_grads, down_w)
        sigmoid = jax.nn.sigmoid(gate_pre)
        activated = gate_pre * sigmoid
        gate_term = jnp.sum(plain_grad * (activated * up_pre), axis=2, keepdims=True)
        hidden_grad = slot_gates * plain_grad
        gate_low = low(hidden_grad * up_pre * sigmoid * (1.0 + gate_pre * (1.0 - sigmoid)))
        up_low = low(hidden_grad * activated)
        slot_out = low(
            each_dot("ecf,edf->ecd", gate_low, gate_w) + each_dot("ecf,edf->ecd", up_low, up_w)
        )
        received = [pass_to(array, to) for to, array in carry]
    expert_grads = (
        low(each_dot("ecd,ecf->edf", slot_rows, gate_low)),
        low(each_dot("ecd,ecf->edf", slot_rows, up_low)),
        low(each_dot("ecf,ecd->efd", scaled, slot_grads)),
    )
    slot_out, *expert_grads = lax.optimization_barrier((slot_out, *expert_grads))
    return slot_out, gate_term, expert_grads, received


def backward_layer(
    number, layer_grad, normed_grad, gate_term, saved, picking, weights, *carry, spread=()
):
    attn_scale, ffn_scale, qkv_w, out_w, router_w = weights
    chosen, pick, _, _ = picking
    (
        layer_in,
        (normed_all, mixed_t, heads, log_total),
        after_update,
        normed_ffn,
        own_gates,
        _,
    ) = saved
    blocks, _, rows = chosen.shape
    count = gate_term.shape[0]
    by_slot = jnp.transpose(gate_term.reshape(count, blocks, CAP), (1, 0, 2))
    gate_terms = jnp.sum(
        pick.reshape(blocks, count, CAP, rows).astype(jnp.float32) * by_slot[..., None], axis=2
    )
    gate_terms = lax.all_to_all(gate_terms, TOKENS, split_axis=0, concat_axis=0, tiled=True)
    gate_terms = jnp.sum(gate_terms.reshape(EXPERTS, -1, rows), axis=1)
    logit_grad = low(
        own_gates * (gate_terms - jnp.sum(own_gates * gate_terms, axis=0, keepdims=True))
    )
    router_grad = dot(logit_grad, normed_ffn)
    normed_grad = normed_grad + t_dot(logit_grad, router_w)
    after_part, ffn_gain_grad = jax.vjp(rms_norm, after_update, ffn_scale)[1](normed_grad)
    after_grad = after_part + layer_grad
    if has_kernels():
        normed_attn, branch_all, qkv_grad, *received = attention_backward_call(
            low(after_grad),
            qkv_w,
            out_w,
            wide_tables(4 * layer_in.shape[0]),
            heads,
            log_total,
            11 + number,
            carry,
            spread,
        )
        branch_all = branch_all.reshape(-1, layer_in.shape[1])
    else:
        branch_all = lax.all_gather(low(after_grad), "seq", axis=0, tiled=True)
        head_grad = low(dot_t(branch_all, out_w))
        qkv_grad = attention_backward(head_grad, *heads, log_total)
        normed_attn = low(dot_t(qkv_grad, qkv_w))
        normed_attn = lax.psum_scatter(normed_attn, "seq", scatter_dimension=0, tiled=True)
        received = [pass_to(array, to) for to, array in carry]
        received = received + [spread_rows(array) for array in spread]
    out_grad = dot(mixed_t, branch_all)
    qkv_weight_grad = t_dot(normed_all, qkv_grad)
    input_part, attn_gain_grad = jax.vjp(rms_norm, layer_in, attn_scale)[1](
        normed_attn.astype(jnp.float32)
    )
    small = [router_grad, attn_gain_grad[None], ffn_gain_grad[None]]
    small = jnp.concatenate(small + [jnp.zeros((128 - EXPERTS - 2, small[0].shape[1]))], axis=0)
    qkv_weight_grad = jnp.concatenate([low(qkv_weight_grad), low(small).T], axis=1)
    return (input_part + after_grad, (qkv_weight_grad, low(out_grad)), received)


def by_layer(number, own, other):
    is_own = lax.axis_index("section") == number
    return jax.tree.map(lambda mine, received: jnp.where(is_own, mine, received), own, other)


def body(
    hidden_in,
    out_grad,
    attn_gain,
    ffn_gain,
    query_matrix,
    key_matrix,
    value_matrix,
    output_matrix,
    router_matrix,
    w_gate,
    w_up,
    w_down,
    routes,
):
    section = lax.axis_index("section")
    dp, seq = lax.axis_size("dp"), lax.axis_size("seq")
    seq_index = lax.axis_index("seq")
    first = section == 0
    width = hidden_in.shape[3]
    depth = query_matrix.shape[1]

    layer_in = lax.dynamic_index_in_dim(hidden_in, section, 0, keepdims=False)[0]
    top_grad = lax.dynamic_index_in_dim(out_grad, section, 0, keepdims=False)[0]
    own_group = jnp.concatenate(
        [
            matrix[0].reshape(depth, seq, -1)
            for matrix in (query_matrix, key_matrix, value_matrix)
        ],
        axis=2,
    )
    own_group = jnp.transpose(own_group, (1, 0, 2))
    to_group = []
    for flat in range(dp * seq):
        to_group.append((flat, (flat % dp) * seq + flat // dp))
    from_group = [(target, source) for source, target in to_group]
    own_out = lax.ppermute(output_matrix[0], TOKENS, to_group)
    other_out = swap(own_out)
    local = w_gate.shape[1]
    hidden_units = w_gate.shape[3]
    if local >= seq:
        count, units = local // seq, hidden_units
        start, unit_start = seq_index * count, 0
    else:
        count, units = 1, hidden_units * local // seq
        start, unit_start = seq_index * local // seq, (seq_index % (seq // local)) * units
    first_expert = lax.axis_index("dp") * local + start
    own_experts = (
        lax.dynamic_slice(w_gate[0], (start, 0, unit_start), (count, width, units)),
        lax.dynamic_slice(w_up[0], (start, 0, unit_start), (count, width, units)),
        lax.dynamic_slice(w_down[0], (start, unit_start, 0), (count, units, width)),
    )
    small = jnp.concatenate([router_matrix[0].T, attn_gain, ffn_gain], axis=0)
    paths = routes[0, :, 0]
    if has_kernels():
        small = jnp.pad(small, ((0, -small.shape[0] % 16), (0, 256 - depth)))
        paths = low(jnp.transpose(paths, (0, 2, 1)).reshape(2 * TOP_K, -1))
        picks, picks_t, chosens, small, qkv_first, qkv_second, other_gate = prepare(
            jnp.concatenate([paths, small], axis=0),
            own_group,
            own_experts[0],
            count,
            hidden_in.shape[2],
            depth,
            13,
        )
        pickings = [(chosens[n], picks[n], picks_t[n], first_expert) for n in range(2)]
        qkv_second = lax.all_gather(
            qkv_second.reshape(seq * depth, -1), "dp", axis=0, tiled=True
        )
        qkv_layers = [qkv_first.reshape(width, -1), qkv_second]
    else:
        small = lax.all_gather(small, ("section", "dp", "seq"), axis=0, tiled=False)
        small = jnp.transpose(small.reshape(2, dp * seq, -1, depth), (0, 2, 1, 3))
        small = small.reshape(2, -1, width)
        paths = lax.all_gather(paths, ("section", "dp", "seq"), axis=0, tiled=False)
        paths = lax.dynamic_index_in_dim(paths, section, 1, keepdims=False)
        paths = paths.reshape(2, dp * seq, -1, TOP_K)
        pickings = [routing(paths[n], first_expert, count) + (first_expert,) for n in range(2)]
        other_gate = swap(own_experts[0])
        other_group = swap(own_group)
        qkv_layers = []
        for number in range(2):
            part = spread_rows(by_layer(number, own_group, other_group))
            part = part.reshape(seq * depth, -1)
            qkv_layers.append(lax.all_gather(part, "dp", axis=0, tiled=True))

    weights = []
    for number in range(2):
        out_w = lax.all_gather(
            by_layer(number, own_out, other_out), "dp", axis=0, tiled=True
        )
        weights.append(
            (
                small[number, EXPERTS].astype(jnp.float32),
                small[number, EXPERTS + 1].astype(jnp.float32),
                qkv_layers[number],
                out_w,
                small[number, :EXPERTS],
            )
        )

    def own_layer(pieces):
        return jnp.where(first, pieces[0], pieces[1])

    def both_micros(own, other):
        return jnp.stack([jnp.where(first, own, other), jnp.where(first, other, own)])[
            None, :, None
        ]

    def summed(own, other):
        return own_layer(own).astype(jnp.float32) + own_layer(other).astype(jnp.float32)

    def dp_sums(dense):
        return [lax.psum_scatter(part, "dp", scatter_dimension=0, tiled=True) for part in dense]

    def row_parts(piece, kind):
        if local >= seq:
            piece = piece.reshape(count, seq, piece.shape[1] // seq, -1)
            return jnp.transpose(piece, (1, 0, 2, 3))
        if kind < 2:
            return piece.reshape(seq, -1, units)
        piece = piece.reshape(-1, hidden_units // seq, width)
        share = seq // local
        parts = jnp.zeros((seq,) + piece.shape[1:], piece.dtype)
        return lax.dynamic_update_slice_in_dim(
            parts, piece, (seq_index % share) * piece.shape[0], axis=0
        )

    def whole_rows(parts, kind):
        parts = parts.astype(jnp.float32)
        if local < seq:
            parts = parts.reshape((local, seq // local) + parts.shape[1:])
            if kind < 2:
                parts = jnp.transpose(parts, (0, 2, 1, 3))
            else:
                parts = jnp.sum(parts, axis=1)
            return parts.reshape((local,) + parts.shape[1 : 2] + (-1,))[None]
        return parts.reshape((local,) + parts.shape[2:])[None]

    experts = (own_experts, (other_gate,))
    first_in = layer_in.astype(jnp.float32)
    updated, slot_out, first_saved, experts, _ = forward_layer(
        0, first_in, pickings[0], weights[0], experts, (None, own_experts[1])
    )
    sums, _ = token_sums(pickings[0][2], slot_out, 3)
    first_out = updated + sums
    second_updated, second_slots, second_saved, experts, (other_out,) = forward_layer(
        1, first_out, pickings[1], weights[1], experts, (0, first_out)
    )
    top_grad = top_grad.astype(jnp.float32)
    slot_out, gate_term, second_experts, _ = expert_gradients(
        1, top_grad, second_saved, pickings[1], experts
    )
    sums, (second_gate,) = token_sums(pickings[1][2], slot_out, 6, (1, second_experts[0]))
    middle_grad, second_dense, (second_up,) = backward_layer(
        1, top_grad, sums, gate_term, second_saved, pickings[1], weights[1], (1, second_experts[1])
    )
    slot_out, gate_term, first_experts, (second_down,) = expert_gradients(
        0, middle_grad, first_saved, pickings[0], experts, (1, second_experts[2])
    )
    sums, (first_gate, other_middle) = token_sums(
        pickings[0][2], slot_out, 7, (0, first_experts[0]), (1, middle_grad)
    )
    sums, *second_dense = lax.optimization_barrier((sums, *second_dense))
    second_dense = dp_sums(second_dense)
    gate_sum = low(summed((first_experts[0], second_experts[0]), (first_gate, second_gate)))
    bottom_grad, first_dense, (first_up, gate_rows) = backward_layer(
        0,
        middle_grad,
        sums,
        gate_term,
        first_saved,
        pickings[0],
        weights[0],
        (0, first_experts[1]),
        spread=(row_parts(gate_sum, 0),),
    )
    up_sum = low(summed((first_experts[1], second_experts[1]), (first_up, second_up)))
    second_slots, *first_dense, second_dense[0], second_dense[1] = lax.optimization_barrier(
        (second_slots, *first_dense, *second_dense)
    )
    first_dense = dp_sums(first_dense)
    sums, (first_down, up_rows) = token_sums(
        pickings[1][2],
        second_slots,
        8,
        (0, first_experts[2]),
        spread=(row_parts(up_sum, 1),),
    )
    sums, *first_dense = lax.optimization_barrier((sums, *first_dense))
    second_out = second_updated + sums
    down_sum = low(summed((first_experts[2], second_experts[2]), (first_down, second_down)))
    own_cols, own_rows = [own_layer((first_dense[k], second_dense[k])) for k in range(2)]
    other_cols, other_rows = [own_layer((second_dense[k], first_dense[k])) for k in range(2)]
    if has_kernels():
        down_rows, cols_sum, out_sum, other_second, other_bottom = last_exchange(
            row_parts(down_sum, 2),
            own_cols.reshape(seq, depth, -1),
            other_cols.reshape(seq, depth, -1),
            own_rows,
            other_rows,
            14,
            ((1, second_out), (0, bottom_grad)),
        )
    else:
        down_rows = spread_rows(row_parts(down_sum, 2))
        cols_sum = low(own_cols.astype(jnp.float32) + swap(other_cols).astype(jnp.float32))
        cols_sum = spread_rows(cols_sum.reshape(seq, depth, -1))
        out_sum = low(own_rows.astype(jnp.float32) + swap(other_rows).astype(jnp.float32))
        out_sum = lax.ppermute(out_sum, TOKENS, from_group)
        other_second, other_bottom = pass_to(second_out, 1), pass_to(bottom_grad, 0)
    expert_sums = [whole_rows(rows, k) for k, rows in enumerate((gate_rows, up_rows, down_rows))]
    layer_outs = both_micros(
        own_layer((first_out, second_out)), own_layer((other_out, other_second))
    )
    section_grads = both_micros(
        own_layer((bottom_grad, middle_grad)), own_layer((other_bottom, other_middle))
    )
    qkv_sum, out_sum = cols_sum.astype(jnp.float32), out_sum.astype(jnp.float32)
    kv_width = KV_HEADS * HEAD_DIM // seq
    q_width = GROUP * kv_width
    qkv_width = q_width + 2 * kv_width
    small_sum = jnp.sum(qkv_sum[:, :, qkv_width:], axis=0)

    def columns(begin, end):
        return jnp.transpose(qkv_sum[:, :, begin:end], (1, 0, 2)).reshape(depth, -1)[None]

    return (
        layer_outs,
        section_grads,
        small_sum[:, EXPERTS][None],
        small_sum[:, EXPERTS + 1][None],
        columns(0, q_width),
        columns(q_width, q_width + kv_width),
        columns(q_width + kv_width, qkv_width),
        out_sum[None],
        small_sum[:, :EXPERTS][None],
        *expert_sums,
    )


def solution(mesh):
    return jax.shard_map(
        body,
        mesh=mesh,
        in_specs=(
            P(None, "dp", "seq", None),
            P(None, "dp", "seq", None),
            P("section", ("dp", "seq")),
            P("section", ("dp", "seq")),
            P("section", ("dp", "seq"), None),
            P("section", ("dp", "seq"), None),
            P("section", ("dp", "seq"), None),
            P("section", ("dp", "seq"), None),
            P("section", ("dp", "seq"), None),
            P("section", "dp", None, None),
            P("section", "dp", None, None),
            P("section", "dp", None, None),
            P("section", None, "dp", "seq", None),
        ),
        out_specs=(
            P("section", None, "dp", "seq", None),
            P("section", None, "dp", "seq", None),
            P("section", ("dp", "seq")),
            P("section", ("dp", "seq")),
            P("section", ("dp", "seq"), None),
            P("section", ("dp", "seq"), None),
            P("section", ("dp", "seq"), None),
            P("section", ("dp", "seq"), None),
            P("section", ("dp", "seq"), None),
            P("section", "dp", "seq", None),
            P("section", "dp", "seq", None),
            P("section", "dp", "seq", None),
        ),
        check_vma=False,
    )
```

```python
import jax
import jax.numpy as jnp
from jax import lax
from jax.experimental import pallas as pl
from jax.experimental.pallas import tpu as pltpu
from jax.sharding import PartitionSpec as P

HEADS = 24
KV_HEADS = 8
HEAD_DIM = 64
TOP_K = 8
EXPERTS = 32
CAP = 80
GROUP = HEADS // KV_HEADS
TOKENS = ("dp", "seq")
MESH = pl.DeviceIdType.MESH
DMA = pltpu.SemaphoreType.DMA

epsilon = 1e-06


def dot(a, b):
    return jnp.dot(a, b, preferred_element_type=jnp.float32)


def dot_t(a, b):
    return lax.dot_general(a, b, (((1,), (1,)), ((), ())), preferred_element_type=jnp.float32)


def t_dot(a, b):
    return lax.dot_general(a, b, (((0,), (0,)), ((), ())), preferred_element_type=jnp.float32)


def low(v):
    return v.astype(jnp.bfloat16)


def swap(block):
    return lax.ppermute(block, "section", [(0, 1), (1, 0)])


def pass_to(block, section):
    return lax.ppermute(block, "section", [(1 - section, section)])


def rms_norm(values, norm_gain):
    return (
        values * lax.rsqrt(jnp.mean(values * values, axis=-1, keepdims=True) + epsilon) * norm_gain
    )


def rotary_tables(length):
    half_dim = HEAD_DIM // 2
    frequency = 10000.0 ** (-jnp.arange(half_dim, dtype=jnp.float32) * 2.0 / HEAD_DIM)
    angles = jnp.arange(length, dtype=jnp.float32)[:, None] * frequency[None, :]
    return (jnp.cos(angles)[:, None, :], jnp.sin(angles)[:, None, :])


def rotate(values, cos_table, sin_table):
    length = values.shape[0]
    split_heads = values.reshape(length, -1, HEAD_DIM)
    first_half = split_heads[..., : HEAD_DIM // 2]
    second_half = split_heads[..., HEAD_DIM // 2 :]
    turned = jnp.concatenate(
        [
            first_half * cos_table - second_half * sin_table,
            second_half * cos_table + first_half * sin_table,
        ],
        axis=-1,
    )
    return turned.reshape(length, -1)


def attention_forward(q_heads, k_heads, v_heads):
    length = q_heads.shape[0]
    local_kv = k_heads.shape[1] // HEAD_DIM
    cos_table, sin_table = rotary_tables(length)
    q_rot = low(rotate(q_heads.astype(jnp.float32), cos_table, sin_table)).reshape(
        length, local_kv, GROUP, HEAD_DIM
    )
    k_rot = low(rotate(k_heads.astype(jnp.float32), cos_table, sin_table)).reshape(
        length, local_kv, HEAD_DIM
    )
    values = v_heads.reshape(length, local_kv, HEAD_DIM)
    block_rows = min(512, length)
    outputs = []
    totals_list = []
    for first_row in range(0, length, block_rows):
        key_end = first_row + block_rows
        scores = (
            jnp.einsum(
                "qhgd,khd->hgqk",
                q_rot[first_row:key_end],
                k_rot[:key_end],
                preferred_element_type=jnp.float32,
            )
            * 0.125
        )
        causal = (first_row + jnp.arange(block_rows, dtype=jnp.int32))[:, None] >= jnp.arange(
            key_end, dtype=jnp.int32
        )[None, :]
        scores = jnp.where(causal, scores, -jnp.inf)
        row_peak = jnp.max(scores, axis=-1, keepdims=True)
        exponents = jnp.exp(scores - row_peak)
        totals = jnp.sum(exponents, axis=-1, keepdims=True)
        attended = jnp.einsum(
            "hgqk,khd->qhgd",
            low(exponents / totals),
            values[:key_end],
            preferred_element_type=jnp.float32,
        )
        outputs.append(low(attended).reshape(block_rows, -1))
        totals_list.append((row_peak + jnp.log(totals))[..., 0])
    return (jnp.concatenate(outputs, axis=0), jnp.stack(totals_list), q_rot, k_rot, values)


def attention_backward(head_grad, q_rot, k_rot, values, log_total):
    length, local_kv = q_rot.shape[:2]
    cos_table, sin_table = rotary_tables(length)
    block_rows = min(512, length)
    grad_rows = head_grad.reshape(length, local_kv, GROUP, HEAD_DIM)
    key_acc = jnp.zeros((length, local_kv, HEAD_DIM), jnp.float32)
    value_acc = jnp.zeros((length, local_kv, HEAD_DIM), jnp.float32)
    query_parts = []
    for block_number, first_row in enumerate(range(0, length, block_rows)):
        key_end = first_row + block_rows
        q_block = q_rot[first_row:key_end]
        grad_block = grad_rows[first_row:key_end]
        key_part = k_rot[:key_end]
        scores = (
            jnp.einsum("qhgd,khd->hgqk", q_block, key_part, preferred_element_type=jnp.float32)
            * 0.125
        )
        causal = (first_row + jnp.arange(block_rows, dtype=jnp.int32))[:, None] >= jnp.arange(
            key_end, dtype=jnp.int32
        )[None, :]
        scores = jnp.where(causal, scores, -jnp.inf)
        probs_full = jnp.exp(scores - log_total[block_number][..., None])
        prob_grad = jnp.einsum(
            "qhgd,khd->hgqk", grad_block, values[:key_end], preferred_element_type=jnp.float32
        )
        score_grad = probs_full * (
            prob_grad - jnp.sum(probs_full * prob_grad, axis=-1, keepdims=True)
        )
        score_low = low(score_grad)
        query_parts.append(
            jnp.einsum("hgqk,khd->qhgd", score_low, key_part, preferred_element_type=jnp.float32)
            * 0.125
        )
        key_acc = key_acc.at[:key_end].add(
            jnp.einsum("hgqk,qhgd->khd", score_low, q_block, preferred_element_type=jnp.float32)
            * 0.125
        )
        value_acc = value_acc.at[:key_end].add(
            jnp.einsum(
                "hgqk,qhgd->khd", low(probs_full), grad_block, preferred_element_type=jnp.float32
            )
        )
    query_all = jnp.concatenate(query_parts, axis=0).reshape(length, -1)
    query_grad = rotate(query_all, cos_table, -sin_table)
    key_grad = rotate(key_acc.reshape(length, -1), cos_table, -sin_table)
    return jnp.concatenate(
        [low(query_grad), low(key_grad), low(value_acc).reshape(length, -1)], axis=1
    )


def remote(src, dst, send_sem, recv_sem, **device):
    return pltpu.make_async_remote_copy(
        src_ref=src,
        dst_ref=dst,
        send_sem=send_sem,
        recv_sem=recv_sem,
        device_id=device,
        device_id_type=MESH,
    )


def greet(d, s, section=None, spread=False):
    barrier = pltpu.get_barrier_semaphore()

    def signal(**device):
        pl.semaphore_signal(barrier, inc=1, device_id=device, device_id_type=MESH)

    signal(seq=s ^ 1)
    signal(seq=s ^ 2)

    @pl.when(d > 0)
    def _():
        signal(dp=d - 1)

    @pl.when(d < 3)
    def _():
        signal(dp=d + 1)

    known = 3
    if section is not None:
        signal(section=1 - section)
        known = 4
    if spread:
        signal(seq=s ^ 3)
        known = known + 1
    inner = (d > 0) & (d < 3)

    @pl.when(inner)
    def _():
        pl.semaphore_wait(barrier, known + 1)

    @pl.when(jnp.logical_not(inner))
    def _():
        pl.semaphore_wait(barrier, known)


class Carried:
    def __init__(self, sections, sources, targets, sems):
        self.section = lax.axis_index("section")
        self.copies = []
        for k, (to, source, target) in enumerate(zip(sections, sources, targets)):
            copy = remote(source, target, sems.at[k, 0], sems.at[k, 1], section=1 - self.section)
            self.copies.append((to, copy))

    def start(self):
        for to, copy in self.copies:
            if to is None:
                copy.start()
            else:

                @pl.when(self.section != to)
                def _():
                    copy.start()

    def finish(self):
        for to, copy in self.copies:
            if to is None:
                copy.wait()
            else:

                @pl.when(self.section != to)
                def _():
                    copy.wait_send()

                @pl.when(self.section == to)
                def _():
                    copy.wait_recv()


class Spread:
    def __init__(self, source, target, sems):
        s = lax.axis_index("seq")
        self.local = pltpu.make_async_copy(source.at[s], target.at[s], sems.at[0, 0])
        self.copies = [
            remote(source.at[s ^ flip], target.at[s], sems.at[flip, 0], sems.at[flip, 1], seq=s ^ flip)
            for flip in (3, 2, 1)
        ]

    def start(self):
        for copy in self.copies:
            copy.start()
        self.local.start()

    def finish(self):
        self.local.wait()
        for copy in self.copies:
            copy.wait()


def cost():
    return pl.CostEstimate(flops=80_000_000_000, bytes_accessed=100_000_000, transcendentals=0)


def gather_scratch(rows, width):
    return [
        pltpu.VMEM((16, rows, width), jnp.bfloat16),
        DMA(()),
        DMA((2, 4)),
        DMA((4,)),
        DMA((4,)),
        DMA((4,)),
        DMA((4, 2)),
        DMA((4, 2)),
    ]


def gather_blocks(x_ref, scratch, compute, carried=None, first=None, spread=False):
    land, lsem, zs, zr, ys, yr, cs, cr = scratch
    d, s = lax.axis_index("dp"), lax.axis_index("seq")

    def place(z, column):
        return land.at[z * 4 + column]

    def z_copy(src, z, right):
        target = d + 1 if right else d - 1
        return remote(src, place(z, s), zs.at[int(right), z], zr.at[z], dp=target)

    def y_copy(src, z):
        return remote(src, place(z, s), ys.at[z], yr.at[z], seq=s ^ 2)

    def core_copy(src, z, across):
        column = s ^ 2 if across else s
        return remote(src, place(z, column), cs.at[z, across], cr.at[z, across], seq=s ^ 1)

    greet(d, s, None if carried is None else carried.section, spread)
    if first is not None:
        first()
    own = pltpu.make_async_copy(x_ref, place(d, s), lsem)
    own.start()
    if carried is not None and first is None:
        carried.start()

    @pl.when(d < 3)
    def _():
        z_copy(x_ref, d, True).start()

    @pl.when(d > 0)
    def _():
        z_copy(x_ref, d, False).start()

    y_copy(x_ref, d).start()
    core_copy(x_ref, d, 0).start()
    own.wait()

    @pl.loop(0, 4)
    def _(i):
        @pl.when(i < 3)
        def _():
            left, right = d - (i + 1), d + (i + 1)

            @pl.when(left >= 0)
            def _():
                z_copy(place(left, s), left, True).wait_recv()

                @pl.when(d < 3)
                def _():
                    z_copy(place(left, s), left, True).start()

            @pl.when(right <= 3)
            def _():
                z_copy(place(right, s), right, False).wait_recv()

                @pl.when(d > 0)
                def _():
                    z_copy(place(right, s), right, False).start()

            following = d ^ (i + 1)
            y_copy(place(following, s), following).start()
            core_copy(place(following, s), following, 0).start()

        z = d ^ i
        y_copy(place(z, s ^ 2), z).wait_recv()
        core_copy(place(z, s ^ 2), z, 1).start()
        core_copy(place(z, s ^ 1), z, 0).wait_recv()
        core_copy(place(z, s ^ 3), z, 1).wait_recv()
        compute(z)

    for z in range(4):

        @pl.when((z <= d) & (d < 3))
        def _():
            z_copy(place(z, s), z, True).wait_send()

        @pl.when((z >= d) & (d > 0))
        def _():
            z_copy(place(z, s), z, False).wait_send()

        y_copy(place(z, s), z).wait_send()
        core_copy(place(z, s), z, 0).wait_send()
        core_copy(place(z, s), z, 1).wait_send()
    return land


def prepare_kernel(
    x_ref, group_ref, gate_ref,
    pick_out, pick_t_out, chosen_out, small_out, qkv_out, parts_out, gate_out,
    both, places, groups, parts, lsem, carry_sem, spread_sem, qs, qr, *gather
):
    d, s, section = lax.axis_index("dp"), lax.axis_index("seq"), lax.axis_index("section")
    known = x_ref.shape[0]
    count = pick_out.shape[2] // CAP
    rows = pick_out.shape[3]
    land = gather[0]
    part = both.at[pl.ds(pl.multiple_of(section * known, known), known)]
    swaps = Carried((None, None), (x_ref, group_ref), (part, groups.at[section]), carry_sem)
    gates = Carried((None,), (share(gate_ref),), (gate_out,), carry_sem.at[pl.ds(2, 1)])
    spreads = [Spread(groups.at[n], parts.at[n], spread_sem.at[n]) for n in range(2)]
    own_columns = pltpu.make_async_copy(parts.at[0], qkv_out.at[d], lsem.at[2])

    def along(src, z, right):
        target = d + 1 if right else d - 1
        return remote(src, qkv_out.at[z], qs.at[int(right), z], qr.at[z], dp=target)

    def first():
        swaps.start()
        own = [
            pltpu.make_async_copy(x_ref, part, lsem.at[0]),
            pltpu.make_async_copy(group_ref, groups.at[section], lsem.at[1]),
        ]
        for copy in own:
            copy.start()
        for copy in own:
            copy.wait()
        swaps.finish()
        gates.start()
        for side in spreads:
            side.start()
        spreads[0].finish()
        own_columns.start()

        @pl.when(d < 3)
        def _():
            along(parts.at[0], d, True).start()

        @pl.when(d > 0)
        def _():
            along(parts.at[0], d, False).start()

    def hop(h):
        @pl.when(d - h >= 0)
        def _():
            along(qkv_out.at[d - h], d - h, True).wait_recv()

            @pl.when(d < 3)
            def _():
                along(qkv_out.at[d - h], d - h, True).start()

        @pl.when(d + h <= 3)
        def _():
            along(qkv_out.at[d + h], d + h, False).wait_recv()

            @pl.when(d > 0)
            def _():
                along(qkv_out.at[d + h], d + h, False).start()

    gather_blocks(both, gather, lambda z: None, gates, first, True)
    hop(1)
    first_expert = (d * 4 + s) * count
    before = lax.broadcasted_iota(jnp.int32, (rows, rows), 0)
    before = low(before < lax.broadcasted_iota(jnp.int32, (rows, rows), 1))
    slot = lax.broadcasted_iota(jnp.int32, (CAP, rows), 0)
    expert = lax.broadcasted_iota(jnp.int32, (EXPERTS, rows), 0)
    lane = lax.broadcasted_iota(jnp.int32, (rows, count * CAP), 1)

    @pl.loop(0, 2)
    def _(layer):
        @pl.loop(0, 16)
        def _(b):
            paths = land[b, pl.ds(pl.multiple_of(layer * known, 16), 16), :].astype(jnp.float32)
            paths = jnp.where(section == 0, paths[:TOP_K], paths[TOP_K:]).astype(jnp.int32)
            chosen = expert == paths[0:1]
            for k in range(1, TOP_K):
                chosen = chosen | (expert == paths[k : k + 1])
            chosen_out[layer, b] = low(chosen)
            mine = [
                jnp.max((paths == first_expert + j).astype(jnp.float32), axis=0, keepdims=True)
                for j in range(count)
            ]
            mine = jnp.concatenate(mine + [jnp.zeros((8 - count, rows), jnp.float32)], axis=0)
            place = jnp.where(mine > 0.5, dot(low(mine), before), -10000.0)
            places[...] = place
            for j in range(count):
                pick_out[layer, b, j * CAP : (j + 1) * CAP, :] = low(
                    slot == place[j : j + 1].astype(jnp.int32)
                )
            turned = places[...].T.astype(jnp.int32)
            pick_t = turned[:, 0:1] == lane
            for j in range(1, count):
                pick_t = pick_t & (lane < j * CAP) | (turned[:, j : j + 1] == lane - j * CAP)
            pick_t_out[layer, b] = low(pick_t)

        depth = small_out.shape[2] // 16
        for b in range(16):
            small = land[b, pl.ds(pl.multiple_of(layer * known + 16, 16), known - 16), :]
            small_out[layer, :, b * depth : (b + 1) * depth] = small[:, :depth]

        @pl.when(layer == 0)
        def _():
            hop(2)

    hop(3)
    spreads[1].finish()
    layer_1 = pltpu.make_async_copy(parts.at[1], parts_out, lsem.at[0])
    layer_1.start()
    for z in range(4):

        @pl.when((z <= d) & (d < 3))
        def _():
            along(parts.at[0], z, True).wait_send()

        @pl.when((z >= d) & (d > 0))
        def _():
            along(parts.at[0], z, False).wait_send()

    own_columns.wait()
    layer_1.wait()
    gates.finish()


def prepare(x, group, gate, count, rows, depth, collective_id):
    known, width = x.shape
    bf = jnp.bfloat16
    anywhere = pl.BlockSpec(memory_space=pl.ANY)
    near = pl.BlockSpec(memory_space=pltpu.VMEM)
    return pl.pallas_call(
        prepare_kernel,
        out_shape=[
            jax.ShapeDtypeStruct((2, 16, count * CAP, rows), bf),
            jax.ShapeDtypeStruct((2, 16, rows, count * CAP), bf),
            jax.ShapeDtypeStruct((2, 16, EXPERTS, rows), bf),
            jax.ShapeDtypeStruct((2, known - 16, 16 * depth), bf),
            jax.ShapeDtypeStruct((4,) + group.shape, bf),
            jax.ShapeDtypeStruct(group.shape, bf),
            jax.ShapeDtypeStruct(share_shape(gate), bf),
        ],
        in_specs=[anywhere] * 3,
        out_specs=[near] * 4 + [anywhere] * 3,
        scratch_shapes=[
            pltpu.VMEM((2 * known, width), bf),
            pltpu.VMEM((8, rows), jnp.float32),
            pltpu.VMEM((2,) + group.shape, bf),
            pltpu.VMEM((2,) + group.shape, bf),
            DMA((3,)),
            DMA((3, 2)),
            DMA((2, 4, 2)),
            DMA((2, 4)),
            DMA((4,)),
        ]
        + gather_scratch(2 * known, width),
        compiler_params=pltpu.CompilerParams(
            collective_id=collective_id, has_side_effects=True, vmem_limit_bytes=60 << 20
        ),
        cost_estimate=cost(),
        name="prepare",
    )(x, group, gate)


def share(ref):
    count = ref.shape[0] // 4
    return ref.at[pl.ds(lax.axis_index("seq") * count, count)]


def share_shape(array):
    return (array.shape[0] // 4,) + array.shape[1:]


def pick_weights(own_refs, other_refs, held, sems, own_layer):
    own_refs = [share(ref) for ref in own_refs]
    mine = lax.axis_index("section") == own_layer

    @pl.when(mine)
    def _():
        for k, ref in enumerate(own_refs):
            pltpu.make_async_copy(ref, held[k], sems.at[k]).start()

    @pl.when(jnp.logical_not(mine))
    def _():
        for k, ref in enumerate(other_refs):
            pltpu.make_async_copy(ref, held[k], sems.at[k]).start()

    def ready(k):
        pltpu.make_async_copy(own_refs[k], held[k], sems.at[k]).wait()

    return ready


def expert_forward_kernel(
    layer, x_ref, pick_ref, chosen_ref, router_ref, mine_ref,
    wg_own, wu_own, wd_own, wg_other, wu_other, wd_other,
    rows_out, gate_out, up_out, hidden_out, slot_gate_out, y_out,
    wg, wu, wd, rows, gate, up, hidden, slot_gate, y, wsem, osem, carry_sem, *gather
):
    count = wg.shape[0]
    carried = None
    if layer == 0:
        carried = Carried((None,), (share(wd_own),), (wd_other,), carry_sem)
        ready = pick_weights((wg_own, wu_own), (wg_other, wu_other), (wg, wu), wsem, layer)
    else:
        ready = pick_weights(
            (wg_own, wu_own, wd_own), (wg_other, wu_other, wd_other), (wg, wu, wd), wsem, layer
        )
    land = gather[0]
    d = lax.axis_index("dp")

    def outs(z):
        part = pl.ds(z * 4 * CAP, 4 * CAP)
        return [
            pltpu.make_async_copy(held.at[:, part], out.at[:, part], osem.at[k, z])
            for k, (held, out) in enumerate(
                ((rows, rows_out), (gate, gate_out), (up, up_out), (hidden, hidden_out), (slot_gate, slot_gate_out))
            )
        ] + [pltpu.make_async_copy(y.at[pl.ds(z * 4, 4)], y_out.at[pl.ds(z * 4, 4)], osem.at[5, z])]

    def down(z):
        part = pl.ds(z * 4 * CAP, 4 * CAP)

        @pl.loop(0, count)
        def _(j):
            result = low(dot(hidden[j, part, :], wd[j]))
            for q in range(4):
                y[z * 4 + q, pl.ds(j * CAP, CAP), :] = result[q * CAP : (q + 1) * CAP]

    def compute(z):
        @pl.when(z == d)
        def _():
            for k in range(2 if layer == 0 else 3):
                ready(k)

        for q in range(4):
            b = z * 4 + q
            picked = low(dot(pick_ref[b], land[b]))
            for j in range(count):
                rows[j, pl.ds(b * CAP, CAP), :] = picked[j * CAP : (j + 1) * CAP]
        part = pl.ds(z * 4 * CAP, 4 * CAP)

        @pl.loop(0, count)
        def _(j):
            x = rows[j, part, :]
            g = dot(x, wg[j])
            u = dot(x, wu[j])
            logits = dot_t(x, router_ref[...])
            for q in range(4):
                b = z * 4 + q
                slots = slice(q * CAP, (q + 1) * CAP)
                seen = dot_t(pick_ref[b, pl.ds(j * CAP, CAP), :], chosen_ref[b])
                masked = jnp.where(seen > 0.5, logits[slots], -1e30)
                power = jnp.exp(masked - jnp.max(masked, axis=1, keepdims=True))
                own = jnp.sum(power * mine_ref[j], axis=1, keepdims=True)
                value = own / jnp.sum(power, axis=1, keepdims=True)
                slot_gate[j, pl.ds(b * CAP, CAP), :] = jnp.broadcast_to(value, (CAP, 128))
            gate[j, part, :] = low(g)
            up[j, part, :] = low(u)
            h = low(g * jax.nn.sigmoid(g) * u * slot_gate[j, part, :][:, :1])
            hidden[j, part, :] = h

        if layer != 0:
            down(z)
        for copy in outs(z)[: 5 if layer == 0 else 6]:
            copy.start()

    gather_blocks(x_ref, gather, compute, carried)
    if layer == 0:
        carried.finish()
        ready = pick_weights((wd_own,), (wd_other,), (wd,), wsem, layer)
        ready(0)
        for z in range(4):
            down(z)
            outs(z)[5].start()
    for z in range(4):
        for copy in outs(z):
            copy.wait()


def expert_forward(layer, x, pick, chosen, router, mine, own, other, collective_id):
    count, width, units = share_shape(own[0])
    rows = x.shape[0]
    slots = 16 * CAP
    bf = jnp.bfloat16
    anywhere = pl.BlockSpec(memory_space=pl.ANY)
    near = pl.BlockSpec(memory_space=pltpu.VMEM)
    results = [
        ((count, slots, width), bf),
        ((count, slots, units), bf),
        ((count, slots, units), bf),
        ((count, slots, units), bf),
        ((count, slots, 128), jnp.float32),
        ((16, count * CAP, width), bf),
    ]

    def kernel(*refs):
        if layer == 0:
            refs = refs[:10] + refs[16:17] + refs[10:16] + refs[17:]
        expert_forward_kernel(layer, *refs)

    shapes = [jax.ShapeDtypeStruct(*result) for result in results]
    if layer == 0:
        shapes.append(jax.ShapeDtypeStruct(share_shape(own[2]), bf))
        other = other[:2]
    operands = (x, pick, chosen, router, mine, *own, *other)
    return pl.pallas_call(
        kernel,
        out_shape=shapes,
        in_specs=[anywhere, near, near, near, near] + [anywhere] * (len(operands) - 5),
        out_specs=[anywhere] * len(shapes),
        scratch_shapes=[pltpu.VMEM(share_shape(weight), bf) for weight in own]
        + [pltpu.VMEM(*result) for result in results]
        + [DMA((3,)), DMA((6, 4)), DMA((1, 2))]
        + gather_scratch(rows, width),
        compiler_params=pltpu.CompilerParams(
            collective_id=collective_id, has_side_effects=True, vmem_limit_bytes=60 << 20
        ),
        cost_estimate=cost(),
        name="expert_forward",
    )(*operands)


class Products:
    def __init__(self, pairs, outs, held, sems):
        self.units = []
        count = outs[0].shape[0]
        for j in range(count):
            at, out_at = 0, 0
            for left, rights in pairs:
                first = at
                loads = [(left, at)] + [(right, at + 1 + k) for k, right in enumerate(rights)]
                at += len(loads)
                for k in range(len(rights)):
                    self.units.append((j, first, first + 1 + k, out_at, loads, k == 0, k + 1 == len(rights)))
                    out_at += 1
        self.count, self.pairs, self.outs, self.held, self.sems = count, at, outs, held, sems

    def load(self, j, source, at):
        return pltpu.make_async_copy(source.at[j], self.held[at], self.sems.at[at])

    def store(self, j, k):
        at = self.pairs + k
        return pltpu.make_async_copy(self.held[at], self.outs[k].at[j], self.sems.at[at])

    def start(self):
        for j, _, _, _, loads, first, _ in self.units:
            if j == 0 and first:
                for source, at in loads:
                    self.load(0, source, at).start()

    def step(self, i):
        for number, (j, left, right, out, loads, first, last) in enumerate(self.units):

            @pl.when(i == number)
            def _():
                if first:
                    for source, at in loads:
                        self.load(j, source, at).wait()
                if j > 0:
                    self.store(j - 1, out).wait()
                a, b, c = self.held[left], self.held[right], self.held[self.pairs + out]

                @pl.loop(0, a.shape[1] // 256)
                def _(m):
                    columns = pl.ds(pl.multiple_of(m * 256, 256), 256)
                    c[columns, :] = low(t_dot(a[:, columns], b[...]))

                self.store(j, out).start()
                if last and j + 1 < self.count:
                    for source, at in loads:
                        self.load(j + 1, source, at).start()

    def finish(self):
        for k in range(len(self.outs)):
            self.store(self.count - 1, k).wait()


def combine_kernel(sections, spreads, pairs, pick_ref, y_ref, *refs):
    kept = len(sections)
    sources, refs = refs[:kept], refs[kept:]
    spread_sources, refs = refs[:spreads], refs[spreads:]
    factors = []
    for rights in pairs:
        factors.append((refs[0], refs[1 : 1 + rights]))
        refs = refs[1 + rights :]
    out_ref, *refs = refs
    targets, refs = refs[:kept], refs[kept:]
    spread_targets, refs = refs[:spreads], refs[spreads:]
    products = sum(pairs)
    product_outs, refs = refs[:products], refs[products:]
    y, sent, own, core_in, y_in, z_in, lsem, zs, zr, ys, yr, cs, cr, carry_sem, spread_sem, *refs = refs
    work = Products(factors, product_outs, refs[:-1], refs[-1]) if pairs else None
    carried = Carried(sections, sources, targets, carry_sem)
    spread = [Spread(a, b, spread_sem) for a, b in zip(spread_sources, spread_targets)]
    d, s = lax.axis_index("dp"), lax.axis_index("seq")
    half = out_ref.shape[0] // 2

    def loaded(b):
        return pltpu.make_async_copy(y_ref.at[b], y.at[b], lsem.at[b])

    def column(across, other_core):
        return s ^ (2 * across) ^ other_core

    for i in range(4):
        z = d ^ (3 - i)
        for across in (1, 0):
            for other_core in (1, 0):
                loaded(z * 4 + column(across, other_core)).start()
    greet(d, s, carried.section, spreads > 0)
    carried.start()

    def rows(k):
        return pl.ds(pl.multiple_of(k * half, half), half)

    def partial_sum(z, k, across, other_core):
        b = z * 4 + column(across, other_core)

        @pl.when(k == 0)
        def _():
            loaded(b).wait()

        return dot(pick_ref[b, rows(k), :], y[b])

    def core_copy(z, k, across):
        return remote(
            sent.at[z, across, rows(k)],
            core_in.at[z, across, rows(k)],
            cs.at[z, k, across],
            cr.at[z, k, across],
            seq=s ^ 1,
        )

    def y_copy(z, k):
        return remote(own.at[z, 1, rows(k)], y_in.at[z, rows(k)], ys.at[z, k], yr.at[z, k], seq=s ^ 2)

    def z_copy(z, k, right):
        target = d + 1 if right else d - 1
        return remote(
            own.at[z, 0, rows(k)],
            z_in.at[int(right), z, rows(k)],
            zs.at[z, k],
            zr.at[int(right), z, k],
            dp=target,
        )

    def start(i):
        z, k = d ^ (3 - i // 2), i % 2
        sent[z, 1, rows(k), :] = low(partial_sum(z, k, 1, 1))
        core_copy(z, k, 1).start()
        total = partial_sum(z, k, 1, 0)
        core_copy(z, k, 1).wait_recv()
        own[z, 1, rows(k), :] = low(total + core_in[z, 1, rows(k), :].astype(jnp.float32))
        y_copy(z, k).start()
        sent[z, 0, rows(k), :] = low(partial_sum(z, k, 0, 1))
        core_copy(z, k, 0).start()

    start(0)
    for side in spread:
        side.start()
    if work:
        work.start()

    @pl.loop(0, 8)
    def _(i):
        @pl.when(i < 7)
        def _():
            start(i + 1)

        if work:
            work.step(i)

        z, k = d ^ (3 - i // 2), i % 2
        total = partial_sum(z, k, 0, 0)
        core_copy(z, k, 0).wait_recv()
        total = total + core_in[z, 0, rows(k), :].astype(jnp.float32)
        y_copy(z, k).wait_recv()
        total = total + y_in[z, rows(k), :].astype(jnp.float32)

        @pl.when(z < d)
        def _():
            @pl.when(d < 3)
            def _():
                z_copy(z, k, False).wait_recv()
                own[z, 0, rows(k), :] = low(total + z_in[0, z, rows(k), :].astype(jnp.float32))

            @pl.when(d == 3)
            def _():
                own[z, 0, rows(k), :] = low(total)

            z_copy(z, k, False).start()

        @pl.when(z > d)
        def _():
            @pl.when(d > 0)
            def _():
                z_copy(z, k, True).wait_recv()
                own[z, 0, rows(k), :] = low(total + z_in[1, z, rows(k), :].astype(jnp.float32))

            @pl.when(d == 0)
            def _():
                own[z, 0, rows(k), :] = low(total)

            z_copy(z, k, True).start()

        @pl.when(z == d)
        def _():
            out_ref[rows(k), :] = total

    for k in range(2):

        @pl.when(d < 3)
        def _():
            z_copy(d, k, False).wait_recv()
            out_ref[rows(k), :] += z_in[0, d, rows(k), :].astype(jnp.float32)

        @pl.when(d > 0)
        def _():
            z_copy(d, k, True).wait_recv()
            out_ref[rows(k), :] += z_in[1, d, rows(k), :].astype(jnp.float32)

    for z in range(4):
        for k in range(2):
            core_copy(z, k, 0).wait_send()
            core_copy(z, k, 1).wait_send()
            y_copy(z, k).wait_send()

            @pl.when(z < d)
            def _():
                z_copy(z, k, False).wait_send()

            @pl.when(z > d)
            def _():
                z_copy(z, k, True).wait_send()

    carried.finish()
    for side in spread:
        side.finish()
    if work:
        work.finish()


def combine(pick_t, y, collective_id, carry, spread=(), products=()):
    rows, width = pick_t.shape[1], y.shape[2]
    anywhere = pl.BlockSpec(memory_space=pl.ANY)
    near = pl.BlockSpec(memory_space=pltpu.VMEM)
    sections = tuple(to for to, _ in carry)
    arrays = [array for _, array in carry]

    arrays = arrays + list(spread)
    pairs = [len(rights) for _, rights in products]
    factors = [factor for left, rights in products for factor in (left, *rights)]
    outs = [
        jax.ShapeDtypeStruct((left.shape[0], left.shape[2], right.shape[2]), jnp.bfloat16)
        for left, rights in products
        for right in rights
    ]
    held = [pltpu.VMEM(array.shape[1:], jnp.bfloat16) for array in factors + outs]
    held = held + [DMA((len(held),))] if held else []

    def kernel(*refs):
        combine_kernel(sections, len(spread), pairs, *refs)

    def blocks(*lead):
        return pltpu.VMEM(lead + (rows, width), jnp.bfloat16)

    return pl.pallas_call(
        kernel,
        out_shape=[jax.ShapeDtypeStruct((rows, width), jnp.float32)]
        + [jax.ShapeDtypeStruct(array.shape, array.dtype) for array in arrays]
        + outs,
        in_specs=[near, anywhere] + [anywhere] * (len(arrays) + len(factors)),
        out_specs=[near] + [anywhere] * (len(arrays) + len(outs)),
        scratch_shapes=[
            pltpu.VMEM(y.shape, jnp.bfloat16),
            blocks(4, 2),
            blocks(4, 2),
            blocks(4, 2),
            blocks(4),
            blocks(2, 4),
            DMA((16,)),
            DMA((4, 2)),
            DMA((2, 4, 2)),
            DMA((4, 2)),
            DMA((4, 2)),
            DMA((4, 2, 2)),
            DMA((4, 2, 2)),
            DMA((max(1, len(arrays)), 2)),
            DMA((4, 2)),
        ]
        + held,
        compiler_params=pltpu.CompilerParams(
            collective_id=collective_id, has_side_effects=True, vmem_limit_bytes=60 << 20
        ),
        cost_estimate=cost(),
        name="combine",
    )(pick_t, y, *arrays, *factors)


def expert_backward_kernel(
    layer, sections, x_ref, pick_ref, gate_in, up_in, slot_gate_in,
    wg_own, wu_own, wd_own, wg_other, wu_other, wd_other, *refs
):
    kept = len(sections)
    sources, refs = refs[:kept], refs[kept:]
    rows_out, gate_out, up_out, term_out, y_out, *refs = refs
    targets, refs = refs[:kept], refs[kept:]
    wg, wu, wd, rows, gate, up, slot_gate, y, wsem, isem, osem, carry_sem, *gather = refs
    carried = Carried(sections, sources, targets, carry_sem)
    count = wg.shape[0]
    ready = pick_weights(
        (wg_own, wu_own, wd_own), (wg_other, wu_other, wd_other), (wg, wu, wd), wsem, layer
    )
    land = gather[0]
    d = lax.axis_index("dp")
    ins = [
        pltpu.make_async_copy(src, held, isem.at[k])
        for k, (src, held) in enumerate(((gate_in, gate), (up_in, up), (slot_gate_in, slot_gate)))
    ]
    for copy in ins:
        copy.start()

    def outs(z):
        part = pl.ds(z * 4 * CAP, 4 * CAP)
        return [
            pltpu.make_async_copy(held.at[:, part], out.at[:, part], osem.at[k, z])
            for k, (held, out) in enumerate(
                ((rows, rows_out), (gate, gate_out), (up, up_out), (slot_gate, term_out))
            )
        ] + [pltpu.make_async_copy(y.at[pl.ds(z * 4, 4)], y_out.at[pl.ds(z * 4, 4)], osem.at[4, z])]

    def compute(z):
        @pl.when(z == d)
        def _():
            for k in range(3):
                ready(k)
            for copy in ins:
                copy.wait()

        for q in range(4):
            b = z * 4 + q
            picked = low(dot(pick_ref[b], land[b]))
            for j in range(count):
                rows[j, pl.ds(b * CAP, CAP), :] = picked[j * CAP : (j + 1) * CAP]
        part = pl.ds(z * 4 * CAP, 4 * CAP)

        @pl.loop(0, count)
        def _(j):
            plain = dot_t(rows[j, part, :], wd[j])
            g = gate[j, part, :].astype(jnp.float32)
            u = up[j, part, :].astype(jnp.float32)
            sigmoid = jax.nn.sigmoid(g)
            active = g * sigmoid
            term = jnp.sum(plain * (active * u), axis=1, keepdims=True)
            grad = plain * slot_gate[j, part, :][:, :1]
            dg = low(grad * u * sigmoid * (1.0 + g * (1.0 - sigmoid)))
            du = low(grad * active)
            slot_gate[j, part, :] = jnp.broadcast_to(term, (4 * CAP, 128))
            gate[j, part, :] = dg
            up[j, part, :] = du
            result = low(dot_t(dg, wg[j]) + dot_t(du, wu[j]))
            for q in range(4):
                y[z * 4 + q, pl.ds(j * CAP, CAP), :] = result[q * CAP : (q + 1) * CAP]

        for copy in outs(z):
            copy.start()

    gather_blocks(x_ref, gather, compute, carried)
    carried.finish()
    for z in range(4):
        for copy in outs(z):
            copy.wait()


def expert_backward(layer, x, pick, gate, up, slot_gate, own, other, collective_id, carry):
    count, width, units = share_shape(own[0])
    rows = x.shape[0]
    slots = 16 * CAP
    bf = jnp.bfloat16
    anywhere = pl.BlockSpec(memory_space=pl.ANY)
    near = pl.BlockSpec(memory_space=pltpu.VMEM)
    results = [
        ((count, slots, width), bf),
        ((count, slots, units), bf),
        ((count, slots, units), bf),
        ((count, slots, 128), jnp.float32),
        ((16, count * CAP, width), bf),
    ]
    sections = tuple(to for to, _ in carry)
    arrays = [array for _, array in carry]

    def kernel(*refs):
        expert_backward_kernel(layer, sections, *refs)

    return pl.pallas_call(
        kernel,
        out_shape=[jax.ShapeDtypeStruct(*result) for result in results]
        + [jax.ShapeDtypeStruct(array.shape, array.dtype) for array in arrays],
        in_specs=[anywhere, near] + [anywhere] * (9 + len(arrays)),
        out_specs=[anywhere] * (5 + len(arrays)),
        scratch_shapes=[pltpu.VMEM(share_shape(weight), bf) for weight in own]
        + [pltpu.VMEM(*result) for result in results]
        + [DMA((3,)), DMA((3,)), DMA((5, 4)), DMA((max(1, len(arrays)), 2))]
        + gather_scratch(rows, width),
        compiler_params=pltpu.CompilerParams(
            collective_id=collective_id, has_side_effects=True, vmem_limit_bytes=60 << 20
        ),
        cost_estimate=cost(),
        name="expert_backward",
    )(x, pick, gate, up, slot_gate, *own, *other, *arrays)


def rope(x, cos_table, sin_table):
    lane = lax.broadcasted_iota(jnp.int32, x.shape, 1)
    turned = jnp.where(lane % HEAD_DIM < HEAD_DIM // 2, pltpu.roll(x, 128 - HEAD_DIM // 2, 1), pltpu.roll(x, HEAD_DIM // 2, 1))
    return x * cos_table + turned * sin_table


def seq_greet(s, section, spread=False):
    barrier = pltpu.get_barrier_semaphore()
    devices = [dict(seq=s ^ 1), dict(seq=s ^ 2), dict(section=1 - section)]
    if spread:
        devices.append(dict(seq=s ^ 3))
    for device in devices:
        pl.semaphore_signal(barrier, inc=1, device_id=device, device_id_type=MESH)
    pl.semaphore_wait(barrier, len(devices))


def seq_scratch(rows, width):
    return [
        pltpu.VMEM((4, rows, width), jnp.bfloat16),
        pltpu.VMEM((2, rows, width), jnp.bfloat16),
        pltpu.VMEM((2, rows, width), jnp.bfloat16),
        pltpu.VMEM((rows, width), jnp.bfloat16),
        pltpu.VMEM((rows, width), jnp.bfloat16),
        DMA(()),
        DMA((4, 2)),
        DMA((3, 2)),
    ]


class Line:
    def __init__(self, scratch):
        self.land, self.sent, self.core_in, self.y_sent, self.y_in, self.lsem, self.ag, self.rs = scratch
        self.s = lax.axis_index("seq")

    def hop(self, src, dst, sems, k, flip):
        return remote(src, dst, sems.at[k, 0], sems.at[k, 1], seq=self.s ^ flip)

    def gather(self, x_ref, use):
        s, land = self.s, self.land
        own = pltpu.make_async_copy(x_ref, land.at[s], self.lsem)
        own.start()
        over = self.hop(x_ref, land.at[s], self.ag, 0, 2)
        beside = self.hop(x_ref, land.at[s], self.ag, 1, 1)
        over.start()
        beside.start()
        own.wait()
        use(s)
        beside.wait_recv()
        use(s ^ 1)
        over.wait_recv()
        further = self.hop(land.at[s ^ 2], land.at[s ^ 2], self.ag, 2, 1)
        further.start()
        use(s ^ 2)
        further.wait_recv()
        use(s ^ 3)
        over.wait_send()
        beside.wait_send()
        further.wait_send()

    def hand_over(self, t, partial, out_ref):
        relation = t ^ self.s

        @pl.when(relation == 3)
        def _():
            self.sent[0] = low(partial[...])
            self.hop(self.sent.at[0], self.core_in.at[0], self.rs, 0, 1).start()

        @pl.when(relation == 2)
        def _():
            self.hop(self.sent.at[0], self.core_in.at[0], self.rs, 0, 1).wait_recv()
            self.y_sent[...] = low(partial[...] + self.core_in[0].astype(jnp.float32))
            self.hop(self.y_sent, self.y_in, self.rs, 1, 2).start()

        @pl.when(relation == 1)
        def _():
            self.sent[1] = low(partial[...])
            self.hop(self.sent.at[1], self.core_in.at[1], self.rs, 2, 1).start()

        @pl.when(relation == 0)
        def _():
            out_ref[...] = partial[...]

    def finish(self, out_ref):
        self.hop(self.sent.at[1], self.core_in.at[1], self.rs, 2, 1).wait()
        out_ref[...] += self.core_in[1].astype(jnp.float32)
        self.hop(self.y_sent, self.y_in, self.rs, 1, 2).wait()
        out_ref[...] += self.y_in[...].astype(jnp.float32)
        self.hop(self.sent.at[0], self.core_in.at[0], self.rs, 0, 1).wait_send()


def attention_forward_kernel(sections, x_ref, qkv_ref, wo_ref, cos_ref, sin_ref, *refs):
    kept = len(sections)
    sources, refs = refs[:kept], refs[kept:]
    sources = [share(ref) if to is None else ref for to, ref in zip(sections, sources)]
    out_ref, all_out, heads_out, lse_out, ot_out, *refs = refs
    targets, refs = refs[:kept], refs[kept:]
    wqkv, wo, heads, lse, ot, partial, wsem, osem, carry_sem, *line = refs
    line = Line(line)
    carried = Carried(sections, sources, targets, carry_sem)
    s = line.s
    rows = out_ref.shape[0]
    kv = heads.shape[0] // (GROUP + 2)
    queries = GROUP * kv
    loads = [pltpu.make_async_copy(qkv_ref, wqkv, wsem.at[0]), pltpu.make_async_copy(wo_ref, wo, wsem.at[1])]
    for load in loads:
        load.start()
    seq_greet(s, carried.section)
    carried.start()
    lse[...] = jnp.zeros_like(lse)

    def project(t):
        part = pl.ds(pl.multiple_of(t * rows, rows), rows)

        @pl.when(t == s)
        def _():
            loads[0].wait()

        qkv = low(dot(line.land[t], wqkv[...]))
        for chunk in range((queries + kv) // 2):
            x = qkv[:, chunk * 128 : (chunk + 1) * 128].astype(jnp.float32)
            x = low(rope(x, cos_ref[part, :], sin_ref[part, :]))
            heads[2 * chunk, part, :] = x[:, :HEAD_DIM]
            heads[2 * chunk + 1, part, :] = x[:, HEAD_DIM:]
        for j in range(kv):
            begin = (queries + kv + j) * HEAD_DIM
            heads[queries + kv + j, part, :] = qkv[:, begin : begin + HEAD_DIM]

    line.gather(x_ref, project)
    saves = [pltpu.make_async_copy(line.land, all_out, osem.at[0]), pltpu.make_async_copy(heads, heads_out, osem.at[1])]
    for save in saves:
        save.start()
    loads[1].wait()

    def attend(block):
        keys = (block + 1) * rows
        columns = slice(block * rows, (block + 1) * rows)

        @pl.loop(0, queries)
        def _(h):
            j = h // GROUP
            scores = dot_t(heads[queries + j, :keys, :], heads[h, columns, :]) * 0.125
            key_at = lax.broadcasted_iota(jnp.int32, scores.shape, 0)
            query_at = lax.broadcasted_iota(jnp.int32, scores.shape, 1) + block * rows
            scores = jnp.where(key_at <= query_at, scores, -jnp.inf)
            peak = jnp.max(scores, axis=0, keepdims=True)
            power = jnp.exp(scores - peak)
            total = jnp.sum(power, axis=0, keepdims=True)
            attended = t_dot(heads[queries + kv + j, :keys, :], low(power / total))
            ot[pl.ds(pl.multiple_of(h * HEAD_DIM, HEAD_DIM), HEAD_DIM), columns] = low(attended)
            lse[pl.ds(h, 1), columns] = peak + jnp.log(total)

        partial[...] = t_dot(ot[:, columns], wo[...])

    @pl.loop(0, 4)
    def _(i):
        t = s ^ (3 - i)
        for block in range(4):

            @pl.when(t == block)
            def _():
                attend(block)

        line.hand_over(t, partial, out_ref)

    saves += [pltpu.make_async_copy(lse, lse_out, osem.at[2]), pltpu.make_async_copy(ot, ot_out, osem.at[3])]
    for save in saves[2:]:
        save.start()
    line.finish(out_ref)
    carried.finish()
    for save in saves:
        save.wait()


def attention_forward_call(x, qkv_w, out_w, tables, collective_id, carry):
    rows, width = x.shape
    local_heads = qkv_w.shape[1] // HEAD_DIM
    bf, f32 = jnp.bfloat16, jnp.float32
    anywhere = pl.BlockSpec(memory_space=pl.ANY)
    near = pl.BlockSpec(memory_space=pltpu.VMEM)
    sections = tuple(to for to, _ in carry)
    arrays = [array for _, array in carry]
    results = [
        ((rows, width), f32),
        ((4, rows, width), bf),
        ((local_heads, 4 * rows, HEAD_DIM), bf),
        ((8, 4 * rows), f32),
        ((out_w.shape[0], 4 * rows), bf),
    ]

    def kernel(*refs):
        attention_forward_kernel(sections, *refs)

    return pl.pallas_call(
        kernel,
        out_shape=[jax.ShapeDtypeStruct(*result) for result in results]
        + [
            jax.ShapeDtypeStruct(share_shape(array) if to is None else array.shape, array.dtype)
            for to, array in carry
        ],
        in_specs=[anywhere] * 3 + [near] * 2 + [anywhere] * len(arrays),
        out_specs=[near] + [anywhere] * (4 + len(arrays)),
        scratch_shapes=[
            pltpu.VMEM(qkv_w.shape, bf),
            pltpu.VMEM(out_w.shape, bf),
            pltpu.VMEM(*results[2]),
            pltpu.VMEM(*results[3]),
            pltpu.VMEM(*results[4]),
            pltpu.VMEM((rows, width), f32),
            DMA((2,)),
            DMA((4,)),
            DMA((max(1, len(arrays)), 2)),
        ]
        + seq_scratch(rows, width),
        compiler_params=pltpu.CompilerParams(
            collective_id=collective_id, has_side_effects=True, vmem_limit_bytes=60 << 20
        ),
        cost_estimate=cost(),
        name="attention_forward",
    )(x, qkv_w, out_w, *tables, *arrays)


def attention_backward_kernel(
    sections, spreads, x_ref, qkv_ref, wo_ref, cos_ref, sin_ref, heads_in, lse_ref, *refs
):
    kept = len(sections)
    sources, refs = refs[:kept], refs[kept:]
    spread_sources, refs = refs[:spreads], refs[spreads:]
    out_ref, all_out, grads_out, *refs = refs
    targets, refs = refs[:kept], refs[kept:]
    spread_targets, refs = refs[:spreads], refs[spreads:]
    wqkv, wo, heads, douts, dk, dv, dqt, grads, partial, wsem, osem, carry_sem, spread_sem, *line = refs
    spread = [Spread(a, b, spread_sem) for a, b in zip(spread_sources, spread_targets)]
    line = Line(line)
    carried = Carried(sections, sources, targets, carry_sem)
    s = line.s
    rows = out_ref.shape[0]
    kv = heads.shape[0] // (GROUP + 2)
    queries = GROUP * kv
    loads = [
        pltpu.make_async_copy(wo_ref, wo, wsem.at[0]),
        pltpu.make_async_copy(qkv_ref, wqkv, wsem.at[1]),
        pltpu.make_async_copy(heads_in, heads, wsem.at[2]),
    ]
    for load in loads:
        load.start()
    seq_greet(s, carried.section, spreads > 0)
    carried.start()
    dk[...] = jnp.zeros_like(dk)
    dv[...] = jnp.zeros_like(dv)

    def project(t):
        part = pl.ds(pl.multiple_of(t * rows, rows), rows)

        @pl.when(t == s)
        def _():
            loads[0].wait()

        grad = low(dot_t(line.land[t], wo[...]))
        for h in range(queries):
            douts[h, part, :] = grad[:, h * HEAD_DIM : (h + 1) * HEAD_DIM]

    line.gather(x_ref, project)
    saves = [pltpu.make_async_copy(line.land, all_out, osem.at[0])]
    saves[0].start()
    for side in spread:
        side.start()
    loads[1].wait()
    loads[2].wait()

    for block in (3, 2, 1, 0):
        keys = (block + 1) * rows
        part = slice(block * rows, (block + 1) * rows)

        @pl.loop(0, queries)
        def _(h):
            j = h // GROUP
            key = heads[queries + j, :keys, :]
            query = heads[h, part, :]
            grad = douts[h, part, :]
            scores = dot_t(key, query) * 0.125
            key_at = lax.broadcasted_iota(jnp.int32, scores.shape, 0)
            query_at = lax.broadcasted_iota(jnp.int32, scores.shape, 1) + block * rows
            scores = jnp.where(key_at <= query_at, scores, -jnp.inf)
            probs = jnp.exp(scores - lse_ref[pl.ds(h, 1), part])
            dprobs = dot_t(heads[queries + kv + j, :keys, :], grad)
            mean = jnp.sum(probs * dprobs, axis=0, keepdims=True)
            dscores = low(probs * (dprobs - mean))
            dk[j, :keys, :] += dot(dscores, query) * 0.125
            dv[j, :keys, :] += dot(low(probs), grad)
            dqt[pl.ds(pl.multiple_of(h * HEAD_DIM, HEAD_DIM), HEAD_DIM), :] = t_dot(key, dscores) * 0.125

        cos_part, sin_part = cos_ref[part, :], -sin_ref[part, :]
        dq = dqt[...].T
        for chunk in range(queries // 2):
            lanes = slice(chunk * 128, (chunk + 1) * 128)
            grads[part, lanes] = low(rope(dq[:, lanes], cos_part, sin_part))
        for pair in range(kv // 2):
            both = jnp.concatenate([dk[2 * pair, part, :], dk[2 * pair + 1, part, :]], axis=1)
            begin = queries * HEAD_DIM + pair * 128
            grads[part, begin : begin + 128] = low(rope(both, cos_part, sin_part))
            both = jnp.concatenate([dv[2 * pair, part, :], dv[2 * pair + 1, part, :]], axis=1)
            begin = (queries + kv) * HEAD_DIM + pair * 128
            grads[part, begin : begin + 128] = low(both)
        partial[...] = dot_t(grads[part, :], wqkv[...])
        line.hand_over(block, partial, out_ref)

    saves.append(pltpu.make_async_copy(grads, grads_out, osem.at[1]))
    saves[1].start()
    line.finish(out_ref)
    carried.finish()
    for side in spread:
        side.finish()
    for save in saves:
        save.wait()


def attention_backward_call(x, qkv_w, out_w, tables, heads, lse, collective_id, carry, spread=()):
    rows, width = x.shape
    bf, f32 = jnp.bfloat16, jnp.float32
    anywhere = pl.BlockSpec(memory_space=pl.ANY)
    near = pl.BlockSpec(memory_space=pltpu.VMEM)
    sections = tuple(to for to, _ in carry)
    arrays = [array for _, array in carry]
    results = [((rows, width), f32), ((4, rows, width), bf), ((4 * rows, qkv_w.shape[1]), bf)]
    kv = heads.shape[0] // (GROUP + 2)
    queries = GROUP * kv

    arrays = arrays + list(spread)

    def kernel(*refs):
        attention_backward_kernel(sections, len(spread), *refs)

    return pl.pallas_call(
        kernel,
        out_shape=[jax.ShapeDtypeStruct(*result) for result in results]
        + [jax.ShapeDtypeStruct(array.shape, array.dtype) for array in arrays],
        in_specs=[anywhere] * 3 + [near] * 2 + [anywhere, near] + [anywhere] * len(arrays),
        out_specs=[near] + [anywhere] * (2 + len(arrays)),
        scratch_shapes=[
            pltpu.VMEM(qkv_w.shape, bf),
            pltpu.VMEM(out_w.shape, bf),
            pltpu.VMEM(heads.shape, bf),
            pltpu.VMEM((queries, 4 * rows, HEAD_DIM), bf),
            pltpu.VMEM((kv, 4 * rows, HEAD_DIM), f32),
            pltpu.VMEM((kv, 4 * rows, HEAD_DIM), f32),
            pltpu.VMEM((queries * HEAD_DIM, rows), f32),
            pltpu.VMEM(*results[2]),
            pltpu.VMEM((rows, width), f32),
            DMA((3,)),
            DMA((2,)),
            DMA((max(1, len(arrays)), 2)),
            DMA((4, 2)),
        ]
        + seq_scratch(rows, width),
        compiler_params=pltpu.CompilerParams(
            collective_id=collective_id, has_side_effects=True, vmem_limit_bytes=60 << 20
        ),
        cost_estimate=cost(),
        name="attention_backward",
    )(x, qkv_w, out_w, *tables, heads, lse, *arrays)


def last_kernel(sections, down_ref, cols_ref, cols_other, out_ref, out_other, *refs):
    kept = len(sections)
    sources, refs = refs[:kept], refs[kept:]
    down_out, cols_out, rows_out, *refs = refs
    targets, refs = refs[:kept], refs[kept:]
    cols_in, cols, out_in, out_sum, down_sem, cols_sem, row_sem, swap_sem, carry_sem = refs
    d, s, section = lax.axis_index("dp"), lax.axis_index("seq"), lax.axis_index("section")
    barrier = pltpu.get_barrier_semaphore()

    def signal(**device):
        pl.semaphore_signal(barrier, inc=1, device_id=device, device_id_type=MESH)

    for flip in (1, 2, 3):
        signal(seq=s ^ flip)
    signal(section=1 - section)

    @pl.when(d != s)
    def _():
        signal(dp=s, seq=d)
        pl.semaphore_wait(barrier, 5)

    @pl.when(d == s)
    def _():
        pl.semaphore_wait(barrier, 4)

    swaps = Carried((None, None), (cols_other, out_other), (cols_in, out_in), swap_sem)
    carried = Carried(sections, sources, targets, carry_sem)
    down = Spread(down_ref, down_out, down_sem)
    swaps.start()
    down.start()
    swaps.finish()
    carried.start()
    cols[...] = low(cols_ref[...].astype(jnp.float32) + cols_in[...].astype(jnp.float32))
    out_sum[...] = low(out_ref[...].astype(jnp.float32) + out_in[...].astype(jnp.float32))
    spread = Spread(cols, cols_out, cols_sem)
    spread.start()
    rows = remote(out_sum, rows_out, row_sem.at[0], row_sem.at[1], dp=s, seq=d)

    @pl.when(d != s)
    def _():
        rows.start()
        rows.wait()

    @pl.when(d == s)
    def _():
        rows_out[...] = out_sum[...]

    spread.finish()
    down.finish()
    carried.finish()


def last_exchange(down, cols, cols_other, out, out_other, collective_id, carry):
    bf = jnp.bfloat16
    anywhere = pl.BlockSpec(memory_space=pl.ANY)
    near = pl.BlockSpec(memory_space=pltpu.VMEM)
    sections = tuple(to for to, _ in carry)
    arrays = [array for _, array in carry]

    def kernel(*refs):
        last_kernel(sections, *refs)

    return pl.pallas_call(
        kernel,
        out_shape=[
            jax.ShapeDtypeStruct(array.shape, array.dtype) for array in (down, cols, out, *arrays)
        ],
        in_specs=[anywhere, near, anywhere, near, anywhere] + [anywhere] * len(arrays),
        out_specs=[anywhere, near, near] + [anywhere] * len(arrays),
        scratch_shapes=[
            pltpu.VMEM(cols.shape, bf),
            pltpu.VMEM(cols.shape, bf),
            pltpu.VMEM(out.shape, bf),
            pltpu.VMEM(out.shape, bf),
            DMA((4, 2)),
            DMA((4, 2)),
            DMA((2,)),
            DMA((2, 2)),
            DMA((max(1, len(arrays)), 2)),
        ],
        compiler_params=pltpu.CompilerParams(
            collective_id=collective_id, has_side_effects=True, vmem_limit_bytes=60 << 20
        ),
        name="last_exchange",
    )(down, cols, cols_other, out, out_other, *arrays)


def wide_tables(length):
    cos_table, sin_table = rotary_tables(length)
    cos_table, sin_table = cos_table[:, 0], sin_table[:, 0]
    return (
        jnp.concatenate([cos_table] * 4, axis=1),
        jnp.concatenate([-sin_table, sin_table] * 2, axis=1),
    )


def token_choice(route):
    return route[..., None] == jnp.arange(EXPERTS, dtype=jnp.int32)


def routing(route_all, first_expert, count):
    chosen = jnp.any(token_choice(route_all), axis=2)
    blocks, rows = chosen.shape[:2]
    mine = lax.dynamic_slice_in_dim(chosen, first_expert, count, axis=2)
    chosen = low(jnp.transpose(chosen, (0, 2, 1)))
    earlier = jnp.tril(jnp.ones((rows, rows), jnp.bfloat16), -1)
    place = jnp.einsum(
        "ts,bsj->bjt", earlier, mine.astype(jnp.bfloat16), preferred_element_type=jnp.float32
    ).astype(jnp.int32)
    mine = jnp.transpose(mine, (0, 2, 1))
    place = jnp.where(mine, place, -1)
    slots = jnp.arange(CAP, dtype=jnp.int32)
    pick = low(place[:, :, None, :] == slots[None, None, :, None]).reshape(blocks, -1, rows)
    return chosen, pick, jnp.transpose(pick, (0, 2, 1))


def choose(pick, rows, count):
    picked = jnp.einsum("bct,btd->bcd", pick, rows, preferred_element_type=jnp.float32)
    blocks = pick.shape[0]
    picked = low(picked).reshape(blocks, count, CAP, -1)
    return jnp.transpose(picked, (1, 0, 2, 3)).reshape(count, blocks * CAP, -1)


def give_back(pick_t, slot_rows):
    blocks, rows = pick_t.shape[:2]
    count, _, width = slot_rows.shape
    slot_rows = jnp.transpose(slot_rows.reshape(count, blocks, CAP, width), (1, 0, 2, 3))
    slot_rows = slot_rows.reshape(blocks, count * CAP, width)
    total = jnp.einsum("btc,bcd->btd", pick_t, slot_rows, preferred_element_type=jnp.float32)
    return low(total).reshape(-1, width)


def each_dot(form, a, b):
    return jnp.einsum(form, a, b, preferred_element_type=jnp.float32)


def after(value, *others):
    return lax.optimization_barrier((value, *others))[0]


def has_kernels():
    return lax.axis_size("dp") == 4 and lax.axis_size("seq") == 4


def forward_layer(number, layer_in, picking, weights, experts, *carry):
    attn_scale, ffn_scale, qkv_w, out_w, router_w = weights
    chosen, pick, pick_t, first_expert = picking
    own, other = experts
    count = pick.shape[1] // CAP
    blocks, _, rows = chosen.shape
    received = []
    normed_input = low(rms_norm(layer_in, attn_scale))
    if has_kernels():
        branch, normed_all, heads, log_total, mixed_t, *received = attention_forward_call(
            normed_input, qkv_w, out_w, wide_tables(4 * layer_in.shape[0]), 9 + number, carry
        )
        attention_state = (normed_all.reshape(-1, layer_in.shape[1]), mixed_t, heads, log_total)
    else:
        received = [swap(array) if to is None else pass_to(array, to) for to, array in carry]
        normed_all = lax.all_gather(normed_input, "seq", axis=0, tiled=True)
        qkv = low(dot(normed_all, qkv_w))
        kv_width = KV_HEADS * HEAD_DIM // lax.axis_size("seq")
        q_width = GROUP * kv_width
        mixed, log_total, q_rot, k_rot, v_heads = attention_forward(
            qkv[:, :q_width], qkv[:, q_width : q_width + kv_width], qkv[:, q_width + kv_width :]
        )
        branch = lax.psum_scatter(low(dot(mixed, out_w)), "seq", scatter_dimension=0, tiled=True)
        attention_state = (normed_all, mixed.T, (q_rot, k_rot, v_heads), log_total)
    after_update = layer_in + branch.astype(jnp.float32)
    normed_ffn = low(rms_norm(after_update, ffn_scale))
    own_block = lax.axis_index("dp") * lax.axis_size("seq") + lax.axis_index("seq")
    own_chosen = lax.dynamic_index_in_dim(chosen, own_block, 0, keepdims=False)
    own_logits = jnp.where(own_chosen > 0, dot_t(router_w, normed_ffn), -jnp.inf)
    own_gates = jax.nn.softmax(own_logits, axis=0)
    if number == 0:
        other = other + (received[0],)
    mine = (
        jnp.arange(EXPERTS)[None, None, :] == first_expert + jnp.arange(count)[:, None, None]
    ).astype(jnp.float32)
    if has_kernels():
        *expert_state, slot_out = expert_forward(
            number, normed_ffn, pick, chosen, router_w, mine, own, other, 1 + number
        )
        if number == 0:
            *expert_state, slot_out, other_down = (*expert_state, slot_out)
            other = other[:2] + (other_down,)
    else:
        if number == 0:
            other = other[:2] + (swap(own[2]),)
        gate_w, up_w, down_w = by_layer(number, own, other)
        ffn_all = lax.all_gather(normed_ffn, TOKENS, axis=0, tiled=True)
        logits = dot_t(ffn_all, router_w).reshape(blocks, rows, EXPERTS)
        used = jnp.transpose(chosen, (0, 2, 1)) > 0
        gates = jax.nn.softmax(jnp.where(used, logits, -jnp.inf), axis=-1)
        slot_rows = choose(pick, ffn_all.reshape(blocks, rows, -1), count)
        mine_gates = jnp.einsum("bte,jxe->bjt", gates, mine, precision=lax.Precision.HIGHEST)
        slot_gates = jnp.sum(
            pick.reshape(blocks, count, CAP, rows).astype(jnp.float32) * mine_gates[:, :, None, :],
            axis=3,
        )
        slot_gates = jnp.transpose(slot_gates, (1, 0, 2)).reshape(count, -1, 1)
        gate_pre = each_dot("ecd,edf->ecf", slot_rows, gate_w)
        up_pre = each_dot("ecd,edf->ecf", slot_rows, up_w)
        scaled = low(slot_gates * jax.nn.silu(gate_pre) * up_pre)
        slot_out = low(each_dot("ecf,efd->ecd", scaled, down_w))
        expert_state = (slot_rows, gate_pre, up_pre, scaled, slot_gates)
    saved = (
        layer_in,
        attention_state,
        after_update,
        normed_ffn,
        own_gates,
        expert_state,
    )
    return (after_update, slot_out, saved, (own, other), received)


def token_sums(pick_t, slot_out, collective_id, *carry, spread=(), products=()):
    if has_kernels():
        sums, *received = combine(pick_t, slot_out, collective_id, carry, spread, products)
        return sums, received
    sums = give_back(pick_t, slot_out).astype(jnp.float32)
    sums = lax.psum_scatter(sums, TOKENS, scatter_dimension=0, tiled=True)
    received = [pass_to(array, to) for to, array in carry]
    grads = [
        low(each_dot("eck,ecn->ekn", left, right)) for left, rights in products for right in rights
    ]
    return sums, received + [spread_rows(array) for array in spread] + grads


def spread_rows(parts):
    return lax.all_to_all(parts, "seq", split_axis=0, concat_axis=0, tiled=True)


def expert_gradients(number, layer_grad, saved, picking, experts, *carry):
    chosen, pick, pick_t, first_expert = picking
    own, other = experts
    count = pick.shape[1] // CAP
    blocks, _, rows = chosen.shape
    slot_rows, gate_pre, up_pre, scaled, slot_gates = saved[-1]
    if has_kernels():
        slot_grads, gate_low, up_low, gate_term, slot_out, *received = expert_backward(
            number, low(layer_grad), pick, gate_pre, up_pre, slot_gates, own, other, 4 + number, carry
        )
        gate_term = gate_term[:, :, :1]
    else:
        gate_w, up_w, down_w = by_layer(number, own, other)
        grad_all = lax.all_gather(low(layer_grad), TOKENS, axis=0, tiled=True)
        slot_grads = choose(pick, grad_all.reshape(blocks, rows, -1), count)
        plain_grad = each_dot("ecd,efd->ecf", slot_grads, down_w)
        sigmoid = jax.nn.sigmoid(gate_pre)
        activated = gate_pre * sigmoid
        gate_term = jnp.sum(plain_grad * (activated * up_pre), axis=2, keepdims=True)
        hidden_grad = slot_gates * plain_grad
        gate_low = low(hidden_grad * up_pre * sigmoid * (1.0 + gate_pre * (1.0 - sigmoid)))
        up_low = low(hidden_grad * activated)
        slot_out = low(
            each_dot("ecf,edf->ecd", gate_low, gate_w) + each_dot("ecf,edf->ecd", up_low, up_w)
        )
        received = [pass_to(array, to) for to, array in carry]
    by_slot = jnp.transpose(gate_term.reshape(count, blocks, CAP), (1, 0, 2))
    gate_terms = jnp.sum(
        pick.reshape(blocks, count, CAP, rows).astype(jnp.float32) * by_slot[..., None], axis=2
    )
    gate_terms = lax.all_to_all(gate_terms, TOKENS, split_axis=0, concat_axis=0, tiled=True)
    products = ((slot_rows, (gate_low, up_low)), (scaled, (slot_grads,)))
    return slot_out, gate_terms, products, received


def backward_layer(
    number, layer_grad, normed_grad, gate_terms, saved, picking, weights, *carry, spread=()
):
    attn_scale, ffn_scale, qkv_w, out_w, router_w = weights
    chosen, pick, _, _ = picking
    (
        layer_in,
        (normed_all, mixed_t, heads, log_total),
        after_update,
        normed_ffn,
        own_gates,
        _,
    ) = saved
    rows = chosen.shape[2]
    gate_terms = jnp.sum(gate_terms.reshape(EXPERTS, -1, rows), axis=1)
    logit_grad = low(
        own_gates * (gate_terms - jnp.sum(own_gates * gate_terms, axis=0, keepdims=True))
    )
    router_grad = dot(logit_grad, normed_ffn)
    normed_grad = normed_grad + t_dot(logit_grad, router_w)
    after_part, ffn_gain_grad = jax.vjp(rms_norm, after_update, ffn_scale)[1](normed_grad)
    after_grad = after_part + layer_grad
    if has_kernels():
        normed_attn, branch_all, qkv_grad, *received = attention_backward_call(
            low(after_grad),
            qkv_w,
            out_w,
            wide_tables(4 * layer_in.shape[0]),
            heads,
            log_total,
            11 + number,
            carry,
            spread,
        )
        branch_all = branch_all.reshape(-1, layer_in.shape[1])
    else:
        branch_all = lax.all_gather(low(after_grad), "seq", axis=0, tiled=True)
        head_grad = low(dot_t(branch_all, out_w))
        qkv_grad = attention_backward(head_grad, *heads, log_total)
        normed_attn = low(dot_t(qkv_grad, qkv_w))
        normed_attn = lax.psum_scatter(normed_attn, "seq", scatter_dimension=0, tiled=True)
        received = [pass_to(array, to) for to, array in carry]
        received = received + [spread_rows(array) for array in spread]
    out_grad = dot(mixed_t, branch_all)
    qkv_weight_grad = t_dot(normed_all, qkv_grad)
    input_part, attn_gain_grad = jax.vjp(rms_norm, layer_in, attn_scale)[1](
        normed_attn.astype(jnp.float32)
    )
    small = [router_grad, attn_gain_grad[None], ffn_gain_grad[None]]
    small = jnp.concatenate(small + [jnp.zeros((128 - EXPERTS - 2, small[0].shape[1]))], axis=0)
    qkv_weight_grad = jnp.concatenate([low(qkv_weight_grad), low(small).T], axis=1)
    return (input_part + after_grad, (qkv_weight_grad, low(out_grad)), received)


def by_layer(number, own, other):
    is_own = lax.axis_index("section") == number
    return jax.tree.map(lambda mine, received: jnp.where(is_own, mine, received), own, other)


def body(
    hidden_in,
    out_grad,
    attn_gain,
    ffn_gain,
    query_matrix,
    key_matrix,
    value_matrix,
    output_matrix,
    router_matrix,
    w_gate,
    w_up,
    w_down,
    routes,
):
    section = lax.axis_index("section")
    dp, seq = lax.axis_size("dp"), lax.axis_size("seq")
    seq_index = lax.axis_index("seq")
    first = section == 0
    width = hidden_in.shape[3]
    depth = query_matrix.shape[1]

    layer_in = lax.dynamic_index_in_dim(hidden_in, section, 0, keepdims=False)[0]
    top_grad = lax.dynamic_index_in_dim(out_grad, section, 0, keepdims=False)[0]
    own_group = jnp.concatenate(
        [
            matrix[0].reshape(depth, seq, -1)
            for matrix in (query_matrix, key_matrix, value_matrix)
        ],
        axis=2,
    )
    own_group = jnp.transpose(own_group, (1, 0, 2))
    to_group = []
    for flat in range(dp * seq):
        to_group.append((flat, (flat % dp) * seq + flat // dp))
    from_group = [(target, source) for source, target in to_group]
    own_out = lax.ppermute(output_matrix[0], TOKENS, to_group)
    other_out = swap(own_out)
    local = w_gate.shape[1]
    hidden_units = w_gate.shape[3]
    if local >= seq:
        count, units = local // seq, hidden_units
        start, unit_start = seq_index * count, 0
    else:
        count, units = 1, hidden_units * local // seq
        start, unit_start = seq_index * local // seq, (seq_index % (seq // local)) * units
    first_expert = lax.axis_index("dp") * local + start
    if has_kernels():
        own_experts = (w_gate[0], w_up[0], w_down[0])
    else:
        own_experts = (
            lax.dynamic_slice(w_gate[0], (start, 0, unit_start), (count, width, units)),
            lax.dynamic_slice(w_up[0], (start, 0, unit_start), (count, width, units)),
            lax.dynamic_slice(w_down[0], (start, unit_start, 0), (count, units, width)),
        )
    small = jnp.concatenate([router_matrix[0].T, attn_gain, ffn_gain], axis=0)
    paths = routes[0, :, 0]
    if has_kernels():
        small = jnp.pad(small, ((0, -small.shape[0] % 16), (0, 256 - depth)))
        paths = low(jnp.transpose(paths, (0, 2, 1)).reshape(2 * TOP_K, -1))
        picks, picks_t, chosens, small, qkv_first, qkv_second, other_gate = prepare(
            jnp.concatenate([paths, small], axis=0),
            own_group,
            own_experts[0],
            count,
            hidden_in.shape[2],
            depth,
            13,
        )
        pickings = [(chosens[n], picks[n], picks_t[n], first_expert) for n in range(2)]
        qkv_second = lax.all_gather(
            qkv_second.reshape(seq * depth, -1), "dp", axis=0, tiled=True
        )
        qkv_layers = [qkv_first.reshape(width, -1), qkv_second]
    else:
        small = lax.all_gather(small, ("section", "dp", "seq"), axis=0, tiled=False)
        small = jnp.transpose(small.reshape(2, dp * seq, -1, depth), (0, 2, 1, 3))
        small = small.reshape(2, -1, width)
        paths = lax.all_gather(paths, ("section", "dp", "seq"), axis=0, tiled=False)
        paths = lax.dynamic_index_in_dim(paths, section, 1, keepdims=False)
        paths = paths.reshape(2, dp * seq, -1, TOP_K)
        pickings = [routing(paths[n], first_expert, count) + (first_expert,) for n in range(2)]
        other_gate = swap(own_experts[0])
        other_group = swap(own_group)
        qkv_layers = []
        for number in range(2):
            part = spread_rows(by_layer(number, own_group, other_group))
            part = part.reshape(seq * depth, -1)
            qkv_layers.append(lax.all_gather(part, "dp", axis=0, tiled=True))

    weights = []
    for number in range(2):
        out_w = lax.all_gather(
            by_layer(number, own_out, other_out), "dp", axis=0, tiled=True
        )
        weights.append(
            (
                small[number, EXPERTS].astype(jnp.float32),
                small[number, EXPERTS + 1].astype(jnp.float32),
                qkv_layers[number],
                out_w,
                small[number, :EXPERTS],
            )
        )

    def own_layer(pieces):
        return jnp.where(first, pieces[0], pieces[1])

    def both_micros(own, other):
        return jnp.stack([jnp.where(first, own, other), jnp.where(first, other, own)])[
            None, :, None
        ]

    def summed(own, other):
        return own_layer(own).astype(jnp.float32) + own_layer(other).astype(jnp.float32)

    def dp_sums(dense):
        return [lax.psum_scatter(part, "dp", scatter_dimension=0, tiled=True) for part in dense]

    def row_parts(piece, kind):
        if local >= seq:
            piece = piece.reshape(count, seq, piece.shape[1] // seq, -1)
            return jnp.transpose(piece, (1, 0, 2, 3))
        if kind < 2:
            return piece.reshape(seq, -1, units)
        piece = piece.reshape(-1, hidden_units // seq, width)
        share = seq // local
        parts = jnp.zeros((seq,) + piece.shape[1:], piece.dtype)
        return lax.dynamic_update_slice_in_dim(
            parts, piece, (seq_index % share) * piece.shape[0], axis=0
        )

    def whole_rows(parts, kind):
        parts = parts.astype(jnp.float32)
        if local < seq:
            parts = parts.reshape((local, seq // local) + parts.shape[1:])
            if kind < 2:
                parts = jnp.transpose(parts, (0, 2, 1, 3))
            else:
                parts = jnp.sum(parts, axis=1)
            return parts.reshape((local,) + parts.shape[1 : 2] + (-1,))[None]
        return parts.reshape((local,) + parts.shape[2:])[None]

    experts = (own_experts, (other_gate,))
    first_in = layer_in.astype(jnp.float32)
    updated, slot_out, first_saved, experts, _ = forward_layer(
        0, first_in, pickings[0], weights[0], experts, (None, own_experts[1])
    )
    sums, _ = token_sums(pickings[0][2], slot_out, 3)
    first_out = updated + sums
    second_updated, second_slots, second_saved, experts, (other_out,) = forward_layer(
        1, first_out, pickings[1], weights[1], experts, (0, first_out)
    )
    top_grad = top_grad.astype(jnp.float32)
    slot_out, gate_terms, products, _ = expert_gradients(
        1, top_grad, second_saved, pickings[1], experts
    )
    sums, second_experts = token_sums(pickings[1][2], slot_out, 6, products=products)
    middle_grad, second_dense, (second_gate,) = backward_layer(
        1, top_grad, sums, gate_terms, second_saved, pickings[1], weights[1], (1, second_experts[0])
    )
    slot_out, gate_terms, products, (second_up,) = expert_gradients(
        0, middle_grad, first_saved, pickings[0], experts, (1, second_experts[1])
    )
    (rows_in, (gate_low, up_low)), down_product = products
    gate_grad = low(each_dot("ecd,ecf->edf", rows_in, gate_low))
    slot_out, gate_grad, gate_terms = lax.optimization_barrier((slot_out, gate_grad, gate_terms))
    sums, (first_gate, second_down, *first_experts) = token_sums(
        pickings[0][2],
        slot_out,
        7,
        (0, gate_grad),
        (1, second_experts[2]),
        products=((rows_in, (up_low,)), down_product),
    )
    first_experts = [gate_grad, *first_experts]
    sums, *second_dense = lax.optimization_barrier((sums, *second_dense))
    second_dense = dp_sums(second_dense)
    gate_sum = low(summed((first_experts[0], second_experts[0]), (first_gate, second_gate)))
    bottom_grad, first_dense, (first_up, other_middle, gate_rows) = backward_layer(
        0,
        middle_grad,
        sums,
        gate_terms,
        first_saved,
        pickings[0],
        weights[0],
        (0, first_experts[1]),
        (1, middle_grad),
        spread=(row_parts(gate_sum, 0),),
    )
    up_sum = low(summed((first_experts[1], second_experts[1]), (first_up, second_up)))
    second_slots, *first_dense, second_dense[0], second_dense[1] = lax.optimization_barrier(
        (second_slots, *first_dense, *second_dense)
    )
    first_dense = dp_sums(first_dense)
    sums, (first_down, up_rows) = token_sums(
        pickings[1][2],
        second_slots,
        8,
        (0, first_experts[2]),
        spread=(row_parts(up_sum, 1),),
    )
    sums, *first_dense = lax.optimization_barrier((sums, *first_dense))
    second_out = second_updated + sums
    down_sum = low(summed((first_experts[2], second_experts[2]), (first_down, second_down)))
    own_cols, own_rows = [own_layer((first_dense[k], second_dense[k])) for k in range(2)]
    other_cols, other_rows = [own_layer((second_dense[k], first_dense[k])) for k in range(2)]
    if has_kernels():
        down_rows, cols_sum, out_sum, other_second, other_bottom = last_exchange(
            row_parts(down_sum, 2),
            own_cols.reshape(seq, depth, -1),
            other_cols.reshape(seq, depth, -1),
            own_rows,
            other_rows,
            14,
            ((1, second_out), (0, bottom_grad)),
        )
    else:
        down_rows = spread_rows(row_parts(down_sum, 2))
        cols_sum = low(own_cols.astype(jnp.float32) + swap(other_cols).astype(jnp.float32))
        cols_sum = spread_rows(cols_sum.reshape(seq, depth, -1))
        out_sum = low(own_rows.astype(jnp.float32) + swap(other_rows).astype(jnp.float32))
        out_sum = lax.ppermute(out_sum, TOKENS, from_group)
        other_second, other_bottom = pass_to(second_out, 1), pass_to(bottom_grad, 0)
    expert_sums = [whole_rows(rows, k) for k, rows in enumerate((gate_rows, up_rows, down_rows))]
    layer_outs = both_micros(
        own_layer((first_out, second_out)), own_layer((other_out, other_second))
    )
    section_grads = both_micros(
        own_layer((bottom_grad, middle_grad)), own_layer((other_bottom, other_middle))
    )
    qkv_sum, out_sum = cols_sum.astype(jnp.float32), out_sum.astype(jnp.float32)
    kv_width = KV_HEADS * HEAD_DIM // seq
    q_width = GROUP * kv_width
    qkv_width = q_width + 2 * kv_width
    small_sum = jnp.sum(qkv_sum[:, :, qkv_width:], axis=0)

    def columns(begin, end):
        return jnp.transpose(qkv_sum[:, :, begin:end], (1, 0, 2)).reshape(depth, -1)[None]

    return (
        layer_outs,
        section_grads,
        small_sum[:, EXPERTS][None],
        small_sum[:, EXPERTS + 1][None],
        columns(0, q_width),
        columns(q_width, q_width + kv_width),
        columns(q_width + kv_width, qkv_width),
        out_sum[None],
        small_sum[:, :EXPERTS][None],
        *expert_sums,
    )


def solution(mesh):
    return jax.shard_map(
        body,
        mesh=mesh,
        in_specs=(
            P(None, "dp", "seq", None),
            P(None, "dp", "seq", None),
            P("section", ("dp", "seq")),
            P("section", ("dp", "seq")),
            P("section", ("dp", "seq"), None),
            P("section", ("dp", "seq"), None),
            P("section", ("dp", "seq"), None),
            P("section", ("dp", "seq"), None),
            P("section", ("dp", "seq"), None),
            P("section", "dp", None, None),
            P("section", "dp", None, None),
            P("section", "dp", None, None),
            P("section", None, "dp", "seq", None),
        ),
        out_specs=(
            P("section", None, "dp", "seq", None),
            P("section", None, "dp", "seq", None),
            P("section", ("dp", "seq")),
            P("section", ("dp", "seq")),
            P("section", ("dp", "seq"), None),
            P("section", ("dp", "seq"), None),
            P("section", ("dp", "seq"), None),
            P("section", ("dp", "seq"), None),
            P("section", ("dp", "seq"), None),
            P("section", "dp", "seq", None),
            P("section", "dp", "seq", None),
            P("section", "dp", "seq", None),
        ),
        check_vma=False,
    )
```

```python
import jax
import jax.numpy as jnp
import numpy as np
from jax import lax
from jax.experimental import pallas as pl
from jax.experimental.pallas import tpu as pltpu
from jax.sharding import PartitionSpec as P

HEADS = 24
KV_HEADS = 8
HEAD_DIM = 64
TOP_K = 8
EXPERTS = 32
CAP = 80
GROUP = HEADS // KV_HEADS
TOKENS = ("dp", "seq")
PIECES = 4
MESH = pl.DeviceIdType.MESH
DMA = pltpu.SemaphoreType.DMA

epsilon = 1e-06


def dot(a, b):
    return jnp.dot(a, b, preferred_element_type=jnp.float32)


def dot_t(a, b):
    return lax.dot_general(a, b, (((1,), (1,)), ((), ())), preferred_element_type=jnp.float32)


def t_dot(a, b):
    return lax.dot_general(a, b, (((0,), (0,)), ((), ())), preferred_element_type=jnp.float32)


def low(v):
    return v.astype(jnp.bfloat16)


def swap(block):
    return lax.ppermute(block, "section", [(0, 1), (1, 0)])


def pass_to(block, section):
    return lax.ppermute(block, "section", [(1 - section, section)])


def rms_norm(values, norm_gain):
    return (
        values * lax.rsqrt(jnp.mean(values * values, axis=-1, keepdims=True) + epsilon) * norm_gain
    )


def rotary_tables(length):
    half_dim = HEAD_DIM // 2
    frequency = 10000.0 ** (-jnp.arange(half_dim, dtype=jnp.float32) * 2.0 / HEAD_DIM)
    angles = jnp.arange(length, dtype=jnp.float32)[:, None] * frequency[None, :]
    return (jnp.cos(angles)[:, None, :], jnp.sin(angles)[:, None, :])


def rotate(values, cos_table, sin_table):
    length = values.shape[0]
    split_heads = values.reshape(length, -1, HEAD_DIM)
    first_half = split_heads[..., : HEAD_DIM // 2]
    second_half = split_heads[..., HEAD_DIM // 2 :]
    turned = jnp.concatenate(
        [
            first_half * cos_table - second_half * sin_table,
            second_half * cos_table + first_half * sin_table,
        ],
        axis=-1,
    )
    return turned.reshape(length, -1)


def attention_forward(q_heads, k_heads, v_heads):
    length = q_heads.shape[0]
    local_kv = k_heads.shape[1] // HEAD_DIM
    cos_table, sin_table = rotary_tables(length)
    q_rot = low(rotate(q_heads.astype(jnp.float32), cos_table, sin_table)).reshape(
        length, local_kv, GROUP, HEAD_DIM
    )
    k_rot = low(rotate(k_heads.astype(jnp.float32), cos_table, sin_table)).reshape(
        length, local_kv, HEAD_DIM
    )
    values = v_heads.reshape(length, local_kv, HEAD_DIM)
    block_rows = min(512, length)
    outputs = []
    totals_list = []
    for first_row in range(0, length, block_rows):
        key_end = first_row + block_rows
        scores = (
            jnp.einsum(
                "qhgd,khd->hgqk",
                q_rot[first_row:key_end],
                k_rot[:key_end],
                preferred_element_type=jnp.float32,
            )
            * 0.125
        )
        causal = (first_row + jnp.arange(block_rows, dtype=jnp.int32))[:, None] >= jnp.arange(
            key_end, dtype=jnp.int32
        )[None, :]
        scores = jnp.where(causal, scores, -jnp.inf)
        row_peak = jnp.max(scores, axis=-1, keepdims=True)
        exponents = jnp.exp(scores - row_peak)
        totals = jnp.sum(exponents, axis=-1, keepdims=True)
        attended = jnp.einsum(
            "hgqk,khd->qhgd",
            low(exponents / totals),
            values[:key_end],
            preferred_element_type=jnp.float32,
        )
        outputs.append(low(attended).reshape(block_rows, -1))
        totals_list.append((row_peak + jnp.log(totals))[..., 0])
    return (jnp.concatenate(outputs, axis=0), jnp.stack(totals_list), q_rot, k_rot, values)


def attention_backward(head_grad, q_rot, k_rot, values, log_total):
    length, local_kv = q_rot.shape[:2]
    cos_table, sin_table = rotary_tables(length)
    block_rows = min(512, length)
    grad_rows = head_grad.reshape(length, local_kv, GROUP, HEAD_DIM)
    key_acc = jnp.zeros((length, local_kv, HEAD_DIM), jnp.float32)
    value_acc = jnp.zeros((length, local_kv, HEAD_DIM), jnp.float32)
    query_parts = []
    for block_number, first_row in enumerate(range(0, length, block_rows)):
        key_end = first_row + block_rows
        q_block = q_rot[first_row:key_end]
        grad_block = grad_rows[first_row:key_end]
        key_part = k_rot[:key_end]
        scores = (
            jnp.einsum("qhgd,khd->hgqk", q_block, key_part, preferred_element_type=jnp.float32)
            * 0.125
        )
        causal = (first_row + jnp.arange(block_rows, dtype=jnp.int32))[:, None] >= jnp.arange(
            key_end, dtype=jnp.int32
        )[None, :]
        scores = jnp.where(causal, scores, -jnp.inf)
        probs_full = jnp.exp(scores - log_total[block_number][..., None])
        prob_grad = jnp.einsum(
            "qhgd,khd->hgqk", grad_block, values[:key_end], preferred_element_type=jnp.float32
        )
        score_grad = probs_full * (
            prob_grad - jnp.sum(probs_full * prob_grad, axis=-1, keepdims=True)
        )
        score_low = low(score_grad)
        query_parts.append(
            jnp.einsum("hgqk,khd->qhgd", score_low, key_part, preferred_element_type=jnp.float32)
            * 0.125
        )
        key_acc = key_acc.at[:key_end].add(
            jnp.einsum("hgqk,qhgd->khd", score_low, q_block, preferred_element_type=jnp.float32)
            * 0.125
        )
        value_acc = value_acc.at[:key_end].add(
            jnp.einsum(
                "hgqk,qhgd->khd", low(probs_full), grad_block, preferred_element_type=jnp.float32
            )
        )
    query_all = jnp.concatenate(query_parts, axis=0).reshape(length, -1)
    query_grad = rotate(query_all, cos_table, -sin_table)
    key_grad = rotate(key_acc.reshape(length, -1), cos_table, -sin_table)
    return jnp.concatenate(
        [low(query_grad), low(key_grad), low(value_acc).reshape(length, -1)], axis=1
    )


def remote(src, dst, send_sem, recv_sem, **device):
    return pltpu.make_async_remote_copy(
        src_ref=src,
        dst_ref=dst,
        send_sem=send_sem,
        recv_sem=recv_sem,
        device_id=device,
        device_id_type=MESH,
    )


def greet(d, s, section=None, spread=False):
    barrier = pltpu.get_barrier_semaphore()

    def signal(**device):
        pl.semaphore_signal(barrier, inc=1, device_id=device, device_id_type=MESH)

    signal(seq=s ^ 1)
    signal(seq=s ^ 2)

    @pl.when(d > 0)
    def _():
        signal(dp=d - 1)

    @pl.when(d < 3)
    def _():
        signal(dp=d + 1)

    known = 3
    if section is not None:
        signal(section=1 - section)
        known = 4
    if spread:
        signal(seq=s ^ 3)
        known = known + 1
    inner = (d > 0) & (d < 3)

    @pl.when(inner)
    def _():
        pl.semaphore_wait(barrier, known + 1)

    @pl.when(jnp.logical_not(inner))
    def _():
        pl.semaphore_wait(barrier, known)


class Carried:
    def __init__(self, sections, sources, targets, sems):
        self.section = lax.axis_index("section")
        self.copies = []
        for k, (to, source, target) in enumerate(zip(sections, sources, targets)):
            copy = remote(source, target, sems.at[k, 0], sems.at[k, 1], section=1 - self.section)
            self.copies.append((to, copy))

    def start(self):
        for to, copy in self.copies:
            if to is None:
                copy.start()
            else:

                @pl.when(self.section != to)
                def _():
                    copy.start()

    def finish(self):
        for to, copy in self.copies:
            if to is None:
                copy.wait()
            else:

                @pl.when(self.section != to)
                def _():
                    copy.wait_send()

                @pl.when(self.section == to)
                def _():
                    copy.wait_recv()


class Spread:
    def __init__(self, source, target, sems):
        s = lax.axis_index("seq")
        self.local = pltpu.make_async_copy(source.at[s], target.at[s], sems.at[0, 0])
        self.copies = [
            remote(source.at[s ^ flip], target.at[s], sems.at[flip, 0], sems.at[flip, 1], seq=s ^ flip)
            for flip in (3, 2, 1)
        ]

    def start(self):
        for copy in self.copies:
            copy.start()
        self.local.start()

    def finish(self):
        self.local.wait()
        for copy in self.copies:
            copy.wait()


class SumSpread:
    def __init__(self, refs, target, held):
        self.refs, self.target = refs, target
        self.a, self.b, self.parts, self.loads, self.sems = held

    def copies(self, own, received):
        return [
            pltpu.make_async_copy(own, self.a, self.loads.at[0]),
            pltpu.make_async_copy(received, self.b, self.loads.at[1]),
        ]

    def load(self):
        own_0, own_1, in_0, in_1 = self.refs

        @pl.when(lax.axis_index("section") == 0)
        def _():
            for copy in self.copies(own_0, in_0):
                copy.start()

        @pl.when(lax.axis_index("section") == 1)
        def _():
            for copy in self.copies(own_1, in_1):
                copy.start()

    def start(self):
        for copy in self.copies(self.refs[0], self.refs[2]):
            copy.wait()
        group, count, rows, width = self.parts.shape
        chunk = 24576 // width
        for g in range(group):
            for j in range(count):

                @pl.loop(0, rows // chunk)
                def _(m):
                    here = pl.ds(pl.multiple_of(m * chunk, chunk), chunk)
                    there = pl.ds(pl.multiple_of(g * rows + m * chunk, chunk), chunk)
                    total = self.a[j, there, :].astype(jnp.float32)
                    total = total + self.b[j, there, :].astype(jnp.float32)
                    self.parts[g, j, here, :] = low(total)

        self.spread = Spread(self.parts, self.target, self.sems)
        self.spread.start()

    def finish(self):
        self.spread.finish()


def parts_shape(array):
    count, rows, width = array.shape
    return (4, count, rows // 4, width)


def sum_scratch(arrays):
    if not arrays:
        return []
    shape, bf = arrays[0].shape, jnp.bfloat16
    return [
        pltpu.VMEM(shape, bf),
        pltpu.VMEM(shape, bf),
        pltpu.VMEM(parts_shape(arrays[0]), bf),
        DMA((2,)),
        DMA((4, 2)),
    ]


def cost():
    return pl.CostEstimate(flops=80_000_000_000, bytes_accessed=100_000_000, transcendentals=0)


def gather_scratch(rows, width):
    return [
        pltpu.VMEM((16, rows, width), jnp.bfloat16),
        DMA(()),
        DMA((2, 4)),
        DMA((4,)),
        DMA((4,)),
        DMA((4,)),
        DMA((4, 2)),
        DMA((4, 2)),
    ]


def gather_blocks(x_ref, scratch, compute, carried=None, first=None, spread=False):
    land, lsem, zs, zr, ys, yr, cs, cr = scratch
    d, s = lax.axis_index("dp"), lax.axis_index("seq")

    def place(z, column):
        return land.at[z * 4 + column]

    def z_copy(src, z, right):
        target = d + 1 if right else d - 1
        return remote(src, place(z, s), zs.at[int(right), z], zr.at[z], dp=target)

    def y_copy(src, z):
        return remote(src, place(z, s), ys.at[z], yr.at[z], seq=s ^ 2)

    def core_copy(src, z, across):
        column = s ^ 2 if across else s
        return remote(src, place(z, column), cs.at[z, across], cr.at[z, across], seq=s ^ 1)

    greet(d, s, None if carried is None else carried.section, spread)
    if first is not None:
        first()
    own = pltpu.make_async_copy(x_ref, place(d, s), lsem)
    own.start()
    if carried is not None and first is None:
        carried.start()

    @pl.when(d < 3)
    def _():
        z_copy(x_ref, d, True).start()

    @pl.when(d > 0)
    def _():
        z_copy(x_ref, d, False).start()

    y_copy(x_ref, d).start()
    core_copy(x_ref, d, 0).start()
    own.wait()

    @pl.loop(0, 4)
    def _(i):
        @pl.when(i < 3)
        def _():
            left, right = d - (i + 1), d + (i + 1)

            @pl.when(left >= 0)
            def _():
                z_copy(place(left, s), left, True).wait_recv()

                @pl.when(d < 3)
                def _():
                    z_copy(place(left, s), left, True).start()

            @pl.when(right <= 3)
            def _():
                z_copy(place(right, s), right, False).wait_recv()

                @pl.when(d > 0)
                def _():
                    z_copy(place(right, s), right, False).start()

            following = d ^ (i + 1)
            y_copy(place(following, s), following).start()
            core_copy(place(following, s), following, 0).start()

        z = d ^ i
        y_copy(place(z, s ^ 2), z).wait_recv()
        core_copy(place(z, s ^ 2), z, 1).start()
        core_copy(place(z, s ^ 1), z, 0).wait_recv()
        core_copy(place(z, s ^ 3), z, 1).wait_recv()
        compute(z)

    for z in range(4):

        @pl.when((z <= d) & (d < 3))
        def _():
            z_copy(place(z, s), z, True).wait_send()

        @pl.when((z >= d) & (d > 0))
        def _():
            z_copy(place(z, s), z, False).wait_send()

        y_copy(place(z, s), z).wait_send()
        core_copy(place(z, s), z, 0).wait_send()
        core_copy(place(z, s), z, 1).wait_send()
    return land


def prepare_kernel(
    x_ref, group_ref, gate_ref,
    pick_out, pick_t_out, chosen_out, small_out, qkv_out, parts_out, gate_out,
    both, places, groups, parts, lsem, carry_sem, spread_sem, qs, qr, *gather
):
    d, s, section = lax.axis_index("dp"), lax.axis_index("seq"), lax.axis_index("section")
    known = x_ref.shape[0]
    count = pick_out.shape[2] // CAP
    rows = pick_out.shape[3]
    land = gather[0]
    part = both.at[pl.ds(pl.multiple_of(section * known, known), known)]
    swaps = Carried((None, None), (x_ref, group_ref), (part, groups.at[section]), carry_sem)
    gates = Carried((None,), (share(gate_ref),), (gate_out,), carry_sem.at[pl.ds(2, 1)])
    spreads = [Spread(groups.at[n], parts.at[n], spread_sem.at[n]) for n in range(2)]
    own_columns = pltpu.make_async_copy(parts.at[0], qkv_out.at[d], lsem.at[2])

    def along(src, z, right):
        target = d + 1 if right else d - 1
        return remote(src, qkv_out.at[z], qs.at[int(right), z], qr.at[z], dp=target)

    def first():
        swaps.start()
        own = [
            pltpu.make_async_copy(x_ref, part, lsem.at[0]),
            pltpu.make_async_copy(group_ref, groups.at[section], lsem.at[1]),
        ]
        for copy in own:
            copy.start()
        for copy in own:
            copy.wait()
        swaps.finish()
        gates.start()
        for side in spreads:
            side.start()
        spreads[0].finish()
        own_columns.start()

        @pl.when(d < 3)
        def _():
            along(parts.at[0], d, True).start()

        @pl.when(d > 0)
        def _():
            along(parts.at[0], d, False).start()

    def hop(h):
        @pl.when(d - h >= 0)
        def _():
            along(qkv_out.at[d - h], d - h, True).wait_recv()

            @pl.when(d < 3)
            def _():
                along(qkv_out.at[d - h], d - h, True).start()

        @pl.when(d + h <= 3)
        def _():
            along(qkv_out.at[d + h], d + h, False).wait_recv()

            @pl.when(d > 0)
            def _():
                along(qkv_out.at[d + h], d + h, False).start()

    gather_blocks(both, gather, lambda z: None, gates, first, True)
    hop(1)
    first_expert = (d * 4 + s) * count
    before = lax.broadcasted_iota(jnp.int32, (rows, rows), 0)
    before = low(before < lax.broadcasted_iota(jnp.int32, (rows, rows), 1))
    slot = lax.broadcasted_iota(jnp.int32, (CAP, rows), 0)
    expert = lax.broadcasted_iota(jnp.int32, (EXPERTS, rows), 0)
    lane = lax.broadcasted_iota(jnp.int32, (rows, count * CAP), 1)

    @pl.loop(0, 2)
    def _(layer):
        @pl.loop(0, 16)
        def _(b):
            paths = land[b, pl.ds(pl.multiple_of(layer * known, 16), 16), :].astype(jnp.float32)
            paths = jnp.where(section == 0, paths[:TOP_K], paths[TOP_K:]).astype(jnp.int32)
            chosen = expert == paths[0:1]
            for k in range(1, TOP_K):
                chosen = chosen | (expert == paths[k : k + 1])
            chosen_out[layer, b] = low(chosen)
            mine = [
                jnp.max((paths == first_expert + j).astype(jnp.float32), axis=0, keepdims=True)
                for j in range(count)
            ]
            mine = jnp.concatenate(mine + [jnp.zeros((8 - count, rows), jnp.float32)], axis=0)
            place = jnp.where(mine > 0.5, dot(low(mine), before), -10000.0)
            places[...] = place
            for j in range(count):
                pick_out[layer, b, j * CAP : (j + 1) * CAP, :] = low(
                    slot == place[j : j + 1].astype(jnp.int32)
                )
            turned = places[...].T.astype(jnp.int32)
            pick_t = turned[:, 0:1] == lane
            for j in range(1, count):
                pick_t = pick_t & (lane < j * CAP) | (turned[:, j : j + 1] == lane - j * CAP)
            pick_t_out[layer, b] = low(pick_t)

        depth = small_out.shape[2] // 16
        for b in range(16):
            small = land[b, pl.ds(pl.multiple_of(layer * known + 16, 16), known - 16), :]
            small_out[layer, :, b * depth : (b + 1) * depth] = small[:, :depth]

        @pl.when(layer == 0)
        def _():
            hop(2)

    hop(3)
    spreads[1].finish()
    layer_1 = pltpu.make_async_copy(parts.at[1], parts_out, lsem.at[0])
    layer_1.start()
    for z in range(4):

        @pl.when((z <= d) & (d < 3))
        def _():
            along(parts.at[0], z, True).wait_send()

        @pl.when((z >= d) & (d > 0))
        def _():
            along(parts.at[0], z, False).wait_send()

    own_columns.wait()
    layer_1.wait()
    gates.finish()


def prepare(x, group, gate, count, rows, depth, collective_id):
    known, width = x.shape
    bf = jnp.bfloat16
    anywhere = pl.BlockSpec(memory_space=pl.ANY)
    near = pl.BlockSpec(memory_space=pltpu.VMEM)
    return pl.pallas_call(
        prepare_kernel,
        out_shape=[
            jax.ShapeDtypeStruct((2, 16, count * CAP, rows), bf),
            jax.ShapeDtypeStruct((2, 16, rows, count * CAP), bf),
            jax.ShapeDtypeStruct((2, 16, EXPERTS, rows), bf),
            jax.ShapeDtypeStruct((2, known - 16, 16 * depth), bf),
            jax.ShapeDtypeStruct((4,) + group.shape, bf),
            jax.ShapeDtypeStruct(group.shape, bf),
            jax.ShapeDtypeStruct(share_shape(gate), bf),
        ],
        in_specs=[anywhere] * 3,
        out_specs=[near] * 4 + [anywhere] * 3,
        scratch_shapes=[
            pltpu.VMEM((2 * known, width), bf),
            pltpu.VMEM((8, rows), jnp.float32),
            pltpu.VMEM((2,) + group.shape, bf),
            pltpu.VMEM((2,) + group.shape, bf),
            DMA((3,)),
            DMA((3, 2)),
            DMA((2, 4, 2)),
            DMA((2, 4)),
            DMA((4,)),
        ]
        + gather_scratch(2 * known, width),
        compiler_params=pltpu.CompilerParams(
            collective_id=collective_id, has_side_effects=True, vmem_limit_bytes=60 << 20
        ),
        cost_estimate=cost(),
        name="prepare",
    )(x, group, gate)


def share(ref):
    count = ref.shape[0] // 4
    return ref.at[pl.ds(lax.axis_index("seq") * count, count)]


def share_shape(array):
    return (array.shape[0] // 4,) + array.shape[1:]


def pick_weights(own_refs, other_refs, held, sems, own_layer):
    own_refs = [share(ref) for ref in own_refs]
    mine = lax.axis_index("section") == own_layer

    @pl.when(mine)
    def _():
        for k, ref in enumerate(own_refs):
            pltpu.make_async_copy(ref, held[k], sems.at[k]).start()

    @pl.when(jnp.logical_not(mine))
    def _():
        for k, ref in enumerate(other_refs):
            pltpu.make_async_copy(ref, held[k], sems.at[k]).start()

    def ready(k):
        pltpu.make_async_copy(own_refs[k], held[k], sems.at[k]).wait()

    return ready


def expert_forward_kernel(
    layer, x_ref, pick_ref, chosen_ref, router_ref, mine_ref,
    wg_own, wu_own, wd_own, wg_other, wu_other, wd_other,
    rows_out, gate_out, up_out, hidden_out, slot_gate_out, y_out,
    wg, wu, wd, rows, gate, up, hidden, slot_gate, y, wsem, osem, carry_sem, *gather
):
    count = wg.shape[0]
    carried = None
    if layer == 0:
        carried = Carried((None,), (share(wd_own),), (wd_other,), carry_sem)
        ready = pick_weights((wg_own, wu_own), (wg_other, wu_other), (wg, wu), wsem, layer)
    else:
        ready = pick_weights(
            (wg_own, wu_own, wd_own), (wg_other, wu_other, wd_other), (wg, wu, wd), wsem, layer
        )
    land = gather[0]
    d = lax.axis_index("dp")

    def outs(z):
        part = pl.ds(z * 4 * CAP, 4 * CAP)
        return [
            pltpu.make_async_copy(held.at[:, part], out.at[:, part], osem.at[k, z])
            for k, (held, out) in enumerate(
                ((rows, rows_out), (gate, gate_out), (up, up_out), (hidden, hidden_out), (slot_gate, slot_gate_out))
            )
        ] + [pltpu.make_async_copy(y.at[pl.ds(z * 4, 4)], y_out.at[pl.ds(z * 4, 4)], osem.at[5, z])]

    def down(z):
        part = pl.ds(z * 4 * CAP, 4 * CAP)

        @pl.loop(0, count)
        def _(j):
            result = low(dot(hidden[j, part, :], wd[j]))
            for q in range(4):
                y[z * 4 + q, pl.ds(j * CAP, CAP), :] = result[q * CAP : (q + 1) * CAP]

    def compute(z):
        @pl.when(z == d)
        def _():
            for k in range(2 if layer == 0 else 3):
                ready(k)

        for q in range(4):
            b = z * 4 + q
            picked = low(dot(pick_ref[b], land[b]))
            for j in range(count):
                rows[j, pl.ds(b * CAP, CAP), :] = picked[j * CAP : (j + 1) * CAP]
        part = pl.ds(z * 4 * CAP, 4 * CAP)

        @pl.loop(0, count)
        def _(j):
            x = rows[j, part, :]
            g = dot(x, wg[j])
            u = dot(x, wu[j])
            logits = dot_t(x, router_ref[...])
            for q in range(4):
                b = z * 4 + q
                slots = slice(q * CAP, (q + 1) * CAP)
                seen = dot_t(pick_ref[b, pl.ds(j * CAP, CAP), :], chosen_ref[b])
                masked = jnp.where(seen > 0.5, logits[slots], -1e30)
                power = jnp.exp(masked - jnp.max(masked, axis=1, keepdims=True))
                own = jnp.sum(power * mine_ref[j], axis=1, keepdims=True)
                value = own / jnp.sum(power, axis=1, keepdims=True)
                slot_gate[j, pl.ds(b * CAP, CAP), :] = jnp.broadcast_to(value, (CAP, 128))
            gate[j, part, :] = low(g)
            up[j, part, :] = low(u)
            h = low(g * jax.nn.sigmoid(g) * u * slot_gate[j, part, :][:, :1])
            hidden[j, part, :] = h

        if layer != 0:
            down(z)
        for copy in outs(z)[: 5 if layer == 0 else 6]:
            copy.start()

    gather_blocks(x_ref, gather, compute, carried)
    if layer == 0:
        carried.finish()
        ready = pick_weights((wd_own,), (wd_other,), (wd,), wsem, layer)
        ready(0)
        for z in range(4):
            down(z)
            outs(z)[5].start()
    for z in range(4):
        for copy in outs(z):
            copy.wait()


def expert_forward(layer, x, pick, chosen, router, mine, own, other, collective_id):
    count, width, units = share_shape(own[0])
    rows = x.shape[0]
    slots = 16 * CAP
    bf = jnp.bfloat16
    anywhere = pl.BlockSpec(memory_space=pl.ANY)
    near = pl.BlockSpec(memory_space=pltpu.VMEM)
    results = [
        ((count, slots, width), bf),
        ((count, slots, units), bf),
        ((count, slots, units), bf),
        ((count, slots, units), bf),
        ((count, slots, 128), jnp.float32),
        ((16, count * CAP, width), bf),
    ]

    def kernel(*refs):
        if layer == 0:
            refs = refs[:10] + refs[16:17] + refs[10:16] + refs[17:]
        expert_forward_kernel(layer, *refs)

    shapes = [jax.ShapeDtypeStruct(*result) for result in results]
    if layer == 0:
        shapes.append(jax.ShapeDtypeStruct(share_shape(own[2]), bf))
        other = other[:2]
    operands = (x, pick, chosen, router, mine, *own, *other)
    return pl.pallas_call(
        kernel,
        out_shape=shapes,
        in_specs=[anywhere, near, near, near, near] + [anywhere] * (len(operands) - 5),
        out_specs=[anywhere] * len(shapes),
        scratch_shapes=[pltpu.VMEM(share_shape(weight), bf) for weight in own]
        + [pltpu.VMEM(*result) for result in results]
        + [DMA((3,)), DMA((6, 4)), DMA((1, 2))]
        + gather_scratch(rows, width),
        compiler_params=pltpu.CompilerParams(
            collective_id=collective_id, has_side_effects=True, vmem_limit_bytes=60 << 20
        ),
        cost_estimate=cost(),
        name="expert_forward",
    )(*operands)


class Products:
    def __init__(self, pairs, outs, held, sems):
        self.units = []
        count = outs[0].shape[0]
        for j in range(count):
            at, out_at = 0, 0
            for left, rights in pairs:
                first = at
                loads = [(left, at)] + [(right, at + 1 + k) for k, right in enumerate(rights)]
                at += len(loads)
                for k in range(len(rights)):
                    self.units.append((j, first, first + 1 + k, out_at, loads, k == 0, k + 1 == len(rights)))
                    out_at += 1
        self.count, self.pairs, self.outs, self.held, self.sems = count, at, outs, held, sems

    def load(self, j, source, at):
        return pltpu.make_async_copy(source.at[j], self.held[at], self.sems.at[at])

    def store(self, j, k):
        at = self.pairs + k
        return pltpu.make_async_copy(self.held[at], self.outs[k].at[j], self.sems.at[at])

    def start(self):
        for j, _, _, _, loads, first, _ in self.units:
            if j == 0 and first:
                for source, at in loads:
                    self.load(0, source, at).start()

    def step(self, i):
        for number, (j, left, right, out, loads, first, last) in enumerate(self.units):

            @pl.when(i == number * (PIECES // 2))
            def _():
                if first:
                    for source, at in loads:
                        self.load(j, source, at).wait()
                if j > 0:
                    self.store(j - 1, out).wait()
                a, b, c = self.held[left], self.held[right], self.held[self.pairs + out]

                @pl.loop(0, a.shape[1] // 256)
                def _(m):
                    columns = pl.ds(pl.multiple_of(m * 256, 256), 256)
                    c[columns, :] = low(t_dot(a[:, columns], b[...]))

                self.store(j, out).start()
                if last and j + 1 < self.count:
                    for source, at in loads:
                        self.load(j + 1, source, at).start()

    def finish(self):
        for k in range(len(self.outs)):
            self.store(self.count - 1, k).wait()


def combine_kernel(sections, spreads, pairs, pick_ref, y_ref, *refs):
    kept = len(sections)
    sources, refs = refs[:kept], refs[kept:]
    spread_sources, refs = refs[:spreads], refs[spreads:]
    spreads = spreads // 4
    factors = []
    for rights in pairs:
        factors.append((refs[0], refs[1 : 1 + rights]))
        refs = refs[1 + rights :]
    out_ref, *refs = refs
    targets, refs = refs[:kept], refs[kept:]
    spread_targets, refs = refs[:spreads], refs[spreads:]
    products = sum(pairs)
    product_outs, refs = refs[:products], refs[products:]
    y, sent, own, core_in, y_in, z_in, lsem, zs, zr, ys, yr, cs, cr, carry_sem, *refs = refs
    held, refs = refs[: 5 * spreads], refs[5 * spreads :]
    work = Products(factors, product_outs, refs[:-1], refs[-1]) if pairs else None
    carried = Carried(sections, sources, targets, carry_sem)
    spread = [SumSpread(spread_sources, spread_targets[0], held)] if spreads else []
    for side in spread:
        side.load()
    d, s = lax.axis_index("dp"), lax.axis_index("seq")
    piece = out_ref.shape[0] // PIECES

    def loaded(b):
        return pltpu.make_async_copy(y_ref.at[b], y.at[b], lsem.at[b])

    def column(across, other_core):
        return s ^ (2 * across) ^ other_core

    for i in range(4):
        z = d ^ (3 - i)
        for across in (1, 0):
            for other_core in (1, 0):
                loaded(z * 4 + column(across, other_core)).start()
    greet(d, s, carried.section, spreads > 0)
    carried.start()

    def rows(k):
        return pl.ds(pl.multiple_of(k * piece, piece), piece)

    def partial_sum(z, k, across, other_core):
        b = z * 4 + column(across, other_core)

        @pl.when(k == 0)
        def _():
            loaded(b).wait()

        return dot(pick_ref[b, rows(k), :], y[b])

    def core_copy(z, k, across):
        return remote(
            sent.at[z, across, rows(k)],
            core_in.at[z, across, rows(k)],
            cs.at[z, k, across],
            cr.at[z, k, across],
            seq=s ^ 1,
        )

    def y_copy(z, k):
        return remote(own.at[z, 1, rows(k)], y_in.at[z, rows(k)], ys.at[z, k], yr.at[z, k], seq=s ^ 2)

    def z_copy(z, k, right):
        target = d + 1 if right else d - 1
        return remote(
            own.at[z, 0, rows(k)],
            z_in.at[int(right), z, rows(k)],
            zs.at[z, k],
            zr.at[int(right), z, k],
            dp=target,
        )

    def start(i):
        z, k = d ^ (3 - i // PIECES), i % PIECES
        sent[z, 1, rows(k), :] = low(partial_sum(z, k, 1, 1))
        core_copy(z, k, 1).start()
        total = partial_sum(z, k, 1, 0)
        core_copy(z, k, 1).wait_recv()
        own[z, 1, rows(k), :] = low(total + core_in[z, 1, rows(k), :].astype(jnp.float32))
        y_copy(z, k).start()
        sent[z, 0, rows(k), :] = low(partial_sum(z, k, 0, 1))
        core_copy(z, k, 0).start()

    start(0)
    for side in spread:
        side.start()
    if work:
        work.start()

    @pl.loop(0, 4 * PIECES)
    def _(i):
        @pl.when(i < 4 * PIECES - 1)
        def _():
            start(i + 1)

        if work:
            work.step(i)

        z, k = d ^ (3 - i // PIECES), i % PIECES
        total = partial_sum(z, k, 0, 0)
        core_copy(z, k, 0).wait_recv()
        total = total + core_in[z, 0, rows(k), :].astype(jnp.float32)
        y_copy(z, k).wait_recv()
        total = total + y_in[z, rows(k), :].astype(jnp.float32)

        @pl.when(z < d)
        def _():
            @pl.when(d < 3)
            def _():
                z_copy(z, k, False).wait_recv()
                own[z, 0, rows(k), :] = low(total + z_in[0, z, rows(k), :].astype(jnp.float32))

            @pl.when(d == 3)
            def _():
                own[z, 0, rows(k), :] = low(total)

            z_copy(z, k, False).start()

        @pl.when(z > d)
        def _():
            @pl.when(d > 0)
            def _():
                z_copy(z, k, True).wait_recv()
                own[z, 0, rows(k), :] = low(total + z_in[1, z, rows(k), :].astype(jnp.float32))

            @pl.when(d == 0)
            def _():
                own[z, 0, rows(k), :] = low(total)

            z_copy(z, k, True).start()

        @pl.when(z == d)
        def _():
            out_ref[rows(k), :] = total

    for k in range(PIECES):

        @pl.when(d < 3)
        def _():
            z_copy(d, k, False).wait_recv()
            out_ref[rows(k), :] += z_in[0, d, rows(k), :].astype(jnp.float32)

        @pl.when(d > 0)
        def _():
            z_copy(d, k, True).wait_recv()
            out_ref[rows(k), :] += z_in[1, d, rows(k), :].astype(jnp.float32)

    for z in range(4):
        for k in range(PIECES):
            core_copy(z, k, 0).wait_send()
            core_copy(z, k, 1).wait_send()
            y_copy(z, k).wait_send()

            @pl.when(z < d)
            def _():
                z_copy(z, k, False).wait_send()

            @pl.when(z > d)
            def _():
                z_copy(z, k, True).wait_send()

    carried.finish()
    for side in spread:
        side.finish()
    if work:
        work.finish()


def combine(pick_t, y, collective_id, carry, spread=(), products=()):
    rows, width = pick_t.shape[1], y.shape[2]
    anywhere = pl.BlockSpec(memory_space=pl.ANY)
    near = pl.BlockSpec(memory_space=pltpu.VMEM)
    sections = tuple(to for to, _ in carry)
    arrays = [array for _, array in carry]

    carries = [jax.ShapeDtypeStruct(array.shape, array.dtype) for array in arrays]
    if spread:
        carries.append(jax.ShapeDtypeStruct(parts_shape(spread[0]), jnp.bfloat16))
    arrays = arrays + list(spread)
    pairs = [len(rights) for _, rights in products]
    factors = [factor for left, rights in products for factor in (left, *rights)]
    outs = [
        jax.ShapeDtypeStruct((left.shape[0], left.shape[2], right.shape[2]), jnp.bfloat16)
        for left, rights in products
        for right in rights
    ]
    held = [pltpu.VMEM(array.shape[1:], jnp.bfloat16) for array in factors + outs]
    held = held + [DMA((len(held),))] if held else []

    def kernel(*refs):
        combine_kernel(sections, len(spread), pairs, *refs)

    def blocks(*lead):
        return pltpu.VMEM(lead + (rows, width), jnp.bfloat16)

    return pl.pallas_call(
        kernel,
        out_shape=[jax.ShapeDtypeStruct((rows, width), jnp.float32)]
        + carries
        + outs,
        in_specs=[near, anywhere] + [anywhere] * (len(arrays) + len(factors)),
        out_specs=[near] + [anywhere] * (len(carries) + len(outs)),
        scratch_shapes=[
            pltpu.VMEM(y.shape, jnp.bfloat16),
            blocks(4, 2),
            blocks(4, 2),
            blocks(4, 2),
            blocks(4),
            blocks(2, 4),
            DMA((16,)),
            DMA((4, PIECES)),
            DMA((2, 4, PIECES)),
            DMA((4, PIECES)),
            DMA((4, PIECES)),
            DMA((4, PIECES, 2)),
            DMA((4, PIECES, 2)),
            DMA((max(1, len(carry)), 2)),
        ]
        + sum_scratch(spread)
        + held,
        compiler_params=pltpu.CompilerParams(
            collective_id=collective_id, has_side_effects=True, vmem_limit_bytes=60 << 20
        ),
        cost_estimate=cost(),
        name="combine",
    )(pick_t, y, *arrays, *factors)


def expert_backward_kernel(
    layer, sections, x_ref, pick_ref, gate_in, up_in, slot_gate_in,
    wg_own, wu_own, wd_own, wg_other, wu_other, wd_other, *refs
):
    kept = len(sections)
    sources, refs = refs[:kept], refs[kept:]
    rows_out, gate_out, up_out, term_out, y_out, *refs = refs
    targets, refs = refs[:kept], refs[kept:]
    wg, wu, wd, rows, gate, up, slot_gate, y, wsem, isem, osem, carry_sem, *gather = refs
    carried = Carried(sections, sources, targets, carry_sem)
    count = wg.shape[0]
    ready = pick_weights(
        (wg_own, wu_own, wd_own), (wg_other, wu_other, wd_other), (wg, wu, wd), wsem, layer
    )
    land = gather[0]
    d = lax.axis_index("dp")
    ins = [
        pltpu.make_async_copy(src, held, isem.at[k])
        for k, (src, held) in enumerate(((gate_in, gate), (up_in, up), (slot_gate_in, slot_gate)))
    ]
    for copy in ins:
        copy.start()

    def outs(z):
        part = pl.ds(z * 4 * CAP, 4 * CAP)
        return [
            pltpu.make_async_copy(held.at[:, part], out.at[:, part], osem.at[k, z])
            for k, (held, out) in enumerate(
                ((rows, rows_out), (gate, gate_out), (up, up_out), (slot_gate, term_out))
            )
        ] + [pltpu.make_async_copy(y.at[pl.ds(z * 4, 4)], y_out.at[pl.ds(z * 4, 4)], osem.at[4, z])]

    def compute(z):
        @pl.when(z == d)
        def _():
            for k in range(3):
                ready(k)
            for copy in ins:
                copy.wait()

        for q in range(4):
            b = z * 4 + q
            picked = low(dot(pick_ref[b], land[b]))
            for j in range(count):
                rows[j, pl.ds(b * CAP, CAP), :] = picked[j * CAP : (j + 1) * CAP]
        part = pl.ds(z * 4 * CAP, 4 * CAP)

        @pl.loop(0, count)
        def _(j):
            plain = dot_t(rows[j, part, :], wd[j])
            g = gate[j, part, :].astype(jnp.float32)
            u = up[j, part, :].astype(jnp.float32)
            sigmoid = jax.nn.sigmoid(g)
            active = g * sigmoid
            term = jnp.sum(plain * (active * u), axis=1, keepdims=True)
            grad = plain * slot_gate[j, part, :][:, :1]
            dg = low(grad * u * sigmoid * (1.0 + g * (1.0 - sigmoid)))
            du = low(grad * active)
            slot_gate[j, part, :] = jnp.broadcast_to(term, (4 * CAP, 128))
            gate[j, part, :] = dg
            up[j, part, :] = du
            result = low(dot_t(dg, wg[j]) + dot_t(du, wu[j]))
            for q in range(4):
                y[z * 4 + q, pl.ds(j * CAP, CAP), :] = result[q * CAP : (q + 1) * CAP]

        for copy in outs(z):
            copy.start()

    gather_blocks(x_ref, gather, compute, carried)
    carried.finish()
    for z in range(4):
        for copy in outs(z):
            copy.wait()


def expert_backward(layer, x, pick, gate, up, slot_gate, own, other, collective_id, carry):
    count, width, units = share_shape(own[0])
    rows = x.shape[0]
    slots = 16 * CAP
    bf = jnp.bfloat16
    anywhere = pl.BlockSpec(memory_space=pl.ANY)
    near = pl.BlockSpec(memory_space=pltpu.VMEM)
    results = [
        ((count, slots, width), bf),
        ((count, slots, units), bf),
        ((count, slots, units), bf),
        ((count, slots, 128), jnp.float32),
        ((16, count * CAP, width), bf),
    ]
    sections = tuple(to for to, _ in carry)
    arrays = [array for _, array in carry]

    def kernel(*refs):
        expert_backward_kernel(layer, sections, *refs)

    return pl.pallas_call(
        kernel,
        out_shape=[jax.ShapeDtypeStruct(*result) for result in results]
        + [jax.ShapeDtypeStruct(array.shape, array.dtype) for array in arrays],
        in_specs=[anywhere, near] + [anywhere] * (9 + len(arrays)),
        out_specs=[anywhere] * (5 + len(arrays)),
        scratch_shapes=[pltpu.VMEM(share_shape(weight), bf) for weight in own]
        + [pltpu.VMEM(*result) for result in results]
        + [DMA((3,)), DMA((3,)), DMA((5, 4)), DMA((max(1, len(arrays)), 2))]
        + gather_scratch(rows, width),
        compiler_params=pltpu.CompilerParams(
            collective_id=collective_id, has_side_effects=True, vmem_limit_bytes=60 << 20
        ),
        cost_estimate=cost(),
        name="expert_backward",
    )(x, pick, gate, up, slot_gate, *own, *other, *arrays)


def rope(x, cos_table, sin_table):
    lane = lax.broadcasted_iota(jnp.int32, x.shape, 1)
    turned = jnp.where(lane % HEAD_DIM < HEAD_DIM // 2, pltpu.roll(x, 128 - HEAD_DIM // 2, 1), pltpu.roll(x, HEAD_DIM // 2, 1))
    return x * cos_table + turned * sin_table


def seq_greet(s, section, spread=False):
    barrier = pltpu.get_barrier_semaphore()
    devices = [dict(seq=s ^ 1), dict(seq=s ^ 2), dict(section=1 - section)]
    if spread:
        devices.append(dict(seq=s ^ 3))
    for device in devices:
        pl.semaphore_signal(barrier, inc=1, device_id=device, device_id_type=MESH)
    pl.semaphore_wait(barrier, len(devices))


def seq_scratch(rows, width):
    return [
        pltpu.VMEM((4, rows, width), jnp.bfloat16),
        pltpu.VMEM((2, rows, width), jnp.bfloat16),
        pltpu.VMEM((2, rows, width), jnp.bfloat16),
        pltpu.VMEM((rows, width), jnp.bfloat16),
        pltpu.VMEM((rows, width), jnp.bfloat16),
        DMA(()),
        DMA((4, 2)),
        DMA((3, 2)),
    ]


class Line:
    def __init__(self, scratch):
        self.land, self.sent, self.core_in, self.y_sent, self.y_in, self.lsem, self.ag, self.rs = scratch
        self.s = lax.axis_index("seq")

    def hop(self, src, dst, sems, k, flip):
        return remote(src, dst, sems.at[k, 0], sems.at[k, 1], seq=self.s ^ flip)

    def gather(self, x_ref, use):
        s, land = self.s, self.land
        own = pltpu.make_async_copy(x_ref, land.at[s], self.lsem)
        own.start()
        over = self.hop(x_ref, land.at[s], self.ag, 0, 2)
        beside = self.hop(x_ref, land.at[s], self.ag, 1, 1)
        over.start()
        beside.start()
        own.wait()
        use(s)
        beside.wait_recv()
        use(s ^ 1)
        over.wait_recv()
        further = self.hop(land.at[s ^ 2], land.at[s ^ 2], self.ag, 2, 1)
        further.start()
        use(s ^ 2)
        further.wait_recv()
        use(s ^ 3)
        over.wait_send()
        beside.wait_send()
        further.wait_send()

    def hand_over(self, t, partial, out_ref):
        relation = t ^ self.s

        @pl.when(relation == 3)
        def _():
            self.sent[0] = low(partial[...])
            self.hop(self.sent.at[0], self.core_in.at[0], self.rs, 0, 1).start()

        @pl.when(relation == 2)
        def _():
            self.hop(self.sent.at[0], self.core_in.at[0], self.rs, 0, 1).wait_recv()
            self.y_sent[...] = low(partial[...] + self.core_in[0].astype(jnp.float32))
            self.hop(self.y_sent, self.y_in, self.rs, 1, 2).start()

        @pl.when(relation == 1)
        def _():
            self.sent[1] = low(partial[...])
            self.hop(self.sent.at[1], self.core_in.at[1], self.rs, 2, 1).start()

        @pl.when(relation == 0)
        def _():
            out_ref[...] = partial[...]

    def finish(self, out_ref):
        self.hop(self.sent.at[1], self.core_in.at[1], self.rs, 2, 1).wait()
        out_ref[...] += self.core_in[1].astype(jnp.float32)
        self.hop(self.y_sent, self.y_in, self.rs, 1, 2).wait()
        out_ref[...] += self.y_in[...].astype(jnp.float32)
        self.hop(self.sent.at[0], self.core_in.at[0], self.rs, 0, 1).wait_send()


def attention_forward_kernel(sections, x_ref, qkv_ref, wo_ref, cos_ref, sin_ref, *refs):
    kept = len(sections)
    sources, refs = refs[:kept], refs[kept:]
    sources = [share(ref) if to is None else ref for to, ref in zip(sections, sources)]
    out_ref, all_out, heads_out, lse_out, ot_out, *refs = refs
    targets, refs = refs[:kept], refs[kept:]
    wqkv, wo, heads, lse, ot, partial, wsem, osem, carry_sem, *line = refs
    line = Line(line)
    carried = Carried(sections, sources, targets, carry_sem)
    s = line.s
    rows = out_ref.shape[0]
    kv = heads.shape[0] // (GROUP + 2)
    queries = GROUP * kv
    loads = [pltpu.make_async_copy(qkv_ref, wqkv, wsem.at[0]), pltpu.make_async_copy(wo_ref, wo, wsem.at[1])]
    for load in loads:
        load.start()
    seq_greet(s, carried.section)
    carried.start()
    lse[...] = jnp.zeros_like(lse)

    def project(t):
        part = pl.ds(pl.multiple_of(t * rows, rows), rows)

        @pl.when(t == s)
        def _():
            loads[0].wait()

        qkv = low(dot(line.land[t], wqkv[...]))
        for chunk in range((queries + kv) // 2):
            x = qkv[:, chunk * 128 : (chunk + 1) * 128].astype(jnp.float32)
            x = low(rope(x, cos_ref[part, :], sin_ref[part, :]))
            heads[2 * chunk, part, :] = x[:, :HEAD_DIM]
            heads[2 * chunk + 1, part, :] = x[:, HEAD_DIM:]
        for j in range(kv):
            begin = (queries + kv + j) * HEAD_DIM
            heads[queries + kv + j, part, :] = qkv[:, begin : begin + HEAD_DIM]

    line.gather(x_ref, project)
    saves = [pltpu.make_async_copy(line.land, all_out, osem.at[0]), pltpu.make_async_copy(heads, heads_out, osem.at[1])]
    for save in saves:
        save.start()
    loads[1].wait()

    def attend(block):
        keys = (block + 1) * rows
        columns = slice(block * rows, (block + 1) * rows)

        @pl.loop(0, queries)
        def _(h):
            j = h // GROUP
            scores = dot_t(heads[queries + j, :keys, :], heads[h, columns, :]) * 0.125
            key_at = lax.broadcasted_iota(jnp.int32, scores.shape, 0)
            query_at = lax.broadcasted_iota(jnp.int32, scores.shape, 1) + block * rows
            scores = jnp.where(key_at <= query_at, scores, -jnp.inf)
            peak = jnp.max(scores, axis=0, keepdims=True)
            power = jnp.exp(scores - peak)
            total = jnp.sum(power, axis=0, keepdims=True)
            attended = t_dot(heads[queries + kv + j, :keys, :], low(power / total))
            ot[pl.ds(pl.multiple_of(h * HEAD_DIM, HEAD_DIM), HEAD_DIM), columns] = low(attended)
            lse[pl.ds(h, 1), columns] = peak + jnp.log(total)

        partial[...] = t_dot(ot[:, columns], wo[...])

    @pl.loop(0, 4)
    def _(i):
        t = s ^ (3 - i)
        for block in range(4):

            @pl.when(t == block)
            def _():
                attend(block)

        line.hand_over(t, partial, out_ref)

    saves += [pltpu.make_async_copy(lse, lse_out, osem.at[2]), pltpu.make_async_copy(ot, ot_out, osem.at[3])]
    for save in saves[2:]:
        save.start()
    line.finish(out_ref)
    carried.finish()
    for save in saves:
        save.wait()


def attention_forward_call(x, qkv_w, out_w, tables, collective_id, carry):
    rows, width = x.shape
    local_heads = qkv_w.shape[1] // HEAD_DIM
    bf, f32 = jnp.bfloat16, jnp.float32
    anywhere = pl.BlockSpec(memory_space=pl.ANY)
    near = pl.BlockSpec(memory_space=pltpu.VMEM)
    sections = tuple(to for to, _ in carry)
    arrays = [array for _, array in carry]
    results = [
        ((rows, width), f32),
        ((4, rows, width), bf),
        ((local_heads, 4 * rows, HEAD_DIM), bf),
        ((8, 4 * rows), f32),
        ((out_w.shape[0], 4 * rows), bf),
    ]

    def kernel(*refs):
        attention_forward_kernel(sections, *refs)

    return pl.pallas_call(
        kernel,
        out_shape=[jax.ShapeDtypeStruct(*result) for result in results]
        + [
            jax.ShapeDtypeStruct(share_shape(array) if to is None else array.shape, array.dtype)
            for to, array in carry
        ],
        in_specs=[anywhere] * 3 + [near] * 2 + [anywhere] * len(arrays),
        out_specs=[near] + [anywhere] * (4 + len(arrays)),
        scratch_shapes=[
            pltpu.VMEM(qkv_w.shape, bf),
            pltpu.VMEM(out_w.shape, bf),
            pltpu.VMEM(*results[2]),
            pltpu.VMEM(*results[3]),
            pltpu.VMEM(*results[4]),
            pltpu.VMEM((rows, width), f32),
            DMA((2,)),
            DMA((4,)),
            DMA((max(1, len(arrays)), 2)),
        ]
        + seq_scratch(rows, width),
        compiler_params=pltpu.CompilerParams(
            collective_id=collective_id, has_side_effects=True, vmem_limit_bytes=60 << 20
        ),
        cost_estimate=cost(),
        name="attention_forward",
    )(x, qkv_w, out_w, *tables, *arrays)


def attention_backward_kernel(
    sections, spreads, x_ref, qkv_ref, wo_ref, cos_ref, sin_ref, heads_in, lse_ref, *refs
):
    kept = len(sections)
    sources, refs = refs[:kept], refs[kept:]
    spread_sources, refs = refs[:spreads], refs[spreads:]
    spreads = spreads // 4
    out_ref, all_out, grads_out, *refs = refs
    targets, refs = refs[:kept], refs[kept:]
    spread_targets, refs = refs[:spreads], refs[spreads:]
    held, refs = refs[: 5 * spreads], refs[5 * spreads :]
    wqkv, wo, heads, douts, dk, dv, dqt, grads, partial, wsem, osem, carry_sem, *line = refs
    spread = [SumSpread(spread_sources, spread_targets[0], held)] if spreads else []
    for side in spread:
        side.load()
    line = Line(line)
    carried = Carried(sections, sources, targets, carry_sem)
    s = line.s
    rows = out_ref.shape[0]
    kv = heads.shape[0] // (GROUP + 2)
    queries = GROUP * kv
    loads = [
        pltpu.make_async_copy(wo_ref, wo, wsem.at[0]),
        pltpu.make_async_copy(qkv_ref, wqkv, wsem.at[1]),
        pltpu.make_async_copy(heads_in, heads, wsem.at[2]),
    ]
    for load in loads:
        load.start()
    seq_greet(s, carried.section, spreads > 0)
    carried.start()
    dk[...] = jnp.zeros_like(dk)
    dv[...] = jnp.zeros_like(dv)

    def project(t):
        part = pl.ds(pl.multiple_of(t * rows, rows), rows)

        @pl.when(t == s)
        def _():
            loads[0].wait()

        grad = low(dot_t(line.land[t], wo[...]))
        for h in range(queries):
            douts[h, part, :] = grad[:, h * HEAD_DIM : (h + 1) * HEAD_DIM]

    line.gather(x_ref, project)
    saves = [pltpu.make_async_copy(line.land, all_out, osem.at[0])]
    saves[0].start()
    for side in spread:
        side.start()
    loads[1].wait()
    loads[2].wait()

    for block in (3, 2, 1, 0):
        keys = (block + 1) * rows
        part = slice(block * rows, (block + 1) * rows)

        @pl.loop(0, queries)
        def _(h):
            j = h // GROUP
            key = heads[queries + j, :keys, :]
            query = heads[h, part, :]
            grad = douts[h, part, :]
            scores = dot_t(key, query) * 0.125
            key_at = lax.broadcasted_iota(jnp.int32, scores.shape, 0)
            query_at = lax.broadcasted_iota(jnp.int32, scores.shape, 1) + block * rows
            scores = jnp.where(key_at <= query_at, scores, -jnp.inf)
            probs = jnp.exp(scores - lse_ref[pl.ds(h, 1), part])
            dprobs = dot_t(heads[queries + kv + j, :keys, :], grad)
            mean = jnp.sum(probs * dprobs, axis=0, keepdims=True)
            dscores = low(probs * (dprobs - mean))
            dk[j, :keys, :] += dot(dscores, query) * 0.125
            dv[j, :keys, :] += dot(low(probs), grad)
            dqt[pl.ds(pl.multiple_of(h * HEAD_DIM, HEAD_DIM), HEAD_DIM), :] = t_dot(key, dscores) * 0.125

        cos_part, sin_part = cos_ref[part, :], -sin_ref[part, :]
        dq = dqt[...].T
        for chunk in range(queries // 2):
            lanes = slice(chunk * 128, (chunk + 1) * 128)
            grads[part, lanes] = low(rope(dq[:, lanes], cos_part, sin_part))
        for pair in range(kv // 2):
            both = jnp.concatenate([dk[2 * pair, part, :], dk[2 * pair + 1, part, :]], axis=1)
            begin = queries * HEAD_DIM + pair * 128
            grads[part, begin : begin + 128] = low(rope(both, cos_part, sin_part))
            both = jnp.concatenate([dv[2 * pair, part, :], dv[2 * pair + 1, part, :]], axis=1)
            begin = (queries + kv) * HEAD_DIM + pair * 128
            grads[part, begin : begin + 128] = low(both)
        partial[...] = dot_t(grads[part, :], wqkv[...])
        line.hand_over(block, partial, out_ref)

    saves.append(pltpu.make_async_copy(grads, grads_out, osem.at[1]))
    saves[1].start()
    line.finish(out_ref)
    carried.finish()
    for side in spread:
        side.finish()
    for save in saves:
        save.wait()


def attention_backward_call(x, qkv_w, out_w, tables, heads, lse, collective_id, carry, spread=()):
    rows, width = x.shape
    bf, f32 = jnp.bfloat16, jnp.float32
    anywhere = pl.BlockSpec(memory_space=pl.ANY)
    near = pl.BlockSpec(memory_space=pltpu.VMEM)
    sections = tuple(to for to, _ in carry)
    arrays = [array for _, array in carry]
    results = [((rows, width), f32), ((4, rows, width), bf), ((4 * rows, qkv_w.shape[1]), bf)]
    kv = heads.shape[0] // (GROUP + 2)
    queries = GROUP * kv

    carries = [jax.ShapeDtypeStruct(array.shape, array.dtype) for array in arrays]
    if spread:
        carries.append(jax.ShapeDtypeStruct(parts_shape(spread[0]), bf))
    arrays = arrays + list(spread)

    def kernel(*refs):
        attention_backward_kernel(sections, len(spread), *refs)

    return pl.pallas_call(
        kernel,
        out_shape=[jax.ShapeDtypeStruct(*result) for result in results]
        + carries,
        in_specs=[anywhere] * 3 + [near] * 2 + [anywhere, near] + [anywhere] * len(arrays),
        out_specs=[near] + [anywhere] * (2 + len(carries)),
        scratch_shapes=sum_scratch(spread)
        + [
            pltpu.VMEM(qkv_w.shape, bf),
            pltpu.VMEM(out_w.shape, bf),
            pltpu.VMEM(heads.shape, bf),
            pltpu.VMEM((queries, 4 * rows, HEAD_DIM), bf),
            pltpu.VMEM((kv, 4 * rows, HEAD_DIM), f32),
            pltpu.VMEM((kv, 4 * rows, HEAD_DIM), f32),
            pltpu.VMEM((queries * HEAD_DIM, rows), f32),
            pltpu.VMEM(*results[2]),
            pltpu.VMEM((rows, width), f32),
            DMA((3,)),
            DMA((2,)),
            DMA((max(1, len(carry)), 2)),
        ]
        + seq_scratch(rows, width),
        compiler_params=pltpu.CompilerParams(
            collective_id=collective_id, has_side_effects=True, vmem_limit_bytes=60 << 20
        ),
        cost_estimate=cost(),
        name="attention_backward",
    )(x, qkv_w, out_w, *tables, heads, lse, *arrays)


def last_kernel(sections, own_0, own_1, in_0, in_1, cols_ref, cols_other, out_ref, out_other, *refs):
    kept = len(sections)
    sources, refs = refs[:kept], refs[kept:]
    down_out, cols_out, rows_out, *refs = refs
    targets, refs = refs[:kept], refs[kept:]
    cols_in, cols, out_in, out_sum, cols_sem, row_sem, swap_sem, carry_sem, *held = refs
    down = SumSpread((own_0, own_1, in_0, in_1), down_out, held)
    down.load()
    d, s, section = lax.axis_index("dp"), lax.axis_index("seq"), lax.axis_index("section")
    barrier = pltpu.get_barrier_semaphore()

    def signal(**device):
        pl.semaphore_signal(barrier, inc=1, device_id=device, device_id_type=MESH)

    for flip in (1, 2, 3):
        signal(seq=s ^ flip)
    signal(section=1 - section)

    @pl.when(d != s)
    def _():
        signal(dp=s, seq=d)
        pl.semaphore_wait(barrier, 5)

    @pl.when(d == s)
    def _():
        pl.semaphore_wait(barrier, 4)

    swaps = Carried((None, None), (cols_other, out_other), (cols_in, out_in), swap_sem)
    carried = Carried(sections, sources, targets, carry_sem)
    swaps.start()
    down.start()
    swaps.finish()
    carried.start()
    cols[...] = low(cols_ref[...].astype(jnp.float32) + cols_in[...].astype(jnp.float32))
    out_sum[...] = low(out_ref[...].astype(jnp.float32) + out_in[...].astype(jnp.float32))
    spread = Spread(cols, cols_out, cols_sem)
    spread.start()
    rows = remote(out_sum, rows_out, row_sem.at[0], row_sem.at[1], dp=s, seq=d)

    @pl.when(d != s)
    def _():
        rows.start()
        rows.wait()

    @pl.when(d == s)
    def _():
        rows_out[...] = out_sum[...]

    spread.finish()
    down.finish()
    carried.finish()


def last_exchange(downs, cols, cols_other, out, out_other, collective_id, carry):
    bf = jnp.bfloat16
    anywhere = pl.BlockSpec(memory_space=pl.ANY)
    near = pl.BlockSpec(memory_space=pltpu.VMEM)
    sections = tuple(to for to, _ in carry)
    arrays = [array for _, array in carry]

    def kernel(*refs):
        last_kernel(sections, *refs)

    return pl.pallas_call(
        kernel,
        out_shape=[
            jax.ShapeDtypeStruct(parts_shape(downs[0]), bf),
            *[jax.ShapeDtypeStruct(array.shape, array.dtype) for array in (cols, out, *arrays)],
        ],
        in_specs=[anywhere] * 4 + [near, anywhere, near, anywhere] + [anywhere] * len(arrays),
        out_specs=[anywhere, near, near] + [anywhere] * len(arrays),
        scratch_shapes=[
            pltpu.VMEM(cols.shape, bf),
            pltpu.VMEM(cols.shape, bf),
            pltpu.VMEM(out.shape, bf),
            pltpu.VMEM(out.shape, bf),
            DMA((4, 2)),
            DMA((2,)),
            DMA((2, 2)),
            DMA((max(1, len(arrays)), 2)),
        ]
        + sum_scratch(downs),
        compiler_params=pltpu.CompilerParams(
            collective_id=collective_id, has_side_effects=True, vmem_limit_bytes=60 << 20
        ),
        name="last_exchange",
    )(*downs, cols, cols_other, out, out_other, *arrays)


def wide_tables(length):
    half_dim = HEAD_DIM // 2
    frequency = 10000.0 ** (-np.arange(half_dim, dtype=np.float32) * 2.0 / HEAD_DIM)
    angles = np.arange(length, dtype=np.float32)[:, None] * frequency.astype(np.float32)[None, :]
    cos_table, sin_table = np.cos(angles), np.sin(angles)
    return (
        jnp.asarray(np.concatenate([cos_table] * 4, axis=1), jnp.float32),
        jnp.asarray(np.concatenate([-sin_table, sin_table] * 2, axis=1), jnp.float32),
    )


def token_choice(route):
    return route[..., None] == jnp.arange(EXPERTS, dtype=jnp.int32)


def routing(route_all, first_expert, count):
    chosen = jnp.any(token_choice(route_all), axis=2)
    blocks, rows = chosen.shape[:2]
    mine = lax.dynamic_slice_in_dim(chosen, first_expert, count, axis=2)
    chosen = low(jnp.transpose(chosen, (0, 2, 1)))
    earlier = jnp.tril(jnp.ones((rows, rows), jnp.bfloat16), -1)
    place = jnp.einsum(
        "ts,bsj->bjt", earlier, mine.astype(jnp.bfloat16), preferred_element_type=jnp.float32
    ).astype(jnp.int32)
    mine = jnp.transpose(mine, (0, 2, 1))
    place = jnp.where(mine, place, -1)
    slots = jnp.arange(CAP, dtype=jnp.int32)
    pick = low(place[:, :, None, :] == slots[None, None, :, None]).reshape(blocks, -1, rows)
    return chosen, pick, jnp.transpose(pick, (0, 2, 1))


def choose(pick, rows, count):
    picked = jnp.einsum("bct,btd->bcd", pick, rows, preferred_element_type=jnp.float32)
    blocks = pick.shape[0]
    picked = low(picked).reshape(blocks, count, CAP, -1)
    return jnp.transpose(picked, (1, 0, 2, 3)).reshape(count, blocks * CAP, -1)


def give_back(pick_t, slot_rows):
    blocks, rows = pick_t.shape[:2]
    count, _, width = slot_rows.shape
    slot_rows = jnp.transpose(slot_rows.reshape(count, blocks, CAP, width), (1, 0, 2, 3))
    slot_rows = slot_rows.reshape(blocks, count * CAP, width)
    total = jnp.einsum("btc,bcd->btd", pick_t, slot_rows, preferred_element_type=jnp.float32)
    return low(total).reshape(-1, width)


def each_dot(form, a, b):
    return jnp.einsum(form, a, b, preferred_element_type=jnp.float32)


def after(value, *others):
    return lax.optimization_barrier((value, *others))[0]


def has_kernels():
    return lax.axis_size("dp") == 4 and lax.axis_size("seq") == 4


def forward_layer(number, layer_in, picking, weights, experts, *carry):
    attn_scale, ffn_scale, qkv_w, out_w, router_w = weights
    chosen, pick, pick_t, first_expert = picking
    own, other = experts
    count = pick.shape[1] // CAP
    blocks, _, rows = chosen.shape
    received = []
    normed_input = low(rms_norm(layer_in, attn_scale))
    if has_kernels():
        branch, normed_all, heads, log_total, mixed_t, *received = attention_forward_call(
            normed_input, qkv_w, out_w, wide_tables(4 * layer_in.shape[0]), 9 + number, carry
        )
        attention_state = (normed_all.reshape(-1, layer_in.shape[1]), mixed_t, heads, log_total)
    else:
        received = [swap(array) if to is None else pass_to(array, to) for to, array in carry]
        normed_all = lax.all_gather(normed_input, "seq", axis=0, tiled=True)
        qkv = low(dot(normed_all, qkv_w))
        kv_width = KV_HEADS * HEAD_DIM // lax.axis_size("seq")
        q_width = GROUP * kv_width
        mixed, log_total, q_rot, k_rot, v_heads = attention_forward(
            qkv[:, :q_width], qkv[:, q_width : q_width + kv_width], qkv[:, q_width + kv_width :]
        )
        branch = lax.psum_scatter(low(dot(mixed, out_w)), "seq", scatter_dimension=0, tiled=True)
        attention_state = (normed_all, mixed.T, (q_rot, k_rot, v_heads), log_total)
    after_update = layer_in + branch.astype(jnp.float32)
    normed_ffn = low(rms_norm(after_update, ffn_scale))
    own_block = lax.axis_index("dp") * lax.axis_size("seq") + lax.axis_index("seq")
    own_chosen = lax.dynamic_index_in_dim(chosen, own_block, 0, keepdims=False)
    own_logits = jnp.where(own_chosen > 0, dot_t(router_w, normed_ffn), -jnp.inf)
    own_gates = jax.nn.softmax(own_logits, axis=0)
    if number == 0:
        other = other + (received[0],)
    mine = (
        jnp.arange(EXPERTS)[None, None, :] == first_expert + jnp.arange(count)[:, None, None]
    ).astype(jnp.float32)
    if has_kernels():
        *expert_state, slot_out = expert_forward(
            number, normed_ffn, pick, chosen, router_w, mine, own, other, 1 + number
        )
        if number == 0:
            *expert_state, slot_out, other_down = (*expert_state, slot_out)
            other = other[:2] + (other_down,)
    else:
        if number == 0:
            other = other[:2] + (swap(own[2]),)
        gate_w, up_w, down_w = by_layer(number, own, other)
        ffn_all = lax.all_gather(normed_ffn, TOKENS, axis=0, tiled=True)
        logits = dot_t(ffn_all, router_w).reshape(blocks, rows, EXPERTS)
        used = jnp.transpose(chosen, (0, 2, 1)) > 0
        gates = jax.nn.softmax(jnp.where(used, logits, -jnp.inf), axis=-1)
        slot_rows = choose(pick, ffn_all.reshape(blocks, rows, -1), count)
        mine_gates = jnp.einsum("bte,jxe->bjt", gates, mine, precision=lax.Precision.HIGHEST)
        slot_gates = jnp.sum(
            pick.reshape(blocks, count, CAP, rows).astype(jnp.float32) * mine_gates[:, :, None, :],
            axis=3,
        )
        slot_gates = jnp.transpose(slot_gates, (1, 0, 2)).reshape(count, -1, 1)
        gate_pre = each_dot("ecd,edf->ecf", slot_rows, gate_w)
        up_pre = each_dot("ecd,edf->ecf", slot_rows, up_w)
        scaled = low(slot_gates * jax.nn.silu(gate_pre) * up_pre)
        slot_out = low(each_dot("ecf,efd->ecd", scaled, down_w))
        expert_state = (slot_rows, gate_pre, up_pre, scaled, slot_gates)
    saved = (
        layer_in,
        attention_state,
        after_update,
        normed_ffn,
        own_gates,
        expert_state,
    )
    return (after_update, slot_out, saved, (own, other), received)


def token_sums(pick_t, slot_out, collective_id, *carry, spread=(), products=()):
    if has_kernels():
        sums, *received = combine(pick_t, slot_out, collective_id, carry, spread, products)
        return sums, received
    sums = give_back(pick_t, slot_out).astype(jnp.float32)
    sums = lax.psum_scatter(sums, TOKENS, scatter_dimension=0, tiled=True)
    received = [pass_to(array, to) for to, array in carry]
    grads = [
        low(each_dot("eck,ecn->ekn", left, right)) for left, rights in products for right in rights
    ]
    return sums, received + list(spread) + grads


def spread_rows(parts):
    return lax.all_to_all(parts, "seq", split_axis=0, concat_axis=0, tiled=True)


def expert_gradients(number, layer_grad, saved, picking, experts, *carry):
    chosen, pick, pick_t, first_expert = picking
    own, other = experts
    count = pick.shape[1] // CAP
    blocks, _, rows = chosen.shape
    slot_rows, gate_pre, up_pre, scaled, slot_gates = saved[-1]
    if has_kernels():
        slot_grads, gate_low, up_low, gate_term, slot_out, *received = expert_backward(
            number, low(layer_grad), pick, gate_pre, up_pre, slot_gates, own, other, 4 + number, carry
        )
        gate_term = gate_term[:, :, :1]
    else:
        gate_w, up_w, down_w = by_layer(number, own, other)
        grad_all = lax.all_gather(low(layer_grad), TOKENS, axis=0, tiled=True)
        slot_grads = choose(pick, grad_all.reshape(blocks, rows, -1), count)
        plain_grad = each_dot("ecd,efd->ecf", slot_grads, down_w)
        sigmoid = jax.nn.sigmoid(gate_pre)
        activated = gate_pre * sigmoid
        gate_term = jnp.sum(plain_grad * (activated * up_pre), axis=2, keepdims=True)
        hidden_grad = slot_gates * plain_grad
        gate_low = low(hidden_grad * up_pre * sigmoid * (1.0 + gate_pre * (1.0 - sigmoid)))
        up_low = low(hidden_grad * activated)
        slot_out = low(
            each_dot("ecf,edf->ecd", gate_low, gate_w) + each_dot("ecf,edf->ecd", up_low, up_w)
        )
        received = [pass_to(array, to) for to, array in carry]
    by_slot = jnp.transpose(gate_term.reshape(count, blocks, CAP), (1, 0, 2))
    gate_terms = jnp.sum(
        pick.reshape(blocks, count, CAP, rows).astype(jnp.float32) * by_slot[..., None], axis=2
    )
    gate_terms = lax.all_to_all(gate_terms, TOKENS, split_axis=0, concat_axis=0, tiled=True)
    products = ((slot_rows, (gate_low, up_low)), (scaled, (slot_grads,)))
    return slot_out, gate_terms, products, received


def backward_layer(
    number, layer_grad, normed_grad, gate_terms, saved, picking, weights, *carry, spread=()
):
    attn_scale, ffn_scale, qkv_w, out_w, router_w = weights
    chosen, pick, _, _ = picking
    (
        layer_in,
        (normed_all, mixed_t, heads, log_total),
        after_update,
        normed_ffn,
        own_gates,
        _,
    ) = saved
    rows = chosen.shape[2]
    gate_terms = jnp.sum(gate_terms.reshape(EXPERTS, -1, rows), axis=1)
    logit_grad = low(
        own_gates * (gate_terms - jnp.sum(own_gates * gate_terms, axis=0, keepdims=True))
    )
    router_grad = dot(logit_grad, normed_ffn)
    normed_grad = normed_grad + t_dot(logit_grad, router_w)
    after_part, ffn_gain_grad = jax.vjp(rms_norm, after_update, ffn_scale)[1](normed_grad)
    after_grad = after_part + layer_grad
    if has_kernels():
        normed_attn, branch_all, qkv_grad, *received = attention_backward_call(
            low(after_grad),
            qkv_w,
            out_w,
            wide_tables(4 * layer_in.shape[0]),
            heads,
            log_total,
            11 + number,
            carry,
            spread,
        )
        branch_all = branch_all.reshape(-1, layer_in.shape[1])
    else:
        branch_all = lax.all_gather(low(after_grad), "seq", axis=0, tiled=True)
        head_grad = low(dot_t(branch_all, out_w))
        qkv_grad = attention_backward(head_grad, *heads, log_total)
        normed_attn = low(dot_t(qkv_grad, qkv_w))
        normed_attn = lax.psum_scatter(normed_attn, "seq", scatter_dimension=0, tiled=True)
        received = [pass_to(array, to) for to, array in carry]
        received = received + list(spread)
    out_grad = dot(mixed_t, branch_all)
    qkv_weight_grad = t_dot(normed_all, qkv_grad)
    input_part, attn_gain_grad = jax.vjp(rms_norm, layer_in, attn_scale)[1](
        normed_attn.astype(jnp.float32)
    )
    small = [router_grad, attn_gain_grad[None], ffn_gain_grad[None]]
    small = jnp.concatenate(small + [jnp.zeros((128 - EXPERTS - 2, small[0].shape[1]))], axis=0)
    qkv_weight_grad = jnp.concatenate([low(qkv_weight_grad), low(small).T], axis=1)
    return (input_part + after_grad, (qkv_weight_grad, low(out_grad)), received)


def by_layer(number, own, other):
    is_own = lax.axis_index("section") == number
    return jax.tree.map(lambda mine, received: jnp.where(is_own, mine, received), own, other)


def body(
    hidden_in,
    out_grad,
    attn_gain,
    ffn_gain,
    query_matrix,
    key_matrix,
    value_matrix,
    output_matrix,
    router_matrix,
    w_gate,
    w_up,
    w_down,
    routes,
):
    section = lax.axis_index("section")
    dp, seq = lax.axis_size("dp"), lax.axis_size("seq")
    seq_index = lax.axis_index("seq")
    first = section == 0
    width = hidden_in.shape[3]
    depth = query_matrix.shape[1]

    layer_in = lax.dynamic_index_in_dim(hidden_in, section, 0, keepdims=False)[0]
    top_grad = lax.dynamic_index_in_dim(out_grad, section, 0, keepdims=False)[0]
    own_group = jnp.concatenate(
        [
            matrix[0].reshape(depth, seq, -1)
            for matrix in (query_matrix, key_matrix, value_matrix)
        ],
        axis=2,
    )
    own_group = jnp.transpose(own_group, (1, 0, 2))
    to_group = []
    for flat in range(dp * seq):
        to_group.append((flat, (flat % dp) * seq + flat // dp))
    from_group = [(target, source) for source, target in to_group]
    own_out = lax.ppermute(output_matrix[0], TOKENS, to_group)
    other_out = swap(own_out)
    local = w_gate.shape[1]
    hidden_units = w_gate.shape[3]
    if local >= seq:
        count, units = local // seq, hidden_units
        start, unit_start = seq_index * count, 0
    else:
        count, units = 1, hidden_units * local // seq
        start, unit_start = seq_index * local // seq, (seq_index % (seq // local)) * units
    first_expert = lax.axis_index("dp") * local + start
    if has_kernels():
        own_experts = (w_gate[0], w_up[0], w_down[0])
    else:
        own_experts = (
            lax.dynamic_slice(w_gate[0], (start, 0, unit_start), (count, width, units)),
            lax.dynamic_slice(w_up[0], (start, 0, unit_start), (count, width, units)),
            lax.dynamic_slice(w_down[0], (start, unit_start, 0), (count, units, width)),
        )
    small = jnp.concatenate([router_matrix[0].T, attn_gain, ffn_gain], axis=0)
    paths = routes[0, :, 0]
    if has_kernels():
        small = jnp.pad(small, ((0, -small.shape[0] % 16), (0, 256 - depth)))
        paths = low(jnp.transpose(paths, (0, 2, 1)).reshape(2 * TOP_K, -1))
        picks, picks_t, chosens, small, qkv_first, qkv_second, other_gate = prepare(
            jnp.concatenate([paths, small], axis=0),
            own_group,
            own_experts[0],
            count,
            hidden_in.shape[2],
            depth,
            13,
        )
        pickings = [(chosens[n], picks[n], picks_t[n], first_expert) for n in range(2)]
        qkv_second = lax.all_gather(
            qkv_second.reshape(seq * depth, -1), "dp", axis=0, tiled=True
        )
        qkv_layers = [qkv_first.reshape(width, -1), qkv_second]
    else:
        small = lax.all_gather(small, ("section", "dp", "seq"), axis=0, tiled=False)
        small = jnp.transpose(small.reshape(2, dp * seq, -1, depth), (0, 2, 1, 3))
        small = small.reshape(2, -1, width)
        paths = lax.all_gather(paths, ("section", "dp", "seq"), axis=0, tiled=False)
        paths = lax.dynamic_index_in_dim(paths, section, 1, keepdims=False)
        paths = paths.reshape(2, dp * seq, -1, TOP_K)
        pickings = [routing(paths[n], first_expert, count) + (first_expert,) for n in range(2)]
        other_gate = swap(own_experts[0])
        other_group = swap(own_group)
        qkv_layers = []
        for number in range(2):
            part = spread_rows(by_layer(number, own_group, other_group))
            part = part.reshape(seq * depth, -1)
            qkv_layers.append(lax.all_gather(part, "dp", axis=0, tiled=True))

    weights = []
    for number in range(2):
        out_w = lax.all_gather(
            by_layer(number, own_out, other_out), "dp", axis=0, tiled=True
        )
        weights.append(
            (
                small[number, EXPERTS].astype(jnp.float32),
                small[number, EXPERTS + 1].astype(jnp.float32),
                qkv_layers[number],
                out_w,
                small[number, :EXPERTS],
            )
        )

    def own_layer(pieces):
        return jnp.where(first, pieces[0], pieces[1])

    def both_micros(own, other):
        return jnp.stack([jnp.where(first, own, other), jnp.where(first, other, own)])[
            None, :, None
        ]

    def summed(own, other):
        return own_layer(own).astype(jnp.float32) + own_layer(other).astype(jnp.float32)

    def dp_sums(dense):
        return [lax.psum_scatter(part, "dp", scatter_dimension=0, tiled=True) for part in dense]

    def row_parts(piece, kind):
        if local >= seq:
            piece = piece.reshape(count, seq, piece.shape[1] // seq, -1)
            return jnp.transpose(piece, (1, 0, 2, 3))
        if kind < 2:
            return piece.reshape(seq, -1, units)
        piece = piece.reshape(-1, hidden_units // seq, width)
        share = seq // local
        parts = jnp.zeros((seq,) + piece.shape[1:], piece.dtype)
        return lax.dynamic_update_slice_in_dim(
            parts, piece, (seq_index % share) * piece.shape[0], axis=0
        )

    def whole_rows(parts, kind):
        parts = parts.astype(jnp.float32)
        if local < seq:
            parts = parts.reshape((local, seq // local) + parts.shape[1:])
            if kind < 2:
                parts = jnp.transpose(parts, (0, 2, 1, 3))
            else:
                parts = jnp.sum(parts, axis=1)
            return parts.reshape((local,) + parts.shape[1 : 2] + (-1,))[None]
        return parts.reshape((local,) + parts.shape[2:])[None]

    experts = (own_experts, (other_gate,))
    first_in = layer_in.astype(jnp.float32)
    updated, slot_out, first_saved, experts, _ = forward_layer(
        0, first_in, pickings[0], weights[0], experts, (None, own_experts[1])
    )
    sums, _ = token_sums(pickings[0][2], slot_out, 3)
    first_out = updated + sums
    second_updated, second_slots, second_saved, experts, (other_out,) = forward_layer(
        1, first_out, pickings[1], weights[1], experts, (0, first_out)
    )
    top_grad = top_grad.astype(jnp.float32)
    slot_out, gate_terms, products, _ = expert_gradients(
        1, top_grad, second_saved, pickings[1], experts
    )
    sums, second_experts = token_sums(pickings[1][2], slot_out, 6, products=products)
    middle_grad, second_dense, (second_gate,) = backward_layer(
        1, top_grad, sums, gate_terms, second_saved, pickings[1], weights[1], (1, second_experts[0])
    )
    slot_out, gate_terms, products, (second_up,) = expert_gradients(
        0, middle_grad, first_saved, pickings[0], experts, (1, second_experts[1])
    )
    (rows_in, (gate_low, up_low)), down_product = products
    gate_grad = low(each_dot("ecd,ecf->edf", rows_in, gate_low))
    slot_out, gate_grad, gate_terms = lax.optimization_barrier((slot_out, gate_grad, gate_terms))
    sums, (first_gate, second_down, *first_experts) = token_sums(
        pickings[0][2],
        slot_out,
        7,
        (0, gate_grad),
        (1, second_experts[2]),
        products=((rows_in, (up_low,)), down_product),
    )
    first_experts = [gate_grad, *first_experts]
    sums, *second_dense = lax.optimization_barrier((sums, *second_dense))
    second_dense = dp_sums(second_dense)

    def handed(kind, *received):
        own = (first_experts[kind], second_experts[kind])
        if has_kernels():
            return (*own, *received)
        return [spread_rows(row_parts(low(summed(own, received)), kind))]

    bottom_grad, first_dense, (first_up, other_middle, gate_rows) = backward_layer(
        0,
        middle_grad,
        sums,
        gate_terms,
        first_saved,
        pickings[0],
        weights[0],
        (0, first_experts[1]),
        (1, middle_grad),
        spread=handed(0, first_gate, second_gate),
    )
    second_slots, *first_dense, second_dense[0], second_dense[1] = lax.optimization_barrier(
        (second_slots, *first_dense, *second_dense)
    )
    first_dense = dp_sums(first_dense)
    sums, (first_down, up_rows) = token_sums(
        pickings[1][2],
        second_slots,
        8,
        (0, first_experts[2]),
        spread=handed(1, first_up, second_up),
    )
    sums, *first_dense = lax.optimization_barrier((sums, *first_dense))
    second_out = second_updated + sums
    own_cols, own_rows = [own_layer((first_dense[k], second_dense[k])) for k in range(2)]
    other_cols, other_rows = [own_layer((second_dense[k], first_dense[k])) for k in range(2)]
    if has_kernels():
        down_rows, cols_sum, out_sum, other_second, other_bottom = last_exchange(
            handed(2, first_down, second_down),
            own_cols.reshape(seq, depth, -1),
            other_cols.reshape(seq, depth, -1),
            own_rows,
            other_rows,
            14,
            ((1, second_out), (0, bottom_grad)),
        )
    else:
        (down_rows,) = handed(2, first_down, second_down)
        cols_sum = low(own_cols.astype(jnp.float32) + swap(other_cols).astype(jnp.float32))
        cols_sum = spread_rows(cols_sum.reshape(seq, depth, -1))
        out_sum = low(own_rows.astype(jnp.float32) + swap(other_rows).astype(jnp.float32))
        out_sum = lax.ppermute(out_sum, TOKENS, from_group)
        other_second, other_bottom = pass_to(second_out, 1), pass_to(bottom_grad, 0)
    expert_sums = [whole_rows(rows, k) for k, rows in enumerate((gate_rows, up_rows, down_rows))]
    layer_outs = both_micros(
        own_layer((first_out, second_out)), own_layer((other_out, other_second))
    )
    section_grads = both_micros(
        own_layer((bottom_grad, middle_grad)), own_layer((other_bottom, other_middle))
    )
    qkv_sum, out_sum = cols_sum.astype(jnp.float32), out_sum.astype(jnp.float32)
    kv_width = KV_HEADS * HEAD_DIM // seq
    q_width = GROUP * kv_width
    qkv_width = q_width + 2 * kv_width
    small_sum = jnp.sum(qkv_sum[:, :, qkv_width:], axis=0)

    def columns(begin, end):
        return jnp.transpose(qkv_sum[:, :, begin:end], (1, 0, 2)).reshape(depth, -1)[None]

    return (
        layer_outs,
        section_grads,
        small_sum[:, EXPERTS][None],
        small_sum[:, EXPERTS + 1][None],
        columns(0, q_width),
        columns(q_width, q_width + kv_width),
        columns(q_width + kv_width, qkv_width),
        out_sum[None],
        small_sum[:, :EXPERTS][None],
        *expert_sums,
    )


def solution(mesh):
    return jax.shard_map(
        body,
        mesh=mesh,
        in_specs=(
            P(None, "dp", "seq", None),
            P(None, "dp", "seq", None),
            P("section", ("dp", "seq")),
            P("section", ("dp", "seq")),
            P("section", ("dp", "seq"), None),
            P("section", ("dp", "seq"), None),
            P("section", ("dp", "seq"), None),
            P("section", ("dp", "seq"), None),
            P("section", ("dp", "seq"), None),
            P("section", "dp", None, None),
            P("section", "dp", None, None),
            P("section", "dp", None, None),
            P("section", None, "dp", "seq", None),
        ),
        out_specs=(
            P("section", None, "dp", "seq", None),
            P("section", None, "dp", "seq", None),
            P("section", ("dp", "seq")),
            P("section", ("dp", "seq")),
            P("section", ("dp", "seq"), None),
            P("section", ("dp", "seq"), None),
            P("section", ("dp", "seq"), None),
            P("section", ("dp", "seq"), None),
            P("section", ("dp", "seq"), None),
            P("section", "dp", "seq", None),
            P("section", "dp", "seq", None),
            P("section", "dp", "seq", None),
        ),
        check_vma=False,
    )
```

```python
import jax
import jax.numpy as jnp
import numpy as np
from jax import lax
from jax.experimental import pallas as pl
from jax.experimental.pallas import tpu as pltpu
from jax.sharding import PartitionSpec as P

HEADS = 24
KV_HEADS = 8
HEAD_DIM = 64
TOP_K = 8
EXPERTS = 32
CAP = 80
GROUP = HEADS // KV_HEADS
TOKENS = ("dp", "seq")
PIECES = 4
MESH = pl.DeviceIdType.MESH
DMA = pltpu.SemaphoreType.DMA

epsilon = 1e-06


def dot(a, b):
    return jnp.dot(a, b, preferred_element_type=jnp.float32)


def dot_t(a, b):
    return lax.dot_general(a, b, (((1,), (1,)), ((), ())), preferred_element_type=jnp.float32)


def t_dot(a, b):
    return lax.dot_general(a, b, (((0,), (0,)), ((), ())), preferred_element_type=jnp.float32)


def low(v):
    return v.astype(jnp.bfloat16)


def swap(block):
    return lax.ppermute(block, "section", [(0, 1), (1, 0)])


def pass_to(block, section):
    return lax.ppermute(block, "section", [(1 - section, section)])


def rms_norm(values, norm_gain):
    return (
        values * lax.rsqrt(jnp.mean(values * values, axis=-1, keepdims=True) + epsilon) * norm_gain
    )


def rotary_tables(length):
    half_dim = HEAD_DIM // 2
    frequency = 10000.0 ** (-jnp.arange(half_dim, dtype=jnp.float32) * 2.0 / HEAD_DIM)
    angles = jnp.arange(length, dtype=jnp.float32)[:, None] * frequency[None, :]
    return (jnp.cos(angles)[:, None, :], jnp.sin(angles)[:, None, :])


def rotate(values, cos_table, sin_table):
    length = values.shape[0]
    split_heads = values.reshape(length, -1, HEAD_DIM)
    first_half = split_heads[..., : HEAD_DIM // 2]
    second_half = split_heads[..., HEAD_DIM // 2 :]
    turned = jnp.concatenate(
        [
            first_half * cos_table - second_half * sin_table,
            second_half * cos_table + first_half * sin_table,
        ],
        axis=-1,
    )
    return turned.reshape(length, -1)


def attention_forward(q_heads, k_heads, v_heads):
    length = q_heads.shape[0]
    local_kv = k_heads.shape[1] // HEAD_DIM
    cos_table, sin_table = rotary_tables(length)
    q_rot = low(rotate(q_heads.astype(jnp.float32), cos_table, sin_table)).reshape(
        length, local_kv, GROUP, HEAD_DIM
    )
    k_rot = low(rotate(k_heads.astype(jnp.float32), cos_table, sin_table)).reshape(
        length, local_kv, HEAD_DIM
    )
    values = v_heads.reshape(length, local_kv, HEAD_DIM)
    block_rows = min(512, length)
    outputs = []
    totals_list = []
    for first_row in range(0, length, block_rows):
        key_end = first_row + block_rows
        scores = (
            jnp.einsum(
                "qhgd,khd->hgqk",
                q_rot[first_row:key_end],
                k_rot[:key_end],
                preferred_element_type=jnp.float32,
            )
            * 0.125
        )
        causal = (first_row + jnp.arange(block_rows, dtype=jnp.int32))[:, None] >= jnp.arange(
            key_end, dtype=jnp.int32
        )[None, :]
        scores = jnp.where(causal, scores, -jnp.inf)
        row_peak = jnp.max(scores, axis=-1, keepdims=True)
        exponents = jnp.exp(scores - row_peak)
        totals = jnp.sum(exponents, axis=-1, keepdims=True)
        attended = jnp.einsum(
            "hgqk,khd->qhgd",
            low(exponents / totals),
            values[:key_end],
            preferred_element_type=jnp.float32,
        )
        outputs.append(low(attended).reshape(block_rows, -1))
        totals_list.append((row_peak + jnp.log(totals))[..., 0])
    return (jnp.concatenate(outputs, axis=0), jnp.stack(totals_list), q_rot, k_rot, values)


def attention_backward(head_grad, q_rot, k_rot, values, log_total):
    length, local_kv = q_rot.shape[:2]
    cos_table, sin_table = rotary_tables(length)
    block_rows = min(512, length)
    grad_rows = head_grad.reshape(length, local_kv, GROUP, HEAD_DIM)
    key_acc = jnp.zeros((length, local_kv, HEAD_DIM), jnp.float32)
    value_acc = jnp.zeros((length, local_kv, HEAD_DIM), jnp.float32)
    query_parts = []
    for block_number, first_row in enumerate(range(0, length, block_rows)):
        key_end = first_row + block_rows
        q_block = q_rot[first_row:key_end]
        grad_block = grad_rows[first_row:key_end]
        key_part = k_rot[:key_end]
        scores = (
            jnp.einsum("qhgd,khd->hgqk", q_block, key_part, preferred_element_type=jnp.float32)
            * 0.125
        )
        causal = (first_row + jnp.arange(block_rows, dtype=jnp.int32))[:, None] >= jnp.arange(
            key_end, dtype=jnp.int32
        )[None, :]
        scores = jnp.where(causal, scores, -jnp.inf)
        probs_full = jnp.exp(scores - log_total[block_number][..., None])
        prob_grad = jnp.einsum(
            "qhgd,khd->hgqk", grad_block, values[:key_end], preferred_element_type=jnp.float32
        )
        score_grad = probs_full * (
            prob_grad - jnp.sum(probs_full * prob_grad, axis=-1, keepdims=True)
        )
        score_low = low(score_grad)
        query_parts.append(
            jnp.einsum("hgqk,khd->qhgd", score_low, key_part, preferred_element_type=jnp.float32)
            * 0.125
        )
        key_acc = key_acc.at[:key_end].add(
            jnp.einsum("hgqk,qhgd->khd", score_low, q_block, preferred_element_type=jnp.float32)
            * 0.125
        )
        value_acc = value_acc.at[:key_end].add(
            jnp.einsum(
                "hgqk,qhgd->khd", low(probs_full), grad_block, preferred_element_type=jnp.float32
            )
        )
    query_all = jnp.concatenate(query_parts, axis=0).reshape(length, -1)
    query_grad = rotate(query_all, cos_table, -sin_table)
    key_grad = rotate(key_acc.reshape(length, -1), cos_table, -sin_table)
    return jnp.concatenate(
        [low(query_grad), low(key_grad), low(value_acc).reshape(length, -1)], axis=1
    )


def remote(src, dst, send_sem, recv_sem, **device):
    return pltpu.make_async_remote_copy(
        src_ref=src,
        dst_ref=dst,
        send_sem=send_sem,
        recv_sem=recv_sem,
        device_id=device,
        device_id_type=MESH,
    )


def greet(d, s, section=None, spread=False):
    barrier = pltpu.get_barrier_semaphore()

    def signal(**device):
        pl.semaphore_signal(barrier, inc=1, device_id=device, device_id_type=MESH)

    signal(seq=s ^ 1)
    signal(seq=s ^ 2)

    @pl.when(d > 0)
    def _():
        signal(dp=d - 1)

    @pl.when(d < 3)
    def _():
        signal(dp=d + 1)

    known = 3
    if section is not None:
        signal(section=1 - section)
        known = 4
    if spread:
        signal(seq=s ^ 3)
        known = known + 1
    inner = (d > 0) & (d < 3)

    @pl.when(inner)
    def _():
        pl.semaphore_wait(barrier, known + 1)

    @pl.when(jnp.logical_not(inner))
    def _():
        pl.semaphore_wait(barrier, known)


class Carried:
    def __init__(self, sections, sources, targets, sems):
        self.section = lax.axis_index("section")
        self.copies = []
        for k, (to, source, target) in enumerate(zip(sections, sources, targets)):
            copy = remote(source, target, sems.at[k, 0], sems.at[k, 1], section=1 - self.section)
            self.copies.append((to, copy))

    def start(self):
        for to, copy in self.copies:
            if to is None:
                copy.start()
            else:

                @pl.when(self.section != to)
                def _():
                    copy.start()

    def finish(self):
        for to, copy in self.copies:
            if to is None:
                copy.wait()
            else:

                @pl.when(self.section != to)
                def _():
                    copy.wait_send()

                @pl.when(self.section == to)
                def _():
                    copy.wait_recv()


class Spread:
    def __init__(self, source, target, sems):
        s = lax.axis_index("seq")
        self.local = pltpu.make_async_copy(source.at[s], target.at[s], sems.at[0, 0])
        self.copies = [
            remote(source.at[s ^ flip], target.at[s], sems.at[flip, 0], sems.at[flip, 1], seq=s ^ flip)
            for flip in (3, 2, 1)
        ]

    def start(self):
        for copy in self.copies:
            copy.start()
        self.local.start()

    def finish(self):
        self.local.wait()
        for copy in self.copies:
            copy.wait()


class SumSpread:
    def __init__(self, refs, target, held):
        self.refs, self.target = refs, target
        self.a, self.b, self.parts, self.loads, self.sems = held

    def copies(self, own, received):
        return [
            pltpu.make_async_copy(own, self.a, self.loads.at[0]),
            pltpu.make_async_copy(received, self.b, self.loads.at[1]),
        ]

    def load(self):
        own_0, own_1, in_0, in_1 = self.refs

        @pl.when(lax.axis_index("section") == 0)
        def _():
            for copy in self.copies(own_0, in_0):
                copy.start()

        @pl.when(lax.axis_index("section") == 1)
        def _():
            for copy in self.copies(own_1, in_1):
                copy.start()

    def start(self):
        for copy in self.copies(self.refs[0], self.refs[2]):
            copy.wait()
        group, count, rows, width = self.parts.shape
        chunk = 24576 // width
        for g in range(group):
            for j in range(count):

                @pl.loop(0, rows // chunk)
                def _(m):
                    here = pl.ds(pl.multiple_of(m * chunk, chunk), chunk)
                    there = pl.ds(pl.multiple_of(g * rows + m * chunk, chunk), chunk)
                    total = self.a[j, there, :].astype(jnp.float32)
                    total = total + self.b[j, there, :].astype(jnp.float32)
                    self.parts[g, j, here, :] = low(total)

        self.spread = Spread(self.parts, self.target, self.sems)
        self.spread.start()

    def finish(self):
        self.spread.finish()


def parts_shape(array):
    count, rows, width = array.shape
    return (4, count, rows // 4, width)


def sum_scratch(arrays):
    if not arrays:
        return []
    shape, bf = arrays[0].shape, jnp.bfloat16
    return [
        pltpu.VMEM(shape, bf),
        pltpu.VMEM(shape, bf),
        pltpu.VMEM(parts_shape(arrays[0]), bf),
        DMA((2,)),
        DMA((4, 2)),
    ]


def cost():
    return pl.CostEstimate(flops=80_000_000_000, bytes_accessed=100_000_000, transcendentals=0)


def gather_scratch(rows, width):
    return [
        pltpu.VMEM((16, rows, width), jnp.bfloat16),
        DMA(()),
        DMA((2, 4)),
        DMA((4,)),
        DMA((4,)),
        DMA((4,)),
        DMA((4, 2)),
        DMA((4, 2)),
    ]


def gather_blocks(x_ref, scratch, compute, carried=None, first=None, spread=False):
    land, lsem, zs, zr, ys, yr, cs, cr = scratch
    d, s = lax.axis_index("dp"), lax.axis_index("seq")

    def place(z, column):
        return land.at[z * 4 + column]

    def z_copy(src, z, right):
        target = d + 1 if right else d - 1
        return remote(src, place(z, s), zs.at[int(right), z], zr.at[z], dp=target)

    def y_copy(src, z):
        return remote(src, place(z, s), ys.at[z], yr.at[z], seq=s ^ 2)

    def core_copy(src, z, across):
        column = s ^ 2 if across else s
        return remote(src, place(z, column), cs.at[z, across], cr.at[z, across], seq=s ^ 1)

    greet(d, s, None if carried is None else carried.section, spread)
    if first is not None:
        first()
    own = pltpu.make_async_copy(x_ref, place(d, s), lsem)
    own.start()
    if carried is not None and first is None:
        carried.start()

    @pl.when(d < 3)
    def _():
        z_copy(x_ref, d, True).start()

    @pl.when(d > 0)
    def _():
        z_copy(x_ref, d, False).start()

    y_copy(x_ref, d).start()
    core_copy(x_ref, d, 0).start()
    own.wait()

    inner = (d > 0) & (d < 3)

    def send_on(q):
        following = near_first(d, q)
        y_copy(place(following, s), following).start()
        core_copy(place(following, s), following, 0).start()

    @pl.loop(0, 4)
    def _(i):
        @pl.when(i < 3)
        def _():
            early = inner & (i > 0)

            @pl.when(early)
            def _():
                send_on(i + 1)

            left, right = d - (i + 1), d + (i + 1)

            @pl.when(left >= 0)
            def _():
                z_copy(place(left, s), left, True).wait_recv()

                @pl.when(d < 3)
                def _():
                    z_copy(place(left, s), left, True).start()

            @pl.when(right <= 3)
            def _():
                z_copy(place(right, s), right, False).wait_recv()

                @pl.when(d > 0)
                def _():
                    z_copy(place(right, s), right, False).start()

            @pl.when(jnp.logical_not(early))
            def _():
                send_on(i + 1)

        z = near_first(d, i)
        y_copy(place(z, s ^ 2), z).wait_recv()
        core_copy(place(z, s ^ 2), z, 1).start()
        core_copy(place(z, s ^ 1), z, 0).wait_recv()
        core_copy(place(z, s ^ 3), z, 1).wait_recv()
        compute(z)

    for z in range(4):

        @pl.when((z <= d) & (d < 3))
        def _():
            z_copy(place(z, s), z, True).wait_send()

        @pl.when((z >= d) & (d > 0))
        def _():
            z_copy(place(z, s), z, False).wait_send()

        y_copy(place(z, s), z).wait_send()
        core_copy(place(z, s), z, 0).wait_send()
        core_copy(place(z, s), z, 1).wait_send()
    return land


def prepare_kernel(
    x_ref, group_ref, gate_ref,
    pick_0, pick_1, pick_t_0, pick_t_1, chosen_0, chosen_1, small_out, qkv_out, parts_out, gate_out,
    both, places, groups, parts, lsem, carry_sem, spread_sem, qs, qr, *gather
):
    d, s, section = lax.axis_index("dp"), lax.axis_index("seq"), lax.axis_index("section")
    known = x_ref.shape[0]
    count = pick_0.shape[1] // CAP
    rows = pick_0.shape[2]
    land = gather[0]
    part = both.at[pl.ds(pl.multiple_of(section * known, known), known)]
    swaps = Carried((None, None), (x_ref, group_ref), (part, groups.at[section]), carry_sem)
    gates = Carried((None,), (share(gate_ref),), (gate_out,), carry_sem.at[pl.ds(2, 1)])
    spreads = [Spread(groups.at[n], parts.at[n], spread_sem.at[n]) for n in range(2)]
    own_columns = pltpu.make_async_copy(parts.at[0], qkv_out.at[d], lsem.at[2])

    def along(src, z, right):
        target = d + 1 if right else d - 1
        return remote(src, qkv_out.at[z], qs.at[int(right), z], qr.at[z], dp=target)

    def first():
        swaps.start()
        own = [
            pltpu.make_async_copy(x_ref, part, lsem.at[0]),
            pltpu.make_async_copy(group_ref, groups.at[section], lsem.at[1]),
        ]
        for copy in own:
            copy.start()
        for copy in own:
            copy.wait()
        swaps.finish()
        gates.start()
        for side in spreads:
            side.start()
        spreads[0].finish()
        own_columns.start()

        @pl.when(d < 3)
        def _():
            along(parts.at[0], d, True).start()

        @pl.when(d > 0)
        def _():
            along(parts.at[0], d, False).start()

    def hop(h):
        @pl.when(d - h >= 0)
        def _():
            along(qkv_out.at[d - h], d - h, True).wait_recv()

            @pl.when(d < 3)
            def _():
                along(qkv_out.at[d - h], d - h, True).start()

        @pl.when(d + h <= 3)
        def _():
            along(qkv_out.at[d + h], d + h, False).wait_recv()

            @pl.when(d > 0)
            def _():
                along(qkv_out.at[d + h], d + h, False).start()

    gather_blocks(both, gather, lambda z: None, gates, first, True)
    hop(1)
    first_expert = (d * 4 + s) * count
    before = lax.broadcasted_iota(jnp.int32, (rows, rows), 0)
    before = low(before < lax.broadcasted_iota(jnp.int32, (rows, rows), 1))
    slot = lax.broadcasted_iota(jnp.int32, (CAP, rows), 0)
    expert = lax.broadcasted_iota(jnp.int32, (EXPERTS, rows), 0)
    lane = lax.broadcasted_iota(jnp.int32, (rows, count * CAP), 1)

    def tables(layer, pick_out, pick_t_out, chosen_out):
        @pl.loop(0, 16)
        def _(b):
            paths = land[b, layer * known : layer * known + 16, :].astype(jnp.float32)
            paths = jnp.where(section == 0, paths[:TOP_K], paths[TOP_K:]).astype(jnp.int32)
            chosen = expert == paths[0:1]
            for k in range(1, TOP_K):
                chosen = chosen | (expert == paths[k : k + 1])
            chosen_out[b] = low(chosen)
            mine = [
                jnp.max((paths == first_expert + j).astype(jnp.float32), axis=0, keepdims=True)
                for j in range(count)
            ]
            mine = jnp.concatenate(mine + [jnp.zeros((8 - count, rows), jnp.float32)], axis=0)
            place = jnp.where(mine > 0.5, dot(low(mine), before), -10000.0)
            places[...] = place
            for j in range(count):
                pick_out[b, j * CAP : (j + 1) * CAP, :] = low(
                    slot == place[j : j + 1].astype(jnp.int32)
                )
            turned = places[...].T.astype(jnp.int32)
            pick_t = turned[:, 0:1] == lane
            for j in range(1, count):
                pick_t = pick_t & (lane < j * CAP) | (turned[:, j : j + 1] == lane - j * CAP)
            pick_t_out[b] = low(pick_t)

        depth = small_out.shape[2] // 16
        for b in range(16):
            small = land[b, layer * known + 16 : (layer + 1) * known, :]
            small_out[layer, :, b * depth : (b + 1) * depth] = small[:, :depth]

    tables(0, pick_0, pick_t_0, chosen_0)
    hop(2)
    tables(1, pick_1, pick_t_1, chosen_1)
    hop(3)
    spreads[1].finish()
    layer_1 = pltpu.make_async_copy(parts.at[1], parts_out, lsem.at[0])
    layer_1.start()
    for z in range(4):

        @pl.when((z <= d) & (d < 3))
        def _():
            along(parts.at[0], z, True).wait_send()

        @pl.when((z >= d) & (d > 0))
        def _():
            along(parts.at[0], z, False).wait_send()

    own_columns.wait()
    layer_1.wait()
    gates.finish()


def prepare(x, group, gate, count, rows, depth, collective_id):
    known, width = x.shape
    bf = jnp.bfloat16
    anywhere = pl.BlockSpec(memory_space=pl.ANY)
    near = pl.BlockSpec(memory_space=pltpu.VMEM)
    return pl.pallas_call(
        prepare_kernel,
        out_shape=[
            jax.ShapeDtypeStruct((16, count * CAP, rows), bf),
            jax.ShapeDtypeStruct((16, count * CAP, rows), bf),
            jax.ShapeDtypeStruct((16, rows, count * CAP), bf),
            jax.ShapeDtypeStruct((16, rows, count * CAP), bf),
            jax.ShapeDtypeStruct((16, EXPERTS, rows), bf),
            jax.ShapeDtypeStruct((16, EXPERTS, rows), bf),
            jax.ShapeDtypeStruct((2, known - 16, 16 * depth), bf),
            jax.ShapeDtypeStruct((4,) + group.shape, bf),
            jax.ShapeDtypeStruct(group.shape, bf),
            jax.ShapeDtypeStruct(share_shape(gate), bf),
        ],
        in_specs=[anywhere] * 3,
        out_specs=[near] * 7 + [anywhere] * 3,
        scratch_shapes=[
            pltpu.VMEM((2 * known, width), bf),
            pltpu.VMEM((8, rows), jnp.float32),
            pltpu.VMEM((2,) + group.shape, bf),
            pltpu.VMEM((2,) + group.shape, bf),
            DMA((3,)),
            DMA((3, 2)),
            DMA((2, 4, 2)),
            DMA((2, 4)),
            DMA((4,)),
        ]
        + gather_scratch(2 * known, width),
        compiler_params=pltpu.CompilerParams(
            collective_id=collective_id, has_side_effects=True, vmem_limit_bytes=60 << 20
        ),
        cost_estimate=cost(),
        name="prepare",
    )(x, group, gate)


def share(ref):
    count = ref.shape[0] // 4
    return ref.at[pl.ds(lax.axis_index("seq") * count, count)]


def share_shape(array):
    return (array.shape[0] // 4,) + array.shape[1:]


def pick_weights(own_refs, other_refs, held, sems, own_layer):
    own_refs = [share(ref) for ref in own_refs]
    mine = lax.axis_index("section") == own_layer

    @pl.when(mine)
    def _():
        for k, ref in enumerate(own_refs):
            pltpu.make_async_copy(ref, held[k], sems.at[k]).start()

    @pl.when(jnp.logical_not(mine))
    def _():
        for k, ref in enumerate(other_refs):
            pltpu.make_async_copy(ref, held[k], sems.at[k]).start()

    def ready(k):
        pltpu.make_async_copy(own_refs[k], held[k], sems.at[k]).wait()

    return ready


def expert_forward_kernel(
    layer, x_ref, pick_ref, chosen_ref, router_ref, mine_ref,
    wg_own, wu_own, wd_own, wg_other, wu_other, wd_other,
    rows_out, gate_out, up_out, hidden_out, slot_gate_out, y_out,
    wg, wu, wd, rows, gate, up, hidden, slot_gate, y, wsem, osem, carry_sem, *gather
):
    count = wg.shape[0]
    carried = None
    if layer == 0:
        carried = Carried((None,), (share(wd_own),), (wd_other,), carry_sem)
        ready = pick_weights((wg_own, wu_own), (wg_other, wu_other), (wg, wu), wsem, layer)
    else:
        ready = pick_weights(
            (wg_own, wu_own, wd_own), (wg_other, wu_other, wd_other), (wg, wu, wd), wsem, layer
        )
    land = gather[0]
    d = lax.axis_index("dp")

    def outs(z):
        part = pl.ds(z * 4 * CAP, 4 * CAP)
        return [
            pltpu.make_async_copy(held.at[:, part], out.at[:, part], osem.at[k, z])
            for k, (held, out) in enumerate(
                ((rows, rows_out), (gate, gate_out), (up, up_out), (hidden, hidden_out), (slot_gate, slot_gate_out))
            )
        ] + [pltpu.make_async_copy(y.at[pl.ds(z * 4, 4)], y_out.at[pl.ds(z * 4, 4)], osem.at[5, z])]

    def down(z):
        part = pl.ds(z * 4 * CAP, 4 * CAP)

        @pl.loop(0, count)
        def _(j):
            result = low(dot(hidden[j, part, :], wd[j]))
            for q in range(4):
                y[z * 4 + q, pl.ds(j * CAP, CAP), :] = result[q * CAP : (q + 1) * CAP]

    def compute(z):
        @pl.when(z == d)
        def _():
            for k in range(2 if layer == 0 else 3):
                ready(k)

        for q in range(4):
            b = z * 4 + q
            picked = low(dot(pick_ref[b], land[b]))
            for j in range(count):
                rows[j, pl.ds(b * CAP, CAP), :] = picked[j * CAP : (j + 1) * CAP]
        part = pl.ds(z * 4 * CAP, 4 * CAP)

        @pl.loop(0, count)
        def _(j):
            x = rows[j, part, :]
            g = dot(x, wg[j])
            u = dot(x, wu[j])
            logits = dot_t(x, router_ref[...])
            for q in range(4):
                b = z * 4 + q
                slots = slice(q * CAP, (q + 1) * CAP)
                seen = dot_t(pick_ref[b, pl.ds(j * CAP, CAP), :], chosen_ref[b])
                masked = jnp.where(seen > 0.5, logits[slots], -1e30)
                power = jnp.exp(masked - jnp.max(masked, axis=1, keepdims=True))
                own = jnp.sum(power * mine_ref[j], axis=1, keepdims=True)
                value = own / jnp.sum(power, axis=1, keepdims=True)
                slot_gate[j, pl.ds(b * CAP, CAP), :] = jnp.broadcast_to(value, (CAP, 128))
            gate[j, part, :] = low(g)
            up[j, part, :] = low(u)
            h = low(g * jax.nn.sigmoid(g) * u * slot_gate[j, part, :][:, :1])
            hidden[j, part, :] = h

        if layer != 0:
            down(z)
        for copy in outs(z)[: 5 if layer == 0 else 6]:
            copy.start()

    gather_blocks(x_ref, gather, compute, carried)
    if layer == 0:
        carried.finish()
        ready = pick_weights((wd_own,), (wd_other,), (wd,), wsem, layer)
        ready(0)
        for z in range(4):
            down(z)
            outs(z)[5].start()
    for z in range(4):
        for copy in outs(z):
            copy.wait()


def expert_forward(layer, x, pick, chosen, router, mine, own, other, collective_id):
    count, width, units = share_shape(own[0])
    rows = x.shape[0]
    slots = 16 * CAP
    bf = jnp.bfloat16
    anywhere = pl.BlockSpec(memory_space=pl.ANY)
    near = pl.BlockSpec(memory_space=pltpu.VMEM)
    results = [
        ((count, slots, width), bf),
        ((count, slots, units), bf),
        ((count, slots, units), bf),
        ((count, slots, units), bf),
        ((count, slots, 128), jnp.float32),
        ((16, count * CAP, width), bf),
    ]

    def kernel(*refs):
        if layer == 0:
            refs = refs[:10] + refs[16:17] + refs[10:16] + refs[17:]
        expert_forward_kernel(layer, *refs)

    shapes = [jax.ShapeDtypeStruct(*result) for result in results]
    if layer == 0:
        shapes.append(jax.ShapeDtypeStruct(share_shape(own[2]), bf))
        other = other[:2]
    operands = (x, pick, chosen, router, mine, *own, *other)
    return pl.pallas_call(
        kernel,
        out_shape=shapes,
        in_specs=[anywhere, near, near, near, near] + [anywhere] * (len(operands) - 5),
        out_specs=[anywhere] * len(shapes),
        scratch_shapes=[pltpu.VMEM(share_shape(weight), bf) for weight in own]
        + [pltpu.VMEM(*result) for result in results]
        + [DMA((3,)), DMA((6, 4)), DMA((1, 2))]
        + gather_scratch(rows, width),
        compiler_params=pltpu.CompilerParams(
            collective_id=collective_id, has_side_effects=True, vmem_limit_bytes=60 << 20
        ),
        cost_estimate=cost(),
        name="expert_forward",
    )(*operands)


class Products:
    def __init__(self, pairs, outs, held, sems):
        self.units = []
        count = outs[0].shape[0]
        for j in range(count):
            at, out_at = 0, 0
            for left, rights in pairs:
                first = at
                loads = [(left, at)] + [(right, at + 1 + k) for k, right in enumerate(rights)]
                at += len(loads)
                for k in range(len(rights)):
                    self.units.append((j, first, first + 1 + k, out_at, loads, k == 0, k + 1 == len(rights)))
                    out_at += 1
        self.count, self.pairs, self.outs, self.held, self.sems = count, at, outs, held, sems

    def load(self, j, source, at):
        return pltpu.make_async_copy(source.at[j], self.held[at], self.sems.at[at])

    def store(self, j, k):
        at = self.pairs + k
        return pltpu.make_async_copy(self.held[at], self.outs[k].at[j], self.sems.at[at])

    def start(self):
        for j, _, _, _, loads, first, _ in self.units:
            if j == 0 and first:
                for source, at in loads:
                    self.load(0, source, at).start()

    def step(self, i):
        for number, (j, left, right, out, loads, first, last) in enumerate(self.units):

            @pl.when(i == number * (PIECES // 2))
            def _():
                if first:
                    for source, at in loads:
                        self.load(j, source, at).wait()
                if j > 0:
                    self.store(j - 1, out).wait()
                a, b, c = self.held[left], self.held[right], self.held[self.pairs + out]

                @pl.loop(0, a.shape[1] // 256)
                def _(m):
                    columns = pl.ds(pl.multiple_of(m * 256, 256), 256)
                    c[columns, :] = low(t_dot(a[:, columns], b[...]))

                self.store(j, out).start()
                if last and j + 1 < self.count:
                    for source, at in loads:
                        self.load(j + 1, source, at).start()

    def finish(self):
        for k in range(len(self.outs)):
            self.store(self.count - 1, k).wait()


def far_first(d, q):
    inner = (d % 3 + 2) // 3
    base = 3 - q + inner * (q // 2) * (2 * q - 5)
    mirrored = d // 2
    return base * (1 - 2 * mirrored) + 3 * mirrored


def near_first(d, q):
    inner = (d % 3 + 2) // 3
    base = q + inner * (1 - q // 2) * (1 - 2 * q)
    mirrored = d // 2
    return base * (1 - 2 * mirrored) + 3 * mirrored


def combine_kernel(sections, spreads, pairs, pick_ref, y_ref, *refs):
    kept = len(sections)
    sources, refs = refs[:kept], refs[kept:]
    spread_sources, refs = refs[:spreads], refs[spreads:]
    spreads = spreads // 4
    factors = []
    for rights in pairs:
        factors.append((refs[0], refs[1 : 1 + rights]))
        refs = refs[1 + rights :]
    out_ref, *refs = refs
    targets, refs = refs[:kept], refs[kept:]
    spread_targets, refs = refs[:spreads], refs[spreads:]
    products = sum(pairs)
    product_outs, refs = refs[:products], refs[products:]
    y, sent, own, core_in, y_in, z_in, lsem, zs, zr, ys, yr, cs, cr, carry_sem, *refs = refs
    held, refs = refs[: 5 * spreads], refs[5 * spreads :]
    work = Products(factors, product_outs, refs[:-1], refs[-1]) if pairs else None
    carried = Carried(sections, sources, targets, carry_sem)
    spread = [SumSpread(spread_sources, spread_targets[0], held)] if spreads else []
    for side in spread:
        side.load()
    d, s = lax.axis_index("dp"), lax.axis_index("seq")
    piece = out_ref.shape[0] // PIECES

    def loaded(b):
        return pltpu.make_async_copy(y_ref.at[b], y.at[b], lsem.at[b])

    def column(across, other_core):
        return s ^ (2 * across) ^ other_core

    for i in range(4):
        z = far_first(d, i)
        for across in (1, 0):
            for other_core in (1, 0):
                loaded(z * 4 + column(across, other_core)).start()
    greet(d, s, carried.section, spreads > 0)
    carried.start()

    def rows(k):
        return pl.ds(pl.multiple_of(k * piece, piece), piece)

    def partial_sum(z, k, across, other_core):
        b = z * 4 + column(across, other_core)

        @pl.when(k == 0)
        def _():
            loaded(b).wait()

        return dot(pick_ref[b, rows(k), :], y[b])

    def core_copy(z, k, across):
        return remote(
            sent.at[z, across, rows(k)],
            core_in.at[z, across, rows(k)],
            cs.at[z, k, across],
            cr.at[z, k, across],
            seq=s ^ 1,
        )

    def y_copy(z, k):
        return remote(own.at[z, 1, rows(k)], y_in.at[z, rows(k)], ys.at[z, k], yr.at[z, k], seq=s ^ 2)

    def z_copy(z, k, right):
        target = d + 1 if right else d - 1
        return remote(
            own.at[z, 0, rows(k)],
            z_in.at[int(right), z, rows(k)],
            zs.at[z, k],
            zr.at[int(right), z, k],
            dp=target,
        )

    def start(i):
        z, k = far_first(d, i // PIECES), i % PIECES
        sent[z, 1, rows(k), :] = low(partial_sum(z, k, 1, 1))
        core_copy(z, k, 1).start()
        total = partial_sum(z, k, 1, 0)
        core_copy(z, k, 1).wait_recv()
        own[z, 1, rows(k), :] = low(total + core_in[z, 1, rows(k), :].astype(jnp.float32))
        y_copy(z, k).start()
        sent[z, 0, rows(k), :] = low(partial_sum(z, k, 0, 1))
        core_copy(z, k, 0).start()

    start(0)
    for side in spread:
        side.start()
    if work:
        work.start()

    @pl.loop(0, 4 * PIECES)
    def _(i):
        @pl.when(i < 4 * PIECES - 1)
        def _():
            start(i + 1)

        if work:
            work.step(i)

        z, k = far_first(d, i // PIECES), i % PIECES
        total = partial_sum(z, k, 0, 0)
        core_copy(z, k, 0).wait_recv()
        total = total + core_in[z, 0, rows(k), :].astype(jnp.float32)
        y_copy(z, k).wait_recv()
        total = total + y_in[z, rows(k), :].astype(jnp.float32)

        @pl.when(z < d)
        def _():
            @pl.when(d < 3)
            def _():
                z_copy(z, k, False).wait_recv()
                own[z, 0, rows(k), :] = low(total + z_in[0, z, rows(k), :].astype(jnp.float32))

            @pl.when(d == 3)
            def _():
                own[z, 0, rows(k), :] = low(total)

            z_copy(z, k, False).start()

        @pl.when(z > d)
        def _():
            @pl.when(d > 0)
            def _():
                z_copy(z, k, True).wait_recv()
                own[z, 0, rows(k), :] = low(total + z_in[1, z, rows(k), :].astype(jnp.float32))

            @pl.when(d == 0)
            def _():
                own[z, 0, rows(k), :] = low(total)

            z_copy(z, k, True).start()

        @pl.when(z == d)
        def _():
            out_ref[rows(k), :] = total

    for k in range(PIECES):

        @pl.when(d < 3)
        def _():
            z_copy(d, k, False).wait_recv()
            out_ref[rows(k), :] += z_in[0, d, rows(k), :].astype(jnp.float32)

        @pl.when(d > 0)
        def _():
            z_copy(d, k, True).wait_recv()
            out_ref[rows(k), :] += z_in[1, d, rows(k), :].astype(jnp.float32)

    for z in range(4):
        for k in range(PIECES):
            core_copy(z, k, 0).wait_send()
            core_copy(z, k, 1).wait_send()
            y_copy(z, k).wait_send()

            @pl.when(z < d)
            def _():
                z_copy(z, k, False).wait_send()

            @pl.when(z > d)
            def _():
                z_copy(z, k, True).wait_send()

    carried.finish()
    for side in spread:
        side.finish()
    if work:
        work.finish()


def combine(pick_t, y, collective_id, carry, spread=(), products=()):
    rows, width = pick_t.shape[1], y.shape[2]
    anywhere = pl.BlockSpec(memory_space=pl.ANY)
    near = pl.BlockSpec(memory_space=pltpu.VMEM)
    sections = tuple(to for to, _ in carry)
    arrays = [array for _, array in carry]

    carries = [jax.ShapeDtypeStruct(array.shape, array.dtype) for array in arrays]
    if spread:
        carries.append(jax.ShapeDtypeStruct(parts_shape(spread[0]), jnp.bfloat16))
    arrays = arrays + list(spread)
    pairs = [len(rights) for _, rights in products]
    factors = [factor for left, rights in products for factor in (left, *rights)]
    outs = [
        jax.ShapeDtypeStruct((left.shape[0], left.shape[2], right.shape[2]), jnp.bfloat16)
        for left, rights in products
        for right in rights
    ]
    held = [pltpu.VMEM(array.shape[1:], jnp.bfloat16) for array in factors + outs]
    held = held + [DMA((len(held),))] if held else []

    def kernel(*refs):
        combine_kernel(sections, len(spread), pairs, *refs)

    def blocks(*lead):
        return pltpu.VMEM(lead + (rows, width), jnp.bfloat16)

    return pl.pallas_call(
        kernel,
        out_shape=[jax.ShapeDtypeStruct((rows, width), jnp.float32)]
        + carries
        + outs,
        in_specs=[near, anywhere] + [anywhere] * (len(arrays) + len(factors)),
        out_specs=[near] + [anywhere] * (len(carries) + len(outs)),
        scratch_shapes=[
            pltpu.VMEM(y.shape, jnp.bfloat16),
            blocks(4, 2),
            blocks(4, 2),
            blocks(4, 2),
            blocks(4),
            blocks(2, 4),
            DMA((16,)),
            DMA((4, PIECES)),
            DMA((2, 4, PIECES)),
            DMA((4, PIECES)),
            DMA((4, PIECES)),
            DMA((4, PIECES, 2)),
            DMA((4, PIECES, 2)),
            DMA((max(1, len(carry)), 2)),
        ]
        + sum_scratch(spread)
        + held,
        compiler_params=pltpu.CompilerParams(
            collective_id=collective_id, has_side_effects=True, vmem_limit_bytes=60 << 20
        ),
        cost_estimate=cost(),
        name="combine",
    )(pick_t, y, *arrays, *factors)


def expert_backward_kernel(
    layer, sections, x_ref, pick_ref, gate_in, up_in, slot_gate_in,
    wg_own, wu_own, wd_own, wg_other, wu_other, wd_other, *refs
):
    kept = len(sections)
    sources, refs = refs[:kept], refs[kept:]
    rows_out, gate_out, up_out, term_out, y_out, *refs = refs
    targets, refs = refs[:kept], refs[kept:]
    wg, wu, wd, rows, gate, up, slot_gate, y, wsem, isem, osem, carry_sem, *gather = refs
    carried = Carried(sections, sources, targets, carry_sem)
    count = wg.shape[0]
    ready = pick_weights(
        (wg_own, wu_own, wd_own), (wg_other, wu_other, wd_other), (wg, wu, wd), wsem, layer
    )
    land = gather[0]
    d = lax.axis_index("dp")
    ins = [
        pltpu.make_async_copy(src, held, isem.at[k])
        for k, (src, held) in enumerate(((gate_in, gate), (up_in, up), (slot_gate_in, slot_gate)))
    ]
    for copy in ins:
        copy.start()

    def outs(z):
        part = pl.ds(z * 4 * CAP, 4 * CAP)
        return [
            pltpu.make_async_copy(held.at[:, part], out.at[:, part], osem.at[k, z])
            for k, (held, out) in enumerate(
                ((rows, rows_out), (gate, gate_out), (up, up_out), (slot_gate, term_out))
            )
        ] + [pltpu.make_async_copy(y.at[pl.ds(z * 4, 4)], y_out.at[pl.ds(z * 4, 4)], osem.at[4, z])]

    def compute(z):
        @pl.when(z == d)
        def _():
            for k in range(3):
                ready(k)
            for copy in ins:
                copy.wait()

        for q in range(4):
            b = z * 4 + q
            picked = low(dot(pick_ref[b], land[b]))
            for j in range(count):
                rows[j, pl.ds(b * CAP, CAP), :] = picked[j * CAP : (j + 1) * CAP]
        part = pl.ds(z * 4 * CAP, 4 * CAP)

        @pl.loop(0, count)
        def _(j):
            plain = dot_t(rows[j, part, :], wd[j])
            g = gate[j, part, :].astype(jnp.float32)
            u = up[j, part, :].astype(jnp.float32)
            sigmoid = jax.nn.sigmoid(g)
            active = g * sigmoid
            term = jnp.sum(plain * (active * u), axis=1, keepdims=True)
            grad = plain * slot_gate[j, part, :][:, :1]
            dg = low(grad * u * sigmoid * (1.0 + g * (1.0 - sigmoid)))
            du = low(grad * active)
            slot_gate[j, part, :] = jnp.broadcast_to(term, (4 * CAP, 128))
            gate[j, part, :] = dg
            up[j, part, :] = du
            result = low(dot_t(dg, wg[j]) + dot_t(du, wu[j]))
            for q in range(4):
                y[z * 4 + q, pl.ds(j * CAP, CAP), :] = result[q * CAP : (q + 1) * CAP]

        for copy in outs(z):
            copy.start()

    gather_blocks(x_ref, gather, compute, carried)
    carried.finish()
    for z in range(4):
        for copy in outs(z):
            copy.wait()


def expert_backward(layer, x, pick, gate, up, slot_gate, own, other, collective_id, carry):
    count, width, units = share_shape(own[0])
    rows = x.shape[0]
    slots = 16 * CAP
    bf = jnp.bfloat16
    anywhere = pl.BlockSpec(memory_space=pl.ANY)
    near = pl.BlockSpec(memory_space=pltpu.VMEM)
    results = [
        ((count, slots, width), bf),
        ((count, slots, units), bf),
        ((count, slots, units), bf),
        ((count, slots, 128), jnp.float32),
        ((16, count * CAP, width), bf),
    ]
    sections = tuple(to for to, _ in carry)
    arrays = [array for _, array in carry]

    def kernel(*refs):
        expert_backward_kernel(layer, sections, *refs)

    return pl.pallas_call(
        kernel,
        out_shape=[jax.ShapeDtypeStruct(*result) for result in results]
        + [jax.ShapeDtypeStruct(array.shape, array.dtype) for array in arrays],
        in_specs=[anywhere, near] + [anywhere] * (9 + len(arrays)),
        out_specs=[anywhere] * (5 + len(arrays)),
        scratch_shapes=[pltpu.VMEM(share_shape(weight), bf) for weight in own]
        + [pltpu.VMEM(*result) for result in results]
        + [DMA((3,)), DMA((3,)), DMA((5, 4)), DMA((max(1, len(arrays)), 2))]
        + gather_scratch(rows, width),
        compiler_params=pltpu.CompilerParams(
            collective_id=collective_id, has_side_effects=True, vmem_limit_bytes=60 << 20
        ),
        cost_estimate=cost(),
        name="expert_backward",
    )(x, pick, gate, up, slot_gate, *own, *other, *arrays)


def rope(x, cos_table, sin_table):
    lane = lax.broadcasted_iota(jnp.int32, x.shape, 1)
    turned = jnp.where(lane % HEAD_DIM < HEAD_DIM // 2, pltpu.roll(x, 128 - HEAD_DIM // 2, 1), pltpu.roll(x, HEAD_DIM // 2, 1))
    return x * cos_table + turned * sin_table


def seq_greet(s, section, spread=False):
    barrier = pltpu.get_barrier_semaphore()
    devices = [dict(seq=s ^ 1), dict(seq=s ^ 2), dict(section=1 - section)]
    if spread:
        devices.append(dict(seq=s ^ 3))
    for device in devices:
        pl.semaphore_signal(barrier, inc=1, device_id=device, device_id_type=MESH)
    pl.semaphore_wait(barrier, len(devices))


def seq_scratch(rows, width):
    return [
        pltpu.VMEM((4, rows, width), jnp.bfloat16),
        pltpu.VMEM((2, rows, width), jnp.bfloat16),
        pltpu.VMEM((2, rows, width), jnp.bfloat16),
        pltpu.VMEM((rows, width), jnp.bfloat16),
        pltpu.VMEM((rows, width), jnp.bfloat16),
        DMA(()),
        DMA((4, 2)),
        DMA((3, 2)),
    ]


class Line:
    def __init__(self, scratch):
        self.land, self.sent, self.core_in, self.y_sent, self.y_in, self.lsem, self.ag, self.rs = scratch
        self.s = lax.axis_index("seq")

    def hop(self, src, dst, sems, k, flip):
        return remote(src, dst, sems.at[k, 0], sems.at[k, 1], seq=self.s ^ flip)

    def gather(self, x_ref, use):
        s, land = self.s, self.land
        own = pltpu.make_async_copy(x_ref, land.at[s], self.lsem)
        own.start()
        over = self.hop(x_ref, land.at[s], self.ag, 0, 2)
        beside = self.hop(x_ref, land.at[s], self.ag, 1, 1)
        over.start()
        beside.start()
        own.wait()
        use(s)
        beside.wait_recv()
        use(s ^ 1)
        over.wait_recv()
        further = self.hop(land.at[s ^ 2], land.at[s ^ 2], self.ag, 2, 1)
        further.start()
        use(s ^ 2)
        further.wait_recv()
        use(s ^ 3)
        over.wait_send()
        beside.wait_send()
        further.wait_send()

    def hand_over(self, t, partial, out_ref):
        relation = t ^ self.s

        @pl.when(relation == 3)
        def _():
            self.sent[0] = low(partial[...])
            self.hop(self.sent.at[0], self.core_in.at[0], self.rs, 0, 1).start()

        @pl.when(relation == 2)
        def _():
            self.hop(self.sent.at[0], self.core_in.at[0], self.rs, 0, 1).wait_recv()
            self.y_sent[...] = low(partial[...] + self.core_in[0].astype(jnp.float32))
            self.hop(self.y_sent, self.y_in, self.rs, 1, 2).start()

        @pl.when(relation == 1)
        def _():
            self.sent[1] = low(partial[...])
            self.hop(self.sent.at[1], self.core_in.at[1], self.rs, 2, 1).start()

        @pl.when(relation == 0)
        def _():
            out_ref[...] = partial[...]

    def finish(self, out_ref):
        self.hop(self.sent.at[1], self.core_in.at[1], self.rs, 2, 1).wait()
        out_ref[...] += self.core_in[1].astype(jnp.float32)
        self.hop(self.y_sent, self.y_in, self.rs, 1, 2).wait()
        out_ref[...] += self.y_in[...].astype(jnp.float32)
        self.hop(self.sent.at[0], self.core_in.at[0], self.rs, 0, 1).wait_send()


def attention_forward_kernel(sections, x_ref, qkv_ref, wo_ref, cos_ref, sin_ref, *refs):
    kept = len(sections)
    sources, refs = refs[:kept], refs[kept:]
    sources = [share(ref) if to is None else ref for to, ref in zip(sections, sources)]
    out_ref, all_out, heads_out, lse_out, ot_out, *refs = refs
    targets, refs = refs[:kept], refs[kept:]
    wqkv, wo, heads, lse, ot, partial, wsem, osem, carry_sem, *line = refs
    line = Line(line)
    carried = Carried(sections, sources, targets, carry_sem)
    s = line.s
    rows = out_ref.shape[0]
    kv = heads.shape[0] // (GROUP + 2)
    queries = GROUP * kv
    loads = [pltpu.make_async_copy(qkv_ref, wqkv, wsem.at[0]), pltpu.make_async_copy(wo_ref, wo, wsem.at[1])]
    for load in loads:
        load.start()
    seq_greet(s, carried.section)
    carried.start()
    lse[...] = jnp.zeros_like(lse)

    def project(t):
        part = pl.ds(pl.multiple_of(t * rows, rows), rows)

        @pl.when(t == s)
        def _():
            loads[0].wait()

        qkv = low(dot(line.land[t], wqkv[...]))
        for chunk in range((queries + kv) // 2):
            x = qkv[:, chunk * 128 : (chunk + 1) * 128].astype(jnp.float32)
            x = low(rope(x, cos_ref[part, :], sin_ref[part, :]))
            heads[2 * chunk, part, :] = x[:, :HEAD_DIM]
            heads[2 * chunk + 1, part, :] = x[:, HEAD_DIM:]
        for j in range(kv):
            begin = (queries + kv + j) * HEAD_DIM
            heads[queries + kv + j, part, :] = qkv[:, begin : begin + HEAD_DIM]

    line.gather(x_ref, project)
    saves = [pltpu.make_async_copy(line.land, all_out, osem.at[0]), pltpu.make_async_copy(heads, heads_out, osem.at[1])]
    for save in saves:
        save.start()
    loads[1].wait()

    def attend(block):
        keys = (block + 1) * rows
        columns = slice(block * rows, (block + 1) * rows)

        @pl.loop(0, queries)
        def _(h):
            j = h // GROUP
            scores = dot_t(heads[queries + j, :keys, :], heads[h, columns, :]) * 0.125
            key_at = lax.broadcasted_iota(jnp.int32, scores.shape, 0)
            query_at = lax.broadcasted_iota(jnp.int32, scores.shape, 1) + block * rows
            scores = jnp.where(key_at <= query_at, scores, -jnp.inf)
            peak = jnp.max(scores, axis=0, keepdims=True)
            power = jnp.exp(scores - peak)
            total = jnp.sum(power, axis=0, keepdims=True)
            attended = t_dot(heads[queries + kv + j, :keys, :], low(power / total))
            ot[pl.ds(pl.multiple_of(h * HEAD_DIM, HEAD_DIM), HEAD_DIM), columns] = low(attended)
            lse[pl.ds(h, 1), columns] = peak + jnp.log(total)

        partial[...] = t_dot(ot[:, columns], wo[...])

    @pl.loop(0, 4)
    def _(i):
        t = s ^ (3 - i)
        for block in range(4):

            @pl.when(t == block)
            def _():
                attend(block)

        line.hand_over(t, partial, out_ref)

    saves += [pltpu.make_async_copy(lse, lse_out, osem.at[2]), pltpu.make_async_copy(ot, ot_out, osem.at[3])]
    for save in saves[2:]:
        save.start()
    line.finish(out_ref)
    carried.finish()
    for save in saves:
        save.wait()


def attention_forward_call(x, qkv_w, out_w, tables, collective_id, carry):
    rows, width = x.shape
    local_heads = qkv_w.shape[1] // HEAD_DIM
    bf, f32 = jnp.bfloat16, jnp.float32
    anywhere = pl.BlockSpec(memory_space=pl.ANY)
    near = pl.BlockSpec(memory_space=pltpu.VMEM)
    sections = tuple(to for to, _ in carry)
    arrays = [array for _, array in carry]
    results = [
        ((rows, width), f32),
        ((4, rows, width), bf),
        ((local_heads, 4 * rows, HEAD_DIM), bf),
        ((8, 4 * rows), f32),
        ((out_w.shape[0], 4 * rows), bf),
    ]

    def kernel(*refs):
        attention_forward_kernel(sections, *refs)

    return pl.pallas_call(
        kernel,
        out_shape=[jax.ShapeDtypeStruct(*result) for result in results]
        + [
            jax.ShapeDtypeStruct(share_shape(array) if to is None else array.shape, array.dtype)
            for to, array in carry
        ],
        in_specs=[anywhere] * 3 + [near] * 2 + [anywhere] * len(arrays),
        out_specs=[near] + [anywhere] * (4 + len(arrays)),
        scratch_shapes=[
            pltpu.VMEM(qkv_w.shape, bf),
            pltpu.VMEM(out_w.shape, bf),
            pltpu.VMEM(*results[2]),
            pltpu.VMEM(*results[3]),
            pltpu.VMEM(*results[4]),
            pltpu.VMEM((rows, width), f32),
            DMA((2,)),
            DMA((4,)),
            DMA((max(1, len(arrays)), 2)),
        ]
        + seq_scratch(rows, width),
        compiler_params=pltpu.CompilerParams(
            collective_id=collective_id, has_side_effects=True, vmem_limit_bytes=60 << 20
        ),
        cost_estimate=cost(),
        name="attention_forward",
    )(x, qkv_w, out_w, *tables, *arrays)


def attention_backward_kernel(
    sections, spreads, x_ref, qkv_ref, wo_ref, cos_ref, sin_ref, heads_in, lse_ref, *refs
):
    kept = len(sections)
    sources, refs = refs[:kept], refs[kept:]
    spread_sources, refs = refs[:spreads], refs[spreads:]
    spreads = spreads // 4
    out_ref, all_out, grads_out, *refs = refs
    targets, refs = refs[:kept], refs[kept:]
    spread_targets, refs = refs[:spreads], refs[spreads:]
    held, refs = refs[: 5 * spreads], refs[5 * spreads :]
    wqkv, wo, heads, douts, dk, dv, dqt, grads, partial, wsem, osem, carry_sem, *line = refs
    spread = [SumSpread(spread_sources, spread_targets[0], held)] if spreads else []
    for side in spread:
        side.load()
    line = Line(line)
    carried = Carried(sections, sources, targets, carry_sem)
    s = line.s
    rows = out_ref.shape[0]
    kv = heads.shape[0] // (GROUP + 2)
    queries = GROUP * kv
    loads = [
        pltpu.make_async_copy(wo_ref, wo, wsem.at[0]),
        pltpu.make_async_copy(qkv_ref, wqkv, wsem.at[1]),
        pltpu.make_async_copy(heads_in, heads, wsem.at[2]),
    ]
    for load in loads:
        load.start()
    seq_greet(s, carried.section, spreads > 0)
    carried.start()
    dk[...] = jnp.zeros_like(dk)
    dv[...] = jnp.zeros_like(dv)

    def project(t):
        part = pl.ds(pl.multiple_of(t * rows, rows), rows)

        @pl.when(t == s)
        def _():
            loads[0].wait()

        grad = low(dot_t(line.land[t], wo[...]))
        for h in range(queries):
            douts[h, part, :] = grad[:, h * HEAD_DIM : (h + 1) * HEAD_DIM]

    line.gather(x_ref, project)
    saves = [pltpu.make_async_copy(line.land, all_out, osem.at[0])]
    saves[0].start()
    for side in spread:
        side.start()
    loads[1].wait()
    loads[2].wait()

    for block in (3, 2, 1, 0):
        keys = (block + 1) * rows
        part = slice(block * rows, (block + 1) * rows)

        @pl.loop(0, queries)
        def _(h):
            j = h // GROUP
            key = heads[queries + j, :keys, :]
            query = heads[h, part, :]
            grad = douts[h, part, :]
            scores = dot_t(key, query) * 0.125
            key_at = lax.broadcasted_iota(jnp.int32, scores.shape, 0)
            query_at = lax.broadcasted_iota(jnp.int32, scores.shape, 1) + block * rows
            scores = jnp.where(key_at <= query_at, scores, -jnp.inf)
            probs = jnp.exp(scores - lse_ref[pl.ds(h, 1), part])
            dprobs = dot_t(heads[queries + kv + j, :keys, :], grad)
            mean = jnp.sum(probs * dprobs, axis=0, keepdims=True)
            dscores = low(probs * (dprobs - mean))
            dk[j, :keys, :] += dot(dscores, query) * 0.125
            dv[j, :keys, :] += dot(low(probs), grad)
            dqt[pl.ds(pl.multiple_of(h * HEAD_DIM, HEAD_DIM), HEAD_DIM), :] = t_dot(key, dscores) * 0.125

        cos_part, sin_part = cos_ref[part, :], -sin_ref[part, :]
        dq = dqt[...].T
        for chunk in range(queries // 2):
            lanes = slice(chunk * 128, (chunk + 1) * 128)
            grads[part, lanes] = low(rope(dq[:, lanes], cos_part, sin_part))
        for pair in range(kv // 2):
            both = jnp.concatenate([dk[2 * pair, part, :], dk[2 * pair + 1, part, :]], axis=1)
            begin = queries * HEAD_DIM + pair * 128
            grads[part, begin : begin + 128] = low(rope(both, cos_part, sin_part))
            both = jnp.concatenate([dv[2 * pair, part, :], dv[2 * pair + 1, part, :]], axis=1)
            begin = (queries + kv) * HEAD_DIM + pair * 128
            grads[part, begin : begin + 128] = low(both)
        partial[...] = dot_t(grads[part, :], wqkv[...])
        line.hand_over(block, partial, out_ref)

    saves.append(pltpu.make_async_copy(grads, grads_out, osem.at[1]))
    saves[1].start()
    line.finish(out_ref)
    carried.finish()
    for side in spread:
        side.finish()
    for save in saves:
        save.wait()


def attention_backward_call(x, qkv_w, out_w, tables, heads, lse, collective_id, carry, spread=()):
    rows, width = x.shape
    bf, f32 = jnp.bfloat16, jnp.float32
    anywhere = pl.BlockSpec(memory_space=pl.ANY)
    near = pl.BlockSpec(memory_space=pltpu.VMEM)
    sections = tuple(to for to, _ in carry)
    arrays = [array for _, array in carry]
    results = [((rows, width), f32), ((4, rows, width), bf), ((4 * rows, qkv_w.shape[1]), bf)]
    kv = heads.shape[0] // (GROUP + 2)
    queries = GROUP * kv

    carries = [jax.ShapeDtypeStruct(array.shape, array.dtype) for array in arrays]
    if spread:
        carries.append(jax.ShapeDtypeStruct(parts_shape(spread[0]), bf))
    arrays = arrays + list(spread)

    def kernel(*refs):
        attention_backward_kernel(sections, len(spread), *refs)

    return pl.pallas_call(
        kernel,
        out_shape=[jax.ShapeDtypeStruct(*result) for result in results]
        + carries,
        in_specs=[anywhere] * 3 + [near] * 2 + [anywhere, near] + [anywhere] * len(arrays),
        out_specs=[near] + [anywhere] * (2 + len(carries)),
        scratch_shapes=sum_scratch(spread)
        + [
            pltpu.VMEM(qkv_w.shape, bf),
            pltpu.VMEM(out_w.shape, bf),
            pltpu.VMEM(heads.shape, bf),
            pltpu.VMEM((queries, 4 * rows, HEAD_DIM), bf),
            pltpu.VMEM((kv, 4 * rows, HEAD_DIM), f32),
            pltpu.VMEM((kv, 4 * rows, HEAD_DIM), f32),
            pltpu.VMEM((queries * HEAD_DIM, rows), f32),
            pltpu.VMEM(*results[2]),
            pltpu.VMEM((rows, width), f32),
            DMA((3,)),
            DMA((2,)),
            DMA((max(1, len(carry)), 2)),
        ]
        + seq_scratch(rows, width),
        compiler_params=pltpu.CompilerParams(
            collective_id=collective_id, has_side_effects=True, vmem_limit_bytes=60 << 20
        ),
        cost_estimate=cost(),
        name="attention_backward",
    )(x, qkv_w, out_w, *tables, heads, lse, *arrays)


def last_kernel(sections, own_0, own_1, in_0, in_1, cols_ref, cols_other, out_ref, out_other, *refs):
    kept = len(sections)
    sources, refs = refs[:kept], refs[kept:]
    down_out, cols_out, rows_out, *refs = refs
    targets, refs = refs[:kept], refs[kept:]
    cols_in, cols, out_in, out_sum, cols_sem, row_sem, swap_sem, carry_sem, *held = refs
    down = SumSpread((own_0, own_1, in_0, in_1), down_out, held)
    down.load()
    d, s, section = lax.axis_index("dp"), lax.axis_index("seq"), lax.axis_index("section")
    barrier = pltpu.get_barrier_semaphore()

    def signal(**device):
        pl.semaphore_signal(barrier, inc=1, device_id=device, device_id_type=MESH)

    for flip in (1, 2, 3):
        signal(seq=s ^ flip)
    signal(section=1 - section)

    @pl.when(d != s)
    def _():
        signal(dp=s, seq=d)
        pl.semaphore_wait(barrier, 5)

    @pl.when(d == s)
    def _():
        pl.semaphore_wait(barrier, 4)

    swaps = Carried((None, None), (cols_other, out_other), (cols_in, out_in), swap_sem)
    carried = Carried(sections, sources, targets, carry_sem)
    swaps.start()
    down.start()
    swaps.finish()
    carried.start()
    cols[...] = low(cols_ref[...].astype(jnp.float32) + cols_in[...].astype(jnp.float32))
    out_sum[...] = low(out_ref[...].astype(jnp.float32) + out_in[...].astype(jnp.float32))
    spread = Spread(cols, cols_out, cols_sem)
    spread.start()
    rows = remote(out_sum, rows_out, row_sem.at[0], row_sem.at[1], dp=s, seq=d)

    @pl.when(d != s)
    def _():
        rows.start()
        rows.wait()

    @pl.when(d == s)
    def _():
        rows_out[...] = out_sum[...]

    spread.finish()
    down.finish()
    carried.finish()


def last_exchange(downs, cols, cols_other, out, out_other, collective_id, carry):
    bf = jnp.bfloat16
    anywhere = pl.BlockSpec(memory_space=pl.ANY)
    near = pl.BlockSpec(memory_space=pltpu.VMEM)
    sections = tuple(to for to, _ in carry)
    arrays = [array for _, array in carry]

    def kernel(*refs):
        last_kernel(sections, *refs)

    return pl.pallas_call(
        kernel,
        out_shape=[
            jax.ShapeDtypeStruct(parts_shape(downs[0]), bf),
            *[jax.ShapeDtypeStruct(array.shape, array.dtype) for array in (cols, out, *arrays)],
        ],
        in_specs=[anywhere] * 4 + [near, anywhere, near, anywhere] + [anywhere] * len(arrays),
        out_specs=[anywhere, near, near] + [anywhere] * len(arrays),
        scratch_shapes=[
            pltpu.VMEM(cols.shape, bf),
            pltpu.VMEM(cols.shape, bf),
            pltpu.VMEM(out.shape, bf),
            pltpu.VMEM(out.shape, bf),
            DMA((4, 2)),
            DMA((2,)),
            DMA((2, 2)),
            DMA((max(1, len(arrays)), 2)),
        ]
        + sum_scratch(downs),
        compiler_params=pltpu.CompilerParams(
            collective_id=collective_id, has_side_effects=True, vmem_limit_bytes=60 << 20
        ),
        name="last_exchange",
    )(*downs, cols, cols_other, out, out_other, *arrays)


def wide_tables(length):
    half_dim = HEAD_DIM // 2
    frequency = 10000.0 ** (-np.arange(half_dim, dtype=np.float32) * 2.0 / HEAD_DIM)
    angles = np.arange(length, dtype=np.float32)[:, None] * frequency.astype(np.float32)[None, :]
    cos_table, sin_table = np.cos(angles), np.sin(angles)
    return (
        jnp.asarray(np.concatenate([cos_table] * 4, axis=1), jnp.float32),
        jnp.asarray(np.concatenate([-sin_table, sin_table] * 2, axis=1), jnp.float32),
    )


def token_choice(route):
    return route[..., None] == jnp.arange(EXPERTS, dtype=jnp.int32)


def routing(route_all, first_expert, count):
    chosen = jnp.any(token_choice(route_all), axis=2)
    blocks, rows = chosen.shape[:2]
    mine = lax.dynamic_slice_in_dim(chosen, first_expert, count, axis=2)
    chosen = low(jnp.transpose(chosen, (0, 2, 1)))
    earlier = jnp.tril(jnp.ones((rows, rows), jnp.bfloat16), -1)
    place = jnp.einsum(
        "ts,bsj->bjt", earlier, mine.astype(jnp.bfloat16), preferred_element_type=jnp.float32
    ).astype(jnp.int32)
    mine = jnp.transpose(mine, (0, 2, 1))
    place = jnp.where(mine, place, -1)
    slots = jnp.arange(CAP, dtype=jnp.int32)
    pick = low(place[:, :, None, :] == slots[None, None, :, None]).reshape(blocks, -1, rows)
    return chosen, pick, jnp.transpose(pick, (0, 2, 1))


def choose(pick, rows, count):
    picked = jnp.einsum("bct,btd->bcd", pick, rows, preferred_element_type=jnp.float32)
    blocks = pick.shape[0]
    picked = low(picked).reshape(blocks, count, CAP, -1)
    return jnp.transpose(picked, (1, 0, 2, 3)).reshape(count, blocks * CAP, -1)


def give_back(pick_t, slot_rows):
    blocks, rows = pick_t.shape[:2]
    count, _, width = slot_rows.shape
    slot_rows = jnp.transpose(slot_rows.reshape(count, blocks, CAP, width), (1, 0, 2, 3))
    slot_rows = slot_rows.reshape(blocks, count * CAP, width)
    total = jnp.einsum("btc,bcd->btd", pick_t, slot_rows, preferred_element_type=jnp.float32)
    return low(total).reshape(-1, width)


def each_dot(form, a, b):
    return jnp.einsum(form, a, b, preferred_element_type=jnp.float32)


def after(value, *others):
    return lax.optimization_barrier((value, *others))[0]


def has_kernels():
    return lax.axis_size("dp") == 4 and lax.axis_size("seq") == 4


def forward_layer(number, layer_in, picking, weights, experts, *carry):
    attn_scale, ffn_scale, qkv_w, out_w, router_w = weights
    chosen, pick, pick_t, first_expert = picking
    own, other = experts
    count = pick.shape[1] // CAP
    blocks, _, rows = chosen.shape
    received = []
    normed_input = low(rms_norm(layer_in, attn_scale))
    if has_kernels():
        branch, normed_all, heads, log_total, mixed_t, *received = attention_forward_call(
            normed_input, qkv_w, out_w, wide_tables(4 * layer_in.shape[0]), 9 + number, carry
        )
        attention_state = (normed_all.reshape(-1, layer_in.shape[1]), mixed_t, heads, log_total)
    else:
        received = [swap(array) if to is None else pass_to(array, to) for to, array in carry]
        normed_all = lax.all_gather(normed_input, "seq", axis=0, tiled=True)
        qkv = low(dot(normed_all, qkv_w))
        kv_width = KV_HEADS * HEAD_DIM // lax.axis_size("seq")
        q_width = GROUP * kv_width
        mixed, log_total, q_rot, k_rot, v_heads = attention_forward(
            qkv[:, :q_width], qkv[:, q_width : q_width + kv_width], qkv[:, q_width + kv_width :]
        )
        branch = lax.psum_scatter(low(dot(mixed, out_w)), "seq", scatter_dimension=0, tiled=True)
        attention_state = (normed_all, mixed.T, (q_rot, k_rot, v_heads), log_total)
    after_update = layer_in + branch.astype(jnp.float32)
    normed_ffn = low(rms_norm(after_update, ffn_scale))
    own_block = lax.axis_index("dp") * lax.axis_size("seq") + lax.axis_index("seq")
    own_chosen = lax.dynamic_index_in_dim(chosen, own_block, 0, keepdims=False)
    own_logits = jnp.where(own_chosen > 0, dot_t(router_w, normed_ffn), -jnp.inf)
    own_gates = jax.nn.softmax(own_logits, axis=0)
    if number == 0:
        other = other + (received[0],)
    mine = (
        jnp.arange(EXPERTS)[None, None, :] == first_expert + jnp.arange(count)[:, None, None]
    ).astype(jnp.float32)
    if has_kernels():
        *expert_state, slot_out = expert_forward(
            number, normed_ffn, pick, chosen, router_w, mine, own, other, 1 + number
        )
        if number == 0:
            *expert_state, slot_out, other_down = (*expert_state, slot_out)
            other = other[:2] + (other_down,)
    else:
        if number == 0:
            other = other[:2] + (swap(own[2]),)
        gate_w, up_w, down_w = by_layer(number, own, other)
        ffn_all = lax.all_gather(normed_ffn, TOKENS, axis=0, tiled=True)
        logits = dot_t(ffn_all, router_w).reshape(blocks, rows, EXPERTS)
        used = jnp.transpose(chosen, (0, 2, 1)) > 0
        gates = jax.nn.softmax(jnp.where(used, logits, -jnp.inf), axis=-1)
        slot_rows = choose(pick, ffn_all.reshape(blocks, rows, -1), count)
        mine_gates = jnp.einsum("bte,jxe->bjt", gates, mine, precision=lax.Precision.HIGHEST)
        slot_gates = jnp.sum(
            pick.reshape(blocks, count, CAP, rows).astype(jnp.float32) * mine_gates[:, :, None, :],
            axis=3,
        )
        slot_gates = jnp.transpose(slot_gates, (1, 0, 2)).reshape(count, -1, 1)
        gate_pre = each_dot("ecd,edf->ecf", slot_rows, gate_w)
        up_pre = each_dot("ecd,edf->ecf", slot_rows, up_w)
        scaled = low(slot_gates * jax.nn.silu(gate_pre) * up_pre)
        slot_out = low(each_dot("ecf,efd->ecd", scaled, down_w))
        expert_state = (slot_rows, gate_pre, up_pre, scaled, slot_gates)
    saved = (
        layer_in,
        attention_state,
        after_update,
        normed_ffn,
        own_gates,
        expert_state,
    )
    return (after_update, slot_out, saved, (own, other), received)


def token_sums(pick_t, slot_out, collective_id, *carry, spread=(), products=()):
    if has_kernels():
        sums, *received = combine(pick_t, slot_out, collective_id, carry, spread, products)
        return sums, received
    sums = give_back(pick_t, slot_out).astype(jnp.float32)
    sums = lax.psum_scatter(sums, TOKENS, scatter_dimension=0, tiled=True)
    received = [pass_to(array, to) for to, array in carry]
    grads = [
        low(each_dot("eck,ecn->ekn", left, right)) for left, rights in products for right in rights
    ]
    return sums, received + list(spread) + grads


def spread_rows(parts):
    return lax.all_to_all(parts, "seq", split_axis=0, concat_axis=0, tiled=True)


def expert_gradients(number, layer_grad, saved, picking, experts, *carry):
    chosen, pick, pick_t, first_expert = picking
    own, other = experts
    count = pick.shape[1] // CAP
    blocks, _, rows = chosen.shape
    slot_rows, gate_pre, up_pre, scaled, slot_gates = saved[-1]
    if has_kernels():
        slot_grads, gate_low, up_low, gate_term, slot_out, *received = expert_backward(
            number, low(layer_grad), pick, gate_pre, up_pre, slot_gates, own, other, 4 + number, carry
        )
        gate_term = gate_term[:, :, :1]
    else:
        gate_w, up_w, down_w = by_layer(number, own, other)
        grad_all = lax.all_gather(low(layer_grad), TOKENS, axis=0, tiled=True)
        slot_grads = choose(pick, grad_all.reshape(blocks, rows, -1), count)
        plain_grad = each_dot("ecd,efd->ecf", slot_grads, down_w)
        sigmoid = jax.nn.sigmoid(gate_pre)
        activated = gate_pre * sigmoid
        gate_term = jnp.sum(plain_grad * (activated * up_pre), axis=2, keepdims=True)
        hidden_grad = slot_gates * plain_grad
        gate_low = low(hidden_grad * up_pre * sigmoid * (1.0 + gate_pre * (1.0 - sigmoid)))
        up_low = low(hidden_grad * activated)
        slot_out = low(
            each_dot("ecf,edf->ecd", gate_low, gate_w) + each_dot("ecf,edf->ecd", up_low, up_w)
        )
        received = [pass_to(array, to) for to, array in carry]
    by_slot = jnp.transpose(gate_term.reshape(count, blocks, CAP), (1, 0, 2))
    gate_terms = jnp.sum(
        pick.reshape(blocks, count, CAP, rows).astype(jnp.float32) * by_slot[..., None], axis=2
    )
    gate_terms = lax.all_to_all(gate_terms, TOKENS, split_axis=0, concat_axis=0, tiled=True)
    products = ((slot_rows, (gate_low, up_low)), (scaled, (slot_grads,)))
    return slot_out, gate_terms, products, received


def backward_layer(
    number, layer_grad, normed_grad, gate_terms, saved, picking, weights, *carry, spread=()
):
    attn_scale, ffn_scale, qkv_w, out_w, router_w = weights
    chosen, pick, _, _ = picking
    (
        layer_in,
        (normed_all, mixed_t, heads, log_total),
        after_update,
        normed_ffn,
        own_gates,
        _,
    ) = saved
    rows = chosen.shape[2]
    gate_terms = jnp.sum(gate_terms.reshape(EXPERTS, -1, rows), axis=1)
    logit_grad = low(
        own_gates * (gate_terms - jnp.sum(own_gates * gate_terms, axis=0, keepdims=True))
    )
    router_grad = dot(logit_grad, normed_ffn)
    normed_grad = normed_grad + t_dot(logit_grad, router_w)
    after_part, ffn_gain_grad = jax.vjp(rms_norm, after_update, ffn_scale)[1](normed_grad)
    after_grad = after_part + layer_grad
    if has_kernels():
        normed_attn, branch_all, qkv_grad, *received = attention_backward_call(
            low(after_grad),
            qkv_w,
            out_w,
            wide_tables(4 * layer_in.shape[0]),
            heads,
            log_total,
            11 + number,
            carry,
            spread,
        )
        branch_all = branch_all.reshape(-1, layer_in.shape[1])
    else:
        branch_all = lax.all_gather(low(after_grad), "seq", axis=0, tiled=True)
        head_grad = low(dot_t(branch_all, out_w))
        qkv_grad = attention_backward(head_grad, *heads, log_total)
        normed_attn = low(dot_t(qkv_grad, qkv_w))
        normed_attn = lax.psum_scatter(normed_attn, "seq", scatter_dimension=0, tiled=True)
        received = [pass_to(array, to) for to, array in carry]
        received = received + list(spread)
    out_grad = dot(mixed_t, branch_all)
    qkv_weight_grad = t_dot(normed_all, qkv_grad)
    input_part, attn_gain_grad = jax.vjp(rms_norm, layer_in, attn_scale)[1](
        normed_attn.astype(jnp.float32)
    )
    small = [router_grad, attn_gain_grad[None], ffn_gain_grad[None]]
    small = jnp.concatenate(small + [jnp.zeros((128 - EXPERTS - 2, small[0].shape[1]))], axis=0)
    qkv_weight_grad = jnp.concatenate([low(qkv_weight_grad), low(small).T], axis=1)
    return (input_part + after_grad, (qkv_weight_grad, low(out_grad)), received)


def by_layer(number, own, other):
    is_own = lax.axis_index("section") == number
    return jax.tree.map(lambda mine, received: jnp.where(is_own, mine, received), own, other)


def body(
    hidden_in,
    out_grad,
    attn_gain,
    ffn_gain,
    query_matrix,
    key_matrix,
    value_matrix,
    output_matrix,
    router_matrix,
    w_gate,
    w_up,
    w_down,
    routes,
):
    section = lax.axis_index("section")
    dp, seq = lax.axis_size("dp"), lax.axis_size("seq")
    seq_index = lax.axis_index("seq")
    first = section == 0
    width = hidden_in.shape[3]
    depth = query_matrix.shape[1]

    layer_in = lax.dynamic_index_in_dim(hidden_in, section, 0, keepdims=False)[0]
    top_grad = lax.dynamic_index_in_dim(out_grad, section, 0, keepdims=False)[0]
    own_group = jnp.concatenate(
        [
            matrix[0].reshape(depth, seq, -1)
            for matrix in (query_matrix, key_matrix, value_matrix)
        ],
        axis=2,
    )
    own_group = jnp.transpose(own_group, (1, 0, 2))
    to_group = []
    for flat in range(dp * seq):
        to_group.append((flat, (flat % dp) * seq + flat // dp))
    from_group = [(target, source) for source, target in to_group]
    own_out = lax.ppermute(output_matrix[0], TOKENS, to_group)
    other_out = swap(own_out)
    local = w_gate.shape[1]
    hidden_units = w_gate.shape[3]
    if local >= seq:
        count, units = local // seq, hidden_units
        start, unit_start = seq_index * count, 0
    else:
        count, units = 1, hidden_units * local // seq
        start, unit_start = seq_index * local // seq, (seq_index % (seq // local)) * units
    first_expert = lax.axis_index("dp") * local + start
    if has_kernels():
        own_experts = (w_gate[0], w_up[0], w_down[0])
    else:
        own_experts = (
            lax.dynamic_slice(w_gate[0], (start, 0, unit_start), (count, width, units)),
            lax.dynamic_slice(w_up[0], (start, 0, unit_start), (count, width, units)),
            lax.dynamic_slice(w_down[0], (start, unit_start, 0), (count, units, width)),
        )
    small = jnp.concatenate([router_matrix[0].T, attn_gain, ffn_gain], axis=0)
    paths = routes[0, :, 0]
    if has_kernels():
        small = jnp.pad(small, ((0, -small.shape[0] % 16), (0, 256 - depth)))
        paths = low(jnp.transpose(paths, (0, 2, 1)).reshape(2 * TOP_K, -1))
        *tables, small, qkv_first, qkv_second, other_gate = prepare(
            jnp.concatenate([paths, small], axis=0),
            own_group,
            own_experts[0],
            count,
            hidden_in.shape[2],
            depth,
            13,
        )
        pickings = [(tables[4 + n], tables[n], tables[2 + n], first_expert) for n in range(2)]
        qkv_second = lax.all_gather(
            qkv_second.reshape(seq * depth, -1), "dp", axis=0, tiled=True
        )
        qkv_layers = [qkv_first.reshape(width, -1), qkv_second]
    else:
        small = lax.all_gather(small, ("section", "dp", "seq"), axis=0, tiled=False)
        small = jnp.transpose(small.reshape(2, dp * seq, -1, depth), (0, 2, 1, 3))
        small = small.reshape(2, -1, width)
        paths = lax.all_gather(paths, ("section", "dp", "seq"), axis=0, tiled=False)
        paths = lax.dynamic_index_in_dim(paths, section, 1, keepdims=False)
        paths = paths.reshape(2, dp * seq, -1, TOP_K)
        pickings = [routing(paths[n], first_expert, count) + (first_expert,) for n in range(2)]
        other_gate = swap(own_experts[0])
        other_group = swap(own_group)
        qkv_layers = []
        for number in range(2):
            part = spread_rows(by_layer(number, own_group, other_group))
            part = part.reshape(seq * depth, -1)
            qkv_layers.append(lax.all_gather(part, "dp", axis=0, tiled=True))

    weights = []
    for number in range(2):
        out_w = lax.all_gather(
            by_layer(number, own_out, other_out), "dp", axis=0, tiled=True
        )
        weights.append(
            (
                small[number, EXPERTS].astype(jnp.float32),
                small[number, EXPERTS + 1].astype(jnp.float32),
                qkv_layers[number],
                out_w,
                small[number, :EXPERTS],
            )
        )

    def own_layer(pieces):
        return jnp.where(first, pieces[0], pieces[1])

    def both_micros(own, other):
        return jnp.stack([jnp.where(first, own, other), jnp.where(first, other, own)])[
            None, :, None
        ]

    def summed(own, other):
        return own_layer(own).astype(jnp.float32) + own_layer(other).astype(jnp.float32)

    def dp_sums(dense):
        return [lax.psum_scatter(part, "dp", scatter_dimension=0, tiled=True) for part in dense]

    def row_parts(piece, kind):
        if local >= seq:
            piece = piece.reshape(count, seq, piece.shape[1] // seq, -1)
            return jnp.transpose(piece, (1, 0, 2, 3))
        if kind < 2:
            return piece.reshape(seq, -1, units)
        piece = piece.reshape(-1, hidden_units // seq, width)
        share = seq // local
        parts = jnp.zeros((seq,) + piece.shape[1:], piece.dtype)
        return lax.dynamic_update_slice_in_dim(
            parts, piece, (seq_index % share) * piece.shape[0], axis=0
        )

    def whole_rows(parts, kind):
        parts = parts.astype(jnp.float32)
        if local < seq:
            parts = parts.reshape((local, seq // local) + parts.shape[1:])
            if kind < 2:
                parts = jnp.transpose(parts, (0, 2, 1, 3))
            else:
                parts = jnp.sum(parts, axis=1)
            return parts.reshape((local,) + parts.shape[1 : 2] + (-1,))[None]
        return parts.reshape((local,) + parts.shape[2:])[None]

    experts = (own_experts, (other_gate,))
    first_in = layer_in.astype(jnp.float32)
    updated, slot_out, first_saved, experts, _ = forward_layer(
        0, first_in, pickings[0], weights[0], experts, (None, own_experts[1])
    )
    sums, _ = token_sums(pickings[0][2], slot_out, 3)
    first_out = updated + sums
    second_updated, second_slots, second_saved, experts, (other_out,) = forward_layer(
        1, first_out, pickings[1], weights[1], experts, (0, first_out)
    )
    top_grad = top_grad.astype(jnp.float32)
    slot_out, gate_terms, products, _ = expert_gradients(
        1, top_grad, second_saved, pickings[1], experts
    )
    sums, second_experts = token_sums(pickings[1][2], slot_out, 6, products=products)
    middle_grad, second_dense, (second_gate,) = backward_layer(
        1, top_grad, sums, gate_terms, second_saved, pickings[1], weights[1], (1, second_experts[0])
    )
    slot_out, gate_terms, products, (second_up,) = expert_gradients(
        0, middle_grad, first_saved, pickings[0], experts, (1, second_experts[1])
    )
    (rows_in, (gate_low, up_low)), down_product = products
    gate_grad = low(each_dot("ecd,ecf->edf", rows_in, gate_low))
    slot_out, gate_grad, gate_terms = lax.optimization_barrier((slot_out, gate_grad, gate_terms))
    sums, (first_gate, second_down, *first_experts) = token_sums(
        pickings[0][2],
        slot_out,
        7,
        (0, gate_grad),
        (1, second_experts[2]),
        products=((rows_in, (up_low,)), down_product),
    )
    first_experts = [gate_grad, *first_experts]
    sums, *second_dense = lax.optimization_barrier((sums, *second_dense))
    second_dense = dp_sums(second_dense)

    def handed(kind, *received):
        own = (first_experts[kind], second_experts[kind])
        if has_kernels():
            return (*own, *received)
        return [spread_rows(row_parts(low(summed(own, received)), kind))]

    bottom_grad, first_dense, (first_up, other_middle, gate_rows) = backward_layer(
        0,
        middle_grad,
        sums,
        gate_terms,
        first_saved,
        pickings[0],
        weights[0],
        (0, first_experts[1]),
        (1, middle_grad),
        spread=handed(0, first_gate, second_gate),
    )
    second_slots, *first_dense = lax.optimization_barrier((second_slots, *first_dense))
    first_dense = dp_sums(first_dense)
    sums, (first_down, up_rows) = token_sums(
        pickings[1][2],
        second_slots,
        8,
        (0, first_experts[2]),
        spread=handed(1, first_up, second_up),
    )
    sums, *first_dense = lax.optimization_barrier((sums, *first_dense))
    second_out = second_updated + sums
    own_cols, own_rows = [own_layer((first_dense[k], second_dense[k])) for k in range(2)]
    other_cols, other_rows = [own_layer((second_dense[k], first_dense[k])) for k in range(2)]
    if has_kernels():
        down_rows, cols_sum, out_sum, other_second, other_bottom = last_exchange(
            handed(2, first_down, second_down),
            own_cols.reshape(seq, depth, -1),
            other_cols.reshape(seq, depth, -1),
            own_rows,
            other_rows,
            14,
            ((1, second_out), (0, bottom_grad)),
        )
    else:
        (down_rows,) = handed(2, first_down, second_down)
        cols_sum = low(own_cols.astype(jnp.float32) + swap(other_cols).astype(jnp.float32))
        cols_sum = spread_rows(cols_sum.reshape(seq, depth, -1))
        out_sum = low(own_rows.astype(jnp.float32) + swap(other_rows).astype(jnp.float32))
        out_sum = lax.ppermute(out_sum, TOKENS, from_group)
        other_second, other_bottom = pass_to(second_out, 1), pass_to(bottom_grad, 0)
    expert_sums = [whole_rows(rows, k) for k, rows in enumerate((gate_rows, up_rows, down_rows))]
    layer_outs = both_micros(
        own_layer((first_out, second_out)), own_layer((other_out, other_second))
    )
    section_grads = both_micros(
        own_layer((bottom_grad, middle_grad)), own_layer((other_bottom, other_middle))
    )
    qkv_sum, out_sum = cols_sum.astype(jnp.float32), out_sum.astype(jnp.float32)
    kv_width = KV_HEADS * HEAD_DIM // seq
    q_width = GROUP * kv_width
    qkv_width = q_width + 2 * kv_width
    small_sum = jnp.sum(qkv_sum[:, :, qkv_width:], axis=0)

    def columns(begin, end):
        return jnp.transpose(qkv_sum[:, :, begin:end], (1, 0, 2)).reshape(depth, -1)[None]

    return (
        layer_outs,
        section_grads,
        small_sum[:, EXPERTS][None],
        small_sum[:, EXPERTS + 1][None],
        columns(0, q_width),
        columns(q_width, q_width + kv_width),
        columns(q_width + kv_width, qkv_width),
        out_sum[None],
        small_sum[:, :EXPERTS][None],
        *expert_sums,
    )


def solution(mesh):
    return jax.shard_map(
        body,
        mesh=mesh,
        in_specs=(
            P(None, "dp", "seq", None),
            P(None, "dp", "seq", None),
            P("section", ("dp", "seq")),
            P("section", ("dp", "seq")),
            P("section", ("dp", "seq"), None),
            P("section", ("dp", "seq"), None),
            P("section", ("dp", "seq"), None),
            P("section", ("dp", "seq"), None),
            P("section", ("dp", "seq"), None),
            P("section", "dp", None, None),
            P("section", "dp", None, None),
            P("section", "dp", None, None),
            P("section", None, "dp", "seq", None),
        ),
        out_specs=(
            P("section", None, "dp", "seq", None),
            P("section", None, "dp", "seq", None),
            P("section", ("dp", "seq")),
            P("section", ("dp", "seq")),
            P("section", ("dp", "seq"), None),
            P("section", ("dp", "seq"), None),
            P("section", ("dp", "seq"), None),
            P("section", ("dp", "seq"), None),
            P("section", ("dp", "seq"), None),
            P("section", "dp", "seq", None),
            P("section", "dp", "seq", None),
            P("section", "dp", "seq", None),
        ),
        check_vma=False,
    )
```

```python
import jax
import jax.numpy as jnp
import numpy as np
from jax import lax
from jax.experimental import pallas as pl
from jax.experimental.pallas import tpu as pltpu
from jax.sharding import PartitionSpec as P

HEADS = 24
KV_HEADS = 8
HEAD_DIM = 64
TOP_K = 8
EXPERTS = 32
CAP = 80
GROUP = HEADS // KV_HEADS
TOKENS = ("dp", "seq")
PIECES = 4
MESH = pl.DeviceIdType.MESH
DMA = pltpu.SemaphoreType.DMA

epsilon = 1e-06


def dot(a, b):
    return jnp.dot(a, b, preferred_element_type=jnp.float32)


def dot_t(a, b):
    return lax.dot_general(a, b, (((1,), (1,)), ((), ())), preferred_element_type=jnp.float32)


def t_dot(a, b):
    return lax.dot_general(a, b, (((0,), (0,)), ((), ())), preferred_element_type=jnp.float32)


def low(v):
    return v.astype(jnp.bfloat16)


def swap(block):
    return lax.ppermute(block, "section", [(0, 1), (1, 0)])


def pass_to(block, section):
    return lax.ppermute(block, "section", [(1 - section, section)])


def rms_norm(values, norm_gain):
    return (
        values * lax.rsqrt(jnp.mean(values * values, axis=-1, keepdims=True) + epsilon) * norm_gain
    )


def rotary_tables(length):
    half_dim = HEAD_DIM // 2
    frequency = 10000.0 ** (-jnp.arange(half_dim, dtype=jnp.float32) * 2.0 / HEAD_DIM)
    angles = jnp.arange(length, dtype=jnp.float32)[:, None] * frequency[None, :]
    return (jnp.cos(angles)[:, None, :], jnp.sin(angles)[:, None, :])


def rotate(values, cos_table, sin_table):
    length = values.shape[0]
    split_heads = values.reshape(length, -1, HEAD_DIM)
    first_half = split_heads[..., : HEAD_DIM // 2]
    second_half = split_heads[..., HEAD_DIM // 2 :]
    turned = jnp.concatenate(
        [
            first_half * cos_table - second_half * sin_table,
            second_half * cos_table + first_half * sin_table,
        ],
        axis=-1,
    )
    return turned.reshape(length, -1)


def attention_forward(q_heads, k_heads, v_heads):
    length = q_heads.shape[0]
    local_kv = k_heads.shape[1] // HEAD_DIM
    cos_table, sin_table = rotary_tables(length)
    q_rot = low(rotate(q_heads.astype(jnp.float32), cos_table, sin_table)).reshape(
        length, local_kv, GROUP, HEAD_DIM
    )
    k_rot = low(rotate(k_heads.astype(jnp.float32), cos_table, sin_table)).reshape(
        length, local_kv, HEAD_DIM
    )
    values = v_heads.reshape(length, local_kv, HEAD_DIM)
    block_rows = min(512, length)
    outputs = []
    totals_list = []
    for first_row in range(0, length, block_rows):
        key_end = first_row + block_rows
        scores = (
            jnp.einsum(
                "qhgd,khd->hgqk",
                q_rot[first_row:key_end],
                k_rot[:key_end],
                preferred_element_type=jnp.float32,
            )
            * 0.125
        )
        causal = (first_row + jnp.arange(block_rows, dtype=jnp.int32))[:, None] >= jnp.arange(
            key_end, dtype=jnp.int32
        )[None, :]
        scores = jnp.where(causal, scores, -jnp.inf)
        row_peak = jnp.max(scores, axis=-1, keepdims=True)
        exponents = jnp.exp(scores - row_peak)
        totals = jnp.sum(exponents, axis=-1, keepdims=True)
        attended = jnp.einsum(
            "hgqk,khd->qhgd",
            low(exponents / totals),
            values[:key_end],
            preferred_element_type=jnp.float32,
        )
        outputs.append(low(attended).reshape(block_rows, -1))
        totals_list.append((row_peak + jnp.log(totals))[..., 0])
    return (jnp.concatenate(outputs, axis=0), jnp.stack(totals_list), q_rot, k_rot, values)


def attention_backward(head_grad, q_rot, k_rot, values, log_total):
    length, local_kv = q_rot.shape[:2]
    cos_table, sin_table = rotary_tables(length)
    block_rows = min(512, length)
    grad_rows = head_grad.reshape(length, local_kv, GROUP, HEAD_DIM)
    key_acc = jnp.zeros((length, local_kv, HEAD_DIM), jnp.float32)
    value_acc = jnp.zeros((length, local_kv, HEAD_DIM), jnp.float32)
    query_parts = []
    for block_number, first_row in enumerate(range(0, length, block_rows)):
        key_end = first_row + block_rows
        q_block = q_rot[first_row:key_end]
        grad_block = grad_rows[first_row:key_end]
        key_part = k_rot[:key_end]
        scores = (
            jnp.einsum("qhgd,khd->hgqk", q_block, key_part, preferred_element_type=jnp.float32)
            * 0.125
        )
        causal = (first_row + jnp.arange(block_rows, dtype=jnp.int32))[:, None] >= jnp.arange(
            key_end, dtype=jnp.int32
        )[None, :]
        scores = jnp.where(causal, scores, -jnp.inf)
        probs_full = jnp.exp(scores - log_total[block_number][..., None])
        prob_grad = jnp.einsum(
            "qhgd,khd->hgqk", grad_block, values[:key_end], preferred_element_type=jnp.float32
        )
        score_grad = probs_full * (
            prob_grad - jnp.sum(probs_full * prob_grad, axis=-1, keepdims=True)
        )
        score_low = low(score_grad)
        query_parts.append(
            jnp.einsum("hgqk,khd->qhgd", score_low, key_part, preferred_element_type=jnp.float32)
            * 0.125
        )
        key_acc = key_acc.at[:key_end].add(
            jnp.einsum("hgqk,qhgd->khd", score_low, q_block, preferred_element_type=jnp.float32)
            * 0.125
        )
        value_acc = value_acc.at[:key_end].add(
            jnp.einsum(
                "hgqk,qhgd->khd", low(probs_full), grad_block, preferred_element_type=jnp.float32
            )
        )
    query_all = jnp.concatenate(query_parts, axis=0).reshape(length, -1)
    query_grad = rotate(query_all, cos_table, -sin_table)
    key_grad = rotate(key_acc.reshape(length, -1), cos_table, -sin_table)
    return jnp.concatenate(
        [low(query_grad), low(key_grad), low(value_acc).reshape(length, -1)], axis=1
    )


def remote(src, dst, send_sem, recv_sem, **device):
    return pltpu.make_async_remote_copy(
        src_ref=src,
        dst_ref=dst,
        send_sem=send_sem,
        recv_sem=recv_sem,
        device_id=device,
        device_id_type=MESH,
    )


def greet(d, s, section=None, spread=False):
    barrier = pltpu.get_barrier_semaphore()

    def signal(**device):
        pl.semaphore_signal(barrier, inc=1, device_id=device, device_id_type=MESH)

    signal(seq=s ^ 1)
    signal(seq=s ^ 2)

    @pl.when(d > 0)
    def _():
        signal(dp=d - 1)

    @pl.when(d < 3)
    def _():
        signal(dp=d + 1)

    known = 3
    if section is not None:
        signal(section=1 - section)
        known = 4
    if spread:
        signal(seq=s ^ 3)
        known = known + 1
    inner = (d > 0) & (d < 3)

    @pl.when(inner)
    def _():
        pl.semaphore_wait(barrier, known + 1)

    @pl.when(jnp.logical_not(inner))
    def _():
        pl.semaphore_wait(barrier, known)


class Carried:
    def __init__(self, sections, sources, targets, sems):
        self.section = lax.axis_index("section")
        self.copies = []
        for k, (to, source, target) in enumerate(zip(sections, sources, targets)):
            copy = remote(source, target, sems.at[k, 0], sems.at[k, 1], section=1 - self.section)
            self.copies.append((to, copy))

    def start(self):
        for to, copy in self.copies:
            if to is None:
                copy.start()
            else:

                @pl.when(self.section != to)
                def _():
                    copy.start()

    def finish(self):
        for to, copy in self.copies:
            if to is None:
                copy.wait()
            else:

                @pl.when(self.section != to)
                def _():
                    copy.wait_send()

                @pl.when(self.section == to)
                def _():
                    copy.wait_recv()


class Spread:
    def __init__(self, source, target, sems):
        s = lax.axis_index("seq")
        self.local = pltpu.make_async_copy(source.at[s], target.at[s], sems.at[0, 0])
        self.copies = [
            remote(source.at[s ^ flip], target.at[s], sems.at[flip, 0], sems.at[flip, 1], seq=s ^ flip)
            for flip in (3, 2, 1)
        ]

    def start(self):
        for copy in self.copies:
            copy.start()
        self.local.start()

    def finish(self):
        self.local.wait()
        for copy in self.copies:
            copy.wait()


class SumSpread:
    def __init__(self, refs, target, held):
        self.refs, self.target = refs, target
        self.a, self.b, self.parts, self.loads, self.sems = held

    def copies(self, own, received):
        return [
            pltpu.make_async_copy(own, self.a, self.loads.at[0]),
            pltpu.make_async_copy(received, self.b, self.loads.at[1]),
        ]

    def load(self):
        own_0, own_1, in_0, in_1 = self.refs

        @pl.when(lax.axis_index("section") == 0)
        def _():
            for copy in self.copies(own_0, in_0):
                copy.start()

        @pl.when(lax.axis_index("section") == 1)
        def _():
            for copy in self.copies(own_1, in_1):
                copy.start()

    def start(self):
        for copy in self.copies(self.refs[0], self.refs[2]):
            copy.wait()
        group, count, rows, width = self.parts.shape
        chunk = 24576 // width
        for g in range(group):
            for j in range(count):

                @pl.loop(0, rows // chunk)
                def _(m):
                    here = pl.ds(pl.multiple_of(m * chunk, chunk), chunk)
                    there = pl.ds(pl.multiple_of(g * rows + m * chunk, chunk), chunk)
                    total = self.a[j, there, :].astype(jnp.float32)
                    total = total + self.b[j, there, :].astype(jnp.float32)
                    self.parts[g, j, here, :] = low(total)

        self.spread = Spread(self.parts, self.target, self.sems)
        self.spread.start()

    def finish(self):
        self.spread.finish()


def parts_shape(array):
    count, rows, width = array.shape
    return (4, count, rows // 4, width)


def sum_scratch(arrays):
    if not arrays:
        return []
    shape, bf = arrays[0].shape, jnp.bfloat16
    return [
        pltpu.VMEM(shape, bf),
        pltpu.VMEM(shape, bf),
        pltpu.VMEM(parts_shape(arrays[0]), bf),
        DMA((2,)),
        DMA((4, 2)),
    ]


def cost():
    return pl.CostEstimate(flops=80_000_000_000, bytes_accessed=100_000_000, transcendentals=0)


def gather_scratch(rows, width):
    return [
        pltpu.VMEM((16, rows, width), jnp.bfloat16),
        DMA(()),
        DMA((2, 4)),
        DMA((4,)),
        DMA((4,)),
        DMA((4,)),
        DMA((4, 2)),
        DMA((4, 2)),
    ]


class Gather:
    def __init__(self, scratch):
        self.land, self.lsem, self.zs, self.zr, self.ys, self.yr, self.cs, self.cr = scratch
        self.d, self.s = lax.axis_index("dp"), lax.axis_index("seq")

    def place(self, z, column):
        return self.land.at[z * 4 + column]

    def z_copy(self, src, z, right):
        target = self.d + 1 if right else self.d - 1
        return remote(src, self.place(z, self.s), self.zs.at[int(right), z], self.zr.at[z], dp=target)

    def y_copy(self, src, z):
        return remote(src, self.place(z, self.s), self.ys.at[z], self.yr.at[z], seq=self.s ^ 2)

    def core_copy(self, src, z, across):
        column = self.s ^ 2 if across else self.s
        return remote(
            src, self.place(z, column), self.cs.at[z, across], self.cr.at[z, across], seq=self.s ^ 1
        )

    def begin(self, x_ref):
        d = self.d
        own = pltpu.make_async_copy(x_ref, self.place(d, self.s), self.lsem)
        own.start()

        @pl.when(d < 3)
        def _():
            self.z_copy(x_ref, d, True).start()

        @pl.when(d > 0)
        def _():
            self.z_copy(x_ref, d, False).start()

        self.y_copy(x_ref, d).start()
        self.core_copy(x_ref, d, 0).start()
        own.wait()

    def send_on(self, q):
        following = near_first(self.d, q)
        here = self.place(following, self.s)
        self.y_copy(here, following).start()
        self.core_copy(here, following, 0).start()

    def step(self, i):
        d, s, place = self.d, self.s, self.place

        @pl.when(i < 3)
        def _():
            early = (d > 0) & (d < 3) & (i > 0)

            @pl.when(early)
            def _():
                self.send_on(i + 1)

            left, right = d - (i + 1), d + (i + 1)

            @pl.when(left >= 0)
            def _():
                self.z_copy(place(left, s), left, True).wait_recv()

                @pl.when(d < 3)
                def _():
                    self.z_copy(place(left, s), left, True).start()

            @pl.when(right <= 3)
            def _():
                self.z_copy(place(right, s), right, False).wait_recv()

                @pl.when(d > 0)
                def _():
                    self.z_copy(place(right, s), right, False).start()

            @pl.when(jnp.logical_not(early))
            def _():
                self.send_on(i + 1)

        z = near_first(d, i)
        self.y_copy(place(z, s ^ 2), z).wait_recv()
        self.core_copy(place(z, s ^ 2), z, 1).start()
        self.core_copy(place(z, s ^ 1), z, 0).wait_recv()
        self.core_copy(place(z, s ^ 3), z, 1).wait_recv()
        return z

    def finish(self):
        d, s, place = self.d, self.s, self.place
        for z in range(4):

            @pl.when((z <= d) & (d < 3))
            def _():
                self.z_copy(place(z, s), z, True).wait_send()

            @pl.when((z >= d) & (d > 0))
            def _():
                self.z_copy(place(z, s), z, False).wait_send()

            self.y_copy(place(z, s), z).wait_send()
            self.core_copy(place(z, s), z, 0).wait_send()
            self.core_copy(place(z, s), z, 1).wait_send()


def gather_blocks(x_ref, scratch, compute, carried=None):
    gather = Gather(scratch)
    greet(gather.d, gather.s, None if carried is None else carried.section)
    gather.begin(x_ref)
    if carried is not None:
        carried.start()

    @pl.loop(0, 4)
    def _(i):
        compute(gather.step(i))

    gather.finish()


def prepare_kernel(
    x_ref, group_ref, gate_ref, grad_ref,
    pick_0, pick_1, pick_t_0, pick_t_1, chosen_0, chosen_1, small_out, qkv_out, parts_out, gate_out, grad_out,
    both, places, groups, parts, lsem, carry_sem, spread_sem, qs, qr, *gather
):
    d, s, section = lax.axis_index("dp"), lax.axis_index("seq"), lax.axis_index("section")
    small_gather, grad_gather = Gather(gather[:8]), Gather([grad_out] + list(gather[8:]))
    known = x_ref.shape[0]
    count = pick_0.shape[1] // CAP
    rows = pick_0.shape[2]
    land = gather[0]
    part = both.at[pl.ds(pl.multiple_of(section * known, known), known)]
    swaps = Carried((None, None), (x_ref, group_ref), (part, groups.at[section]), carry_sem)
    gates = Carried((None,), (share(gate_ref),), (gate_out,), carry_sem.at[pl.ds(2, 1)])
    spreads = [Spread(groups.at[n], parts.at[n], spread_sem.at[n]) for n in range(2)]
    own_columns = pltpu.make_async_copy(parts.at[0], qkv_out.at[d], lsem.at[2])

    def along(src, z, right):
        target = d + 1 if right else d - 1
        return remote(src, qkv_out.at[z], qs.at[int(right), z], qr.at[z], dp=target)

    def first():
        swaps.start()
        own = [
            pltpu.make_async_copy(x_ref, part, lsem.at[0]),
            pltpu.make_async_copy(group_ref, groups.at[section], lsem.at[1]),
        ]
        for copy in own:
            copy.start()
        for copy in own:
            copy.wait()
        swaps.finish()
        gates.start()
        for side in spreads:
            side.start()
        spreads[0].finish()
        own_columns.start()

        @pl.when(d < 3)
        def _():
            along(parts.at[0], d, True).start()

        @pl.when(d > 0)
        def _():
            along(parts.at[0], d, False).start()

    def hop(h):
        @pl.when(d - h >= 0)
        def _():
            along(qkv_out.at[d - h], d - h, True).wait_recv()

            @pl.when(d < 3)
            def _():
                along(qkv_out.at[d - h], d - h, True).start()

        @pl.when(d + h <= 3)
        def _():
            along(qkv_out.at[d + h], d + h, False).wait_recv()

            @pl.when(d > 0)
            def _():
                along(qkv_out.at[d + h], d + h, False).start()

    greet(d, s, section, True)
    first()
    small_gather.begin(both)
    grad_gather.begin(grad_ref)

    @pl.loop(0, 4)
    def _(i):
        small_gather.step(i)

    small_gather.finish()
    hop(1)
    grad_gather.step(0)
    first_expert = (d * 4 + s) * count
    before = lax.broadcasted_iota(jnp.int32, (rows, rows), 0)
    before = low(before < lax.broadcasted_iota(jnp.int32, (rows, rows), 1))
    slot = lax.broadcasted_iota(jnp.int32, (CAP, rows), 0)
    expert = lax.broadcasted_iota(jnp.int32, (EXPERTS, rows), 0)
    lane = lax.broadcasted_iota(jnp.int32, (rows, count * CAP), 1)

    def tables(layer, pick_out, pick_t_out, chosen_out):
        @pl.loop(0, 16)
        def _(b):
            paths = land[b, layer * known : layer * known + 16, :].astype(jnp.float32)
            paths = jnp.where(section == 0, paths[:TOP_K], paths[TOP_K:]).astype(jnp.int32)
            chosen = expert == paths[0:1]
            for k in range(1, TOP_K):
                chosen = chosen | (expert == paths[k : k + 1])
            chosen_out[b] = low(chosen)
            mine = [
                jnp.max((paths == first_expert + j).astype(jnp.float32), axis=0, keepdims=True)
                for j in range(count)
            ]
            mine = jnp.concatenate(mine + [jnp.zeros((8 - count, rows), jnp.float32)], axis=0)
            place = jnp.where(mine > 0.5, dot(low(mine), before), -10000.0)
            places[...] = place
            for j in range(count):
                pick_out[b, j * CAP : (j + 1) * CAP, :] = low(
                    slot == place[j : j + 1].astype(jnp.int32)
                )
            turned = places[...].T.astype(jnp.int32)
            pick_t = turned[:, 0:1] == lane
            for j in range(1, count):
                pick_t = pick_t & (lane < j * CAP) | (turned[:, j : j + 1] == lane - j * CAP)
            pick_t_out[b] = low(pick_t)

        depth = small_out.shape[2] // 16
        for b in range(16):
            small = land[b, layer * known + 16 : (layer + 1) * known, :]
            small_out[layer, :, b * depth : (b + 1) * depth] = small[:, :depth]

    tables(0, pick_0, pick_t_0, chosen_0)
    hop(2)
    grad_gather.step(1)
    tables(1, pick_1, pick_t_1, chosen_1)
    hop(3)
    grad_gather.step(2)
    grad_gather.step(3)
    grad_gather.finish()
    spreads[1].finish()
    layer_1 = pltpu.make_async_copy(parts.at[1], parts_out, lsem.at[0])
    layer_1.start()
    for z in range(4):

        @pl.when((z <= d) & (d < 3))
        def _():
            along(parts.at[0], z, True).wait_send()

        @pl.when((z >= d) & (d > 0))
        def _():
            along(parts.at[0], z, False).wait_send()

    own_columns.wait()
    layer_1.wait()
    gates.finish()


def prepare(x, group, gate, grad, count, depth, collective_id):
    known, width = x.shape
    rows = grad.shape[0]
    bf = jnp.bfloat16
    anywhere = pl.BlockSpec(memory_space=pl.ANY)
    near = pl.BlockSpec(memory_space=pltpu.VMEM)
    return pl.pallas_call(
        prepare_kernel,
        out_shape=[
            jax.ShapeDtypeStruct((16, count * CAP, rows), bf),
            jax.ShapeDtypeStruct((16, count * CAP, rows), bf),
            jax.ShapeDtypeStruct((16, rows, count * CAP), bf),
            jax.ShapeDtypeStruct((16, rows, count * CAP), bf),
            jax.ShapeDtypeStruct((16, EXPERTS, rows), bf),
            jax.ShapeDtypeStruct((16, EXPERTS, rows), bf),
            jax.ShapeDtypeStruct((2, known - 16, 16 * depth), bf),
            jax.ShapeDtypeStruct((4,) + group.shape, bf),
            jax.ShapeDtypeStruct(group.shape, bf),
            jax.ShapeDtypeStruct(share_shape(gate), bf),
            jax.ShapeDtypeStruct((16,) + grad.shape, bf),
        ],
        in_specs=[anywhere] * 4,
        out_specs=[near] * 7 + [anywhere] * 4,
        scratch_shapes=[
            pltpu.VMEM((2 * known, width), bf),
            pltpu.VMEM((8, rows), jnp.float32),
            pltpu.VMEM((2,) + group.shape, bf),
            pltpu.VMEM((2,) + group.shape, bf),
            DMA((3,)),
            DMA((3, 2)),
            DMA((2, 4, 2)),
            DMA((2, 4)),
            DMA((4,)),
        ]
        + gather_scratch(2 * known, width)
        + gather_scratch(*grad.shape)[1:],
        compiler_params=pltpu.CompilerParams(
            collective_id=collective_id, has_side_effects=True, vmem_limit_bytes=60 << 20
        ),
        cost_estimate=cost(),
        name="prepare",
    )(x, group, gate, grad)


def share(ref):
    count = ref.shape[0] // 4
    return ref.at[pl.ds(lax.axis_index("seq") * count, count)]


def share_shape(array):
    return (array.shape[0] // 4,) + array.shape[1:]


def pick_weights(own_refs, other_refs, held, sems, own_layer):
    own_refs = [share(ref) for ref in own_refs]
    mine = lax.axis_index("section") == own_layer

    @pl.when(mine)
    def _():
        for k, ref in enumerate(own_refs):
            pltpu.make_async_copy(ref, held[k], sems.at[k]).start()

    @pl.when(jnp.logical_not(mine))
    def _():
        for k, ref in enumerate(other_refs):
            pltpu.make_async_copy(ref, held[k], sems.at[k]).start()

    def ready(k):
        pltpu.make_async_copy(own_refs[k], held[k], sems.at[k]).wait()

    return ready


def expert_forward_kernel(
    layer, x_ref, pick_ref, chosen_ref, router_ref, mine_ref,
    wg_own, wu_own, wd_own, wg_other, wu_other, wd_other,
    rows_out, gate_out, up_out, hidden_out, slot_gate_out, y_out,
    wg, wu, wd, rows, gate, up, hidden, slot_gate, y, wsem, osem, carry_sem, *gather
):
    count = wg.shape[0]
    carried = None
    if layer == 0:
        carried = Carried((None,), (share(wd_own),), (wd_other,), carry_sem)
        ready = pick_weights((wg_own, wu_own), (wg_other, wu_other), (wg, wu), wsem, layer)
    else:
        ready = pick_weights(
            (wg_own, wu_own, wd_own), (wg_other, wu_other, wd_other), (wg, wu, wd), wsem, layer
        )
    land = gather[0]
    d = lax.axis_index("dp")

    def outs(z):
        part = pl.ds(z * 4 * CAP, 4 * CAP)
        return [
            pltpu.make_async_copy(held.at[:, part], out.at[:, part], osem.at[k, z])
            for k, (held, out) in enumerate(
                ((rows, rows_out), (gate, gate_out), (up, up_out), (hidden, hidden_out), (slot_gate, slot_gate_out))
            )
        ] + [pltpu.make_async_copy(y.at[pl.ds(z * 4, 4)], y_out.at[pl.ds(z * 4, 4)], osem.at[5, z])]

    def down(z):
        part = pl.ds(z * 4 * CAP, 4 * CAP)

        @pl.loop(0, count)
        def _(j):
            result = low(dot(hidden[j, part, :], wd[j]))
            for q in range(4):
                y[z * 4 + q, pl.ds(j * CAP, CAP), :] = result[q * CAP : (q + 1) * CAP]

    def compute(z):
        @pl.when(z == d)
        def _():
            for k in range(2 if layer == 0 else 3):
                ready(k)

        for q in range(4):
            b = z * 4 + q
            picked = low(dot(pick_ref[b], land[b]))
            for j in range(count):
                rows[j, pl.ds(b * CAP, CAP), :] = picked[j * CAP : (j + 1) * CAP]
        part = pl.ds(z * 4 * CAP, 4 * CAP)

        @pl.loop(0, count)
        def _(j):
            x = rows[j, part, :]
            g = dot(x, wg[j])
            u = dot(x, wu[j])
            logits = dot_t(x, router_ref[...])
            for q in range(4):
                b = z * 4 + q
                slots = slice(q * CAP, (q + 1) * CAP)
                seen = dot_t(pick_ref[b, pl.ds(j * CAP, CAP), :], chosen_ref[b])
                masked = jnp.where(seen > 0.5, logits[slots], -1e30)
                power = jnp.exp(masked - jnp.max(masked, axis=1, keepdims=True))
                own = jnp.sum(power * mine_ref[j], axis=1, keepdims=True)
                value = own / jnp.sum(power, axis=1, keepdims=True)
                slot_gate[j, pl.ds(b * CAP, CAP), :] = jnp.broadcast_to(value, (CAP, 128))
            gate[j, part, :] = low(g)
            up[j, part, :] = low(u)
            h = low(g * jax.nn.sigmoid(g) * u * slot_gate[j, part, :][:, :1])
            hidden[j, part, :] = h

        if layer != 0:
            down(z)
        for copy in outs(z)[: 5 if layer == 0 else 6]:
            copy.start()

    gather_blocks(x_ref, gather, compute, carried)
    if layer == 0:
        carried.finish()
        ready = pick_weights((wd_own,), (wd_other,), (wd,), wsem, layer)
        ready(0)
        for z in range(4):
            down(z)
            outs(z)[5].start()
    for z in range(4):
        for copy in outs(z):
            copy.wait()


def expert_forward(layer, x, pick, chosen, router, mine, own, other, collective_id):
    count, width, units = share_shape(own[0])
    rows = x.shape[0]
    slots = 16 * CAP
    bf = jnp.bfloat16
    anywhere = pl.BlockSpec(memory_space=pl.ANY)
    near = pl.BlockSpec(memory_space=pltpu.VMEM)
    results = [
        ((count, slots, width), bf),
        ((count, slots, units), bf),
        ((count, slots, units), bf),
        ((count, slots, units), bf),
        ((count, slots, 128), jnp.float32),
        ((16, count * CAP, width), bf),
    ]

    def kernel(*refs):
        if layer == 0:
            refs = refs[:10] + refs[16:17] + refs[10:16] + refs[17:]
        expert_forward_kernel(layer, *refs)

    shapes = [jax.ShapeDtypeStruct(*result) for result in results]
    if layer == 0:
        shapes.append(jax.ShapeDtypeStruct(share_shape(own[2]), bf))
        other = other[:2]
    operands = (x, pick, chosen, router, mine, *own, *other)
    return pl.pallas_call(
        kernel,
        out_shape=shapes,
        in_specs=[anywhere, near, near, near, near] + [anywhere] * (len(operands) - 5),
        out_specs=[anywhere] * len(shapes),
        scratch_shapes=[pltpu.VMEM(share_shape(weight), bf) for weight in own]
        + [pltpu.VMEM(*result) for result in results]
        + [DMA((3,)), DMA((6, 4)), DMA((1, 2))]
        + gather_scratch(rows, width),
        compiler_params=pltpu.CompilerParams(
            collective_id=collective_id, has_side_effects=True, vmem_limit_bytes=60 << 20
        ),
        cost_estimate=cost(),
        name="expert_forward",
    )(*operands)


class Products:
    def __init__(self, pairs, outs, held, sems):
        self.units = []
        count = outs[0].shape[0]
        for j in range(count):
            at, out_at = 0, 0
            for left, rights in pairs:
                first = at
                loads = [(left, at)] + [(right, at + 1 + k) for k, right in enumerate(rights)]
                at += len(loads)
                for k in range(len(rights)):
                    self.units.append((j, first, first + 1 + k, out_at, loads, k == 0, k + 1 == len(rights)))
                    out_at += 1
        self.count, self.pairs, self.outs, self.held, self.sems = count, at, outs, held, sems

    def load(self, j, source, at):
        return pltpu.make_async_copy(source.at[j], self.held[at], self.sems.at[at])

    def store(self, j, k):
        at = self.pairs + k
        return pltpu.make_async_copy(self.held[at], self.outs[k].at[j], self.sems.at[at])

    def start(self):
        for j, _, _, _, loads, first, _ in self.units:
            if j == 0 and first:
                for source, at in loads:
                    self.load(0, source, at).start()

    def step(self, i):
        for number, (j, left, right, out, loads, first, last) in enumerate(self.units):

            @pl.when(i == number * (PIECES // 2))
            def _():
                if first:
                    for source, at in loads:
                        self.load(j, source, at).wait()
                if j > 0:
                    self.store(j - 1, out).wait()
                a, b, c = self.held[left], self.held[right], self.held[self.pairs + out]

                @pl.loop(0, a.shape[1] // 256)
                def _(m):
                    columns = pl.ds(pl.multiple_of(m * 256, 256), 256)
                    c[columns, :] = low(t_dot(a[:, columns], b[...]))

                self.store(j, out).start()
                if last and j + 1 < self.count:
                    for source, at in loads:
                        self.load(j + 1, source, at).start()

    def finish(self):
        for k in range(len(self.outs)):
            self.store(self.count - 1, k).wait()


def far_first(d, q):
    inner = (d % 3 + 2) // 3
    base = 3 - q + inner * (q // 2) * (2 * q - 5)
    mirrored = d // 2
    return base * (1 - 2 * mirrored) + 3 * mirrored


def near_first(d, q):
    inner = (d % 3 + 2) // 3
    base = q + inner * (1 - q // 2) * (1 - 2 * q)
    mirrored = d // 2
    return base * (1 - 2 * mirrored) + 3 * mirrored


def combine_kernel(sections, spreads, pairs, pick_ref, y_ref, *refs):
    kept = len(sections)
    sources, refs = refs[:kept], refs[kept:]
    spread_sources, refs = refs[:spreads], refs[spreads:]
    spreads = spreads // 4
    factors = []
    for rights in pairs:
        factors.append((refs[0], refs[1 : 1 + rights]))
        refs = refs[1 + rights :]
    out_ref, *refs = refs
    targets, refs = refs[:kept], refs[kept:]
    spread_targets, refs = refs[:spreads], refs[spreads:]
    products = sum(pairs)
    product_outs, refs = refs[:products], refs[products:]
    y, sent, own, core_in, y_in, z_in, lsem, zs, zr, ys, yr, cs, cr, carry_sem, *refs = refs
    held, refs = refs[: 5 * spreads], refs[5 * spreads :]
    work = Products(factors, product_outs, refs[:-1], refs[-1]) if pairs else None
    carried = Carried(sections, sources, targets, carry_sem)
    spread = [SumSpread(spread_sources, spread_targets[0], held)] if spreads else []
    for side in spread:
        side.load()
    d, s = lax.axis_index("dp"), lax.axis_index("seq")
    piece = out_ref.shape[0] // PIECES

    def loaded(b):
        return pltpu.make_async_copy(y_ref.at[b], y.at[b], lsem.at[b])

    def column(across, other_core):
        return s ^ (2 * across) ^ other_core

    for i in range(4):
        z = far_first(d, i)
        for across in (1, 0):
            for other_core in (1, 0):
                loaded(z * 4 + column(across, other_core)).start()
    greet(d, s, carried.section, spreads > 0)
    carried.start()

    def rows(k):
        return pl.ds(pl.multiple_of(k * piece, piece), piece)

    def partial_sum(z, k, across, other_core):
        b = z * 4 + column(across, other_core)

        @pl.when(k == 0)
        def _():
            loaded(b).wait()

        return dot(pick_ref[b, rows(k), :], y[b])

    def core_copy(z, k, across):
        return remote(
            sent.at[z, across, rows(k)],
            core_in.at[z, across, rows(k)],
            cs.at[z, k, across],
            cr.at[z, k, across],
            seq=s ^ 1,
        )

    def y_copy(z, k):
        return remote(own.at[z, 1, rows(k)], y_in.at[z, rows(k)], ys.at[z, k], yr.at[z, k], seq=s ^ 2)

    def z_copy(z, k, right):
        target = d + 1 if right else d - 1
        return remote(
            own.at[z, 0, rows(k)],
            z_in.at[int(right), z, rows(k)],
            zs.at[z, k],
            zr.at[int(right), z, k],
            dp=target,
        )

    def start(i):
        z, k = far_first(d, i // PIECES), i % PIECES
        sent[z, 1, rows(k), :] = low(partial_sum(z, k, 1, 1))
        core_copy(z, k, 1).start()
        total = partial_sum(z, k, 1, 0)
        core_copy(z, k, 1).wait_recv()
        own[z, 1, rows(k), :] = low(total + core_in[z, 1, rows(k), :].astype(jnp.float32))
        y_copy(z, k).start()
        sent[z, 0, rows(k), :] = low(partial_sum(z, k, 0, 1))
        core_copy(z, k, 0).start()

    start(0)
    for side in spread:
        side.start()
    if work:
        work.start()

    @pl.loop(0, 4 * PIECES)
    def _(i):
        @pl.when(i < 4 * PIECES - 1)
        def _():
            start(i + 1)

        if work:
            work.step(i)

        z, k = far_first(d, i // PIECES), i % PIECES
        total = partial_sum(z, k, 0, 0)
        core_copy(z, k, 0).wait_recv()
        total = total + core_in[z, 0, rows(k), :].astype(jnp.float32)
        y_copy(z, k).wait_recv()
        total = total + y_in[z, rows(k), :].astype(jnp.float32)

        @pl.when(z < d)
        def _():
            @pl.when(d < 3)
            def _():
                z_copy(z, k, False).wait_recv()
                own[z, 0, rows(k), :] = low(total + z_in[0, z, rows(k), :].astype(jnp.float32))

            @pl.when(d == 3)
            def _():
                own[z, 0, rows(k), :] = low(total)

            z_copy(z, k, False).start()

        @pl.when(z > d)
        def _():
            @pl.when(d > 0)
            def _():
                z_copy(z, k, True).wait_recv()
                own[z, 0, rows(k), :] = low(total + z_in[1, z, rows(k), :].astype(jnp.float32))

            @pl.when(d == 0)
            def _():
                own[z, 0, rows(k), :] = low(total)

            z_copy(z, k, True).start()

        @pl.when(z == d)
        def _():
            out_ref[rows(k), :] = total

    for k in range(PIECES):

        @pl.when(d < 3)
        def _():
            z_copy(d, k, False).wait_recv()
            out_ref[rows(k), :] += z_in[0, d, rows(k), :].astype(jnp.float32)

        @pl.when(d > 0)
        def _():
            z_copy(d, k, True).wait_recv()
            out_ref[rows(k), :] += z_in[1, d, rows(k), :].astype(jnp.float32)

    for z in range(4):
        for k in range(PIECES):
            core_copy(z, k, 0).wait_send()
            core_copy(z, k, 1).wait_send()
            y_copy(z, k).wait_send()

            @pl.when(z < d)
            def _():
                z_copy(z, k, False).wait_send()

            @pl.when(z > d)
            def _():
                z_copy(z, k, True).wait_send()

    carried.finish()
    for side in spread:
        side.finish()
    if work:
        work.finish()


def combine(pick_t, y, collective_id, carry, spread=(), products=()):
    rows, width = pick_t.shape[1], y.shape[2]
    anywhere = pl.BlockSpec(memory_space=pl.ANY)
    near = pl.BlockSpec(memory_space=pltpu.VMEM)
    sections = tuple(to for to, _ in carry)
    arrays = [array for _, array in carry]

    carries = [jax.ShapeDtypeStruct(array.shape, array.dtype) for array in arrays]
    if spread:
        carries.append(jax.ShapeDtypeStruct(parts_shape(spread[0]), jnp.bfloat16))
    arrays = arrays + list(spread)
    pairs = [len(rights) for _, rights in products]
    factors = [factor for left, rights in products for factor in (left, *rights)]
    outs = [
        jax.ShapeDtypeStruct((left.shape[0], left.shape[2], right.shape[2]), jnp.bfloat16)
        for left, rights in products
        for right in rights
    ]
    held = [pltpu.VMEM(array.shape[1:], jnp.bfloat16) for array in factors + outs]
    held = held + [DMA((len(held),))] if held else []

    def kernel(*refs):
        combine_kernel(sections, len(spread), pairs, *refs)

    def blocks(*lead):
        return pltpu.VMEM(lead + (rows, width), jnp.bfloat16)

    return pl.pallas_call(
        kernel,
        out_shape=[jax.ShapeDtypeStruct((rows, width), jnp.float32)]
        + carries
        + outs,
        in_specs=[near, anywhere] + [anywhere] * (len(arrays) + len(factors)),
        out_specs=[near] + [anywhere] * (len(carries) + len(outs)),
        scratch_shapes=[
            pltpu.VMEM(y.shape, jnp.bfloat16),
            blocks(4, 2),
            blocks(4, 2),
            blocks(4, 2),
            blocks(4),
            blocks(2, 4),
            DMA((16,)),
            DMA((4, PIECES)),
            DMA((2, 4, PIECES)),
            DMA((4, PIECES)),
            DMA((4, PIECES)),
            DMA((4, PIECES, 2)),
            DMA((4, PIECES, 2)),
            DMA((max(1, len(carry)), 2)),
        ]
        + sum_scratch(spread)
        + held,
        compiler_params=pltpu.CompilerParams(
            collective_id=collective_id, has_side_effects=True, vmem_limit_bytes=60 << 20
        ),
        cost_estimate=cost(),
        name="combine",
    )(pick_t, y, *arrays, *factors)


def expert_backward_kernel(
    layer, sections, x_ref, pick_ref, gate_in, up_in, slot_gate_in,
    wg_own, wu_own, wd_own, wg_other, wu_other, wd_other, *refs
):
    kept = len(sections)
    sources, refs = refs[:kept], refs[kept:]
    rows_out, gate_out, up_out, term_out, y_out, *refs = refs
    targets, refs = refs[:kept], refs[kept:]
    wg, wu, wd, rows, gate, up, slot_gate, y, wsem, isem, osem, carry_sem, *gather = refs
    gathered = len(x_ref.shape) == 3
    carried = Carried(sections, sources, targets, carry_sem)
    count = wg.shape[0]
    ready = pick_weights(
        (wg_own, wu_own, wd_own), (wg_other, wu_other, wd_other), (wg, wu, wd), wsem, layer
    )
    land = gather[0]
    d = lax.axis_index("dp")
    ins = [
        pltpu.make_async_copy(src, held, isem.at[k])
        for k, (src, held) in enumerate(((gate_in, gate), (up_in, up), (slot_gate_in, slot_gate)))
    ]
    for copy in ins:
        copy.start()

    def outs(z):
        part = pl.ds(z * 4 * CAP, 4 * CAP)
        return [
            pltpu.make_async_copy(held.at[:, part], out.at[:, part], osem.at[k, z])
            for k, (held, out) in enumerate(
                ((rows, rows_out), (gate, gate_out), (up, up_out), (slot_gate, term_out))
            )
        ] + [pltpu.make_async_copy(y.at[pl.ds(z * 4, 4)], y_out.at[pl.ds(z * 4, 4)], osem.at[4, z])]

    def compute(z):
        @pl.when(z == (0 if gathered else d))
        def _():
            for k in range(3):
                ready(k)
            for copy in ins:
                copy.wait()

        for q in range(4):
            b = z * 4 + q
            picked = low(dot(pick_ref[b], land[b]))
            for j in range(count):
                rows[j, pl.ds(b * CAP, CAP), :] = picked[j * CAP : (j + 1) * CAP]
        part = pl.ds(z * 4 * CAP, 4 * CAP)

        @pl.loop(0, count)
        def _(j):
            plain = dot_t(rows[j, part, :], wd[j])
            g = gate[j, part, :].astype(jnp.float32)
            u = up[j, part, :].astype(jnp.float32)
            sigmoid = jax.nn.sigmoid(g)
            active = g * sigmoid
            term = jnp.sum(plain * (active * u), axis=1, keepdims=True)
            grad = plain * slot_gate[j, part, :][:, :1]
            dg = low(grad * u * sigmoid * (1.0 + g * (1.0 - sigmoid)))
            du = low(grad * active)
            slot_gate[j, part, :] = jnp.broadcast_to(term, (4 * CAP, 128))
            gate[j, part, :] = dg
            up[j, part, :] = du
            result = low(dot_t(dg, wg[j]) + dot_t(du, wu[j]))
            for q in range(4):
                y[z * 4 + q, pl.ds(j * CAP, CAP), :] = result[q * CAP : (q + 1) * CAP]

        for copy in outs(z):
            copy.start()

    if gathered:

        def arriving(z):
            part = pl.ds(z * 4, 4)
            return pltpu.make_async_copy(x_ref.at[part], land.at[part], gather[1].at[z])

        for z in range(4):
            arriving(z).start()

        @pl.loop(0, 4)
        def _(z):
            arriving(z).wait()
            compute(z)

    else:
        gather_blocks(x_ref, gather, compute, carried)
        carried.finish()
    for z in range(4):
        for copy in outs(z):
            copy.wait()


def expert_backward(layer, x, pick, gate, up, slot_gate, own, other, collective_id, carry):
    count, width, units = share_shape(own[0])
    rows = x.shape[-2]
    gathered = x.ndim == 3
    slots = 16 * CAP
    bf = jnp.bfloat16
    anywhere = pl.BlockSpec(memory_space=pl.ANY)
    near = pl.BlockSpec(memory_space=pltpu.VMEM)
    results = [
        ((count, slots, width), bf),
        ((count, slots, units), bf),
        ((count, slots, units), bf),
        ((count, slots, 128), jnp.float32),
        ((16, count * CAP, width), bf),
    ]
    sections = tuple(to for to, _ in carry)
    arrays = [array for _, array in carry]

    def kernel(*refs):
        expert_backward_kernel(layer, sections, *refs)

    return pl.pallas_call(
        kernel,
        out_shape=[jax.ShapeDtypeStruct(*result) for result in results]
        + [jax.ShapeDtypeStruct(array.shape, array.dtype) for array in arrays],
        in_specs=[anywhere, near] + [anywhere] * (9 + len(arrays)),
        out_specs=[anywhere] * (5 + len(arrays)),
        scratch_shapes=[pltpu.VMEM(share_shape(weight), bf) for weight in own]
        + [pltpu.VMEM(*result) for result in results]
        + [DMA((3,)), DMA((3,)), DMA((5, 4)), DMA((max(1, len(arrays)), 2))]
        + ([pltpu.VMEM(x.shape, bf), DMA((4,))] if gathered else gather_scratch(rows, width)),
        compiler_params=pltpu.CompilerParams(
            collective_id=None if gathered else collective_id,
            has_side_effects=not gathered,
            vmem_limit_bytes=60 << 20,
        ),
        cost_estimate=cost(),
        name="expert_backward",
    )(x, pick, gate, up, slot_gate, *own, *other, *arrays)


def rope(x, cos_table, sin_table):
    lane = lax.broadcasted_iota(jnp.int32, x.shape, 1)
    turned = jnp.where(lane % HEAD_DIM < HEAD_DIM // 2, pltpu.roll(x, 128 - HEAD_DIM // 2, 1), pltpu.roll(x, HEAD_DIM // 2, 1))
    return x * cos_table + turned * sin_table


def seq_greet(s, section, spread=False):
    barrier = pltpu.get_barrier_semaphore()
    devices = [dict(seq=s ^ 1), dict(seq=s ^ 2), dict(section=1 - section)]
    if spread:
        devices.append(dict(seq=s ^ 3))
    for device in devices:
        pl.semaphore_signal(barrier, inc=1, device_id=device, device_id_type=MESH)
    pl.semaphore_wait(barrier, len(devices))


def seq_scratch(rows, width):
    return [
        pltpu.VMEM((4, rows, width), jnp.bfloat16),
        pltpu.VMEM((2, rows, width), jnp.bfloat16),
        pltpu.VMEM((2, rows, width), jnp.bfloat16),
        pltpu.VMEM((rows, width), jnp.bfloat16),
        pltpu.VMEM((rows, width), jnp.bfloat16),
        DMA(()),
        DMA((4, 2)),
        DMA((3, 2)),
    ]


class Line:
    def __init__(self, scratch):
        self.land, self.sent, self.core_in, self.y_sent, self.y_in, self.lsem, self.ag, self.rs = scratch
        self.s = lax.axis_index("seq")

    def hop(self, src, dst, sems, k, flip):
        return remote(src, dst, sems.at[k, 0], sems.at[k, 1], seq=self.s ^ flip)

    def gather(self, x_ref, use):
        s, land = self.s, self.land
        own = pltpu.make_async_copy(x_ref, land.at[s], self.lsem)
        own.start()
        over = self.hop(x_ref, land.at[s], self.ag, 0, 2)
        beside = self.hop(x_ref, land.at[s], self.ag, 1, 1)
        over.start()
        beside.start()
        own.wait()
        use(s)
        beside.wait_recv()
        use(s ^ 1)
        over.wait_recv()
        further = self.hop(land.at[s ^ 2], land.at[s ^ 2], self.ag, 2, 1)
        further.start()
        use(s ^ 2)
        further.wait_recv()
        use(s ^ 3)
        over.wait_send()
        beside.wait_send()
        further.wait_send()

    def hand_over(self, t, partial, out_ref):
        relation = t ^ self.s

        @pl.when(relation == 3)
        def _():
            self.sent[0] = low(partial[...])
            self.hop(self.sent.at[0], self.core_in.at[0], self.rs, 0, 1).start()

        @pl.when(relation == 2)
        def _():
            self.hop(self.sent.at[0], self.core_in.at[0], self.rs, 0, 1).wait_recv()
            self.y_sent[...] = low(partial[...] + self.core_in[0].astype(jnp.float32))
            self.hop(self.y_sent, self.y_in, self.rs, 1, 2).start()

        @pl.when(relation == 1)
        def _():
            self.sent[1] = low(partial[...])
            self.hop(self.sent.at[1], self.core_in.at[1], self.rs, 2, 1).start()

        @pl.when(relation == 0)
        def _():
            out_ref[...] = partial[...]

    def finish(self, out_ref):
        self.hop(self.sent.at[1], self.core_in.at[1], self.rs, 2, 1).wait()
        out_ref[...] += self.core_in[1].astype(jnp.float32)
        self.hop(self.y_sent, self.y_in, self.rs, 1, 2).wait()
        out_ref[...] += self.y_in[...].astype(jnp.float32)
        self.hop(self.sent.at[0], self.core_in.at[0], self.rs, 0, 1).wait_send()


def attention_forward_kernel(sections, x_ref, qkv_ref, wo_ref, cos_ref, sin_ref, *refs):
    kept = len(sections)
    sources, refs = refs[:kept], refs[kept:]
    sources = [share(ref) if to is None else ref for to, ref in zip(sections, sources)]
    out_ref, all_out, heads_out, lse_out, ot_out, *refs = refs
    targets, refs = refs[:kept], refs[kept:]
    wqkv, wo, heads, lse, ot, partial, wsem, osem, carry_sem, *line = refs
    line = Line(line)
    carried = Carried(sections, sources, targets, carry_sem)
    s = line.s
    rows = out_ref.shape[0]
    kv = heads.shape[0] // (GROUP + 2)
    queries = GROUP * kv
    loads = [pltpu.make_async_copy(qkv_ref, wqkv, wsem.at[0]), pltpu.make_async_copy(wo_ref, wo, wsem.at[1])]
    for load in loads:
        load.start()
    seq_greet(s, carried.section)
    carried.start()
    lse[...] = jnp.zeros_like(lse)

    def project(t):
        part = pl.ds(pl.multiple_of(t * rows, rows), rows)

        @pl.when(t == s)
        def _():
            loads[0].wait()

        qkv = low(dot(line.land[t], wqkv[...]))
        for chunk in range((queries + kv) // 2):
            x = qkv[:, chunk * 128 : (chunk + 1) * 128].astype(jnp.float32)
            x = low(rope(x, cos_ref[part, :], sin_ref[part, :]))
            heads[2 * chunk, part, :] = x[:, :HEAD_DIM]
            heads[2 * chunk + 1, part, :] = x[:, HEAD_DIM:]
        for j in range(kv):
            begin = (queries + kv + j) * HEAD_DIM
            heads[queries + kv + j, part, :] = qkv[:, begin : begin + HEAD_DIM]

    line.gather(x_ref, project)
    saves = [pltpu.make_async_copy(line.land, all_out, osem.at[0]), pltpu.make_async_copy(heads, heads_out, osem.at[1])]
    for save in saves:
        save.start()
    loads[1].wait()

    def attend(block):
        keys = (block + 1) * rows
        columns = slice(block * rows, (block + 1) * rows)

        @pl.loop(0, queries)
        def _(h):
            j = h // GROUP
            scores = dot_t(heads[queries + j, :keys, :], heads[h, columns, :]) * 0.125
            key_at = lax.broadcasted_iota(jnp.int32, scores.shape, 0)
            query_at = lax.broadcasted_iota(jnp.int32, scores.shape, 1) + block * rows
            scores = jnp.where(key_at <= query_at, scores, -jnp.inf)
            peak = jnp.max(scores, axis=0, keepdims=True)
            power = jnp.exp(scores - peak)
            total = jnp.sum(power, axis=0, keepdims=True)
            attended = t_dot(heads[queries + kv + j, :keys, :], low(power / total))
            ot[pl.ds(pl.multiple_of(h * HEAD_DIM, HEAD_DIM), HEAD_DIM), columns] = low(attended)
            lse[pl.ds(h, 1), columns] = peak + jnp.log(total)

        partial[...] = t_dot(ot[:, columns], wo[...])

    @pl.loop(0, 4)
    def _(i):
        t = s ^ (3 - i)
        for block in range(4):

            @pl.when(t == block)
            def _():
                attend(block)

        line.hand_over(t, partial, out_ref)

    saves += [pltpu.make_async_copy(lse, lse_out, osem.at[2]), pltpu.make_async_copy(ot, ot_out, osem.at[3])]
    for save in saves[2:]:
        save.start()
    line.finish(out_ref)
    carried.finish()
    for save in saves:
        save.wait()


def attention_forward_call(x, qkv_w, out_w, tables, collective_id, carry):
    rows, width = x.shape
    local_heads = qkv_w.shape[1] // HEAD_DIM
    bf, f32 = jnp.bfloat16, jnp.float32
    anywhere = pl.BlockSpec(memory_space=pl.ANY)
    near = pl.BlockSpec(memory_space=pltpu.VMEM)
    sections = tuple(to for to, _ in carry)
    arrays = [array for _, array in carry]
    results = [
        ((rows, width), f32),
        ((4, rows, width), bf),
        ((local_heads, 4 * rows, HEAD_DIM), bf),
        ((8, 4 * rows), f32),
        ((out_w.shape[0], 4 * rows), bf),
    ]

    def kernel(*refs):
        attention_forward_kernel(sections, *refs)

    return pl.pallas_call(
        kernel,
        out_shape=[jax.ShapeDtypeStruct(*result) for result in results]
        + [
            jax.ShapeDtypeStruct(share_shape(array) if to is None else array.shape, array.dtype)
            for to, array in carry
        ],
        in_specs=[anywhere] * 3 + [near] * 2 + [anywhere] * len(arrays),
        out_specs=[near] + [anywhere] * (4 + len(arrays)),
        scratch_shapes=[
            pltpu.VMEM(qkv_w.shape, bf),
            pltpu.VMEM(out_w.shape, bf),
            pltpu.VMEM(*results[2]),
            pltpu.VMEM(*results[3]),
            pltpu.VMEM(*results[4]),
            pltpu.VMEM((rows, width), f32),
            DMA((2,)),
            DMA((4,)),
            DMA((max(1, len(arrays)), 2)),
        ]
        + seq_scratch(rows, width),
        compiler_params=pltpu.CompilerParams(
            collective_id=collective_id, has_side_effects=True, vmem_limit_bytes=60 << 20
        ),
        cost_estimate=cost(),
        name="attention_forward",
    )(x, qkv_w, out_w, *tables, *arrays)


def attention_backward_kernel(
    sections, spreads, x_ref, qkv_ref, wo_ref, cos_ref, sin_ref, heads_in, lse_ref, *refs
):
    kept = len(sections)
    sources, refs = refs[:kept], refs[kept:]
    spread_sources, refs = refs[:spreads], refs[spreads:]
    spreads = spreads // 4
    out_ref, all_out, grads_out, *refs = refs
    targets, refs = refs[:kept], refs[kept:]
    spread_targets, refs = refs[:spreads], refs[spreads:]
    held, refs = refs[: 5 * spreads], refs[5 * spreads :]
    wqkv, wo, heads, douts, dk, dv, dqt, grads, partial, wsem, osem, carry_sem, *line = refs
    spread = [SumSpread(spread_sources, spread_targets[0], held)] if spreads else []
    for side in spread:
        side.load()
    line = Line(line)
    carried = Carried(sections, sources, targets, carry_sem)
    s = line.s
    rows = out_ref.shape[0]
    kv = heads.shape[0] // (GROUP + 2)
    queries = GROUP * kv
    loads = [
        pltpu.make_async_copy(wo_ref, wo, wsem.at[0]),
        pltpu.make_async_copy(qkv_ref, wqkv, wsem.at[1]),
        pltpu.make_async_copy(heads_in, heads, wsem.at[2]),
    ]
    for load in loads:
        load.start()
    seq_greet(s, carried.section, spreads > 0)
    carried.start()
    dk[...] = jnp.zeros_like(dk)
    dv[...] = jnp.zeros_like(dv)

    def project(t):
        part = pl.ds(pl.multiple_of(t * rows, rows), rows)

        @pl.when(t == s)
        def _():
            loads[0].wait()

        grad = low(dot_t(line.land[t], wo[...]))
        for h in range(queries):
            douts[h, part, :] = grad[:, h * HEAD_DIM : (h + 1) * HEAD_DIM]

    line.gather(x_ref, project)
    saves = [pltpu.make_async_copy(line.land, all_out, osem.at[0])]
    saves[0].start()
    for side in spread:
        side.start()
    loads[1].wait()
    loads[2].wait()

    for block in (3, 2, 1, 0):
        keys = (block + 1) * rows
        part = slice(block * rows, (block + 1) * rows)

        @pl.loop(0, queries)
        def _(h):
            j = h // GROUP
            key = heads[queries + j, :keys, :]
            query = heads[h, part, :]
            grad = douts[h, part, :]
            scores = dot_t(key, query) * 0.125
            key_at = lax.broadcasted_iota(jnp.int32, scores.shape, 0)
            query_at = lax.broadcasted_iota(jnp.int32, scores.shape, 1) + block * rows
            scores = jnp.where(key_at <= query_at, scores, -jnp.inf)
            probs = jnp.exp(scores - lse_ref[pl.ds(h, 1), part])
            dprobs = dot_t(heads[queries + kv + j, :keys, :], grad)
            mean = jnp.sum(probs * dprobs, axis=0, keepdims=True)
            dscores = low(probs * (dprobs - mean))
            dk[j, :keys, :] += dot(dscores, query) * 0.125
            dv[j, :keys, :] += dot(low(probs), grad)
            dqt[pl.ds(pl.multiple_of(h * HEAD_DIM, HEAD_DIM), HEAD_DIM), :] = t_dot(key, dscores) * 0.125

        cos_part, sin_part = cos_ref[part, :], -sin_ref[part, :]
        dq = dqt[...].T
        for chunk in range(queries // 2):
            lanes = slice(chunk * 128, (chunk + 1) * 128)
            grads[part, lanes] = low(rope(dq[:, lanes], cos_part, sin_part))
        for pair in range(kv // 2):
            both = jnp.concatenate([dk[2 * pair, part, :], dk[2 * pair + 1, part, :]], axis=1)
            begin = queries * HEAD_DIM + pair * 128
            grads[part, begin : begin + 128] = low(rope(both, cos_part, sin_part))
            both = jnp.concatenate([dv[2 * pair, part, :], dv[2 * pair + 1, part, :]], axis=1)
            begin = (queries + kv) * HEAD_DIM + pair * 128
            grads[part, begin : begin + 128] = low(both)
        partial[...] = dot_t(grads[part, :], wqkv[...])
        line.hand_over(block, partial, out_ref)

    saves.append(pltpu.make_async_copy(grads, grads_out, osem.at[1]))
    saves[1].start()
    line.finish(out_ref)
    carried.finish()
    for side in spread:
        side.finish()
    for save in saves:
        save.wait()


def attention_backward_call(x, qkv_w, out_w, tables, heads, lse, collective_id, carry, spread=()):
    rows, width = x.shape
    bf, f32 = jnp.bfloat16, jnp.float32
    anywhere = pl.BlockSpec(memory_space=pl.ANY)
    near = pl.BlockSpec(memory_space=pltpu.VMEM)
    sections = tuple(to for to, _ in carry)
    arrays = [array for _, array in carry]
    results = [((rows, width), f32), ((4, rows, width), bf), ((4 * rows, qkv_w.shape[1]), bf)]
    kv = heads.shape[0] // (GROUP + 2)
    queries = GROUP * kv

    carries = [jax.ShapeDtypeStruct(array.shape, array.dtype) for array in arrays]
    if spread:
        carries.append(jax.ShapeDtypeStruct(parts_shape(spread[0]), bf))
    arrays = arrays + list(spread)

    def kernel(*refs):
        attention_backward_kernel(sections, len(spread), *refs)

    return pl.pallas_call(
        kernel,
        out_shape=[jax.ShapeDtypeStruct(*result) for result in results]
        + carries,
        in_specs=[anywhere] * 3 + [near] * 2 + [anywhere, near] + [anywhere] * len(arrays),
        out_specs=[near] + [anywhere] * (2 + len(carries)),
        scratch_shapes=sum_scratch(spread)
        + [
            pltpu.VMEM(qkv_w.shape, bf),
            pltpu.VMEM(out_w.shape, bf),
            pltpu.VMEM(heads.shape, bf),
            pltpu.VMEM((queries, 4 * rows, HEAD_DIM), bf),
            pltpu.VMEM((kv, 4 * rows, HEAD_DIM), f32),
            pltpu.VMEM((kv, 4 * rows, HEAD_DIM), f32),
            pltpu.VMEM((queries * HEAD_DIM, rows), f32),
            pltpu.VMEM(*results[2]),
            pltpu.VMEM((rows, width), f32),
            DMA((3,)),
            DMA((2,)),
            DMA((max(1, len(carry)), 2)),
        ]
        + seq_scratch(rows, width),
        compiler_params=pltpu.CompilerParams(
            collective_id=collective_id, has_side_effects=True, vmem_limit_bytes=60 << 20
        ),
        cost_estimate=cost(),
        name="attention_backward",
    )(x, qkv_w, out_w, *tables, heads, lse, *arrays)


def last_kernel(sections, own_0, own_1, in_0, in_1, cols_ref, cols_other, out_ref, out_other, *refs):
    kept = len(sections)
    sources, refs = refs[:kept], refs[kept:]
    down_out, cols_out, rows_out, *refs = refs
    targets, refs = refs[:kept], refs[kept:]
    cols_in, cols, out_in, out_sum, cols_sem, row_sem, swap_sem, carry_sem, *held = refs
    down = SumSpread((own_0, own_1, in_0, in_1), down_out, held)
    down.load()
    d, s, section = lax.axis_index("dp"), lax.axis_index("seq"), lax.axis_index("section")
    barrier = pltpu.get_barrier_semaphore()

    def signal(**device):
        pl.semaphore_signal(barrier, inc=1, device_id=device, device_id_type=MESH)

    for flip in (1, 2, 3):
        signal(seq=s ^ flip)
    signal(section=1 - section)

    @pl.when(d != s)
    def _():
        signal(dp=s, seq=d)
        pl.semaphore_wait(barrier, 5)

    @pl.when(d == s)
    def _():
        pl.semaphore_wait(barrier, 4)

    swaps = Carried((None, None), (cols_other, out_other), (cols_in, out_in), swap_sem)
    carried = Carried(sections, sources, targets, carry_sem)
    swaps.start()
    down.start()
    swaps.finish()
    carried.start()
    cols[...] = low(cols_ref[...].astype(jnp.float32) + cols_in[...].astype(jnp.float32))
    out_sum[...] = low(out_ref[...].astype(jnp.float32) + out_in[...].astype(jnp.float32))
    spread = Spread(cols, cols_out, cols_sem)
    spread.start()
    rows = remote(out_sum, rows_out, row_sem.at[0], row_sem.at[1], dp=s, seq=d)

    @pl.when(d != s)
    def _():
        rows.start()
        rows.wait()

    @pl.when(d == s)
    def _():
        rows_out[...] = out_sum[...]

    spread.finish()
    down.finish()
    carried.finish()


def last_exchange(downs, cols, cols_other, out, out_other, collective_id, carry):
    bf = jnp.bfloat16
    anywhere = pl.BlockSpec(memory_space=pl.ANY)
    near = pl.BlockSpec(memory_space=pltpu.VMEM)
    sections = tuple(to for to, _ in carry)
    arrays = [array for _, array in carry]

    def kernel(*refs):
        last_kernel(sections, *refs)

    return pl.pallas_call(
        kernel,
        out_shape=[
            jax.ShapeDtypeStruct(parts_shape(downs[0]), bf),
            *[jax.ShapeDtypeStruct(array.shape, array.dtype) for array in (cols, out, *arrays)],
        ],
        in_specs=[anywhere] * 4 + [near, anywhere, near, anywhere] + [anywhere] * len(arrays),
        out_specs=[anywhere, near, near] + [anywhere] * len(arrays),
        scratch_shapes=[
            pltpu.VMEM(cols.shape, bf),
            pltpu.VMEM(cols.shape, bf),
            pltpu.VMEM(out.shape, bf),
            pltpu.VMEM(out.shape, bf),
            DMA((4, 2)),
            DMA((2,)),
            DMA((2, 2)),
            DMA((max(1, len(arrays)), 2)),
        ]
        + sum_scratch(downs),
        compiler_params=pltpu.CompilerParams(
            collective_id=collective_id, has_side_effects=True, vmem_limit_bytes=60 << 20
        ),
        name="last_exchange",
    )(*downs, cols, cols_other, out, out_other, *arrays)


def wide_tables(length):
    half_dim = HEAD_DIM // 2
    frequency = 10000.0 ** (-np.arange(half_dim, dtype=np.float32) * 2.0 / HEAD_DIM)
    angles = np.arange(length, dtype=np.float32)[:, None] * frequency.astype(np.float32)[None, :]
    cos_table, sin_table = np.cos(angles), np.sin(angles)
    return (
        jnp.asarray(np.concatenate([cos_table] * 4, axis=1), jnp.float32),
        jnp.asarray(np.concatenate([-sin_table, sin_table] * 2, axis=1), jnp.float32),
    )


def token_choice(route):
    return route[..., None] == jnp.arange(EXPERTS, dtype=jnp.int32)


def routing(route_all, first_expert, count):
    chosen = jnp.any(token_choice(route_all), axis=2)
    blocks, rows = chosen.shape[:2]
    mine = lax.dynamic_slice_in_dim(chosen, first_expert, count, axis=2)
    chosen = low(jnp.transpose(chosen, (0, 2, 1)))
    earlier = jnp.tril(jnp.ones((rows, rows), jnp.bfloat16), -1)
    place = jnp.einsum(
        "ts,bsj->bjt", earlier, mine.astype(jnp.bfloat16), preferred_element_type=jnp.float32
    ).astype(jnp.int32)
    mine = jnp.transpose(mine, (0, 2, 1))
    place = jnp.where(mine, place, -1)
    slots = jnp.arange(CAP, dtype=jnp.int32)
    pick = low(place[:, :, None, :] == slots[None, None, :, None]).reshape(blocks, -1, rows)
    return chosen, pick, jnp.transpose(pick, (0, 2, 1))


def choose(pick, rows, count):
    picked = jnp.einsum("bct,btd->bcd", pick, rows, preferred_element_type=jnp.float32)
    blocks = pick.shape[0]
    picked = low(picked).reshape(blocks, count, CAP, -1)
    return jnp.transpose(picked, (1, 0, 2, 3)).reshape(count, blocks * CAP, -1)


def give_back(pick_t, slot_rows):
    blocks, rows = pick_t.shape[:2]
    count, _, width = slot_rows.shape
    slot_rows = jnp.transpose(slot_rows.reshape(count, blocks, CAP, width), (1, 0, 2, 3))
    slot_rows = slot_rows.reshape(blocks, count * CAP, width)
    total = jnp.einsum("btc,bcd->btd", pick_t, slot_rows, preferred_element_type=jnp.float32)
    return low(total).reshape(-1, width)


def each_dot(form, a, b):
    return jnp.einsum(form, a, b, preferred_element_type=jnp.float32)


def after(value, *others):
    return lax.optimization_barrier((value, *others))[0]


def has_kernels():
    return lax.axis_size("dp") == 4 and lax.axis_size("seq") == 4


def forward_layer(number, layer_in, picking, weights, experts, *carry):
    attn_scale, ffn_scale, qkv_w, out_w, router_w = weights
    chosen, pick, pick_t, first_expert = picking
    own, other = experts
    count = pick.shape[1] // CAP
    blocks, _, rows = chosen.shape
    received = []
    normed_input = low(rms_norm(layer_in, attn_scale))
    if has_kernels():
        branch, normed_all, heads, log_total, mixed_t, *received = attention_forward_call(
            normed_input, qkv_w, out_w, wide_tables(4 * layer_in.shape[0]), 9 + number, carry
        )
        attention_state = (normed_all.reshape(-1, layer_in.shape[1]), mixed_t, heads, log_total)
    else:
        received = [swap(array) if to is None else pass_to(array, to) for to, array in carry]
        normed_all = lax.all_gather(normed_input, "seq", axis=0, tiled=True)
        qkv = low(dot(normed_all, qkv_w))
        kv_width = KV_HEADS * HEAD_DIM // lax.axis_size("seq")
        q_width = GROUP * kv_width
        mixed, log_total, q_rot, k_rot, v_heads = attention_forward(
            qkv[:, :q_width], qkv[:, q_width : q_width + kv_width], qkv[:, q_width + kv_width :]
        )
        branch = lax.psum_scatter(low(dot(mixed, out_w)), "seq", scatter_dimension=0, tiled=True)
        attention_state = (normed_all, mixed.T, (q_rot, k_rot, v_heads), log_total)
    after_update = layer_in + branch.astype(jnp.float32)
    normed_ffn = low(rms_norm(after_update, ffn_scale))
    own_block = lax.axis_index("dp") * lax.axis_size("seq") + lax.axis_index("seq")
    own_chosen = lax.dynamic_index_in_dim(chosen, own_block, 0, keepdims=False)
    own_logits = jnp.where(own_chosen > 0, dot_t(router_w, normed_ffn), -jnp.inf)
    own_gates = jax.nn.softmax(own_logits, axis=0)
    if number == 0:
        other = other + (received[0],)
    mine = (
        jnp.arange(EXPERTS)[None, None, :] == first_expert + jnp.arange(count)[:, None, None]
    ).astype(jnp.float32)
    if has_kernels():
        *expert_state, slot_out = expert_forward(
            number, normed_ffn, pick, chosen, router_w, mine, own, other, 1 + number
        )
        if number == 0:
            *expert_state, slot_out, other_down = (*expert_state, slot_out)
            other = other[:2] + (other_down,)
    else:
        if number == 0:
            other = other[:2] + (swap(own[2]),)
        gate_w, up_w, down_w = by_layer(number, own, other)
        ffn_all = lax.all_gather(normed_ffn, TOKENS, axis=0, tiled=True)
        logits = dot_t(ffn_all, router_w).reshape(blocks, rows, EXPERTS)
        used = jnp.transpose(chosen, (0, 2, 1)) > 0
        gates = jax.nn.softmax(jnp.where(used, logits, -jnp.inf), axis=-1)
        slot_rows = choose(pick, ffn_all.reshape(blocks, rows, -1), count)
        mine_gates = jnp.einsum("bte,jxe->bjt", gates, mine, precision=lax.Precision.HIGHEST)
        slot_gates = jnp.sum(
            pick.reshape(blocks, count, CAP, rows).astype(jnp.float32) * mine_gates[:, :, None, :],
            axis=3,
        )
        slot_gates = jnp.transpose(slot_gates, (1, 0, 2)).reshape(count, -1, 1)
        gate_pre = each_dot("ecd,edf->ecf", slot_rows, gate_w)
        up_pre = each_dot("ecd,edf->ecf", slot_rows, up_w)
        scaled = low(slot_gates * jax.nn.silu(gate_pre) * up_pre)
        slot_out = low(each_dot("ecf,efd->ecd", scaled, down_w))
        expert_state = (slot_rows, gate_pre, up_pre, scaled, slot_gates)
    saved = (
        layer_in,
        attention_state,
        after_update,
        normed_ffn,
        own_gates,
        expert_state,
    )
    return (after_update, slot_out, saved, (own, other), received)


def token_sums(pick_t, slot_out, collective_id, *carry, spread=(), products=()):
    if has_kernels():
        sums, *received = combine(pick_t, slot_out, collective_id, carry, spread, products)
        return sums, received
    sums = give_back(pick_t, slot_out).astype(jnp.float32)
    sums = lax.psum_scatter(sums, TOKENS, scatter_dimension=0, tiled=True)
    received = [pass_to(array, to) for to, array in carry]
    grads = [
        low(each_dot("eck,ecn->ekn", left, right)) for left, rights in products for right in rights
    ]
    return sums, received + list(spread) + grads


def spread_rows(parts):
    return lax.all_to_all(parts, "seq", split_axis=0, concat_axis=0, tiled=True)


def expert_gradients(number, layer_grad, saved, picking, experts, *carry, grad_all=None):
    chosen, pick, pick_t, first_expert = picking
    own, other = experts
    count = pick.shape[1] // CAP
    blocks, _, rows = chosen.shape
    slot_rows, gate_pre, up_pre, scaled, slot_gates = saved[-1]
    if has_kernels():
        slot_grads, gate_low, up_low, gate_term, slot_out, *received = expert_backward(
            number, low(layer_grad) if grad_all is None else grad_all, pick, gate_pre, up_pre, slot_gates, own, other, 4 + number, carry
        )
        gate_term = gate_term[:, :, :1]
    else:
        gate_w, up_w, down_w = by_layer(number, own, other)
        grad_all = lax.all_gather(low(layer_grad), TOKENS, axis=0, tiled=True)
        slot_grads = choose(pick, grad_all.reshape(blocks, rows, -1), count)
        plain_grad = each_dot("ecd,efd->ecf", slot_grads, down_w)
        sigmoid = jax.nn.sigmoid(gate_pre)
        activated = gate_pre * sigmoid
        gate_term = jnp.sum(plain_grad * (activated * up_pre), axis=2, keepdims=True)
        hidden_grad = slot_gates * plain_grad
        gate_low = low(hidden_grad * up_pre * sigmoid * (1.0 + gate_pre * (1.0 - sigmoid)))
        up_low = low(hidden_grad * activated)
        slot_out = low(
            each_dot("ecf,edf->ecd", gate_low, gate_w) + each_dot("ecf,edf->ecd", up_low, up_w)
        )
        received = [pass_to(array, to) for to, array in carry]
    by_slot = jnp.transpose(gate_term.reshape(count, blocks, CAP), (1, 0, 2))
    gate_terms = jnp.sum(
        pick.reshape(blocks, count, CAP, rows).astype(jnp.float32) * by_slot[..., None], axis=2
    )
    gate_terms = lax.all_to_all(gate_terms, TOKENS, split_axis=0, concat_axis=0, tiled=True)
    products = ((slot_rows, (gate_low, up_low)), (scaled, (slot_grads,)))
    return slot_out, gate_terms, products, received


def backward_layer(
    number, layer_grad, normed_grad, gate_terms, saved, picking, weights, *carry, spread=()
):
    attn_scale, ffn_scale, qkv_w, out_w, router_w = weights
    chosen, pick, _, _ = picking
    (
        layer_in,
        (normed_all, mixed_t, heads, log_total),
        after_update,
        normed_ffn,
        own_gates,
        _,
    ) = saved
    rows = chosen.shape[2]
    gate_terms = jnp.sum(gate_terms.reshape(EXPERTS, -1, rows), axis=1)
    logit_grad = low(
        own_gates * (gate_terms - jnp.sum(own_gates * gate_terms, axis=0, keepdims=True))
    )
    router_grad = dot(logit_grad, normed_ffn)
    normed_grad = normed_grad + t_dot(logit_grad, router_w)
    after_part, ffn_gain_grad = jax.vjp(rms_norm, after_update, ffn_scale)[1](normed_grad)
    after_grad = after_part + layer_grad
    if has_kernels():
        normed_attn, branch_all, qkv_grad, *received = attention_backward_call(
            low(after_grad),
            qkv_w,
            out_w,
            wide_tables(4 * layer_in.shape[0]),
            heads,
            log_total,
            11 + number,
            carry,
            spread,
        )
        branch_all = branch_all.reshape(-1, layer_in.shape[1])
    else:
        branch_all = lax.all_gather(low(after_grad), "seq", axis=0, tiled=True)
        head_grad = low(dot_t(branch_all, out_w))
        qkv_grad = attention_backward(head_grad, *heads, log_total)
        normed_attn = low(dot_t(qkv_grad, qkv_w))
        normed_attn = lax.psum_scatter(normed_attn, "seq", scatter_dimension=0, tiled=True)
        received = [pass_to(array, to) for to, array in carry]
        received = received + list(spread)
    out_grad = dot(mixed_t, branch_all)
    qkv_weight_grad = t_dot(normed_all, qkv_grad)
    input_part, attn_gain_grad = jax.vjp(rms_norm, layer_in, attn_scale)[1](
        normed_attn.astype(jnp.float32)
    )
    small = [router_grad, attn_gain_grad[None], ffn_gain_grad[None]]
    small = jnp.concatenate(small + [jnp.zeros((128 - EXPERTS - 2, small[0].shape[1]))], axis=0)
    qkv_weight_grad = jnp.concatenate([low(qkv_weight_grad), low(small).T], axis=1)
    return (input_part + after_grad, (qkv_weight_grad, low(out_grad)), received)


def by_layer(number, own, other):
    is_own = lax.axis_index("section") == number
    return jax.tree.map(lambda mine, received: jnp.where(is_own, mine, received), own, other)


def body(
    hidden_in,
    out_grad,
    attn_gain,
    ffn_gain,
    query_matrix,
    key_matrix,
    value_matrix,
    output_matrix,
    router_matrix,
    w_gate,
    w_up,
    w_down,
    routes,
):
    section = lax.axis_index("section")
    dp, seq = lax.axis_size("dp"), lax.axis_size("seq")
    seq_index = lax.axis_index("seq")
    first = section == 0
    width = hidden_in.shape[3]
    depth = query_matrix.shape[1]

    layer_in = lax.dynamic_index_in_dim(hidden_in, section, 0, keepdims=False)[0]
    top_grad = lax.dynamic_index_in_dim(out_grad, section, 0, keepdims=False)[0]
    own_group = jnp.concatenate(
        [
            matrix[0].reshape(depth, seq, -1)
            for matrix in (query_matrix, key_matrix, value_matrix)
        ],
        axis=2,
    )
    own_group = jnp.transpose(own_group, (1, 0, 2))
    to_group = []
    for flat in range(dp * seq):
        to_group.append((flat, (flat % dp) * seq + flat // dp))
    from_group = [(target, source) for source, target in to_group]
    own_out = lax.ppermute(output_matrix[0], TOKENS, to_group)
    other_out = swap(own_out)
    local = w_gate.shape[1]
    hidden_units = w_gate.shape[3]
    if local >= seq:
        count, units = local // seq, hidden_units
        start, unit_start = seq_index * count, 0
    else:
        count, units = 1, hidden_units * local // seq
        start, unit_start = seq_index * local // seq, (seq_index % (seq // local)) * units
    first_expert = lax.axis_index("dp") * local + start
    if has_kernels():
        own_experts = (w_gate[0], w_up[0], w_down[0])
    else:
        own_experts = (
            lax.dynamic_slice(w_gate[0], (start, 0, unit_start), (count, width, units)),
            lax.dynamic_slice(w_up[0], (start, 0, unit_start), (count, width, units)),
            lax.dynamic_slice(w_down[0], (start, unit_start, 0), (count, units, width)),
        )
    small = jnp.concatenate([router_matrix[0].T, attn_gain, ffn_gain], axis=0)
    paths = routes[0, :, 0]
    if has_kernels():
        small = jnp.pad(small, ((0, -small.shape[0] % 16), (0, 256 - depth)))
        paths = low(jnp.transpose(paths, (0, 2, 1)).reshape(2 * TOP_K, -1))
        *tables, small, qkv_first, qkv_second, other_gate, top_all = prepare(
            jnp.concatenate([paths, small], axis=0),
            own_group,
            own_experts[0],
            top_grad,
            count,
            depth,
            13,
        )
        pickings = [(tables[4 + n], tables[n], tables[2 + n], first_expert) for n in range(2)]
        qkv_second = lax.all_gather(
            qkv_second.reshape(seq * depth, -1), "dp", axis=0, tiled=True
        )
        qkv_layers = [qkv_first.reshape(width, -1), qkv_second]
    else:
        small = lax.all_gather(small, ("section", "dp", "seq"), axis=0, tiled=False)
        small = jnp.transpose(small.reshape(2, dp * seq, -1, depth), (0, 2, 1, 3))
        small = small.reshape(2, -1, width)
        paths = lax.all_gather(paths, ("section", "dp", "seq"), axis=0, tiled=False)
        paths = lax.dynamic_index_in_dim(paths, section, 1, keepdims=False)
        paths = paths.reshape(2, dp * seq, -1, TOP_K)
        pickings = [routing(paths[n], first_expert, count) + (first_expert,) for n in range(2)]
        other_gate = swap(own_experts[0])
        top_all = None
        other_group = swap(own_group)
        qkv_layers = []
        for number in range(2):
            part = spread_rows(by_layer(number, own_group, other_group))
            part = part.reshape(seq * depth, -1)
            qkv_layers.append(lax.all_gather(part, "dp", axis=0, tiled=True))

    weights = []
    for number in range(2):
        out_w = lax.all_gather(
            by_layer(number, own_out, other_out), "dp", axis=0, tiled=True
        )
        weights.append(
            (
                small[number, EXPERTS].astype(jnp.float32),
                small[number, EXPERTS + 1].astype(jnp.float32),
                qkv_layers[number],
                out_w,
                small[number, :EXPERTS],
            )
        )

    def own_layer(pieces):
        return jnp.where(first, pieces[0], pieces[1])

    def both_micros(own, other):
        return jnp.stack([jnp.where(first, own, other), jnp.where(first, other, own)])[
            None, :, None
        ]

    def summed(own, other):
        return own_layer(own).astype(jnp.float32) + own_layer(other).astype(jnp.float32)

    def dp_sums(dense):
        return [lax.psum_scatter(part, "dp", scatter_dimension=0, tiled=True) for part in dense]

    def row_parts(piece, kind):
        if local >= seq:
            piece = piece.reshape(count, seq, piece.shape[1] // seq, -1)
            return jnp.transpose(piece, (1, 0, 2, 3))
        if kind < 2:
            return piece.reshape(seq, -1, units)
        piece = piece.reshape(-1, hidden_units // seq, width)
        share = seq // local
        parts = jnp.zeros((seq,) + piece.shape[1:], piece.dtype)
        return lax.dynamic_update_slice_in_dim(
            parts, piece, (seq_index % share) * piece.shape[0], axis=0
        )

    def whole_rows(parts, kind):
        parts = parts.astype(jnp.float32)
        if local < seq:
            parts = parts.reshape((local, seq // local) + parts.shape[1:])
            if kind < 2:
                parts = jnp.transpose(parts, (0, 2, 1, 3))
            else:
                parts = jnp.sum(parts, axis=1)
            return parts.reshape((local,) + parts.shape[1 : 2] + (-1,))[None]
        return parts.reshape((local,) + parts.shape[2:])[None]

    experts = (own_experts, (other_gate,))
    first_in = layer_in.astype(jnp.float32)
    updated, slot_out, first_saved, experts, _ = forward_layer(
        0, first_in, pickings[0], weights[0], experts, (None, own_experts[1])
    )
    sums, _ = token_sums(pickings[0][2], slot_out, 3)
    first_out = updated + sums
    second_updated, second_slots, second_saved, experts, (other_out,) = forward_layer(
        1, first_out, pickings[1], weights[1], experts, (0, first_out)
    )
    top_grad = top_grad.astype(jnp.float32)
    slot_out, gate_terms, products, _ = expert_gradients(
        1, top_grad, second_saved, pickings[1], experts, grad_all=top_all
    )
    sums, second_experts = token_sums(pickings[1][2], slot_out, 6, products=products)
    middle_grad, second_dense, _ = backward_layer(
        1, top_grad, sums, gate_terms, second_saved, pickings[1], weights[1]
    )
    slot_out, gate_terms, products, (second_gate,) = expert_gradients(
        0, middle_grad, first_saved, pickings[0], experts, (1, second_experts[0])
    )
    (rows_in, (gate_low, up_low)), down_product = products
    gate_grad = low(each_dot("ecd,ecf->edf", rows_in, gate_low))
    slot_out, gate_grad, gate_terms = lax.optimization_barrier((slot_out, gate_grad, gate_terms))
    sums, (first_gate, second_up, *first_experts) = token_sums(
        pickings[0][2],
        slot_out,
        7,
        (0, gate_grad),
        (1, second_experts[1]),
        products=((rows_in, (up_low,)), down_product),
    )
    first_experts = [gate_grad, *first_experts]
    sums, *second_dense = lax.optimization_barrier((sums, *second_dense))
    second_dense = dp_sums(second_dense)

    def handed(kind, *received):
        own = (first_experts[kind], second_experts[kind])
        if has_kernels():
            return (*own, *received)
        return [spread_rows(row_parts(low(summed(own, received)), kind))]

    bottom_grad, first_dense, (first_up, second_down, gate_rows) = backward_layer(
        0,
        middle_grad,
        sums,
        gate_terms,
        first_saved,
        pickings[0],
        weights[0],
        (0, first_experts[1]),
        (1, second_experts[2]),
        spread=handed(0, first_gate, second_gate),
    )
    second_slots, *dense = lax.optimization_barrier((second_slots, *first_dense, *second_dense))
    first_dense, second_dense = dense[:2], dense[2:]
    first_dense = dp_sums(first_dense)
    sums, (first_down, other_middle, up_rows) = token_sums(
        pickings[1][2],
        second_slots,
        8,
        (0, first_experts[2]),
        (1, middle_grad),
        spread=handed(1, first_up, second_up),
    )
    sums, *first_dense = lax.optimization_barrier((sums, *first_dense))
    second_out = second_updated + sums
    own_cols, own_rows = [own_layer((first_dense[k], second_dense[k])) for k in range(2)]
    other_cols, other_rows = [own_layer((second_dense[k], first_dense[k])) for k in range(2)]
    if has_kernels():
        down_rows, cols_sum, out_sum, other_second, other_bottom = last_exchange(
            handed(2, first_down, second_down),
            own_cols.reshape(seq, depth, -1),
            other_cols.reshape(seq, depth, -1),
            own_rows,
            other_rows,
            14,
            ((1, second_out), (0, bottom_grad)),
        )
    else:
        (down_rows,) = handed(2, first_down, second_down)
        cols_sum = low(own_cols.astype(jnp.float32) + swap(other_cols).astype(jnp.float32))
        cols_sum = spread_rows(cols_sum.reshape(seq, depth, -1))
        out_sum = low(own_rows.astype(jnp.float32) + swap(other_rows).astype(jnp.float32))
        out_sum = lax.ppermute(out_sum, TOKENS, from_group)
        other_second, other_bottom = pass_to(second_out, 1), pass_to(bottom_grad, 0)
    expert_sums = [whole_rows(rows, k) for k, rows in enumerate((gate_rows, up_rows, down_rows))]
    layer_outs = both_micros(
        own_layer((first_out, second_out)), own_layer((other_out, other_second))
    )
    section_grads = both_micros(
        own_layer((bottom_grad, middle_grad)), own_layer((other_bottom, other_middle))
    )
    qkv_sum, out_sum = cols_sum.astype(jnp.float32), out_sum.astype(jnp.float32)
    kv_width = KV_HEADS * HEAD_DIM // seq
    q_width = GROUP * kv_width
    qkv_width = q_width + 2 * kv_width
    small_sum = jnp.sum(qkv_sum[:, :, qkv_width:], axis=0)

    def columns(begin, end):
        return jnp.transpose(qkv_sum[:, :, begin:end], (1, 0, 2)).reshape(depth, -1)[None]

    return (
        layer_outs,
        section_grads,
        small_sum[:, EXPERTS][None],
        small_sum[:, EXPERTS + 1][None],
        columns(0, q_width),
        columns(q_width, q_width + kv_width),
        columns(q_width + kv_width, qkv_width),
        out_sum[None],
        small_sum[:, :EXPERTS][None],
        *expert_sums,
    )


def solution(mesh):
    return jax.shard_map(
        body,
        mesh=mesh,
        in_specs=(
            P(None, "dp", "seq", None),
            P(None, "dp", "seq", None),
            P("section", ("dp", "seq")),
            P("section", ("dp", "seq")),
            P("section", ("dp", "seq"), None),
            P("section", ("dp", "seq"), None),
            P("section", ("dp", "seq"), None),
            P("section", ("dp", "seq"), None),
            P("section", ("dp", "seq"), None),
            P("section", "dp", None, None),
            P("section", "dp", None, None),
            P("section", "dp", None, None),
            P("section", None, "dp", "seq", None),
        ),
        out_specs=(
            P("section", None, "dp", "seq", None),
            P("section", None, "dp", "seq", None),
            P("section", ("dp", "seq")),
            P("section", ("dp", "seq")),
            P("section", ("dp", "seq"), None),
            P("section", ("dp", "seq"), None),
            P("section", ("dp", "seq"), None),
            P("section", ("dp", "seq"), None),
            P("section", ("dp", "seq"), None),
            P("section", "dp", "seq", None),
            P("section", "dp", "seq", None),
            P("section", "dp", "seq", None),
        ),
        check_vma=False,
    )
```

```python
import jax
import jax.numpy as jnp
import numpy as np
from jax import lax
from jax.experimental import pallas as pl
from jax.experimental.pallas import tpu as pltpu
from jax.sharding import PartitionSpec as P

HEADS = 24
KV_HEADS = 8
HEAD_DIM = 64
TOP_K = 8
EXPERTS = 32
CAP = 80
GROUP = HEADS // KV_HEADS
TOKENS = ("dp", "seq")
PIECES = 4
MESH = pl.DeviceIdType.MESH
DMA = pltpu.SemaphoreType.DMA

epsilon = 1e-06


def dot(a, b):
    return jnp.dot(a, b, preferred_element_type=jnp.float32)


def dot_t(a, b):
    return lax.dot_general(a, b, (((1,), (1,)), ((), ())), preferred_element_type=jnp.float32)


def t_dot(a, b):
    return lax.dot_general(a, b, (((0,), (0,)), ((), ())), preferred_element_type=jnp.float32)


def low(v):
    return v.astype(jnp.bfloat16)


def swap(block):
    return lax.ppermute(block, "section", [(0, 1), (1, 0)])


def pass_to(block, section):
    return lax.ppermute(block, "section", [(1 - section, section)])


def rms_norm(values, norm_gain):
    return (
        values * lax.rsqrt(jnp.mean(values * values, axis=-1, keepdims=True) + epsilon) * norm_gain
    )


def rotary_tables(length):
    half_dim = HEAD_DIM // 2
    frequency = 10000.0 ** (-jnp.arange(half_dim, dtype=jnp.float32) * 2.0 / HEAD_DIM)
    angles = jnp.arange(length, dtype=jnp.float32)[:, None] * frequency[None, :]
    return (jnp.cos(angles)[:, None, :], jnp.sin(angles)[:, None, :])


def rotate(values, cos_table, sin_table):
    length = values.shape[0]
    split_heads = values.reshape(length, -1, HEAD_DIM)
    first_half = split_heads[..., : HEAD_DIM // 2]
    second_half = split_heads[..., HEAD_DIM // 2 :]
    turned = jnp.concatenate(
        [
            first_half * cos_table - second_half * sin_table,
            second_half * cos_table + first_half * sin_table,
        ],
        axis=-1,
    )
    return turned.reshape(length, -1)


def attention_forward(q_heads, k_heads, v_heads):
    length = q_heads.shape[0]
    local_kv = k_heads.shape[1] // HEAD_DIM
    cos_table, sin_table = rotary_tables(length)
    q_rot = low(rotate(q_heads.astype(jnp.float32), cos_table, sin_table)).reshape(
        length, local_kv, GROUP, HEAD_DIM
    )
    k_rot = low(rotate(k_heads.astype(jnp.float32), cos_table, sin_table)).reshape(
        length, local_kv, HEAD_DIM
    )
    values = v_heads.reshape(length, local_kv, HEAD_DIM)
    block_rows = min(512, length)
    outputs = []
    totals_list = []
    for first_row in range(0, length, block_rows):
        key_end = first_row + block_rows
        scores = (
            jnp.einsum(
                "qhgd,khd->hgqk",
                q_rot[first_row:key_end],
                k_rot[:key_end],
                preferred_element_type=jnp.float32,
            )
            * 0.125
        )
        causal = (first_row + jnp.arange(block_rows, dtype=jnp.int32))[:, None] >= jnp.arange(
            key_end, dtype=jnp.int32
        )[None, :]
        scores = jnp.where(causal, scores, -jnp.inf)
        row_peak = jnp.max(scores, axis=-1, keepdims=True)
        exponents = jnp.exp(scores - row_peak)
        totals = jnp.sum(exponents, axis=-1, keepdims=True)
        attended = jnp.einsum(
            "hgqk,khd->qhgd",
            low(exponents / totals),
            values[:key_end],
            preferred_element_type=jnp.float32,
        )
        outputs.append(low(attended).reshape(block_rows, -1))
        totals_list.append((row_peak + jnp.log(totals))[..., 0])
    return (jnp.concatenate(outputs, axis=0), jnp.stack(totals_list), q_rot, k_rot, values)


def attention_backward(head_grad, q_rot, k_rot, values, log_total):
    length, local_kv = q_rot.shape[:2]
    cos_table, sin_table = rotary_tables(length)
    block_rows = min(512, length)
    grad_rows = head_grad.reshape(length, local_kv, GROUP, HEAD_DIM)
    key_acc = jnp.zeros((length, local_kv, HEAD_DIM), jnp.float32)
    value_acc = jnp.zeros((length, local_kv, HEAD_DIM), jnp.float32)
    query_parts = []
    for block_number, first_row in enumerate(range(0, length, block_rows)):
        key_end = first_row + block_rows
        q_block = q_rot[first_row:key_end]
        grad_block = grad_rows[first_row:key_end]
        key_part = k_rot[:key_end]
        scores = (
            jnp.einsum("qhgd,khd->hgqk", q_block, key_part, preferred_element_type=jnp.float32)
            * 0.125
        )
        causal = (first_row + jnp.arange(block_rows, dtype=jnp.int32))[:, None] >= jnp.arange(
            key_end, dtype=jnp.int32
        )[None, :]
        scores = jnp.where(causal, scores, -jnp.inf)
        probs_full = jnp.exp(scores - log_total[block_number][..., None])
        prob_grad = jnp.einsum(
            "qhgd,khd->hgqk", grad_block, values[:key_end], preferred_element_type=jnp.float32
        )
        score_grad = probs_full * (
            prob_grad - jnp.sum(probs_full * prob_grad, axis=-1, keepdims=True)
        )
        score_low = low(score_grad)
        query_parts.append(
            jnp.einsum("hgqk,khd->qhgd", score_low, key_part, preferred_element_type=jnp.float32)
            * 0.125
        )
        key_acc = key_acc.at[:key_end].add(
            jnp.einsum("hgqk,qhgd->khd", score_low, q_block, preferred_element_type=jnp.float32)
            * 0.125
        )
        value_acc = value_acc.at[:key_end].add(
            jnp.einsum(
                "hgqk,qhgd->khd", low(probs_full), grad_block, preferred_element_type=jnp.float32
            )
        )
    query_all = jnp.concatenate(query_parts, axis=0).reshape(length, -1)
    query_grad = rotate(query_all, cos_table, -sin_table)
    key_grad = rotate(key_acc.reshape(length, -1), cos_table, -sin_table)
    return jnp.concatenate(
        [low(query_grad), low(key_grad), low(value_acc).reshape(length, -1)], axis=1
    )


def remote(src, dst, send_sem, recv_sem, **device):
    return pltpu.make_async_remote_copy(
        src_ref=src,
        dst_ref=dst,
        send_sem=send_sem,
        recv_sem=recv_sem,
        device_id=device,
        device_id_type=MESH,
    )


def greet(d, s, section=None, spread=False):
    barrier = pltpu.get_barrier_semaphore()

    def signal(**device):
        pl.semaphore_signal(barrier, inc=1, device_id=device, device_id_type=MESH)

    signal(seq=s ^ 1)
    signal(seq=s ^ 2)

    @pl.when(d > 0)
    def _():
        signal(dp=d - 1)

    @pl.when(d < 3)
    def _():
        signal(dp=d + 1)

    known = 3
    if section is not None:
        signal(section=1 - section)
        known = 4
    if spread:
        signal(seq=s ^ 3)
        known = known + 1
    inner = (d > 0) & (d < 3)

    @pl.when(inner)
    def _():
        pl.semaphore_wait(barrier, known + 1)

    @pl.when(jnp.logical_not(inner))
    def _():
        pl.semaphore_wait(barrier, known)


class Carried:
    def __init__(self, sections, sources, targets, sems):
        self.section = lax.axis_index("section")
        self.copies = []
        for k, (to, source, target) in enumerate(zip(sections, sources, targets)):
            copy = remote(source, target, sems.at[k, 0], sems.at[k, 1], section=1 - self.section)
            self.copies.append((to, copy))

    def start(self):
        for to, copy in self.copies:
            if to is None:
                copy.start()
            else:

                @pl.when(self.section != to)
                def _():
                    copy.start()

    def finish(self):
        for to, copy in self.copies:
            if to is None:
                copy.wait()
            else:

                @pl.when(self.section != to)
                def _():
                    copy.wait_send()

                @pl.when(self.section == to)
                def _():
                    copy.wait_recv()


class Spread:
    def __init__(self, source, target, sems):
        s = lax.axis_index("seq")
        self.local = pltpu.make_async_copy(source.at[s], target.at[s], sems.at[0, 0])
        self.copies = [
            remote(source.at[s ^ flip], target.at[s], sems.at[flip, 0], sems.at[flip, 1], seq=s ^ flip)
            for flip in (3, 2, 1)
        ]

    def start(self):
        for copy in self.copies:
            copy.start()
        self.local.start()

    def finish(self):
        self.local.wait()
        for copy in self.copies:
            copy.wait()


class SumSpread:
    def __init__(self, refs, target, held):
        self.refs, self.target = refs, target
        self.a, self.b, self.parts, self.loads, self.sems = held

    def copies(self, own, received):
        return [
            pltpu.make_async_copy(own, self.a, self.loads.at[0]),
            pltpu.make_async_copy(received, self.b, self.loads.at[1]),
        ]

    def load(self):
        own_0, own_1, in_0, in_1 = self.refs

        @pl.when(lax.axis_index("section") == 0)
        def _():
            for copy in self.copies(own_0, in_0):
                copy.start()

        @pl.when(lax.axis_index("section") == 1)
        def _():
            for copy in self.copies(own_1, in_1):
                copy.start()

    def start(self):
        for copy in self.copies(self.refs[0], self.refs[2]):
            copy.wait()
        group, count, rows, width = self.parts.shape
        chunk = 24576 // width
        for g in range(group):
            for j in range(count):

                @pl.loop(0, rows // chunk)
                def _(m):
                    here = pl.ds(pl.multiple_of(m * chunk, chunk), chunk)
                    there = pl.ds(pl.multiple_of(g * rows + m * chunk, chunk), chunk)
                    total = self.a[j, there, :].astype(jnp.float32)
                    total = total + self.b[j, there, :].astype(jnp.float32)
                    self.parts[g, j, here, :] = low(total)

        self.spread = Spread(self.parts, self.target, self.sems)
        self.spread.start()

    def finish(self):
        self.spread.finish()


def parts_shape(array):
    count, rows, width = array.shape
    return (4, count, rows // 4, width)


def sum_scratch(arrays):
    if not arrays:
        return []
    shape, bf = arrays[0].shape, jnp.bfloat16
    return [
        pltpu.VMEM(shape, bf),
        pltpu.VMEM(shape, bf),
        pltpu.VMEM(parts_shape(arrays[0]), bf),
        DMA((2,)),
        DMA((4, 2)),
    ]


def cost():
    return pl.CostEstimate(flops=80_000_000_000, bytes_accessed=100_000_000, transcendentals=0)


def gather_scratch(rows, width):
    return [
        pltpu.VMEM((16, rows, width), jnp.bfloat16),
        DMA(()),
        DMA((2, 4)),
        DMA((4,)),
        DMA((4,)),
        DMA((4,)),
        DMA((4, 2)),
        DMA((4, 2)),
    ]


class Gather:
    def __init__(self, scratch):
        self.land, self.lsem, self.zs, self.zr, self.ys, self.yr, self.cs, self.cr = scratch
        self.d, self.s = lax.axis_index("dp"), lax.axis_index("seq")

    def place(self, z, column):
        return self.land.at[z * 4 + column]

    def z_copy(self, src, z, right):
        target = self.d + 1 if right else self.d - 1
        return remote(src, self.place(z, self.s), self.zs.at[int(right), z], self.zr.at[z], dp=target)

    def y_copy(self, src, z):
        return remote(src, self.place(z, self.s), self.ys.at[z], self.yr.at[z], seq=self.s ^ 2)

    def core_copy(self, src, z, across):
        column = self.s ^ 2 if across else self.s
        return remote(
            src, self.place(z, column), self.cs.at[z, across], self.cr.at[z, across], seq=self.s ^ 1
        )

    def begin(self, x_ref):
        d = self.d
        own = pltpu.make_async_copy(x_ref, self.place(d, self.s), self.lsem)
        own.start()

        @pl.when(d < 3)
        def _():
            self.z_copy(x_ref, d, True).start()

        @pl.when(d > 0)
        def _():
            self.z_copy(x_ref, d, False).start()

        self.y_copy(x_ref, d).start()
        self.core_copy(x_ref, d, 0).start()
        own.wait()

    def send_on(self, q):
        following = near_first(self.d, q)
        here = self.place(following, self.s)
        self.y_copy(here, following).start()
        self.core_copy(here, following, 0).start()

    def step(self, i):
        d, s, place = self.d, self.s, self.place

        @pl.when(i < 3)
        def _():
            early = (d > 0) & (d < 3) & (i > 0)

            @pl.when(early)
            def _():
                self.send_on(i + 1)

            left, right = d - (i + 1), d + (i + 1)

            @pl.when(left >= 0)
            def _():
                self.z_copy(place(left, s), left, True).wait_recv()

                @pl.when(d < 3)
                def _():
                    self.z_copy(place(left, s), left, True).start()

            @pl.when(right <= 3)
            def _():
                self.z_copy(place(right, s), right, False).wait_recv()

                @pl.when(d > 0)
                def _():
                    self.z_copy(place(right, s), right, False).start()

            @pl.when(jnp.logical_not(early))
            def _():
                self.send_on(i + 1)

        z = near_first(d, i)
        self.y_copy(place(z, s ^ 2), z).wait_recv()
        self.core_copy(place(z, s ^ 2), z, 1).start()
        self.core_copy(place(z, s ^ 1), z, 0).wait_recv()
        self.core_copy(place(z, s ^ 3), z, 1).wait_recv()
        return z

    def finish(self):
        d, s, place = self.d, self.s, self.place
        for z in range(4):

            @pl.when((z <= d) & (d < 3))
            def _():
                self.z_copy(place(z, s), z, True).wait_send()

            @pl.when((z >= d) & (d > 0))
            def _():
                self.z_copy(place(z, s), z, False).wait_send()

            self.y_copy(place(z, s), z).wait_send()
            self.core_copy(place(z, s), z, 0).wait_send()
            self.core_copy(place(z, s), z, 1).wait_send()


def gather_blocks(x_ref, scratch, compute, carried=None):
    gather = Gather(scratch)
    greet(gather.d, gather.s, None if carried is None else carried.section)
    gather.begin(x_ref)
    if carried is not None:
        carried.start()

    @pl.loop(0, 4)
    def _(i):
        compute(gather.step(i))

    gather.finish()


def prepare_kernel(
    x_ref, group_ref, gate_ref, grad_ref,
    pick_0, pick_1, pick_t_0, pick_t_1, chosen_0, chosen_1, small_out, qkv_out, parts_out, gate_out, grad_out,
    both, places, block, groups, parts, lsem, osem, carry_sem, spread_sem, qs, qr, *gather
):
    d, s, section = lax.axis_index("dp"), lax.axis_index("seq"), lax.axis_index("section")
    gather = Gather(gather)
    land = gather.land
    known = x_ref.shape[0]
    count = pick_0.shape[1] // CAP
    rows = pick_0.shape[2]
    width = x_ref.shape[1]
    part = both.at[pl.ds(pl.multiple_of(section * known, known), known)]
    swaps = Carried((None, None), (x_ref, group_ref), (part, groups.at[section]), carry_sem)
    gates = Carried((None,), (share(gate_ref),), (gate_out,), carry_sem.at[pl.ds(2, 1)])
    spreads = [Spread(groups.at[n], parts.at[n], spread_sem.at[n]) for n in range(2)]
    own_columns = pltpu.make_async_copy(parts.at[0], qkv_out.at[d], lsem.at[3])

    def along(src, z, right):
        target = d + 1 if right else d - 1
        return remote(src, qkv_out.at[z], qs.at[int(right), z], qr.at[z], dp=target)

    def first():
        swaps.start()
        own = [
            pltpu.make_async_copy(x_ref, part, lsem.at[0]),
            pltpu.make_async_copy(group_ref, groups.at[section], lsem.at[1]),
            pltpu.make_async_copy(grad_ref, block.at[pl.ds(0, rows)], lsem.at[2]),
        ]
        for copy in own:
            copy.start()
        for copy in own:
            copy.wait()
        swaps.finish()
        gates.start()
        for side in spreads:
            side.start()
        spreads[0].finish()
        own_columns.start()

        @pl.when(d < 3)
        def _():
            along(parts.at[0], d, True).start()

        @pl.when(d > 0)
        def _():
            along(parts.at[0], d, False).start()

    def hop(h):
        @pl.when(d - h >= 0)
        def _():
            along(qkv_out.at[d - h], d - h, True).wait_recv()

            @pl.when(d < 3)
            def _():
                along(qkv_out.at[d - h], d - h, True).start()

        @pl.when(d + h <= 3)
        def _():
            along(qkv_out.at[d + h], d + h, False).wait_recv()

            @pl.when(d > 0)
            def _():
                along(qkv_out.at[d + h], d + h, False).start()

    first_expert = (d * 4 + s) * count
    before = lax.broadcasted_iota(jnp.int32, (rows, rows), 0)
    before = low(before < lax.broadcasted_iota(jnp.int32, (rows, rows), 1))
    slot = lax.broadcasted_iota(jnp.int32, (CAP, rows), 0)
    expert = lax.broadcasted_iota(jnp.int32, (EXPERTS, rows), 0)
    lane = lax.broadcasted_iota(jnp.int32, (rows, count * CAP), 1)

    def tables(z, layer, pick_out, pick_t_out, chosen_out):
        @pl.loop(z * 4, z * 4 + 4)
        def _(b):
            lanes = slice(2 * layer * width, (2 * layer + 1) * width)
            paths = land[b, rows : rows + 16, lanes].astype(jnp.float32)
            paths = jnp.where(section == 0, paths[:TOP_K], paths[TOP_K:]).astype(jnp.int32)
            chosen = expert == paths[0:1]
            for k in range(1, TOP_K):
                chosen = chosen | (expert == paths[k : k + 1])
            chosen_out[b] = low(chosen)
            mine = [
                jnp.max((paths == first_expert + j).astype(jnp.float32), axis=0, keepdims=True)
                for j in range(count)
            ]
            mine = jnp.concatenate(mine + [jnp.zeros((8 - count, rows), jnp.float32)], axis=0)
            place = jnp.where(mine > 0.5, dot(low(mine), before), -10000.0)
            places[...] = place
            for j in range(count):
                pick_out[b, j * CAP : (j + 1) * CAP, :] = low(
                    slot == place[j : j + 1].astype(jnp.int32)
                )
            turned = places[...].T.astype(jnp.int32)
            pick_t = turned[:, 0:1] == lane
            for j in range(1, count):
                pick_t = pick_t & (lane < j * CAP) | (turned[:, j : j + 1] == lane - j * CAP)
            pick_t_out[b] = low(pick_t)

    greet(d, s, section, True)
    first()
    for part_of in range(4):
        lanes = slice(part_of * width, (part_of + 1) * width)
        block[rows:, lanes] = both[part_of * known // 2 : (part_of + 1) * known // 2, :]
    block[rows:, 4 * width :] = jnp.zeros((known // 2, block.shape[1] - 4 * width), block.dtype)
    gather.begin(block)

    def grad_copy(z):
        four = pl.ds(z * 4, 4)
        return pltpu.make_async_copy(land.at[four, pl.ds(0, rows)], grad_out.at[four], osem.at[z])

    @pl.loop(0, 4)
    def _(i):
        z = gather.step(i)
        grad_copy(z).start()
        for h in (1, 2, 3):

            @pl.when(i == h - 1)
            def _():
                hop(h)

        tables(z, 0, pick_0, pick_t_0, chosen_0)
        tables(z, 1, pick_1, pick_t_1, chosen_1)

    depth = small_out.shape[2] // 16
    rest = known // 2 - 16
    for layer in range(2):
        for b in range(16):
            columns = slice(b * depth, (b + 1) * depth)
            begin = 2 * layer * width
            small_out[layer, :rest, columns] = land[b, rows + 16 :, begin : begin + depth]
            begin = begin + width
            small_out[layer, rest:, columns] = land[b, rows:, begin : begin + depth]
    gather.finish()
    for z in range(4):
        grad_copy(z).wait()
    spreads[1].finish()
    layer_1 = pltpu.make_async_copy(parts.at[1], parts_out, lsem.at[0])
    layer_1.start()
    for z in range(4):

        @pl.when((z <= d) & (d < 3))
        def _():
            along(parts.at[0], z, True).wait_send()

        @pl.when((z >= d) & (d > 0))
        def _():
            along(parts.at[0], z, False).wait_send()

    own_columns.wait()
    layer_1.wait()
    gates.finish()


def prepare(x, group, gate, grad, count, depth, collective_id):
    known, width = x.shape
    rows = grad.shape[0]
    bf = jnp.bfloat16
    anywhere = pl.BlockSpec(memory_space=pl.ANY)
    near = pl.BlockSpec(memory_space=pltpu.VMEM)
    return pl.pallas_call(
        prepare_kernel,
        out_shape=[
            jax.ShapeDtypeStruct((16, count * CAP, rows), bf),
            jax.ShapeDtypeStruct((16, count * CAP, rows), bf),
            jax.ShapeDtypeStruct((16, rows, count * CAP), bf),
            jax.ShapeDtypeStruct((16, rows, count * CAP), bf),
            jax.ShapeDtypeStruct((16, EXPERTS, rows), bf),
            jax.ShapeDtypeStruct((16, EXPERTS, rows), bf),
            jax.ShapeDtypeStruct((2, known - 16, 16 * depth), bf),
            jax.ShapeDtypeStruct((4,) + group.shape, bf),
            jax.ShapeDtypeStruct(group.shape, bf),
            jax.ShapeDtypeStruct(share_shape(gate), bf),
            jax.ShapeDtypeStruct((16,) + grad.shape, bf),
        ],
        in_specs=[anywhere] * 4,
        out_specs=[near] * 7 + [anywhere] * 4,
        scratch_shapes=[
            pltpu.VMEM((2 * known, width), bf),
            pltpu.VMEM((8, rows), jnp.float32),
            pltpu.VMEM((rows + known // 2, grad.shape[1]), bf),
            pltpu.VMEM((2,) + group.shape, bf),
            pltpu.VMEM((2,) + group.shape, bf),
            DMA((4,)),
            DMA((4,)),
            DMA((3, 2)),
            DMA((2, 4, 2)),
            DMA((2, 4)),
            DMA((4,)),
        ]
        + gather_scratch(rows + known // 2, grad.shape[1]),
        compiler_params=pltpu.CompilerParams(
            collective_id=collective_id, has_side_effects=True, vmem_limit_bytes=60 << 20
        ),
        cost_estimate=cost(),
        name="prepare",
    )(x, group, gate, grad)


def share(ref):
    count = ref.shape[0] // 4
    return ref.at[pl.ds(lax.axis_index("seq") * count, count)]


def share_shape(array):
    return (array.shape[0] // 4,) + array.shape[1:]


def pick_weights(own_refs, other_refs, held, sems, own_layer):
    own_refs = [share(ref) for ref in own_refs]
    mine = lax.axis_index("section") == own_layer

    @pl.when(mine)
    def _():
        for k, ref in enumerate(own_refs):
            pltpu.make_async_copy(ref, held[k], sems.at[k]).start()

    @pl.when(jnp.logical_not(mine))
    def _():
        for k, ref in enumerate(other_refs):
            pltpu.make_async_copy(ref, held[k], sems.at[k]).start()

    def ready(k):
        pltpu.make_async_copy(own_refs[k], held[k], sems.at[k]).wait()

    return ready


def expert_forward_kernel(
    layer, x_ref, pick_ref, chosen_ref, router_ref, mine_ref,
    wg_own, wu_own, wd_own, wg_other, wu_other, wd_other,
    rows_out, gate_out, up_out, hidden_out, slot_gate_out, y_out,
    wg, wu, wd, rows, gate, up, hidden, slot_gate, y, wsem, osem, carry_sem, *gather
):
    count = wg.shape[0]
    carried = None
    if layer == 0:
        carried = Carried((None,), (share(wd_own),), (wd_other,), carry_sem)
        ready = pick_weights((wg_own, wu_own), (wg_other, wu_other), (wg, wu), wsem, layer)
    else:
        ready = pick_weights(
            (wg_own, wu_own, wd_own), (wg_other, wu_other, wd_other), (wg, wu, wd), wsem, layer
        )
    land = gather[0]
    d = lax.axis_index("dp")

    def outs(z):
        part = pl.ds(z * 4 * CAP, 4 * CAP)
        return [
            pltpu.make_async_copy(held.at[:, part], out.at[:, part], osem.at[k, z])
            for k, (held, out) in enumerate(
                ((rows, rows_out), (gate, gate_out), (up, up_out), (hidden, hidden_out), (slot_gate, slot_gate_out))
            )
        ] + [pltpu.make_async_copy(y.at[pl.ds(z * 4, 4)], y_out.at[pl.ds(z * 4, 4)], osem.at[5, z])]

    def down(z):
        part = pl.ds(z * 4 * CAP, 4 * CAP)

        @pl.loop(0, count)
        def _(j):
            result = low(dot(hidden[j, part, :], wd[j]))
            for q in range(4):
                y[z * 4 + q, pl.ds(j * CAP, CAP), :] = result[q * CAP : (q + 1) * CAP]

    def compute(z):
        @pl.when(z == d)
        def _():
            for k in range(2 if layer == 0 else 3):
                ready(k)

        for q in range(4):
            b = z * 4 + q
            picked = low(dot(pick_ref[b], land[b]))
            for j in range(count):
                rows[j, pl.ds(b * CAP, CAP), :] = picked[j * CAP : (j + 1) * CAP]
        part = pl.ds(z * 4 * CAP, 4 * CAP)

        @pl.loop(0, count)
        def _(j):
            x = rows[j, part, :]
            g = dot(x, wg[j])
            u = dot(x, wu[j])
            logits = dot_t(x, router_ref[...])
            for q in range(4):
                b = z * 4 + q
                slots = slice(q * CAP, (q + 1) * CAP)
                seen = dot_t(pick_ref[b, pl.ds(j * CAP, CAP), :], chosen_ref[b])
                masked = jnp.where(seen > 0.5, logits[slots], -1e30)
                power = jnp.exp(masked - jnp.max(masked, axis=1, keepdims=True))
                own = jnp.sum(power * mine_ref[j], axis=1, keepdims=True)
                value = own / jnp.sum(power, axis=1, keepdims=True)
                slot_gate[j, pl.ds(b * CAP, CAP), :] = jnp.broadcast_to(value, (CAP, 128))
            gate[j, part, :] = low(g)
            up[j, part, :] = low(u)
            h = low(g * jax.nn.sigmoid(g) * u * slot_gate[j, part, :][:, :1])
            hidden[j, part, :] = h

        if layer != 0:
            down(z)
        for copy in outs(z)[: 5 if layer == 0 else 6]:
            copy.start()

    gather_blocks(x_ref, gather, compute, carried)
    if layer == 0:
        carried.finish()
        ready = pick_weights((wd_own,), (wd_other,), (wd,), wsem, layer)
        ready(0)
        for z in range(4):
            down(z)
            outs(z)[5].start()
    for z in range(4):
        for copy in outs(z):
            copy.wait()


def expert_forward(layer, x, pick, chosen, router, mine, own, other, collective_id):
    count, width, units = share_shape(own[0])
    rows = x.shape[0]
    slots = 16 * CAP
    bf = jnp.bfloat16
    anywhere = pl.BlockSpec(memory_space=pl.ANY)
    near = pl.BlockSpec(memory_space=pltpu.VMEM)
    results = [
        ((count, slots, width), bf),
        ((count, slots, units), bf),
        ((count, slots, units), bf),
        ((count, slots, units), bf),
        ((count, slots, 128), jnp.float32),
        ((16, count * CAP, width), bf),
    ]

    def kernel(*refs):
        if layer == 0:
            refs = refs[:10] + refs[16:17] + refs[10:16] + refs[17:]
        expert_forward_kernel(layer, *refs)

    shapes = [jax.ShapeDtypeStruct(*result) for result in results]
    if layer == 0:
        shapes.append(jax.ShapeDtypeStruct(share_shape(own[2]), bf))
        other = other[:2]
    operands = (x, pick, chosen, router, mine, *own, *other)
    return pl.pallas_call(
        kernel,
        out_shape=shapes,
        in_specs=[anywhere, near, near, near, near] + [anywhere] * (len(operands) - 5),
        out_specs=[anywhere] * len(shapes),
        scratch_shapes=[pltpu.VMEM(share_shape(weight), bf) for weight in own]
        + [pltpu.VMEM(*result) for result in results]
        + [DMA((3,)), DMA((6, 4)), DMA((1, 2))]
        + gather_scratch(rows, width),
        compiler_params=pltpu.CompilerParams(
            collective_id=collective_id, has_side_effects=True, vmem_limit_bytes=60 << 20
        ),
        cost_estimate=cost(),
        name="expert_forward",
    )(*operands)


class Products:
    def __init__(self, pairs, outs, held, sems):
        self.units = []
        count = outs[0].shape[0]
        for j in range(count):
            at, out_at = 0, 0
            for left, rights in pairs:
                first = at
                loads = [(left, at)] + [(right, at + 1 + k) for k, right in enumerate(rights)]
                at += len(loads)
                for k in range(len(rights)):
                    self.units.append((j, first, first + 1 + k, out_at, loads, k == 0, k + 1 == len(rights)))
                    out_at += 1
        self.count, self.pairs, self.outs, self.held, self.sems = count, at, outs, held, sems

    def load(self, j, source, at):
        return pltpu.make_async_copy(source.at[j], self.held[at], self.sems.at[at])

    def store(self, j, k):
        at = self.pairs + k
        return pltpu.make_async_copy(self.held[at], self.outs[k].at[j], self.sems.at[at])

    def start(self):
        for j, _, _, _, loads, first, _ in self.units:
            if j == 0 and first:
                for source, at in loads:
                    self.load(0, source, at).start()

    def step(self, i):
        for number, (j, left, right, out, loads, first, last) in enumerate(self.units):

            @pl.when(i == number * (PIECES // 2))
            def _():
                if first:
                    for source, at in loads:
                        self.load(j, source, at).wait()
                if j > 0:
                    self.store(j - 1, out).wait()
                a, b, c = self.held[left], self.held[right], self.held[self.pairs + out]

                @pl.loop(0, a.shape[1] // 256)
                def _(m):
                    columns = pl.ds(pl.multiple_of(m * 256, 256), 256)
                    c[columns, :] = low(t_dot(a[:, columns], b[...]))

                self.store(j, out).start()
                if last and j + 1 < self.count:
                    for source, at in loads:
                        self.load(j + 1, source, at).start()

    def finish(self):
        for k in range(len(self.outs)):
            self.store(self.count - 1, k).wait()


def far_first(d, q):
    inner = (d % 3 + 2) // 3
    base = 3 - q + inner * (q // 2) * (2 * q - 5)
    mirrored = d // 2
    return base * (1 - 2 * mirrored) + 3 * mirrored


def near_first(d, q):
    inner = (d % 3 + 2) // 3
    base = q + inner * (1 - q // 2) * (1 - 2 * q)
    mirrored = d // 2
    return base * (1 - 2 * mirrored) + 3 * mirrored


def combine_kernel(sections, spreads, pairs, pick_ref, y_ref, *refs):
    kept = len(sections)
    sources, refs = refs[:kept], refs[kept:]
    spread_sources, refs = refs[:spreads], refs[spreads:]
    spreads = spreads // 4
    factors = []
    for rights in pairs:
        factors.append((refs[0], refs[1 : 1 + rights]))
        refs = refs[1 + rights :]
    out_ref, *refs = refs
    targets, refs = refs[:kept], refs[kept:]
    spread_targets, refs = refs[:spreads], refs[spreads:]
    products = sum(pairs)
    product_outs, refs = refs[:products], refs[products:]
    y, sent, own, core_in, y_in, z_in, lsem, zs, zr, ys, yr, cs, cr, carry_sem, *refs = refs
    held, refs = refs[: 5 * spreads], refs[5 * spreads :]
    work = Products(factors, product_outs, refs[:-1], refs[-1]) if pairs else None
    carried = Carried(sections, sources, targets, carry_sem)
    spread = [SumSpread(spread_sources, spread_targets[0], held)] if spreads else []
    for side in spread:
        side.load()
    d, s = lax.axis_index("dp"), lax.axis_index("seq")
    piece = out_ref.shape[0] // PIECES

    def loaded(b):
        return pltpu.make_async_copy(y_ref.at[b], y.at[b], lsem.at[b])

    def column(across, other_core):
        return s ^ (2 * across) ^ other_core

    for i in range(4):
        z = far_first(d, i)
        for across in (1, 0):
            for other_core in (1, 0):
                loaded(z * 4 + column(across, other_core)).start()
    greet(d, s, carried.section, spreads > 0)
    carried.start()

    def rows(k):
        return pl.ds(pl.multiple_of(k * piece, piece), piece)

    def partial_sum(z, k, across, other_core):
        b = z * 4 + column(across, other_core)

        @pl.when(k == 0)
        def _():
            loaded(b).wait()

        return dot(pick_ref[b, rows(k), :], y[b])

    def core_copy(z, k, across):
        return remote(
            sent.at[z, across, rows(k)],
            core_in.at[z, across, rows(k)],
            cs.at[z, k, across],
            cr.at[z, k, across],
            seq=s ^ 1,
        )

    def y_copy(z, k):
        return remote(own.at[z, 1, rows(k)], y_in.at[z, rows(k)], ys.at[z, k], yr.at[z, k], seq=s ^ 2)

    def z_copy(z, k, right):
        target = d + 1 if right else d - 1
        return remote(
            own.at[z, 0, rows(k)],
            z_in.at[int(right), z, rows(k)],
            zs.at[z, k],
            zr.at[int(right), z, k],
            dp=target,
        )

    def start(i):
        z, k = far_first(d, i // PIECES), i % PIECES
        sent[z, 1, rows(k), :] = low(partial_sum(z, k, 1, 1))
        core_copy(z, k, 1).start()
        total = partial_sum(z, k, 1, 0)
        core_copy(z, k, 1).wait_recv()
        own[z, 1, rows(k), :] = low(total + core_in[z, 1, rows(k), :].astype(jnp.float32))
        y_copy(z, k).start()
        sent[z, 0, rows(k), :] = low(partial_sum(z, k, 0, 1))
        core_copy(z, k, 0).start()

    start(0)
    for side in spread:
        side.start()
    if work:
        work.start()

    @pl.loop(0, 4 * PIECES)
    def _(i):
        @pl.when(i < 4 * PIECES - 1)
        def _():
            start(i + 1)

        if work:
            work.step(i)

        z, k = far_first(d, i // PIECES), i % PIECES
        total = partial_sum(z, k, 0, 0)
        core_copy(z, k, 0).wait_recv()
        total = total + core_in[z, 0, rows(k), :].astype(jnp.float32)
        y_copy(z, k).wait_recv()
        total = total + y_in[z, rows(k), :].astype(jnp.float32)

        @pl.when(z < d)
        def _():
            @pl.when(d < 3)
            def _():
                z_copy(z, k, False).wait_recv()
                own[z, 0, rows(k), :] = low(total + z_in[0, z, rows(k), :].astype(jnp.float32))

            @pl.when(d == 3)
            def _():
                own[z, 0, rows(k), :] = low(total)

            z_copy(z, k, False).start()

        @pl.when(z > d)
        def _():
            @pl.when(d > 0)
            def _():
                z_copy(z, k, True).wait_recv()
                own[z, 0, rows(k), :] = low(total + z_in[1, z, rows(k), :].astype(jnp.float32))

            @pl.when(d == 0)
            def _():
                own[z, 0, rows(k), :] = low(total)

            z_copy(z, k, True).start()

        @pl.when(z == d)
        def _():
            out_ref[rows(k), :] = total

    for k in range(PIECES):

        @pl.when(d < 3)
        def _():
            z_copy(d, k, False).wait_recv()
            out_ref[rows(k), :] += z_in[0, d, rows(k), :].astype(jnp.float32)

        @pl.when(d > 0)
        def _():
            z_copy(d, k, True).wait_recv()
            out_ref[rows(k), :] += z_in[1, d, rows(k), :].astype(jnp.float32)

    for z in range(4):
        for k in range(PIECES):
            core_copy(z, k, 0).wait_send()
            core_copy(z, k, 1).wait_send()
            y_copy(z, k).wait_send()

            @pl.when(z < d)
            def _():
                z_copy(z, k, False).wait_send()

            @pl.when(z > d)
            def _():
                z_copy(z, k, True).wait_send()

    carried.finish()
    for side in spread:
        side.finish()
    if work:
        work.finish()


def combine(pick_t, y, collective_id, carry, spread=(), products=()):
    rows, width = pick_t.shape[1], y.shape[2]
    anywhere = pl.BlockSpec(memory_space=pl.ANY)
    near = pl.BlockSpec(memory_space=pltpu.VMEM)
    sections = tuple(to for to, _ in carry)
    arrays = [array for _, array in carry]

    carries = [jax.ShapeDtypeStruct(array.shape, array.dtype) for array in arrays]
    if spread:
        carries.append(jax.ShapeDtypeStruct(parts_shape(spread[0]), jnp.bfloat16))
    arrays = arrays + list(spread)
    pairs = [len(rights) for _, rights in products]
    factors = [factor for left, rights in products for factor in (left, *rights)]
    outs = [
        jax.ShapeDtypeStruct((left.shape[0], left.shape[2], right.shape[2]), jnp.bfloat16)
        for left, rights in products
        for right in rights
    ]
    held = [pltpu.VMEM(array.shape[1:], jnp.bfloat16) for array in factors + outs]
    held = held + [DMA((len(held),))] if held else []

    def kernel(*refs):
        combine_kernel(sections, len(spread), pairs, *refs)

    def blocks(*lead):
        return pltpu.VMEM(lead + (rows, width), jnp.bfloat16)

    return pl.pallas_call(
        kernel,
        out_shape=[jax.ShapeDtypeStruct((rows, width), jnp.float32)]
        + carries
        + outs,
        in_specs=[near, anywhere] + [anywhere] * (len(arrays) + len(factors)),
        out_specs=[near] + [anywhere] * (len(carries) + len(outs)),
        scratch_shapes=[
            pltpu.VMEM(y.shape, jnp.bfloat16),
            blocks(4, 2),
            blocks(4, 2),
            blocks(4, 2),
            blocks(4),
            blocks(2, 4),
            DMA((16,)),
            DMA((4, PIECES)),
            DMA((2, 4, PIECES)),
            DMA((4, PIECES)),
            DMA((4, PIECES)),
            DMA((4, PIECES, 2)),
            DMA((4, PIECES, 2)),
            DMA((max(1, len(carry)), 2)),
        ]
        + sum_scratch(spread)
        + held,
        compiler_params=pltpu.CompilerParams(
            collective_id=collective_id, has_side_effects=True, vmem_limit_bytes=60 << 20
        ),
        cost_estimate=cost(),
        name="combine",
    )(pick_t, y, *arrays, *factors)


def expert_backward_kernel(
    layer, sections, x_ref, pick_ref, gate_in, up_in, slot_gate_in,
    wg_own, wu_own, wd_own, wg_other, wu_other, wd_other, *refs
):
    kept = len(sections)
    sources, refs = refs[:kept], refs[kept:]
    rows_out, gate_out, up_out, term_out, y_out, *refs = refs
    targets, refs = refs[:kept], refs[kept:]
    wg, wu, wd, rows, gate, up, slot_gate, y, wsem, isem, osem, carry_sem, *gather = refs
    gathered = len(x_ref.shape) == 3
    carried = Carried(sections, sources, targets, carry_sem)
    count = wg.shape[0]
    ready = pick_weights(
        (wg_own, wu_own, wd_own), (wg_other, wu_other, wd_other), (wg, wu, wd), wsem, layer
    )
    land = gather[0]
    d = lax.axis_index("dp")
    ins = [
        pltpu.make_async_copy(src, held, isem.at[k])
        for k, (src, held) in enumerate(((gate_in, gate), (up_in, up), (slot_gate_in, slot_gate)))
    ]
    for copy in ins:
        copy.start()

    def outs(z):
        part = pl.ds(z * 4 * CAP, 4 * CAP)
        return [
            pltpu.make_async_copy(held.at[:, part], out.at[:, part], osem.at[k, z])
            for k, (held, out) in enumerate(
                ((rows, rows_out), (gate, gate_out), (up, up_out), (slot_gate, term_out))
            )
        ] + [pltpu.make_async_copy(y.at[pl.ds(z * 4, 4)], y_out.at[pl.ds(z * 4, 4)], osem.at[4, z])]

    def compute(z):
        @pl.when(z == (0 if gathered else d))
        def _():
            for k in range(3):
                ready(k)
            for copy in ins:
                copy.wait()

        for q in range(4):
            b = z * 4 + q
            picked = low(dot(pick_ref[b], land[b]))
            for j in range(count):
                rows[j, pl.ds(b * CAP, CAP), :] = picked[j * CAP : (j + 1) * CAP]
        part = pl.ds(z * 4 * CAP, 4 * CAP)

        @pl.loop(0, count)
        def _(j):
            plain = dot_t(rows[j, part, :], wd[j])
            g = gate[j, part, :].astype(jnp.float32)
            u = up[j, part, :].astype(jnp.float32)
            sigmoid = jax.nn.sigmoid(g)
            active = g * sigmoid
            term = jnp.sum(plain * (active * u), axis=1, keepdims=True)
            grad = plain * slot_gate[j, part, :][:, :1]
            dg = low(grad * u * sigmoid * (1.0 + g * (1.0 - sigmoid)))
            du = low(grad * active)
            slot_gate[j, part, :] = jnp.broadcast_to(term, (4 * CAP, 128))
            gate[j, part, :] = dg
            up[j, part, :] = du
            result = low(dot_t(dg, wg[j]) + dot_t(du, wu[j]))
            for q in range(4):
                y[z * 4 + q, pl.ds(j * CAP, CAP), :] = result[q * CAP : (q + 1) * CAP]

        for copy in outs(z):
            copy.start()

    if gathered:

        def arriving(z):
            part = pl.ds(z * 4, 4)
            return pltpu.make_async_copy(x_ref.at[part], land.at[part], gather[1].at[z])

        for z in range(4):
            arriving(z).start()

        @pl.loop(0, 4)
        def _(z):
            arriving(z).wait()
            compute(z)

    else:
        gather_blocks(x_ref, gather, compute, carried)
        carried.finish()
    for z in range(4):
        for copy in outs(z):
            copy.wait()


def expert_backward(layer, x, pick, gate, up, slot_gate, own, other, collective_id, carry):
    count, width, units = share_shape(own[0])
    rows = x.shape[-2]
    gathered = x.ndim == 3
    slots = 16 * CAP
    bf = jnp.bfloat16
    anywhere = pl.BlockSpec(memory_space=pl.ANY)
    near = pl.BlockSpec(memory_space=pltpu.VMEM)
    results = [
        ((count, slots, width), bf),
        ((count, slots, units), bf),
        ((count, slots, units), bf),
        ((count, slots, 128), jnp.float32),
        ((16, count * CAP, width), bf),
    ]
    sections = tuple(to for to, _ in carry)
    arrays = [array for _, array in carry]

    def kernel(*refs):
        expert_backward_kernel(layer, sections, *refs)

    return pl.pallas_call(
        kernel,
        out_shape=[jax.ShapeDtypeStruct(*result) for result in results]
        + [jax.ShapeDtypeStruct(array.shape, array.dtype) for array in arrays],
        in_specs=[anywhere, near] + [anywhere] * (9 + len(arrays)),
        out_specs=[anywhere] * (5 + len(arrays)),
        scratch_shapes=[pltpu.VMEM(share_shape(weight), bf) for weight in own]
        + [pltpu.VMEM(*result) for result in results]
        + [DMA((3,)), DMA((3,)), DMA((5, 4)), DMA((max(1, len(arrays)), 2))]
        + ([pltpu.VMEM(x.shape, bf), DMA((4,))] if gathered else gather_scratch(rows, width)),
        compiler_params=pltpu.CompilerParams(
            collective_id=None if gathered else collective_id,
            has_side_effects=not gathered,
            vmem_limit_bytes=60 << 20,
        ),
        cost_estimate=cost(),
        name="expert_backward",
    )(x, pick, gate, up, slot_gate, *own, *other, *arrays)


def rope(x, cos_table, sin_table):
    lane = lax.broadcasted_iota(jnp.int32, x.shape, 1)
    turned = jnp.where(lane % HEAD_DIM < HEAD_DIM // 2, pltpu.roll(x, 128 - HEAD_DIM // 2, 1), pltpu.roll(x, HEAD_DIM // 2, 1))
    return x * cos_table + turned * sin_table


def seq_greet(s, section, spread=False):
    barrier = pltpu.get_barrier_semaphore()
    devices = [dict(seq=s ^ 1), dict(seq=s ^ 2), dict(section=1 - section)]
    if spread:
        devices.append(dict(seq=s ^ 3))
    for device in devices:
        pl.semaphore_signal(barrier, inc=1, device_id=device, device_id_type=MESH)
    pl.semaphore_wait(barrier, len(devices))


def seq_scratch(rows, width):
    return [
        pltpu.VMEM((4, rows, width), jnp.bfloat16),
        pltpu.VMEM((2, rows, width), jnp.bfloat16),
        pltpu.VMEM((2, rows, width), jnp.bfloat16),
        pltpu.VMEM((rows, width), jnp.bfloat16),
        pltpu.VMEM((rows, width), jnp.bfloat16),
        DMA(()),
        DMA((4, 2)),
        DMA((3, 2)),
    ]


class Line:
    def __init__(self, scratch):
        self.land, self.sent, self.core_in, self.y_sent, self.y_in, self.lsem, self.ag, self.rs = scratch
        self.s = lax.axis_index("seq")

    def hop(self, src, dst, sems, k, flip):
        return remote(src, dst, sems.at[k, 0], sems.at[k, 1], seq=self.s ^ flip)

    def gather(self, x_ref, use):
        s, land = self.s, self.land
        own = pltpu.make_async_copy(x_ref, land.at[s], self.lsem)
        own.start()
        over = self.hop(x_ref, land.at[s], self.ag, 0, 2)
        beside = self.hop(x_ref, land.at[s], self.ag, 1, 1)
        over.start()
        beside.start()
        own.wait()
        use(s)
        beside.wait_recv()
        use(s ^ 1)
        over.wait_recv()
        further = self.hop(land.at[s ^ 2], land.at[s ^ 2], self.ag, 2, 1)
        further.start()
        use(s ^ 2)
        further.wait_recv()
        use(s ^ 3)
        over.wait_send()
        beside.wait_send()
        further.wait_send()

    def hand_over(self, t, partial, out_ref):
        relation = t ^ self.s

        @pl.when(relation == 3)
        def _():
            self.sent[0] = low(partial[...])
            self.hop(self.sent.at[0], self.core_in.at[0], self.rs, 0, 1).start()

        @pl.when(relation == 2)
        def _():
            self.hop(self.sent.at[0], self.core_in.at[0], self.rs, 0, 1).wait_recv()
            self.y_sent[...] = low(partial[...] + self.core_in[0].astype(jnp.float32))
            self.hop(self.y_sent, self.y_in, self.rs, 1, 2).start()

        @pl.when(relation == 1)
        def _():
            self.sent[1] = low(partial[...])
            self.hop(self.sent.at[1], self.core_in.at[1], self.rs, 2, 1).start()

        @pl.when(relation == 0)
        def _():
            out_ref[...] = partial[...]

    def finish(self, out_ref):
        self.hop(self.sent.at[1], self.core_in.at[1], self.rs, 2, 1).wait()
        out_ref[...] += self.core_in[1].astype(jnp.float32)
        self.hop(self.y_sent, self.y_in, self.rs, 1, 2).wait()
        out_ref[...] += self.y_in[...].astype(jnp.float32)
        self.hop(self.sent.at[0], self.core_in.at[0], self.rs, 0, 1).wait_send()


def attention_forward_kernel(sections, x_ref, qkv_ref, wo_ref, cos_ref, sin_ref, *refs):
    kept = len(sections)
    sources, refs = refs[:kept], refs[kept:]
    sources = [share(ref) if to is None else ref for to, ref in zip(sections, sources)]
    out_ref, all_out, heads_out, lse_out, ot_out, *refs = refs
    targets, refs = refs[:kept], refs[kept:]
    wqkv, wo, heads, lse, ot, partial, wsem, osem, carry_sem, *line = refs
    line = Line(line)
    carried = Carried(sections, sources, targets, carry_sem)
    s = line.s
    rows = out_ref.shape[0]
    kv = heads.shape[0] // (GROUP + 2)
    queries = GROUP * kv
    loads = [pltpu.make_async_copy(qkv_ref, wqkv, wsem.at[0]), pltpu.make_async_copy(wo_ref, wo, wsem.at[1])]
    for load in loads:
        load.start()
    seq_greet(s, carried.section)
    carried.start()
    lse[...] = jnp.zeros_like(lse)

    def project(t):
        part = pl.ds(pl.multiple_of(t * rows, rows), rows)

        @pl.when(t == s)
        def _():
            loads[0].wait()

        qkv = low(dot(line.land[t], wqkv[...]))
        for chunk in range((queries + kv) // 2):
            x = qkv[:, chunk * 128 : (chunk + 1) * 128].astype(jnp.float32)
            x = low(rope(x, cos_ref[part, :], sin_ref[part, :]))
            heads[2 * chunk, part, :] = x[:, :HEAD_DIM]
            heads[2 * chunk + 1, part, :] = x[:, HEAD_DIM:]
        for j in range(kv):
            begin = (queries + kv + j) * HEAD_DIM
            heads[queries + kv + j, part, :] = qkv[:, begin : begin + HEAD_DIM]

    line.gather(x_ref, project)
    saves = [pltpu.make_async_copy(line.land, all_out, osem.at[0]), pltpu.make_async_copy(heads, heads_out, osem.at[1])]
    for save in saves:
        save.start()
    loads[1].wait()

    def attend(block):
        keys = (block + 1) * rows
        columns = slice(block * rows, (block + 1) * rows)

        @pl.loop(0, queries)
        def _(h):
            j = h // GROUP
            scores = dot_t(heads[queries + j, :keys, :], heads[h, columns, :]) * 0.125
            key_at = lax.broadcasted_iota(jnp.int32, scores.shape, 0)
            query_at = lax.broadcasted_iota(jnp.int32, scores.shape, 1) + block * rows
            scores = jnp.where(key_at <= query_at, scores, -jnp.inf)
            peak = jnp.max(scores, axis=0, keepdims=True)
            power = jnp.exp(scores - peak)
            total = jnp.sum(power, axis=0, keepdims=True)
            attended = t_dot(heads[queries + kv + j, :keys, :], low(power / total))
            ot[pl.ds(pl.multiple_of(h * HEAD_DIM, HEAD_DIM), HEAD_DIM), columns] = low(attended)
            lse[pl.ds(h, 1), columns] = peak + jnp.log(total)

        partial[...] = t_dot(ot[:, columns], wo[...])

    @pl.loop(0, 4)
    def _(i):
        t = s ^ (3 - i)
        for block in range(4):

            @pl.when(t == block)
            def _():
                attend(block)

        line.hand_over(t, partial, out_ref)

    saves += [pltpu.make_async_copy(lse, lse_out, osem.at[2]), pltpu.make_async_copy(ot, ot_out, osem.at[3])]
    for save in saves[2:]:
        save.start()
    line.finish(out_ref)
    carried.finish()
    for save in saves:
        save.wait()


def attention_forward_call(x, qkv_w, out_w, tables, collective_id, carry):
    rows, width = x.shape
    local_heads = qkv_w.shape[1] // HEAD_DIM
    bf, f32 = jnp.bfloat16, jnp.float32
    anywhere = pl.BlockSpec(memory_space=pl.ANY)
    near = pl.BlockSpec(memory_space=pltpu.VMEM)
    sections = tuple(to for to, _ in carry)
    arrays = [array for _, array in carry]
    results = [
        ((rows, width), f32),
        ((4, rows, width), bf),
        ((local_heads, 4 * rows, HEAD_DIM), bf),
        ((8, 4 * rows), f32),
        ((out_w.shape[0], 4 * rows), bf),
    ]

    def kernel(*refs):
        attention_forward_kernel(sections, *refs)

    return pl.pallas_call(
        kernel,
        out_shape=[jax.ShapeDtypeStruct(*result) for result in results]
        + [
            jax.ShapeDtypeStruct(share_shape(array) if to is None else array.shape, array.dtype)
            for to, array in carry
        ],
        in_specs=[anywhere] * 3 + [near] * 2 + [anywhere] * len(arrays),
        out_specs=[near] + [anywhere] * (4 + len(arrays)),
        scratch_shapes=[
            pltpu.VMEM(qkv_w.shape, bf),
            pltpu.VMEM(out_w.shape, bf),
            pltpu.VMEM(*results[2]),
            pltpu.VMEM(*results[3]),
            pltpu.VMEM(*results[4]),
            pltpu.VMEM((rows, width), f32),
            DMA((2,)),
            DMA((4,)),
            DMA((max(1, len(arrays)), 2)),
        ]
        + seq_scratch(rows, width),
        compiler_params=pltpu.CompilerParams(
            collective_id=collective_id, has_side_effects=True, vmem_limit_bytes=60 << 20
        ),
        cost_estimate=cost(),
        name="attention_forward",
    )(x, qkv_w, out_w, *tables, *arrays)


def attention_backward_kernel(
    sections, spreads, x_ref, qkv_ref, wo_ref, cos_ref, sin_ref, heads_in, lse_ref, *refs
):
    kept = len(sections)
    sources, refs = refs[:kept], refs[kept:]
    spread_sources, refs = refs[:spreads], refs[spreads:]
    spreads = spreads // 4
    out_ref, all_out, grads_out, *refs = refs
    targets, refs = refs[:kept], refs[kept:]
    spread_targets, refs = refs[:spreads], refs[spreads:]
    held, refs = refs[: 5 * spreads], refs[5 * spreads :]
    wqkv, wo, heads, douts, dk, dv, dqt, grads, partial, wsem, osem, carry_sem, *line = refs
    spread = [SumSpread(spread_sources, spread_targets[0], held)] if spreads else []
    for side in spread:
        side.load()
    line = Line(line)
    carried = Carried(sections, sources, targets, carry_sem)
    s = line.s
    rows = out_ref.shape[0]
    kv = heads.shape[0] // (GROUP + 2)
    queries = GROUP * kv
    loads = [
        pltpu.make_async_copy(wo_ref, wo, wsem.at[0]),
        pltpu.make_async_copy(qkv_ref, wqkv, wsem.at[1]),
        pltpu.make_async_copy(heads_in, heads, wsem.at[2]),
    ]
    for load in loads:
        load.start()
    seq_greet(s, carried.section, spreads > 0)
    carried.start()
    dk[...] = jnp.zeros_like(dk)
    dv[...] = jnp.zeros_like(dv)

    def project(t):
        part = pl.ds(pl.multiple_of(t * rows, rows), rows)

        @pl.when(t == s)
        def _():
            loads[0].wait()

        grad = low(dot_t(line.land[t], wo[...]))
        for h in range(queries):
            douts[h, part, :] = grad[:, h * HEAD_DIM : (h + 1) * HEAD_DIM]

    line.gather(x_ref, project)
    saves = [pltpu.make_async_copy(line.land, all_out, osem.at[0])]
    saves[0].start()
    for side in spread:
        side.start()
    loads[1].wait()
    loads[2].wait()

    for block in (3, 2, 1, 0):
        keys = (block + 1) * rows
        part = slice(block * rows, (block + 1) * rows)

        @pl.loop(0, queries)
        def _(h):
            j = h // GROUP
            key = heads[queries + j, :keys, :]
            query = heads[h, part, :]
            grad = douts[h, part, :]
            scores = dot_t(key, query) * 0.125
            key_at = lax.broadcasted_iota(jnp.int32, scores.shape, 0)
            query_at = lax.broadcasted_iota(jnp.int32, scores.shape, 1) + block * rows
            scores = jnp.where(key_at <= query_at, scores, -jnp.inf)
            probs = jnp.exp(scores - lse_ref[pl.ds(h, 1), part])
            dprobs = dot_t(heads[queries + kv + j, :keys, :], grad)
            mean = jnp.sum(probs * dprobs, axis=0, keepdims=True)
            dscores = low(probs * (dprobs - mean))
            dk[j, :keys, :] += dot(dscores, query) * 0.125
            dv[j, :keys, :] += dot(low(probs), grad)
            dqt[pl.ds(pl.multiple_of(h * HEAD_DIM, HEAD_DIM), HEAD_DIM), :] = t_dot(key, dscores) * 0.125

        cos_part, sin_part = cos_ref[part, :], -sin_ref[part, :]
        dq = dqt[...].T
        for chunk in range(queries // 2):
            lanes = slice(chunk * 128, (chunk + 1) * 128)
            grads[part, lanes] = low(rope(dq[:, lanes], cos_part, sin_part))
        for pair in range(kv // 2):
            both = jnp.concatenate([dk[2 * pair, part, :], dk[2 * pair + 1, part, :]], axis=1)
            begin = queries * HEAD_DIM + pair * 128
            grads[part, begin : begin + 128] = low(rope(both, cos_part, sin_part))
            both = jnp.concatenate([dv[2 * pair, part, :], dv[2 * pair + 1, part, :]], axis=1)
            begin = (queries + kv) * HEAD_DIM + pair * 128
            grads[part, begin : begin + 128] = low(both)
        partial[...] = dot_t(grads[part, :], wqkv[...])
        line.hand_over(block, partial, out_ref)

    saves.append(pltpu.make_async_copy(grads, grads_out, osem.at[1]))
    saves[1].start()
    line.finish(out_ref)
    carried.finish()
    for side in spread:
        side.finish()
    for save in saves:
        save.wait()


def attention_backward_call(x, qkv_w, out_w, tables, heads, lse, collective_id, carry, spread=()):
    rows, width = x.shape
    bf, f32 = jnp.bfloat16, jnp.float32
    anywhere = pl.BlockSpec(memory_space=pl.ANY)
    near = pl.BlockSpec(memory_space=pltpu.VMEM)
    sections = tuple(to for to, _ in carry)
    arrays = [array for _, array in carry]
    results = [((rows, width), f32), ((4, rows, width), bf), ((4 * rows, qkv_w.shape[1]), bf)]
    kv = heads.shape[0] // (GROUP + 2)
    queries = GROUP * kv

    carries = [jax.ShapeDtypeStruct(array.shape, array.dtype) for array in arrays]
    if spread:
        carries.append(jax.ShapeDtypeStruct(parts_shape(spread[0]), bf))
    arrays = arrays + list(spread)

    def kernel(*refs):
        attention_backward_kernel(sections, len(spread), *refs)

    return pl.pallas_call(
        kernel,
        out_shape=[jax.ShapeDtypeStruct(*result) for result in results]
        + carries,
        in_specs=[anywhere] * 3 + [near] * 2 + [anywhere, near] + [anywhere] * len(arrays),
        out_specs=[near] + [anywhere] * (2 + len(carries)),
        scratch_shapes=sum_scratch(spread)
        + [
            pltpu.VMEM(qkv_w.shape, bf),
            pltpu.VMEM(out_w.shape, bf),
            pltpu.VMEM(heads.shape, bf),
            pltpu.VMEM((queries, 4 * rows, HEAD_DIM), bf),
            pltpu.VMEM((kv, 4 * rows, HEAD_DIM), f32),
            pltpu.VMEM((kv, 4 * rows, HEAD_DIM), f32),
            pltpu.VMEM((queries * HEAD_DIM, rows), f32),
            pltpu.VMEM(*results[2]),
            pltpu.VMEM((rows, width), f32),
            DMA((3,)),
            DMA((2,)),
            DMA((max(1, len(carry)), 2)),
        ]
        + seq_scratch(rows, width),
        compiler_params=pltpu.CompilerParams(
            collective_id=collective_id, has_side_effects=True, vmem_limit_bytes=60 << 20
        ),
        cost_estimate=cost(),
        name="attention_backward",
    )(x, qkv_w, out_w, *tables, heads, lse, *arrays)


def last_kernel(sections, own_0, own_1, in_0, in_1, cols_ref, cols_other, out_ref, out_other, *refs):
    kept = len(sections)
    sources, refs = refs[:kept], refs[kept:]
    down_out, cols_out, rows_out, *refs = refs
    targets, refs = refs[:kept], refs[kept:]
    cols_in, cols, out_in, out_sum, cols_sem, row_sem, swap_sem, carry_sem, *held = refs
    down = SumSpread((own_0, own_1, in_0, in_1), down_out, held)
    down.load()
    d, s, section = lax.axis_index("dp"), lax.axis_index("seq"), lax.axis_index("section")
    barrier = pltpu.get_barrier_semaphore()

    def signal(**device):
        pl.semaphore_signal(barrier, inc=1, device_id=device, device_id_type=MESH)

    for flip in (1, 2, 3):
        signal(seq=s ^ flip)
    signal(section=1 - section)

    @pl.when(d != s)
    def _():
        signal(dp=s, seq=d)
        pl.semaphore_wait(barrier, 5)

    @pl.when(d == s)
    def _():
        pl.semaphore_wait(barrier, 4)

    swaps = Carried((None, None), (cols_other, out_other), (cols_in, out_in), swap_sem)
    carried = Carried(sections, sources, targets, carry_sem)
    swaps.start()
    down.start()
    swaps.finish()
    carried.start()
    cols[...] = low(cols_ref[...].astype(jnp.float32) + cols_in[...].astype(jnp.float32))
    out_sum[...] = low(out_ref[...].astype(jnp.float32) + out_in[...].astype(jnp.float32))
    spread = Spread(cols, cols_out, cols_sem)
    spread.start()
    rows = remote(out_sum, rows_out, row_sem.at[0], row_sem.at[1], dp=s, seq=d)

    @pl.when(d != s)
    def _():
        rows.start()
        rows.wait()

    @pl.when(d == s)
    def _():
        rows_out[...] = out_sum[...]

    spread.finish()
    down.finish()
    carried.finish()


def last_exchange(downs, cols, cols_other, out, out_other, collective_id, carry):
    bf = jnp.bfloat16
    anywhere = pl.BlockSpec(memory_space=pl.ANY)
    near = pl.BlockSpec(memory_space=pltpu.VMEM)
    sections = tuple(to for to, _ in carry)
    arrays = [array for _, array in carry]

    def kernel(*refs):
        last_kernel(sections, *refs)

    return pl.pallas_call(
        kernel,
        out_shape=[
            jax.ShapeDtypeStruct(parts_shape(downs[0]), bf),
            *[jax.ShapeDtypeStruct(array.shape, array.dtype) for array in (cols, out, *arrays)],
        ],
        in_specs=[anywhere] * 4 + [near, anywhere, near, anywhere] + [anywhere] * len(arrays),
        out_specs=[anywhere, near, near] + [anywhere] * len(arrays),
        scratch_shapes=[
            pltpu.VMEM(cols.shape, bf),
            pltpu.VMEM(cols.shape, bf),
            pltpu.VMEM(out.shape, bf),
            pltpu.VMEM(out.shape, bf),
            DMA((4, 2)),
            DMA((2,)),
            DMA((2, 2)),
            DMA((max(1, len(arrays)), 2)),
        ]
        + sum_scratch(downs),
        compiler_params=pltpu.CompilerParams(
            collective_id=collective_id, has_side_effects=True, vmem_limit_bytes=60 << 20
        ),
        name="last_exchange",
    )(*downs, cols, cols_other, out, out_other, *arrays)


def wide_tables(length):
    half_dim = HEAD_DIM // 2
    frequency = 10000.0 ** (-np.arange(half_dim, dtype=np.float32) * 2.0 / HEAD_DIM)
    angles = np.arange(length, dtype=np.float32)[:, None] * frequency.astype(np.float32)[None, :]
    cos_table, sin_table = np.cos(angles), np.sin(angles)
    return (
        jnp.asarray(np.concatenate([cos_table] * 4, axis=1), jnp.float32),
        jnp.asarray(np.concatenate([-sin_table, sin_table] * 2, axis=1), jnp.float32),
    )


def token_choice(route):
    return route[..., None] == jnp.arange(EXPERTS, dtype=jnp.int32)


def routing(route_all, first_expert, count):
    chosen = jnp.any(token_choice(route_all), axis=2)
    blocks, rows = chosen.shape[:2]
    mine = lax.dynamic_slice_in_dim(chosen, first_expert, count, axis=2)
    chosen = low(jnp.transpose(chosen, (0, 2, 1)))
    earlier = jnp.tril(jnp.ones((rows, rows), jnp.bfloat16), -1)
    place = jnp.einsum(
        "ts,bsj->bjt", earlier, mine.astype(jnp.bfloat16), preferred_element_type=jnp.float32
    ).astype(jnp.int32)
    mine = jnp.transpose(mine, (0, 2, 1))
    place = jnp.where(mine, place, -1)
    slots = jnp.arange(CAP, dtype=jnp.int32)
    pick = low(place[:, :, None, :] == slots[None, None, :, None]).reshape(blocks, -1, rows)
    return chosen, pick, jnp.transpose(pick, (0, 2, 1))


def choose(pick, rows, count):
    picked = jnp.einsum("bct,btd->bcd", pick, rows, preferred_element_type=jnp.float32)
    blocks = pick.shape[0]
    picked = low(picked).reshape(blocks, count, CAP, -1)
    return jnp.transpose(picked, (1, 0, 2, 3)).reshape(count, blocks * CAP, -1)


def give_back(pick_t, slot_rows):
    blocks, rows = pick_t.shape[:2]
    count, _, width = slot_rows.shape
    slot_rows = jnp.transpose(slot_rows.reshape(count, blocks, CAP, width), (1, 0, 2, 3))
    slot_rows = slot_rows.reshape(blocks, count * CAP, width)
    total = jnp.einsum("btc,bcd->btd", pick_t, slot_rows, preferred_element_type=jnp.float32)
    return low(total).reshape(-1, width)


def each_dot(form, a, b):
    return jnp.einsum(form, a, b, preferred_element_type=jnp.float32)


def after(value, *others):
    return lax.optimization_barrier((value, *others))[0]


def has_kernels():
    return lax.axis_size("dp") == 4 and lax.axis_size("seq") == 4


def forward_layer(number, layer_in, picking, weights, experts, *carry):
    attn_scale, ffn_scale, qkv_w, out_w, router_w = weights
    chosen, pick, pick_t, first_expert = picking
    own, other = experts
    count = pick.shape[1] // CAP
    blocks, _, rows = chosen.shape
    received = []
    normed_input = low(rms_norm(layer_in, attn_scale))
    if has_kernels():
        branch, normed_all, heads, log_total, mixed_t, *received = attention_forward_call(
            normed_input, qkv_w, out_w, wide_tables(4 * layer_in.shape[0]), 9 + number, carry
        )
        attention_state = (normed_all.reshape(-1, layer_in.shape[1]), mixed_t, heads, log_total)
    else:
        received = [swap(array) if to is None else pass_to(array, to) for to, array in carry]
        normed_all = lax.all_gather(normed_input, "seq", axis=0, tiled=True)
        qkv = low(dot(normed_all, qkv_w))
        kv_width = KV_HEADS * HEAD_DIM // lax.axis_size("seq")
        q_width = GROUP * kv_width
        mixed, log_total, q_rot, k_rot, v_heads = attention_forward(
            qkv[:, :q_width], qkv[:, q_width : q_width + kv_width], qkv[:, q_width + kv_width :]
        )
        branch = lax.psum_scatter(low(dot(mixed, out_w)), "seq", scatter_dimension=0, tiled=True)
        attention_state = (normed_all, mixed.T, (q_rot, k_rot, v_heads), log_total)
    after_update = layer_in + branch.astype(jnp.float32)
    normed_ffn = low(rms_norm(after_update, ffn_scale))
    own_block = lax.axis_index("dp") * lax.axis_size("seq") + lax.axis_index("seq")
    own_chosen = lax.dynamic_index_in_dim(chosen, own_block, 0, keepdims=False)
    own_logits = jnp.where(own_chosen > 0, dot_t(router_w, normed_ffn), -jnp.inf)
    own_gates = jax.nn.softmax(own_logits, axis=0)
    if number == 0:
        other = other + (received[0],)
    mine = (
        jnp.arange(EXPERTS)[None, None, :] == first_expert + jnp.arange(count)[:, None, None]
    ).astype(jnp.float32)
    if has_kernels():
        *expert_state, slot_out = expert_forward(
            number, normed_ffn, pick, chosen, router_w, mine, own, other, 1 + number
        )
        if number == 0:
            *expert_state, slot_out, other_down = (*expert_state, slot_out)
            other = other[:2] + (other_down,)
    else:
        if number == 0:
            other = other[:2] + (swap(own[2]),)
        gate_w, up_w, down_w = by_layer(number, own, other)
        ffn_all = lax.all_gather(normed_ffn, TOKENS, axis=0, tiled=True)
        logits = dot_t(ffn_all, router_w).reshape(blocks, rows, EXPERTS)
        used = jnp.transpose(chosen, (0, 2, 1)) > 0
        gates = jax.nn.softmax(jnp.where(used, logits, -jnp.inf), axis=-1)
        slot_rows = choose(pick, ffn_all.reshape(blocks, rows, -1), count)
        mine_gates = jnp.einsum("bte,jxe->bjt", gates, mine, precision=lax.Precision.HIGHEST)
        slot_gates = jnp.sum(
            pick.reshape(blocks, count, CAP, rows).astype(jnp.float32) * mine_gates[:, :, None, :],
            axis=3,
        )
        slot_gates = jnp.transpose(slot_gates, (1, 0, 2)).reshape(count, -1, 1)
        gate_pre = each_dot("ecd,edf->ecf", slot_rows, gate_w)
        up_pre = each_dot("ecd,edf->ecf", slot_rows, up_w)
        scaled = low(slot_gates * jax.nn.silu(gate_pre) * up_pre)
        slot_out = low(each_dot("ecf,efd->ecd", scaled, down_w))
        expert_state = (slot_rows, gate_pre, up_pre, scaled, slot_gates)
    saved = (
        layer_in,
        attention_state,
        after_update,
        normed_ffn,
        own_gates,
        expert_state,
    )
    return (after_update, slot_out, saved, (own, other), received)


def token_sums(pick_t, slot_out, collective_id, *carry, spread=(), products=()):
    if has_kernels():
        sums, *received = combine(pick_t, slot_out, collective_id, carry, spread, products)
        return sums, received
    sums = give_back(pick_t, slot_out).astype(jnp.float32)
    sums = lax.psum_scatter(sums, TOKENS, scatter_dimension=0, tiled=True)
    received = [pass_to(array, to) for to, array in carry]
    grads = [
        low(each_dot("eck,ecn->ekn", left, right)) for left, rights in products for right in rights
    ]
    return sums, received + list(spread) + grads


def spread_rows(parts):
    return lax.all_to_all(parts, "seq", split_axis=0, concat_axis=0, tiled=True)


def expert_gradients(number, layer_grad, saved, picking, experts, *carry, grad_all=None):
    chosen, pick, pick_t, first_expert = picking
    own, other = experts
    count = pick.shape[1] // CAP
    blocks, _, rows = chosen.shape
    slot_rows, gate_pre, up_pre, scaled, slot_gates = saved[-1]
    if has_kernels():
        slot_grads, gate_low, up_low, gate_term, slot_out, *received = expert_backward(
            number, low(layer_grad) if grad_all is None else grad_all, pick, gate_pre, up_pre, slot_gates, own, other, 4 + number, carry
        )
        gate_term = gate_term[:, :, :1]
    else:
        gate_w, up_w, down_w = by_layer(number, own, other)
        grad_all = lax.all_gather(low(layer_grad), TOKENS, axis=0, tiled=True)
        slot_grads = choose(pick, grad_all.reshape(blocks, rows, -1), count)
        plain_grad = each_dot("ecd,efd->ecf", slot_grads, down_w)
        sigmoid = jax.nn.sigmoid(gate_pre)
        activated = gate_pre * sigmoid
        gate_term = jnp.sum(plain_grad * (activated * up_pre), axis=2, keepdims=True)
        hidden_grad = slot_gates * plain_grad
        gate_low = low(hidden_grad * up_pre * sigmoid * (1.0 + gate_pre * (1.0 - sigmoid)))
        up_low = low(hidden_grad * activated)
        slot_out = low(
            each_dot("ecf,edf->ecd", gate_low, gate_w) + each_dot("ecf,edf->ecd", up_low, up_w)
        )
        received = [pass_to(array, to) for to, array in carry]
    by_slot = jnp.transpose(gate_term.reshape(count, blocks, CAP), (1, 0, 2))
    gate_terms = jnp.sum(
        pick.reshape(blocks, count, CAP, rows).astype(jnp.float32) * by_slot[..., None], axis=2
    )
    gate_terms = lax.all_to_all(gate_terms, TOKENS, split_axis=0, concat_axis=0, tiled=True)
    products = ((slot_rows, (gate_low, up_low)), (scaled, (slot_grads,)))
    return slot_out, gate_terms, products, received


def backward_layer(
    number, layer_grad, normed_grad, gate_terms, saved, picking, weights, *carry, spread=()
):
    attn_scale, ffn_scale, qkv_w, out_w, router_w = weights
    chosen, pick, _, _ = picking
    (
        layer_in,
        (normed_all, mixed_t, heads, log_total),
        after_update,
        normed_ffn,
        own_gates,
        _,
    ) = saved
    rows = chosen.shape[2]
    gate_terms = jnp.sum(gate_terms.reshape(EXPERTS, -1, rows), axis=1)
    logit_grad = low(
        own_gates * (gate_terms - jnp.sum(own_gates * gate_terms, axis=0, keepdims=True))
    )
    router_grad = dot(logit_grad, normed_ffn)
    normed_grad = normed_grad + t_dot(logit_grad, router_w)
    after_part, ffn_gain_grad = jax.vjp(rms_norm, after_update, ffn_scale)[1](normed_grad)
    after_grad = after_part + layer_grad
    if has_kernels():
        normed_attn, branch_all, qkv_grad, *received = attention_backward_call(
            low(after_grad),
            qkv_w,
            out_w,
            wide_tables(4 * layer_in.shape[0]),
            heads,
            log_total,
            11 + number,
            carry,
            spread,
        )
        branch_all = branch_all.reshape(-1, layer_in.shape[1])
    else:
        branch_all = lax.all_gather(low(after_grad), "seq", axis=0, tiled=True)
        head_grad = low(dot_t(branch_all, out_w))
        qkv_grad = attention_backward(head_grad, *heads, log_total)
        normed_attn = low(dot_t(qkv_grad, qkv_w))
        normed_attn = lax.psum_scatter(normed_attn, "seq", scatter_dimension=0, tiled=True)
        received = [pass_to(array, to) for to, array in carry]
        received = received + list(spread)
    out_grad = dot(mixed_t, branch_all)
    qkv_weight_grad = t_dot(normed_all, qkv_grad)
    input_part, attn_gain_grad = jax.vjp(rms_norm, layer_in, attn_scale)[1](
        normed_attn.astype(jnp.float32)
    )
    small = [router_grad, attn_gain_grad[None], ffn_gain_grad[None]]
    small = jnp.concatenate(small + [jnp.zeros((128 - EXPERTS - 2, small[0].shape[1]))], axis=0)
    qkv_weight_grad = jnp.concatenate([low(qkv_weight_grad), low(small).T], axis=1)
    return (input_part + after_grad, (qkv_weight_grad, low(out_grad)), received)


def by_layer(number, own, other):
    is_own = lax.axis_index("section") == number
    return jax.tree.map(lambda mine, received: jnp.where(is_own, mine, received), own, other)


def body(
    hidden_in,
    out_grad,
    attn_gain,
    ffn_gain,
    query_matrix,
    key_matrix,
    value_matrix,
    output_matrix,
    router_matrix,
    w_gate,
    w_up,
    w_down,
    routes,
):
    section = lax.axis_index("section")
    dp, seq = lax.axis_size("dp"), lax.axis_size("seq")
    seq_index = lax.axis_index("seq")
    first = section == 0
    width = hidden_in.shape[3]
    depth = query_matrix.shape[1]

    layer_in = lax.dynamic_index_in_dim(hidden_in, section, 0, keepdims=False)[0]
    top_grad = lax.dynamic_index_in_dim(out_grad, section, 0, keepdims=False)[0]
    own_group = jnp.concatenate(
        [
            matrix[0].reshape(depth, seq, -1)
            for matrix in (query_matrix, key_matrix, value_matrix)
        ],
        axis=2,
    )
    own_group = jnp.transpose(own_group, (1, 0, 2))
    to_group = []
    for flat in range(dp * seq):
        to_group.append((flat, (flat % dp) * seq + flat // dp))
    from_group = [(target, source) for source, target in to_group]
    own_out = lax.ppermute(output_matrix[0], TOKENS, to_group)
    other_out = swap(own_out)
    local = w_gate.shape[1]
    hidden_units = w_gate.shape[3]
    if local >= seq:
        count, units = local // seq, hidden_units
        start, unit_start = seq_index * count, 0
    else:
        count, units = 1, hidden_units * local // seq
        start, unit_start = seq_index * local // seq, (seq_index % (seq // local)) * units
    first_expert = lax.axis_index("dp") * local + start
    if has_kernels():
        own_experts = (w_gate[0], w_up[0], w_down[0])
    else:
        own_experts = (
            lax.dynamic_slice(w_gate[0], (start, 0, unit_start), (count, width, units)),
            lax.dynamic_slice(w_up[0], (start, 0, unit_start), (count, width, units)),
            lax.dynamic_slice(w_down[0], (start, unit_start, 0), (count, units, width)),
        )
    small = jnp.concatenate([router_matrix[0].T, attn_gain, ffn_gain], axis=0)
    paths = routes[0, :, 0]
    if has_kernels():
        small = jnp.pad(small, ((0, -small.shape[0] % 16), (0, 256 - depth)))
        paths = low(jnp.transpose(paths, (0, 2, 1)).reshape(2 * TOP_K, -1))
        *tables, small, qkv_first, qkv_second, other_gate, top_all = prepare(
            jnp.concatenate([paths, small], axis=0),
            own_group,
            own_experts[0],
            top_grad,
            count,
            depth,
            13,
        )
        pickings = [(tables[4 + n], tables[n], tables[2 + n], first_expert) for n in range(2)]
        qkv_second = lax.all_gather(
            qkv_second.reshape(seq * depth, -1), "dp", axis=0, tiled=True
        )
        qkv_layers = [qkv_first.reshape(width, -1), qkv_second]
    else:
        small = lax.all_gather(small, ("section", "dp", "seq"), axis=0, tiled=False)
        small = jnp.transpose(small.reshape(2, dp * seq, -1, depth), (0, 2, 1, 3))
        small = small.reshape(2, -1, width)
        paths = lax.all_gather(paths, ("section", "dp", "seq"), axis=0, tiled=False)
        paths = lax.dynamic_index_in_dim(paths, section, 1, keepdims=False)
        paths = paths.reshape(2, dp * seq, -1, TOP_K)
        pickings = [routing(paths[n], first_expert, count) + (first_expert,) for n in range(2)]
        other_gate = swap(own_experts[0])
        top_all = None
        other_group = swap(own_group)
        qkv_layers = []
        for number in range(2):
            part = spread_rows(by_layer(number, own_group, other_group))
            part = part.reshape(seq * depth, -1)
            qkv_layers.append(lax.all_gather(part, "dp", axis=0, tiled=True))

    weights = []
    for number in range(2):
        out_w = lax.all_gather(
            by_layer(number, own_out, other_out), "dp", axis=0, tiled=True
        )
        weights.append(
            (
                small[number, EXPERTS].astype(jnp.float32),
                small[number, EXPERTS + 1].astype(jnp.float32),
                qkv_layers[number],
                out_w,
                small[number, :EXPERTS],
            )
        )

    def own_layer(pieces):
        return jnp.where(first, pieces[0], pieces[1])

    def both_micros(own, other):
        return jnp.stack([jnp.where(first, own, other), jnp.where(first, other, own)])[
            None, :, None
        ]

    def summed(own, other):
        return own_layer(own).astype(jnp.float32) + own_layer(other).astype(jnp.float32)

    def dp_sums(dense):
        return [lax.psum_scatter(part, "dp", scatter_dimension=0, tiled=True) for part in dense]

    def row_parts(piece, kind):
        if local >= seq:
            piece = piece.reshape(count, seq, piece.shape[1] // seq, -1)
            return jnp.transpose(piece, (1, 0, 2, 3))
        if kind < 2:
            return piece.reshape(seq, -1, units)
        piece = piece.reshape(-1, hidden_units // seq, width)
        share = seq // local
        parts = jnp.zeros((seq,) + piece.shape[1:], piece.dtype)
        return lax.dynamic_update_slice_in_dim(
            parts, piece, (seq_index % share) * piece.shape[0], axis=0
        )

    def whole_rows(parts, kind):
        parts = parts.astype(jnp.float32)
        if local < seq:
            parts = parts.reshape((local, seq // local) + parts.shape[1:])
            if kind < 2:
                parts = jnp.transpose(parts, (0, 2, 1, 3))
            else:
                parts = jnp.sum(parts, axis=1)
            return parts.reshape((local,) + parts.shape[1 : 2] + (-1,))[None]
        return parts.reshape((local,) + parts.shape[2:])[None]

    experts = (own_experts, (other_gate,))
    first_in = layer_in.astype(jnp.float32)
    updated, slot_out, first_saved, experts, _ = forward_layer(
        0, first_in, pickings[0], weights[0], experts, (None, own_experts[1])
    )
    sums, _ = token_sums(pickings[0][2], slot_out, 3)
    first_out = updated + sums
    second_updated, second_slots, second_saved, experts, (other_out,) = forward_layer(
        1, first_out, pickings[1], weights[1], experts, (0, first_out)
    )
    top_grad = top_grad.astype(jnp.float32)
    slot_out, gate_terms, products, _ = expert_gradients(
        1, top_grad, second_saved, pickings[1], experts, grad_all=top_all
    )
    sums, second_experts = token_sums(pickings[1][2], slot_out, 6, products=products)
    middle_grad, second_dense, _ = backward_layer(
        1, top_grad, sums, gate_terms, second_saved, pickings[1], weights[1]
    )
    slot_out, gate_terms, products, (second_gate,) = expert_gradients(
        0, middle_grad, first_saved, pickings[0], experts, (1, second_experts[0])
    )
    (rows_in, (gate_low, up_low)), down_product = products
    gate_grad = low(each_dot("ecd,ecf->edf", rows_in, gate_low))
    slot_out, gate_grad, gate_terms = lax.optimization_barrier((slot_out, gate_grad, gate_terms))
    sums, (first_gate, second_up, *first_experts) = token_sums(
        pickings[0][2],
        slot_out,
        7,
        (0, gate_grad),
        (1, second_experts[1]),
        products=((rows_in, (up_low,)), down_product),
    )
    first_experts = [gate_grad, *first_experts]
    sums, *second_dense = lax.optimization_barrier((sums, *second_dense))
    second_dense = dp_sums(second_dense)

    def handed(kind, *received):
        own = (first_experts[kind], second_experts[kind])
        if has_kernels():
            return (*own, *received)
        return [spread_rows(row_parts(low(summed(own, received)), kind))]

    bottom_grad, first_dense, (first_up, second_down, gate_rows) = backward_layer(
        0,
        middle_grad,
        sums,
        gate_terms,
        first_saved,
        pickings[0],
        weights[0],
        (0, first_experts[1]),
        (1, second_experts[2]),
        spread=handed(0, first_gate, second_gate),
    )
    second_slots, *dense = lax.optimization_barrier((second_slots, *first_dense, *second_dense))
    first_dense, second_dense = dense[:2], dense[2:]
    first_dense = dp_sums(first_dense)
    sums, (first_down, other_middle, up_rows) = token_sums(
        pickings[1][2],
        second_slots,
        8,
        (0, first_experts[2]),
        (1, middle_grad),
        spread=handed(1, first_up, second_up),
    )
    sums, *first_dense = lax.optimization_barrier((sums, *first_dense))
    second_out = second_updated + sums
    own_cols, own_rows = [own_layer((first_dense[k], second_dense[k])) for k in range(2)]
    other_cols, other_rows = [own_layer((second_dense[k], first_dense[k])) for k in range(2)]
    if has_kernels():
        down_rows, cols_sum, out_sum, other_second, other_bottom = last_exchange(
            handed(2, first_down, second_down),
            own_cols.reshape(seq, depth, -1),
            other_cols.reshape(seq, depth, -1),
            own_rows,
            other_rows,
            14,
            ((1, second_out), (0, bottom_grad)),
        )
    else:
        (down_rows,) = handed(2, first_down, second_down)
        cols_sum = low(own_cols.astype(jnp.float32) + swap(other_cols).astype(jnp.float32))
        cols_sum = spread_rows(cols_sum.reshape(seq, depth, -1))
        out_sum = low(own_rows.astype(jnp.float32) + swap(other_rows).astype(jnp.float32))
        out_sum = lax.ppermute(out_sum, TOKENS, from_group)
        other_second, other_bottom = pass_to(second_out, 1), pass_to(bottom_grad, 0)
    expert_sums = [whole_rows(rows, k) for k, rows in enumerate((gate_rows, up_rows, down_rows))]
    layer_outs = both_micros(
        own_layer((first_out, second_out)), own_layer((other_out, other_second))
    )
    section_grads = both_micros(
        own_layer((bottom_grad, middle_grad)), own_layer((other_bottom, other_middle))
    )
    qkv_sum, out_sum = cols_sum.astype(jnp.float32), out_sum.astype(jnp.float32)
    kv_width = KV_HEADS * HEAD_DIM // seq
    q_width = GROUP * kv_width
    qkv_width = q_width + 2 * kv_width
    small_sum = jnp.sum(qkv_sum[:, :, qkv_width:], axis=0)

    def columns(begin, end):
        return jnp.transpose(qkv_sum[:, :, begin:end], (1, 0, 2)).reshape(depth, -1)[None]

    return (
        layer_outs,
        section_grads,
        small_sum[:, EXPERTS][None],
        small_sum[:, EXPERTS + 1][None],
        columns(0, q_width),
        columns(q_width, q_width + kv_width),
        columns(q_width + kv_width, qkv_width),
        out_sum[None],
        small_sum[:, :EXPERTS][None],
        *expert_sums,
    )


def solution(mesh):
    return jax.shard_map(
        body,
        mesh=mesh,
        in_specs=(
            P(None, "dp", "seq", None),
            P(None, "dp", "seq", None),
            P("section", ("dp", "seq")),
            P("section", ("dp", "seq")),
            P("section", ("dp", "seq"), None),
            P("section", ("dp", "seq"), None),
            P("section", ("dp", "seq"), None),
            P("section", ("dp", "seq"), None),
            P("section", ("dp", "seq"), None),
            P("section", "dp", None, None),
            P("section", "dp", None, None),
            P("section", "dp", None, None),
            P("section", None, "dp", "seq", None),
        ),
        out_specs=(
            P("section", None, "dp", "seq", None),
            P("section", None, "dp", "seq", None),
            P("section", ("dp", "seq")),
            P("section", ("dp", "seq")),
            P("section", ("dp", "seq"), None),
            P("section", ("dp", "seq"), None),
            P("section", ("dp", "seq"), None),
            P("section", ("dp", "seq"), None),
            P("section", ("dp", "seq"), None),
            P("section", "dp", "seq", None),
            P("section", "dp", "seq", None),
            P("section", "dp", "seq", None),
        ),
        check_vma=False,
    )
```
